32 devices in a mesh: parts: 2 (over y), space: 16 (over z, x, core).
Axes of the slice: x: 2, y: 2, z: 4, core: 2. Of those that a mesh axis runs over, the one named last changes fastest.
Arguments:
- density: float32 [32, 32, 128], P('space', 'parts'), parts along dimension 1, may hold values from 0.14 to 1
- displacement: float32 [16, 3, 32, 32, 128], P('space', None, None, 'parts'), parts along dimension 3, may hold values from -6 to 6
- fixed: int32 [32, 256], P(None, 'parts'), parts along dimension 1, may hold values 0 or 1
- load_index: int32 [32], P('parts'), parts along dimension 0, may hold values from 0 to 65535
- load_force: float32 [32, 3], P('parts'), parts along dimension 0, may hold values from -120 to 120
- radius: int32 [32], P('parts'), parts along dimension 0, may hold values from 1 to 3
Outputs:
- new_density: float32 [32, 32, 128], P('space', 'parts'), parts along dimension 1
- new_displacement: float32 [16, 3, 32, 32, 128], P('space', None, None, 'parts'), parts along dimension 3
The draws below stay inside these ranges and needn't reach their ends.
There are 2 independent parts, one for each index of `parts`. The reference program is written for one: setup_inputs(seed, part) draws one part's arguments, and reference() takes and returns one part's arrays. A program takes and returns all parts, laid end to end along the dimension named above; each array names one. Nothing has to cross between parts.
All inputs are finite; a program needn't handle non-finite values.
Results may differ from the reference program's by a relative error of at most 0.0003.
Values sent between devices are 32-bit elements; how exact they have to be, the bound alone decides.
No kernel may reach another device: no remote copies, remote signals or barrier semaphores. Data moves between devices by JAX's collectives and lax.ppermute only.
A program may use at most 64 MiB of HBM per device.

```python
import math
import jax
import jax.numpy as jnp
from jax import lax

NZ = 16
NY = 128
LOADS = 16
SWEEPS = 3
DESIGN_ITERS = 1
SEARCH = 12
NX = 32
SLAB = 32
SLABS = 1


def draw_density(key, part):
    key = jax.random.fold_in(key, 11)
    position = jnp.arange(NX, dtype=jnp.float32)[:, None, None] / max(NX - 1, 1)
    spread = jax.random.uniform(key, (NX, NZ, NY), jnp.float32, 0.5, 1.0)
    return 0.1 + spread * (0.15 + 0.75 * position)


def part_factor(part, smaller, larger):
    return jnp.where(part % 2 == 0, jnp.float32(smaller), jnp.float32(larger))


def draw_displacement(key, part):
    key = jax.random.fold_in(key, 23)
    shape_all = (SLABS * LOADS, 3, SLAB, NZ, NY)
    values = jax.random.truncated_normal(key, -6.0, 6.0, shape_all, jnp.float32)
    factor = part_factor(part, 0.05, 1.0)
    return values * factor


def draw_load_force(key, part):
    key = jax.random.fold_in(key, 37)
    values = 20.0 * jax.random.truncated_normal(key, -6.0, 6.0, (LOADS, 3), jnp.float32)
    factor = part_factor(part, 0.05, 1.0)
    return values * factor


def touch_ends(values, stream_key, least, largest):
    longest = values.shape.index(max(values.shape))
    spots = []
    for shift in (0, 1):
        where = [jax.random.randint(jax.random.fold_in(stream_key, axis), (), 0, length) for axis, length in enumerate(values.shape)]
        where[longest] = (where[longest] + shift) % values.shape[longest]
        spots.append(tuple(where))
    return values.at[spots[0]].set(least).at[spots[1]].set(largest)


def setup_inputs(seed: int = 0, part: int = 0) -> dict:
    key_of = jax.random.split(jax.random.key(seed), 7)
    own_keys = jax.random.split(jax.random.fold_in(key_of[6], part), 7)
    density = draw_density(jax.random.fold_in(jax.random.fold_in(key_of[6], part), 71), part)
    displacement = draw_displacement(jax.random.fold_in(jax.random.fold_in(key_of[6], part), 71), part)
    fixed = touch_ends((jax.random.randint(own_keys[2], (NX, NY), 0, 8) < 1).astype(jnp.int32), jax.random.fold_in(own_keys[2], 1), 0, 1)
    load_index = touch_ends(jax.random.randint(own_keys[3], (LOADS,), 0, NX * NZ * NY), jax.random.fold_in(own_keys[3], 1), 0, (NX * NZ * NY) - 1).astype(jnp.int32)
    load_force = draw_load_force(jax.random.fold_in(jax.random.fold_in(key_of[6], part), 71), part)
    radius = touch_ends(jax.random.randint(own_keys[5], (NZ,), 1, 4), jax.random.fold_in(own_keys[5], 1), 1, 3).astype(jnp.int32)
    return {"density": density, "displacement": displacement, "fixed": fixed, "load_index": load_index, "load_force": load_force, "radius": radius}


floor_modulus = 0.05
relax_factor = 0.6
move_limit = 0.2
density_floor = 0.01
volume_share = 0.5
log_lower = -16.0
log_span = 32.0
window_reach = 2

def window_offsets():
    offsets_list = []
    for across in range(-window_reach, window_reach + 1):
        for upward in range(-window_reach, window_reach + 1):
            for sideways in range(-window_reach, window_reach + 1):
                length = math.sqrt(across * across + upward * upward + sideways * sideways)
                offsets_list.append((across, upward, sideways, length))
    return offsets_list

def layer_weights(radius):
    radial = radius.astype(jnp.float32)
    return jnp.stack([jnp.maximum(radial - length, 0.0) for across, upward, sideways, length in window_offsets()])

def pad_axis(grid_field, along_axis, before, after_cells):
    widths = [(0, 0)] * grid_field.ndim
    widths[along_axis] = (before, after_cells)
    return jnp.pad(grid_field, widths)

def filter_forward(padded, weights):
    out_rows = padded.shape[0] - 2 * window_reach
    layers = padded.shape[1] - 2 * window_reach
    row_width = padded.shape[2] - 2 * window_reach
    result = jnp.zeros((out_rows, layers, row_width), jnp.float32)
    for offset_index, (across, upward, sideways, length) in enumerate(window_offsets()):
        shifted = padded[window_reach + across:window_reach + across + out_rows, window_reach + upward:window_reach + upward + layers, window_reach + sideways:window_reach + sideways + row_width]
        result = result + weights[offset_index][None, :, None] * shifted
    return result

def filter_backward(padded, padded_weights):
    out_rows = padded.shape[0] - 2 * window_reach
    layers = padded.shape[1] - 2 * window_reach
    row_width = padded.shape[2] - 2 * window_reach
    result = jnp.zeros((out_rows, layers, row_width), jnp.float32)
    for offset_index, (across, upward, sideways, length) in enumerate(window_offsets()):
        shifted = padded[window_reach - across:window_reach - across + out_rows, window_reach - upward:window_reach - upward + layers, window_reach - sideways:window_reach - sideways + row_width]
        layer_part = padded_weights[offset_index, window_reach - upward:window_reach - upward + layers]
        result = result + layer_part[None, :, None] * shifted
    return result

def stiff_factors(direction):
    return jnp.array([2.0 if component == direction else 1.0 for component in range(3)], jnp.float32).reshape(3, 1, 1, 1)

def relax_sweep(padded, displace, face_x, face_z, face_y, force_field, free_cells, diagonal):
    flux_x = stiff_factors(0) * face_x * jnp.diff(padded, axis=2)
    stencil_image = flux_x[:, :, :-1] - flux_x[:, :, 1:]
    flux_z = stiff_factors(1) * face_z * jnp.diff(displace, axis=3)
    stencil_image = stencil_image + pad_axis(flux_z, 3, 1, 0) - pad_axis(flux_z, 3, 0, 1)
    flux_y = stiff_factors(2) * face_y * jnp.diff(displace, axis=4)
    stencil_image = stencil_image + pad_axis(flux_y, 4, 1, 0) - pad_axis(flux_y, 4, 0, 1)
    return free_cells * (displace + relax_factor * (force_field - stencil_image) / diagonal)

def face_energy(grid_field, along_axis, direction, load_cases):
    change = jnp.diff(grid_field, axis=along_axis)
    return lax.optimization_barrier(jnp.sum(stiff_factors(direction) * change * change, axis=(0, 1))) / load_cases

def unpack_blocks(blocks):
    grouped = blocks.reshape(SLABS, LOADS, 3, SLAB, NZ, NY)
    return jnp.transpose(grouped, (1, 2, 0, 3, 4, 5)).reshape(LOADS, 3, NX, NZ, NY)

def pack_blocks(field):
    grouped = field.reshape(LOADS, 3, SLABS, SLAB, NZ, NY)
    return jnp.transpose(grouped, (2, 0, 1, 3, 4, 5)).reshape(SLABS * LOADS, 3, SLAB, NZ, NY)

def reference(density, displacement, fixed, load_index, load_force, radius):
    weights = layer_weights(radius)
    padded_weights = pad_axis(weights, 1, window_reach, window_reach)
    total_weight = filter_forward(jnp.pad(jnp.ones_like(density), window_reach), weights)
    bottom_layer = (jnp.arange(NZ, dtype=jnp.int32) == 0).astype(jnp.float32)
    free_cells = 1.0 - bottom_layer[None, :, None] * fixed.astype(jnp.float32)[:, None, :]
    cell_index = jnp.arange(NX * NZ * NY, dtype=jnp.int32)
    load_hits = (cell_index[None, :] == load_index[:, None]).astype(jnp.float32)
    force_field = (load_force[:, :, None] * load_hits[:, None, :]).reshape(LOADS, 3, NX, NZ, NY)
    displace = unpack_blocks(displacement) * free_cells
    face_valid = jnp.pad(jnp.ones((NX - 1,), jnp.float32), 1)
    target = volume_share * NX * NZ * NY
    for design_step in range(DESIGN_ITERS):
        filtered = filter_forward(jnp.pad(density, window_reach), weights) / total_weight
        moduli = floor_modulus + (1.0 - floor_modulus) * filtered ** 3
        face_x = pad_axis(0.5 * (moduli[1:] + moduli[:-1]), 0, 1, 1)
        face_z = 0.5 * (moduli[:, 1:] + moduli[:, :-1])
        face_y = 0.5 * (moduli[:, :, 1:] + moduli[:, :, :-1])
        sum_x = face_x[:-1] + face_x[1:]
        sum_z = pad_axis(face_z, 1, 1, 0) + pad_axis(face_z, 1, 0, 1)
        sum_y = pad_axis(face_y, 2, 1, 0) + pad_axis(face_y, 2, 0, 1)
        diagonal = stiff_factors(0) * sum_x + stiff_factors(1) * sum_z + stiff_factors(2) * sum_y
        for sweep_index in range(SWEEPS):
            padded = pad_axis(displace, 2, 1, 1)
            displace = relax_sweep(padded, displace, face_x, face_z, face_y, force_field, free_cells, diagonal)
        energy_x = face_energy(pad_axis(displace, 2, 1, 1), 2, 0, LOADS) * face_valid[:, None, None]
        energy_z = face_energy(displace, 3, 1, LOADS)
        energy_y = face_energy(displace, 4, 2, LOADS)
        sensitive = 0.5 * (energy_x[:-1] + energy_x[1:] + pad_axis(energy_z, 1, 1, 0) + pad_axis(energy_z, 1, 0, 1) + pad_axis(energy_y, 2, 1, 0) + pad_axis(energy_y, 2, 0, 1))
        weighted_share = 3.0 * (1.0 - floor_modulus) * filtered ** 2 * sensitive / total_weight
        root_term = jnp.sqrt(filter_backward(jnp.pad(weighted_share, window_reach), padded_weights))
        lowest = jnp.maximum(density - move_limit, density_floor)
        highest = jnp.minimum(density + move_limit, 1.0)
        design_now = density

        def trial_design(log_level):
            return jnp.clip(design_now * root_term * jnp.exp(-0.5 * log_level), lowest, highest)

        def halve(search_step, search_state):
            lower_end, span_width = search_state
            half_span = span_width * 0.5
            middle = lower_end + half_span
            volume_total = jnp.sum(trial_design(middle))
            return (jnp.where(volume_total > target, middle, lower_end), half_span)
        start_state = (jnp.asarray(log_lower, jnp.float32), jnp.asarray(log_span, jnp.float32))
        lower_end, span_width = lax.fori_loop(0, SEARCH, halve, start_state)
        density = trial_design(lower_end + 0.5 * span_width)
    new_density = density
    new_displacement = pack_blocks(displace)
    return (new_density, new_displacement)
```

```python
import math

import jax
import jax.numpy as jnp
from jax import lax
from jax.experimental import pallas as pl
from jax.experimental.pallas import tpu as pltpu
from jax.sharding import PartitionSpec as P

SWEEPS = 3
SEARCH = 12


floor_modulus = 0.05
relax_factor = 0.6
move_limit = 0.2
density_floor = 0.01
volume_share = 0.5
log_lower = -16.0
log_span = 32.0
window_reach = 2

PLANE_SQUARES = (0, 1, 2, 4, 5, 8)
ALL_SQUARES = (0, 1, 2, 3, 4, 5, 6, 8, 9, 12)


def spot_iota(shape, dim):
    return lax.broadcasted_iota(jnp.int32, shape, dim)


def layer_radius(radius_ref, layers, row_width):
    z = spot_iota((layers, row_width), 0)
    result = jnp.zeros((layers, row_width), jnp.int32)
    for layer in range(layers):
        result = jnp.where(z == layer, radius_ref[layer], result)
    return result.astype(jnp.float32)


def class_weights(radius_ref, weight_ref):
    layers, row_width = weight_ref.shape[1:]
    radial = layer_radius(radius_ref, layers, row_width)
    for place, square in enumerate(ALL_SQUARES):
        weight_ref[place] = jnp.maximum(radial - math.sqrt(square), 0.0)


def shift_sum(field, dim, distance):
    size = field.shape[dim]
    spot = spot_iota(field.shape, dim)
    ahead = jnp.where(spot < size - distance, pltpu.roll(field, size - distance, dim), 0.0)
    behind = jnp.where(spot >= distance, pltpu.roll(field, distance, dim), 0.0)
    return ahead + behind


def plane_sums(plane):
    beside = shift_sum(plane, 1, 1)
    further = shift_sum(plane, 1, 2)
    return {
        0: plane,
        1: beside + shift_sum(plane, 0, 1),
        2: shift_sum(beside, 0, 1),
        4: further + shift_sum(plane, 0, 2),
        5: shift_sum(further, 0, 1) + shift_sum(beside, 0, 2),
        8: shift_sum(further, 0, 2),
    }


def weigh(sums, weight_ref, square):
    result = None
    for inner in PLANE_SQUARES:
        term = weight_ref[ALL_SQUARES.index(inner + square)] * sums[inner]
        result = term if result is None else result + term
    return result


def forward_planes(plane, weight_ref):
    sums = plane_sums(plane)
    return [weigh(sums, weight_ref, square) for square in (0, 1, 4)]


def backward_planes(plane, weight_ref):
    beside = shift_sum(plane, 1, 1)
    further = shift_sum(plane, 1, 2)
    results = []
    for square in (0, 1, 4):

        def weight(more):
            return weight_ref[ALL_SQUARES.index(square + more)]

        level = weight(0) * plane + weight(1) * beside + weight(4) * further
        near = weight(1) * plane + weight(2) * beside + weight(5) * further
        far = weight(4) * plane + weight(5) * beside + weight(8) * further
        results.append(level + shift_sum(near, 0, 1) + shift_sum(far, 0, 2))
    return results


def edge_class(x, planes):
    return jnp.minimum(x, 2) + jnp.maximum(x - (planes - 3), 0)


def zero_edges(ref):
    planes = ref.shape[0]
    for place in (0, 1, planes - 2, planes - 1):
        ref[place] = jnp.zeros(ref.shape[1:], ref.dtype)


def sweep_kernel(
    radius_ref,
    index_ref,
    force_ref,
    density_ref,
    fixed_ref,
    start_ref,
    disp_ref,
    sens_ref,
    coef_ref,
    weight_ref,
    total_ref,
    near_ref,
    side_ref,
    far_ref,
    modulus_ref,
    across_ref,
    up_ref,
    down_ref,
    right_ref,
    left_ref,
    rate_ref,
    keep_ref,
    first_ref,
    second_ref,
):
    planes, layers, row_width = density_ref.shape
    load_cases = index_ref.shape[0]
    load_place = lax.axis_index("space")
    shape = (layers, row_width)
    z = spot_iota(shape, 0)
    y = spot_iota(shape, 1)
    zero = jnp.zeros(shape, jnp.float32)

    class_weights(radius_ref, weight_ref)
    for ref in (side_ref, far_ref):
        zero_edges(ref)

    ones = forward_planes(jnp.ones(shape, jnp.float32), weight_ref)
    for place, (lower, upper) in enumerate(((0, 2), (1, 2), (2, 2), (2, 1), (2, 0))):
        total_ref[place] = (
            ones[0] + min(lower, 1) * ones[1] + min(upper, 1) * ones[1]
            + (lower // 2) * ones[2] + (upper // 2) * ones[2]
        )

    def filter_plane(x, carry):
        near, side, far = forward_planes(density_ref[x], weight_ref)
        near_ref[x + 2] = near
        side_ref[x + 2] = side
        far_ref[x + 2] = far
        return carry

    lax.fori_loop(0, planes, filter_plane, 0, unroll=2)

    def modulus_plane(x, carry):
        total = total_ref[edge_class(x, planes)]
        filtered = (
            near_ref[x + 2]
            + side_ref[x + 1]
            + side_ref[x + 3]
            + far_ref[x]
            + far_ref[x + 4]
        ) / total
        modulus = floor_modulus + (1.0 - floor_modulus) * (filtered * filtered * filtered)
        modulus_ref[x] = modulus
        coef_ref[x] = 3.0 * (1.0 - floor_modulus) * (filtered * filtered) / total
        return carry

    lax.fori_loop(0, planes, modulus_plane, 0, unroll=2)

    across_ref[0] = zero
    across_ref[planes] = zero
    first_ref[:, 0] = jnp.zeros((3,) + shape, jnp.float32)
    second_ref[:, 0] = jnp.zeros((3,) + shape, jnp.float32)
    first_ref[:, planes + 1] = jnp.zeros((3,) + shape, jnp.float32)
    second_ref[:, planes + 1] = jnp.zeros((3,) + shape, jnp.float32)

    def face_plane(x, carry):
        modulus = modulus_ref[x]
        later = modulus_ref[jnp.minimum(x + 1, planes - 1)]
        ahead = jnp.where(x + 1 < planes, 0.5 * (modulus + later), 0.0)
        across_ref[x + 1] = ahead
        up = jnp.where(z < layers - 1, 0.5 * (modulus + pltpu.roll(modulus, layers - 1, 0)), 0.0)
        down = pltpu.roll(up, 1, 0)
        right = jnp.where(
            y < row_width - 1, 0.5 * (modulus + pltpu.roll(modulus, row_width - 1, 1)), 0.0
        )
        left = pltpu.roll(right, 1, 1)
        up_ref[x] = up
        down_ref[x] = down
        right_ref[x] = right
        left_ref[x] = left
        free = jnp.where(z == 0, 1.0 - fixed_ref[pl.ds(x, 1), :].astype(jnp.float32), 1.0)
        keep_ref[x] = (1.0 - relax_factor) * free
        sums = (carry + ahead, up + down, left + right)
        every = sums[0] + sums[1] + sums[2]
        push = relax_factor * free
        for part in range(3):
            rate_ref[part, x] = push / (every + sums[part])
            first_ref[part, x + 1] = start_ref[part, x] * free
        return ahead

    lax.fori_loop(0, planes, face_plane, zero, unroll=2)

    own_index = index_ref[load_place]
    own_x = own_index // (layers * row_width)
    own_z = own_index // row_width % layers
    own_y = own_index % row_width
    hit = (z == own_z) & (y == own_y)

    def sweep(source, target, lead):
        def sweep_plane(x, carry):
            before, after = across_ref[x], across_ref[x + 1]
            up, down, right, left = up_ref[x], down_ref[x], right_ref[x], left_ref[x]
            keep = keep_ref[x]
            for part in range(3):
                here = source[part, x + 1]
                pulls = [
                    before * source[part, x] + after * source[part, x + 2],
                    up * pltpu.roll(here, layers - 1, 0) + down * pltpu.roll(here, 1, 0),
                    right * pltpu.roll(here, row_width - 1, 1) + left * pltpu.roll(here, 1, 1),
                ]
                pull = pulls[0] + pulls[1] + pulls[2] + pulls[part]
                target[part, x + lead] = keep * here + rate_ref[part, x] * pull
            return carry

        lax.fori_loop(0, planes, sweep_plane, 0, unroll=2)
        for part in range(3):
            push = rate_ref[part, own_x] * force_ref[load_place, part]
            target[part, own_x + lead] += jnp.where(hit, push, 0.0)

    stages = [first_ref, second_ref]
    for turn in range(SWEEPS - 1):
        sweep(stages[turn % 2], stages[(turn + 1) % 2], 1)
    sweep(stages[(SWEEPS - 1) % 2], disp_ref, 0)

    def energy_plane(x, carry):
        later = jnp.minimum(x + 1, planes - 1)
        ahead, upward, right = zero, zero, zero
        for part in range(3):
            here = disp_ref[part, x]
            step = disp_ref[part, later] - here
            climb = pltpu.roll(here, layers - 1, 0) - here
            slide = pltpu.roll(here, row_width - 1, 1) - here
            ahead = ahead + (2.0 if part == 0 else 1.0) * (step * step)
            upward = upward + (2.0 if part == 1 else 1.0) * (climb * climb)
            right = right + (2.0 if part == 2 else 1.0) * (slide * slide)
        upward = jnp.where(z < layers - 1, upward, 0.0)
        right = jnp.where(y < row_width - 1, right, 0.0)
        total = carry + ahead + upward + pltpu.roll(upward, 1, 0) + right + pltpu.roll(right, 1, 1)
        sens_ref[x] = (0.5 / load_cases) * total
        return ahead

    lax.fori_loop(0, planes, energy_plane, zero, unroll=2)


def design_kernel(
    radius_ref,
    sens_ref,
    coef_ref,
    density_ref,
    new_ref,
    weight_ref,
    near_ref,
    side_ref,
    far_ref,
    pull_ref,
    low_ref,
    high_ref,
):
    planes, layers, row_width = density_ref.shape
    own_planes = new_ref.shape[0]
    place = lax.axis_index("space")
    shape = (layers, row_width)
    zero = jnp.zeros(shape, jnp.float32)
    class_weights(radius_ref, weight_ref)
    for ref in (side_ref, far_ref):
        zero_edges(ref)

    def filter_plane(x, carry):
        near, side, far = backward_planes(sens_ref[x] * coef_ref[x], weight_ref)
        near_ref[x + 2] = near
        side_ref[x + 2] = side
        far_ref[x + 2] = far
        return carry

    lax.fori_loop(0, planes, filter_plane, 0, unroll=2)

    def root_plane(x, carry):
        root = jnp.sqrt(
            near_ref[x + 2] + side_ref[x + 1] + side_ref[x + 3] + far_ref[x] + far_ref[x + 4]
        )
        density = density_ref[x]
        pull_ref[x] = density * root
        low_ref[x] = jnp.maximum(density - move_limit, density_floor)
        high_ref[x] = jnp.minimum(density + move_limit, 1.0)
        return carry

    lax.fori_loop(0, planes, root_plane, 0, unroll=2)

    target = volume_share * planes * layers * row_width

    def trial(x, factor):
        return jnp.minimum(jnp.maximum(pull_ref[x] * factor, low_ref[x]), high_ref[x])

    def halve(step, state):
        lower, span = state
        half = span * 0.5
        middle = lower + half
        factor = jnp.exp(-0.5 * middle)
        total = lax.fori_loop(
            0, planes, lambda x, acc: acc + trial(x, factor), zero, unroll=8
        )
        volume = jnp.sum(jnp.sum(total, axis=0, keepdims=True), axis=1, keepdims=True)
        return jnp.where(volume > target, middle, lower), half

    start = (jnp.full((1, 1), log_lower, jnp.float32), jnp.full((1, 1), log_span, jnp.float32))
    lower, span = lax.fori_loop(0, SEARCH, halve, start)
    factor = jnp.exp(-0.5 * (lower + 0.5 * span))
    for own in range(own_planes):
        new_ref[own] = trial(place * own_planes + own, factor)


def in_vmem():
    return pl.BlockSpec(memory_space=pltpu.VMEM)


def in_smem():
    return pl.BlockSpec(memory_space=pltpu.SMEM)


KERNEL_VMEM = 24 * 2**20


def sweep_call(radius, load_index, load_force, density, fixed, displacement):
    planes, layers, row_width = density.shape
    grid_field = (planes, layers, row_width)

    def scratch(*lead):
        return pltpu.VMEM(lead + (layers, row_width), jnp.float32)

    return pl.pallas_call(
        sweep_kernel,
        out_shape=[
            jax.ShapeDtypeStruct((3,) + grid_field, jnp.float32),
            jax.ShapeDtypeStruct(grid_field, jnp.float32),
            jax.ShapeDtypeStruct(grid_field, jnp.float32),
        ],
        in_specs=[in_smem()] * 3 + [in_vmem()] * 3,
        out_specs=[in_vmem()] * 3,
        scratch_shapes=[
            scratch(len(ALL_SQUARES)),
            scratch(2 * window_reach + 1),
            scratch(planes + 4),
            scratch(planes + 4),
            scratch(planes + 4),
            scratch(planes),
            scratch(planes + 1),
            scratch(planes),
            scratch(planes),
            scratch(planes),
            scratch(planes),
            scratch(3, planes),
            scratch(planes),
            scratch(3, planes + 2),
            scratch(3, planes + 2),
        ],
        compiler_params=pltpu.CompilerParams(vmem_limit_bytes=KERNEL_VMEM),
        name="sweeps",
    )(radius, load_index, load_force, density, fixed, displacement)


def design_call(radius, sens, coef, density, own_planes):
    planes, layers, row_width = density.shape

    def scratch(*lead):
        return pltpu.VMEM(lead + (layers, row_width), jnp.float32)

    return pl.pallas_call(
        design_kernel,
        out_shape=jax.ShapeDtypeStruct((own_planes, layers, row_width), jnp.float32),
        in_specs=[in_smem()] + [in_vmem()] * 3,
        out_specs=in_vmem(),
        scratch_shapes=[
            scratch(len(ALL_SQUARES)),
            scratch(planes + 4),
            scratch(planes + 4),
            scratch(planes + 4),
            scratch(planes),
            scratch(planes),
            scratch(planes),
        ],
        compiler_params=pltpu.CompilerParams(vmem_limit_bytes=KERNEL_VMEM),
        name="design",
    )(radius, sens, coef, density)


def gathered(block):
    return lax.all_gather(block, "space", axis=0, tiled=True)


def scattered_sum(field):
    devices = lax.axis_size("space")
    pieces = field.reshape((devices, field.shape[0] // devices) + field.shape[1:])
    return jnp.sum(lax.all_to_all(pieces, "space", 0, 0), axis=0)


def one_slab(density, displacement, fixed, load_index, load_force, radius):
    whole = gathered(density)
    new_displacement, sens, coef = sweep_call(
        radius, load_index, load_force, whole, fixed, displacement[0]
    )
    sens = gathered(scattered_sum(sens))
    new_density = design_call(radius, sens, coef, whole, density.shape[0])
    return new_density, new_displacement[None]


def from_behind(block, axis, distance):
    devices = range(lax.axis_size(axis))
    route = [(i - distance, i) for i in devices if i - distance in devices]
    return lax.ppermute(block, axis, route)


def extended(x, sides, width):
    for axis, dim in sides:
        size, length = (lax.axis_size(axis), x.shape[dim])
        up = [(i, (i + 1) % size) for i in range(size - 1)]
        down = [(j, i) for i, j in up]
        last = lax.slice_in_dim(x, length - width, length, axis=dim)
        first = lax.slice_in_dim(x, 0, width, axis=dim)
        before = lax.ppermute(last, axis, up)
        after = lax.ppermute(first, axis, down)
        x = jnp.concatenate([before, x, after], axis=dim)
    return x


def from_partner(x, axis, bit):
    return lax.ppermute(x, axis, [(i, i ^ 1 << bit) for i in range(lax.axis_size(axis))])


def window_offsets():
    offsets_list = []
    for across in range(-window_reach, window_reach + 1):
        for upward in range(-window_reach, window_reach + 1):
            for sideways in range(-window_reach, window_reach + 1):
                length = math.sqrt(across * across + upward * upward + sideways * sideways)
                offsets_list.append((across, upward, sideways, length))
    return offsets_list


def layer_weights(radius):
    radial = radius.astype(jnp.float32)
    return jnp.stack(
        [jnp.maximum(radial - length, 0.0) for across, upward, sideways, length in window_offsets()]
    )


def pad_axis(grid_field, along_axis, before, after_cells):
    widths = [(0, 0)] * grid_field.ndim
    widths[along_axis] = (before, after_cells)
    return jnp.pad(grid_field, widths)


def pad_sides(grid_field):
    return jnp.pad(grid_field, ((0, 0), (window_reach, window_reach), (window_reach, window_reach)))


def filter_forward(padded, weights):
    out_rows = padded.shape[0] - 2 * window_reach
    layers = padded.shape[1] - 2 * window_reach
    row_width = padded.shape[2] - 2 * window_reach
    result = jnp.zeros((out_rows, layers, row_width), jnp.float32)
    for offset_index, (across, upward, sideways, length) in enumerate(window_offsets()):
        shifted = padded[
            window_reach + across : window_reach + across + out_rows,
            window_reach + upward : window_reach + upward + layers,
            window_reach + sideways : window_reach + sideways + row_width,
        ]
        result = result + weights[offset_index][None, :, None] * shifted
    return result


def filter_backward(padded, padded_weights):
    out_rows = padded.shape[0] - 2 * window_reach
    layers = padded.shape[1] - 2 * window_reach
    row_width = padded.shape[2] - 2 * window_reach
    result = jnp.zeros((out_rows, layers, row_width), jnp.float32)
    for offset_index, (across, upward, sideways, length) in enumerate(window_offsets()):
        shifted = padded[
            window_reach - across : window_reach - across + out_rows,
            window_reach - upward : window_reach - upward + layers,
            window_reach - sideways : window_reach - sideways + row_width,
        ]
        layer_part = padded_weights[
            offset_index, window_reach - upward : window_reach - upward + layers
        ]
        result = result + layer_part[None, :, None] * shifted
    return result


def stiff_factors(direction):
    return jnp.array(
        [2.0 if component == direction else 1.0 for component in range(3)], jnp.float32
    ).reshape(3, 1, 1, 1)


def relax_slab(padded, displace, face_x, face_z, face_y, force_field, free_cells, diagonal):
    flux_x = stiff_factors(0) * face_x * jnp.diff(padded, axis=1)
    stencil_image = flux_x[:, :-1] - flux_x[:, 1:]
    flux_z = stiff_factors(1) * face_z * jnp.diff(displace, axis=2)
    stencil_image = stencil_image + pad_axis(flux_z, 2, 1, 0) - pad_axis(flux_z, 2, 0, 1)
    flux_y = stiff_factors(2) * face_y * jnp.diff(displace, axis=3)
    stencil_image = stencil_image + pad_axis(flux_y, 3, 1, 0) - pad_axis(flux_y, 3, 0, 1)
    return free_cells * (displace + relax_factor * (force_field - stencil_image) / diagonal)


def slab_energy(grid_field, along_axis, direction, load_cases):
    change = jnp.diff(grid_field, axis=along_axis)
    return jnp.sum(stiff_factors(direction) * change * change, axis=0) / load_cases


def neighbour_planes(displace, load_cases, axis_devices):
    if axis_devices > load_cases:
        below = from_behind(displace[:, -1:], "space", load_cases)
        above = from_behind(displace[:, :1], "space", -load_cases)
    else:
        below = jnp.zeros_like(displace[:, :1])
        above = jnp.zeros_like(displace[:, :1])
    return jnp.concatenate([below, displace, above], axis=1)


def many_slabs(density, displacement, fixed, load_index, load_force, radius):
    slab_rows, layers, row_width = density.shape
    load_cases = load_index.shape[0]
    level_count = load_cases.bit_length() - 1
    axis_devices = lax.axis_size("space")
    axis_place = lax.axis_index("space")
    slab_planes = slab_rows * load_cases
    slab_place = axis_place // load_cases
    load_place = axis_place % load_cases
    total_rows = slab_rows * axis_devices
    weights = layer_weights(radius)
    padded_weights = pad_axis(weights, 1, window_reach, window_reach)
    global_rows = (
        jnp.arange(slab_rows + 2 * window_reach, dtype=jnp.int32)
        + axis_place * slab_rows
        - window_reach
    )
    deep_inside = ((global_rows >= 0) & (global_rows < total_rows)).astype(jnp.float32)
    inside_field = deep_inside[:, None, None] * pad_sides(
        jnp.ones((slab_rows + 2 * window_reach, layers, row_width), jnp.float32)
    )
    total_weight = filter_forward(inside_field, weights)
    slab_start = slab_place * slab_planes
    margin_rows = jnp.arange(slab_planes + 2, dtype=jnp.int32) + slab_start - 1
    margin_inside = ((margin_rows >= 0) & (margin_rows < total_rows)).astype(jnp.float32)
    face_valid = margin_inside[1:] * margin_inside[:-1]
    fixed_slab = lax.dynamic_slice_in_dim(fixed, slab_start, slab_planes, 0).astype(jnp.float32)
    bottom_layer = (jnp.arange(layers, dtype=jnp.int32) == 0).astype(jnp.float32)
    free_cells = 1.0 - bottom_layer[None, :, None] * fixed_slab[:, None, :]
    slab_cells = slab_planes * layers * row_width
    cell_index = jnp.arange(slab_cells, dtype=jnp.int32) + slab_place * slab_cells
    load_hot = jnp.arange(load_cases, dtype=jnp.int32) == load_place
    own_index = jnp.sum(jnp.where(load_hot, load_index, 0))
    own_force = jnp.sum(load_hot.astype(jnp.float32)[:, None] * load_force, axis=0)
    load_hits = (cell_index == own_index).astype(jnp.float32)
    force_field = (own_force[:, None] * load_hits[None, :]).reshape(
        3, slab_planes, layers, row_width
    )
    displace = displacement[0] * free_cells
    target = volume_share * total_rows * layers * row_width
    padded = neighbour_planes(displace, load_cases, axis_devices)
    halo_density = extended(density, (("space", 0),), window_reach)
    filtered = filter_forward(pad_sides(halo_density), weights) / total_weight
    whole_field = lax.all_gather(filtered, "space", axis=0, tiled=True)
    margin = lax.dynamic_slice_in_dim(
        pad_axis(whole_field, 0, 1, 1), slab_start, slab_planes + 2, 0
    )
    moduli = floor_modulus + (1.0 - floor_modulus) * margin**3
    face_x = 0.5 * (moduli[1:] + moduli[:-1]) * face_valid[:, None, None]
    inner_moduli = moduli[1:-1]
    face_z = 0.5 * (inner_moduli[:, 1:] + inner_moduli[:, :-1])
    face_y = 0.5 * (inner_moduli[:, :, 1:] + inner_moduli[:, :, :-1])
    sum_x = face_x[:-1] + face_x[1:]
    sum_z = pad_axis(face_z, 1, 1, 0) + pad_axis(face_z, 1, 0, 1)
    sum_y = pad_axis(face_y, 2, 1, 0) + pad_axis(face_y, 2, 0, 1)
    diagonal = stiff_factors(0) * sum_x + stiff_factors(1) * sum_z + stiff_factors(2) * sum_y
    for sweep_index in range(SWEEPS):
        displace = relax_slab(
            padded, displace, face_x, face_z, face_y, force_field, free_cells, diagonal
        )
        padded = neighbour_planes(displace, load_cases, axis_devices)
    energy_x = slab_energy(padded, 1, 0, load_cases) * face_valid[:, None, None]
    energy_z = slab_energy(displace, 2, 1, load_cases)
    energy_y = slab_energy(displace, 3, 2, load_cases)
    sens_term = 0.5 * (
        energy_x[:-1]
        + energy_x[1:]
        + pad_axis(energy_z, 1, 1, 0)
        + pad_axis(energy_z, 1, 0, 1)
        + pad_axis(energy_y, 2, 1, 0)
        + pad_axis(energy_y, 2, 0, 1)
    )
    sensitive = sens_term
    for level in reversed(range(level_count)):
        half_rows = sensitive.shape[0] // 2
        upper_side = load_place // 2**level % 2 == 1
        outgoing = jnp.where(upper_side, sensitive[:half_rows], sensitive[half_rows:])
        keeping = jnp.where(upper_side, sensitive[half_rows:], sensitive[:half_rows])
        sensitive = keeping + from_partner(outgoing, "space", level)
    weighted_share = 3.0 * (1.0 - floor_modulus) * filtered**2 * sensitive / total_weight
    halo_share = extended(weighted_share, (("space", 0),), window_reach)
    root_term = jnp.sqrt(filter_backward(pad_sides(halo_share), padded_weights))
    lowest = jnp.maximum(density - move_limit, density_floor)
    highest = jnp.minimum(density + move_limit, 1.0)
    design_now = density

    def trial_design(log_level):
        return jnp.clip(design_now * root_term * jnp.exp(-0.5 * log_level), lowest, highest)

    start_state = (jnp.asarray(log_lower, jnp.float32), jnp.asarray(log_span, jnp.float32))

    def halve(search_step, search_state):
        lower_end, span_width = search_state
        half_span = span_width * 0.5
        middle = lower_end + half_span
        volume_total = lax.psum(jnp.sum(trial_design(middle)), "space")
        return (jnp.where(volume_total > target, middle, lower_end), half_span)

    lower_end, span_width = lax.fori_loop(0, SEARCH, halve, start_state)
    density = trial_design(lower_end + 0.5 * span_width)
    new_displacement = displace[None]
    return (density, new_displacement)


def solution(mesh):
    in_specs = (
        P("space", "parts", None),
        P("space", None, None, "parts", None),
        P(None, "parts"),
        P("parts"),
        P("parts", None),
        P("parts"),
    )
    out_specs = (P("space", "parts", None), P("space", None, None, "parts", None))

    def local(density, displacement, fixed, load_index, load_force, radius):
        alone = lax.axis_size("space") == load_index.shape[0]
        run = one_slab if alone else many_slabs
        return run(density, displacement, fixed, load_index, load_force, radius)

    return jax.shard_map(local, mesh=mesh, in_specs=in_specs, out_specs=out_specs, check_vma=False)
```

```python
import math

import jax
import jax.numpy as jnp
from jax import lax
from jax.experimental import pallas as pl
from jax.experimental.pallas import tpu as pltpu
from jax.sharding import PartitionSpec as P

SWEEPS = 3
SEARCH = 12


floor_modulus = 0.05
relax_factor = 0.6
move_limit = 0.2
density_floor = 0.01
volume_share = 0.5
log_lower = -16.0
log_span = 32.0
window_reach = 2

PLANE_SQUARES = (0, 1, 2, 4, 5, 8)
ALL_SQUARES = (0, 1, 2, 3, 4, 5, 6, 8, 9, 12)


def spot_iota(shape, dim):
    return lax.broadcasted_iota(jnp.int32, shape, dim)


def layer_radius(radius_ref, layers, row_width):
    z = spot_iota((layers, row_width), 0)
    result = jnp.zeros((layers, row_width), jnp.int32)
    for layer in range(layers):
        result = jnp.where(z == layer, radius_ref[layer], result)
    return result.astype(jnp.float32)


def class_weights(radius_ref, weight_ref):
    layers, row_width = weight_ref.shape[1:]
    radial = layer_radius(radius_ref, layers, row_width)
    for place, square in enumerate(ALL_SQUARES):
        weight_ref[place] = jnp.maximum(radial - math.sqrt(square), 0.0)


def shift_sum(field, dim, distance):
    size = field.shape[dim]
    spot = spot_iota(field.shape, dim)
    ahead = jnp.where(spot < size - distance, pltpu.roll(field, size - distance, dim), 0.0)
    behind = jnp.where(spot >= distance, pltpu.roll(field, distance, dim), 0.0)
    return ahead + behind


def plane_sums(plane):
    beside = shift_sum(plane, 1, 1)
    further = shift_sum(plane, 1, 2)
    return {
        0: plane,
        1: beside + shift_sum(plane, 0, 1),
        2: shift_sum(beside, 0, 1),
        4: further + shift_sum(plane, 0, 2),
        5: shift_sum(further, 0, 1) + shift_sum(beside, 0, 2),
        8: shift_sum(further, 0, 2),
    }


def weigh(sums, weight_ref, square):
    result = None
    for inner in PLANE_SQUARES:
        term = weight_ref[ALL_SQUARES.index(inner + square)] * sums[inner]
        result = term if result is None else result + term
    return result


def forward_planes(plane, weight_ref):
    sums = plane_sums(plane)
    return [weigh(sums, weight_ref, square) for square in (0, 1, 4)]


def backward_planes(plane, weight_ref):
    beside = shift_sum(plane, 1, 1)
    further = shift_sum(plane, 1, 2)
    results = []
    for square in (0, 1, 4):

        def weight(more):
            return weight_ref[ALL_SQUARES.index(square + more)]

        level = weight(0) * plane + weight(1) * beside + weight(4) * further
        near = weight(1) * plane + weight(2) * beside + weight(5) * further
        far = weight(4) * plane + weight(5) * beside + weight(8) * further
        results.append(level + shift_sum(near, 0, 1) + shift_sum(far, 0, 2))
    return results


def edge_class(x, planes):
    return jnp.minimum(x, 2) + jnp.maximum(x - (planes - 3), 0)


def zero_edges(ref):
    planes = ref.shape[0]
    for place in (0, 1, planes - 2, planes - 1):
        ref[place] = jnp.zeros(ref.shape[1:], ref.dtype)


def sweep_kernel(
    radius_ref,
    index_ref,
    force_ref,
    density_ref,
    fixed_ref,
    start_ref,
    disp_ref,
    sens_ref,
    coef_ref,
    weight_ref,
    total_ref,
    near_ref,
    side_ref,
    far_ref,
    modulus_ref,
    across_ref,
    up_ref,
    down_ref,
    right_ref,
    left_ref,
    rate_ref,
    keep_ref,
    first_ref,
    second_ref,
):
    planes, layers, row_width = density_ref.shape
    load_cases = index_ref.shape[0]
    load_place = lax.axis_index("space")
    shape = (layers, row_width)
    z = spot_iota(shape, 0)
    y = spot_iota(shape, 1)
    zero = jnp.zeros(shape, jnp.float32)

    class_weights(radius_ref, weight_ref)
    for ref in (side_ref, far_ref):
        zero_edges(ref)

    ones = forward_planes(jnp.ones(shape, jnp.float32), weight_ref)
    for place, (lower, upper) in enumerate(((0, 2), (1, 2), (2, 2), (2, 1), (2, 0))):
        total_ref[place] = (
            ones[0] + min(lower, 1) * ones[1] + min(upper, 1) * ones[1]
            + (lower // 2) * ones[2] + (upper // 2) * ones[2]
        )

    def filter_plane(x, carry):
        near, side, far = forward_planes(density_ref[x], weight_ref)
        near_ref[x + 2] = near
        side_ref[x + 2] = side
        far_ref[x + 2] = far
        return carry

    lax.fori_loop(0, planes, filter_plane, 0, unroll=2)

    def modulus_plane(x, carry):
        total = total_ref[edge_class(x, planes)]
        filtered = (
            near_ref[x + 2]
            + side_ref[x + 1]
            + side_ref[x + 3]
            + far_ref[x]
            + far_ref[x + 4]
        ) / total
        modulus = floor_modulus + (1.0 - floor_modulus) * (filtered * filtered * filtered)
        modulus_ref[x] = modulus
        coef_ref[x] = 3.0 * (1.0 - floor_modulus) * (filtered * filtered) / total
        return carry

    lax.fori_loop(0, planes, modulus_plane, 0, unroll=2)

    across_ref[0] = zero
    across_ref[planes] = zero
    first_ref[:, 0] = jnp.zeros((3,) + shape, jnp.float32)
    second_ref[:, 0] = jnp.zeros((3,) + shape, jnp.float32)
    first_ref[:, planes + 1] = jnp.zeros((3,) + shape, jnp.float32)
    second_ref[:, planes + 1] = jnp.zeros((3,) + shape, jnp.float32)

    def face_plane(x, carry):
        modulus = modulus_ref[x]
        later = modulus_ref[jnp.minimum(x + 1, planes - 1)]
        ahead = jnp.where(x + 1 < planes, 0.5 * (modulus + later), 0.0)
        across_ref[x + 1] = ahead
        up = jnp.where(z < layers - 1, 0.5 * (modulus + pltpu.roll(modulus, layers - 1, 0)), 0.0)
        down = pltpu.roll(up, 1, 0)
        right = jnp.where(
            y < row_width - 1, 0.5 * (modulus + pltpu.roll(modulus, row_width - 1, 1)), 0.0
        )
        left = pltpu.roll(right, 1, 1)
        up_ref[x] = up
        down_ref[x] = down
        right_ref[x] = right
        left_ref[x] = left
        free = jnp.where(z == 0, 1.0 - fixed_ref[pl.ds(x, 1), :].astype(jnp.float32), 1.0)
        keep_ref[x] = (1.0 - relax_factor) * free
        sums = (carry + ahead, up + down, left + right)
        every = sums[0] + sums[1] + sums[2]
        push = relax_factor * free
        for part in range(3):
            rate_ref[part, x] = push / (every + sums[part])
            first_ref[part, x + 1] = start_ref[part, x] * free
        return ahead

    lax.fori_loop(0, planes, face_plane, zero, unroll=2)

    own_index = index_ref[load_place]
    own_x = own_index // (layers * row_width)
    own_z = own_index // row_width % layers
    own_y = own_index % row_width
    hit = (z == own_z) & (y == own_y)

    def sweep(source, target, lead):
        def sweep_plane(x, carry):
            before, after = across_ref[x], across_ref[x + 1]
            up, down, right, left = up_ref[x], down_ref[x], right_ref[x], left_ref[x]
            keep = keep_ref[x]
            for part in range(3):
                here = source[part, x + 1]
                pulls = [
                    before * source[part, x] + after * source[part, x + 2],
                    up * pltpu.roll(here, layers - 1, 0) + down * pltpu.roll(here, 1, 0),
                    right * pltpu.roll(here, row_width - 1, 1) + left * pltpu.roll(here, 1, 1),
                ]
                pull = pulls[0] + pulls[1] + pulls[2] + pulls[part]
                target[part, x + lead] = keep * here + rate_ref[part, x] * pull
            return carry

        lax.fori_loop(0, planes, sweep_plane, 0, unroll=2)
        for part in range(3):
            push = rate_ref[part, own_x] * force_ref[load_place, part]
            target[part, own_x + lead] += jnp.where(hit, push, 0.0)

    stages = [first_ref, second_ref]
    for turn in range(SWEEPS - 1):
        sweep(stages[turn % 2], stages[(turn + 1) % 2], 1)
    sweep(stages[(SWEEPS - 1) % 2], disp_ref, 0)

    def energy_plane(x, carry):
        later = jnp.minimum(x + 1, planes - 1)
        ahead, upward, right = zero, zero, zero
        for part in range(3):
            here = disp_ref[part, x]
            step = disp_ref[part, later] - here
            climb = pltpu.roll(here, layers - 1, 0) - here
            slide = pltpu.roll(here, row_width - 1, 1) - here
            ahead = ahead + (2.0 if part == 0 else 1.0) * (step * step)
            upward = upward + (2.0 if part == 1 else 1.0) * (climb * climb)
            right = right + (2.0 if part == 2 else 1.0) * (slide * slide)
        upward = jnp.where(z < layers - 1, upward, 0.0)
        right = jnp.where(y < row_width - 1, right, 0.0)
        total = carry + ahead + upward + pltpu.roll(upward, 1, 0) + right + pltpu.roll(right, 1, 1)
        sens_ref[x] = (0.5 / load_cases) * total
        return ahead

    lax.fori_loop(0, planes, energy_plane, zero, unroll=2)


def design_kernel(
    radius_ref,
    sens_ref,
    coef_ref,
    density_ref,
    new_ref,
    weight_ref,
    near_ref,
    side_ref,
    far_ref,
    pull_ref,
    low_ref,
    high_ref,
):
    planes, layers, row_width = density_ref.shape
    own_planes = new_ref.shape[0]
    place = lax.axis_index("space")
    shape = (layers, row_width)
    zero = jnp.zeros(shape, jnp.float32)
    class_weights(radius_ref, weight_ref)
    for ref in (side_ref, far_ref):
        zero_edges(ref)

    def filter_plane(x, carry):
        near, side, far = backward_planes(sens_ref[x] * coef_ref[x], weight_ref)
        near_ref[x + 2] = near
        side_ref[x + 2] = side
        far_ref[x + 2] = far
        return carry

    lax.fori_loop(0, planes, filter_plane, 0, unroll=2)

    def root_plane(x, carry):
        root = jnp.sqrt(
            near_ref[x + 2] + side_ref[x + 1] + side_ref[x + 3] + far_ref[x] + far_ref[x + 4]
        )
        density = density_ref[x]
        pull_ref[x] = density * root
        low_ref[x] = jnp.maximum(density - move_limit, density_floor)
        high_ref[x] = jnp.minimum(density + move_limit, 1.0)
        return carry

    lax.fori_loop(0, planes, root_plane, 0, unroll=2)

    target = volume_share * planes * layers * row_width

    def trial(x, factor):
        return jnp.minimum(jnp.maximum(pull_ref[x] * factor, low_ref[x]), high_ref[x])

    def halve(step, state):
        lower, span = state
        half = span * 0.5
        middle = lower + half
        factor = jnp.exp(-0.5 * middle)
        total = lax.fori_loop(
            0, planes, lambda x, acc: acc + trial(x, factor), zero, unroll=8
        )
        volume = jnp.sum(jnp.sum(total, axis=0, keepdims=True), axis=1, keepdims=True)
        return jnp.where(volume > target, middle, lower), half

    start = (jnp.full((1, 1), log_lower, jnp.float32), jnp.full((1, 1), log_span, jnp.float32))
    lower, span = lax.fori_loop(0, SEARCH, halve, start)
    factor = jnp.exp(-0.5 * (lower + 0.5 * span))
    for own in range(own_planes):
        new_ref[own] = trial(place * own_planes + own, factor)


def in_vmem():
    return pl.BlockSpec(memory_space=pltpu.VMEM)


def in_smem():
    return pl.BlockSpec(memory_space=pltpu.SMEM)


KERNEL_VMEM = 24 * 2**20


def sweep_call(radius, load_index, load_force, density, fixed, displacement):
    planes, layers, row_width = density.shape
    grid_field = (planes, layers, row_width)

    def scratch(*lead):
        return pltpu.VMEM(lead + (layers, row_width), jnp.float32)

    return pl.pallas_call(
        sweep_kernel,
        out_shape=[
            jax.ShapeDtypeStruct((3,) + grid_field, jnp.float32),
            jax.ShapeDtypeStruct(grid_field, jnp.float32),
            jax.ShapeDtypeStruct(grid_field, jnp.float32),
        ],
        in_specs=[in_smem()] * 3 + [in_vmem()] * 3,
        out_specs=[in_vmem()] * 3,
        scratch_shapes=[
            scratch(len(ALL_SQUARES)),
            scratch(2 * window_reach + 1),
            scratch(planes + 4),
            scratch(planes + 4),
            scratch(planes + 4),
            scratch(planes),
            scratch(planes + 1),
            scratch(planes),
            scratch(planes),
            scratch(planes),
            scratch(planes),
            scratch(3, planes),
            scratch(planes),
            scratch(3, planes + 2),
            scratch(3, planes + 2),
        ],
        compiler_params=pltpu.CompilerParams(vmem_limit_bytes=KERNEL_VMEM),
        name="sweeps",
    )(radius, load_index, load_force, density, fixed, displacement)


def design_call(radius, sens, coef, density, own_planes):
    planes, layers, row_width = density.shape

    def scratch(*lead):
        return pltpu.VMEM(lead + (layers, row_width), jnp.float32)

    return pl.pallas_call(
        design_kernel,
        out_shape=jax.ShapeDtypeStruct((own_planes, layers, row_width), jnp.float32),
        in_specs=[in_smem()] + [in_vmem()] * 3,
        out_specs=in_vmem(),
        scratch_shapes=[
            scratch(len(ALL_SQUARES)),
            scratch(planes + 4),
            scratch(planes + 4),
            scratch(planes + 4),
            scratch(planes),
            scratch(planes),
            scratch(planes),
        ],
        compiler_params=pltpu.CompilerParams(vmem_limit_bytes=KERNEL_VMEM),
        name="design",
    )(radius, sens, coef, density)


def gathered(block):
    devices = lax.axis_size("space")
    copies = jnp.broadcast_to(block[None], (devices,) + block.shape)
    blocks = lax.all_to_all(copies, "space", 0, 0)
    return blocks.reshape((devices * block.shape[0],) + block.shape[1:])


def scattered_sum(field):
    devices = lax.axis_size("space")
    pieces = field.reshape((devices, field.shape[0] // devices) + field.shape[1:])
    return jnp.sum(lax.all_to_all(pieces, "space", 0, 0), axis=0)


def one_slab(density, displacement, fixed, load_index, load_force, radius):
    whole = gathered(density)
    new_displacement, sens, coef = sweep_call(
        radius, load_index, load_force, whole, fixed, displacement[0]
    )
    sens = gathered(scattered_sum(sens))
    new_density = design_call(radius, sens, coef, whole, density.shape[0])
    return new_density, new_displacement[None]


def from_behind(block, axis, distance):
    devices = range(lax.axis_size(axis))
    route = [(i - distance, i) for i in devices if i - distance in devices]
    return lax.ppermute(block, axis, route)


def extended(x, sides, width):
    for axis, dim in sides:
        size, length = (lax.axis_size(axis), x.shape[dim])
        up = [(i, (i + 1) % size) for i in range(size - 1)]
        down = [(j, i) for i, j in up]
        last = lax.slice_in_dim(x, length - width, length, axis=dim)
        first = lax.slice_in_dim(x, 0, width, axis=dim)
        before = lax.ppermute(last, axis, up)
        after = lax.ppermute(first, axis, down)
        x = jnp.concatenate([before, x, after], axis=dim)
    return x


def from_partner(x, axis, bit):
    return lax.ppermute(x, axis, [(i, i ^ 1 << bit) for i in range(lax.axis_size(axis))])


def window_offsets():
    offsets_list = []
    for across in range(-window_reach, window_reach + 1):
        for upward in range(-window_reach, window_reach + 1):
            for sideways in range(-window_reach, window_reach + 1):
                length = math.sqrt(across * across + upward * upward + sideways * sideways)
                offsets_list.append((across, upward, sideways, length))
    return offsets_list


def layer_weights(radius):
    radial = radius.astype(jnp.float32)
    return jnp.stack(
        [jnp.maximum(radial - length, 0.0) for across, upward, sideways, length in window_offsets()]
    )


def pad_axis(grid_field, along_axis, before, after_cells):
    widths = [(0, 0)] * grid_field.ndim
    widths[along_axis] = (before, after_cells)
    return jnp.pad(grid_field, widths)


def pad_sides(grid_field):
    return jnp.pad(grid_field, ((0, 0), (window_reach, window_reach), (window_reach, window_reach)))


def filter_forward(padded, weights):
    out_rows = padded.shape[0] - 2 * window_reach
    layers = padded.shape[1] - 2 * window_reach
    row_width = padded.shape[2] - 2 * window_reach
    result = jnp.zeros((out_rows, layers, row_width), jnp.float32)
    for offset_index, (across, upward, sideways, length) in enumerate(window_offsets()):
        shifted = padded[
            window_reach + across : window_reach + across + out_rows,
            window_reach + upward : window_reach + upward + layers,
            window_reach + sideways : window_reach + sideways + row_width,
        ]
        result = result + weights[offset_index][None, :, None] * shifted
    return result


def filter_backward(padded, padded_weights):
    out_rows = padded.shape[0] - 2 * window_reach
    layers = padded.shape[1] - 2 * window_reach
    row_width = padded.shape[2] - 2 * window_reach
    result = jnp.zeros((out_rows, layers, row_width), jnp.float32)
    for offset_index, (across, upward, sideways, length) in enumerate(window_offsets()):
        shifted = padded[
            window_reach - across : window_reach - across + out_rows,
            window_reach - upward : window_reach - upward + layers,
            window_reach - sideways : window_reach - sideways + row_width,
        ]
        layer_part = padded_weights[
            offset_index, window_reach - upward : window_reach - upward + layers
        ]
        result = result + layer_part[None, :, None] * shifted
    return result


def stiff_factors(direction):
    return jnp.array(
        [2.0 if component == direction else 1.0 for component in range(3)], jnp.float32
    ).reshape(3, 1, 1, 1)


def relax_slab(padded, displace, face_x, face_z, face_y, force_field, free_cells, diagonal):
    flux_x = stiff_factors(0) * face_x * jnp.diff(padded, axis=1)
    stencil_image = flux_x[:, :-1] - flux_x[:, 1:]
    flux_z = stiff_factors(1) * face_z * jnp.diff(displace, axis=2)
    stencil_image = stencil_image + pad_axis(flux_z, 2, 1, 0) - pad_axis(flux_z, 2, 0, 1)
    flux_y = stiff_factors(2) * face_y * jnp.diff(displace, axis=3)
    stencil_image = stencil_image + pad_axis(flux_y, 3, 1, 0) - pad_axis(flux_y, 3, 0, 1)
    return free_cells * (displace + relax_factor * (force_field - stencil_image) / diagonal)


def slab_energy(grid_field, along_axis, direction, load_cases):
    change = jnp.diff(grid_field, axis=along_axis)
    return jnp.sum(stiff_factors(direction) * change * change, axis=0) / load_cases


def neighbour_planes(displace, load_cases, axis_devices):
    if axis_devices > load_cases:
        below = from_behind(displace[:, -1:], "space", load_cases)
        above = from_behind(displace[:, :1], "space", -load_cases)
    else:
        below = jnp.zeros_like(displace[:, :1])
        above = jnp.zeros_like(displace[:, :1])
    return jnp.concatenate([below, displace, above], axis=1)


def many_slabs(density, displacement, fixed, load_index, load_force, radius):
    slab_rows, layers, row_width = density.shape
    load_cases = load_index.shape[0]
    level_count = load_cases.bit_length() - 1
    axis_devices = lax.axis_size("space")
    axis_place = lax.axis_index("space")
    slab_planes = slab_rows * load_cases
    slab_place = axis_place // load_cases
    load_place = axis_place % load_cases
    total_rows = slab_rows * axis_devices
    weights = layer_weights(radius)
    padded_weights = pad_axis(weights, 1, window_reach, window_reach)
    global_rows = (
        jnp.arange(slab_rows + 2 * window_reach, dtype=jnp.int32)
        + axis_place * slab_rows
        - window_reach
    )
    deep_inside = ((global_rows >= 0) & (global_rows < total_rows)).astype(jnp.float32)
    inside_field = deep_inside[:, None, None] * pad_sides(
        jnp.ones((slab_rows + 2 * window_reach, layers, row_width), jnp.float32)
    )
    total_weight = filter_forward(inside_field, weights)
    slab_start = slab_place * slab_planes
    margin_rows = jnp.arange(slab_planes + 2, dtype=jnp.int32) + slab_start - 1
    margin_inside = ((margin_rows >= 0) & (margin_rows < total_rows)).astype(jnp.float32)
    face_valid = margin_inside[1:] * margin_inside[:-1]
    fixed_slab = lax.dynamic_slice_in_dim(fixed, slab_start, slab_planes, 0).astype(jnp.float32)
    bottom_layer = (jnp.arange(layers, dtype=jnp.int32) == 0).astype(jnp.float32)
    free_cells = 1.0 - bottom_layer[None, :, None] * fixed_slab[:, None, :]
    slab_cells = slab_planes * layers * row_width
    cell_index = jnp.arange(slab_cells, dtype=jnp.int32) + slab_place * slab_cells
    load_hot = jnp.arange(load_cases, dtype=jnp.int32) == load_place
    own_index = jnp.sum(jnp.where(load_hot, load_index, 0))
    own_force = jnp.sum(load_hot.astype(jnp.float32)[:, None] * load_force, axis=0)
    load_hits = (cell_index == own_index).astype(jnp.float32)
    force_field = (own_force[:, None] * load_hits[None, :]).reshape(
        3, slab_planes, layers, row_width
    )
    displace = displacement[0] * free_cells
    target = volume_share * total_rows * layers * row_width
    padded = neighbour_planes(displace, load_cases, axis_devices)
    halo_density = extended(density, (("space", 0),), window_reach)
    filtered = filter_forward(pad_sides(halo_density), weights) / total_weight
    whole_field = lax.all_gather(filtered, "space", axis=0, tiled=True)
    margin = lax.dynamic_slice_in_dim(
        pad_axis(whole_field, 0, 1, 1), slab_start, slab_planes + 2, 0
    )
    moduli = floor_modulus + (1.0 - floor_modulus) * margin**3
    face_x = 0.5 * (moduli[1:] + moduli[:-1]) * face_valid[:, None, None]
    inner_moduli = moduli[1:-1]
    face_z = 0.5 * (inner_moduli[:, 1:] + inner_moduli[:, :-1])
    face_y = 0.5 * (inner_moduli[:, :, 1:] + inner_moduli[:, :, :-1])
    sum_x = face_x[:-1] + face_x[1:]
    sum_z = pad_axis(face_z, 1, 1, 0) + pad_axis(face_z, 1, 0, 1)
    sum_y = pad_axis(face_y, 2, 1, 0) + pad_axis(face_y, 2, 0, 1)
    diagonal = stiff_factors(0) * sum_x + stiff_factors(1) * sum_z + stiff_factors(2) * sum_y
    for sweep_index in range(SWEEPS):
        displace = relax_slab(
            padded, displace, face_x, face_z, face_y, force_field, free_cells, diagonal
        )
        padded = neighbour_planes(displace, load_cases, axis_devices)
    energy_x = slab_energy(padded, 1, 0, load_cases) * face_valid[:, None, None]
    energy_z = slab_energy(displace, 2, 1, load_cases)
    energy_y = slab_energy(displace, 3, 2, load_cases)
    sens_term = 0.5 * (
        energy_x[:-1]
        + energy_x[1:]
        + pad_axis(energy_z, 1, 1, 0)
        + pad_axis(energy_z, 1, 0, 1)
        + pad_axis(energy_y, 2, 1, 0)
        + pad_axis(energy_y, 2, 0, 1)
    )
    sensitive = sens_term
    for level in reversed(range(level_count)):
        half_rows = sensitive.shape[0] // 2
        upper_side = load_place // 2**level % 2 == 1
        outgoing = jnp.where(upper_side, sensitive[:half_rows], sensitive[half_rows:])
        keeping = jnp.where(upper_side, sensitive[half_rows:], sensitive[:half_rows])
        sensitive = keeping + from_partner(outgoing, "space", level)
    weighted_share = 3.0 * (1.0 - floor_modulus) * filtered**2 * sensitive / total_weight
    halo_share = extended(weighted_share, (("space", 0),), window_reach)
    root_term = jnp.sqrt(filter_backward(pad_sides(halo_share), padded_weights))
    lowest = jnp.maximum(density - move_limit, density_floor)
    highest = jnp.minimum(density + move_limit, 1.0)
    design_now = density

    def trial_design(log_level):
        return jnp.clip(design_now * root_term * jnp.exp(-0.5 * log_level), lowest, highest)

    start_state = (jnp.asarray(log_lower, jnp.float32), jnp.asarray(log_span, jnp.float32))

    def halve(search_step, search_state):
        lower_end, span_width = search_state
        half_span = span_width * 0.5
        middle = lower_end + half_span
        volume_total = lax.psum(jnp.sum(trial_design(middle)), "space")
        return (jnp.where(volume_total > target, middle, lower_end), half_span)

    lower_end, span_width = lax.fori_loop(0, SEARCH, halve, start_state)
    density = trial_design(lower_end + 0.5 * span_width)
    new_displacement = displace[None]
    return (density, new_displacement)


def solution(mesh):
    in_specs = (
        P("space", "parts", None),
        P("space", None, None, "parts", None),
        P(None, "parts"),
        P("parts"),
        P("parts", None),
        P("parts"),
    )
    out_specs = (P("space", "parts", None), P("space", None, None, "parts", None))

    def local(density, displacement, fixed, load_index, load_force, radius):
        alone = lax.axis_size("space") == load_index.shape[0]
        run = one_slab if alone else many_slabs
        return run(density, displacement, fixed, load_index, load_force, radius)

    return jax.shard_map(local, mesh=mesh, in_specs=in_specs, out_specs=out_specs, check_vma=False)
```

```python
import math

import jax
import jax.numpy as jnp
from jax import lax
from jax.experimental import pallas as pl
from jax.experimental.pallas import tpu as pltpu
from jax.sharding import PartitionSpec as P

SWEEPS = 3
SEARCH = 12


floor_modulus = 0.05
relax_factor = 0.6
move_limit = 0.2
density_floor = 0.01
volume_share = 0.5
log_lower = -16.0
log_span = 32.0
window_reach = 2

PLANE_SQUARES = (0, 1, 2, 4, 5, 8)
ALL_SQUARES = (0, 1, 2, 3, 4, 5, 6, 8, 9, 12)


def spot_iota(shape, dim):
    return lax.broadcasted_iota(jnp.int32, shape, dim)


def layer_radius(radius_ref, layers, row_width):
    z = spot_iota((layers, row_width), 0)
    result = jnp.zeros((layers, row_width), jnp.int32)
    for layer in range(layers):
        result = jnp.where(z == layer, radius_ref[layer], result)
    return result.astype(jnp.float32)


def class_weights(radius_ref, weight_ref):
    layers, row_width = weight_ref.shape[1:]
    radial = layer_radius(radius_ref, layers, row_width)
    for place, square in enumerate(ALL_SQUARES):
        weight_ref[place] = jnp.maximum(radial - math.sqrt(square), 0.0)


def shift_sum(field, dim, distance):
    size = field.shape[dim]
    spot = spot_iota(field.shape, dim)
    ahead = jnp.where(spot < size - distance, pltpu.roll(field, size - distance, dim), 0.0)
    behind = jnp.where(spot >= distance, pltpu.roll(field, distance, dim), 0.0)
    return ahead + behind


def plane_sums(plane):
    beside = shift_sum(plane, 1, 1)
    further = shift_sum(plane, 1, 2)
    return {
        0: plane,
        1: beside + shift_sum(plane, 0, 1),
        2: shift_sum(beside, 0, 1),
        4: further + shift_sum(plane, 0, 2),
        5: shift_sum(further, 0, 1) + shift_sum(beside, 0, 2),
        8: shift_sum(further, 0, 2),
    }


def weigh(sums, weight_ref, square):
    result = None
    for inner in PLANE_SQUARES:
        term = weight_ref[ALL_SQUARES.index(inner + square)] * sums[inner]
        result = term if result is None else result + term
    return result


def forward_planes(plane, weight_ref):
    sums = plane_sums(plane)
    return [weigh(sums, weight_ref, square) for square in (0, 1, 4)]


def backward_planes(plane, weight_ref):
    beside = shift_sum(plane, 1, 1)
    further = shift_sum(plane, 1, 2)
    results = []
    for square in (0, 1, 4):

        def weight(more):
            return weight_ref[ALL_SQUARES.index(square + more)]

        level = weight(0) * plane + weight(1) * beside + weight(4) * further
        near = weight(1) * plane + weight(2) * beside + weight(5) * further
        far = weight(4) * plane + weight(5) * beside + weight(8) * further
        results.append(level + shift_sum(near, 0, 1) + shift_sum(far, 0, 2))
    return results


def edge_class(x, planes):
    return jnp.minimum(x, 2) + jnp.maximum(x - (planes - 3), 0)


def zero_edges(ref):
    planes = ref.shape[0]
    for place in (0, 1, planes - 2, planes - 1):
        ref[place] = jnp.zeros(ref.shape[1:], ref.dtype)


def sweep_kernel(
    radius_ref,
    index_ref,
    force_ref,
    density_ref,
    fixed_ref,
    start_ref,
    disp_ref,
    sens_ref,
    coef_ref,
    weight_ref,
    total_ref,
    near_ref,
    side_ref,
    far_ref,
    modulus_ref,
    across_ref,
    up_ref,
    down_ref,
    right_ref,
    left_ref,
    rate_ref,
    keep_ref,
    first_ref,
    second_ref,
):
    planes, layers, row_width = density_ref.shape
    load_cases = index_ref.shape[0]
    load_place = lax.axis_index("space")
    shape = (layers, row_width)
    z = spot_iota(shape, 0)
    y = spot_iota(shape, 1)
    zero = jnp.zeros(shape, jnp.float32)

    class_weights(radius_ref, weight_ref)
    for ref in (side_ref, far_ref):
        zero_edges(ref)

    ones = forward_planes(jnp.ones(shape, jnp.float32), weight_ref)
    for place, (lower, upper) in enumerate(((0, 2), (1, 2), (2, 2), (2, 1), (2, 0))):
        total_ref[place] = (
            ones[0] + min(lower, 1) * ones[1] + min(upper, 1) * ones[1]
            + (lower // 2) * ones[2] + (upper // 2) * ones[2]
        )

    def filter_plane(x, carry):
        near, side, far = forward_planes(density_ref[x], weight_ref)
        near_ref[x + 2] = near
        side_ref[x + 2] = side
        far_ref[x + 2] = far
        return carry

    lax.fori_loop(0, planes, filter_plane, 0, unroll=8)

    def modulus_plane(x, carry):
        total = total_ref[edge_class(x, planes)]
        filtered = (
            near_ref[x + 2]
            + side_ref[x + 1]
            + side_ref[x + 3]
            + far_ref[x]
            + far_ref[x + 4]
        ) / total
        modulus = floor_modulus + (1.0 - floor_modulus) * (filtered * filtered * filtered)
        modulus_ref[x] = modulus
        coef_ref[x] = 3.0 * (1.0 - floor_modulus) * (filtered * filtered) / total
        return carry

    lax.fori_loop(0, planes, modulus_plane, 0, unroll=8)

    across_ref[0] = zero
    across_ref[planes] = zero
    first_ref[:, 0] = jnp.zeros((3,) + shape, jnp.float32)
    second_ref[:, 0] = jnp.zeros((3,) + shape, jnp.float32)
    first_ref[:, planes + 1] = jnp.zeros((3,) + shape, jnp.float32)
    second_ref[:, planes + 1] = jnp.zeros((3,) + shape, jnp.float32)

    def face_plane(x, carry):
        modulus = modulus_ref[x]
        later = modulus_ref[jnp.minimum(x + 1, planes - 1)]
        ahead = jnp.where(x + 1 < planes, 0.5 * (modulus + later), 0.0)
        across_ref[x + 1] = ahead
        up = jnp.where(z < layers - 1, 0.5 * (modulus + pltpu.roll(modulus, layers - 1, 0)), 0.0)
        down = pltpu.roll(up, 1, 0)
        right = jnp.where(
            y < row_width - 1, 0.5 * (modulus + pltpu.roll(modulus, row_width - 1, 1)), 0.0
        )
        left = pltpu.roll(right, 1, 1)
        up_ref[x] = up
        down_ref[x] = down
        right_ref[x] = right
        left_ref[x] = left
        free = jnp.where(z == 0, 1.0 - fixed_ref[pl.ds(x, 1), :].astype(jnp.float32), 1.0)
        keep_ref[x] = (1.0 - relax_factor) * free
        sums = (carry + ahead, up + down, left + right)
        every = sums[0] + sums[1] + sums[2]
        push = relax_factor * free
        for part in range(3):
            rate_ref[part, x] = push / (every + sums[part])
            first_ref[part, x + 1] = start_ref[part, x] * free
        return ahead

    lax.fori_loop(0, planes, face_plane, zero, unroll=8)

    own_index = index_ref[load_place]
    own_x = own_index // (layers * row_width)
    own_z = own_index // row_width % layers
    own_y = own_index % row_width
    hit = (z == own_z) & (y == own_y)

    def sweep(source, target, lead):
        def sweep_plane(x, carry):
            before, after = across_ref[x], across_ref[x + 1]
            up, down, right, left = up_ref[x], down_ref[x], right_ref[x], left_ref[x]
            keep = keep_ref[x]
            for part in range(3):
                here = source[part, x + 1]
                pulls = [
                    before * source[part, x] + after * source[part, x + 2],
                    up * pltpu.roll(here, layers - 1, 0) + down * pltpu.roll(here, 1, 0),
                    right * pltpu.roll(here, row_width - 1, 1) + left * pltpu.roll(here, 1, 1),
                ]
                pull = pulls[0] + pulls[1] + pulls[2] + pulls[part]
                target[part, x + lead] = keep * here + rate_ref[part, x] * pull
            return carry

        lax.fori_loop(0, planes, sweep_plane, 0, unroll=8)
        for part in range(3):
            push = rate_ref[part, own_x] * force_ref[load_place, part]
            target[part, own_x + lead] += jnp.where(hit, push, 0.0)

    stages = [first_ref, second_ref]
    for turn in range(SWEEPS - 1):
        sweep(stages[turn % 2], stages[(turn + 1) % 2], 1)
    sweep(stages[(SWEEPS - 1) % 2], disp_ref, 0)

    def energy_plane(x, carry):
        later = jnp.minimum(x + 1, planes - 1)
        ahead, upward, right = zero, zero, zero
        for part in range(3):
            here = disp_ref[part, x]
            step = disp_ref[part, later] - here
            climb = pltpu.roll(here, layers - 1, 0) - here
            slide = pltpu.roll(here, row_width - 1, 1) - here
            ahead = ahead + (2.0 if part == 0 else 1.0) * (step * step)
            upward = upward + (2.0 if part == 1 else 1.0) * (climb * climb)
            right = right + (2.0 if part == 2 else 1.0) * (slide * slide)
        upward = jnp.where(z < layers - 1, upward, 0.0)
        right = jnp.where(y < row_width - 1, right, 0.0)
        total = carry + ahead + upward + pltpu.roll(upward, 1, 0) + right + pltpu.roll(right, 1, 1)
        sens_ref[x] = (0.5 / load_cases) * total
        return ahead

    lax.fori_loop(0, planes, energy_plane, zero, unroll=8)


def design_kernel(
    radius_ref,
    sens_ref,
    coef_ref,
    density_ref,
    new_ref,
    weight_ref,
    near_ref,
    side_ref,
    far_ref,
    pull_ref,
    low_ref,
    high_ref,
):
    planes, layers, row_width = density_ref.shape
    own_planes = new_ref.shape[0]
    place = lax.axis_index("space")
    shape = (layers, row_width)
    zero = jnp.zeros(shape, jnp.float32)
    class_weights(radius_ref, weight_ref)
    for ref in (side_ref, far_ref):
        zero_edges(ref)

    def filter_plane(x, carry):
        near, side, far = backward_planes(sens_ref[x] * coef_ref[x], weight_ref)
        near_ref[x + 2] = near
        side_ref[x + 2] = side
        far_ref[x + 2] = far
        return carry

    lax.fori_loop(0, planes, filter_plane, 0, unroll=8)

    def root_plane(x, carry):
        root = jnp.sqrt(
            near_ref[x + 2] + side_ref[x + 1] + side_ref[x + 3] + far_ref[x] + far_ref[x + 4]
        )
        density = density_ref[x]
        pull_ref[x] = density * root
        low_ref[x] = jnp.maximum(density - move_limit, density_floor)
        high_ref[x] = jnp.minimum(density + move_limit, 1.0)
        return carry

    lax.fori_loop(0, planes, root_plane, 0, unroll=8)

    target = volume_share * planes * layers * row_width

    def trial(x, factor):
        return jnp.minimum(jnp.maximum(pull_ref[x] * factor, low_ref[x]), high_ref[x])

    def halve(step, state):
        lower, span = state
        half = span * 0.5
        middle = lower + half
        factor = jnp.exp(-0.5 * middle)
        total = lax.fori_loop(
            0, planes, lambda x, acc: acc + trial(x, factor), zero, unroll=8
        )
        volume = jnp.sum(jnp.sum(total, axis=0, keepdims=True), axis=1, keepdims=True)
        return jnp.where(volume > target, middle, lower), half

    start = (jnp.full((1, 1), log_lower, jnp.float32), jnp.full((1, 1), log_span, jnp.float32))
    lower, span = lax.fori_loop(0, SEARCH, halve, start)
    factor = jnp.exp(-0.5 * (lower + 0.5 * span))
    for own in range(own_planes):
        new_ref[own] = trial(place * own_planes + own, factor)


def in_vmem():
    return pl.BlockSpec(memory_space=pltpu.VMEM)


def in_smem():
    return pl.BlockSpec(memory_space=pltpu.SMEM)


KERNEL_VMEM = 24 * 2**20


def sweep_call(radius, load_index, load_force, density, fixed, displacement):
    planes, layers, row_width = density.shape
    grid_field = (planes, layers, row_width)

    def scratch(*lead):
        return pltpu.VMEM(lead + (layers, row_width), jnp.float32)

    return pl.pallas_call(
        sweep_kernel,
        out_shape=[
            jax.ShapeDtypeStruct((3,) + grid_field, jnp.float32),
            jax.ShapeDtypeStruct(grid_field, jnp.float32),
            jax.ShapeDtypeStruct(grid_field, jnp.float32),
        ],
        in_specs=[in_smem()] * 3 + [in_vmem()] * 3,
        out_specs=[in_vmem()] * 3,
        scratch_shapes=[
            scratch(len(ALL_SQUARES)),
            scratch(2 * window_reach + 1),
            scratch(planes + 4),
            scratch(planes + 4),
            scratch(planes + 4),
            scratch(planes),
            scratch(planes + 1),
            scratch(planes),
            scratch(planes),
            scratch(planes),
            scratch(planes),
            scratch(3, planes),
            scratch(planes),
            scratch(3, planes + 2),
            scratch(3, planes + 2),
        ],
        compiler_params=pltpu.CompilerParams(vmem_limit_bytes=KERNEL_VMEM),
        name="sweeps",
    )(radius, load_index, load_force, density, fixed, displacement)


def design_call(radius, sens, coef, density, own_planes):
    planes, layers, row_width = density.shape

    def scratch(*lead):
        return pltpu.VMEM(lead + (layers, row_width), jnp.float32)

    return pl.pallas_call(
        design_kernel,
        out_shape=jax.ShapeDtypeStruct((own_planes, layers, row_width), jnp.float32),
        in_specs=[in_smem()] + [in_vmem()] * 3,
        out_specs=in_vmem(),
        scratch_shapes=[
            scratch(len(ALL_SQUARES)),
            scratch(planes + 4),
            scratch(planes + 4),
            scratch(planes + 4),
            scratch(planes),
            scratch(planes),
            scratch(planes),
        ],
        compiler_params=pltpu.CompilerParams(vmem_limit_bytes=KERNEL_VMEM),
        name="design",
    )(radius, sens, coef, density)


def gathered(block):
    devices = lax.axis_size("space")
    copies = jnp.broadcast_to(block[None], (devices,) + block.shape)
    blocks = lax.all_to_all(copies, "space", 0, 0)
    return blocks.reshape((devices * block.shape[0],) + block.shape[1:])


def scattered_sum(field):
    devices = lax.axis_size("space")
    pieces = field.reshape((devices, field.shape[0] // devices) + field.shape[1:])
    return jnp.sum(lax.all_to_all(pieces, "space", 0, 0), axis=0)


def one_slab(density, displacement, fixed, load_index, load_force, radius):
    whole = gathered(density)
    new_displacement, sens, coef = sweep_call(
        radius, load_index, load_force, whole, fixed, displacement[0]
    )
    sens = gathered(scattered_sum(sens))
    new_density = design_call(radius, sens, coef, whole, density.shape[0])
    return new_density, new_displacement[None]


def from_behind(block, axis, distance):
    devices = range(lax.axis_size(axis))
    route = [(i - distance, i) for i in devices if i - distance in devices]
    return lax.ppermute(block, axis, route)


def extended(x, sides, width):
    for axis, dim in sides:
        size, length = (lax.axis_size(axis), x.shape[dim])
        up = [(i, (i + 1) % size) for i in range(size - 1)]
        down = [(j, i) for i, j in up]
        last = lax.slice_in_dim(x, length - width, length, axis=dim)
        first = lax.slice_in_dim(x, 0, width, axis=dim)
        before = lax.ppermute(last, axis, up)
        after = lax.ppermute(first, axis, down)
        x = jnp.concatenate([before, x, after], axis=dim)
    return x


def from_partner(x, axis, bit):
    return lax.ppermute(x, axis, [(i, i ^ 1 << bit) for i in range(lax.axis_size(axis))])


def window_offsets():
    offsets_list = []
    for across in range(-window_reach, window_reach + 1):
        for upward in range(-window_reach, window_reach + 1):
            for sideways in range(-window_reach, window_reach + 1):
                length = math.sqrt(across * across + upward * upward + sideways * sideways)
                offsets_list.append((across, upward, sideways, length))
    return offsets_list


def layer_weights(radius):
    radial = radius.astype(jnp.float32)
    return jnp.stack(
        [jnp.maximum(radial - length, 0.0) for across, upward, sideways, length in window_offsets()]
    )


def pad_axis(grid_field, along_axis, before, after_cells):
    widths = [(0, 0)] * grid_field.ndim
    widths[along_axis] = (before, after_cells)
    return jnp.pad(grid_field, widths)


def pad_sides(grid_field):
    return jnp.pad(grid_field, ((0, 0), (window_reach, window_reach), (window_reach, window_reach)))


def filter_forward(padded, weights):
    out_rows = padded.shape[0] - 2 * window_reach
    layers = padded.shape[1] - 2 * window_reach
    row_width = padded.shape[2] - 2 * window_reach
    result = jnp.zeros((out_rows, layers, row_width), jnp.float32)
    for offset_index, (across, upward, sideways, length) in enumerate(window_offsets()):
        shifted = padded[
            window_reach + across : window_reach + across + out_rows,
            window_reach + upward : window_reach + upward + layers,
            window_reach + sideways : window_reach + sideways + row_width,
        ]
        result = result + weights[offset_index][None, :, None] * shifted
    return result


def filter_backward(padded, padded_weights):
    out_rows = padded.shape[0] - 2 * window_reach
    layers = padded.shape[1] - 2 * window_reach
    row_width = padded.shape[2] - 2 * window_reach
    result = jnp.zeros((out_rows, layers, row_width), jnp.float32)
    for offset_index, (across, upward, sideways, length) in enumerate(window_offsets()):
        shifted = padded[
            window_reach - across : window_reach - across + out_rows,
            window_reach - upward : window_reach - upward + layers,
            window_reach - sideways : window_reach - sideways + row_width,
        ]
        layer_part = padded_weights[
            offset_index, window_reach - upward : window_reach - upward + layers
        ]
        result = result + layer_part[None, :, None] * shifted
    return result


def stiff_factors(direction):
    return jnp.array(
        [2.0 if component == direction else 1.0 for component in range(3)], jnp.float32
    ).reshape(3, 1, 1, 1)


def relax_slab(padded, displace, face_x, face_z, face_y, force_field, free_cells, diagonal):
    flux_x = stiff_factors(0) * face_x * jnp.diff(padded, axis=1)
    stencil_image = flux_x[:, :-1] - flux_x[:, 1:]
    flux_z = stiff_factors(1) * face_z * jnp.diff(displace, axis=2)
    stencil_image = stencil_image + pad_axis(flux_z, 2, 1, 0) - pad_axis(flux_z, 2, 0, 1)
    flux_y = stiff_factors(2) * face_y * jnp.diff(displace, axis=3)
    stencil_image = stencil_image + pad_axis(flux_y, 3, 1, 0) - pad_axis(flux_y, 3, 0, 1)
    return free_cells * (displace + relax_factor * (force_field - stencil_image) / diagonal)


def slab_energy(grid_field, along_axis, direction, load_cases):
    change = jnp.diff(grid_field, axis=along_axis)
    return jnp.sum(stiff_factors(direction) * change * change, axis=0) / load_cases


def neighbour_planes(displace, load_cases, axis_devices):
    if axis_devices > load_cases:
        below = from_behind(displace[:, -1:], "space", load_cases)
        above = from_behind(displace[:, :1], "space", -load_cases)
    else:
        below = jnp.zeros_like(displace[:, :1])
        above = jnp.zeros_like(displace[:, :1])
    return jnp.concatenate([below, displace, above], axis=1)


def many_slabs(density, displacement, fixed, load_index, load_force, radius):
    slab_rows, layers, row_width = density.shape
    load_cases = load_index.shape[0]
    level_count = load_cases.bit_length() - 1
    axis_devices = lax.axis_size("space")
    axis_place = lax.axis_index("space")
    slab_planes = slab_rows * load_cases
    slab_place = axis_place // load_cases
    load_place = axis_place % load_cases
    total_rows = slab_rows * axis_devices
    weights = layer_weights(radius)
    padded_weights = pad_axis(weights, 1, window_reach, window_reach)
    global_rows = (
        jnp.arange(slab_rows + 2 * window_reach, dtype=jnp.int32)
        + axis_place * slab_rows
        - window_reach
    )
    deep_inside = ((global_rows >= 0) & (global_rows < total_rows)).astype(jnp.float32)
    inside_field = deep_inside[:, None, None] * pad_sides(
        jnp.ones((slab_rows + 2 * window_reach, layers, row_width), jnp.float32)
    )
    total_weight = filter_forward(inside_field, weights)
    slab_start = slab_place * slab_planes
    margin_rows = jnp.arange(slab_planes + 2, dtype=jnp.int32) + slab_start - 1
    margin_inside = ((margin_rows >= 0) & (margin_rows < total_rows)).astype(jnp.float32)
    face_valid = margin_inside[1:] * margin_inside[:-1]
    fixed_slab = lax.dynamic_slice_in_dim(fixed, slab_start, slab_planes, 0).astype(jnp.float32)
    bottom_layer = (jnp.arange(layers, dtype=jnp.int32) == 0).astype(jnp.float32)
    free_cells = 1.0 - bottom_layer[None, :, None] * fixed_slab[:, None, :]
    slab_cells = slab_planes * layers * row_width
    cell_index = jnp.arange(slab_cells, dtype=jnp.int32) + slab_place * slab_cells
    load_hot = jnp.arange(load_cases, dtype=jnp.int32) == load_place
    own_index = jnp.sum(jnp.where(load_hot, load_index, 0))
    own_force = jnp.sum(load_hot.astype(jnp.float32)[:, None] * load_force, axis=0)
    load_hits = (cell_index == own_index).astype(jnp.float32)
    force_field = (own_force[:, None] * load_hits[None, :]).reshape(
        3, slab_planes, layers, row_width
    )
    displace = displacement[0] * free_cells
    target = volume_share * total_rows * layers * row_width
    padded = neighbour_planes(displace, load_cases, axis_devices)
    halo_density = extended(density, (("space", 0),), window_reach)
    filtered = filter_forward(pad_sides(halo_density), weights) / total_weight
    whole_field = lax.all_gather(filtered, "space", axis=0, tiled=True)
    margin = lax.dynamic_slice_in_dim(
        pad_axis(whole_field, 0, 1, 1), slab_start, slab_planes + 2, 0
    )
    moduli = floor_modulus + (1.0 - floor_modulus) * margin**3
    face_x = 0.5 * (moduli[1:] + moduli[:-1]) * face_valid[:, None, None]
    inner_moduli = moduli[1:-1]
    face_z = 0.5 * (inner_moduli[:, 1:] + inner_moduli[:, :-1])
    face_y = 0.5 * (inner_moduli[:, :, 1:] + inner_moduli[:, :, :-1])
    sum_x = face_x[:-1] + face_x[1:]
    sum_z = pad_axis(face_z, 1, 1, 0) + pad_axis(face_z, 1, 0, 1)
    sum_y = pad_axis(face_y, 2, 1, 0) + pad_axis(face_y, 2, 0, 1)
    diagonal = stiff_factors(0) * sum_x + stiff_factors(1) * sum_z + stiff_factors(2) * sum_y
    for sweep_index in range(SWEEPS):
        displace = relax_slab(
            padded, displace, face_x, face_z, face_y, force_field, free_cells, diagonal
        )
        padded = neighbour_planes(displace, load_cases, axis_devices)
    energy_x = slab_energy(padded, 1, 0, load_cases) * face_valid[:, None, None]
    energy_z = slab_energy(displace, 2, 1, load_cases)
    energy_y = slab_energy(displace, 3, 2, load_cases)
    sens_term = 0.5 * (
        energy_x[:-1]
        + energy_x[1:]
        + pad_axis(energy_z, 1, 1, 0)
        + pad_axis(energy_z, 1, 0, 1)
        + pad_axis(energy_y, 2, 1, 0)
        + pad_axis(energy_y, 2, 0, 1)
    )
    sensitive = sens_term
    for level in reversed(range(level_count)):
        half_rows = sensitive.shape[0] // 2
        upper_side = load_place // 2**level % 2 == 1
        outgoing = jnp.where(upper_side, sensitive[:half_rows], sensitive[half_rows:])
        keeping = jnp.where(upper_side, sensitive[half_rows:], sensitive[:half_rows])
        sensitive = keeping + from_partner(outgoing, "space", level)
    weighted_share = 3.0 * (1.0 - floor_modulus) * filtered**2 * sensitive / total_weight
    halo_share = extended(weighted_share, (("space", 0),), window_reach)
    root_term = jnp.sqrt(filter_backward(pad_sides(halo_share), padded_weights))
    lowest = jnp.maximum(density - move_limit, density_floor)
    highest = jnp.minimum(density + move_limit, 1.0)
    design_now = density

    def trial_design(log_level):
        return jnp.clip(design_now * root_term * jnp.exp(-0.5 * log_level), lowest, highest)

    start_state = (jnp.asarray(log_lower, jnp.float32), jnp.asarray(log_span, jnp.float32))

    def halve(search_step, search_state):
        lower_end, span_width = search_state
        half_span = span_width * 0.5
        middle = lower_end + half_span
        volume_total = lax.psum(jnp.sum(trial_design(middle)), "space")
        return (jnp.where(volume_total > target, middle, lower_end), half_span)

    lower_end, span_width = lax.fori_loop(0, SEARCH, halve, start_state)
    density = trial_design(lower_end + 0.5 * span_width)
    new_displacement = displace[None]
    return (density, new_displacement)


def solution(mesh):
    in_specs = (
        P("space", "parts", None),
        P("space", None, None, "parts", None),
        P(None, "parts"),
        P("parts"),
        P("parts", None),
        P("parts"),
    )
    out_specs = (P("space", "parts", None), P("space", None, None, "parts", None))

    def local(density, displacement, fixed, load_index, load_force, radius):
        alone = lax.axis_size("space") == load_index.shape[0]
        run = one_slab if alone else many_slabs
        return run(density, displacement, fixed, load_index, load_force, radius)

    return jax.shard_map(local, mesh=mesh, in_specs=in_specs, out_specs=out_specs, check_vma=False)
```

```python
import math

import jax
import jax.numpy as jnp
from jax import lax
from jax.experimental import pallas as pl
from jax.experimental.pallas import tpu as pltpu
from jax.sharding import PartitionSpec as P

SWEEPS = 3
SEARCH = 12


floor_modulus = 0.05
relax_factor = 0.6
move_limit = 0.2
density_floor = 0.01
volume_share = 0.5
log_lower = -16.0
log_span = 32.0
window_reach = 2

PLANE_SQUARES = (0, 1, 2, 4, 5, 8)
ALL_SQUARES = (0, 1, 2, 3, 4, 5, 6, 8, 9, 12)


def spot_iota(shape, dim):
    return lax.broadcasted_iota(jnp.int32, shape, dim)


def layer_radius(radius_ref, layers, row_width):
    z = spot_iota((layers, row_width), 0)
    result = jnp.zeros((layers, row_width), jnp.int32)
    for layer in range(layers):
        result = jnp.where(z == layer, radius_ref[layer], result)
    return result.astype(jnp.float32)


def class_weights(radius_ref, weight_ref):
    layers, row_width = weight_ref.shape[1:]
    radial = layer_radius(radius_ref, layers, row_width)
    for place, square in enumerate(ALL_SQUARES):
        weight_ref[place] = jnp.maximum(radial - math.sqrt(square), 0.0)


def shift_sum(field, dim, distance):
    size = field.shape[dim]
    spot = spot_iota(field.shape, dim)
    ahead = jnp.where(spot < size - distance, pltpu.roll(field, size - distance, dim), 0.0)
    behind = jnp.where(spot >= distance, pltpu.roll(field, distance, dim), 0.0)
    return ahead + behind


def plane_sums(plane):
    beside = shift_sum(plane, 1, 1)
    further = shift_sum(plane, 1, 2)
    return {
        0: plane,
        1: beside + shift_sum(plane, 0, 1),
        2: shift_sum(beside, 0, 1),
        4: further + shift_sum(plane, 0, 2),
        5: shift_sum(further, 0, 1) + shift_sum(beside, 0, 2),
        8: shift_sum(further, 0, 2),
    }


def weigh(sums, weight_ref, square):
    result = None
    for inner in PLANE_SQUARES:
        term = weight_ref[ALL_SQUARES.index(inner + square)] * sums[inner]
        result = term if result is None else result + term
    return result


def forward_planes(plane, weight_ref):
    sums = plane_sums(plane)
    return [weigh(sums, weight_ref, square) for square in (0, 1, 4)]


def backward_planes(plane, weight_ref):
    beside = shift_sum(plane, 1, 1)
    further = shift_sum(plane, 1, 2)
    results = []
    for square in (0, 1, 4):

        def weight(more):
            return weight_ref[ALL_SQUARES.index(square + more)]

        level = weight(0) * plane + weight(1) * beside + weight(4) * further
        near = weight(1) * plane + weight(2) * beside + weight(5) * further
        far = weight(4) * plane + weight(5) * beside + weight(8) * further
        results.append(level + shift_sum(near, 0, 1) + shift_sum(far, 0, 2))
    return results


def reverse_bits(value, count):
    result = 0
    for bit in range(count):
        result = result + ((value >> bit) & 1) * (1 << (count - 1 - bit))
    return result


def partner_spot(x, own_planes, devices):
    mine = lax.axis_index("space")
    order = reverse_bits((x // own_planes) ^ mine, devices.bit_length() - 1)
    return order, x % own_planes


def edge_class(x, planes):
    return jnp.minimum(x, 2) + jnp.maximum(x - (planes - 3), 0)


def zero_edges(ref):
    planes = ref.shape[0]
    for place in (0, 1, planes - 2, planes - 1):
        ref[place] = jnp.zeros(ref.shape[1:], ref.dtype)


def sweep_kernel(
    radius_ref,
    index_ref,
    force_ref,
    density_ref,
    fixed_ref,
    start_ref,
    disp_ref,
    sens_ref,
    coef_ref,
    weight_ref,
    total_ref,
    near_ref,
    side_ref,
    far_ref,
    modulus_ref,
    across_ref,
    up_ref,
    down_ref,
    right_ref,
    left_ref,
    rate_ref,
    keep_ref,
    first_ref,
    second_ref,
):
    devices, own_planes, layers, row_width = density_ref.shape
    planes = devices * own_planes
    load_cases = index_ref.shape[0]
    load_place = lax.axis_index("space")
    shape = (layers, row_width)
    z = spot_iota(shape, 0)
    y = spot_iota(shape, 1)
    zero = jnp.zeros(shape, jnp.float32)

    class_weights(radius_ref, weight_ref)
    for ref in (side_ref, far_ref):
        zero_edges(ref)

    ones = forward_planes(jnp.ones(shape, jnp.float32), weight_ref)
    for place, (lower, upper) in enumerate(((0, 2), (1, 2), (2, 2), (2, 1), (2, 0))):
        total_ref[place] = (
            ones[0] + min(lower, 1) * ones[1] + min(upper, 1) * ones[1]
            + (lower // 2) * ones[2] + (upper // 2) * ones[2]
        )

    def filter_plane(x, carry):
        near, side, far = forward_planes(
            density_ref[partner_spot(x, own_planes, devices)], weight_ref
        )
        near_ref[x + 2] = near
        side_ref[x + 2] = side
        far_ref[x + 2] = far
        return carry

    lax.fori_loop(0, planes, filter_plane, 0, unroll=8)

    def modulus_plane(x, carry):
        total = total_ref[edge_class(x, planes)]
        filtered = (
            near_ref[x + 2]
            + side_ref[x + 1]
            + side_ref[x + 3]
            + far_ref[x]
            + far_ref[x + 4]
        ) / total
        modulus = floor_modulus + (1.0 - floor_modulus) * (filtered * filtered * filtered)
        modulus_ref[x] = modulus
        coef_ref[x] = 3.0 * (1.0 - floor_modulus) * (filtered * filtered) / total
        return carry

    lax.fori_loop(0, planes, modulus_plane, 0, unroll=8)

    across_ref[0] = zero
    across_ref[planes] = zero
    first_ref[:, 0] = jnp.zeros((3,) + shape, jnp.float32)
    second_ref[:, 0] = jnp.zeros((3,) + shape, jnp.float32)
    first_ref[:, planes + 1] = jnp.zeros((3,) + shape, jnp.float32)
    second_ref[:, planes + 1] = jnp.zeros((3,) + shape, jnp.float32)

    def face_plane(x, carry):
        modulus = modulus_ref[x]
        later = modulus_ref[jnp.minimum(x + 1, planes - 1)]
        ahead = jnp.where(x + 1 < planes, 0.5 * (modulus + later), 0.0)
        across_ref[x + 1] = ahead
        up = jnp.where(z < layers - 1, 0.5 * (modulus + pltpu.roll(modulus, layers - 1, 0)), 0.0)
        down = pltpu.roll(up, 1, 0)
        right = jnp.where(
            y < row_width - 1, 0.5 * (modulus + pltpu.roll(modulus, row_width - 1, 1)), 0.0
        )
        left = pltpu.roll(right, 1, 1)
        up_ref[x] = up
        down_ref[x] = down
        right_ref[x] = right
        left_ref[x] = left
        free = jnp.where(z == 0, 1.0 - fixed_ref[pl.ds(x, 1), :].astype(jnp.float32), 1.0)
        keep_ref[x] = (1.0 - relax_factor) * free
        sums = (carry + ahead, up + down, left + right)
        every = sums[0] + sums[1] + sums[2]
        push = relax_factor * free
        for part in range(3):
            rate_ref[part, x] = push / (every + sums[part])
            first_ref[part, x + 1] = start_ref[part, x] * free
        return ahead

    lax.fori_loop(0, planes, face_plane, zero, unroll=8)

    own_index = index_ref[load_place]
    own_x = own_index // (layers * row_width)
    own_z = own_index // row_width % layers
    own_y = own_index % row_width
    hit = (z == own_z) & (y == own_y)

    def sweep(source, target, lead):
        def sweep_plane(x, carry):
            before, after = across_ref[x], across_ref[x + 1]
            up, down, right, left = up_ref[x], down_ref[x], right_ref[x], left_ref[x]
            keep = keep_ref[x]
            for part in range(3):
                here = source[part, x + 1]
                pulls = [
                    before * source[part, x] + after * source[part, x + 2],
                    up * pltpu.roll(here, layers - 1, 0) + down * pltpu.roll(here, 1, 0),
                    right * pltpu.roll(here, row_width - 1, 1) + left * pltpu.roll(here, 1, 1),
                ]
                pull = pulls[0] + pulls[1] + pulls[2] + pulls[part]
                target[part, x + lead] = keep * here + rate_ref[part, x] * pull
            return carry

        lax.fori_loop(0, planes, sweep_plane, 0, unroll=8)
        for part in range(3):
            push = rate_ref[part, own_x] * force_ref[load_place, part]
            target[part, own_x + lead] += jnp.where(hit, push, 0.0)

    stages = [first_ref, second_ref]
    for turn in range(SWEEPS - 1):
        sweep(stages[turn % 2], stages[(turn + 1) % 2], 1)
    sweep(stages[(SWEEPS - 1) % 2], disp_ref, 0)

    def energy_plane(x, carry):
        later = jnp.minimum(x + 1, planes - 1)
        ahead, upward, right = zero, zero, zero
        for part in range(3):
            here = disp_ref[part, x]
            step = disp_ref[part, later] - here
            climb = pltpu.roll(here, layers - 1, 0) - here
            slide = pltpu.roll(here, row_width - 1, 1) - here
            ahead = ahead + (2.0 if part == 0 else 1.0) * (step * step)
            upward = upward + (2.0 if part == 1 else 1.0) * (climb * climb)
            right = right + (2.0 if part == 2 else 1.0) * (slide * slide)
        upward = jnp.where(z < layers - 1, upward, 0.0)
        right = jnp.where(y < row_width - 1, right, 0.0)
        total = carry + ahead + upward + pltpu.roll(upward, 1, 0) + right + pltpu.roll(right, 1, 1)
        sens_ref[partner_spot(x, own_planes, devices)] = (0.5 / load_cases) * total
        return ahead

    lax.fori_loop(0, planes, energy_plane, zero, unroll=8)


def design_kernel(
    radius_ref,
    sens_ref,
    coef_ref,
    density_ref,
    new_ref,
    weight_ref,
    near_ref,
    side_ref,
    far_ref,
    pull_ref,
    low_ref,
    high_ref,
):
    devices, own_planes, layers, row_width = density_ref.shape
    planes = devices * own_planes
    place = lax.axis_index("space")
    shape = (layers, row_width)
    zero = jnp.zeros(shape, jnp.float32)
    class_weights(radius_ref, weight_ref)
    for ref in (side_ref, far_ref):
        zero_edges(ref)

    def filter_plane(x, carry):
        near, side, far = backward_planes(
            sens_ref[partner_spot(x, own_planes, devices)] * coef_ref[x], weight_ref
        )
        near_ref[x + 2] = near
        side_ref[x + 2] = side
        far_ref[x + 2] = far
        return carry

    lax.fori_loop(0, planes, filter_plane, 0, unroll=8)

    def root_plane(x, carry):
        root = jnp.sqrt(
            near_ref[x + 2] + side_ref[x + 1] + side_ref[x + 3] + far_ref[x] + far_ref[x + 4]
        )
        density = density_ref[partner_spot(x, own_planes, devices)]
        pull_ref[x] = density * root
        low_ref[x] = jnp.maximum(density - move_limit, density_floor)
        high_ref[x] = jnp.minimum(density + move_limit, 1.0)
        return carry

    lax.fori_loop(0, planes, root_plane, 0, unroll=8)

    target = volume_share * planes * layers * row_width

    def trial(x, factor):
        return jnp.minimum(jnp.maximum(pull_ref[x] * factor, low_ref[x]), high_ref[x])

    def halve(step, state):
        lower, span = state
        half = span * 0.5
        middle = lower + half
        factor = jnp.exp(-0.5 * middle)
        total = lax.fori_loop(
            0, planes, lambda x, acc: acc + trial(x, factor), zero, unroll=8
        )
        volume = jnp.sum(jnp.sum(total, axis=0, keepdims=True), axis=1, keepdims=True)
        return jnp.where(volume > target, middle, lower), half

    start = (jnp.full((1, 1), log_lower, jnp.float32), jnp.full((1, 1), log_span, jnp.float32))
    lower, span = lax.fori_loop(0, SEARCH, halve, start)
    factor = jnp.exp(-0.5 * (lower + 0.5 * span))
    for own in range(own_planes):
        new_ref[own] = trial(place * own_planes + own, factor)


def in_vmem():
    return pl.BlockSpec(memory_space=pltpu.VMEM)


def in_smem():
    return pl.BlockSpec(memory_space=pltpu.SMEM)


KERNEL_VMEM = 24 * 2**20


def sweep_call(radius, load_index, load_force, density, fixed, displacement):
    devices, own_planes, layers, row_width = density.shape
    planes = devices * own_planes
    grid_field = (planes, layers, row_width)

    def scratch(*lead):
        return pltpu.VMEM(lead + (layers, row_width), jnp.float32)

    return pl.pallas_call(
        sweep_kernel,
        out_shape=[
            jax.ShapeDtypeStruct((3,) + grid_field, jnp.float32),
            jax.ShapeDtypeStruct(density.shape, jnp.float32),
            jax.ShapeDtypeStruct(grid_field, jnp.float32),
        ],
        in_specs=[in_smem()] * 3 + [in_vmem()] * 3,
        out_specs=[in_vmem()] * 3,
        scratch_shapes=[
            scratch(len(ALL_SQUARES)),
            scratch(2 * window_reach + 1),
            scratch(planes + 4),
            scratch(planes + 4),
            scratch(planes + 4),
            scratch(planes),
            scratch(planes + 1),
            scratch(planes),
            scratch(planes),
            scratch(planes),
            scratch(planes),
            scratch(3, planes),
            scratch(planes),
            scratch(3, planes + 2),
            scratch(3, planes + 2),
        ],
        compiler_params=pltpu.CompilerParams(vmem_limit_bytes=KERNEL_VMEM),
        name="sweeps",
    )(radius, load_index, load_force, density, fixed, displacement)


def design_call(radius, sens, coef, density):
    devices, own_planes, layers, row_width = density.shape
    planes = devices * own_planes

    def scratch(*lead):
        return pltpu.VMEM(lead + (layers, row_width), jnp.float32)

    return pl.pallas_call(
        design_kernel,
        out_shape=jax.ShapeDtypeStruct((own_planes, layers, row_width), jnp.float32),
        in_specs=[in_smem()] + [in_vmem()] * 3,
        out_specs=in_vmem(),
        scratch_shapes=[
            scratch(len(ALL_SQUARES)),
            scratch(planes + 4),
            scratch(planes + 4),
            scratch(planes + 4),
            scratch(planes),
            scratch(planes),
            scratch(planes),
        ],
        compiler_params=pltpu.CompilerParams(vmem_limit_bytes=KERNEL_VMEM),
        name="design",
    )(radius, sens, coef, density)


def swapped(block, bit):
    devices = lax.axis_size("space")
    return lax.ppermute(block, "space", [(i, i ^ 1 << bit) for i in range(devices)])


def partner_bits(devices):
    return devices.bit_length() - 1


def gathered(block):
    pieces = block[None]
    for bit in reversed(range(partner_bits(lax.axis_size("space")))):
        pieces = jnp.concatenate([pieces, swapped(pieces, bit)])
    return pieces


def scattered_sum(pieces):
    for bit in range(partner_bits(lax.axis_size("space"))):
        half = pieces.shape[0] // 2
        pieces = pieces[:half] + swapped(pieces[half:], bit)
    return pieces[0]


def one_slab(density, displacement, fixed, load_index, load_force, radius):
    whole = gathered(density)
    new_displacement, sens, coef = sweep_call(
        radius, load_index, load_force, whole, fixed, displacement[0]
    )
    sens = gathered(scattered_sum(sens))
    new_density = design_call(radius, sens, coef, whole)
    return new_density, new_displacement[None]


def from_behind(block, axis, distance):
    devices = range(lax.axis_size(axis))
    route = [(i - distance, i) for i in devices if i - distance in devices]
    return lax.ppermute(block, axis, route)


def extended(x, sides, width):
    for axis, dim in sides:
        size, length = (lax.axis_size(axis), x.shape[dim])
        up = [(i, (i + 1) % size) for i in range(size - 1)]
        down = [(j, i) for i, j in up]
        last = lax.slice_in_dim(x, length - width, length, axis=dim)
        first = lax.slice_in_dim(x, 0, width, axis=dim)
        before = lax.ppermute(last, axis, up)
        after = lax.ppermute(first, axis, down)
        x = jnp.concatenate([before, x, after], axis=dim)
    return x


def from_partner(x, axis, bit):
    return lax.ppermute(x, axis, [(i, i ^ 1 << bit) for i in range(lax.axis_size(axis))])


def window_offsets():
    offsets_list = []
    for across in range(-window_reach, window_reach + 1):
        for upward in range(-window_reach, window_reach + 1):
            for sideways in range(-window_reach, window_reach + 1):
                length = math.sqrt(across * across + upward * upward + sideways * sideways)
                offsets_list.append((across, upward, sideways, length))
    return offsets_list


def layer_weights(radius):
    radial = radius.astype(jnp.float32)
    return jnp.stack(
        [jnp.maximum(radial - length, 0.0) for across, upward, sideways, length in window_offsets()]
    )


def pad_axis(grid_field, along_axis, before, after_cells):
    widths = [(0, 0)] * grid_field.ndim
    widths[along_axis] = (before, after_cells)
    return jnp.pad(grid_field, widths)


def pad_sides(grid_field):
    return jnp.pad(grid_field, ((0, 0), (window_reach, window_reach), (window_reach, window_reach)))


def filter_forward(padded, weights):
    out_rows = padded.shape[0] - 2 * window_reach
    layers = padded.shape[1] - 2 * window_reach
    row_width = padded.shape[2] - 2 * window_reach
    result = jnp.zeros((out_rows, layers, row_width), jnp.float32)
    for offset_index, (across, upward, sideways, length) in enumerate(window_offsets()):
        shifted = padded[
            window_reach + across : window_reach + across + out_rows,
            window_reach + upward : window_reach + upward + layers,
            window_reach + sideways : window_reach + sideways + row_width,
        ]
        result = result + weights[offset_index][None, :, None] * shifted
    return result


def filter_backward(padded, padded_weights):
    out_rows = padded.shape[0] - 2 * window_reach
    layers = padded.shape[1] - 2 * window_reach
    row_width = padded.shape[2] - 2 * window_reach
    result = jnp.zeros((out_rows, layers, row_width), jnp.float32)
    for offset_index, (across, upward, sideways, length) in enumerate(window_offsets()):
        shifted = padded[
            window_reach - across : window_reach - across + out_rows,
            window_reach - upward : window_reach - upward + layers,
            window_reach - sideways : window_reach - sideways + row_width,
        ]
        layer_part = padded_weights[
            offset_index, window_reach - upward : window_reach - upward + layers
        ]
        result = result + layer_part[None, :, None] * shifted
    return result


def stiff_factors(direction):
    return jnp.array(
        [2.0 if component == direction else 1.0 for component in range(3)], jnp.float32
    ).reshape(3, 1, 1, 1)


def relax_slab(padded, displace, face_x, face_z, face_y, force_field, free_cells, diagonal):
    flux_x = stiff_factors(0) * face_x * jnp.diff(padded, axis=1)
    stencil_image = flux_x[:, :-1] - flux_x[:, 1:]
    flux_z = stiff_factors(1) * face_z * jnp.diff(displace, axis=2)
    stencil_image = stencil_image + pad_axis(flux_z, 2, 1, 0) - pad_axis(flux_z, 2, 0, 1)
    flux_y = stiff_factors(2) * face_y * jnp.diff(displace, axis=3)
    stencil_image = stencil_image + pad_axis(flux_y, 3, 1, 0) - pad_axis(flux_y, 3, 0, 1)
    return free_cells * (displace + relax_factor * (force_field - stencil_image) / diagonal)


def slab_energy(grid_field, along_axis, direction, load_cases):
    change = jnp.diff(grid_field, axis=along_axis)
    return jnp.sum(stiff_factors(direction) * change * change, axis=0) / load_cases


def neighbour_planes(displace, load_cases, axis_devices):
    if axis_devices > load_cases:
        below = from_behind(displace[:, -1:], "space", load_cases)
        above = from_behind(displace[:, :1], "space", -load_cases)
    else:
        below = jnp.zeros_like(displace[:, :1])
        above = jnp.zeros_like(displace[:, :1])
    return jnp.concatenate([below, displace, above], axis=1)


def many_slabs(density, displacement, fixed, load_index, load_force, radius):
    slab_rows, layers, row_width = density.shape
    load_cases = load_index.shape[0]
    level_count = load_cases.bit_length() - 1
    axis_devices = lax.axis_size("space")
    axis_place = lax.axis_index("space")
    slab_planes = slab_rows * load_cases
    slab_place = axis_place // load_cases
    load_place = axis_place % load_cases
    total_rows = slab_rows * axis_devices
    weights = layer_weights(radius)
    padded_weights = pad_axis(weights, 1, window_reach, window_reach)
    global_rows = (
        jnp.arange(slab_rows + 2 * window_reach, dtype=jnp.int32)
        + axis_place * slab_rows
        - window_reach
    )
    deep_inside = ((global_rows >= 0) & (global_rows < total_rows)).astype(jnp.float32)
    inside_field = deep_inside[:, None, None] * pad_sides(
        jnp.ones((slab_rows + 2 * window_reach, layers, row_width), jnp.float32)
    )
    total_weight = filter_forward(inside_field, weights)
    slab_start = slab_place * slab_planes
    margin_rows = jnp.arange(slab_planes + 2, dtype=jnp.int32) + slab_start - 1
    margin_inside = ((margin_rows >= 0) & (margin_rows < total_rows)).astype(jnp.float32)
    face_valid = margin_inside[1:] * margin_inside[:-1]
    fixed_slab = lax.dynamic_slice_in_dim(fixed, slab_start, slab_planes, 0).astype(jnp.float32)
    bottom_layer = (jnp.arange(layers, dtype=jnp.int32) == 0).astype(jnp.float32)
    free_cells = 1.0 - bottom_layer[None, :, None] * fixed_slab[:, None, :]
    slab_cells = slab_planes * layers * row_width
    cell_index = jnp.arange(slab_cells, dtype=jnp.int32) + slab_place * slab_cells
    load_hot = jnp.arange(load_cases, dtype=jnp.int32) == load_place
    own_index = jnp.sum(jnp.where(load_hot, load_index, 0))
    own_force = jnp.sum(load_hot.astype(jnp.float32)[:, None] * load_force, axis=0)
    load_hits = (cell_index == own_index).astype(jnp.float32)
    force_field = (own_force[:, None] * load_hits[None, :]).reshape(
        3, slab_planes, layers, row_width
    )
    displace = displacement[0] * free_cells
    target = volume_share * total_rows * layers * row_width
    padded = neighbour_planes(displace, load_cases, axis_devices)
    halo_density = extended(density, (("space", 0),), window_reach)
    filtered = filter_forward(pad_sides(halo_density), weights) / total_weight
    whole_field = lax.all_gather(filtered, "space", axis=0, tiled=True)
    margin = lax.dynamic_slice_in_dim(
        pad_axis(whole_field, 0, 1, 1), slab_start, slab_planes + 2, 0
    )
    moduli = floor_modulus + (1.0 - floor_modulus) * margin**3
    face_x = 0.5 * (moduli[1:] + moduli[:-1]) * face_valid[:, None, None]
    inner_moduli = moduli[1:-1]
    face_z = 0.5 * (inner_moduli[:, 1:] + inner_moduli[:, :-1])
    face_y = 0.5 * (inner_moduli[:, :, 1:] + inner_moduli[:, :, :-1])
    sum_x = face_x[:-1] + face_x[1:]
    sum_z = pad_axis(face_z, 1, 1, 0) + pad_axis(face_z, 1, 0, 1)
    sum_y = pad_axis(face_y, 2, 1, 0) + pad_axis(face_y, 2, 0, 1)
    diagonal = stiff_factors(0) * sum_x + stiff_factors(1) * sum_z + stiff_factors(2) * sum_y
    for sweep_index in range(SWEEPS):
        displace = relax_slab(
            padded, displace, face_x, face_z, face_y, force_field, free_cells, diagonal
        )
        padded = neighbour_planes(displace, load_cases, axis_devices)
    energy_x = slab_energy(padded, 1, 0, load_cases) * face_valid[:, None, None]
    energy_z = slab_energy(displace, 2, 1, load_cases)
    energy_y = slab_energy(displace, 3, 2, load_cases)
    sens_term = 0.5 * (
        energy_x[:-1]
        + energy_x[1:]
        + pad_axis(energy_z, 1, 1, 0)
        + pad_axis(energy_z, 1, 0, 1)
        + pad_axis(energy_y, 2, 1, 0)
        + pad_axis(energy_y, 2, 0, 1)
    )
    sensitive = sens_term
    for level in reversed(range(level_count)):
        half_rows = sensitive.shape[0] // 2
        upper_side = load_place // 2**level % 2 == 1
        outgoing = jnp.where(upper_side, sensitive[:half_rows], sensitive[half_rows:])
        keeping = jnp.where(upper_side, sensitive[half_rows:], sensitive[:half_rows])
        sensitive = keeping + from_partner(outgoing, "space", level)
    weighted_share = 3.0 * (1.0 - floor_modulus) * filtered**2 * sensitive / total_weight
    halo_share = extended(weighted_share, (("space", 0),), window_reach)
    root_term = jnp.sqrt(filter_backward(pad_sides(halo_share), padded_weights))
    lowest = jnp.maximum(density - move_limit, density_floor)
    highest = jnp.minimum(density + move_limit, 1.0)
    design_now = density

    def trial_design(log_level):
        return jnp.clip(design_now * root_term * jnp.exp(-0.5 * log_level), lowest, highest)

    start_state = (jnp.asarray(log_lower, jnp.float32), jnp.asarray(log_span, jnp.float32))

    def halve(search_step, search_state):
        lower_end, span_width = search_state
        half_span = span_width * 0.5
        middle = lower_end + half_span
        volume_total = lax.psum(jnp.sum(trial_design(middle)), "space")
        return (jnp.where(volume_total > target, middle, lower_end), half_span)

    lower_end, span_width = lax.fori_loop(0, SEARCH, halve, start_state)
    density = trial_design(lower_end + 0.5 * span_width)
    new_displacement = displace[None]
    return (density, new_displacement)


def solution(mesh):
    in_specs = (
        P("space", "parts", None),
        P("space", None, None, "parts", None),
        P(None, "parts"),
        P("parts"),
        P("parts", None),
        P("parts"),
    )
    out_specs = (P("space", "parts", None), P("space", None, None, "parts", None))

    def local(density, displacement, fixed, load_index, load_force, radius):
        alone = lax.axis_size("space") == load_index.shape[0]
        run = one_slab if alone else many_slabs
        return run(density, displacement, fixed, load_index, load_force, radius)

    return jax.shard_map(local, mesh=mesh, in_specs=in_specs, out_specs=out_specs, check_vma=False)
```

```python
import math

import jax
import jax.numpy as jnp
from jax import lax
from jax.experimental import pallas as pl
from jax.experimental.pallas import tpu as pltpu
from jax.sharding import PartitionSpec as P

SWEEPS = 3
SEARCH = 12


floor_modulus = 0.05
relax_factor = 0.6
move_limit = 0.2
density_floor = 0.01
volume_share = 0.5
log_lower = -16.0
log_span = 32.0
window_reach = 2

PLANE_SQUARES = (0, 1, 2, 4, 5, 8)
ALL_SQUARES = (0, 1, 2, 3, 4, 5, 6, 8, 9, 12)


def spot_iota(shape, dim):
    return lax.broadcasted_iota(jnp.int32, shape, dim)


def layer_radius(radius_ref, layers, row_width):
    z = spot_iota((layers, row_width), 0)
    result = jnp.zeros((layers, row_width), jnp.int32)
    for layer in range(layers):
        result = jnp.where(z == layer, radius_ref[layer], result)
    return result.astype(jnp.float32)


def class_weights(radius_ref, weight_ref):
    layers, row_width = weight_ref.shape[1:]
    radial = layer_radius(radius_ref, layers, row_width)
    for place, square in enumerate(ALL_SQUARES):
        weight_ref[place] = jnp.maximum(radial - math.sqrt(square), 0.0)


def shift_sum(field, dim, distance):
    size = field.shape[dim]
    spot = spot_iota(field.shape, dim)
    ahead = jnp.where(spot < size - distance, pltpu.roll(field, size - distance, dim), 0.0)
    behind = jnp.where(spot >= distance, pltpu.roll(field, distance, dim), 0.0)
    return ahead + behind


def plane_sums(plane):
    beside = shift_sum(plane, 1, 1)
    further = shift_sum(plane, 1, 2)
    return {
        0: plane,
        1: beside + shift_sum(plane, 0, 1),
        2: shift_sum(beside, 0, 1),
        4: further + shift_sum(plane, 0, 2),
        5: shift_sum(further, 0, 1) + shift_sum(beside, 0, 2),
        8: shift_sum(further, 0, 2),
    }


def weigh(sums, weight_ref, square):
    result = None
    for inner in PLANE_SQUARES:
        term = weight_ref[ALL_SQUARES.index(inner + square)] * sums[inner]
        result = term if result is None else result + term
    return result


def forward_planes(plane, weight_ref):
    sums = plane_sums(plane)
    return [weigh(sums, weight_ref, square) for square in (0, 1, 4)]


def backward_planes(plane, weight_ref):
    beside = shift_sum(plane, 1, 1)
    further = shift_sum(plane, 1, 2)
    results = []
    for square in (0, 1, 4):

        def weight(more):
            return weight_ref[ALL_SQUARES.index(square + more)]

        level = weight(0) * plane + weight(1) * beside + weight(4) * further
        near = weight(1) * plane + weight(2) * beside + weight(5) * further
        far = weight(4) * plane + weight(5) * beside + weight(8) * further
        results.append(level + shift_sum(near, 0, 1) + shift_sum(far, 0, 2))
    return results


def pair_spot(x, own_planes):
    device = x // own_planes
    core = (device ^ lax.axis_index("space")) & 1
    return core, device >> 1, x % own_planes


def edge_class(x, planes):
    return jnp.minimum(x, 2) + jnp.maximum(x - (planes - 3), 0)


def zero_edges(ref):
    planes = ref.shape[0]
    for place in (0, 1, planes - 2, planes - 1):
        ref[place] = jnp.zeros(ref.shape[1:], ref.dtype)


def sweep_kernel(
    radius_ref,
    index_ref,
    force_ref,
    density_ref,
    fixed_ref,
    start_ref,
    disp_ref,
    sens_ref,
    coef_ref,
    weight_ref,
    total_ref,
    near_ref,
    side_ref,
    far_ref,
    modulus_ref,
    across_ref,
    up_ref,
    down_ref,
    right_ref,
    left_ref,
    rate_ref,
    keep_ref,
    first_ref,
    second_ref,
):
    cores, chips, own_planes, layers, row_width = density_ref.shape
    planes = cores * chips * own_planes
    load_cases = index_ref.shape[0]
    load_place = lax.axis_index("space")
    shape = (layers, row_width)
    z = spot_iota(shape, 0)
    y = spot_iota(shape, 1)
    zero = jnp.zeros(shape, jnp.float32)

    class_weights(radius_ref, weight_ref)
    for ref in (side_ref, far_ref):
        zero_edges(ref)

    ones = forward_planes(jnp.ones(shape, jnp.float32), weight_ref)
    for place, (lower, upper) in enumerate(((0, 2), (1, 2), (2, 2), (2, 1), (2, 0))):
        total_ref[place] = (
            ones[0] + min(lower, 1) * ones[1] + min(upper, 1) * ones[1]
            + (lower // 2) * ones[2] + (upper // 2) * ones[2]
        )

    def filter_plane(x, carry):
        near, side, far = forward_planes(
            density_ref[pair_spot(x, own_planes)], weight_ref
        )
        near_ref[x + 2] = near
        side_ref[x + 2] = side
        far_ref[x + 2] = far
        return carry

    lax.fori_loop(0, planes, filter_plane, 0, unroll=8)

    def modulus_plane(x, carry):
        total = total_ref[edge_class(x, planes)]
        filtered = (
            near_ref[x + 2]
            + side_ref[x + 1]
            + side_ref[x + 3]
            + far_ref[x]
            + far_ref[x + 4]
        ) / total
        modulus = floor_modulus + (1.0 - floor_modulus) * (filtered * filtered * filtered)
        modulus_ref[x] = modulus
        coef_ref[x] = 3.0 * (1.0 - floor_modulus) * (filtered * filtered) / total
        return carry

    lax.fori_loop(0, planes, modulus_plane, 0, unroll=8)

    across_ref[0] = zero
    across_ref[planes] = zero
    first_ref[:, 0] = jnp.zeros((3,) + shape, jnp.float32)
    second_ref[:, 0] = jnp.zeros((3,) + shape, jnp.float32)
    first_ref[:, planes + 1] = jnp.zeros((3,) + shape, jnp.float32)
    second_ref[:, planes + 1] = jnp.zeros((3,) + shape, jnp.float32)

    def face_plane(x, carry):
        modulus = modulus_ref[x]
        later = modulus_ref[jnp.minimum(x + 1, planes - 1)]
        ahead = jnp.where(x + 1 < planes, 0.5 * (modulus + later), 0.0)
        across_ref[x + 1] = ahead
        up = jnp.where(z < layers - 1, 0.5 * (modulus + pltpu.roll(modulus, layers - 1, 0)), 0.0)
        down = pltpu.roll(up, 1, 0)
        right = jnp.where(
            y < row_width - 1, 0.5 * (modulus + pltpu.roll(modulus, row_width - 1, 1)), 0.0
        )
        left = pltpu.roll(right, 1, 1)
        up_ref[x] = up
        down_ref[x] = down
        right_ref[x] = right
        left_ref[x] = left
        free = jnp.where(z == 0, 1.0 - fixed_ref[pl.ds(x, 1), :].astype(jnp.float32), 1.0)
        keep_ref[x] = (1.0 - relax_factor) * free
        sums = (carry + ahead, up + down, left + right)
        every = sums[0] + sums[1] + sums[2]
        push = relax_factor * free
        for part in range(3):
            rate_ref[part, x] = push / (every + sums[part])
            first_ref[part, x + 1] = start_ref[part, x] * free
        return ahead

    lax.fori_loop(0, planes, face_plane, zero, unroll=8)

    own_index = index_ref[load_place]
    own_x = own_index // (layers * row_width)
    own_z = own_index // row_width % layers
    own_y = own_index % row_width
    hit = (z == own_z) & (y == own_y)

    def sweep(source, target, lead):
        def sweep_plane(x, carry):
            before, after = across_ref[x], across_ref[x + 1]
            up, down, right, left = up_ref[x], down_ref[x], right_ref[x], left_ref[x]
            keep = keep_ref[x]
            for part in range(3):
                here = source[part, x + 1]
                pulls = [
                    before * source[part, x] + after * source[part, x + 2],
                    up * pltpu.roll(here, layers - 1, 0) + down * pltpu.roll(here, 1, 0),
                    right * pltpu.roll(here, row_width - 1, 1) + left * pltpu.roll(here, 1, 1),
                ]
                pull = pulls[0] + pulls[1] + pulls[2] + pulls[part]
                target[part, x + lead] = keep * here + rate_ref[part, x] * pull
            return carry

        lax.fori_loop(0, planes, sweep_plane, 0, unroll=8)
        for part in range(3):
            push = rate_ref[part, own_x] * force_ref[load_place, part]
            target[part, own_x + lead] += jnp.where(hit, push, 0.0)

    stages = [first_ref, second_ref]
    for turn in range(SWEEPS - 1):
        sweep(stages[turn % 2], stages[(turn + 1) % 2], 1)
    sweep(stages[(SWEEPS - 1) % 2], disp_ref, 0)

    def energy_plane(x, carry):
        later = jnp.minimum(x + 1, planes - 1)
        ahead, upward, right = zero, zero, zero
        for part in range(3):
            here = disp_ref[part, x]
            step = disp_ref[part, later] - here
            climb = pltpu.roll(here, layers - 1, 0) - here
            slide = pltpu.roll(here, row_width - 1, 1) - here
            ahead = ahead + (2.0 if part == 0 else 1.0) * (step * step)
            upward = upward + (2.0 if part == 1 else 1.0) * (climb * climb)
            right = right + (2.0 if part == 2 else 1.0) * (slide * slide)
        upward = jnp.where(z < layers - 1, upward, 0.0)
        right = jnp.where(y < row_width - 1, right, 0.0)
        total = carry + ahead + upward + pltpu.roll(upward, 1, 0) + right + pltpu.roll(right, 1, 1)
        sens_ref[pair_spot(x, own_planes)] = (0.5 / load_cases) * total
        return ahead

    lax.fori_loop(0, planes, energy_plane, zero, unroll=8)


def design_kernel(
    radius_ref,
    sens_ref,
    coef_ref,
    density_ref,
    new_ref,
    weight_ref,
    near_ref,
    side_ref,
    far_ref,
    pull_ref,
    low_ref,
    high_ref,
):
    cores, chips, own_planes, layers, row_width = density_ref.shape
    planes = cores * chips * own_planes
    place = lax.axis_index("space")
    shape = (layers, row_width)
    zero = jnp.zeros(shape, jnp.float32)
    class_weights(radius_ref, weight_ref)
    for ref in (side_ref, far_ref):
        zero_edges(ref)

    def filter_plane(x, carry):
        near, side, far = backward_planes(
            sens_ref[pair_spot(x, own_planes)] * coef_ref[x], weight_ref
        )
        near_ref[x + 2] = near
        side_ref[x + 2] = side
        far_ref[x + 2] = far
        return carry

    lax.fori_loop(0, planes, filter_plane, 0, unroll=8)

    def root_plane(x, carry):
        root = jnp.sqrt(
            near_ref[x + 2] + side_ref[x + 1] + side_ref[x + 3] + far_ref[x] + far_ref[x + 4]
        )
        density = density_ref[pair_spot(x, own_planes)]
        pull_ref[x] = density * root
        low_ref[x] = jnp.maximum(density - move_limit, density_floor)
        high_ref[x] = jnp.minimum(density + move_limit, 1.0)
        return carry

    lax.fori_loop(0, planes, root_plane, 0, unroll=8)

    target = volume_share * planes * layers * row_width

    def trial(x, factor):
        return jnp.minimum(jnp.maximum(pull_ref[x] * factor, low_ref[x]), high_ref[x])

    def halve(step, state):
        lower, span = state
        half = span * 0.5
        middle = lower + half
        factor = jnp.exp(-0.5 * middle)
        total = lax.fori_loop(
            0, planes, lambda x, acc: acc + trial(x, factor), zero, unroll=8
        )
        volume = jnp.sum(jnp.sum(total, axis=0, keepdims=True), axis=1, keepdims=True)
        return jnp.where(volume > target, middle, lower), half

    start = (jnp.full((1, 1), log_lower, jnp.float32), jnp.full((1, 1), log_span, jnp.float32))
    lower, span = lax.fori_loop(0, SEARCH, halve, start)
    factor = jnp.exp(-0.5 * (lower + 0.5 * span))
    for own in range(own_planes):
        new_ref[own] = trial(place * own_planes + own, factor)


def in_vmem():
    return pl.BlockSpec(memory_space=pltpu.VMEM)


def in_smem():
    return pl.BlockSpec(memory_space=pltpu.SMEM)


KERNEL_VMEM = 24 * 2**20


def sweep_call(radius, load_index, load_force, density, fixed, displacement):
    cores, chips, own_planes, layers, row_width = density.shape
    planes = cores * chips * own_planes
    grid_field = (planes, layers, row_width)

    def scratch(*lead):
        return pltpu.VMEM(lead + (layers, row_width), jnp.float32)

    return pl.pallas_call(
        sweep_kernel,
        out_shape=[
            jax.ShapeDtypeStruct((3,) + grid_field, jnp.float32),
            jax.ShapeDtypeStruct(density.shape, jnp.float32),
            jax.ShapeDtypeStruct(grid_field, jnp.float32),
        ],
        in_specs=[in_smem()] * 3 + [in_vmem()] * 3,
        out_specs=[in_vmem()] * 3,
        scratch_shapes=[
            scratch(len(ALL_SQUARES)),
            scratch(2 * window_reach + 1),
            scratch(planes + 4),
            scratch(planes + 4),
            scratch(planes + 4),
            scratch(planes),
            scratch(planes + 1),
            scratch(planes),
            scratch(planes),
            scratch(planes),
            scratch(planes),
            scratch(3, planes),
            scratch(planes),
            scratch(3, planes + 2),
            scratch(3, planes + 2),
        ],
        compiler_params=pltpu.CompilerParams(vmem_limit_bytes=KERNEL_VMEM),
        name="sweeps",
    )(radius, load_index, load_force, density, fixed, displacement)


def design_call(radius, sens, coef, density):
    cores, chips, own_planes, layers, row_width = density.shape
    planes = cores * chips * own_planes

    def scratch(*lead):
        return pltpu.VMEM(lead + (layers, row_width), jnp.float32)

    return pl.pallas_call(
        design_kernel,
        out_shape=jax.ShapeDtypeStruct((own_planes, layers, row_width), jnp.float32),
        in_specs=[in_smem()] + [in_vmem()] * 3,
        out_specs=in_vmem(),
        scratch_shapes=[
            scratch(len(ALL_SQUARES)),
            scratch(planes + 4),
            scratch(planes + 4),
            scratch(planes + 4),
            scratch(planes),
            scratch(planes),
            scratch(planes),
        ],
        compiler_params=pltpu.CompilerParams(vmem_limit_bytes=KERNEL_VMEM),
        name="design",
    )(radius, sens, coef, density)


def other_core(block):
    devices = lax.axis_size("space")
    return lax.ppermute(block, "space", [(i, i ^ 1) for i in range(devices)])


def between_chips(pieces):
    devices = lax.axis_size("space")
    groups = [list(range(core, devices, 2)) for core in range(2)]
    return lax.all_to_all(pieces, "space", 0, 0, axis_index_groups=groups)


def gathered(block):
    chips = lax.axis_size("space") // 2
    same = between_chips(jnp.broadcast_to(block[None], (chips,) + block.shape))
    return jnp.stack([same, other_core(same)])


def scattered_sum(pieces):
    return jnp.sum(between_chips(pieces[0] + other_core(pieces[1])), axis=0)


def one_slab(density, displacement, fixed, load_index, load_force, radius):
    whole = gathered(density)
    new_displacement, sens, coef = sweep_call(
        radius, load_index, load_force, whole, fixed, displacement[0]
    )
    sens = gathered(scattered_sum(sens))
    new_density = design_call(radius, sens, coef, whole)
    return new_density, new_displacement[None]


def from_behind(block, axis, distance):
    devices = range(lax.axis_size(axis))
    route = [(i - distance, i) for i in devices if i - distance in devices]
    return lax.ppermute(block, axis, route)


def extended(x, sides, width):
    for axis, dim in sides:
        size, length = (lax.axis_size(axis), x.shape[dim])
        up = [(i, (i + 1) % size) for i in range(size - 1)]
        down = [(j, i) for i, j in up]
        last = lax.slice_in_dim(x, length - width, length, axis=dim)
        first = lax.slice_in_dim(x, 0, width, axis=dim)
        before = lax.ppermute(last, axis, up)
        after = lax.ppermute(first, axis, down)
        x = jnp.concatenate([before, x, after], axis=dim)
    return x


def from_partner(x, axis, bit):
    return lax.ppermute(x, axis, [(i, i ^ 1 << bit) for i in range(lax.axis_size(axis))])


def window_offsets():
    offsets_list = []
    for across in range(-window_reach, window_reach + 1):
        for upward in range(-window_reach, window_reach + 1):
            for sideways in range(-window_reach, window_reach + 1):
                length = math.sqrt(across * across + upward * upward + sideways * sideways)
                offsets_list.append((across, upward, sideways, length))
    return offsets_list


def layer_weights(radius):
    radial = radius.astype(jnp.float32)
    return jnp.stack(
        [jnp.maximum(radial - length, 0.0) for across, upward, sideways, length in window_offsets()]
    )


def pad_axis(grid_field, along_axis, before, after_cells):
    widths = [(0, 0)] * grid_field.ndim
    widths[along_axis] = (before, after_cells)
    return jnp.pad(grid_field, widths)


def pad_sides(grid_field):
    return jnp.pad(grid_field, ((0, 0), (window_reach, window_reach), (window_reach, window_reach)))


def filter_forward(padded, weights):
    out_rows = padded.shape[0] - 2 * window_reach
    layers = padded.shape[1] - 2 * window_reach
    row_width = padded.shape[2] - 2 * window_reach
    result = jnp.zeros((out_rows, layers, row_width), jnp.float32)
    for offset_index, (across, upward, sideways, length) in enumerate(window_offsets()):
        shifted = padded[
            window_reach + across : window_reach + across + out_rows,
            window_reach + upward : window_reach + upward + layers,
            window_reach + sideways : window_reach + sideways + row_width,
        ]
        result = result + weights[offset_index][None, :, None] * shifted
    return result


def filter_backward(padded, padded_weights):
    out_rows = padded.shape[0] - 2 * window_reach
    layers = padded.shape[1] - 2 * window_reach
    row_width = padded.shape[2] - 2 * window_reach
    result = jnp.zeros((out_rows, layers, row_width), jnp.float32)
    for offset_index, (across, upward, sideways, length) in enumerate(window_offsets()):
        shifted = padded[
            window_reach - across : window_reach - across + out_rows,
            window_reach - upward : window_reach - upward + layers,
            window_reach - sideways : window_reach - sideways + row_width,
        ]
        layer_part = padded_weights[
            offset_index, window_reach - upward : window_reach - upward + layers
        ]
        result = result + layer_part[None, :, None] * shifted
    return result


def stiff_factors(direction):
    return jnp.array(
        [2.0 if component == direction else 1.0 for component in range(3)], jnp.float32
    ).reshape(3, 1, 1, 1)


def relax_slab(padded, displace, face_x, face_z, face_y, force_field, free_cells, diagonal):
    flux_x = stiff_factors(0) * face_x * jnp.diff(padded, axis=1)
    stencil_image = flux_x[:, :-1] - flux_x[:, 1:]
    flux_z = stiff_factors(1) * face_z * jnp.diff(displace, axis=2)
    stencil_image = stencil_image + pad_axis(flux_z, 2, 1, 0) - pad_axis(flux_z, 2, 0, 1)
    flux_y = stiff_factors(2) * face_y * jnp.diff(displace, axis=3)
    stencil_image = stencil_image + pad_axis(flux_y, 3, 1, 0) - pad_axis(flux_y, 3, 0, 1)
    return free_cells * (displace + relax_factor * (force_field - stencil_image) / diagonal)


def slab_energy(grid_field, along_axis, direction, load_cases):
    change = jnp.diff(grid_field, axis=along_axis)
    return jnp.sum(stiff_factors(direction) * change * change, axis=0) / load_cases


def neighbour_planes(displace, load_cases, axis_devices):
    if axis_devices > load_cases:
        below = from_behind(displace[:, -1:], "space", load_cases)
        above = from_behind(displace[:, :1], "space", -load_cases)
    else:
        below = jnp.zeros_like(displace[:, :1])
        above = jnp.zeros_like(displace[:, :1])
    return jnp.concatenate([below, displace, above], axis=1)


def many_slabs(density, displacement, fixed, load_index, load_force, radius):
    slab_rows, layers, row_width = density.shape
    load_cases = load_index.shape[0]
    level_count = load_cases.bit_length() - 1
    axis_devices = lax.axis_size("space")
    axis_place = lax.axis_index("space")
    slab_planes = slab_rows * load_cases
    slab_place = axis_place // load_cases
    load_place = axis_place % load_cases
    total_rows = slab_rows * axis_devices
    weights = layer_weights(radius)
    padded_weights = pad_axis(weights, 1, window_reach, window_reach)
    global_rows = (
        jnp.arange(slab_rows + 2 * window_reach, dtype=jnp.int32)
        + axis_place * slab_rows
        - window_reach
    )
    deep_inside = ((global_rows >= 0) & (global_rows < total_rows)).astype(jnp.float32)
    inside_field = deep_inside[:, None, None] * pad_sides(
        jnp.ones((slab_rows + 2 * window_reach, layers, row_width), jnp.float32)
    )
    total_weight = filter_forward(inside_field, weights)
    slab_start = slab_place * slab_planes
    margin_rows = jnp.arange(slab_planes + 2, dtype=jnp.int32) + slab_start - 1
    margin_inside = ((margin_rows >= 0) & (margin_rows < total_rows)).astype(jnp.float32)
    face_valid = margin_inside[1:] * margin_inside[:-1]
    fixed_slab = lax.dynamic_slice_in_dim(fixed, slab_start, slab_planes, 0).astype(jnp.float32)
    bottom_layer = (jnp.arange(layers, dtype=jnp.int32) == 0).astype(jnp.float32)
    free_cells = 1.0 - bottom_layer[None, :, None] * fixed_slab[:, None, :]
    slab_cells = slab_planes * layers * row_width
    cell_index = jnp.arange(slab_cells, dtype=jnp.int32) + slab_place * slab_cells
    load_hot = jnp.arange(load_cases, dtype=jnp.int32) == load_place
    own_index = jnp.sum(jnp.where(load_hot, load_index, 0))
    own_force = jnp.sum(load_hot.astype(jnp.float32)[:, None] * load_force, axis=0)
    load_hits = (cell_index == own_index).astype(jnp.float32)
    force_field = (own_force[:, None] * load_hits[None, :]).reshape(
        3, slab_planes, layers, row_width
    )
    displace = displacement[0] * free_cells
    target = volume_share * total_rows * layers * row_width
    padded = neighbour_planes(displace, load_cases, axis_devices)
    halo_density = extended(density, (("space", 0),), window_reach)
    filtered = filter_forward(pad_sides(halo_density), weights) / total_weight
    whole_field = lax.all_gather(filtered, "space", axis=0, tiled=True)
    margin = lax.dynamic_slice_in_dim(
        pad_axis(whole_field, 0, 1, 1), slab_start, slab_planes + 2, 0
    )
    moduli = floor_modulus + (1.0 - floor_modulus) * margin**3
    face_x = 0.5 * (moduli[1:] + moduli[:-1]) * face_valid[:, None, None]
    inner_moduli = moduli[1:-1]
    face_z = 0.5 * (inner_moduli[:, 1:] + inner_moduli[:, :-1])
    face_y = 0.5 * (inner_moduli[:, :, 1:] + inner_moduli[:, :, :-1])
    sum_x = face_x[:-1] + face_x[1:]
    sum_z = pad_axis(face_z, 1, 1, 0) + pad_axis(face_z, 1, 0, 1)
    sum_y = pad_axis(face_y, 2, 1, 0) + pad_axis(face_y, 2, 0, 1)
    diagonal = stiff_factors(0) * sum_x + stiff_factors(1) * sum_z + stiff_factors(2) * sum_y
    for sweep_index in range(SWEEPS):
        displace = relax_slab(
            padded, displace, face_x, face_z, face_y, force_field, free_cells, diagonal
        )
        padded = neighbour_planes(displace, load_cases, axis_devices)
    energy_x = slab_energy(padded, 1, 0, load_cases) * face_valid[:, None, None]
    energy_z = slab_energy(displace, 2, 1, load_cases)
    energy_y = slab_energy(displace, 3, 2, load_cases)
    sens_term = 0.5 * (
        energy_x[:-1]
        + energy_x[1:]
        + pad_axis(energy_z, 1, 1, 0)
        + pad_axis(energy_z, 1, 0, 1)
        + pad_axis(energy_y, 2, 1, 0)
        + pad_axis(energy_y, 2, 0, 1)
    )
    sensitive = sens_term
    for level in reversed(range(level_count)):
        half_rows = sensitive.shape[0] // 2
        upper_side = load_place // 2**level % 2 == 1
        outgoing = jnp.where(upper_side, sensitive[:half_rows], sensitive[half_rows:])
        keeping = jnp.where(upper_side, sensitive[half_rows:], sensitive[:half_rows])
        sensitive = keeping + from_partner(outgoing, "space", level)
    weighted_share = 3.0 * (1.0 - floor_modulus) * filtered**2 * sensitive / total_weight
    halo_share = extended(weighted_share, (("space", 0),), window_reach)
    root_term = jnp.sqrt(filter_backward(pad_sides(halo_share), padded_weights))
    lowest = jnp.maximum(density - move_limit, density_floor)
    highest = jnp.minimum(density + move_limit, 1.0)
    design_now = density

    def trial_design(log_level):
        return jnp.clip(design_now * root_term * jnp.exp(-0.5 * log_level), lowest, highest)

    start_state = (jnp.asarray(log_lower, jnp.float32), jnp.asarray(log_span, jnp.float32))

    def halve(search_step, search_state):
        lower_end, span_width = search_state
        half_span = span_width * 0.5
        middle = lower_end + half_span
        volume_total = lax.psum(jnp.sum(trial_design(middle)), "space")
        return (jnp.where(volume_total > target, middle, lower_end), half_span)

    lower_end, span_width = lax.fori_loop(0, SEARCH, halve, start_state)
    density = trial_design(lower_end + 0.5 * span_width)
    new_displacement = displace[None]
    return (density, new_displacement)


def solution(mesh):
    in_specs = (
        P("space", "parts", None),
        P("space", None, None, "parts", None),
        P(None, "parts"),
        P("parts"),
        P("parts", None),
        P("parts"),
    )
    out_specs = (P("space", "parts", None), P("space", None, None, "parts", None))

    def local(density, displacement, fixed, load_index, load_force, radius):
        alone = lax.axis_size("space") == load_index.shape[0]
        run = one_slab if alone else many_slabs
        return run(density, displacement, fixed, load_index, load_force, radius)

    return jax.shard_map(local, mesh=mesh, in_specs=in_specs, out_specs=out_specs, check_vma=False)
```

```python
import math

import jax
import jax.numpy as jnp
from jax import lax
from jax.experimental import pallas as pl
from jax.experimental.pallas import tpu as pltpu
from jax.sharding import PartitionSpec as P

SWEEPS = 3
SEARCH = 12


floor_modulus = 0.05
relax_factor = 0.6
move_limit = 0.2
density_floor = 0.01
volume_share = 0.5
log_lower = -16.0
log_span = 32.0
window_reach = 2

PLANE_SQUARES = (0, 1, 2, 4, 5, 8)
ALL_SQUARES = (0, 1, 2, 3, 4, 5, 6, 8, 9, 12)


def spot_iota(shape, dim):
    return lax.broadcasted_iota(jnp.int32, shape, dim)


def layer_radius(radius_ref, layers, row_width):
    z = spot_iota((layers, row_width), 0)
    result = jnp.zeros((layers, row_width), jnp.int32)
    for layer in range(layers):
        result = jnp.where(z == layer, radius_ref[layer], result)
    return result.astype(jnp.float32)


def class_weights(radius_ref, weight_ref):
    layers, row_width = weight_ref.shape[1:]
    radial = layer_radius(radius_ref, layers, row_width)
    for place, square in enumerate(ALL_SQUARES):
        weight_ref[place] = jnp.maximum(radial - math.sqrt(square), 0.0)


def shift_sum(field, dim, distance):
    size = field.shape[dim]
    spot = spot_iota(field.shape, dim)
    ahead = jnp.where(spot < size - distance, pltpu.roll(field, size - distance, dim), 0.0)
    behind = jnp.where(spot >= distance, pltpu.roll(field, distance, dim), 0.0)
    return ahead + behind


def plane_sums(plane):
    beside = shift_sum(plane, 1, 1)
    further = shift_sum(plane, 1, 2)
    return {
        0: plane,
        1: beside + shift_sum(plane, 0, 1),
        2: shift_sum(beside, 0, 1),
        4: further + shift_sum(plane, 0, 2),
        5: shift_sum(further, 0, 1) + shift_sum(beside, 0, 2),
        8: shift_sum(further, 0, 2),
    }


def weigh(sums, weight_ref, square):
    result = None
    for inner in PLANE_SQUARES:
        term = weight_ref[ALL_SQUARES.index(inner + square)] * sums[inner]
        result = term if result is None else result + term
    return result


def forward_planes(plane, weight_ref):
    sums = plane_sums(plane)
    return [weigh(sums, weight_ref, square) for square in (0, 1, 4)]


def backward_planes(plane, weight_ref):
    beside = shift_sum(plane, 1, 1)
    further = shift_sum(plane, 1, 2)
    results = []
    for square in (0, 1, 4):

        def weight(more):
            return weight_ref[ALL_SQUARES.index(square + more)]

        level = weight(0) * plane + weight(1) * beside + weight(4) * further
        near = weight(1) * plane + weight(2) * beside + weight(5) * further
        far = weight(4) * plane + weight(5) * beside + weight(8) * further
        results.append(level + shift_sum(near, 0, 1) + shift_sum(far, 0, 2))
    return results


def pair_spot(x, own_planes):
    device = x // own_planes
    core = (device ^ lax.axis_index("space")) & 1
    return core, device >> 1, x % own_planes


def edge_class(x, planes):
    return jnp.minimum(x, 2) + jnp.maximum(x - (planes - 3), 0)


def zero_edges(ref):
    planes = ref.shape[0]
    for place in (0, 1, planes - 2, planes - 1):
        ref[place] = jnp.zeros(ref.shape[1:], ref.dtype)


def prepare_kernel(
    radius_ref,
    index_ref,
    force_ref,
    fixed_ref,
    start_ref,
    weight_ref,
    total_ref,
    first_ref,
    push_ref,
    load_ref,
    spot_ref,
):
    planes, layers, row_width = start_ref.shape[1:]
    load_place = lax.axis_index("space")
    shape = (layers, row_width)
    z = spot_iota(shape, 0)
    y = spot_iota(shape, 1)

    class_weights(radius_ref, weight_ref)
    ones = forward_planes(jnp.ones(shape, jnp.float32), weight_ref)
    for place, (lower, upper) in enumerate(((0, 2), (1, 2), (2, 2), (2, 1), (2, 0))):
        total_ref[place] = (
            ones[0] + min(lower, 1) * ones[1] + min(upper, 1) * ones[1]
            + (lower // 2) * ones[2] + (upper // 2) * ones[2]
        )

    def free_plane(x, carry):
        free = jnp.where(z == 0, 1.0 - fixed_ref[pl.ds(x, 1), :].astype(jnp.float32), 1.0)
        push_ref[x] = relax_factor * free
        for part in range(3):
            first_ref[part, x + 1] = start_ref[part, x] * free
        return carry

    lax.fori_loop(0, planes, free_plane, 0, unroll=8)
    for part in range(3):
        first_ref[part, 0] = jnp.zeros(shape, jnp.float32)
        first_ref[part, planes + 1] = jnp.zeros(shape, jnp.float32)

    own_index = index_ref[load_place]
    own_z = own_index // row_width % layers
    own_y = own_index % row_width
    hit = (z == own_z) & (y == own_y)
    for part in range(3):
        load_ref[part] = jnp.where(hit, force_ref[part, load_place], 0.0)
    spot_ref[0] = own_index // (layers * row_width)


def sweep_kernel(
    spot_ref,
    load_ref,
    weight_ref,
    total_ref,
    push_ref,
    density_ref,
    first_ref,
    disp_ref,
    sens_ref,
    coef_ref,
    near_ref,
    side_ref,
    far_ref,
    modulus_ref,
    across_ref,
    up_ref,
    down_ref,
    right_ref,
    left_ref,
    rate_ref,
    second_ref,
    third_ref,
):
    cores, chips, own_planes, layers, row_width = density_ref.shape
    planes = cores * chips * own_planes
    load_cases = lax.axis_size("space")
    shape = (layers, row_width)
    z = spot_iota(shape, 0)
    y = spot_iota(shape, 1)
    zero = jnp.zeros(shape, jnp.float32)

    for ref in (side_ref, far_ref):
        zero_edges(ref)

    def filter_plane(x, carry):
        near, side, far = forward_planes(
            density_ref[pair_spot(x, own_planes)], weight_ref
        )
        near_ref[x + 2] = near
        side_ref[x + 2] = side
        far_ref[x + 2] = far
        return carry

    lax.fori_loop(0, planes, filter_plane, 0, unroll=8)

    def modulus_plane(x, carry):
        total = total_ref[edge_class(x, planes)]
        filtered = (
            near_ref[x + 2]
            + side_ref[x + 1]
            + side_ref[x + 3]
            + far_ref[x]
            + far_ref[x + 4]
        ) / total
        modulus = floor_modulus + (1.0 - floor_modulus) * (filtered * filtered * filtered)
        modulus_ref[x] = modulus
        coef_ref[x] = 3.0 * (1.0 - floor_modulus) * (filtered * filtered) / total
        return carry

    lax.fori_loop(0, planes, modulus_plane, 0, unroll=8)

    across_ref[0] = zero
    across_ref[planes] = zero
    for ref in (second_ref, third_ref):
        for part in range(3):
            ref[part, 0] = zero
            ref[part, planes + 1] = zero

    def face_plane(x, carry):
        modulus = modulus_ref[x]
        later = modulus_ref[jnp.minimum(x + 1, planes - 1)]
        ahead = jnp.where(x + 1 < planes, 0.5 * (modulus + later), 0.0)
        across_ref[x + 1] = ahead
        up = jnp.where(z < layers - 1, 0.5 * (modulus + pltpu.roll(modulus, layers - 1, 0)), 0.0)
        down = pltpu.roll(up, 1, 0)
        right = jnp.where(
            y < row_width - 1, 0.5 * (modulus + pltpu.roll(modulus, row_width - 1, 1)), 0.0
        )
        left = pltpu.roll(right, 1, 1)
        up_ref[x] = up
        down_ref[x] = down
        right_ref[x] = right
        left_ref[x] = left
        sums = (carry + ahead, up + down, left + right)
        every = sums[0] + sums[1] + sums[2]
        push = push_ref[x]
        for part in range(3):
            rate_ref[part, x] = push / (every + sums[part])
        return ahead

    lax.fori_loop(0, planes, face_plane, zero, unroll=8)

    own_x = spot_ref[0]

    def sweep(source, target, lead):
        def sweep_plane(x, carry):
            before, after = across_ref[x], across_ref[x + 1]
            up, down, right, left = up_ref[x], down_ref[x], right_ref[x], left_ref[x]
            for part in range(3):
                here = source[part, x + 1]
                pulls = [
                    before * source[part, x] + after * source[part, x + 2],
                    up * pltpu.roll(here, layers - 1, 0) + down * pltpu.roll(here, 1, 0),
                    right * pltpu.roll(here, row_width - 1, 1) + left * pltpu.roll(here, 1, 1),
                ]
                pull = pulls[0] + pulls[1] + pulls[2] + pulls[part]
                target[part, x + lead] = (1.0 - relax_factor) * here + rate_ref[part, x] * pull
            return carry

        lax.fori_loop(0, planes, sweep_plane, 0, unroll=8)
        for part in range(3):
            target[part, own_x + lead] += rate_ref[part, own_x] * load_ref[part]

    source = first_ref
    for turn in range(SWEEPS - 1):
        target = (second_ref, third_ref)[turn % 2]
        sweep(source, target, 1)
        source = target
    sweep(source, disp_ref, 0)

    def energy_plane(x, carry):
        later = jnp.minimum(x + 1, planes - 1)
        ahead, upward, right = zero, zero, zero
        for part in range(3):
            here = disp_ref[part, x]
            step = disp_ref[part, later] - here
            climb = pltpu.roll(here, layers - 1, 0) - here
            slide = pltpu.roll(here, row_width - 1, 1) - here
            ahead = ahead + (2.0 if part == 0 else 1.0) * (step * step)
            upward = upward + (2.0 if part == 1 else 1.0) * (climb * climb)
            right = right + (2.0 if part == 2 else 1.0) * (slide * slide)
        upward = jnp.where(z < layers - 1, upward, 0.0)
        right = jnp.where(y < row_width - 1, right, 0.0)
        total = carry + ahead + upward + pltpu.roll(upward, 1, 0) + right + pltpu.roll(right, 1, 1)
        sens_ref[pair_spot(x, own_planes)] = (0.5 / load_cases) * total
        return ahead

    lax.fori_loop(0, planes, energy_plane, zero, unroll=8)


def design_kernel(
    weight_ref,
    sens_ref,
    coef_ref,
    density_ref,
    new_ref,
    near_ref,
    side_ref,
    far_ref,
    pull_ref,
    low_ref,
    high_ref,
):
    cores, chips, own_planes, layers, row_width = density_ref.shape
    planes = cores * chips * own_planes
    place = lax.axis_index("space")
    shape = (layers, row_width)
    zero = jnp.zeros(shape, jnp.float32)
    for ref in (side_ref, far_ref):
        zero_edges(ref)

    def filter_plane(x, carry):
        near, side, far = backward_planes(
            sens_ref[pair_spot(x, own_planes)] * coef_ref[x], weight_ref
        )
        near_ref[x + 2] = near
        side_ref[x + 2] = side
        far_ref[x + 2] = far
        return carry

    lax.fori_loop(0, planes, filter_plane, 0, unroll=8)

    def root_plane(x, carry):
        root = jnp.sqrt(
            near_ref[x + 2] + side_ref[x + 1] + side_ref[x + 3] + far_ref[x] + far_ref[x + 4]
        )
        density = density_ref[pair_spot(x, own_planes)]
        pull_ref[x] = density * root
        low_ref[x] = jnp.maximum(density - move_limit, density_floor)
        high_ref[x] = jnp.minimum(density + move_limit, 1.0)
        return carry

    lax.fori_loop(0, planes, root_plane, 0, unroll=8)

    target = volume_share * planes * layers * row_width

    def trial(x, factor):
        return jnp.minimum(jnp.maximum(pull_ref[x] * factor, low_ref[x]), high_ref[x])

    def halve(step, state):
        lower, span = state
        half = span * 0.5
        middle = lower + half
        factor = jnp.exp(-0.5 * middle)
        total = lax.fori_loop(
            0, planes, lambda x, acc: acc + trial(x, factor), zero, unroll=8
        )
        volume = jnp.sum(jnp.sum(total, axis=0, keepdims=True), axis=1, keepdims=True)
        return jnp.where(volume > target, middle, lower), half

    start = (jnp.full((1, 1), log_lower, jnp.float32), jnp.full((1, 1), log_span, jnp.float32))
    lower, span = lax.fori_loop(0, SEARCH, halve, start)
    factor = jnp.exp(-0.5 * (lower + 0.5 * span))
    for own in range(own_planes):
        new_ref[own] = trial(place * own_planes + own, factor)


def in_vmem():
    return pl.BlockSpec(memory_space=pltpu.VMEM)


def in_smem():
    return pl.BlockSpec(memory_space=pltpu.SMEM)


KERNEL_VMEM = 24 * 2**20


def floats(*shape):
    return jax.ShapeDtypeStruct(shape, jnp.float32)


def prepare_call(radius, load_index, load_force, fixed, displacement):
    planes, layers, row_width = displacement.shape[1:]
    return pl.pallas_call(
        prepare_kernel,
        out_shape=[
            floats(len(ALL_SQUARES), layers, row_width),
            floats(2 * window_reach + 1, layers, row_width),
            floats(3, planes + 2, layers, row_width),
            floats(planes, layers, row_width),
            floats(3, layers, row_width),
            jax.ShapeDtypeStruct((1,), jnp.int32),
        ],
        in_specs=[in_smem()] * 3 + [in_vmem()] * 2,
        out_specs=[in_vmem()] * 5 + [in_smem()],
        compiler_params=pltpu.CompilerParams(vmem_limit_bytes=KERNEL_VMEM),
        cost_estimate=pl.CostEstimate(
            flops=4 * displacement.size,
            bytes_accessed=8 * displacement.size,
            transcendentals=0,
        ),
        name="prepare",
    )(radius, load_index, load_force, fixed, displacement)


def sweep_call(spot, load, weights, totals, push, density, first):
    cores, chips, own_planes, layers, row_width = density.shape
    planes = cores * chips * own_planes

    def scratch(*lead):
        return pltpu.VMEM(lead + (layers, row_width), jnp.float32)

    return pl.pallas_call(
        sweep_kernel,
        out_shape=[
            floats(3, planes, layers, row_width),
            floats(*density.shape),
            floats(planes, layers, row_width),
        ],
        in_specs=[in_smem()] + [in_vmem()] * 6,
        out_specs=[in_vmem()] * 3,
        scratch_shapes=[
            scratch(planes + 4),
            scratch(planes + 4),
            scratch(planes + 4),
            scratch(planes),
            scratch(planes + 1),
            scratch(planes),
            scratch(planes),
            scratch(planes),
            scratch(planes),
            scratch(3, planes),
            scratch(3, planes + 2),
            scratch(3, planes + 2),
        ],
        compiler_params=pltpu.CompilerParams(vmem_limit_bytes=KERNEL_VMEM),
        name="sweeps",
    )(spot, load, weights, totals, push, density, first)


def design_call(weights, sens, coef, density):
    cores, chips, own_planes, layers, row_width = density.shape
    planes = cores * chips * own_planes

    def scratch(*lead):
        return pltpu.VMEM(lead + (layers, row_width), jnp.float32)

    return pl.pallas_call(
        design_kernel,
        out_shape=jax.ShapeDtypeStruct((own_planes, layers, row_width), jnp.float32),
        in_specs=[in_vmem()] * 4,
        out_specs=in_vmem(),
        scratch_shapes=[
            scratch(planes + 4),
            scratch(planes + 4),
            scratch(planes + 4),
            scratch(planes),
            scratch(planes),
            scratch(planes),
        ],
        compiler_params=pltpu.CompilerParams(vmem_limit_bytes=KERNEL_VMEM),
        name="design",
    )(weights, sens, coef, density)


def other_core(block):
    devices = lax.axis_size("space")
    return lax.ppermute(block, "space", [(i, i ^ 1) for i in range(devices)])


def between_chips(pieces):
    devices = lax.axis_size("space")
    groups = [list(range(core, devices, 2)) for core in range(2)]
    return lax.all_to_all(pieces, "space", 0, 0, axis_index_groups=groups)


def gathered(block, beside=()):
    chips = lax.axis_size("space") // 2
    same = between_chips(jnp.broadcast_to(block[None], (chips,) + block.shape))
    same, beside = lax.optimization_barrier((same, beside))
    return jnp.stack([same, other_core(same)]), beside


def scattered_sum(pieces):
    return jnp.sum(between_chips(pieces[0] + other_core(pieces[1])), axis=0)


def one_slab(density, displacement, fixed, load_index, load_force, radius):
    prepared = prepare_call(radius, load_index, load_force.T, fixed, displacement[0])
    whole, prepared = gathered(density, prepared)
    weights, totals, first, push, load, spot = prepared
    new_displacement, sens, coef = sweep_call(spot, load, weights, totals, push, whole, first)
    sens, _ = gathered(scattered_sum(sens))
    new_density = design_call(weights, sens, coef, whole)
    return new_density, new_displacement[None]


def from_behind(block, axis, distance):
    devices = range(lax.axis_size(axis))
    route = [(i - distance, i) for i in devices if i - distance in devices]
    return lax.ppermute(block, axis, route)


def extended(x, sides, width):
    for axis, dim in sides:
        size, length = (lax.axis_size(axis), x.shape[dim])
        up = [(i, (i + 1) % size) for i in range(size - 1)]
        down = [(j, i) for i, j in up]
        last = lax.slice_in_dim(x, length - width, length, axis=dim)
        first = lax.slice_in_dim(x, 0, width, axis=dim)
        before = lax.ppermute(last, axis, up)
        after = lax.ppermute(first, axis, down)
        x = jnp.concatenate([before, x, after], axis=dim)
    return x


def from_partner(x, axis, bit):
    return lax.ppermute(x, axis, [(i, i ^ 1 << bit) for i in range(lax.axis_size(axis))])


def window_offsets():
    offsets_list = []
    for across in range(-window_reach, window_reach + 1):
        for upward in range(-window_reach, window_reach + 1):
            for sideways in range(-window_reach, window_reach + 1):
                length = math.sqrt(across * across + upward * upward + sideways * sideways)
                offsets_list.append((across, upward, sideways, length))
    return offsets_list


def layer_weights(radius):
    radial = radius.astype(jnp.float32)
    return jnp.stack(
        [jnp.maximum(radial - length, 0.0) for across, upward, sideways, length in window_offsets()]
    )


def pad_axis(grid_field, along_axis, before, after_cells):
    widths = [(0, 0)] * grid_field.ndim
    widths[along_axis] = (before, after_cells)
    return jnp.pad(grid_field, widths)


def pad_sides(grid_field):
    return jnp.pad(grid_field, ((0, 0), (window_reach, window_reach), (window_reach, window_reach)))


def filter_forward(padded, weights):
    out_rows = padded.shape[0] - 2 * window_reach
    layers = padded.shape[1] - 2 * window_reach
    row_width = padded.shape[2] - 2 * window_reach
    result = jnp.zeros((out_rows, layers, row_width), jnp.float32)
    for offset_index, (across, upward, sideways, length) in enumerate(window_offsets()):
        shifted = padded[
            window_reach + across : window_reach + across + out_rows,
            window_reach + upward : window_reach + upward + layers,
            window_reach + sideways : window_reach + sideways + row_width,
        ]
        result = result + weights[offset_index][None, :, None] * shifted
    return result


def filter_backward(padded, padded_weights):
    out_rows = padded.shape[0] - 2 * window_reach
    layers = padded.shape[1] - 2 * window_reach
    row_width = padded.shape[2] - 2 * window_reach
    result = jnp.zeros((out_rows, layers, row_width), jnp.float32)
    for offset_index, (across, upward, sideways, length) in enumerate(window_offsets()):
        shifted = padded[
            window_reach - across : window_reach - across + out_rows,
            window_reach - upward : window_reach - upward + layers,
            window_reach - sideways : window_reach - sideways + row_width,
        ]
        layer_part = padded_weights[
            offset_index, window_reach - upward : window_reach - upward + layers
        ]
        result = result + layer_part[None, :, None] * shifted
    return result


def stiff_factors(direction):
    return jnp.array(
        [2.0 if component == direction else 1.0 for component in range(3)], jnp.float32
    ).reshape(3, 1, 1, 1)


def relax_slab(padded, displace, face_x, face_z, face_y, force_field, free_cells, diagonal):
    flux_x = stiff_factors(0) * face_x * jnp.diff(padded, axis=1)
    stencil_image = flux_x[:, :-1] - flux_x[:, 1:]
    flux_z = stiff_factors(1) * face_z * jnp.diff(displace, axis=2)
    stencil_image = stencil_image + pad_axis(flux_z, 2, 1, 0) - pad_axis(flux_z, 2, 0, 1)
    flux_y = stiff_factors(2) * face_y * jnp.diff(displace, axis=3)
    stencil_image = stencil_image + pad_axis(flux_y, 3, 1, 0) - pad_axis(flux_y, 3, 0, 1)
    return free_cells * (displace + relax_factor * (force_field - stencil_image) / diagonal)


def slab_energy(grid_field, along_axis, direction, load_cases):
    change = jnp.diff(grid_field, axis=along_axis)
    return jnp.sum(stiff_factors(direction) * change * change, axis=0) / load_cases


def neighbour_planes(displace, load_cases, axis_devices):
    if axis_devices > load_cases:
        below = from_behind(displace[:, -1:], "space", load_cases)
        above = from_behind(displace[:, :1], "space", -load_cases)
    else:
        below = jnp.zeros_like(displace[:, :1])
        above = jnp.zeros_like(displace[:, :1])
    return jnp.concatenate([below, displace, above], axis=1)


def many_slabs(density, displacement, fixed, load_index, load_force, radius):
    slab_rows, layers, row_width = density.shape
    load_cases = load_index.shape[0]
    level_count = load_cases.bit_length() - 1
    axis_devices = lax.axis_size("space")
    axis_place = lax.axis_index("space")
    slab_planes = slab_rows * load_cases
    slab_place = axis_place // load_cases
    load_place = axis_place % load_cases
    total_rows = slab_rows * axis_devices
    weights = layer_weights(radius)
    padded_weights = pad_axis(weights, 1, window_reach, window_reach)
    global_rows = (
        jnp.arange(slab_rows + 2 * window_reach, dtype=jnp.int32)
        + axis_place * slab_rows
        - window_reach
    )
    deep_inside = ((global_rows >= 0) & (global_rows < total_rows)).astype(jnp.float32)
    inside_field = deep_inside[:, None, None] * pad_sides(
        jnp.ones((slab_rows + 2 * window_reach, layers, row_width), jnp.float32)
    )
    total_weight = filter_forward(inside_field, weights)
    slab_start = slab_place * slab_planes
    margin_rows = jnp.arange(slab_planes + 2, dtype=jnp.int32) + slab_start - 1
    margin_inside = ((margin_rows >= 0) & (margin_rows < total_rows)).astype(jnp.float32)
    face_valid = margin_inside[1:] * margin_inside[:-1]
    fixed_slab = lax.dynamic_slice_in_dim(fixed, slab_start, slab_planes, 0).astype(jnp.float32)
    bottom_layer = (jnp.arange(layers, dtype=jnp.int32) == 0).astype(jnp.float32)
    free_cells = 1.0 - bottom_layer[None, :, None] * fixed_slab[:, None, :]
    slab_cells = slab_planes * layers * row_width
    cell_index = jnp.arange(slab_cells, dtype=jnp.int32) + slab_place * slab_cells
    load_hot = jnp.arange(load_cases, dtype=jnp.int32) == load_place
    own_index = jnp.sum(jnp.where(load_hot, load_index, 0))
    own_force = jnp.sum(load_hot.astype(jnp.float32)[:, None] * load_force, axis=0)
    load_hits = (cell_index == own_index).astype(jnp.float32)
    force_field = (own_force[:, None] * load_hits[None, :]).reshape(
        3, slab_planes, layers, row_width
    )
    displace = displacement[0] * free_cells
    target = volume_share * total_rows * layers * row_width
    padded = neighbour_planes(displace, load_cases, axis_devices)
    halo_density = extended(density, (("space", 0),), window_reach)
    filtered = filter_forward(pad_sides(halo_density), weights) / total_weight
    whole_field = lax.all_gather(filtered, "space", axis=0, tiled=True)
    margin = lax.dynamic_slice_in_dim(
        pad_axis(whole_field, 0, 1, 1), slab_start, slab_planes + 2, 0
    )
    moduli = floor_modulus + (1.0 - floor_modulus) * margin**3
    face_x = 0.5 * (moduli[1:] + moduli[:-1]) * face_valid[:, None, None]
    inner_moduli = moduli[1:-1]
    face_z = 0.5 * (inner_moduli[:, 1:] + inner_moduli[:, :-1])
    face_y = 0.5 * (inner_moduli[:, :, 1:] + inner_moduli[:, :, :-1])
    sum_x = face_x[:-1] + face_x[1:]
    sum_z = pad_axis(face_z, 1, 1, 0) + pad_axis(face_z, 1, 0, 1)
    sum_y = pad_axis(face_y, 2, 1, 0) + pad_axis(face_y, 2, 0, 1)
    diagonal = stiff_factors(0) * sum_x + stiff_factors(1) * sum_z + stiff_factors(2) * sum_y
    for sweep_index in range(SWEEPS):
        displace = relax_slab(
            padded, displace, face_x, face_z, face_y, force_field, free_cells, diagonal
        )
        padded = neighbour_planes(displace, load_cases, axis_devices)
    energy_x = slab_energy(padded, 1, 0, load_cases) * face_valid[:, None, None]
    energy_z = slab_energy(displace, 2, 1, load_cases)
    energy_y = slab_energy(displace, 3, 2, load_cases)
    sens_term = 0.5 * (
        energy_x[:-1]
        + energy_x[1:]
        + pad_axis(energy_z, 1, 1, 0)
        + pad_axis(energy_z, 1, 0, 1)
        + pad_axis(energy_y, 2, 1, 0)
        + pad_axis(energy_y, 2, 0, 1)
    )
    sensitive = sens_term
    for level in reversed(range(level_count)):
        half_rows = sensitive.shape[0] // 2
        upper_side = load_place // 2**level % 2 == 1
        outgoing = jnp.where(upper_side, sensitive[:half_rows], sensitive[half_rows:])
        keeping = jnp.where(upper_side, sensitive[half_rows:], sensitive[:half_rows])
        sensitive = keeping + from_partner(outgoing, "space", level)
    weighted_share = 3.0 * (1.0 - floor_modulus) * filtered**2 * sensitive / total_weight
    halo_share = extended(weighted_share, (("space", 0),), window_reach)
    root_term = jnp.sqrt(filter_backward(pad_sides(halo_share), padded_weights))
    lowest = jnp.maximum(density - move_limit, density_floor)
    highest = jnp.minimum(density + move_limit, 1.0)
    design_now = density

    def trial_design(log_level):
        return jnp.clip(design_now * root_term * jnp.exp(-0.5 * log_level), lowest, highest)

    start_state = (jnp.asarray(log_lower, jnp.float32), jnp.asarray(log_span, jnp.float32))

    def halve(search_step, search_state):
        lower_end, span_width = search_state
        half_span = span_width * 0.5
        middle = lower_end + half_span
        volume_total = lax.psum(jnp.sum(trial_design(middle)), "space")
        return (jnp.where(volume_total > target, middle, lower_end), half_span)

    lower_end, span_width = lax.fori_loop(0, SEARCH, halve, start_state)
    density = trial_design(lower_end + 0.5 * span_width)
    new_displacement = displace[None]
    return (density, new_displacement)


def solution(mesh):
    in_specs = (
        P("space", "parts", None),
        P("space", None, None, "parts", None),
        P(None, "parts"),
        P("parts"),
        P("parts", None),
        P("parts"),
    )
    out_specs = (P("space", "parts", None), P("space", None, None, "parts", None))

    def local(density, displacement, fixed, load_index, load_force, radius):
        alone = lax.axis_size("space") == load_index.shape[0]
        run = one_slab if alone else many_slabs
        return run(density, displacement, fixed, load_index, load_force, radius)

    return jax.shard_map(local, mesh=mesh, in_specs=in_specs, out_specs=out_specs, check_vma=False)
```

```python
import math

import jax
import jax.numpy as jnp
from jax import lax
from jax.experimental import pallas as pl
from jax.experimental.pallas import tpu as pltpu
from jax.sharding import PartitionSpec as P

SWEEPS = 3
SEARCH = 12


floor_modulus = 0.05
relax_factor = 0.6
move_limit = 0.2
density_floor = 0.01
volume_share = 0.5
log_lower = -16.0
log_span = 32.0
window_reach = 2

PLANE_SQUARES = (0, 1, 2, 4, 5, 8)
ALL_SQUARES = (0, 1, 2, 3, 4, 5, 6, 8, 9, 12)


def spot_iota(shape, dim):
    return lax.broadcasted_iota(jnp.int32, shape, dim)


def layer_radius(radius_ref, layers, row_width):
    z = spot_iota((layers, row_width), 0)
    result = jnp.zeros((layers, row_width), jnp.int32)
    for layer in range(layers):
        result = jnp.where(z == layer, radius_ref[layer], result)
    return result.astype(jnp.float32)


def class_weights(radius_ref, weight_ref):
    layers, row_width = weight_ref.shape[1:]
    radial = layer_radius(radius_ref, layers, row_width)
    for place, square in enumerate(ALL_SQUARES):
        weight_ref[place] = jnp.maximum(radial - math.sqrt(square), 0.0)


def shift_sum(field, dim, distance):
    size = field.shape[dim]
    spot = spot_iota(field.shape, dim)
    ahead = jnp.where(spot < size - distance, pltpu.roll(field, size - distance, dim), 0.0)
    behind = jnp.where(spot >= distance, pltpu.roll(field, distance, dim), 0.0)
    return ahead + behind


def plane_sums(plane):
    beside = shift_sum(plane, 1, 1)
    further = shift_sum(plane, 1, 2)
    return {
        0: plane,
        1: beside + shift_sum(plane, 0, 1),
        2: shift_sum(beside, 0, 1),
        4: further + shift_sum(plane, 0, 2),
        5: shift_sum(further, 0, 1) + shift_sum(beside, 0, 2),
        8: shift_sum(further, 0, 2),
    }


def weigh(sums, weight_ref, square):
    result = None
    for inner in PLANE_SQUARES:
        term = weight_ref[ALL_SQUARES.index(inner + square)] * sums[inner]
        result = term if result is None else result + term
    return result


def forward_planes(plane, weight_ref):
    sums = plane_sums(plane)
    return [weigh(sums, weight_ref, square) for square in (0, 1, 4)]


def backward_planes(plane, weight_ref):
    beside = shift_sum(plane, 1, 1)
    further = shift_sum(plane, 1, 2)
    results = []
    for square in (0, 1, 4):

        def weight(more):
            return weight_ref[ALL_SQUARES.index(square + more)]

        level = weight(0) * plane + weight(1) * beside + weight(4) * further
        near = weight(1) * plane + weight(2) * beside + weight(5) * further
        far = weight(4) * plane + weight(5) * beside + weight(8) * further
        results.append(level + shift_sum(near, 0, 1) + shift_sum(far, 0, 2))
    return results


def pair_spot(x, own_planes):
    device = x // own_planes
    core = (device ^ lax.axis_index("space")) & 1
    return core, device >> 1, x % own_planes


def edge_class(x, planes):
    return jnp.minimum(x, 2) + jnp.maximum(x - (planes - 3), 0)


def zero_edges(ref):
    planes = ref.shape[0]
    for place in (0, 1, planes - 2, planes - 1):
        ref[place] = jnp.zeros(ref.shape[1:], ref.dtype)


def prepare_kernel(
    radius_ref,
    index_ref,
    force_ref,
    fixed_ref,
    start_ref,
    weight_ref,
    total_ref,
    first_ref,
    push_ref,
    load_ref,
    spot_ref,
):
    planes, layers, row_width = start_ref.shape[1:]
    load_place = lax.axis_index("space")
    shape = (layers, row_width)
    z = spot_iota(shape, 0)
    y = spot_iota(shape, 1)

    class_weights(radius_ref, weight_ref)
    ones = forward_planes(jnp.ones(shape, jnp.float32), weight_ref)
    for place, (lower, upper) in enumerate(((0, 2), (1, 2), (2, 2), (2, 1), (2, 0))):
        total_ref[place] = (
            ones[0] + min(lower, 1) * ones[1] + min(upper, 1) * ones[1]
            + (lower // 2) * ones[2] + (upper // 2) * ones[2]
        )

    def free_plane(x, carry):
        free = jnp.where(z == 0, 1.0 - fixed_ref[pl.ds(x, 1), :].astype(jnp.float32), 1.0)
        push_ref[x] = relax_factor * free
        for part in range(3):
            first_ref[part, x + 1] = start_ref[part, x] * free
        return carry

    lax.fori_loop(0, planes, free_plane, 0, unroll=8)
    for part in range(3):
        first_ref[part, 0] = jnp.zeros(shape, jnp.float32)
        first_ref[part, planes + 1] = jnp.zeros(shape, jnp.float32)

    own_index = index_ref[load_place]
    own_z = own_index // row_width % layers
    own_y = own_index % row_width
    hit = (z == own_z) & (y == own_y)
    for part in range(3):
        load_ref[part] = jnp.where(hit, force_ref[part, load_place], 0.0)
    spot_ref[0] = own_index // (layers * row_width)


def sweep_kernel(
    spot_ref,
    load_ref,
    weight_ref,
    total_ref,
    push_ref,
    density_ref,
    first_ref,
    disp_ref,
    sens_ref,
    coef_ref,
    near_ref,
    side_ref,
    far_ref,
    modulus_ref,
    across_ref,
    up_ref,
    down_ref,
    right_ref,
    left_ref,
    rate_ref,
    second_ref,
    third_ref,
):
    cores, chips, own_planes, layers, row_width = density_ref.shape
    planes = cores * chips * own_planes
    load_cases = lax.axis_size("space")
    shape = (layers, row_width)
    z = spot_iota(shape, 0)
    y = spot_iota(shape, 1)
    zero = jnp.zeros(shape, jnp.float32)

    for ref in (side_ref, far_ref):
        zero_edges(ref)

    def filter_plane(x, carry):
        near, side, far = forward_planes(
            density_ref[pair_spot(x, own_planes)], weight_ref
        )
        near_ref[x + 2] = near
        side_ref[x + 2] = side
        far_ref[x + 2] = far
        return carry

    lax.fori_loop(0, planes, filter_plane, 0, unroll=8)

    def modulus_plane(x, carry):
        total = total_ref[edge_class(x, planes)]
        filtered = (
            near_ref[x + 2]
            + side_ref[x + 1]
            + side_ref[x + 3]
            + far_ref[x]
            + far_ref[x + 4]
        ) / total
        modulus = floor_modulus + (1.0 - floor_modulus) * (filtered * filtered * filtered)
        modulus_ref[x] = modulus
        coef_ref[x] = 3.0 * (1.0 - floor_modulus) * (filtered * filtered) / total
        return carry

    lax.fori_loop(0, planes, modulus_plane, 0, unroll=8)

    across_ref[0] = zero
    across_ref[planes] = zero
    for ref in (second_ref, third_ref):
        for part in range(3):
            ref[part, 0] = zero
            ref[part, planes + 1] = zero

    def face_plane(x, carry):
        modulus = modulus_ref[x]
        later = modulus_ref[jnp.minimum(x + 1, planes - 1)]
        ahead = jnp.where(x + 1 < planes, 0.5 * (modulus + later), 0.0)
        across_ref[x + 1] = ahead
        up = jnp.where(z < layers - 1, 0.5 * (modulus + pltpu.roll(modulus, layers - 1, 0)), 0.0)
        down = pltpu.roll(up, 1, 0)
        right = jnp.where(
            y < row_width - 1, 0.5 * (modulus + pltpu.roll(modulus, row_width - 1, 1)), 0.0
        )
        left = pltpu.roll(right, 1, 1)
        up_ref[x] = up
        down_ref[x] = down
        right_ref[x] = right
        left_ref[x] = left
        sums = (carry + ahead, up + down, left + right)
        every = sums[0] + sums[1] + sums[2]
        push = push_ref[x]
        for part in range(3):
            rate_ref[part, x] = push / (every + sums[part])
        return ahead

    lax.fori_loop(0, planes, face_plane, zero, unroll=8)

    own_x = spot_ref[0]

    def sweep(source, target, lead):
        def sweep_plane(x, carry):
            before, after = across_ref[x], across_ref[x + 1]
            up, down, right, left = up_ref[x], down_ref[x], right_ref[x], left_ref[x]
            for part in range(3):
                here = source[part, x + 1]
                pulls = [
                    before * source[part, x] + after * source[part, x + 2],
                    up * pltpu.roll(here, layers - 1, 0) + down * pltpu.roll(here, 1, 0),
                    right * pltpu.roll(here, row_width - 1, 1) + left * pltpu.roll(here, 1, 1),
                ]
                pull = pulls[0] + pulls[1] + pulls[2] + pulls[part]
                target[part, x + lead] = (1.0 - relax_factor) * here + rate_ref[part, x] * pull
            return carry

        lax.fori_loop(0, planes, sweep_plane, 0, unroll=8)
        for part in range(3):
            target[part, own_x + lead] += rate_ref[part, own_x] * load_ref[part]

    source = first_ref
    for turn in range(SWEEPS - 1):
        target = (second_ref, third_ref)[turn % 2]
        sweep(source, target, 1)
        source = target
    sweep(source, disp_ref, 0)

    def energy_plane(x, carry):
        later = jnp.minimum(x + 1, planes - 1)
        ahead, upward, right = zero, zero, zero
        for part in range(3):
            here = disp_ref[part, x]
            step = disp_ref[part, later] - here
            climb = pltpu.roll(here, layers - 1, 0) - here
            slide = pltpu.roll(here, row_width - 1, 1) - here
            ahead = ahead + (2.0 if part == 0 else 1.0) * (step * step)
            upward = upward + (2.0 if part == 1 else 1.0) * (climb * climb)
            right = right + (2.0 if part == 2 else 1.0) * (slide * slide)
        upward = jnp.where(z < layers - 1, upward, 0.0)
        right = jnp.where(y < row_width - 1, right, 0.0)
        total = carry + ahead + upward + pltpu.roll(upward, 1, 0) + right + pltpu.roll(right, 1, 1)
        sens_ref[pair_spot(x, own_planes)] = (0.5 / load_cases) * total
        return ahead

    lax.fori_loop(0, planes, energy_plane, zero, unroll=8)


def design_kernel(
    weight_ref,
    sens_ref,
    coef_ref,
    density_ref,
    new_ref,
    near_ref,
    side_ref,
    far_ref,
    pull_ref,
    low_ref,
    high_ref,
):
    cores, chips, own_planes, layers, row_width = density_ref.shape
    planes = cores * chips * own_planes
    place = lax.axis_index("space")
    shape = (layers, row_width)
    zero = jnp.zeros(shape, jnp.float32)
    for ref in (side_ref, far_ref):
        zero_edges(ref)

    def filter_plane(x, carry):
        near, side, far = backward_planes(
            sens_ref[pair_spot(x, own_planes)] * coef_ref[x], weight_ref
        )
        near_ref[x + 2] = near
        side_ref[x + 2] = side
        far_ref[x + 2] = far
        return carry

    lax.fori_loop(0, planes, filter_plane, 0, unroll=8)

    def root_plane(x, carry):
        root = jnp.sqrt(
            near_ref[x + 2] + side_ref[x + 1] + side_ref[x + 3] + far_ref[x] + far_ref[x + 4]
        )
        density = density_ref[pair_spot(x, own_planes)]
        pull_ref[x] = density * root
        low_ref[x] = jnp.maximum(density - move_limit, density_floor)
        high_ref[x] = jnp.minimum(density + move_limit, 1.0)
        return carry

    lax.fori_loop(0, planes, root_plane, 0, unroll=8)

    target = volume_share * planes * layers * row_width

    def trial(x, factor):
        return jnp.minimum(jnp.maximum(pull_ref[x] * factor, low_ref[x]), high_ref[x])

    def halve(step, state):
        lower, span = state
        half = span * 0.5
        middle = lower + half
        factor = jnp.exp(-0.5 * middle)
        total = lax.fori_loop(
            0, planes, lambda x, acc: acc + trial(x, factor), zero, unroll=8
        )
        volume = jnp.sum(jnp.sum(total, axis=0, keepdims=True), axis=1, keepdims=True)
        return jnp.where(volume > target, middle, lower), half

    start = (jnp.full((1, 1), log_lower, jnp.float32), jnp.full((1, 1), log_span, jnp.float32))
    lower, span = lax.fori_loop(0, SEARCH, halve, start)
    factor = jnp.exp(-0.5 * (lower + 0.5 * span))
    for own in range(own_planes):
        new_ref[own] = trial(place * own_planes + own, factor)


def in_vmem():
    return pl.BlockSpec(memory_space=pltpu.VMEM)


def in_smem():
    return pl.BlockSpec(memory_space=pltpu.SMEM)


KERNEL_VMEM = 24 * 2**20


def floats(*shape):
    return jax.ShapeDtypeStruct(shape, jnp.float32)


def prepare_call(radius, load_index, load_force, fixed, displacement):
    planes, layers, row_width = displacement.shape[1:]
    return pl.pallas_call(
        prepare_kernel,
        out_shape=[
            floats(len(ALL_SQUARES), layers, row_width),
            floats(2 * window_reach + 1, layers, row_width),
            floats(3, planes + 2, layers, row_width),
            floats(planes, layers, row_width),
            floats(3, layers, row_width),
            jax.ShapeDtypeStruct((1,), jnp.int32),
        ],
        in_specs=[in_smem()] * 3 + [in_vmem()] * 2,
        out_specs=[in_vmem()] * 5 + [in_smem()],
        compiler_params=pltpu.CompilerParams(vmem_limit_bytes=KERNEL_VMEM),
        cost_estimate=pl.CostEstimate(
            flops=4 * displacement.size,
            bytes_accessed=8 * displacement.size,
            transcendentals=0,
        ),
        name="prepare",
    )(radius, load_index, load_force, fixed, displacement)


def sweep_call(spot, load, weights, totals, push, density, first):
    cores, chips, own_planes, layers, row_width = density.shape
    planes = cores * chips * own_planes

    def scratch(*lead):
        return pltpu.VMEM(lead + (layers, row_width), jnp.float32)

    return pl.pallas_call(
        sweep_kernel,
        out_shape=[
            floats(3, planes, layers, row_width),
            floats(*density.shape),
            floats(planes, layers, row_width),
        ],
        in_specs=[in_smem()] + [in_vmem()] * 6,
        out_specs=[in_vmem()] * 3,
        scratch_shapes=[
            scratch(planes + 4),
            scratch(planes + 4),
            scratch(planes + 4),
            scratch(planes),
            scratch(planes + 1),
            scratch(planes),
            scratch(planes),
            scratch(planes),
            scratch(planes),
            scratch(3, planes),
            scratch(3, planes + 2),
            scratch(3, planes + 2),
        ],
        compiler_params=pltpu.CompilerParams(vmem_limit_bytes=KERNEL_VMEM),
        name="sweeps",
    )(spot, load, weights, totals, push, density, first)


def design_call(weights, sens, coef, density):
    cores, chips, own_planes, layers, row_width = density.shape
    planes = cores * chips * own_planes

    def scratch(*lead):
        return pltpu.VMEM(lead + (layers, row_width), jnp.float32)

    return pl.pallas_call(
        design_kernel,
        out_shape=jax.ShapeDtypeStruct((own_planes, layers, row_width), jnp.float32),
        in_specs=[in_vmem()] * 4,
        out_specs=in_vmem(),
        scratch_shapes=[
            scratch(planes + 4),
            scratch(planes + 4),
            scratch(planes + 4),
            scratch(planes),
            scratch(planes),
            scratch(planes),
        ],
        compiler_params=pltpu.CompilerParams(vmem_limit_bytes=KERNEL_VMEM),
        name="design",
    )(weights, sens, coef, density)


def other_core(block):
    devices = lax.axis_size("space")
    return lax.ppermute(block, "space", [(i, i ^ 1) for i in range(devices)])


def same_core_groups():
    devices = lax.axis_size("space")
    return [list(range(core, devices, 2)) for core in range(2)]


def between_chips(pieces):
    return lax.all_to_all(pieces, "space", 0, 0, axis_index_groups=same_core_groups())


def gathered(block, beside=()):
    same = lax.all_gather(block, "space", axis_index_groups=same_core_groups())
    same, beside = lax.optimization_barrier((same, beside))
    return jnp.stack([same, other_core(same)]), beside


def scattered_sum(pieces):
    return jnp.sum(between_chips(pieces[0] + other_core(pieces[1])), axis=0)


def one_slab(density, displacement, fixed, load_index, load_force, radius):
    prepared = prepare_call(radius, load_index, load_force.T, fixed, displacement[0])
    whole, prepared = gathered(density, prepared)
    weights, totals, first, push, load, spot = prepared
    new_displacement, sens, coef = sweep_call(spot, load, weights, totals, push, whole, first)
    sens, _ = gathered(scattered_sum(sens))
    new_density = design_call(weights, sens, coef, whole)
    return new_density, new_displacement[None]


def from_behind(block, axis, distance):
    devices = range(lax.axis_size(axis))
    route = [(i - distance, i) for i in devices if i - distance in devices]
    return lax.ppermute(block, axis, route)


def extended(x, sides, width):
    for axis, dim in sides:
        size, length = (lax.axis_size(axis), x.shape[dim])
        up = [(i, (i + 1) % size) for i in range(size - 1)]
        down = [(j, i) for i, j in up]
        last = lax.slice_in_dim(x, length - width, length, axis=dim)
        first = lax.slice_in_dim(x, 0, width, axis=dim)
        before = lax.ppermute(last, axis, up)
        after = lax.ppermute(first, axis, down)
        x = jnp.concatenate([before, x, after], axis=dim)
    return x


def from_partner(x, axis, bit):
    return lax.ppermute(x, axis, [(i, i ^ 1 << bit) for i in range(lax.axis_size(axis))])


def window_offsets():
    offsets_list = []
    for across in range(-window_reach, window_reach + 1):
        for upward in range(-window_reach, window_reach + 1):
            for sideways in range(-window_reach, window_reach + 1):
                length = math.sqrt(across * across + upward * upward + sideways * sideways)
                offsets_list.append((across, upward, sideways, length))
    return offsets_list


def layer_weights(radius):
    radial = radius.astype(jnp.float32)
    return jnp.stack(
        [jnp.maximum(radial - length, 0.0) for across, upward, sideways, length in window_offsets()]
    )


def pad_axis(grid_field, along_axis, before, after_cells):
    widths = [(0, 0)] * grid_field.ndim
    widths[along_axis] = (before, after_cells)
    return jnp.pad(grid_field, widths)


def pad_sides(grid_field):
    return jnp.pad(grid_field, ((0, 0), (window_reach, window_reach), (window_reach, window_reach)))


def filter_forward(padded, weights):
    out_rows = padded.shape[0] - 2 * window_reach
    layers = padded.shape[1] - 2 * window_reach
    row_width = padded.shape[2] - 2 * window_reach
    result = jnp.zeros((out_rows, layers, row_width), jnp.float32)
    for offset_index, (across, upward, sideways, length) in enumerate(window_offsets()):
        shifted = padded[
            window_reach + across : window_reach + across + out_rows,
            window_reach + upward : window_reach + upward + layers,
            window_reach + sideways : window_reach + sideways + row_width,
        ]
        result = result + weights[offset_index][None, :, None] * shifted
    return result


def filter_backward(padded, padded_weights):
    out_rows = padded.shape[0] - 2 * window_reach
    layers = padded.shape[1] - 2 * window_reach
    row_width = padded.shape[2] - 2 * window_reach
    result = jnp.zeros((out_rows, layers, row_width), jnp.float32)
    for offset_index, (across, upward, sideways, length) in enumerate(window_offsets()):
        shifted = padded[
            window_reach - across : window_reach - across + out_rows,
            window_reach - upward : window_reach - upward + layers,
            window_reach - sideways : window_reach - sideways + row_width,
        ]
        layer_part = padded_weights[
            offset_index, window_reach - upward : window_reach - upward + layers
        ]
        result = result + layer_part[None, :, None] * shifted
    return result


def stiff_factors(direction):
    return jnp.array(
        [2.0 if component == direction else 1.0 for component in range(3)], jnp.float32
    ).reshape(3, 1, 1, 1)


def relax_slab(padded, displace, face_x, face_z, face_y, force_field, free_cells, diagonal):
    flux_x = stiff_factors(0) * face_x * jnp.diff(padded, axis=1)
    stencil_image = flux_x[:, :-1] - flux_x[:, 1:]
    flux_z = stiff_factors(1) * face_z * jnp.diff(displace, axis=2)
    stencil_image = stencil_image + pad_axis(flux_z, 2, 1, 0) - pad_axis(flux_z, 2, 0, 1)
    flux_y = stiff_factors(2) * face_y * jnp.diff(displace, axis=3)
    stencil_image = stencil_image + pad_axis(flux_y, 3, 1, 0) - pad_axis(flux_y, 3, 0, 1)
    return free_cells * (displace + relax_factor * (force_field - stencil_image) / diagonal)


def slab_energy(grid_field, along_axis, direction, load_cases):
    change = jnp.diff(grid_field, axis=along_axis)
    return jnp.sum(stiff_factors(direction) * change * change, axis=0) / load_cases


def neighbour_planes(displace, load_cases, axis_devices):
    if axis_devices > load_cases:
        below = from_behind(displace[:, -1:], "space", load_cases)
        above = from_behind(displace[:, :1], "space", -load_cases)
    else:
        below = jnp.zeros_like(displace[:, :1])
        above = jnp.zeros_like(displace[:, :1])
    return jnp.concatenate([below, displace, above], axis=1)


def many_slabs(density, displacement, fixed, load_index, load_force, radius):
    slab_rows, layers, row_width = density.shape
    load_cases = load_index.shape[0]
    level_count = load_cases.bit_length() - 1
    axis_devices = lax.axis_size("space")
    axis_place = lax.axis_index("space")
    slab_planes = slab_rows * load_cases
    slab_place = axis_place // load_cases
    load_place = axis_place % load_cases
    total_rows = slab_rows * axis_devices
    weights = layer_weights(radius)
    padded_weights = pad_axis(weights, 1, window_reach, window_reach)
    global_rows = (
        jnp.arange(slab_rows + 2 * window_reach, dtype=jnp.int32)
        + axis_place * slab_rows
        - window_reach
    )
    deep_inside = ((global_rows >= 0) & (global_rows < total_rows)).astype(jnp.float32)
    inside_field = deep_inside[:, None, None] * pad_sides(
        jnp.ones((slab_rows + 2 * window_reach, layers, row_width), jnp.float32)
    )
    total_weight = filter_forward(inside_field, weights)
    slab_start = slab_place * slab_planes
    margin_rows = jnp.arange(slab_planes + 2, dtype=jnp.int32) + slab_start - 1
    margin_inside = ((margin_rows >= 0) & (margin_rows < total_rows)).astype(jnp.float32)
    face_valid = margin_inside[1:] * margin_inside[:-1]
    fixed_slab = lax.dynamic_slice_in_dim(fixed, slab_start, slab_planes, 0).astype(jnp.float32)
    bottom_layer = (jnp.arange(layers, dtype=jnp.int32) == 0).astype(jnp.float32)
    free_cells = 1.0 - bottom_layer[None, :, None] * fixed_slab[:, None, :]
    slab_cells = slab_planes * layers * row_width
    cell_index = jnp.arange(slab_cells, dtype=jnp.int32) + slab_place * slab_cells
    load_hot = jnp.arange(load_cases, dtype=jnp.int32) == load_place
    own_index = jnp.sum(jnp.where(load_hot, load_index, 0))
    own_force = jnp.sum(load_hot.astype(jnp.float32)[:, None] * load_force, axis=0)
    load_hits = (cell_index == own_index).astype(jnp.float32)
    force_field = (own_force[:, None] * load_hits[None, :]).reshape(
        3, slab_planes, layers, row_width
    )
    displace = displacement[0] * free_cells
    target = volume_share * total_rows * layers * row_width
    padded = neighbour_planes(displace, load_cases, axis_devices)
    halo_density = extended(density, (("space", 0),), window_reach)
    filtered = filter_forward(pad_sides(halo_density), weights) / total_weight
    whole_field = lax.all_gather(filtered, "space", axis=0, tiled=True)
    margin = lax.dynamic_slice_in_dim(
        pad_axis(whole_field, 0, 1, 1), slab_start, slab_planes + 2, 0
    )
    moduli = floor_modulus + (1.0 - floor_modulus) * margin**3
    face_x = 0.5 * (moduli[1:] + moduli[:-1]) * face_valid[:, None, None]
    inner_moduli = moduli[1:-1]
    face_z = 0.5 * (inner_moduli[:, 1:] + inner_moduli[:, :-1])
    face_y = 0.5 * (inner_moduli[:, :, 1:] + inner_moduli[:, :, :-1])
    sum_x = face_x[:-1] + face_x[1:]
    sum_z = pad_axis(face_z, 1, 1, 0) + pad_axis(face_z, 1, 0, 1)
    sum_y = pad_axis(face_y, 2, 1, 0) + pad_axis(face_y, 2, 0, 1)
    diagonal = stiff_factors(0) * sum_x + stiff_factors(1) * sum_z + stiff_factors(2) * sum_y
    for sweep_index in range(SWEEPS):
        displace = relax_slab(
            padded, displace, face_x, face_z, face_y, force_field, free_cells, diagonal
        )
        padded = neighbour_planes(displace, load_cases, axis_devices)
    energy_x = slab_energy(padded, 1, 0, load_cases) * face_valid[:, None, None]
    energy_z = slab_energy(displace, 2, 1, load_cases)
    energy_y = slab_energy(displace, 3, 2, load_cases)
    sens_term = 0.5 * (
        energy_x[:-1]
        + energy_x[1:]
        + pad_axis(energy_z, 1, 1, 0)
        + pad_axis(energy_z, 1, 0, 1)
        + pad_axis(energy_y, 2, 1, 0)
        + pad_axis(energy_y, 2, 0, 1)
    )
    sensitive = sens_term
    for level in reversed(range(level_count)):
        half_rows = sensitive.shape[0] // 2
        upper_side = load_place // 2**level % 2 == 1
        outgoing = jnp.where(upper_side, sensitive[:half_rows], sensitive[half_rows:])
        keeping = jnp.where(upper_side, sensitive[half_rows:], sensitive[:half_rows])
        sensitive = keeping + from_partner(outgoing, "space", level)
    weighted_share = 3.0 * (1.0 - floor_modulus) * filtered**2 * sensitive / total_weight
    halo_share = extended(weighted_share, (("space", 0),), window_reach)
    root_term = jnp.sqrt(filter_backward(pad_sides(halo_share), padded_weights))
    lowest = jnp.maximum(density - move_limit, density_floor)
    highest = jnp.minimum(density + move_limit, 1.0)
    design_now = density

    def trial_design(log_level):
        return jnp.clip(design_now * root_term * jnp.exp(-0.5 * log_level), lowest, highest)

    start_state = (jnp.asarray(log_lower, jnp.float32), jnp.asarray(log_span, jnp.float32))

    def halve(search_step, search_state):
        lower_end, span_width = search_state
        half_span = span_width * 0.5
        middle = lower_end + half_span
        volume_total = lax.psum(jnp.sum(trial_design(middle)), "space")
        return (jnp.where(volume_total > target, middle, lower_end), half_span)

    lower_end, span_width = lax.fori_loop(0, SEARCH, halve, start_state)
    density = trial_design(lower_end + 0.5 * span_width)
    new_displacement = displace[None]
    return (density, new_displacement)


def solution(mesh):
    in_specs = (
        P("space", "parts", None),
        P("space", None, None, "parts", None),
        P(None, "parts"),
        P("parts"),
        P("parts", None),
        P("parts"),
    )
    out_specs = (P("space", "parts", None), P("space", None, None, "parts", None))

    def local(density, displacement, fixed, load_index, load_force, radius):
        alone = lax.axis_size("space") == load_index.shape[0]
        run = one_slab if alone else many_slabs
        return run(density, displacement, fixed, load_index, load_force, radius)

    return jax.shard_map(local, mesh=mesh, in_specs=in_specs, out_specs=out_specs, check_vma=False)
```

```python
import math

import jax
import jax.numpy as jnp
from jax import lax
from jax.experimental import pallas as pl
from jax.experimental.pallas import tpu as pltpu
from jax.sharding import PartitionSpec as P

SWEEPS = 3
SEARCH = 12


floor_modulus = 0.05
relax_factor = 0.6
move_limit = 0.2
density_floor = 0.01
volume_share = 0.5
log_lower = -16.0
log_span = 32.0
window_reach = 2

PLANE_SQUARES = (0, 1, 2, 4, 5, 8)
ALL_SQUARES = (0, 1, 2, 3, 4, 5, 6, 8, 9, 12)


def spot_iota(shape, dim):
    return lax.broadcasted_iota(jnp.int32, shape, dim)


def layer_radius(radius_ref, layers, row_width):
    z = spot_iota((layers, row_width), 0)
    result = jnp.zeros((layers, row_width), jnp.int32)
    for layer in range(layers):
        result = jnp.where(z == layer, radius_ref[layer], result)
    return result.astype(jnp.float32)


def class_weights(radius_ref, weight_ref):
    layers, row_width = weight_ref.shape[1:]
    radial = layer_radius(radius_ref, layers, row_width)
    for place, square in enumerate(ALL_SQUARES):
        weight_ref[place] = jnp.maximum(radial - math.sqrt(square), 0.0)


def shift_sum(field, dim, distance):
    size = field.shape[dim]
    spot = spot_iota(field.shape, dim)
    ahead = jnp.where(spot < size - distance, pltpu.roll(field, size - distance, dim), 0.0)
    behind = jnp.where(spot >= distance, pltpu.roll(field, distance, dim), 0.0)
    return ahead + behind


def plane_sums(plane):
    beside = shift_sum(plane, 1, 1)
    further = shift_sum(plane, 1, 2)
    return {
        0: plane,
        1: beside + shift_sum(plane, 0, 1),
        2: shift_sum(beside, 0, 1),
        4: further + shift_sum(plane, 0, 2),
        5: shift_sum(further, 0, 1) + shift_sum(beside, 0, 2),
        8: shift_sum(further, 0, 2),
    }


def weigh(sums, weight_ref, square):
    result = None
    for inner in PLANE_SQUARES:
        term = weight_ref[ALL_SQUARES.index(inner + square)] * sums[inner]
        result = term if result is None else result + term
    return result


def forward_planes(plane, weight_ref):
    sums = plane_sums(plane)
    return [weigh(sums, weight_ref, square) for square in (0, 1, 4)]


def backward_planes(plane, weight_ref):
    beside = shift_sum(plane, 1, 1)
    further = shift_sum(plane, 1, 2)
    results = []
    for square in (0, 1, 4):

        def weight(more):
            return weight_ref[ALL_SQUARES.index(square + more)]

        level = weight(0) * plane + weight(1) * beside + weight(4) * further
        near = weight(1) * plane + weight(2) * beside + weight(5) * further
        far = weight(4) * plane + weight(5) * beside + weight(8) * further
        results.append(level + shift_sum(near, 0, 1) + shift_sum(far, 0, 2))
    return results


def reverse_bits(value, count):
    result = 0
    for bit in range(count):
        result = result + ((value >> bit) & 1) * (1 << (count - 1 - bit))
    return result


def partner_spot(x, own_planes):
    devices = lax.axis_size("space")
    order = reverse_bits((x // own_planes) ^ lax.axis_index("space"), devices.bit_length() - 1)
    return order, x % own_planes


def pair_spot(x, own_planes):
    device = x // own_planes
    core = (device ^ lax.axis_index("space")) & 1
    return core, device >> 1, x % own_planes


def edge_class(x, planes):
    return jnp.minimum(x, 2) + jnp.maximum(x - (planes - 3), 0)


def zero_edges(ref):
    planes = ref.shape[0]
    for place in (0, 1, planes - 2, planes - 1):
        ref[place] = jnp.zeros(ref.shape[1:], ref.dtype)


def prepare_kernel(
    radius_ref,
    index_ref,
    force_ref,
    fixed_ref,
    density_ref,
    own_ref,
    weight_ref,
    total_ref,
    free_ref,
    load_ref,
    spot_ref,
):
    planes, row_width = fixed_ref.shape
    layers = density_ref.shape[1]
    load_place = lax.axis_index("space")
    shape = (layers, row_width)
    z = spot_iota(shape, 0)
    y = spot_iota(shape, 1)

    own_ref[0] = density_ref[...]
    class_weights(radius_ref, weight_ref)
    ones = forward_planes(jnp.ones(shape, jnp.float32), weight_ref)
    for place, (lower, upper) in enumerate(((0, 2), (1, 2), (2, 2), (2, 1), (2, 0))):
        total_ref[place] = (
            ones[0] + min(lower, 1) * ones[1] + min(upper, 1) * ones[1]
            + (lower // 2) * ones[2] + (upper // 2) * ones[2]
        )

    def free_plane(x, carry):
        free_ref[x] = jnp.where(
            z == 0, 1.0 - fixed_ref[pl.ds(x, 1), :].astype(jnp.float32), 1.0
        )
        return carry

    lax.fori_loop(0, planes, free_plane, 0, unroll=8)

    own_index = index_ref[load_place]
    own_z = own_index // row_width % layers
    own_y = own_index % row_width
    hit = (z == own_z) & (y == own_y)
    for part in range(3):
        load_ref[part] = jnp.where(hit, force_ref[part, load_place], 0.0)
    spot_ref[0] = own_index // (layers * row_width)


def sweep_kernel(
    spot_ref,
    load_ref,
    weight_ref,
    total_ref,
    free_ref,
    density_ref,
    start_ref,
    disp_ref,
    sens_ref,
    coef_ref,
    near_ref,
    side_ref,
    far_ref,
    modulus_ref,
    across_ref,
    up_ref,
    down_ref,
    right_ref,
    left_ref,
    rate_ref,
    first_ref,
    second_ref,
):
    planes, layers, row_width = coef_ref.shape
    own_planes = density_ref.shape[1]
    load_cases = lax.axis_size("space")
    shape = (layers, row_width)
    z = spot_iota(shape, 0)
    y = spot_iota(shape, 1)
    zero = jnp.zeros(shape, jnp.float32)

    for ref in (side_ref, far_ref):
        zero_edges(ref)

    def filter_plane(x, carry):
        near, side, far = forward_planes(density_ref[partner_spot(x, own_planes)], weight_ref)
        near_ref[x + 2] = near
        side_ref[x + 2] = side
        far_ref[x + 2] = far
        return carry

    lax.fori_loop(0, planes, filter_plane, 0, unroll=8)

    def modulus_plane(x, carry):
        total = total_ref[edge_class(x, planes)]
        filtered = (
            near_ref[x + 2]
            + side_ref[x + 1]
            + side_ref[x + 3]
            + far_ref[x]
            + far_ref[x + 4]
        ) / total
        modulus = floor_modulus + (1.0 - floor_modulus) * (filtered * filtered * filtered)
        modulus_ref[x] = modulus
        coef_ref[x] = 3.0 * (1.0 - floor_modulus) * (filtered * filtered) / total
        return carry

    lax.fori_loop(0, planes, modulus_plane, 0, unroll=8)

    across_ref[0] = zero
    across_ref[planes] = zero
    for ref in (first_ref, second_ref):
        for part in range(3):
            ref[part, 0] = zero
            ref[part, planes + 1] = zero

    def face_plane(x, carry):
        modulus = modulus_ref[x]
        later = modulus_ref[jnp.minimum(x + 1, planes - 1)]
        ahead = jnp.where(x + 1 < planes, 0.5 * (modulus + later), 0.0)
        across_ref[x + 1] = ahead
        up = jnp.where(z < layers - 1, 0.5 * (modulus + pltpu.roll(modulus, layers - 1, 0)), 0.0)
        down = pltpu.roll(up, 1, 0)
        right = jnp.where(
            y < row_width - 1, 0.5 * (modulus + pltpu.roll(modulus, row_width - 1, 1)), 0.0
        )
        left = pltpu.roll(right, 1, 1)
        up_ref[x] = up
        down_ref[x] = down
        right_ref[x] = right
        left_ref[x] = left
        sums = (carry + ahead, up + down, left + right)
        every = sums[0] + sums[1] + sums[2]
        free = free_ref[x]
        push = relax_factor * free
        for part in range(3):
            rate_ref[part, x] = push / (every + sums[part])
            first_ref[part, x + 1] = start_ref[part, x] * free
        return ahead

    lax.fori_loop(0, planes, face_plane, zero, unroll=8)

    own_x = spot_ref[0]

    def sweep(source, target, lead):
        def sweep_plane(x, carry):
            before, after = across_ref[x], across_ref[x + 1]
            up, down, right, left = up_ref[x], down_ref[x], right_ref[x], left_ref[x]
            for part in range(3):
                here = source[part, x + 1]
                pulls = [
                    before * source[part, x] + after * source[part, x + 2],
                    up * pltpu.roll(here, layers - 1, 0) + down * pltpu.roll(here, 1, 0),
                    right * pltpu.roll(here, row_width - 1, 1) + left * pltpu.roll(here, 1, 1),
                ]
                pull = pulls[0] + pulls[1] + pulls[2] + pulls[part]
                target[part, x + lead] = (1.0 - relax_factor) * here + rate_ref[part, x] * pull
            return carry

        lax.fori_loop(0, planes, sweep_plane, 0, unroll=8)
        for part in range(3):
            target[part, own_x + lead] += rate_ref[part, own_x] * load_ref[part]

    stages = (first_ref, second_ref)
    for turn in range(SWEEPS - 1):
        sweep(stages[turn % 2], stages[(turn + 1) % 2], 1)
    sweep(stages[(SWEEPS - 1) % 2], disp_ref, 0)

    def energy_plane(x, carry):
        later = jnp.minimum(x + 1, planes - 1)
        ahead, upward, right = zero, zero, zero
        for part in range(3):
            here = disp_ref[part, x]
            step = disp_ref[part, later] - here
            climb = pltpu.roll(here, layers - 1, 0) - here
            slide = pltpu.roll(here, row_width - 1, 1) - here
            ahead = ahead + (2.0 if part == 0 else 1.0) * (step * step)
            upward = upward + (2.0 if part == 1 else 1.0) * (climb * climb)
            right = right + (2.0 if part == 2 else 1.0) * (slide * slide)
        upward = jnp.where(z < layers - 1, upward, 0.0)
        right = jnp.where(y < row_width - 1, right, 0.0)
        total = carry + ahead + upward + pltpu.roll(upward, 1, 0) + right + pltpu.roll(right, 1, 1)
        sens_ref[pair_spot(x, own_planes)] = (0.5 / load_cases) * total
        return ahead

    lax.fori_loop(0, planes, energy_plane, zero, unroll=8)


def design_kernel(
    weight_ref,
    sens_ref,
    coef_ref,
    density_ref,
    new_ref,
    near_ref,
    side_ref,
    far_ref,
    pull_ref,
    low_ref,
    high_ref,
):
    planes, layers, row_width = coef_ref.shape
    own_planes = density_ref.shape[1]
    place = lax.axis_index("space")
    shape = (layers, row_width)
    zero = jnp.zeros(shape, jnp.float32)
    for ref in (side_ref, far_ref):
        zero_edges(ref)

    def filter_plane(x, carry):
        near, side, far = backward_planes(
            sens_ref[pair_spot(x, own_planes)] * coef_ref[x], weight_ref
        )
        near_ref[x + 2] = near
        side_ref[x + 2] = side
        far_ref[x + 2] = far
        return carry

    lax.fori_loop(0, planes, filter_plane, 0, unroll=8)

    def root_plane(x, carry):
        root = jnp.sqrt(
            near_ref[x + 2] + side_ref[x + 1] + side_ref[x + 3] + far_ref[x] + far_ref[x + 4]
        )
        density = density_ref[partner_spot(x, own_planes)]
        pull_ref[x] = density * root
        low_ref[x] = jnp.maximum(density - move_limit, density_floor)
        high_ref[x] = jnp.minimum(density + move_limit, 1.0)
        return carry

    lax.fori_loop(0, planes, root_plane, 0, unroll=8)

    target = volume_share * planes * layers * row_width

    def trial(x, factor):
        return jnp.minimum(jnp.maximum(pull_ref[x] * factor, low_ref[x]), high_ref[x])

    def halve(step, state):
        lower, span = state
        half = span * 0.5
        middle = lower + half
        factor = jnp.exp(-0.5 * middle)
        total = lax.fori_loop(
            0, planes, lambda x, acc: acc + trial(x, factor), zero, unroll=8
        )
        volume = jnp.sum(jnp.sum(total, axis=0, keepdims=True), axis=1, keepdims=True)
        return jnp.where(volume > target, middle, lower), half

    start = (jnp.full((1, 1), log_lower, jnp.float32), jnp.full((1, 1), log_span, jnp.float32))
    lower, span = lax.fori_loop(0, SEARCH, halve, start)
    factor = jnp.exp(-0.5 * (lower + 0.5 * span))
    for own in range(own_planes):
        new_ref[own] = trial(place * own_planes + own, factor)


def in_vmem():
    return pl.BlockSpec(memory_space=pltpu.VMEM)


def in_smem():
    return pl.BlockSpec(memory_space=pltpu.SMEM)


KERNEL_VMEM = 24 * 2**20


def floats(*shape):
    return jax.ShapeDtypeStruct(shape, jnp.float32)


def prepare_call(radius, load_index, load_force, fixed, density):
    layers, row_width = density.shape[1:]
    planes = fixed.shape[0]
    return pl.pallas_call(
        prepare_kernel,
        out_shape=[
            floats(1, *density.shape),
            floats(len(ALL_SQUARES), layers, row_width),
            floats(2 * window_reach + 1, layers, row_width),
            floats(planes, layers, row_width),
            floats(3, layers, row_width),
            jax.ShapeDtypeStruct((1,), jnp.int32),
        ],
        in_specs=[in_smem()] * 3 + [in_vmem()] * 2,
        out_specs=[in_vmem()] * 5 + [in_smem()],
        compiler_params=pltpu.CompilerParams(vmem_limit_bytes=KERNEL_VMEM),
        cost_estimate=pl.CostEstimate(
            flops=40 * planes * layers * row_width,
            bytes_accessed=8 * planes * layers * row_width,
            transcendentals=0,
        ),
        name="prepare",
    )(radius, load_index, load_force, fixed, density)


def sweep_call(spot, load, weights, totals, free, density, displacement):
    devices, own_planes, layers, row_width = density.shape
    planes = devices * own_planes

    def scratch(*lead):
        return pltpu.VMEM(lead + (layers, row_width), jnp.float32)

    return pl.pallas_call(
        sweep_kernel,
        out_shape=[
            floats(3, planes, layers, row_width),
            floats(2, devices // 2, own_planes, layers, row_width),
            floats(planes, layers, row_width),
        ],
        in_specs=[in_smem()] + [in_vmem()] * 6,
        out_specs=[in_vmem()] * 3,
        scratch_shapes=[
            scratch(planes + 4),
            scratch(planes + 4),
            scratch(planes + 4),
            scratch(planes),
            scratch(planes + 1),
            scratch(planes),
            scratch(planes),
            scratch(planes),
            scratch(planes),
            scratch(3, planes),
            scratch(3, planes + 2),
            scratch(3, planes + 2),
        ],
        compiler_params=pltpu.CompilerParams(vmem_limit_bytes=KERNEL_VMEM),
        name="sweeps",
    )(spot, load, weights, totals, free, density, displacement)


def design_call(weights, sens, coef, density):
    devices, own_planes, layers, row_width = density.shape
    planes = devices * own_planes

    def scratch(*lead):
        return pltpu.VMEM(lead + (layers, row_width), jnp.float32)

    return pl.pallas_call(
        design_kernel,
        out_shape=jax.ShapeDtypeStruct((own_planes, layers, row_width), jnp.float32),
        in_specs=[in_vmem()] * 4,
        out_specs=in_vmem(),
        scratch_shapes=[
            scratch(planes + 4),
            scratch(planes + 4),
            scratch(planes + 4),
            scratch(planes),
            scratch(planes),
            scratch(planes),
        ],
        compiler_params=pltpu.CompilerParams(vmem_limit_bytes=KERNEL_VMEM),
        name="design",
    )(weights, sens, coef, density)


def other_core(block):
    devices = lax.axis_size("space")
    return lax.ppermute(block, "space", [(i, i ^ 1) for i in range(devices)])


def between_chips(pieces):
    devices = lax.axis_size("space")
    groups = [list(range(core, devices, 2)) for core in range(2)]
    return lax.all_to_all(pieces, "space", 0, 0, axis_index_groups=groups)


def gathered(block):
    chips = lax.axis_size("space") // 2
    same = between_chips(jnp.broadcast_to(block[None], (chips,) + block.shape))
    return jnp.stack([same, other_core(same)])


def partner_gathered(block, prepare):
    devices = lax.axis_size("space")

    def swapped(pieces, bit):
        return lax.ppermute(pieces, "space", [(i, i ^ 1 << bit) for i in range(devices)])

    first, *bits = reversed(range(devices.bit_length() - 1))
    other = swapped(block[None], first)
    other, (own, *prepared) = lax.optimization_barrier((other, prepare()))
    pieces = jnp.concatenate([own, other])
    for bit in bits:
        pieces = jnp.concatenate([pieces, swapped(pieces, bit)])
    return pieces, prepared


def scattered_sum(pieces):
    return jnp.sum(between_chips(pieces[0] + other_core(pieces[1])), axis=0)


def one_slab(density, displacement, fixed, load_index, load_force, radius):
    whole, prepared = partner_gathered(
        density, lambda: prepare_call(radius, load_index, load_force.T, fixed, density)
    )
    weights, totals, free, load, spot = prepared
    new_displacement, sens, coef = sweep_call(
        spot, load, weights, totals, free, whole, displacement[0]
    )
    sens = gathered(scattered_sum(sens))
    new_density = design_call(weights, sens, coef, whole)
    return new_density, new_displacement[None]


def from_behind(block, axis, distance):
    devices = range(lax.axis_size(axis))
    route = [(i - distance, i) for i in devices if i - distance in devices]
    return lax.ppermute(block, axis, route)


def extended(x, sides, width):
    for axis, dim in sides:
        size, length = (lax.axis_size(axis), x.shape[dim])
        up = [(i, (i + 1) % size) for i in range(size - 1)]
        down = [(j, i) for i, j in up]
        last = lax.slice_in_dim(x, length - width, length, axis=dim)
        first = lax.slice_in_dim(x, 0, width, axis=dim)
        before = lax.ppermute(last, axis, up)
        after = lax.ppermute(first, axis, down)
        x = jnp.concatenate([before, x, after], axis=dim)
    return x


def from_partner(x, axis, bit):
    return lax.ppermute(x, axis, [(i, i ^ 1 << bit) for i in range(lax.axis_size(axis))])


def window_offsets():
    offsets_list = []
    for across in range(-window_reach, window_reach + 1):
        for upward in range(-window_reach, window_reach + 1):
            for sideways in range(-window_reach, window_reach + 1):
                length = math.sqrt(across * across + upward * upward + sideways * sideways)
                offsets_list.append((across, upward, sideways, length))
    return offsets_list


def layer_weights(radius):
    radial = radius.astype(jnp.float32)
    return jnp.stack(
        [jnp.maximum(radial - length, 0.0) for across, upward, sideways, length in window_offsets()]
    )


def pad_axis(grid_field, along_axis, before, after_cells):
    widths = [(0, 0)] * grid_field.ndim
    widths[along_axis] = (before, after_cells)
    return jnp.pad(grid_field, widths)


def pad_sides(grid_field):
    return jnp.pad(grid_field, ((0, 0), (window_reach, window_reach), (window_reach, window_reach)))


def filter_forward(padded, weights):
    out_rows = padded.shape[0] - 2 * window_reach
    layers = padded.shape[1] - 2 * window_reach
    row_width = padded.shape[2] - 2 * window_reach
    result = jnp.zeros((out_rows, layers, row_width), jnp.float32)
    for offset_index, (across, upward, sideways, length) in enumerate(window_offsets()):
        shifted = padded[
            window_reach + across : window_reach + across + out_rows,
            window_reach + upward : window_reach + upward + layers,
            window_reach + sideways : window_reach + sideways + row_width,
        ]
        result = result + weights[offset_index][None, :, None] * shifted
    return result


def filter_backward(padded, padded_weights):
    out_rows = padded.shape[0] - 2 * window_reach
    layers = padded.shape[1] - 2 * window_reach
    row_width = padded.shape[2] - 2 * window_reach
    result = jnp.zeros((out_rows, layers, row_width), jnp.float32)
    for offset_index, (across, upward, sideways, length) in enumerate(window_offsets()):
        shifted = padded[
            window_reach - across : window_reach - across + out_rows,
            window_reach - upward : window_reach - upward + layers,
            window_reach - sideways : window_reach - sideways + row_width,
        ]
        layer_part = padded_weights[
            offset_index, window_reach - upward : window_reach - upward + layers
        ]
        result = result + layer_part[None, :, None] * shifted
    return result


def stiff_factors(direction):
    return jnp.array(
        [2.0 if component == direction else 1.0 for component in range(3)], jnp.float32
    ).reshape(3, 1, 1, 1)


def relax_slab(padded, displace, face_x, face_z, face_y, force_field, free_cells, diagonal):
    flux_x = stiff_factors(0) * face_x * jnp.diff(padded, axis=1)
    stencil_image = flux_x[:, :-1] - flux_x[:, 1:]
    flux_z = stiff_factors(1) * face_z * jnp.diff(displace, axis=2)
    stencil_image = stencil_image + pad_axis(flux_z, 2, 1, 0) - pad_axis(flux_z, 2, 0, 1)
    flux_y = stiff_factors(2) * face_y * jnp.diff(displace, axis=3)
    stencil_image = stencil_image + pad_axis(flux_y, 3, 1, 0) - pad_axis(flux_y, 3, 0, 1)
    return free_cells * (displace + relax_factor * (force_field - stencil_image) / diagonal)


def slab_energy(grid_field, along_axis, direction, load_cases):
    change = jnp.diff(grid_field, axis=along_axis)
    return jnp.sum(stiff_factors(direction) * change * change, axis=0) / load_cases


def neighbour_planes(displace, load_cases, axis_devices):
    if axis_devices > load_cases:
        below = from_behind(displace[:, -1:], "space", load_cases)
        above = from_behind(displace[:, :1], "space", -load_cases)
    else:
        below = jnp.zeros_like(displace[:, :1])
        above = jnp.zeros_like(displace[:, :1])
    return jnp.concatenate([below, displace, above], axis=1)


def many_slabs(density, displacement, fixed, load_index, load_force, radius):
    slab_rows, layers, row_width = density.shape
    load_cases = load_index.shape[0]
    level_count = load_cases.bit_length() - 1
    axis_devices = lax.axis_size("space")
    axis_place = lax.axis_index("space")
    slab_planes = slab_rows * load_cases
    slab_place = axis_place // load_cases
    load_place = axis_place % load_cases
    total_rows = slab_rows * axis_devices
    weights = layer_weights(radius)
    padded_weights = pad_axis(weights, 1, window_reach, window_reach)
    global_rows = (
        jnp.arange(slab_rows + 2 * window_reach, dtype=jnp.int32)
        + axis_place * slab_rows
        - window_reach
    )
    deep_inside = ((global_rows >= 0) & (global_rows < total_rows)).astype(jnp.float32)
    inside_field = deep_inside[:, None, None] * pad_sides(
        jnp.ones((slab_rows + 2 * window_reach, layers, row_width), jnp.float32)
    )
    total_weight = filter_forward(inside_field, weights)
    slab_start = slab_place * slab_planes
    margin_rows = jnp.arange(slab_planes + 2, dtype=jnp.int32) + slab_start - 1
    margin_inside = ((margin_rows >= 0) & (margin_rows < total_rows)).astype(jnp.float32)
    face_valid = margin_inside[1:] * margin_inside[:-1]
    fixed_slab = lax.dynamic_slice_in_dim(fixed, slab_start, slab_planes, 0).astype(jnp.float32)
    bottom_layer = (jnp.arange(layers, dtype=jnp.int32) == 0).astype(jnp.float32)
    free_cells = 1.0 - bottom_layer[None, :, None] * fixed_slab[:, None, :]
    slab_cells = slab_planes * layers * row_width
    cell_index = jnp.arange(slab_cells, dtype=jnp.int32) + slab_place * slab_cells
    load_hot = jnp.arange(load_cases, dtype=jnp.int32) == load_place
    own_index = jnp.sum(jnp.where(load_hot, load_index, 0))
    own_force = jnp.sum(load_hot.astype(jnp.float32)[:, None] * load_force, axis=0)
    load_hits = (cell_index == own_index).astype(jnp.float32)
    force_field = (own_force[:, None] * load_hits[None, :]).reshape(
        3, slab_planes, layers, row_width
    )
    displace = displacement[0] * free_cells
    target = volume_share * total_rows * layers * row_width
    padded = neighbour_planes(displace, load_cases, axis_devices)
    halo_density = extended(density, (("space", 0),), window_reach)
    filtered = filter_forward(pad_sides(halo_density), weights) / total_weight
    whole_field = lax.all_gather(filtered, "space", axis=0, tiled=True)
    margin = lax.dynamic_slice_in_dim(
        pad_axis(whole_field, 0, 1, 1), slab_start, slab_planes + 2, 0
    )
    moduli = floor_modulus + (1.0 - floor_modulus) * margin**3
    face_x = 0.5 * (moduli[1:] + moduli[:-1]) * face_valid[:, None, None]
    inner_moduli = moduli[1:-1]
    face_z = 0.5 * (inner_moduli[:, 1:] + inner_moduli[:, :-1])
    face_y = 0.5 * (inner_moduli[:, :, 1:] + inner_moduli[:, :, :-1])
    sum_x = face_x[:-1] + face_x[1:]
    sum_z = pad_axis(face_z, 1, 1, 0) + pad_axis(face_z, 1, 0, 1)
    sum_y = pad_axis(face_y, 2, 1, 0) + pad_axis(face_y, 2, 0, 1)
    diagonal = stiff_factors(0) * sum_x + stiff_factors(1) * sum_z + stiff_factors(2) * sum_y
    for sweep_index in range(SWEEPS):
        displace = relax_slab(
            padded, displace, face_x, face_z, face_y, force_field, free_cells, diagonal
        )
        padded = neighbour_planes(displace, load_cases, axis_devices)
    energy_x = slab_energy(padded, 1, 0, load_cases) * face_valid[:, None, None]
    energy_z = slab_energy(displace, 2, 1, load_cases)
    energy_y = slab_energy(displace, 3, 2, load_cases)
    sens_term = 0.5 * (
        energy_x[:-1]
        + energy_x[1:]
        + pad_axis(energy_z, 1, 1, 0)
        + pad_axis(energy_z, 1, 0, 1)
        + pad_axis(energy_y, 2, 1, 0)
        + pad_axis(energy_y, 2, 0, 1)
    )
    sensitive = sens_term
    for level in reversed(range(level_count)):
        half_rows = sensitive.shape[0] // 2
        upper_side = load_place // 2**level % 2 == 1
        outgoing = jnp.where(upper_side, sensitive[:half_rows], sensitive[half_rows:])
        keeping = jnp.where(upper_side, sensitive[half_rows:], sensitive[:half_rows])
        sensitive = keeping + from_partner(outgoing, "space", level)
    weighted_share = 3.0 * (1.0 - floor_modulus) * filtered**2 * sensitive / total_weight
    halo_share = extended(weighted_share, (("space", 0),), window_reach)
    root_term = jnp.sqrt(filter_backward(pad_sides(halo_share), padded_weights))
    lowest = jnp.maximum(density - move_limit, density_floor)
    highest = jnp.minimum(density + move_limit, 1.0)
    design_now = density

    def trial_design(log_level):
        return jnp.clip(design_now * root_term * jnp.exp(-0.5 * log_level), lowest, highest)

    start_state = (jnp.asarray(log_lower, jnp.float32), jnp.asarray(log_span, jnp.float32))

    def halve(search_step, search_state):
        lower_end, span_width = search_state
        half_span = span_width * 0.5
        middle = lower_end + half_span
        volume_total = lax.psum(jnp.sum(trial_design(middle)), "space")
        return (jnp.where(volume_total > target, middle, lower_end), half_span)

    lower_end, span_width = lax.fori_loop(0, SEARCH, halve, start_state)
    density = trial_design(lower_end + 0.5 * span_width)
    new_displacement = displace[None]
    return (density, new_displacement)


def solution(mesh):
    in_specs = (
        P("space", "parts", None),
        P("space", None, None, "parts", None),
        P(None, "parts"),
        P("parts"),
        P("parts", None),
        P("parts"),
    )
    out_specs = (P("space", "parts", None), P("space", None, None, "parts", None))

    def local(density, displacement, fixed, load_index, load_force, radius):
        alone = lax.axis_size("space") == load_index.shape[0]
        run = one_slab if alone else many_slabs
        return run(density, displacement, fixed, load_index, load_force, radius)

    return jax.shard_map(local, mesh=mesh, in_specs=in_specs, out_specs=out_specs, check_vma=False)
```

```python
import math

import jax
import jax.numpy as jnp
from jax import lax
from jax.experimental import pallas as pl
from jax.experimental.pallas import tpu as pltpu
from jax.sharding import PartitionSpec as P

SWEEPS = 3
SEARCH = 12


floor_modulus = 0.05
relax_factor = 0.6
move_limit = 0.2
density_floor = 0.01
volume_share = 0.5
log_lower = -16.0
log_span = 32.0
window_reach = 2

PLANE_SQUARES = (0, 1, 2, 4, 5, 8)
ALL_SQUARES = (0, 1, 2, 3, 4, 5, 6, 8, 9, 12)


def spot_iota(shape, dim):
    return lax.broadcasted_iota(jnp.int32, shape, dim)


def layer_radius(radius_ref, layers, row_width):
    z = spot_iota((layers, row_width), 0)
    result = jnp.zeros((layers, row_width), jnp.int32)
    for layer in range(layers):
        result = jnp.where(z == layer, radius_ref[layer], result)
    return result.astype(jnp.float32)


def class_weights(radius_ref, weight_ref):
    layers, row_width = weight_ref.shape[1:]
    radial = layer_radius(radius_ref, layers, row_width)
    for place, square in enumerate(ALL_SQUARES):
        weight_ref[place] = jnp.maximum(radial - math.sqrt(square), 0.0)


def shift_sum(field, dim, distance):
    size = field.shape[dim]
    spot = spot_iota(field.shape, dim)
    ahead = jnp.where(spot < size - distance, pltpu.roll(field, size - distance, dim), 0.0)
    behind = jnp.where(spot >= distance, pltpu.roll(field, distance, dim), 0.0)
    return ahead + behind


def plane_sums(plane):
    beside = shift_sum(plane, 1, 1)
    further = shift_sum(plane, 1, 2)
    return {
        0: plane,
        1: beside + shift_sum(plane, 0, 1),
        2: shift_sum(beside, 0, 1),
        4: further + shift_sum(plane, 0, 2),
        5: shift_sum(further, 0, 1) + shift_sum(beside, 0, 2),
        8: shift_sum(further, 0, 2),
    }


def weigh(sums, weight_ref, square):
    result = None
    for inner in PLANE_SQUARES:
        term = weight_ref[ALL_SQUARES.index(inner + square)] * sums[inner]
        result = term if result is None else result + term
    return result


def forward_planes(plane, weight_ref):
    sums = plane_sums(plane)
    return [weigh(sums, weight_ref, square) for square in (0, 1, 4)]


def backward_planes(plane, weight_ref):
    beside = shift_sum(plane, 1, 1)
    further = shift_sum(plane, 1, 2)
    results = []
    for square in (0, 1, 4):

        def weight(more):
            return weight_ref[ALL_SQUARES.index(square + more)]

        level = weight(0) * plane + weight(1) * beside + weight(4) * further
        near = weight(1) * plane + weight(2) * beside + weight(5) * further
        far = weight(4) * plane + weight(5) * beside + weight(8) * further
        results.append(level + shift_sum(near, 0, 1) + shift_sum(far, 0, 2))
    return results


def reverse_bits(value, count):
    result = 0
    for bit in range(count):
        result = result + ((value >> bit) & 1) * (1 << (count - 1 - bit))
    return result


def partner_spot(x, own_planes):
    devices = lax.axis_size("space")
    order = reverse_bits((x // own_planes) ^ lax.axis_index("space"), devices.bit_length() - 1)
    return order, x % own_planes


def pair_spot(x, own_planes):
    device = x // own_planes
    core = (device ^ lax.axis_index("space")) & 1
    return core, device >> 1, x % own_planes


def edge_class(x, planes):
    return jnp.minimum(x, 2) + jnp.maximum(x - (planes - 3), 0)


def zero_edges(ref):
    planes = ref.shape[0]
    for place in (0, 1, planes - 2, planes - 1):
        ref[place] = jnp.zeros(ref.shape[1:], ref.dtype)


def prepare_kernel(
    radius_hbm,
    index_hbm,
    force_hbm,
    fixed_hbm,
    density_hbm,
    own_ref,
    weight_ref,
    total_ref,
    free_ref,
    load_ref,
    spot_ref,
    radius_ref,
    index_ref,
    force_ref,
    fixed_ref,
    arrived,
):
    copies = [
        pltpu.make_async_copy(source, target, arrived.at[place])
        for place, (source, target) in enumerate(
            (
                (radius_hbm, radius_ref),
                (index_hbm, index_ref),
                (force_hbm, force_ref),
                (fixed_hbm, fixed_ref),
                (density_hbm, own_ref.at[0]),
            )
        )
    ]
    for copy in copies:
        copy.start()
    for copy in copies:
        copy.wait()
    planes, row_width = fixed_ref.shape
    layers = own_ref.shape[2]
    load_place = lax.axis_index("space")
    shape = (layers, row_width)
    z = spot_iota(shape, 0)
    y = spot_iota(shape, 1)

    class_weights(radius_ref, weight_ref)
    ones = forward_planes(jnp.ones(shape, jnp.float32), weight_ref)
    for place, (lower, upper) in enumerate(((0, 2), (1, 2), (2, 2), (2, 1), (2, 0))):
        total_ref[place] = (
            ones[0] + min(lower, 1) * ones[1] + min(upper, 1) * ones[1]
            + (lower // 2) * ones[2] + (upper // 2) * ones[2]
        )

    def free_plane(x, carry):
        free_ref[x] = jnp.where(
            z == 0, 1.0 - fixed_ref[pl.ds(x, 1), :].astype(jnp.float32), 1.0
        )
        return carry

    lax.fori_loop(0, planes, free_plane, 0, unroll=8)

    own_index = index_ref[load_place]
    own_z = own_index // row_width % layers
    own_y = own_index % row_width
    hit = (z == own_z) & (y == own_y)
    for part in range(3):
        load_ref[part] = jnp.where(hit, force_ref[part, load_place], 0.0)
    spot_ref[0] = own_index // (layers * row_width)


def sweep_kernel(
    spot_ref,
    load_ref,
    weight_ref,
    total_ref,
    free_ref,
    density_ref,
    start_ref,
    disp_ref,
    sens_ref,
    coef_ref,
    near_ref,
    side_ref,
    far_ref,
    modulus_ref,
    across_ref,
    up_ref,
    down_ref,
    right_ref,
    left_ref,
    rate_ref,
    first_ref,
    second_ref,
):
    planes, layers, row_width = coef_ref.shape
    own_planes = density_ref.shape[1]
    load_cases = lax.axis_size("space")
    shape = (layers, row_width)
    z = spot_iota(shape, 0)
    y = spot_iota(shape, 1)
    zero = jnp.zeros(shape, jnp.float32)

    for ref in (side_ref, far_ref):
        zero_edges(ref)

    def filter_plane(x, carry):
        near, side, far = forward_planes(density_ref[partner_spot(x, own_planes)], weight_ref)
        near_ref[x + 2] = near
        side_ref[x + 2] = side
        far_ref[x + 2] = far
        return carry

    lax.fori_loop(0, planes, filter_plane, 0, unroll=8)

    def modulus_plane(x, carry):
        total = total_ref[edge_class(x, planes)]
        filtered = (
            near_ref[x + 2]
            + side_ref[x + 1]
            + side_ref[x + 3]
            + far_ref[x]
            + far_ref[x + 4]
        ) / total
        modulus = floor_modulus + (1.0 - floor_modulus) * (filtered * filtered * filtered)
        modulus_ref[x] = modulus
        coef_ref[x] = 3.0 * (1.0 - floor_modulus) * (filtered * filtered) / total
        return carry

    lax.fori_loop(0, planes, modulus_plane, 0, unroll=8)

    across_ref[0] = zero
    across_ref[planes] = zero
    for ref in (first_ref, second_ref):
        for part in range(3):
            ref[part, 0] = zero
            ref[part, planes + 1] = zero

    def face_plane(x, carry):
        modulus = modulus_ref[x]
        later = modulus_ref[jnp.minimum(x + 1, planes - 1)]
        ahead = jnp.where(x + 1 < planes, 0.5 * (modulus + later), 0.0)
        across_ref[x + 1] = ahead
        up = jnp.where(z < layers - 1, 0.5 * (modulus + pltpu.roll(modulus, layers - 1, 0)), 0.0)
        down = pltpu.roll(up, 1, 0)
        right = jnp.where(
            y < row_width - 1, 0.5 * (modulus + pltpu.roll(modulus, row_width - 1, 1)), 0.0
        )
        left = pltpu.roll(right, 1, 1)
        up_ref[x] = up
        down_ref[x] = down
        right_ref[x] = right
        left_ref[x] = left
        sums = (carry + ahead, up + down, left + right)
        every = sums[0] + sums[1] + sums[2]
        free = free_ref[x]
        push = relax_factor * free
        for part in range(3):
            rate_ref[part, x] = push / (every + sums[part])
            first_ref[part, x + 1] = start_ref[part, x] * free
        return ahead

    lax.fori_loop(0, planes, face_plane, zero, unroll=8)

    own_x = spot_ref[0]

    def sweep(source, target, lead):
        def sweep_plane(x, carry):
            before, after = across_ref[x], across_ref[x + 1]
            up, down, right, left = up_ref[x], down_ref[x], right_ref[x], left_ref[x]
            for part in range(3):
                here = source[part, x + 1]
                pulls = [
                    before * source[part, x] + after * source[part, x + 2],
                    up * pltpu.roll(here, layers - 1, 0) + down * pltpu.roll(here, 1, 0),
                    right * pltpu.roll(here, row_width - 1, 1) + left * pltpu.roll(here, 1, 1),
                ]
                pull = pulls[0] + pulls[1] + pulls[2] + pulls[part]
                target[part, x + lead] = (1.0 - relax_factor) * here + rate_ref[part, x] * pull
            return carry

        lax.fori_loop(0, planes, sweep_plane, 0, unroll=8)
        for part in range(3):
            target[part, own_x + lead] += rate_ref[part, own_x] * load_ref[part]

    stages = (first_ref, second_ref)
    for turn in range(SWEEPS - 1):
        sweep(stages[turn % 2], stages[(turn + 1) % 2], 1)
    sweep(stages[(SWEEPS - 1) % 2], disp_ref, 0)

    def energy_plane(x, carry):
        later = jnp.minimum(x + 1, planes - 1)
        ahead, upward, right = zero, zero, zero
        for part in range(3):
            here = disp_ref[part, x]
            step = disp_ref[part, later] - here
            climb = pltpu.roll(here, layers - 1, 0) - here
            slide = pltpu.roll(here, row_width - 1, 1) - here
            ahead = ahead + (2.0 if part == 0 else 1.0) * (step * step)
            upward = upward + (2.0 if part == 1 else 1.0) * (climb * climb)
            right = right + (2.0 if part == 2 else 1.0) * (slide * slide)
        upward = jnp.where(z < layers - 1, upward, 0.0)
        right = jnp.where(y < row_width - 1, right, 0.0)
        total = carry + ahead + upward + pltpu.roll(upward, 1, 0) + right + pltpu.roll(right, 1, 1)
        sens_ref[pair_spot(x, own_planes)] = (0.5 / load_cases) * total
        return ahead

    lax.fori_loop(0, planes, energy_plane, zero, unroll=8)


def design_kernel(
    weight_ref,
    sens_ref,
    coef_ref,
    density_ref,
    new_ref,
    near_ref,
    side_ref,
    far_ref,
    pull_ref,
    low_ref,
    high_ref,
):
    planes, layers, row_width = coef_ref.shape
    own_planes = density_ref.shape[1]
    place = lax.axis_index("space")
    shape = (layers, row_width)
    zero = jnp.zeros(shape, jnp.float32)
    for ref in (side_ref, far_ref):
        zero_edges(ref)

    def filter_plane(x, carry):
        near, side, far = backward_planes(
            sens_ref[pair_spot(x, own_planes)] * coef_ref[x], weight_ref
        )
        near_ref[x + 2] = near
        side_ref[x + 2] = side
        far_ref[x + 2] = far
        return carry

    lax.fori_loop(0, planes, filter_plane, 0, unroll=8)

    def root_plane(x, carry):
        root = jnp.sqrt(
            near_ref[x + 2] + side_ref[x + 1] + side_ref[x + 3] + far_ref[x] + far_ref[x + 4]
        )
        density = density_ref[partner_spot(x, own_planes)]
        pull_ref[x] = density * root
        low_ref[x] = jnp.maximum(density - move_limit, density_floor)
        high_ref[x] = jnp.minimum(density + move_limit, 1.0)
        return carry

    lax.fori_loop(0, planes, root_plane, 0, unroll=8)

    target = volume_share * planes * layers * row_width

    def trial(x, factor):
        return jnp.minimum(jnp.maximum(pull_ref[x] * factor, low_ref[x]), high_ref[x])

    def halve(step, state):
        lower, span = state
        half = span * 0.5
        middle = lower + half
        factor = jnp.exp(-0.5 * middle)
        total = lax.fori_loop(
            0, planes, lambda x, acc: acc + trial(x, factor), zero, unroll=8
        )
        volume = jnp.sum(jnp.sum(total, axis=0, keepdims=True), axis=1, keepdims=True)
        return jnp.where(volume > target, middle, lower), half

    start = (jnp.full((1, 1), log_lower, jnp.float32), jnp.full((1, 1), log_span, jnp.float32))
    lower, span = lax.fori_loop(0, SEARCH, halve, start)
    factor = jnp.exp(-0.5 * (lower + 0.5 * span))
    for own in range(own_planes):
        new_ref[own] = trial(place * own_planes + own, factor)


def in_vmem():
    return pl.BlockSpec(memory_space=pltpu.VMEM)


def in_smem():
    return pl.BlockSpec(memory_space=pltpu.SMEM)


KERNEL_VMEM = 24 * 2**20


def floats(*shape):
    return jax.ShapeDtypeStruct(shape, jnp.float32)


def prepare_call(radius, load_index, load_force, fixed, density):
    layers, row_width = density.shape[1:]
    planes = fixed.shape[0]
    return pl.pallas_call(
        prepare_kernel,
        out_shape=[
            floats(1, *density.shape),
            floats(len(ALL_SQUARES), layers, row_width),
            floats(2 * window_reach + 1, layers, row_width),
            floats(planes, layers, row_width),
            floats(3, layers, row_width),
            jax.ShapeDtypeStruct((1,), jnp.int32),
        ],
        in_specs=[pl.BlockSpec(memory_space=pltpu.HBM)] * 5,
        out_specs=[in_vmem()] * 5 + [in_smem()],
        scratch_shapes=[
            pltpu.SMEM(radius.shape, radius.dtype),
            pltpu.SMEM(load_index.shape, load_index.dtype),
            pltpu.SMEM(load_force.shape, load_force.dtype),
            pltpu.VMEM(fixed.shape, fixed.dtype),
            pltpu.SemaphoreType.DMA((5,)),
        ],
        compiler_params=pltpu.CompilerParams(vmem_limit_bytes=KERNEL_VMEM),
        cost_estimate=pl.CostEstimate(
            flops=40 * planes * layers * row_width,
            bytes_accessed=8 * planes * layers * row_width,
            transcendentals=0,
        ),
        name="prepare",
    )(
        *(
            pltpu.with_memory_space_constraint(array, pltpu.HBM)
            for array in (radius, load_index, load_force, fixed, density)
        )
    )


def sweep_call(spot, load, weights, totals, free, density, displacement):
    devices, own_planes, layers, row_width = density.shape
    planes = devices * own_planes

    def scratch(*lead):
        return pltpu.VMEM(lead + (layers, row_width), jnp.float32)

    return pl.pallas_call(
        sweep_kernel,
        out_shape=[
            floats(3, planes, layers, row_width),
            floats(2, devices // 2, own_planes, layers, row_width),
            floats(planes, layers, row_width),
        ],
        in_specs=[in_smem()] + [in_vmem()] * 6,
        out_specs=[in_vmem()] * 3,
        scratch_shapes=[
            scratch(planes + 4),
            scratch(planes + 4),
            scratch(planes + 4),
            scratch(planes),
            scratch(planes + 1),
            scratch(planes),
            scratch(planes),
            scratch(planes),
            scratch(planes),
            scratch(3, planes),
            scratch(3, planes + 2),
            scratch(3, planes + 2),
        ],
        compiler_params=pltpu.CompilerParams(vmem_limit_bytes=KERNEL_VMEM),
        name="sweeps",
    )(spot, load, weights, totals, free, density, displacement)


def design_call(weights, sens, coef, density):
    devices, own_planes, layers, row_width = density.shape
    planes = devices * own_planes

    def scratch(*lead):
        return pltpu.VMEM(lead + (layers, row_width), jnp.float32)

    return pl.pallas_call(
        design_kernel,
        out_shape=jax.ShapeDtypeStruct((own_planes, layers, row_width), jnp.float32),
        in_specs=[in_vmem()] * 4,
        out_specs=in_vmem(),
        scratch_shapes=[
            scratch(planes + 4),
            scratch(planes + 4),
            scratch(planes + 4),
            scratch(planes),
            scratch(planes),
            scratch(planes),
        ],
        compiler_params=pltpu.CompilerParams(vmem_limit_bytes=KERNEL_VMEM),
        name="design",
    )(weights, sens, coef, density)


def other_core(block):
    devices = lax.axis_size("space")
    return lax.ppermute(block, "space", [(i, i ^ 1) for i in range(devices)])


def between_chips(pieces):
    devices = lax.axis_size("space")
    groups = [list(range(core, devices, 2)) for core in range(2)]
    return lax.all_to_all(pieces, "space", 0, 0, axis_index_groups=groups)


def gathered(block):
    chips = lax.axis_size("space") // 2
    same = between_chips(jnp.broadcast_to(block[None], (chips,) + block.shape))
    return jnp.stack([same, other_core(same)])


def partner_gathered(block, prepare):
    devices = lax.axis_size("space")

    def swapped(pieces, bit):
        return lax.ppermute(pieces, "space", [(i, i ^ 1 << bit) for i in range(devices)])

    first, *bits = reversed(range(devices.bit_length() - 1))
    other = swapped(block[None], first)
    other, (own, *prepared) = lax.optimization_barrier((other, prepare()))
    pieces = jnp.concatenate([own, other])
    for bit in bits:
        pieces = jnp.concatenate([pieces, swapped(pieces, bit)])
    return pieces, prepared


def scattered_sum(pieces):
    return jnp.sum(between_chips(pieces[0] + other_core(pieces[1])), axis=0)


def one_slab(density, displacement, fixed, load_index, load_force, radius):
    whole, prepared = partner_gathered(
        density, lambda: prepare_call(radius, load_index, load_force.T, fixed, density)
    )
    weights, totals, free, load, spot = prepared
    new_displacement, sens, coef = sweep_call(
        spot, load, weights, totals, free, whole, displacement[0]
    )
    sens = gathered(scattered_sum(sens))
    new_density = design_call(weights, sens, coef, whole)
    return new_density, new_displacement[None]


def from_behind(block, axis, distance):
    devices = range(lax.axis_size(axis))
    route = [(i - distance, i) for i in devices if i - distance in devices]
    return lax.ppermute(block, axis, route)


def extended(x, sides, width):
    for axis, dim in sides:
        size, length = (lax.axis_size(axis), x.shape[dim])
        up = [(i, (i + 1) % size) for i in range(size - 1)]
        down = [(j, i) for i, j in up]
        last = lax.slice_in_dim(x, length - width, length, axis=dim)
        first = lax.slice_in_dim(x, 0, width, axis=dim)
        before = lax.ppermute(last, axis, up)
        after = lax.ppermute(first, axis, down)
        x = jnp.concatenate([before, x, after], axis=dim)
    return x


def from_partner(x, axis, bit):
    return lax.ppermute(x, axis, [(i, i ^ 1 << bit) for i in range(lax.axis_size(axis))])


def window_offsets():
    offsets_list = []
    for across in range(-window_reach, window_reach + 1):
        for upward in range(-window_reach, window_reach + 1):
            for sideways in range(-window_reach, window_reach + 1):
                length = math.sqrt(across * across + upward * upward + sideways * sideways)
                offsets_list.append((across, upward, sideways, length))
    return offsets_list


def layer_weights(radius):
    radial = radius.astype(jnp.float32)
    return jnp.stack(
        [jnp.maximum(radial - length, 0.0) for across, upward, sideways, length in window_offsets()]
    )


def pad_axis(grid_field, along_axis, before, after_cells):
    widths = [(0, 0)] * grid_field.ndim
    widths[along_axis] = (before, after_cells)
    return jnp.pad(grid_field, widths)


def pad_sides(grid_field):
    return jnp.pad(grid_field, ((0, 0), (window_reach, window_reach), (window_reach, window_reach)))


def filter_forward(padded, weights):
    out_rows = padded.shape[0] - 2 * window_reach
    layers = padded.shape[1] - 2 * window_reach
    row_width = padded.shape[2] - 2 * window_reach
    result = jnp.zeros((out_rows, layers, row_width), jnp.float32)
    for offset_index, (across, upward, sideways, length) in enumerate(window_offsets()):
        shifted = padded[
            window_reach + across : window_reach + across + out_rows,
            window_reach + upward : window_reach + upward + layers,
            window_reach + sideways : window_reach + sideways + row_width,
        ]
        result = result + weights[offset_index][None, :, None] * shifted
    return result


def filter_backward(padded, padded_weights):
    out_rows = padded.shape[0] - 2 * window_reach
    layers = padded.shape[1] - 2 * window_reach
    row_width = padded.shape[2] - 2 * window_reach
    result = jnp.zeros((out_rows, layers, row_width), jnp.float32)
    for offset_index, (across, upward, sideways, length) in enumerate(window_offsets()):
        shifted = padded[
            window_reach - across : window_reach - across + out_rows,
            window_reach - upward : window_reach - upward + layers,
            window_reach - sideways : window_reach - sideways + row_width,
        ]
        layer_part = padded_weights[
            offset_index, window_reach - upward : window_reach - upward + layers
        ]
        result = result + layer_part[None, :, None] * shifted
    return result


def stiff_factors(direction):
    return jnp.array(
        [2.0 if component == direction else 1.0 for component in range(3)], jnp.float32
    ).reshape(3, 1, 1, 1)


def relax_slab(padded, displace, face_x, face_z, face_y, force_field, free_cells, diagonal):
    flux_x = stiff_factors(0) * face_x * jnp.diff(padded, axis=1)
    stencil_image = flux_x[:, :-1] - flux_x[:, 1:]
    flux_z = stiff_factors(1) * face_z * jnp.diff(displace, axis=2)
    stencil_image = stencil_image + pad_axis(flux_z, 2, 1, 0) - pad_axis(flux_z, 2, 0, 1)
    flux_y = stiff_factors(2) * face_y * jnp.diff(displace, axis=3)
    stencil_image = stencil_image + pad_axis(flux_y, 3, 1, 0) - pad_axis(flux_y, 3, 0, 1)
    return free_cells * (displace + relax_factor * (force_field - stencil_image) / diagonal)


def slab_energy(grid_field, along_axis, direction, load_cases):
    change = jnp.diff(grid_field, axis=along_axis)
    return jnp.sum(stiff_factors(direction) * change * change, axis=0) / load_cases


def neighbour_planes(displace, load_cases, axis_devices):
    if axis_devices > load_cases:
        below = from_behind(displace[:, -1:], "space", load_cases)
        above = from_behind(displace[:, :1], "space", -load_cases)
    else:
        below = jnp.zeros_like(displace[:, :1])
        above = jnp.zeros_like(displace[:, :1])
    return jnp.concatenate([below, displace, above], axis=1)


def many_slabs(density, displacement, fixed, load_index, load_force, radius):
    slab_rows, layers, row_width = density.shape
    load_cases = load_index.shape[0]
    level_count = load_cases.bit_length() - 1
    axis_devices = lax.axis_size("space")
    axis_place = lax.axis_index("space")
    slab_planes = slab_rows * load_cases
    slab_place = axis_place // load_cases
    load_place = axis_place % load_cases
    total_rows = slab_rows * axis_devices
    weights = layer_weights(radius)
    padded_weights = pad_axis(weights, 1, window_reach, window_reach)
    global_rows = (
        jnp.arange(slab_rows + 2 * window_reach, dtype=jnp.int32)
        + axis_place * slab_rows
        - window_reach
    )
    deep_inside = ((global_rows >= 0) & (global_rows < total_rows)).astype(jnp.float32)
    inside_field = deep_inside[:, None, None] * pad_sides(
        jnp.ones((slab_rows + 2 * window_reach, layers, row_width), jnp.float32)
    )
    total_weight = filter_forward(inside_field, weights)
    slab_start = slab_place * slab_planes
    margin_rows = jnp.arange(slab_planes + 2, dtype=jnp.int32) + slab_start - 1
    margin_inside = ((margin_rows >= 0) & (margin_rows < total_rows)).astype(jnp.float32)
    face_valid = margin_inside[1:] * margin_inside[:-1]
    fixed_slab = lax.dynamic_slice_in_dim(fixed, slab_start, slab_planes, 0).astype(jnp.float32)
    bottom_layer = (jnp.arange(layers, dtype=jnp.int32) == 0).astype(jnp.float32)
    free_cells = 1.0 - bottom_layer[None, :, None] * fixed_slab[:, None, :]
    slab_cells = slab_planes * layers * row_width
    cell_index = jnp.arange(slab_cells, dtype=jnp.int32) + slab_place * slab_cells
    load_hot = jnp.arange(load_cases, dtype=jnp.int32) == load_place
    own_index = jnp.sum(jnp.where(load_hot, load_index, 0))
    own_force = jnp.sum(load_hot.astype(jnp.float32)[:, None] * load_force, axis=0)
    load_hits = (cell_index == own_index).astype(jnp.float32)
    force_field = (own_force[:, None] * load_hits[None, :]).reshape(
        3, slab_planes, layers, row_width
    )
    displace = displacement[0] * free_cells
    target = volume_share * total_rows * layers * row_width
    padded = neighbour_planes(displace, load_cases, axis_devices)
    halo_density = extended(density, (("space", 0),), window_reach)
    filtered = filter_forward(pad_sides(halo_density), weights) / total_weight
    whole_field = lax.all_gather(filtered, "space", axis=0, tiled=True)
    margin = lax.dynamic_slice_in_dim(
        pad_axis(whole_field, 0, 1, 1), slab_start, slab_planes + 2, 0
    )
    moduli = floor_modulus + (1.0 - floor_modulus) * margin**3
    face_x = 0.5 * (moduli[1:] + moduli[:-1]) * face_valid[:, None, None]
    inner_moduli = moduli[1:-1]
    face_z = 0.5 * (inner_moduli[:, 1:] + inner_moduli[:, :-1])
    face_y = 0.5 * (inner_moduli[:, :, 1:] + inner_moduli[:, :, :-1])
    sum_x = face_x[:-1] + face_x[1:]
    sum_z = pad_axis(face_z, 1, 1, 0) + pad_axis(face_z, 1, 0, 1)
    sum_y = pad_axis(face_y, 2, 1, 0) + pad_axis(face_y, 2, 0, 1)
    diagonal = stiff_factors(0) * sum_x + stiff_factors(1) * sum_z + stiff_factors(2) * sum_y
    for sweep_index in range(SWEEPS):
        displace = relax_slab(
            padded, displace, face_x, face_z, face_y, force_field, free_cells, diagonal
        )
        padded = neighbour_planes(displace, load_cases, axis_devices)
    energy_x = slab_energy(padded, 1, 0, load_cases) * face_valid[:, None, None]
    energy_z = slab_energy(displace, 2, 1, load_cases)
    energy_y = slab_energy(displace, 3, 2, load_cases)
    sens_term = 0.5 * (
        energy_x[:-1]
        + energy_x[1:]
        + pad_axis(energy_z, 1, 1, 0)
        + pad_axis(energy_z, 1, 0, 1)
        + pad_axis(energy_y, 2, 1, 0)
        + pad_axis(energy_y, 2, 0, 1)
    )
    sensitive = sens_term
    for level in reversed(range(level_count)):
        half_rows = sensitive.shape[0] // 2
        upper_side = load_place // 2**level % 2 == 1
        outgoing = jnp.where(upper_side, sensitive[:half_rows], sensitive[half_rows:])
        keeping = jnp.where(upper_side, sensitive[half_rows:], sensitive[:half_rows])
        sensitive = keeping + from_partner(outgoing, "space", level)
    weighted_share = 3.0 * (1.0 - floor_modulus) * filtered**2 * sensitive / total_weight
    halo_share = extended(weighted_share, (("space", 0),), window_reach)
    root_term = jnp.sqrt(filter_backward(pad_sides(halo_share), padded_weights))
    lowest = jnp.maximum(density - move_limit, density_floor)
    highest = jnp.minimum(density + move_limit, 1.0)
    design_now = density

    def trial_design(log_level):
        return jnp.clip(design_now * root_term * jnp.exp(-0.5 * log_level), lowest, highest)

    start_state = (jnp.asarray(log_lower, jnp.float32), jnp.asarray(log_span, jnp.float32))

    def halve(search_step, search_state):
        lower_end, span_width = search_state
        half_span = span_width * 0.5
        middle = lower_end + half_span
        volume_total = lax.psum(jnp.sum(trial_design(middle)), "space")
        return (jnp.where(volume_total > target, middle, lower_end), half_span)

    lower_end, span_width = lax.fori_loop(0, SEARCH, halve, start_state)
    density = trial_design(lower_end + 0.5 * span_width)
    new_displacement = displace[None]
    return (density, new_displacement)


def solution(mesh):
    in_specs = (
        P("space", "parts", None),
        P("space", None, None, "parts", None),
        P(None, "parts"),
        P("parts"),
        P("parts", None),
        P("parts"),
    )
    out_specs = (P("space", "parts", None), P("space", None, None, "parts", None))

    def local(density, displacement, fixed, load_index, load_force, radius):
        alone = lax.axis_size("space") == load_index.shape[0]
        run = one_slab if alone else many_slabs
        return run(density, displacement, fixed, load_index, load_force, radius)

    return jax.shard_map(local, mesh=mesh, in_specs=in_specs, out_specs=out_specs, check_vma=False)
```

```python
import math

import jax
import jax.numpy as jnp
from jax import lax
from jax.experimental import pallas as pl
from jax.experimental.pallas import tpu as pltpu
from jax.sharding import PartitionSpec as P

SWEEPS = 3
SEARCH = 12


floor_modulus = 0.05
relax_factor = 0.6
move_limit = 0.2
density_floor = 0.01
volume_share = 0.5
log_lower = -16.0
log_span = 32.0
window_reach = 2

PLANE_SQUARES = (0, 1, 2, 4, 5, 8)
ALL_SQUARES = (0, 1, 2, 3, 4, 5, 6, 8, 9, 12)


def spot_iota(shape, dim):
    return lax.broadcasted_iota(jnp.int32, shape, dim)


def layer_radius(radius_ref, layers, row_width):
    z = spot_iota((layers, row_width), 0)
    result = jnp.zeros((layers, row_width), jnp.int32)
    for layer in range(layers):
        result = jnp.where(z == layer, radius_ref[layer], result)
    return result.astype(jnp.float32)


def class_weights(radius_ref, weight_ref):
    layers, row_width = weight_ref.shape[1:]
    radial = layer_radius(radius_ref, layers, row_width)
    for place, square in enumerate(ALL_SQUARES):
        weight_ref[place] = jnp.maximum(radial - math.sqrt(square), 0.0)


def shift_sum(field, dim, distance):
    size = field.shape[dim]
    spot = spot_iota(field.shape, dim)
    ahead = jnp.where(spot < size - distance, pltpu.roll(field, size - distance, dim), 0.0)
    behind = jnp.where(spot >= distance, pltpu.roll(field, distance, dim), 0.0)
    return ahead + behind


def plane_sums(plane):
    beside = shift_sum(plane, 1, 1)
    further = shift_sum(plane, 1, 2)
    return {
        0: plane,
        1: beside + shift_sum(plane, 0, 1),
        2: shift_sum(beside, 0, 1),
        4: further + shift_sum(plane, 0, 2),
        5: shift_sum(further, 0, 1) + shift_sum(beside, 0, 2),
        8: shift_sum(further, 0, 2),
    }


def weigh(sums, weight_ref, square):
    result = None
    for inner in PLANE_SQUARES:
        term = weight_ref[ALL_SQUARES.index(inner + square)] * sums[inner]
        result = term if result is None else result + term
    return result


def forward_planes(plane, weight_ref):
    sums = plane_sums(plane)
    return [weigh(sums, weight_ref, square) for square in (0, 1, 4)]


def backward_planes(plane, weight_ref):
    beside = shift_sum(plane, 1, 1)
    further = shift_sum(plane, 1, 2)
    results = []
    for square in (0, 1, 4):

        def weight(more):
            return weight_ref[ALL_SQUARES.index(square + more)]

        level = weight(0) * plane + weight(1) * beside + weight(4) * further
        near = weight(1) * plane + weight(2) * beside + weight(5) * further
        far = weight(4) * plane + weight(5) * beside + weight(8) * further
        results.append(level + shift_sum(near, 0, 1) + shift_sum(far, 0, 2))
    return results


def pair_spot(x, own_planes):
    device = x // own_planes
    core = (device ^ lax.axis_index("space")) & 1
    return core, device >> 1, x % own_planes


def edge_class(x, planes):
    return jnp.minimum(x, 2) + jnp.maximum(x - (planes - 3), 0)


def zero_edges(ref):
    planes = ref.shape[0]
    for place in (0, 1, planes - 2, planes - 1):
        ref[place] = jnp.zeros(ref.shape[1:], ref.dtype)


def prepare_kernel(
    radius_hbm,
    index_hbm,
    force_hbm,
    fixed_hbm,
    weight_ref,
    total_ref,
    free_ref,
    load_ref,
    spot_ref,
    radius_ref,
    index_ref,
    force_ref,
    fixed_ref,
    arrived,
):
    copies = [
        pltpu.make_async_copy(source, target, arrived.at[place])
        for place, (source, target) in enumerate(
            (
                (radius_hbm, radius_ref),
                (index_hbm, index_ref),
                (force_hbm, force_ref),
                (fixed_hbm, fixed_ref),
            )
        )
    ]
    for copy in copies:
        copy.start()
    for copy in copies:
        copy.wait()
    planes, layers, row_width = free_ref.shape
    load_place = lax.axis_index("space")
    shape = (layers, row_width)
    z = spot_iota(shape, 0)
    y = spot_iota(shape, 1)

    class_weights(radius_ref, weight_ref)
    ones = forward_planes(jnp.ones(shape, jnp.float32), weight_ref)
    for place, (lower, upper) in enumerate(((0, 2), (1, 2), (2, 2), (2, 1), (2, 0))):
        total_ref[place] = (
            ones[0] + min(lower, 1) * ones[1] + min(upper, 1) * ones[1]
            + (lower // 2) * ones[2] + (upper // 2) * ones[2]
        )

    def free_plane(x, carry):
        free_ref[x] = jnp.where(
            z == 0, 1.0 - fixed_ref[pl.ds(x, 1), :].astype(jnp.float32), 1.0
        )
        return carry

    lax.fori_loop(0, planes, free_plane, 0, unroll=8)

    own_index = index_ref[load_place]
    own_z = own_index // row_width % layers
    own_y = own_index % row_width
    hit = (z == own_z) & (y == own_y)
    for part in range(3):
        load_ref[part] = jnp.where(hit, force_ref[part, load_place], 0.0)
    spot_ref[0] = own_index // (layers * row_width)


def sweep_kernel(
    spot_ref,
    load_ref,
    weight_ref,
    total_ref,
    free_ref,
    density_ref,
    start_ref,
    disp_ref,
    sens_ref,
    coef_ref,
    near_ref,
    side_ref,
    far_ref,
    modulus_ref,
    across_ref,
    up_ref,
    down_ref,
    right_ref,
    left_ref,
    rate_ref,
    first_ref,
    second_ref,
):
    planes, layers, row_width = coef_ref.shape
    own_planes = density_ref.shape[2]
    load_cases = lax.axis_size("space")
    shape = (layers, row_width)
    z = spot_iota(shape, 0)
    y = spot_iota(shape, 1)
    zero = jnp.zeros(shape, jnp.float32)

    for ref in (side_ref, far_ref):
        zero_edges(ref)

    def filter_plane(x, carry):
        near, side, far = forward_planes(density_ref[pair_spot(x, own_planes)], weight_ref)
        near_ref[x + 2] = near
        side_ref[x + 2] = side
        far_ref[x + 2] = far
        return carry

    lax.fori_loop(0, planes, filter_plane, 0, unroll=8)

    def modulus_plane(x, carry):
        total = total_ref[edge_class(x, planes)]
        filtered = (
            near_ref[x + 2]
            + side_ref[x + 1]
            + side_ref[x + 3]
            + far_ref[x]
            + far_ref[x + 4]
        ) / total
        modulus = floor_modulus + (1.0 - floor_modulus) * (filtered * filtered * filtered)
        modulus_ref[x] = modulus
        coef_ref[x] = 3.0 * (1.0 - floor_modulus) * (filtered * filtered) / total
        return carry

    lax.fori_loop(0, planes, modulus_plane, 0, unroll=8)

    across_ref[0] = zero
    across_ref[planes] = zero
    for ref in (first_ref, second_ref):
        for part in range(3):
            ref[part, 0] = zero
            ref[part, planes + 1] = zero

    def face_plane(x, carry):
        modulus = modulus_ref[x]
        later = modulus_ref[jnp.minimum(x + 1, planes - 1)]
        ahead = jnp.where(x + 1 < planes, 0.5 * (modulus + later), 0.0)
        across_ref[x + 1] = ahead
        up = jnp.where(z < layers - 1, 0.5 * (modulus + pltpu.roll(modulus, layers - 1, 0)), 0.0)
        down = pltpu.roll(up, 1, 0)
        right = jnp.where(
            y < row_width - 1, 0.5 * (modulus + pltpu.roll(modulus, row_width - 1, 1)), 0.0
        )
        left = pltpu.roll(right, 1, 1)
        up_ref[x] = up
        down_ref[x] = down
        right_ref[x] = right
        left_ref[x] = left
        sums = (carry + ahead, up + down, left + right)
        every = sums[0] + sums[1] + sums[2]
        free = free_ref[x]
        push = relax_factor * free
        for part in range(3):
            rate_ref[part, x] = push / (every + sums[part])
            first_ref[part, x + 1] = start_ref[part, x] * free
        return ahead

    lax.fori_loop(0, planes, face_plane, zero, unroll=8)

    own_x = spot_ref[0]

    def sweep(source, target, lead):
        def sweep_plane(x, carry):
            before, after = across_ref[x], across_ref[x + 1]
            up, down, right, left = up_ref[x], down_ref[x], right_ref[x], left_ref[x]
            for part in range(3):
                here = source[part, x + 1]
                pulls = [
                    before * source[part, x] + after * source[part, x + 2],
                    up * pltpu.roll(here, layers - 1, 0) + down * pltpu.roll(here, 1, 0),
                    right * pltpu.roll(here, row_width - 1, 1) + left * pltpu.roll(here, 1, 1),
                ]
                pull = pulls[0] + pulls[1] + pulls[2] + pulls[part]
                target[part, x + lead] = (1.0 - relax_factor) * here + rate_ref[part, x] * pull
            return carry

        lax.fori_loop(0, planes, sweep_plane, 0, unroll=8)
        for part in range(3):
            target[part, own_x + lead] += rate_ref[part, own_x] * load_ref[part]

    stages = (first_ref, second_ref)
    for turn in range(SWEEPS - 1):
        sweep(stages[turn % 2], stages[(turn + 1) % 2], 1)
    sweep(stages[(SWEEPS - 1) % 2], disp_ref, 0)

    def energy_plane(x, carry):
        later = jnp.minimum(x + 1, planes - 1)
        ahead, upward, right = zero, zero, zero
        for part in range(3):
            here = disp_ref[part, x]
            step = disp_ref[part, later] - here
            climb = pltpu.roll(here, layers - 1, 0) - here
            slide = pltpu.roll(here, row_width - 1, 1) - here
            ahead = ahead + (2.0 if part == 0 else 1.0) * (step * step)
            upward = upward + (2.0 if part == 1 else 1.0) * (climb * climb)
            right = right + (2.0 if part == 2 else 1.0) * (slide * slide)
        upward = jnp.where(z < layers - 1, upward, 0.0)
        right = jnp.where(y < row_width - 1, right, 0.0)
        total = carry + ahead + upward + pltpu.roll(upward, 1, 0) + right + pltpu.roll(right, 1, 1)
        sens_ref[pair_spot(x, own_planes)] = (0.5 / load_cases) * total
        return ahead

    lax.fori_loop(0, planes, energy_plane, zero, unroll=8)


def design_kernel(
    weight_ref,
    sens_ref,
    coef_ref,
    density_ref,
    new_ref,
    near_ref,
    side_ref,
    far_ref,
    pull_ref,
    low_ref,
    high_ref,
):
    planes, layers, row_width = coef_ref.shape
    own_planes = density_ref.shape[2]
    place = lax.axis_index("space")
    shape = (layers, row_width)
    zero = jnp.zeros(shape, jnp.float32)
    for ref in (side_ref, far_ref):
        zero_edges(ref)

    def filter_plane(x, carry):
        near, side, far = backward_planes(
            sens_ref[pair_spot(x, own_planes)] * coef_ref[x], weight_ref
        )
        near_ref[x + 2] = near
        side_ref[x + 2] = side
        far_ref[x + 2] = far
        return carry

    lax.fori_loop(0, planes, filter_plane, 0, unroll=8)

    def root_plane(x, carry):
        root = jnp.sqrt(
            near_ref[x + 2] + side_ref[x + 1] + side_ref[x + 3] + far_ref[x] + far_ref[x + 4]
        )
        density = density_ref[pair_spot(x, own_planes)]
        pull_ref[x] = density * root
        low_ref[x] = jnp.maximum(density - move_limit, density_floor)
        high_ref[x] = jnp.minimum(density + move_limit, 1.0)
        return carry

    lax.fori_loop(0, planes, root_plane, 0, unroll=8)

    target = volume_share * planes * layers * row_width

    def trial(x, factor):
        return jnp.minimum(jnp.maximum(pull_ref[x] * factor, low_ref[x]), high_ref[x])

    def halve(step, state):
        lower, span = state
        half = span * 0.5
        middle = lower + half
        factor = jnp.exp(-0.5 * middle)
        total = lax.fori_loop(
            0, planes, lambda x, acc: acc + trial(x, factor), zero, unroll=8
        )
        volume = jnp.sum(jnp.sum(total, axis=0, keepdims=True), axis=1, keepdims=True)
        return jnp.where(volume > target, middle, lower), half

    start = (jnp.full((1, 1), log_lower, jnp.float32), jnp.full((1, 1), log_span, jnp.float32))
    lower, span = lax.fori_loop(0, SEARCH, halve, start)
    factor = jnp.exp(-0.5 * (lower + 0.5 * span))
    for own in range(own_planes):
        new_ref[own] = trial(place * own_planes + own, factor)


def in_vmem():
    return pl.BlockSpec(memory_space=pltpu.VMEM)


def in_smem():
    return pl.BlockSpec(memory_space=pltpu.SMEM)


KERNEL_VMEM = 24 * 2**20


def floats(*shape):
    return jax.ShapeDtypeStruct(shape, jnp.float32)


def prepare_call(radius, load_index, load_force, fixed):
    planes, row_width = fixed.shape
    layers = radius.shape[0]
    return pl.pallas_call(
        prepare_kernel,
        out_shape=[
            floats(len(ALL_SQUARES), layers, row_width),
            floats(2 * window_reach + 1, layers, row_width),
            floats(planes, layers, row_width),
            floats(3, layers, row_width),
            jax.ShapeDtypeStruct((1,), jnp.int32),
        ],
        in_specs=[pl.BlockSpec(memory_space=pltpu.HBM)] * 4,
        out_specs=[in_vmem()] * 4 + [in_smem()],
        scratch_shapes=[
            pltpu.SMEM(radius.shape, radius.dtype),
            pltpu.SMEM(load_index.shape, load_index.dtype),
            pltpu.SMEM(load_force.shape, load_force.dtype),
            pltpu.VMEM(fixed.shape, fixed.dtype),
            pltpu.SemaphoreType.DMA((4,)),
        ],
        compiler_params=pltpu.CompilerParams(vmem_limit_bytes=KERNEL_VMEM),
        cost_estimate=pl.CostEstimate(
            flops=40 * planes * layers * row_width,
            bytes_accessed=8 * planes * layers * row_width,
            transcendentals=0,
        ),
        name="prepare",
    )(
        *(
            pltpu.with_memory_space_constraint(array, pltpu.HBM)
            for array in (radius, load_index, load_force, fixed)
        )
    )


def sweep_call(spot, load, weights, totals, free, density, displacement):
    cores, chips, own_planes, layers, row_width = density.shape
    planes = cores * chips * own_planes

    def scratch(*lead):
        return pltpu.VMEM(lead + (layers, row_width), jnp.float32)

    return pl.pallas_call(
        sweep_kernel,
        out_shape=[
            floats(3, planes, layers, row_width),
            floats(*density.shape),
            floats(planes, layers, row_width),
        ],
        in_specs=[in_smem()] + [in_vmem()] * 6,
        out_specs=[in_vmem()] * 3,
        scratch_shapes=[
            scratch(planes + 4),
            scratch(planes + 4),
            scratch(planes + 4),
            scratch(planes),
            scratch(planes + 1),
            scratch(planes),
            scratch(planes),
            scratch(planes),
            scratch(planes),
            scratch(3, planes),
            scratch(3, planes + 2),
            scratch(3, planes + 2),
        ],
        compiler_params=pltpu.CompilerParams(vmem_limit_bytes=KERNEL_VMEM),
        name="sweeps",
    )(spot, load, weights, totals, free, density, displacement)


def design_call(weights, sens, coef, density):
    cores, chips, own_planes, layers, row_width = density.shape
    planes = cores * chips * own_planes

    def scratch(*lead):
        return pltpu.VMEM(lead + (layers, row_width), jnp.float32)

    return pl.pallas_call(
        design_kernel,
        out_shape=jax.ShapeDtypeStruct((own_planes, layers, row_width), jnp.float32),
        in_specs=[in_vmem()] * 4,
        out_specs=in_vmem(),
        scratch_shapes=[
            scratch(planes + 4),
            scratch(planes + 4),
            scratch(planes + 4),
            scratch(planes),
            scratch(planes),
            scratch(planes),
        ],
        compiler_params=pltpu.CompilerParams(vmem_limit_bytes=KERNEL_VMEM),
        name="design",
    )(weights, sens, coef, density)


def other_core(block):
    devices = lax.axis_size("space")
    return lax.ppermute(block, "space", [(i, i ^ 1) for i in range(devices)])


def between_chips(pieces):
    devices = lax.axis_size("space")
    groups = [list(range(core, devices, 2)) for core in range(2)]
    return lax.all_to_all(pieces, "space", 0, 0, axis_index_groups=groups)


def chip_gathered(block):
    chips = lax.axis_size("space") // 2
    return between_chips(jnp.broadcast_to(block[None], (chips,) + block.shape))


def with_other_core(blocks):
    return jnp.stack([blocks, other_core(blocks)])


def scattered_sum(pieces):
    return jnp.sum(between_chips(pieces[0] + other_core(pieces[1])), axis=0)


def one_slab(density, displacement, fixed, load_index, load_force, radius):
    same_core, small = lax.optimization_barrier(
        (chip_gathered(density), (radius, load_index, load_force.T, fixed))
    )
    whole = with_other_core(same_core)
    weights, totals, free, load, spot = prepare_call(*small)
    new_displacement, sens, coef = sweep_call(
        spot, load, weights, totals, free, whole, displacement[0]
    )
    sens = with_other_core(chip_gathered(scattered_sum(sens)))
    new_density = design_call(weights, sens, coef, whole)
    return new_density, new_displacement[None]


def from_behind(block, axis, distance):
    devices = range(lax.axis_size(axis))
    route = [(i - distance, i) for i in devices if i - distance in devices]
    return lax.ppermute(block, axis, route)


def extended(x, sides, width):
    for axis, dim in sides:
        size, length = (lax.axis_size(axis), x.shape[dim])
        up = [(i, (i + 1) % size) for i in range(size - 1)]
        down = [(j, i) for i, j in up]
        last = lax.slice_in_dim(x, length - width, length, axis=dim)
        first = lax.slice_in_dim(x, 0, width, axis=dim)
        before = lax.ppermute(last, axis, up)
        after = lax.ppermute(first, axis, down)
        x = jnp.concatenate([before, x, after], axis=dim)
    return x


def from_partner(x, axis, bit):
    return lax.ppermute(x, axis, [(i, i ^ 1 << bit) for i in range(lax.axis_size(axis))])


def window_offsets():
    offsets_list = []
    for across in range(-window_reach, window_reach + 1):
        for upward in range(-window_reach, window_reach + 1):
            for sideways in range(-window_reach, window_reach + 1):
                length = math.sqrt(across * across + upward * upward + sideways * sideways)
                offsets_list.append((across, upward, sideways, length))
    return offsets_list


def layer_weights(radius):
    radial = radius.astype(jnp.float32)
    return jnp.stack(
        [jnp.maximum(radial - length, 0.0) for across, upward, sideways, length in window_offsets()]
    )


def pad_axis(grid_field, along_axis, before, after_cells):
    widths = [(0, 0)] * grid_field.ndim
    widths[along_axis] = (before, after_cells)
    return jnp.pad(grid_field, widths)


def pad_sides(grid_field):
    return jnp.pad(grid_field, ((0, 0), (window_reach, window_reach), (window_reach, window_reach)))


def filter_forward(padded, weights):
    out_rows = padded.shape[0] - 2 * window_reach
    layers = padded.shape[1] - 2 * window_reach
    row_width = padded.shape[2] - 2 * window_reach
    result = jnp.zeros((out_rows, layers, row_width), jnp.float32)
    for offset_index, (across, upward, sideways, length) in enumerate(window_offsets()):
        shifted = padded[
            window_reach + across : window_reach + across + out_rows,
            window_reach + upward : window_reach + upward + layers,
            window_reach + sideways : window_reach + sideways + row_width,
        ]
        result = result + weights[offset_index][None, :, None] * shifted
    return result


def filter_backward(padded, padded_weights):
    out_rows = padded.shape[0] - 2 * window_reach
    layers = padded.shape[1] - 2 * window_reach
    row_width = padded.shape[2] - 2 * window_reach
    result = jnp.zeros((out_rows, layers, row_width), jnp.float32)
    for offset_index, (across, upward, sideways, length) in enumerate(window_offsets()):
        shifted = padded[
            window_reach - across : window_reach - across + out_rows,
            window_reach - upward : window_reach - upward + layers,
            window_reach - sideways : window_reach - sideways + row_width,
        ]
        layer_part = padded_weights[
            offset_index, window_reach - upward : window_reach - upward + layers
        ]
        result = result + layer_part[None, :, None] * shifted
    return result


def stiff_factors(direction):
    return jnp.array(
        [2.0 if component == direction else 1.0 for component in range(3)], jnp.float32
    ).reshape(3, 1, 1, 1)


def relax_slab(padded, displace, face_x, face_z, face_y, force_field, free_cells, diagonal):
    flux_x = stiff_factors(0) * face_x * jnp.diff(padded, axis=1)
    stencil_image = flux_x[:, :-1] - flux_x[:, 1:]
    flux_z = stiff_factors(1) * face_z * jnp.diff(displace, axis=2)
    stencil_image = stencil_image + pad_axis(flux_z, 2, 1, 0) - pad_axis(flux_z, 2, 0, 1)
    flux_y = stiff_factors(2) * face_y * jnp.diff(displace, axis=3)
    stencil_image = stencil_image + pad_axis(flux_y, 3, 1, 0) - pad_axis(flux_y, 3, 0, 1)
    return free_cells * (displace + relax_factor * (force_field - stencil_image) / diagonal)


def slab_energy(grid_field, along_axis, direction, load_cases):
    change = jnp.diff(grid_field, axis=along_axis)
    return jnp.sum(stiff_factors(direction) * change * change, axis=0) / load_cases


def neighbour_planes(displace, load_cases, axis_devices):
    if axis_devices > load_cases:
        below = from_behind(displace[:, -1:], "space", load_cases)
        above = from_behind(displace[:, :1], "space", -load_cases)
    else:
        below = jnp.zeros_like(displace[:, :1])
        above = jnp.zeros_like(displace[:, :1])
    return jnp.concatenate([below, displace, above], axis=1)


def many_slabs(density, displacement, fixed, load_index, load_force, radius):
    slab_rows, layers, row_width = density.shape
    load_cases = load_index.shape[0]
    level_count = load_cases.bit_length() - 1
    axis_devices = lax.axis_size("space")
    axis_place = lax.axis_index("space")
    slab_planes = slab_rows * load_cases
    slab_place = axis_place // load_cases
    load_place = axis_place % load_cases
    total_rows = slab_rows * axis_devices
    weights = layer_weights(radius)
    padded_weights = pad_axis(weights, 1, window_reach, window_reach)
    global_rows = (
        jnp.arange(slab_rows + 2 * window_reach, dtype=jnp.int32)
        + axis_place * slab_rows
        - window_reach
    )
    deep_inside = ((global_rows >= 0) & (global_rows < total_rows)).astype(jnp.float32)
    inside_field = deep_inside[:, None, None] * pad_sides(
        jnp.ones((slab_rows + 2 * window_reach, layers, row_width), jnp.float32)
    )
    total_weight = filter_forward(inside_field, weights)
    slab_start = slab_place * slab_planes
    margin_rows = jnp.arange(slab_planes + 2, dtype=jnp.int32) + slab_start - 1
    margin_inside = ((margin_rows >= 0) & (margin_rows < total_rows)).astype(jnp.float32)
    face_valid = margin_inside[1:] * margin_inside[:-1]
    fixed_slab = lax.dynamic_slice_in_dim(fixed, slab_start, slab_planes, 0).astype(jnp.float32)
    bottom_layer = (jnp.arange(layers, dtype=jnp.int32) == 0).astype(jnp.float32)
    free_cells = 1.0 - bottom_layer[None, :, None] * fixed_slab[:, None, :]
    slab_cells = slab_planes * layers * row_width
    cell_index = jnp.arange(slab_cells, dtype=jnp.int32) + slab_place * slab_cells
    load_hot = jnp.arange(load_cases, dtype=jnp.int32) == load_place
    own_index = jnp.sum(jnp.where(load_hot, load_index, 0))
    own_force = jnp.sum(load_hot.astype(jnp.float32)[:, None] * load_force, axis=0)
    load_hits = (cell_index == own_index).astype(jnp.float32)
    force_field = (own_force[:, None] * load_hits[None, :]).reshape(
        3, slab_planes, layers, row_width
    )
    displace = displacement[0] * free_cells
    target = volume_share * total_rows * layers * row_width
    padded = neighbour_planes(displace, load_cases, axis_devices)
    halo_density = extended(density, (("space", 0),), window_reach)
    filtered = filter_forward(pad_sides(halo_density), weights) / total_weight
    whole_field = lax.all_gather(filtered, "space", axis=0, tiled=True)
    margin = lax.dynamic_slice_in_dim(
        pad_axis(whole_field, 0, 1, 1), slab_start, slab_planes + 2, 0
    )
    moduli = floor_modulus + (1.0 - floor_modulus) * margin**3
    face_x = 0.5 * (moduli[1:] + moduli[:-1]) * face_valid[:, None, None]
    inner_moduli = moduli[1:-1]
    face_z = 0.5 * (inner_moduli[:, 1:] + inner_moduli[:, :-1])
    face_y = 0.5 * (inner_moduli[:, :, 1:] + inner_moduli[:, :, :-1])
    sum_x = face_x[:-1] + face_x[1:]
    sum_z = pad_axis(face_z, 1, 1, 0) + pad_axis(face_z, 1, 0, 1)
    sum_y = pad_axis(face_y, 2, 1, 0) + pad_axis(face_y, 2, 0, 1)
    diagonal = stiff_factors(0) * sum_x + stiff_factors(1) * sum_z + stiff_factors(2) * sum_y
    for sweep_index in range(SWEEPS):
        displace = relax_slab(
            padded, displace, face_x, face_z, face_y, force_field, free_cells, diagonal
        )
        padded = neighbour_planes(displace, load_cases, axis_devices)
    energy_x = slab_energy(padded, 1, 0, load_cases) * face_valid[:, None, None]
    energy_z = slab_energy(displace, 2, 1, load_cases)
    energy_y = slab_energy(displace, 3, 2, load_cases)
    sens_term = 0.5 * (
        energy_x[:-1]
        + energy_x[1:]
        + pad_axis(energy_z, 1, 1, 0)
        + pad_axis(energy_z, 1, 0, 1)
        + pad_axis(energy_y, 2, 1, 0)
        + pad_axis(energy_y, 2, 0, 1)
    )
    sensitive = sens_term
    for level in reversed(range(level_count)):
        half_rows = sensitive.shape[0] // 2
        upper_side = load_place // 2**level % 2 == 1
        outgoing = jnp.where(upper_side, sensitive[:half_rows], sensitive[half_rows:])
        keeping = jnp.where(upper_side, sensitive[half_rows:], sensitive[:half_rows])
        sensitive = keeping + from_partner(outgoing, "space", level)
    weighted_share = 3.0 * (1.0 - floor_modulus) * filtered**2 * sensitive / total_weight
    halo_share = extended(weighted_share, (("space", 0),), window_reach)
    root_term = jnp.sqrt(filter_backward(pad_sides(halo_share), padded_weights))
    lowest = jnp.maximum(density - move_limit, density_floor)
    highest = jnp.minimum(density + move_limit, 1.0)
    design_now = density

    def trial_design(log_level):
        return jnp.clip(design_now * root_term * jnp.exp(-0.5 * log_level), lowest, highest)

    start_state = (jnp.asarray(log_lower, jnp.float32), jnp.asarray(log_span, jnp.float32))

    def halve(search_step, search_state):
        lower_end, span_width = search_state
        half_span = span_width * 0.5
        middle = lower_end + half_span
        volume_total = lax.psum(jnp.sum(trial_design(middle)), "space")
        return (jnp.where(volume_total > target, middle, lower_end), half_span)

    lower_end, span_width = lax.fori_loop(0, SEARCH, halve, start_state)
    density = trial_design(lower_end + 0.5 * span_width)
    new_displacement = displace[None]
    return (density, new_displacement)


def solution(mesh):
    in_specs = (
        P("space", "parts", None),
        P("space", None, None, "parts", None),
        P(None, "parts"),
        P("parts"),
        P("parts", None),
        P("parts"),
    )
    out_specs = (P("space", "parts", None), P("space", None, None, "parts", None))

    def local(density, displacement, fixed, load_index, load_force, radius):
        alone = lax.axis_size("space") == load_index.shape[0]
        run = one_slab if alone else many_slabs
        return run(density, displacement, fixed, load_index, load_force, radius)

    return jax.shard_map(local, mesh=mesh, in_specs=in_specs, out_specs=out_specs, check_vma=False)
```

```python
import math

import jax
import jax.numpy as jnp
from jax import lax
from jax.experimental import pallas as pl
from jax.experimental.pallas import tpu as pltpu
from jax.sharding import PartitionSpec as P

SWEEPS = 3
SEARCH = 12


floor_modulus = 0.05
relax_factor = 0.6
move_limit = 0.2
density_floor = 0.01
volume_share = 0.5
log_lower = -16.0
log_span = 32.0
window_reach = 2

PLANE_SQUARES = (0, 1, 2, 4, 5, 8)
ALL_SQUARES = (0, 1, 2, 3, 4, 5, 6, 8, 9, 12)


def spot_iota(shape, dim):
    return lax.broadcasted_iota(jnp.int32, shape, dim)


def layer_radius(radius_ref, layers, row_width):
    z = spot_iota((layers, row_width), 0)
    result = jnp.zeros((layers, row_width), jnp.int32)
    for layer in range(layers):
        result = jnp.where(z == layer, radius_ref[layer], result)
    return result.astype(jnp.float32)


def class_weights(radius_ref, weight_ref):
    layers, row_width = weight_ref.shape[1:]
    radial = layer_radius(radius_ref, layers, row_width)
    for place, square in enumerate(ALL_SQUARES):
        weight_ref[place] = jnp.maximum(radial - math.sqrt(square), 0.0)


def shift_sum(field, dim, distance):
    size = field.shape[dim]
    spot = spot_iota(field.shape, dim)
    ahead = jnp.where(spot < size - distance, pltpu.roll(field, size - distance, dim), 0.0)
    behind = jnp.where(spot >= distance, pltpu.roll(field, distance, dim), 0.0)
    return ahead + behind


def plane_sums(plane):
    beside = shift_sum(plane, 1, 1)
    further = shift_sum(plane, 1, 2)
    return {
        0: plane,
        1: beside + shift_sum(plane, 0, 1),
        2: shift_sum(beside, 0, 1),
        4: further + shift_sum(plane, 0, 2),
        5: shift_sum(further, 0, 1) + shift_sum(beside, 0, 2),
        8: shift_sum(further, 0, 2),
    }


def weigh(sums, weight_ref, square):
    result = None
    for inner in PLANE_SQUARES:
        term = weight_ref[ALL_SQUARES.index(inner + square)] * sums[inner]
        result = term if result is None else result + term
    return result


def forward_planes(plane, weight_ref):
    sums = plane_sums(plane)
    return [weigh(sums, weight_ref, square) for square in (0, 1, 4)]


def backward_planes(plane, weight_ref):
    beside = shift_sum(plane, 1, 1)
    further = shift_sum(plane, 1, 2)
    results = []
    for square in (0, 1, 4):

        def weight(more):
            return weight_ref[ALL_SQUARES.index(square + more)]

        level = weight(0) * plane + weight(1) * beside + weight(4) * further
        near = weight(1) * plane + weight(2) * beside + weight(5) * further
        far = weight(4) * plane + weight(5) * beside + weight(8) * further
        results.append(level + shift_sum(near, 0, 1) + shift_sum(far, 0, 2))
    return results


def pair_spot(x, own_planes):
    device = x // own_planes
    core = (device ^ lax.axis_index("space")) & 1
    return core, device >> 1, x % own_planes


def edge_class(x, planes):
    return jnp.minimum(x, 2) + jnp.maximum(x - (planes - 3), 0)


def zero_edges(ref):
    planes = ref.shape[0]
    for place in (0, 1, planes - 2, planes - 1):
        ref[place] = jnp.zeros(ref.shape[1:], ref.dtype)


def prepare_kernel(
    radius_hbm,
    index_hbm,
    force_hbm,
    fixed_hbm,
    weight_ref,
    total_ref,
    free_ref,
    load_ref,
    spot_ref,
    radius_ref,
    index_ref,
    force_ref,
    fixed_ref,
    arrived,
):
    copies = [
        pltpu.make_async_copy(source, target, arrived.at[place])
        for place, (source, target) in enumerate(
            (
                (radius_hbm, radius_ref),
                (index_hbm, index_ref),
                (force_hbm, force_ref),
                (fixed_hbm, fixed_ref),
            )
        )
    ]
    for copy in copies:
        copy.start()
    for copy in copies:
        copy.wait()
    planes, layers, row_width = free_ref.shape
    load_place = lax.axis_index("space")
    shape = (layers, row_width)
    z = spot_iota(shape, 0)
    y = spot_iota(shape, 1)

    class_weights(radius_ref, weight_ref)
    ones = forward_planes(jnp.ones(shape, jnp.float32), weight_ref)
    for place, (lower, upper) in enumerate(((0, 2), (1, 2), (2, 2), (2, 1), (2, 0))):
        total_ref[place] = (
            ones[0] + min(lower, 1) * ones[1] + min(upper, 1) * ones[1]
            + (lower // 2) * ones[2] + (upper // 2) * ones[2]
        )

    def free_plane(x, carry):
        free_ref[x] = jnp.where(
            z == 0, 1.0 - fixed_ref[pl.ds(x, 1), :].astype(jnp.float32), 1.0
        )
        return carry

    lax.fori_loop(0, planes, free_plane, 0, unroll=16)

    own_index = index_ref[load_place]
    own_z = own_index // row_width % layers
    own_y = own_index % row_width
    hit = (z == own_z) & (y == own_y)
    for part in range(3):
        load_ref[part] = jnp.where(hit, force_ref[part, load_place], 0.0)
    spot_ref[0] = own_index // (layers * row_width)


def sweep_kernel(
    spot_ref,
    load_ref,
    weight_ref,
    total_ref,
    free_ref,
    density_ref,
    start_ref,
    disp_ref,
    sens_ref,
    coef_ref,
    near_ref,
    side_ref,
    far_ref,
    modulus_ref,
    across_ref,
    up_ref,
    down_ref,
    right_ref,
    left_ref,
    rate_ref,
    first_ref,
    second_ref,
):
    planes, layers, row_width = coef_ref.shape
    own_planes = density_ref.shape[2]
    load_cases = lax.axis_size("space")
    shape = (layers, row_width)
    z = spot_iota(shape, 0)
    y = spot_iota(shape, 1)
    zero = jnp.zeros(shape, jnp.float32)

    for ref in (side_ref, far_ref):
        zero_edges(ref)

    def filter_plane(x, carry):
        near, side, far = forward_planes(density_ref[pair_spot(x, own_planes)], weight_ref)
        near_ref[x + 2] = near
        side_ref[x + 2] = side
        far_ref[x + 2] = far
        return carry

    lax.fori_loop(0, planes, filter_plane, 0, unroll=16)

    def modulus_plane(x, carry):
        total = total_ref[edge_class(x, planes)]
        filtered = (
            near_ref[x + 2]
            + side_ref[x + 1]
            + side_ref[x + 3]
            + far_ref[x]
            + far_ref[x + 4]
        ) / total
        modulus = floor_modulus + (1.0 - floor_modulus) * (filtered * filtered * filtered)
        modulus_ref[x] = modulus
        coef_ref[x] = 3.0 * (1.0 - floor_modulus) * (filtered * filtered) / total
        return carry

    lax.fori_loop(0, planes, modulus_plane, 0, unroll=16)

    across_ref[0] = zero
    across_ref[planes] = zero
    for ref in (first_ref, second_ref):
        for part in range(3):
            ref[part, 0] = zero
            ref[part, planes + 1] = zero

    def face_plane(x, carry):
        modulus = modulus_ref[x]
        later = modulus_ref[jnp.minimum(x + 1, planes - 1)]
        ahead = jnp.where(x + 1 < planes, 0.5 * (modulus + later), 0.0)
        across_ref[x + 1] = ahead
        up = jnp.where(z < layers - 1, 0.5 * (modulus + pltpu.roll(modulus, layers - 1, 0)), 0.0)
        down = pltpu.roll(up, 1, 0)
        right = jnp.where(
            y < row_width - 1, 0.5 * (modulus + pltpu.roll(modulus, row_width - 1, 1)), 0.0
        )
        left = pltpu.roll(right, 1, 1)
        up_ref[x] = up
        down_ref[x] = down
        right_ref[x] = right
        left_ref[x] = left
        sums = (carry + ahead, up + down, left + right)
        every = sums[0] + sums[1] + sums[2]
        free = free_ref[x]
        push = relax_factor * free
        for part in range(3):
            rate_ref[part, x] = push / (every + sums[part])
            first_ref[part, x + 1] = start_ref[part, x] * free
        return ahead

    lax.fori_loop(0, planes, face_plane, zero, unroll=16)

    own_x = spot_ref[0]

    def sweep(source, target, lead):
        def sweep_plane(x, carry):
            before, after = across_ref[x], across_ref[x + 1]
            up, down, right, left = up_ref[x], down_ref[x], right_ref[x], left_ref[x]
            for part in range(3):
                here = source[part, x + 1]
                pulls = [
                    before * source[part, x] + after * source[part, x + 2],
                    up * pltpu.roll(here, layers - 1, 0) + down * pltpu.roll(here, 1, 0),
                    right * pltpu.roll(here, row_width - 1, 1) + left * pltpu.roll(here, 1, 1),
                ]
                pull = pulls[0] + pulls[1] + pulls[2] + pulls[part]
                target[part, x + lead] = (1.0 - relax_factor) * here + rate_ref[part, x] * pull
            return carry

        lax.fori_loop(0, planes, sweep_plane, 0, unroll=16)
        for part in range(3):
            target[part, own_x + lead] += rate_ref[part, own_x] * load_ref[part]

    stages = (first_ref, second_ref)
    for turn in range(SWEEPS - 1):
        sweep(stages[turn % 2], stages[(turn + 1) % 2], 1)
    sweep(stages[(SWEEPS - 1) % 2], disp_ref, 0)

    def energy_plane(x, carry):
        later = jnp.minimum(x + 1, planes - 1)
        ahead, upward, right = zero, zero, zero
        for part in range(3):
            here = disp_ref[part, x]
            step = disp_ref[part, later] - here
            climb = pltpu.roll(here, layers - 1, 0) - here
            slide = pltpu.roll(here, row_width - 1, 1) - here
            ahead = ahead + (2.0 if part == 0 else 1.0) * (step * step)
            upward = upward + (2.0 if part == 1 else 1.0) * (climb * climb)
            right = right + (2.0 if part == 2 else 1.0) * (slide * slide)
        upward = jnp.where(z < layers - 1, upward, 0.0)
        right = jnp.where(y < row_width - 1, right, 0.0)
        total = carry + ahead + upward + pltpu.roll(upward, 1, 0) + right + pltpu.roll(right, 1, 1)
        sens_ref[pair_spot(x, own_planes)] = (0.5 / load_cases) * total
        return ahead

    lax.fori_loop(0, planes, energy_plane, zero, unroll=16)


def design_kernel(
    weight_ref,
    sens_ref,
    coef_ref,
    density_ref,
    new_ref,
    near_ref,
    side_ref,
    far_ref,
    pull_ref,
    low_ref,
    high_ref,
):
    planes, layers, row_width = coef_ref.shape
    own_planes = density_ref.shape[2]
    place = lax.axis_index("space")
    shape = (layers, row_width)
    zero = jnp.zeros(shape, jnp.float32)
    for ref in (side_ref, far_ref):
        zero_edges(ref)

    def filter_plane(x, carry):
        near, side, far = backward_planes(
            sens_ref[pair_spot(x, own_planes)] * coef_ref[x], weight_ref
        )
        near_ref[x + 2] = near
        side_ref[x + 2] = side
        far_ref[x + 2] = far
        return carry

    lax.fori_loop(0, planes, filter_plane, 0, unroll=16)

    def root_plane(x, carry):
        root = jnp.sqrt(
            near_ref[x + 2] + side_ref[x + 1] + side_ref[x + 3] + far_ref[x] + far_ref[x + 4]
        )
        density = density_ref[pair_spot(x, own_planes)]
        pull_ref[x] = density * root
        low_ref[x] = jnp.maximum(density - move_limit, density_floor)
        high_ref[x] = jnp.minimum(density + move_limit, 1.0)
        return carry

    lax.fori_loop(0, planes, root_plane, 0, unroll=16)

    target = volume_share * planes * layers * row_width

    def trial(x, factor):
        return jnp.minimum(jnp.maximum(pull_ref[x] * factor, low_ref[x]), high_ref[x])

    def halve(step, state):
        lower, span = state
        half = span * 0.5
        middle = lower + half
        factor = jnp.exp(-0.5 * middle)
        total = lax.fori_loop(
            0, planes, lambda x, acc: acc + trial(x, factor), zero, unroll=8
        )
        volume = jnp.sum(jnp.sum(total, axis=0, keepdims=True), axis=1, keepdims=True)
        return jnp.where(volume > target, middle, lower), half

    start = (jnp.full((1, 1), log_lower, jnp.float32), jnp.full((1, 1), log_span, jnp.float32))
    lower, span = lax.fori_loop(0, SEARCH, halve, start)
    factor = jnp.exp(-0.5 * (lower + 0.5 * span))
    for own in range(own_planes):
        new_ref[own] = trial(place * own_planes + own, factor)


def in_vmem():
    return pl.BlockSpec(memory_space=pltpu.VMEM)


def in_smem():
    return pl.BlockSpec(memory_space=pltpu.SMEM)


KERNEL_VMEM = 24 * 2**20


def floats(*shape):
    return jax.ShapeDtypeStruct(shape, jnp.float32)


def prepare_call(radius, load_index, load_force, fixed):
    planes, row_width = fixed.shape
    layers = radius.shape[0]
    return pl.pallas_call(
        prepare_kernel,
        out_shape=[
            floats(len(ALL_SQUARES), layers, row_width),
            floats(2 * window_reach + 1, layers, row_width),
            floats(planes, layers, row_width),
            floats(3, layers, row_width),
            jax.ShapeDtypeStruct((1,), jnp.int32),
        ],
        in_specs=[pl.BlockSpec(memory_space=pltpu.HBM)] * 4,
        out_specs=[in_vmem()] * 4 + [in_smem()],
        scratch_shapes=[
            pltpu.SMEM(radius.shape, radius.dtype),
            pltpu.SMEM(load_index.shape, load_index.dtype),
            pltpu.SMEM(load_force.shape, load_force.dtype),
            pltpu.VMEM(fixed.shape, fixed.dtype),
            pltpu.SemaphoreType.DMA((4,)),
        ],
        compiler_params=pltpu.CompilerParams(vmem_limit_bytes=KERNEL_VMEM),
        cost_estimate=pl.CostEstimate(
            flops=40 * planes * layers * row_width,
            bytes_accessed=8 * planes * layers * row_width,
            transcendentals=0,
        ),
        name="prepare",
    )(
        *(
            pltpu.with_memory_space_constraint(array, pltpu.HBM)
            for array in (radius, load_index, load_force, fixed)
        )
    )


def sweep_call(spot, load, weights, totals, free, density, displacement):
    cores, chips, own_planes, layers, row_width = density.shape
    planes = cores * chips * own_planes

    def scratch(*lead):
        return pltpu.VMEM(lead + (layers, row_width), jnp.float32)

    return pl.pallas_call(
        sweep_kernel,
        out_shape=[
            floats(3, planes, layers, row_width),
            floats(*density.shape),
            floats(planes, layers, row_width),
        ],
        in_specs=[in_smem()] + [in_vmem()] * 6,
        out_specs=[in_vmem()] * 3,
        scratch_shapes=[
            scratch(planes + 4),
            scratch(planes + 4),
            scratch(planes + 4),
            scratch(planes),
            scratch(planes + 1),
            scratch(planes),
            scratch(planes),
            scratch(planes),
            scratch(planes),
            scratch(3, planes),
            scratch(3, planes + 2),
            scratch(3, planes + 2),
        ],
        compiler_params=pltpu.CompilerParams(vmem_limit_bytes=KERNEL_VMEM),
        name="sweeps",
    )(spot, load, weights, totals, free, density, displacement)


def design_call(weights, sens, coef, density):
    cores, chips, own_planes, layers, row_width = density.shape
    planes = cores * chips * own_planes

    def scratch(*lead):
        return pltpu.VMEM(lead + (layers, row_width), jnp.float32)

    return pl.pallas_call(
        design_kernel,
        out_shape=jax.ShapeDtypeStruct((own_planes, layers, row_width), jnp.float32),
        in_specs=[in_vmem()] * 4,
        out_specs=in_vmem(),
        scratch_shapes=[
            scratch(planes + 4),
            scratch(planes + 4),
            scratch(planes + 4),
            scratch(planes),
            scratch(planes),
            scratch(planes),
        ],
        compiler_params=pltpu.CompilerParams(vmem_limit_bytes=KERNEL_VMEM),
        name="design",
    )(weights, sens, coef, density)


def other_core(block):
    devices = lax.axis_size("space")
    return lax.ppermute(block, "space", [(i, i ^ 1) for i in range(devices)])


def between_chips(pieces):
    devices = lax.axis_size("space")
    groups = [list(range(core, devices, 2)) for core in range(2)]
    return lax.all_to_all(pieces, "space", 0, 0, axis_index_groups=groups)


def chip_gathered(block):
    chips = lax.axis_size("space") // 2
    return between_chips(jnp.broadcast_to(block[None], (chips,) + block.shape))


def with_other_core(blocks):
    return jnp.stack([blocks, other_core(blocks)])


def scattered_sum(pieces):
    return jnp.sum(between_chips(pieces[0] + other_core(pieces[1])), axis=0)


def one_slab(density, displacement, fixed, load_index, load_force, radius):
    same_core, small = lax.optimization_barrier(
        (chip_gathered(density), (radius, load_index, load_force.T, fixed))
    )
    whole = with_other_core(same_core)
    weights, totals, free, load, spot = prepare_call(*small)
    new_displacement, sens, coef = sweep_call(
        spot, load, weights, totals, free, whole, displacement[0]
    )
    sens = with_other_core(chip_gathered(scattered_sum(sens)))
    new_density = design_call(weights, sens, coef, whole)
    return new_density, new_displacement[None]


def from_behind(block, axis, distance):
    devices = range(lax.axis_size(axis))
    route = [(i - distance, i) for i in devices if i - distance in devices]
    return lax.ppermute(block, axis, route)


def extended(x, sides, width):
    for axis, dim in sides:
        size, length = (lax.axis_size(axis), x.shape[dim])
        up = [(i, (i + 1) % size) for i in range(size - 1)]
        down = [(j, i) for i, j in up]
        last = lax.slice_in_dim(x, length - width, length, axis=dim)
        first = lax.slice_in_dim(x, 0, width, axis=dim)
        before = lax.ppermute(last, axis, up)
        after = lax.ppermute(first, axis, down)
        x = jnp.concatenate([before, x, after], axis=dim)
    return x


def from_partner(x, axis, bit):
    return lax.ppermute(x, axis, [(i, i ^ 1 << bit) for i in range(lax.axis_size(axis))])


def window_offsets():
    offsets_list = []
    for across in range(-window_reach, window_reach + 1):
        for upward in range(-window_reach, window_reach + 1):
            for sideways in range(-window_reach, window_reach + 1):
                length = math.sqrt(across * across + upward * upward + sideways * sideways)
                offsets_list.append((across, upward, sideways, length))
    return offsets_list


def layer_weights(radius):
    radial = radius.astype(jnp.float32)
    return jnp.stack(
        [jnp.maximum(radial - length, 0.0) for across, upward, sideways, length in window_offsets()]
    )


def pad_axis(grid_field, along_axis, before, after_cells):
    widths = [(0, 0)] * grid_field.ndim
    widths[along_axis] = (before, after_cells)
    return jnp.pad(grid_field, widths)


def pad_sides(grid_field):
    return jnp.pad(grid_field, ((0, 0), (window_reach, window_reach), (window_reach, window_reach)))


def filter_forward(padded, weights):
    out_rows = padded.shape[0] - 2 * window_reach
    layers = padded.shape[1] - 2 * window_reach
    row_width = padded.shape[2] - 2 * window_reach
    result = jnp.zeros((out_rows, layers, row_width), jnp.float32)
    for offset_index, (across, upward, sideways, length) in enumerate(window_offsets()):
        shifted = padded[
            window_reach + across : window_reach + across + out_rows,
            window_reach + upward : window_reach + upward + layers,
            window_reach + sideways : window_reach + sideways + row_width,
        ]
        result = result + weights[offset_index][None, :, None] * shifted
    return result


def filter_backward(padded, padded_weights):
    out_rows = padded.shape[0] - 2 * window_reach
    layers = padded.shape[1] - 2 * window_reach
    row_width = padded.shape[2] - 2 * window_reach
    result = jnp.zeros((out_rows, layers, row_width), jnp.float32)
    for offset_index, (across, upward, sideways, length) in enumerate(window_offsets()):
        shifted = padded[
            window_reach - across : window_reach - across + out_rows,
            window_reach - upward : window_reach - upward + layers,
            window_reach - sideways : window_reach - sideways + row_width,
        ]
        layer_part = padded_weights[
            offset_index, window_reach - upward : window_reach - upward + layers
        ]
        result = result + layer_part[None, :, None] * shifted
    return result


def stiff_factors(direction):
    return jnp.array(
        [2.0 if component == direction else 1.0 for component in range(3)], jnp.float32
    ).reshape(3, 1, 1, 1)


def relax_slab(padded, displace, face_x, face_z, face_y, force_field, free_cells, diagonal):
    flux_x = stiff_factors(0) * face_x * jnp.diff(padded, axis=1)
    stencil_image = flux_x[:, :-1] - flux_x[:, 1:]
    flux_z = stiff_factors(1) * face_z * jnp.diff(displace, axis=2)
    stencil_image = stencil_image + pad_axis(flux_z, 2, 1, 0) - pad_axis(flux_z, 2, 0, 1)
    flux_y = stiff_factors(2) * face_y * jnp.diff(displace, axis=3)
    stencil_image = stencil_image + pad_axis(flux_y, 3, 1, 0) - pad_axis(flux_y, 3, 0, 1)
    return free_cells * (displace + relax_factor * (force_field - stencil_image) / diagonal)


def slab_energy(grid_field, along_axis, direction, load_cases):
    change = jnp.diff(grid_field, axis=along_axis)
    return jnp.sum(stiff_factors(direction) * change * change, axis=0) / load_cases


def neighbour_planes(displace, load_cases, axis_devices):
    if axis_devices > load_cases:
        below = from_behind(displace[:, -1:], "space", load_cases)
        above = from_behind(displace[:, :1], "space", -load_cases)
    else:
        below = jnp.zeros_like(displace[:, :1])
        above = jnp.zeros_like(displace[:, :1])
    return jnp.concatenate([below, displace, above], axis=1)


def many_slabs(density, displacement, fixed, load_index, load_force, radius):
    slab_rows, layers, row_width = density.shape
    load_cases = load_index.shape[0]
    level_count = load_cases.bit_length() - 1
    axis_devices = lax.axis_size("space")
    axis_place = lax.axis_index("space")
    slab_planes = slab_rows * load_cases
    slab_place = axis_place // load_cases
    load_place = axis_place % load_cases
    total_rows = slab_rows * axis_devices
    weights = layer_weights(radius)
    padded_weights = pad_axis(weights, 1, window_reach, window_reach)
    global_rows = (
        jnp.arange(slab_rows + 2 * window_reach, dtype=jnp.int32)
        + axis_place * slab_rows
        - window_reach
    )
    deep_inside = ((global_rows >= 0) & (global_rows < total_rows)).astype(jnp.float32)
    inside_field = deep_inside[:, None, None] * pad_sides(
        jnp.ones((slab_rows + 2 * window_reach, layers, row_width), jnp.float32)
    )
    total_weight = filter_forward(inside_field, weights)
    slab_start = slab_place * slab_planes
    margin_rows = jnp.arange(slab_planes + 2, dtype=jnp.int32) + slab_start - 1
    margin_inside = ((margin_rows >= 0) & (margin_rows < total_rows)).astype(jnp.float32)
    face_valid = margin_inside[1:] * margin_inside[:-1]
    fixed_slab = lax.dynamic_slice_in_dim(fixed, slab_start, slab_planes, 0).astype(jnp.float32)
    bottom_layer = (jnp.arange(layers, dtype=jnp.int32) == 0).astype(jnp.float32)
    free_cells = 1.0 - bottom_layer[None, :, None] * fixed_slab[:, None, :]
    slab_cells = slab_planes * layers * row_width
    cell_index = jnp.arange(slab_cells, dtype=jnp.int32) + slab_place * slab_cells
    load_hot = jnp.arange(load_cases, dtype=jnp.int32) == load_place
    own_index = jnp.sum(jnp.where(load_hot, load_index, 0))
    own_force = jnp.sum(load_hot.astype(jnp.float32)[:, None] * load_force, axis=0)
    load_hits = (cell_index == own_index).astype(jnp.float32)
    force_field = (own_force[:, None] * load_hits[None, :]).reshape(
        3, slab_planes, layers, row_width
    )
    displace = displacement[0] * free_cells
    target = volume_share * total_rows * layers * row_width
    padded = neighbour_planes(displace, load_cases, axis_devices)
    halo_density = extended(density, (("space", 0),), window_reach)
    filtered = filter_forward(pad_sides(halo_density), weights) / total_weight
    whole_field = lax.all_gather(filtered, "space", axis=0, tiled=True)
    margin = lax.dynamic_slice_in_dim(
        pad_axis(whole_field, 0, 1, 1), slab_start, slab_planes + 2, 0
    )
    moduli = floor_modulus + (1.0 - floor_modulus) * margin**3
    face_x = 0.5 * (moduli[1:] + moduli[:-1]) * face_valid[:, None, None]
    inner_moduli = moduli[1:-1]
    face_z = 0.5 * (inner_moduli[:, 1:] + inner_moduli[:, :-1])
    face_y = 0.5 * (inner_moduli[:, :, 1:] + inner_moduli[:, :, :-1])
    sum_x = face_x[:-1] + face_x[1:]
    sum_z = pad_axis(face_z, 1, 1, 0) + pad_axis(face_z, 1, 0, 1)
    sum_y = pad_axis(face_y, 2, 1, 0) + pad_axis(face_y, 2, 0, 1)
    diagonal = stiff_factors(0) * sum_x + stiff_factors(1) * sum_z + stiff_factors(2) * sum_y
    for sweep_index in range(SWEEPS):
        displace = relax_slab(
            padded, displace, face_x, face_z, face_y, force_field, free_cells, diagonal
        )
        padded = neighbour_planes(displace, load_cases, axis_devices)
    energy_x = slab_energy(padded, 1, 0, load_cases) * face_valid[:, None, None]
    energy_z = slab_energy(displace, 2, 1, load_cases)
    energy_y = slab_energy(displace, 3, 2, load_cases)
    sens_term = 0.5 * (
        energy_x[:-1]
        + energy_x[1:]
        + pad_axis(energy_z, 1, 1, 0)
        + pad_axis(energy_z, 1, 0, 1)
        + pad_axis(energy_y, 2, 1, 0)
        + pad_axis(energy_y, 2, 0, 1)
    )
    sensitive = sens_term
    for level in reversed(range(level_count)):
        half_rows = sensitive.shape[0] // 2
        upper_side = load_place // 2**level % 2 == 1
        outgoing = jnp.where(upper_side, sensitive[:half_rows], sensitive[half_rows:])
        keeping = jnp.where(upper_side, sensitive[half_rows:], sensitive[:half_rows])
        sensitive = keeping + from_partner(outgoing, "space", level)
    weighted_share = 3.0 * (1.0 - floor_modulus) * filtered**2 * sensitive / total_weight
    halo_share = extended(weighted_share, (("space", 0),), window_reach)
    root_term = jnp.sqrt(filter_backward(pad_sides(halo_share), padded_weights))
    lowest = jnp.maximum(density - move_limit, density_floor)
    highest = jnp.minimum(density + move_limit, 1.0)
    design_now = density

    def trial_design(log_level):
        return jnp.clip(design_now * root_term * jnp.exp(-0.5 * log_level), lowest, highest)

    start_state = (jnp.asarray(log_lower, jnp.float32), jnp.asarray(log_span, jnp.float32))

    def halve(search_step, search_state):
        lower_end, span_width = search_state
        half_span = span_width * 0.5
        middle = lower_end + half_span
        volume_total = lax.psum(jnp.sum(trial_design(middle)), "space")
        return (jnp.where(volume_total > target, middle, lower_end), half_span)

    lower_end, span_width = lax.fori_loop(0, SEARCH, halve, start_state)
    density = trial_design(lower_end + 0.5 * span_width)
    new_displacement = displace[None]
    return (density, new_displacement)


def solution(mesh):
    in_specs = (
        P("space", "parts", None),
        P("space", None, None, "parts", None),
        P(None, "parts"),
        P("parts"),
        P("parts", None),
        P("parts"),
    )
    out_specs = (P("space", "parts", None), P("space", None, None, "parts", None))

    def local(density, displacement, fixed, load_index, load_force, radius):
        alone = lax.axis_size("space") == load_index.shape[0]
        run = one_slab if alone else many_slabs
        return run(density, displacement, fixed, load_index, load_force, radius)

    return jax.shard_map(local, mesh=mesh, in_specs=in_specs, out_specs=out_specs, check_vma=False)
```

```python
import math

import jax
import jax.numpy as jnp
from jax import lax
from jax.experimental import pallas as pl
from jax.experimental.pallas import tpu as pltpu
from jax.sharding import PartitionSpec as P

SWEEPS = 3
SEARCH = 12


floor_modulus = 0.05
relax_factor = 0.6
move_limit = 0.2
density_floor = 0.01
volume_share = 0.5
log_lower = -16.0
log_span = 32.0
window_reach = 2

PLANE_SQUARES = (0, 1, 2, 4, 5, 8)
ALL_SQUARES = (0, 1, 2, 3, 4, 5, 6, 8, 9, 12)


def spot_iota(shape, dim):
    return lax.broadcasted_iota(jnp.int32, shape, dim)


def layer_radius(radius_ref, layers, row_width):
    z = spot_iota((layers, row_width), 0)
    result = jnp.zeros((layers, row_width), jnp.int32)
    for layer in range(layers):
        result = jnp.where(z == layer, radius_ref[layer], result)
    return result.astype(jnp.float32)


def class_weights(radius_ref, weight_ref):
    layers, row_width = weight_ref.shape[1:]
    radial = layer_radius(radius_ref, layers, row_width)
    for place, square in enumerate(ALL_SQUARES):
        weight_ref[place] = jnp.maximum(radial - math.sqrt(square), 0.0)


def shift_sum(field, dim, distance):
    size = field.shape[dim]
    spot = spot_iota(field.shape, dim)
    ahead = jnp.where(spot < size - distance, pltpu.roll(field, size - distance, dim), 0.0)
    behind = jnp.where(spot >= distance, pltpu.roll(field, distance, dim), 0.0)
    return ahead + behind


def plane_sums(plane):
    beside = shift_sum(plane, 1, 1)
    further = shift_sum(plane, 1, 2)
    return {
        0: plane,
        1: beside + shift_sum(plane, 0, 1),
        2: shift_sum(beside, 0, 1),
        4: further + shift_sum(plane, 0, 2),
        5: shift_sum(further, 0, 1) + shift_sum(beside, 0, 2),
        8: shift_sum(further, 0, 2),
    }


def weigh(sums, weight_ref, square):
    result = None
    for inner in PLANE_SQUARES:
        term = weight_ref[ALL_SQUARES.index(inner + square)] * sums[inner]
        result = term if result is None else result + term
    return result


def forward_planes(plane, weight_ref):
    sums = plane_sums(plane)
    return [weigh(sums, weight_ref, square) for square in (0, 1, 4)]


def backward_planes(plane, weight_ref):
    beside = shift_sum(plane, 1, 1)
    further = shift_sum(plane, 1, 2)
    results = []
    for square in (0, 1, 4):

        def weight(more):
            return weight_ref[ALL_SQUARES.index(square + more)]

        level = weight(0) * plane + weight(1) * beside + weight(4) * further
        near = weight(1) * plane + weight(2) * beside + weight(5) * further
        far = weight(4) * plane + weight(5) * beside + weight(8) * further
        results.append(level + shift_sum(near, 0, 1) + shift_sum(far, 0, 2))
    return results


def pair_spot(x, own_planes):
    device = x // own_planes
    core = (device ^ lax.axis_index("space")) & 1
    return core, device >> 1, x % own_planes


def edge_class(x, planes):
    return jnp.minimum(x, 2) + jnp.maximum(x - (planes - 3), 0)


def zero_edges(ref):
    planes = ref.shape[0]
    for place in (0, 1, planes - 2, planes - 1):
        ref[place] = jnp.zeros(ref.shape[1:], ref.dtype)


def prepare_kernel(
    radius_hbm,
    index_hbm,
    force_hbm,
    fixed_hbm,
    weight_ref,
    inverse_ref,
    free_ref,
    load_ref,
    spot_ref,
    radius_ref,
    index_ref,
    force_ref,
    fixed_ref,
    arrived,
):
    copies = [
        pltpu.make_async_copy(source, target, arrived.at[place])
        for place, (source, target) in enumerate(
            (
                (radius_hbm, radius_ref),
                (index_hbm, index_ref),
                (force_hbm, force_ref),
                (fixed_hbm, fixed_ref),
            )
        )
    ]
    for copy in copies:
        copy.start()
    for copy in copies:
        copy.wait()
    planes, layers, row_width = free_ref.shape
    load_place = lax.axis_index("space")
    shape = (layers, row_width)
    z = spot_iota(shape, 0)
    y = spot_iota(shape, 1)

    class_weights(radius_ref, weight_ref)
    ones = forward_planes(jnp.ones(shape, jnp.float32), weight_ref)
    for place, (lower, upper) in enumerate(((0, 2), (1, 2), (2, 2), (2, 1), (2, 0))):
        inverse_ref[place] = 1.0 / (
            ones[0] + min(lower, 1) * ones[1] + min(upper, 1) * ones[1]
            + (lower // 2) * ones[2] + (upper // 2) * ones[2]
        )

    def free_plane(x, carry):
        free_ref[x] = jnp.where(
            z == 0, 1.0 - fixed_ref[pl.ds(x, 1), :].astype(jnp.float32), 1.0
        )
        return carry

    lax.fori_loop(0, planes, free_plane, 0, unroll=16)

    own_index = index_ref[load_place]
    own_z = own_index // row_width % layers
    own_y = own_index % row_width
    hit = (z == own_z) & (y == own_y)
    for part in range(3):
        load_ref[part] = jnp.where(hit, force_ref[part, load_place], 0.0)
    spot_ref[0] = own_index // (layers * row_width)


def sweep_kernel(
    spot_ref,
    load_ref,
    weight_ref,
    inverse_ref,
    free_ref,
    density_ref,
    start_ref,
    disp_hbm,
    sens_ref,
    coef_ref,
    near_ref,
    side_ref,
    far_ref,
    modulus_ref,
    across_ref,
    up_ref,
    down_ref,
    right_ref,
    left_ref,
    rate_ref,
    first_ref,
    second_ref,
    disp_ref,
    stored,
):
    planes, layers, row_width = coef_ref.shape
    own_planes = density_ref.shape[2]
    load_cases = lax.axis_size("space")
    shape = (layers, row_width)
    z = spot_iota(shape, 0)
    y = spot_iota(shape, 1)
    zero = jnp.zeros(shape, jnp.float32)

    for ref in (side_ref, far_ref):
        zero_edges(ref)

    def filter_plane(x, carry):
        near, side, far = forward_planes(density_ref[pair_spot(x, own_planes)], weight_ref)
        near_ref[x + 2] = near
        side_ref[x + 2] = side
        far_ref[x + 2] = far
        return carry

    lax.fori_loop(0, planes, filter_plane, 0, unroll=16)

    def modulus_plane(x, carry):
        inverse = inverse_ref[edge_class(x, planes)]
        filtered = (
            near_ref[x + 2]
            + side_ref[x + 1]
            + side_ref[x + 3]
            + far_ref[x]
            + far_ref[x + 4]
        ) * inverse
        modulus = floor_modulus + (1.0 - floor_modulus) * (filtered * filtered * filtered)
        modulus_ref[x] = modulus
        coef_ref[x] = 3.0 * (1.0 - floor_modulus) * (filtered * filtered) * inverse
        return carry

    lax.fori_loop(0, planes, modulus_plane, 0, unroll=16)

    across_ref[0] = zero
    across_ref[planes] = zero
    for ref in (first_ref, second_ref):
        for part in range(3):
            ref[part, 0] = zero
            ref[part, planes + 1] = zero

    def face_plane(x, carry):
        modulus = modulus_ref[x]
        later = modulus_ref[jnp.minimum(x + 1, planes - 1)]
        ahead = jnp.where(x + 1 < planes, 0.5 * (modulus + later), 0.0)
        across_ref[x + 1] = ahead
        up = jnp.where(z < layers - 1, 0.5 * (modulus + pltpu.roll(modulus, layers - 1, 0)), 0.0)
        down = pltpu.roll(up, 1, 0)
        right = jnp.where(
            y < row_width - 1, 0.5 * (modulus + pltpu.roll(modulus, row_width - 1, 1)), 0.0
        )
        left = pltpu.roll(right, 1, 1)
        up_ref[x] = up
        down_ref[x] = down
        right_ref[x] = right
        left_ref[x] = left
        sums = (carry + ahead, up + down, left + right)
        every = sums[0] + sums[1] + sums[2]
        free = free_ref[x]
        push = relax_factor * free
        diagonal = [every + part_sum for part_sum in sums]
        pair = diagonal[0] * diagonal[1]
        push = push / (pair * diagonal[2])
        side = push * diagonal[2]
        rate_ref[0, x] = side * diagonal[1]
        rate_ref[1, x] = side * diagonal[0]
        rate_ref[2, x] = push * pair
        for part in range(3):
            first_ref[part, x + 1] = start_ref[part, x] * free
        return ahead

    lax.fori_loop(0, planes, face_plane, zero, unroll=16)

    own_x = spot_ref[0]

    def sweep(source, target, lead):
        def sweep_plane(x, carry):
            before, after = across_ref[x], across_ref[x + 1]
            up, down, right, left = up_ref[x], down_ref[x], right_ref[x], left_ref[x]
            for part in range(3):
                here = source[part, x + 1]
                pulls = [
                    before * source[part, x] + after * source[part, x + 2],
                    up * pltpu.roll(here, layers - 1, 0) + down * pltpu.roll(here, 1, 0),
                    right * pltpu.roll(here, row_width - 1, 1) + left * pltpu.roll(here, 1, 1),
                ]
                pull = pulls[0] + pulls[1] + pulls[2] + pulls[part]
                target[part, x + lead] = (1.0 - relax_factor) * here + rate_ref[part, x] * pull
            return carry

        lax.fori_loop(0, planes, sweep_plane, 0, unroll=16)
        for part in range(3):
            target[part, own_x + lead] += rate_ref[part, own_x] * load_ref[part]

    stages = (first_ref, second_ref)
    for turn in range(SWEEPS - 1):
        sweep(stages[turn % 2], stages[(turn + 1) % 2], 1)
    sweep(stages[(SWEEPS - 1) % 2], disp_ref, 0)
    store = pltpu.make_async_copy(disp_ref, disp_hbm, stored)
    store.start()

    def energy_plane(x, carry):
        later = jnp.minimum(x + 1, planes - 1)
        ahead, upward, right = zero, zero, zero
        for part in range(3):
            here = disp_ref[part, x]
            step = disp_ref[part, later] - here
            climb = pltpu.roll(here, layers - 1, 0) - here
            slide = pltpu.roll(here, row_width - 1, 1) - here
            ahead = ahead + (2.0 if part == 0 else 1.0) * (step * step)
            upward = upward + (2.0 if part == 1 else 1.0) * (climb * climb)
            right = right + (2.0 if part == 2 else 1.0) * (slide * slide)
        upward = jnp.where(z < layers - 1, upward, 0.0)
        right = jnp.where(y < row_width - 1, right, 0.0)
        total = carry + ahead + upward + pltpu.roll(upward, 1, 0) + right + pltpu.roll(right, 1, 1)
        sens_ref[pair_spot(x, own_planes)] = (0.5 / load_cases) * total
        return ahead

    lax.fori_loop(0, planes, energy_plane, zero, unroll=16)
    store.wait()


def design_kernel(
    weight_ref,
    sens_ref,
    coef_ref,
    density_ref,
    new_ref,
    near_ref,
    side_ref,
    far_ref,
    pull_ref,
    low_ref,
    high_ref,
):
    planes, layers, row_width = coef_ref.shape
    own_planes = density_ref.shape[2]
    place = lax.axis_index("space")
    shape = (layers, row_width)
    zero = jnp.zeros(shape, jnp.float32)
    for ref in (side_ref, far_ref):
        zero_edges(ref)

    def filter_plane(x, carry):
        near, side, far = backward_planes(
            sens_ref[pair_spot(x, own_planes)] * coef_ref[x], weight_ref
        )
        near_ref[x + 2] = near
        side_ref[x + 2] = side
        far_ref[x + 2] = far
        return carry

    lax.fori_loop(0, planes, filter_plane, 0, unroll=16)

    def root_plane(x, carry):
        root = jnp.sqrt(
            near_ref[x + 2] + side_ref[x + 1] + side_ref[x + 3] + far_ref[x] + far_ref[x + 4]
        )
        density = density_ref[pair_spot(x, own_planes)]
        pull_ref[x] = density * root
        low_ref[x] = jnp.maximum(density - move_limit, density_floor)
        high_ref[x] = jnp.minimum(density + move_limit, 1.0)
        return carry

    lax.fori_loop(0, planes, root_plane, 0, unroll=16)

    target = volume_share * planes * layers * row_width

    def trial(x, factor):
        return jnp.minimum(jnp.maximum(pull_ref[x] * factor, low_ref[x]), high_ref[x])

    def halve(step, state):
        lower, span = state
        half = span * 0.5
        middle = lower + half
        factor = jnp.exp(-0.5 * middle)
        total = lax.fori_loop(
            0, planes, lambda x, acc: acc + trial(x, factor), zero, unroll=8
        )
        volume = jnp.sum(jnp.sum(total, axis=0, keepdims=True), axis=1, keepdims=True)
        return jnp.where(volume > target, middle, lower), half

    start = (jnp.full((1, 1), log_lower, jnp.float32), jnp.full((1, 1), log_span, jnp.float32))
    lower, span = lax.fori_loop(0, SEARCH, halve, start)
    factor = jnp.exp(-0.5 * (lower + 0.5 * span))
    for own in range(own_planes):
        new_ref[own] = trial(place * own_planes + own, factor)


def in_vmem():
    return pl.BlockSpec(memory_space=pltpu.VMEM)


def in_smem():
    return pl.BlockSpec(memory_space=pltpu.SMEM)


KERNEL_VMEM = 24 * 2**20


def floats(*shape):
    return jax.ShapeDtypeStruct(shape, jnp.float32)


def prepare_call(radius, load_index, load_force, fixed):
    planes, row_width = fixed.shape
    layers = radius.shape[0]
    return pl.pallas_call(
        prepare_kernel,
        out_shape=[
            floats(len(ALL_SQUARES), layers, row_width),
            floats(2 * window_reach + 1, layers, row_width),
            floats(planes, layers, row_width),
            floats(3, layers, row_width),
            jax.ShapeDtypeStruct((1,), jnp.int32),
        ],
        in_specs=[pl.BlockSpec(memory_space=pltpu.HBM)] * 4,
        out_specs=[in_vmem()] * 4 + [in_smem()],
        scratch_shapes=[
            pltpu.SMEM(radius.shape, radius.dtype),
            pltpu.SMEM(load_index.shape, load_index.dtype),
            pltpu.SMEM(load_force.shape, load_force.dtype),
            pltpu.VMEM(fixed.shape, fixed.dtype),
            pltpu.SemaphoreType.DMA((4,)),
        ],
        compiler_params=pltpu.CompilerParams(vmem_limit_bytes=KERNEL_VMEM),
        cost_estimate=pl.CostEstimate(
            flops=40 * planes * layers * row_width,
            bytes_accessed=8 * planes * layers * row_width,
            transcendentals=0,
        ),
        name="prepare",
    )(
        *(
            pltpu.with_memory_space_constraint(array, pltpu.HBM)
            for array in (radius, load_index, load_force, fixed)
        )
    )


def sweep_call(spot, load, weights, inverses, free, density, displacement):
    cores, chips, own_planes, layers, row_width = density.shape
    planes = cores * chips * own_planes

    def scratch(*lead):
        return pltpu.VMEM(lead + (layers, row_width), jnp.float32)

    return pl.pallas_call(
        sweep_kernel,
        out_shape=[
            floats(3, planes, layers, row_width),
            floats(*density.shape),
            floats(planes, layers, row_width),
        ],
        in_specs=[in_smem()] + [in_vmem()] * 6,
        out_specs=[pl.BlockSpec(memory_space=pltpu.HBM), in_vmem(), in_vmem()],
        scratch_shapes=[
            scratch(planes + 4),
            scratch(planes + 4),
            scratch(planes + 4),
            scratch(planes),
            scratch(planes + 1),
            scratch(planes),
            scratch(planes),
            scratch(planes),
            scratch(planes),
            scratch(3, planes),
            scratch(3, planes + 2),
            scratch(3, planes + 2),
            scratch(3, planes),
            pltpu.SemaphoreType.DMA(()),
        ],
        compiler_params=pltpu.CompilerParams(vmem_limit_bytes=KERNEL_VMEM),
        name="sweeps",
    )(spot, load, weights, inverses, free, density, displacement)


def design_call(weights, sens, coef, density):
    cores, chips, own_planes, layers, row_width = density.shape
    planes = cores * chips * own_planes

    def scratch(*lead):
        return pltpu.VMEM(lead + (layers, row_width), jnp.float32)

    return pl.pallas_call(
        design_kernel,
        out_shape=jax.ShapeDtypeStruct((own_planes, layers, row_width), jnp.float32),
        in_specs=[in_vmem()] * 4,
        out_specs=in_vmem(),
        scratch_shapes=[
            scratch(planes + 4),
            scratch(planes + 4),
            scratch(planes + 4),
            scratch(planes),
            scratch(planes),
            scratch(planes),
        ],
        compiler_params=pltpu.CompilerParams(vmem_limit_bytes=KERNEL_VMEM),
        name="design",
    )(weights, sens, coef, density)


def other_core(block):
    devices = lax.axis_size("space")
    return lax.ppermute(block, "space", [(i, i ^ 1) for i in range(devices)])


def between_chips(pieces):
    devices = lax.axis_size("space")
    groups = [list(range(core, devices, 2)) for core in range(2)]
    return lax.all_to_all(pieces, "space", 0, 0, axis_index_groups=groups)


def chip_gathered(block):
    chips = lax.axis_size("space") // 2
    return between_chips(jnp.broadcast_to(block[None], (chips,) + block.shape))


def with_other_core(blocks):
    return jnp.stack([blocks, other_core(blocks)])


def scattered_sum(pieces):
    return jnp.sum(between_chips(pieces[0] + other_core(pieces[1])), axis=0)


def one_slab(density, displacement, fixed, load_index, load_force, radius):
    same_core, small = lax.optimization_barrier(
        (chip_gathered(density), (radius, load_index, load_force.T, fixed))
    )
    whole = with_other_core(same_core)
    weights, inverses, free, load, spot = prepare_call(*small)
    new_displacement, sens, coef = sweep_call(
        spot, load, weights, inverses, free, whole, displacement[0]
    )
    sens = with_other_core(chip_gathered(scattered_sum(sens)))
    new_density = design_call(weights, sens, coef, whole)
    return new_density, new_displacement[None]


def from_behind(block, axis, distance):
    devices = range(lax.axis_size(axis))
    route = [(i - distance, i) for i in devices if i - distance in devices]
    return lax.ppermute(block, axis, route)


def extended(x, sides, width):
    for axis, dim in sides:
        size, length = (lax.axis_size(axis), x.shape[dim])
        up = [(i, (i + 1) % size) for i in range(size - 1)]
        down = [(j, i) for i, j in up]
        last = lax.slice_in_dim(x, length - width, length, axis=dim)
        first = lax.slice_in_dim(x, 0, width, axis=dim)
        before = lax.ppermute(last, axis, up)
        after = lax.ppermute(first, axis, down)
        x = jnp.concatenate([before, x, after], axis=dim)
    return x


def from_partner(x, axis, bit):
    return lax.ppermute(x, axis, [(i, i ^ 1 << bit) for i in range(lax.axis_size(axis))])


def window_offsets():
    offsets_list = []
    for across in range(-window_reach, window_reach + 1):
        for upward in range(-window_reach, window_reach + 1):
            for sideways in range(-window_reach, window_reach + 1):
                length = math.sqrt(across * across + upward * upward + sideways * sideways)
                offsets_list.append((across, upward, sideways, length))
    return offsets_list


def layer_weights(radius):
    radial = radius.astype(jnp.float32)
    return jnp.stack(
        [jnp.maximum(radial - length, 0.0) for across, upward, sideways, length in window_offsets()]
    )


def pad_axis(grid_field, along_axis, before, after_cells):
    widths = [(0, 0)] * grid_field.ndim
    widths[along_axis] = (before, after_cells)
    return jnp.pad(grid_field, widths)


def pad_sides(grid_field):
    return jnp.pad(grid_field, ((0, 0), (window_reach, window_reach), (window_reach, window_reach)))


def filter_forward(padded, weights):
    out_rows = padded.shape[0] - 2 * window_reach
    layers = padded.shape[1] - 2 * window_reach
    row_width = padded.shape[2] - 2 * window_reach
    result = jnp.zeros((out_rows, layers, row_width), jnp.float32)
    for offset_index, (across, upward, sideways, length) in enumerate(window_offsets()):
        shifted = padded[
            window_reach + across : window_reach + across + out_rows,
            window_reach + upward : window_reach + upward + layers,
            window_reach + sideways : window_reach + sideways + row_width,
        ]
        result = result + weights[offset_index][None, :, None] * shifted
    return result


def filter_backward(padded, padded_weights):
    out_rows = padded.shape[0] - 2 * window_reach
    layers = padded.shape[1] - 2 * window_reach
    row_width = padded.shape[2] - 2 * window_reach
    result = jnp.zeros((out_rows, layers, row_width), jnp.float32)
    for offset_index, (across, upward, sideways, length) in enumerate(window_offsets()):
        shifted = padded[
            window_reach - across : window_reach - across + out_rows,
            window_reach - upward : window_reach - upward + layers,
            window_reach - sideways : window_reach - sideways + row_width,
        ]
        layer_part = padded_weights[
            offset_index, window_reach - upward : window_reach - upward + layers
        ]
        result = result + layer_part[None, :, None] * shifted
    return result


def stiff_factors(direction):
    return jnp.array(
        [2.0 if component == direction else 1.0 for component in range(3)], jnp.float32
    ).reshape(3, 1, 1, 1)


def relax_slab(padded, displace, face_x, face_z, face_y, force_field, free_cells, diagonal):
    flux_x = stiff_factors(0) * face_x * jnp.diff(padded, axis=1)
    stencil_image = flux_x[:, :-1] - flux_x[:, 1:]
    flux_z = stiff_factors(1) * face_z * jnp.diff(displace, axis=2)
    stencil_image = stencil_image + pad_axis(flux_z, 2, 1, 0) - pad_axis(flux_z, 2, 0, 1)
    flux_y = stiff_factors(2) * face_y * jnp.diff(displace, axis=3)
    stencil_image = stencil_image + pad_axis(flux_y, 3, 1, 0) - pad_axis(flux_y, 3, 0, 1)
    return free_cells * (displace + relax_factor * (force_field - stencil_image) / diagonal)


def slab_energy(grid_field, along_axis, direction, load_cases):
    change = jnp.diff(grid_field, axis=along_axis)
    return jnp.sum(stiff_factors(direction) * change * change, axis=0) / load_cases


def neighbour_planes(displace, load_cases, axis_devices):
    if axis_devices > load_cases:
        below = from_behind(displace[:, -1:], "space", load_cases)
        above = from_behind(displace[:, :1], "space", -load_cases)
    else:
        below = jnp.zeros_like(displace[:, :1])
        above = jnp.zeros_like(displace[:, :1])
    return jnp.concatenate([below, displace, above], axis=1)


def many_slabs(density, displacement, fixed, load_index, load_force, radius):
    slab_rows, layers, row_width = density.shape
    load_cases = load_index.shape[0]
    level_count = load_cases.bit_length() - 1
    axis_devices = lax.axis_size("space")
    axis_place = lax.axis_index("space")
    slab_planes = slab_rows * load_cases
    slab_place = axis_place // load_cases
    load_place = axis_place % load_cases
    total_rows = slab_rows * axis_devices
    weights = layer_weights(radius)
    padded_weights = pad_axis(weights, 1, window_reach, window_reach)
    global_rows = (
        jnp.arange(slab_rows + 2 * window_reach, dtype=jnp.int32)
        + axis_place * slab_rows
        - window_reach
    )
    deep_inside = ((global_rows >= 0) & (global_rows < total_rows)).astype(jnp.float32)
    inside_field = deep_inside[:, None, None] * pad_sides(
        jnp.ones((slab_rows + 2 * window_reach, layers, row_width), jnp.float32)
    )
    total_weight = filter_forward(inside_field, weights)
    slab_start = slab_place * slab_planes
    margin_rows = jnp.arange(slab_planes + 2, dtype=jnp.int32) + slab_start - 1
    margin_inside = ((margin_rows >= 0) & (margin_rows < total_rows)).astype(jnp.float32)
    face_valid = margin_inside[1:] * margin_inside[:-1]
    fixed_slab = lax.dynamic_slice_in_dim(fixed, slab_start, slab_planes, 0).astype(jnp.float32)
    bottom_layer = (jnp.arange(layers, dtype=jnp.int32) == 0).astype(jnp.float32)
    free_cells = 1.0 - bottom_layer[None, :, None] * fixed_slab[:, None, :]
    slab_cells = slab_planes * layers * row_width
    cell_index = jnp.arange(slab_cells, dtype=jnp.int32) + slab_place * slab_cells
    load_hot = jnp.arange(load_cases, dtype=jnp.int32) == load_place
    own_index = jnp.sum(jnp.where(load_hot, load_index, 0))
    own_force = jnp.sum(load_hot.astype(jnp.float32)[:, None] * load_force, axis=0)
    load_hits = (cell_index == own_index).astype(jnp.float32)
    force_field = (own_force[:, None] * load_hits[None, :]).reshape(
        3, slab_planes, layers, row_width
    )
    displace = displacement[0] * free_cells
    target = volume_share * total_rows * layers * row_width
    padded = neighbour_planes(displace, load_cases, axis_devices)
    halo_density = extended(density, (("space", 0),), window_reach)
    filtered = filter_forward(pad_sides(halo_density), weights) / total_weight
    whole_field = lax.all_gather(filtered, "space", axis=0, tiled=True)
    margin = lax.dynamic_slice_in_dim(
        pad_axis(whole_field, 0, 1, 1), slab_start, slab_planes + 2, 0
    )
    moduli = floor_modulus + (1.0 - floor_modulus) * margin**3
    face_x = 0.5 * (moduli[1:] + moduli[:-1]) * face_valid[:, None, None]
    inner_moduli = moduli[1:-1]
    face_z = 0.5 * (inner_moduli[:, 1:] + inner_moduli[:, :-1])
    face_y = 0.5 * (inner_moduli[:, :, 1:] + inner_moduli[:, :, :-1])
    sum_x = face_x[:-1] + face_x[1:]
    sum_z = pad_axis(face_z, 1, 1, 0) + pad_axis(face_z, 1, 0, 1)
    sum_y = pad_axis(face_y, 2, 1, 0) + pad_axis(face_y, 2, 0, 1)
    diagonal = stiff_factors(0) * sum_x + stiff_factors(1) * sum_z + stiff_factors(2) * sum_y
    for sweep_index in range(SWEEPS):
        displace = relax_slab(
            padded, displace, face_x, face_z, face_y, force_field, free_cells, diagonal
        )
        padded = neighbour_planes(displace, load_cases, axis_devices)
    energy_x = slab_energy(padded, 1, 0, load_cases) * face_valid[:, None, None]
    energy_z = slab_energy(displace, 2, 1, load_cases)
    energy_y = slab_energy(displace, 3, 2, load_cases)
    sens_term = 0.5 * (
        energy_x[:-1]
        + energy_x[1:]
        + pad_axis(energy_z, 1, 1, 0)
        + pad_axis(energy_z, 1, 0, 1)
        + pad_axis(energy_y, 2, 1, 0)
        + pad_axis(energy_y, 2, 0, 1)
    )
    sensitive = sens_term
    for level in reversed(range(level_count)):
        half_rows = sensitive.shape[0] // 2
        upper_side = load_place // 2**level % 2 == 1
        outgoing = jnp.where(upper_side, sensitive[:half_rows], sensitive[half_rows:])
        keeping = jnp.where(upper_side, sensitive[half_rows:], sensitive[:half_rows])
        sensitive = keeping + from_partner(outgoing, "space", level)
    weighted_share = 3.0 * (1.0 - floor_modulus) * filtered**2 * sensitive / total_weight
    halo_share = extended(weighted_share, (("space", 0),), window_reach)
    root_term = jnp.sqrt(filter_backward(pad_sides(halo_share), padded_weights))
    lowest = jnp.maximum(density - move_limit, density_floor)
    highest = jnp.minimum(density + move_limit, 1.0)
    design_now = density

    def trial_design(log_level):
        return jnp.clip(design_now * root_term * jnp.exp(-0.5 * log_level), lowest, highest)

    start_state = (jnp.asarray(log_lower, jnp.float32), jnp.asarray(log_span, jnp.float32))

    def halve(search_step, search_state):
        lower_end, span_width = search_state
        half_span = span_width * 0.5
        middle = lower_end + half_span
        volume_total = lax.psum(jnp.sum(trial_design(middle)), "space")
        return (jnp.where(volume_total > target, middle, lower_end), half_span)

    lower_end, span_width = lax.fori_loop(0, SEARCH, halve, start_state)
    density = trial_design(lower_end + 0.5 * span_width)
    new_displacement = displace[None]
    return (density, new_displacement)


def solution(mesh):
    in_specs = (
        P("space", "parts", None),
        P("space", None, None, "parts", None),
        P(None, "parts"),
        P("parts"),
        P("parts", None),
        P("parts"),
    )
    out_specs = (P("space", "parts", None), P("space", None, None, "parts", None))

    def local(density, displacement, fixed, load_index, load_force, radius):
        alone = lax.axis_size("space") == load_index.shape[0]
        run = one_slab if alone else many_slabs
        return run(density, displacement, fixed, load_index, load_force, radius)

    return jax.shard_map(local, mesh=mesh, in_specs=in_specs, out_specs=out_specs, check_vma=False)
```

```python
import math

import jax
import jax.numpy as jnp
from jax import lax
from jax.experimental import pallas as pl
from jax.experimental.pallas import tpu as pltpu
from jax.sharding import PartitionSpec as P

SWEEPS = 3
SEARCH = 12


floor_modulus = 0.05
relax_factor = 0.6
move_limit = 0.2
density_floor = 0.01
volume_share = 0.5
log_lower = -16.0
log_span = 32.0
window_reach = 2

PLANE_SQUARES = (0, 1, 2, 4, 5, 8)
ALL_SQUARES = (0, 1, 2, 3, 4, 5, 6, 8, 9, 12)


def spot_iota(shape, dim):
    return lax.broadcasted_iota(jnp.int32, shape, dim)


def layer_radius(radius_ref, layers, row_width):
    z = spot_iota((layers, row_width), 0)
    result = jnp.zeros((layers, row_width), jnp.int32)
    for layer in range(layers):
        result = jnp.where(z == layer, radius_ref[layer], result)
    return result.astype(jnp.float32)


def class_weights(radius_ref, weight_ref):
    layers, row_width = weight_ref.shape[1:]
    radial = layer_radius(radius_ref, layers, row_width)
    for place, square in enumerate(ALL_SQUARES):
        weight_ref[place] = jnp.maximum(radial - math.sqrt(square), 0.0)


def shift_sum(field, dim, distance):
    size = field.shape[dim]
    spot = spot_iota(field.shape, dim)
    ahead = jnp.where(spot < size - distance, pltpu.roll(field, size - distance, dim), 0.0)
    behind = jnp.where(spot >= distance, pltpu.roll(field, distance, dim), 0.0)
    return ahead + behind


def plane_sums(plane):
    beside = shift_sum(plane, 1, 1)
    further = shift_sum(plane, 1, 2)
    return {
        0: plane,
        1: beside + shift_sum(plane, 0, 1),
        2: shift_sum(beside, 0, 1),
        4: further + shift_sum(plane, 0, 2),
        5: shift_sum(further, 0, 1) + shift_sum(beside, 0, 2),
        8: shift_sum(further, 0, 2),
    }


def weigh(sums, weight_ref, square):
    result = None
    for inner in PLANE_SQUARES:
        term = weight_ref[ALL_SQUARES.index(inner + square)] * sums[inner]
        result = term if result is None else result + term
    return result


def forward_planes(plane, weight_ref):
    sums = plane_sums(plane)
    return [weigh(sums, weight_ref, square) for square in (0, 1, 4)]


def backward_planes(plane, weight_ref):
    beside = shift_sum(plane, 1, 1)
    further = shift_sum(plane, 1, 2)
    results = []
    for square in (0, 1, 4):

        def weight(more):
            return weight_ref[ALL_SQUARES.index(square + more)]

        level = weight(0) * plane + weight(1) * beside + weight(4) * further
        near = weight(1) * plane + weight(2) * beside + weight(5) * further
        far = weight(4) * plane + weight(5) * beside + weight(8) * further
        results.append(level + shift_sum(near, 0, 1) + shift_sum(far, 0, 2))
    return results


def pair_spot(x, own_planes):
    device = x // own_planes
    apart = device ^ lax.axis_index("space")
    return (apart ^ apart >> 1) & 1, device >> 1, x % own_planes


def edge_class(x, planes):
    return jnp.minimum(x, 2) + jnp.maximum(x - (planes - 3), 0)


def zero_edges(ref):
    planes = ref.shape[0]
    for place in (0, 1, planes - 2, planes - 1):
        ref[place] = jnp.zeros(ref.shape[1:], ref.dtype)


def prepare_kernel(
    radius_hbm,
    index_hbm,
    force_hbm,
    fixed_hbm,
    weight_ref,
    inverse_ref,
    free_ref,
    load_ref,
    spot_ref,
    radius_ref,
    index_ref,
    force_ref,
    fixed_ref,
    arrived,
):
    copies = [
        pltpu.make_async_copy(source, target, arrived.at[place])
        for place, (source, target) in enumerate(
            (
                (radius_hbm, radius_ref),
                (index_hbm, index_ref),
                (force_hbm, force_ref),
                (fixed_hbm, fixed_ref),
            )
        )
    ]
    for copy in copies:
        copy.start()
    for copy in copies:
        copy.wait()
    planes, layers, row_width = free_ref.shape
    load_place = lax.axis_index("space")
    shape = (layers, row_width)
    z = spot_iota(shape, 0)
    y = spot_iota(shape, 1)

    class_weights(radius_ref, weight_ref)
    ones = forward_planes(jnp.ones(shape, jnp.float32), weight_ref)
    for place, (lower, upper) in enumerate(((0, 2), (1, 2), (2, 2), (2, 1), (2, 0))):
        inverse_ref[place] = 1.0 / (
            ones[0] + min(lower, 1) * ones[1] + min(upper, 1) * ones[1]
            + (lower // 2) * ones[2] + (upper // 2) * ones[2]
        )

    def free_plane(x, carry):
        free_ref[x] = jnp.where(
            z == 0, 1.0 - fixed_ref[pl.ds(x, 1), :].astype(jnp.float32), 1.0
        )
        return carry

    lax.fori_loop(0, planes, free_plane, 0, unroll=16)

    own_index = index_ref[load_place]
    own_z = own_index // row_width % layers
    own_y = own_index % row_width
    hit = (z == own_z) & (y == own_y)
    for part in range(3):
        load_ref[part] = jnp.where(hit, force_ref[part, load_place], 0.0)
    spot_ref[0] = own_index // (layers * row_width)


def sweep_kernel(
    spot_ref,
    load_ref,
    weight_ref,
    inverse_ref,
    free_ref,
    density_ref,
    start_ref,
    disp_hbm,
    sens_ref,
    coef_ref,
    near_ref,
    side_ref,
    far_ref,
    modulus_ref,
    across_ref,
    up_ref,
    down_ref,
    right_ref,
    left_ref,
    rate_ref,
    first_ref,
    second_ref,
    disp_ref,
    stored,
):
    planes, layers, row_width = coef_ref.shape
    own_planes = density_ref.shape[2]
    load_cases = lax.axis_size("space")
    shape = (layers, row_width)
    z = spot_iota(shape, 0)
    y = spot_iota(shape, 1)
    zero = jnp.zeros(shape, jnp.float32)

    for ref in (side_ref, far_ref):
        zero_edges(ref)

    def filter_plane(x, carry):
        near, side, far = forward_planes(density_ref[pair_spot(x, own_planes)], weight_ref)
        near_ref[x + 2] = near
        side_ref[x + 2] = side
        far_ref[x + 2] = far
        return carry

    lax.fori_loop(0, planes, filter_plane, 0, unroll=16)

    def modulus_plane(x, carry):
        inverse = inverse_ref[edge_class(x, planes)]
        filtered = (
            near_ref[x + 2]
            + side_ref[x + 1]
            + side_ref[x + 3]
            + far_ref[x]
            + far_ref[x + 4]
        ) * inverse
        modulus = floor_modulus + (1.0 - floor_modulus) * (filtered * filtered * filtered)
        modulus_ref[x] = modulus
        coef_ref[x] = 3.0 * (1.0 - floor_modulus) * (filtered * filtered) * inverse
        return carry

    lax.fori_loop(0, planes, modulus_plane, 0, unroll=16)

    across_ref[0] = zero
    across_ref[planes] = zero
    for ref in (first_ref, second_ref):
        for part in range(3):
            ref[part, 0] = zero
            ref[part, planes + 1] = zero

    def face_plane(x, carry):
        modulus = modulus_ref[x]
        later = modulus_ref[jnp.minimum(x + 1, planes - 1)]
        ahead = jnp.where(x + 1 < planes, 0.5 * (modulus + later), 0.0)
        across_ref[x + 1] = ahead
        up = jnp.where(z < layers - 1, 0.5 * (modulus + pltpu.roll(modulus, layers - 1, 0)), 0.0)
        down = pltpu.roll(up, 1, 0)
        right = jnp.where(
            y < row_width - 1, 0.5 * (modulus + pltpu.roll(modulus, row_width - 1, 1)), 0.0
        )
        left = pltpu.roll(right, 1, 1)
        up_ref[x] = up
        down_ref[x] = down
        right_ref[x] = right
        left_ref[x] = left
        sums = (carry + ahead, up + down, left + right)
        every = sums[0] + sums[1] + sums[2]
        free = free_ref[x]
        push = relax_factor * free
        diagonal = [every + part_sum for part_sum in sums]
        pair = diagonal[0] * diagonal[1]
        push = push / (pair * diagonal[2])
        side = push * diagonal[2]
        rate_ref[0, x] = side * diagonal[1]
        rate_ref[1, x] = side * diagonal[0]
        rate_ref[2, x] = push * pair
        for part in range(3):
            first_ref[part, x + 1] = start_ref[part, x] * free
        return ahead

    lax.fori_loop(0, planes, face_plane, zero, unroll=16)

    own_x = spot_ref[0]

    def sweep(source, target, lead):
        def sweep_plane(x, carry):
            before, after = across_ref[x], across_ref[x + 1]
            up, down, right, left = up_ref[x], down_ref[x], right_ref[x], left_ref[x]
            for part in range(3):
                here = source[part, x + 1]
                pulls = [
                    before * source[part, x] + after * source[part, x + 2],
                    up * pltpu.roll(here, layers - 1, 0) + down * pltpu.roll(here, 1, 0),
                    right * pltpu.roll(here, row_width - 1, 1) + left * pltpu.roll(here, 1, 1),
                ]
                pull = pulls[0] + pulls[1] + pulls[2] + pulls[part]
                target[part, x + lead] = (1.0 - relax_factor) * here + rate_ref[part, x] * pull
            return carry

        lax.fori_loop(0, planes, sweep_plane, 0, unroll=16)
        for part in range(3):
            target[part, own_x + lead] += rate_ref[part, own_x] * load_ref[part]

    stages = (first_ref, second_ref)
    for turn in range(SWEEPS - 1):
        sweep(stages[turn % 2], stages[(turn + 1) % 2], 1)
    sweep(stages[(SWEEPS - 1) % 2], disp_ref, 0)
    store = pltpu.make_async_copy(disp_ref, disp_hbm, stored)
    store.start()

    def energy_plane(x, carry):
        later = jnp.minimum(x + 1, planes - 1)
        ahead, upward, right = zero, zero, zero
        for part in range(3):
            here = disp_ref[part, x]
            step = disp_ref[part, later] - here
            climb = pltpu.roll(here, layers - 1, 0) - here
            slide = pltpu.roll(here, row_width - 1, 1) - here
            ahead = ahead + (2.0 if part == 0 else 1.0) * (step * step)
            upward = upward + (2.0 if part == 1 else 1.0) * (climb * climb)
            right = right + (2.0 if part == 2 else 1.0) * (slide * slide)
        upward = jnp.where(z < layers - 1, upward, 0.0)
        right = jnp.where(y < row_width - 1, right, 0.0)
        total = carry + ahead + upward + pltpu.roll(upward, 1, 0) + right + pltpu.roll(right, 1, 1)
        sens_ref[pair_spot(x, own_planes)] = (0.5 / load_cases) * total
        return ahead

    lax.fori_loop(0, planes, energy_plane, zero, unroll=16)
    store.wait()


def design_kernel(
    weight_ref,
    sens_ref,
    coef_ref,
    density_ref,
    new_ref,
    near_ref,
    side_ref,
    far_ref,
    pull_ref,
    low_ref,
    high_ref,
):
    planes, layers, row_width = coef_ref.shape
    own_planes = density_ref.shape[2]
    place = lax.axis_index("space")
    shape = (layers, row_width)
    zero = jnp.zeros(shape, jnp.float32)
    for ref in (side_ref, far_ref):
        zero_edges(ref)

    def filter_plane(x, carry):
        near, side, far = backward_planes(
            sens_ref[pair_spot(x, own_planes)] * coef_ref[x], weight_ref
        )
        near_ref[x + 2] = near
        side_ref[x + 2] = side
        far_ref[x + 2] = far
        return carry

    lax.fori_loop(0, planes, filter_plane, 0, unroll=16)

    def root_plane(x, carry):
        root = jnp.sqrt(
            near_ref[x + 2] + side_ref[x + 1] + side_ref[x + 3] + far_ref[x] + far_ref[x + 4]
        )
        density = density_ref[pair_spot(x, own_planes)]
        pull_ref[x] = density * root
        low_ref[x] = jnp.maximum(density - move_limit, density_floor)
        high_ref[x] = jnp.minimum(density + move_limit, 1.0)
        return carry

    lax.fori_loop(0, planes, root_plane, 0, unroll=16)

    target = volume_share * planes * layers * row_width

    def trial(x, factor):
        return jnp.minimum(jnp.maximum(pull_ref[x] * factor, low_ref[x]), high_ref[x])

    def halve(step, state):
        lower, span = state
        half = span * 0.5
        middle = lower + half
        factor = jnp.exp(-0.5 * middle)
        total = lax.fori_loop(
            0, planes, lambda x, acc: acc + trial(x, factor), zero, unroll=8
        )
        volume = jnp.sum(jnp.sum(total, axis=0, keepdims=True), axis=1, keepdims=True)
        return jnp.where(volume > target, middle, lower), half

    start = (jnp.full((1, 1), log_lower, jnp.float32), jnp.full((1, 1), log_span, jnp.float32))
    lower, span = lax.fori_loop(0, SEARCH, halve, start)
    factor = jnp.exp(-0.5 * (lower + 0.5 * span))
    for own in range(own_planes):
        new_ref[own] = trial(place * own_planes + own, factor)


def in_vmem():
    return pl.BlockSpec(memory_space=pltpu.VMEM)


def in_smem():
    return pl.BlockSpec(memory_space=pltpu.SMEM)


KERNEL_VMEM = 24 * 2**20


def floats(*shape):
    return jax.ShapeDtypeStruct(shape, jnp.float32)


def prepare_call(radius, load_index, load_force, fixed):
    planes, row_width = fixed.shape
    layers = radius.shape[0]
    return pl.pallas_call(
        prepare_kernel,
        out_shape=[
            floats(len(ALL_SQUARES), layers, row_width),
            floats(2 * window_reach + 1, layers, row_width),
            floats(planes, layers, row_width),
            floats(3, layers, row_width),
            jax.ShapeDtypeStruct((1,), jnp.int32),
        ],
        in_specs=[pl.BlockSpec(memory_space=pltpu.HBM)] * 4,
        out_specs=[in_vmem()] * 4 + [in_smem()],
        scratch_shapes=[
            pltpu.SMEM(radius.shape, radius.dtype),
            pltpu.SMEM(load_index.shape, load_index.dtype),
            pltpu.SMEM(load_force.shape, load_force.dtype),
            pltpu.VMEM(fixed.shape, fixed.dtype),
            pltpu.SemaphoreType.DMA((4,)),
        ],
        compiler_params=pltpu.CompilerParams(vmem_limit_bytes=KERNEL_VMEM),
        cost_estimate=pl.CostEstimate(
            flops=40 * planes * layers * row_width,
            bytes_accessed=8 * planes * layers * row_width,
            transcendentals=0,
        ),
        name="prepare",
    )(
        *(
            pltpu.with_memory_space_constraint(array, pltpu.HBM)
            for array in (radius, load_index, load_force, fixed)
        )
    )


def sweep_call(spot, load, weights, inverses, free, density, displacement):
    cores, chips, own_planes, layers, row_width = density.shape
    planes = cores * chips * own_planes

    def scratch(*lead):
        return pltpu.VMEM(lead + (layers, row_width), jnp.float32)

    return pl.pallas_call(
        sweep_kernel,
        out_shape=[
            floats(3, planes, layers, row_width),
            floats(*density.shape),
            floats(planes, layers, row_width),
        ],
        in_specs=[in_smem()] + [in_vmem()] * 6,
        out_specs=[pl.BlockSpec(memory_space=pltpu.HBM), in_vmem(), in_vmem()],
        scratch_shapes=[
            scratch(planes + 4),
            scratch(planes + 4),
            scratch(planes + 4),
            scratch(planes),
            scratch(planes + 1),
            scratch(planes),
            scratch(planes),
            scratch(planes),
            scratch(planes),
            scratch(3, planes),
            scratch(3, planes + 2),
            scratch(3, planes + 2),
            scratch(3, planes),
            pltpu.SemaphoreType.DMA(()),
        ],
        compiler_params=pltpu.CompilerParams(vmem_limit_bytes=KERNEL_VMEM),
        name="sweeps",
    )(spot, load, weights, inverses, free, density, displacement)


def design_call(weights, sens, coef, density):
    cores, chips, own_planes, layers, row_width = density.shape
    planes = cores * chips * own_planes

    def scratch(*lead):
        return pltpu.VMEM(lead + (layers, row_width), jnp.float32)

    return pl.pallas_call(
        design_kernel,
        out_shape=jax.ShapeDtypeStruct((own_planes, layers, row_width), jnp.float32),
        in_specs=[in_vmem()] * 4,
        out_specs=in_vmem(),
        scratch_shapes=[
            scratch(planes + 4),
            scratch(planes + 4),
            scratch(planes + 4),
            scratch(planes),
            scratch(planes),
            scratch(planes),
        ],
        compiler_params=pltpu.CompilerParams(vmem_limit_bytes=KERNEL_VMEM),
        name="design",
    )(weights, sens, coef, density)


def other_core(block):
    devices = lax.axis_size("space")
    return lax.ppermute(block, "space", [(i, i ^ 1) for i in range(devices)])


def chip_groups():
    chips = lax.axis_size("space") // 2
    return [[2 * chip + (chip ^ group) % 2 for chip in range(chips)] for group in range(2)]


def between_chips(pieces):
    return lax.all_to_all(pieces, "space", 0, 0, axis_index_groups=chip_groups())


def chip_gathered(block):
    chips = lax.axis_size("space") // 2
    return between_chips(jnp.broadcast_to(block[None], (chips,) + block.shape))


def with_other_core(blocks):
    return jnp.stack([blocks, other_core(blocks)])


def scattered_sum(pieces):
    return jnp.sum(between_chips(pieces[0] + other_core(pieces[1])), axis=0)


def one_slab(density, displacement, fixed, load_index, load_force, radius):
    same_group, small = lax.optimization_barrier(
        (chip_gathered(density), (radius, load_index, load_force.T, fixed))
    )
    whole = with_other_core(same_group)
    weights, inverses, free, load, spot = prepare_call(*small)
    new_displacement, sens, coef = sweep_call(
        spot, load, weights, inverses, free, whole, displacement[0]
    )
    sens = with_other_core(chip_gathered(scattered_sum(sens)))
    new_density = design_call(weights, sens, coef, whole)
    return new_density, new_displacement[None]


def from_behind(block, axis, distance):
    devices = range(lax.axis_size(axis))
    route = [(i - distance, i) for i in devices if i - distance in devices]
    return lax.ppermute(block, axis, route)


def extended(x, sides, width):
    for axis, dim in sides:
        size, length = (lax.axis_size(axis), x.shape[dim])
        up = [(i, (i + 1) % size) for i in range(size - 1)]
        down = [(j, i) for i, j in up]
        last = lax.slice_in_dim(x, length - width, length, axis=dim)
        first = lax.slice_in_dim(x, 0, width, axis=dim)
        before = lax.ppermute(last, axis, up)
        after = lax.ppermute(first, axis, down)
        x = jnp.concatenate([before, x, after], axis=dim)
    return x


def from_partner(x, axis, bit):
    return lax.ppermute(x, axis, [(i, i ^ 1 << bit) for i in range(lax.axis_size(axis))])


def window_offsets():
    offsets_list = []
    for across in range(-window_reach, window_reach + 1):
        for upward in range(-window_reach, window_reach + 1):
            for sideways in range(-window_reach, window_reach + 1):
                length = math.sqrt(across * across + upward * upward + sideways * sideways)
                offsets_list.append((across, upward, sideways, length))
    return offsets_list


def layer_weights(radius):
    radial = radius.astype(jnp.float32)
    return jnp.stack(
        [jnp.maximum(radial - length, 0.0) for across, upward, sideways, length in window_offsets()]
    )


def pad_axis(grid_field, along_axis, before, after_cells):
    widths = [(0, 0)] * grid_field.ndim
    widths[along_axis] = (before, after_cells)
    return jnp.pad(grid_field, widths)


def pad_sides(grid_field):
    return jnp.pad(grid_field, ((0, 0), (window_reach, window_reach), (window_reach, window_reach)))


def filter_forward(padded, weights):
    out_rows = padded.shape[0] - 2 * window_reach
    layers = padded.shape[1] - 2 * window_reach
    row_width = padded.shape[2] - 2 * window_reach
    result = jnp.zeros((out_rows, layers, row_width), jnp.float32)
    for offset_index, (across, upward, sideways, length) in enumerate(window_offsets()):
        shifted = padded[
            window_reach + across : window_reach + across + out_rows,
            window_reach + upward : window_reach + upward + layers,
            window_reach + sideways : window_reach + sideways + row_width,
        ]
        result = result + weights[offset_index][None, :, None] * shifted
    return result


def filter_backward(padded, padded_weights):
    out_rows = padded.shape[0] - 2 * window_reach
    layers = padded.shape[1] - 2 * window_reach
    row_width = padded.shape[2] - 2 * window_reach
    result = jnp.zeros((out_rows, layers, row_width), jnp.float32)
    for offset_index, (across, upward, sideways, length) in enumerate(window_offsets()):
        shifted = padded[
            window_reach - across : window_reach - across + out_rows,
            window_reach - upward : window_reach - upward + layers,
            window_reach - sideways : window_reach - sideways + row_width,
        ]
        layer_part = padded_weights[
            offset_index, window_reach - upward : window_reach - upward + layers
        ]
        result = result + layer_part[None, :, None] * shifted
    return result


def stiff_factors(direction):
    return jnp.array(
        [2.0 if component == direction else 1.0 for component in range(3)], jnp.float32
    ).reshape(3, 1, 1, 1)


def relax_slab(padded, displace, face_x, face_z, face_y, force_field, free_cells, diagonal):
    flux_x = stiff_factors(0) * face_x * jnp.diff(padded, axis=1)
    stencil_image = flux_x[:, :-1] - flux_x[:, 1:]
    flux_z = stiff_factors(1) * face_z * jnp.diff(displace, axis=2)
    stencil_image = stencil_image + pad_axis(flux_z, 2, 1, 0) - pad_axis(flux_z, 2, 0, 1)
    flux_y = stiff_factors(2) * face_y * jnp.diff(displace, axis=3)
    stencil_image = stencil_image + pad_axis(flux_y, 3, 1, 0) - pad_axis(flux_y, 3, 0, 1)
    return free_cells * (displace + relax_factor * (force_field - stencil_image) / diagonal)


def slab_energy(grid_field, along_axis, direction, load_cases):
    change = jnp.diff(grid_field, axis=along_axis)
    return jnp.sum(stiff_factors(direction) * change * change, axis=0) / load_cases


def neighbour_planes(displace, load_cases, axis_devices):
    if axis_devices > load_cases:
        below = from_behind(displace[:, -1:], "space", load_cases)
        above = from_behind(displace[:, :1], "space", -load_cases)
    else:
        below = jnp.zeros_like(displace[:, :1])
        above = jnp.zeros_like(displace[:, :1])
    return jnp.concatenate([below, displace, above], axis=1)


def many_slabs(density, displacement, fixed, load_index, load_force, radius):
    slab_rows, layers, row_width = density.shape
    load_cases = load_index.shape[0]
    level_count = load_cases.bit_length() - 1
    axis_devices = lax.axis_size("space")
    axis_place = lax.axis_index("space")
    slab_planes = slab_rows * load_cases
    slab_place = axis_place // load_cases
    load_place = axis_place % load_cases
    total_rows = slab_rows * axis_devices
    weights = layer_weights(radius)
    padded_weights = pad_axis(weights, 1, window_reach, window_reach)
    global_rows = (
        jnp.arange(slab_rows + 2 * window_reach, dtype=jnp.int32)
        + axis_place * slab_rows
        - window_reach
    )
    deep_inside = ((global_rows >= 0) & (global_rows < total_rows)).astype(jnp.float32)
    inside_field = deep_inside[:, None, None] * pad_sides(
        jnp.ones((slab_rows + 2 * window_reach, layers, row_width), jnp.float32)
    )
    total_weight = filter_forward(inside_field, weights)
    slab_start = slab_place * slab_planes
    margin_rows = jnp.arange(slab_planes + 2, dtype=jnp.int32) + slab_start - 1
    margin_inside = ((margin_rows >= 0) & (margin_rows < total_rows)).astype(jnp.float32)
    face_valid = margin_inside[1:] * margin_inside[:-1]
    fixed_slab = lax.dynamic_slice_in_dim(fixed, slab_start, slab_planes, 0).astype(jnp.float32)
    bottom_layer = (jnp.arange(layers, dtype=jnp.int32) == 0).astype(jnp.float32)
    free_cells = 1.0 - bottom_layer[None, :, None] * fixed_slab[:, None, :]
    slab_cells = slab_planes * layers * row_width
    cell_index = jnp.arange(slab_cells, dtype=jnp.int32) + slab_place * slab_cells
    load_hot = jnp.arange(load_cases, dtype=jnp.int32) == load_place
    own_index = jnp.sum(jnp.where(load_hot, load_index, 0))
    own_force = jnp.sum(load_hot.astype(jnp.float32)[:, None] * load_force, axis=0)
    load_hits = (cell_index == own_index).astype(jnp.float32)
    force_field = (own_force[:, None] * load_hits[None, :]).reshape(
        3, slab_planes, layers, row_width
    )
    displace = displacement[0] * free_cells
    target = volume_share * total_rows * layers * row_width
    padded = neighbour_planes(displace, load_cases, axis_devices)
    halo_density = extended(density, (("space", 0),), window_reach)
    filtered = filter_forward(pad_sides(halo_density), weights) / total_weight
    whole_field = lax.all_gather(filtered, "space", axis=0, tiled=True)
    margin = lax.dynamic_slice_in_dim(
        pad_axis(whole_field, 0, 1, 1), slab_start, slab_planes + 2, 0
    )
    moduli = floor_modulus + (1.0 - floor_modulus) * margin**3
    face_x = 0.5 * (moduli[1:] + moduli[:-1]) * face_valid[:, None, None]
    inner_moduli = moduli[1:-1]
    face_z = 0.5 * (inner_moduli[:, 1:] + inner_moduli[:, :-1])
    face_y = 0.5 * (inner_moduli[:, :, 1:] + inner_moduli[:, :, :-1])
    sum_x = face_x[:-1] + face_x[1:]
    sum_z = pad_axis(face_z, 1, 1, 0) + pad_axis(face_z, 1, 0, 1)
    sum_y = pad_axis(face_y, 2, 1, 0) + pad_axis(face_y, 2, 0, 1)
    diagonal = stiff_factors(0) * sum_x + stiff_factors(1) * sum_z + stiff_factors(2) * sum_y
    for sweep_index in range(SWEEPS):
        displace = relax_slab(
            padded, displace, face_x, face_z, face_y, force_field, free_cells, diagonal
        )
        padded = neighbour_planes(displace, load_cases, axis_devices)
    energy_x = slab_energy(padded, 1, 0, load_cases) * face_valid[:, None, None]
    energy_z = slab_energy(displace, 2, 1, load_cases)
    energy_y = slab_energy(displace, 3, 2, load_cases)
    sens_term = 0.5 * (
        energy_x[:-1]
        + energy_x[1:]
        + pad_axis(energy_z, 1, 1, 0)
        + pad_axis(energy_z, 1, 0, 1)
        + pad_axis(energy_y, 2, 1, 0)
        + pad_axis(energy_y, 2, 0, 1)
    )
    sensitive = sens_term
    for level in reversed(range(level_count)):
        half_rows = sensitive.shape[0] // 2
        upper_side = load_place // 2**level % 2 == 1
        outgoing = jnp.where(upper_side, sensitive[:half_rows], sensitive[half_rows:])
        keeping = jnp.where(upper_side, sensitive[half_rows:], sensitive[:half_rows])
        sensitive = keeping + from_partner(outgoing, "space", level)
    weighted_share = 3.0 * (1.0 - floor_modulus) * filtered**2 * sensitive / total_weight
    halo_share = extended(weighted_share, (("space", 0),), window_reach)
    root_term = jnp.sqrt(filter_backward(pad_sides(halo_share), padded_weights))
    lowest = jnp.maximum(density - move_limit, density_floor)
    highest = jnp.minimum(density + move_limit, 1.0)
    design_now = density

    def trial_design(log_level):
        return jnp.clip(design_now * root_term * jnp.exp(-0.5 * log_level), lowest, highest)

    start_state = (jnp.asarray(log_lower, jnp.float32), jnp.asarray(log_span, jnp.float32))

    def halve(search_step, search_state):
        lower_end, span_width = search_state
        half_span = span_width * 0.5
        middle = lower_end + half_span
        volume_total = lax.psum(jnp.sum(trial_design(middle)), "space")
        return (jnp.where(volume_total > target, middle, lower_end), half_span)

    lower_end, span_width = lax.fori_loop(0, SEARCH, halve, start_state)
    density = trial_design(lower_end + 0.5 * span_width)
    new_displacement = displace[None]
    return (density, new_displacement)


def solution(mesh):
    in_specs = (
        P("space", "parts", None),
        P("space", None, None, "parts", None),
        P(None, "parts"),
        P("parts"),
        P("parts", None),
        P("parts"),
    )
    out_specs = (P("space", "parts", None), P("space", None, None, "parts", None))

    def local(density, displacement, fixed, load_index, load_force, radius):
        alone = lax.axis_size("space") == load_index.shape[0]
        run = one_slab if alone else many_slabs
        return run(density, displacement, fixed, load_index, load_force, radius)

    return jax.shard_map(local, mesh=mesh, in_specs=in_specs, out_specs=out_specs, check_vma=False)
```

```python
import math

import jax
import jax.numpy as jnp
from jax import lax
from jax.experimental import pallas as pl
from jax.experimental.pallas import tpu as pltpu
from jax.sharding import PartitionSpec as P

SWEEPS = 3
SEARCH = 12


floor_modulus = 0.05
relax_factor = 0.6
move_limit = 0.2
density_floor = 0.01
volume_share = 0.5
log_lower = -16.0
log_span = 32.0
window_reach = 2

PLANE_SQUARES = (0, 1, 2, 4, 5, 8)
ALL_SQUARES = (0, 1, 2, 3, 4, 5, 6, 8, 9, 12)


def spot_iota(shape, dim):
    return lax.broadcasted_iota(jnp.int32, shape, dim)


def layer_radius(radius_ref, layers, row_width):
    z = spot_iota((layers, row_width), 0)
    result = jnp.zeros((layers, row_width), jnp.int32)
    for layer in range(layers):
        result = jnp.where(z == layer, radius_ref[layer], result)
    return result.astype(jnp.float32)


def class_weights(radius_ref, weight_ref):
    layers, row_width = weight_ref.shape[1:]
    radial = layer_radius(radius_ref, layers, row_width)
    for place, square in enumerate(ALL_SQUARES):
        weight_ref[place] = jnp.maximum(radial - math.sqrt(square), 0.0)


def shift_sum(field, dim, distance):
    size = field.shape[dim]
    spot = spot_iota(field.shape, dim)
    ahead = jnp.where(spot < size - distance, pltpu.roll(field, size - distance, dim), 0.0)
    behind = jnp.where(spot >= distance, pltpu.roll(field, distance, dim), 0.0)
    return ahead + behind


def plane_sums(plane):
    beside = shift_sum(plane, 1, 1)
    further = shift_sum(plane, 1, 2)
    return {
        0: plane,
        1: beside + shift_sum(plane, 0, 1),
        2: shift_sum(beside, 0, 1),
        4: further + shift_sum(plane, 0, 2),
        5: shift_sum(further, 0, 1) + shift_sum(beside, 0, 2),
        8: shift_sum(further, 0, 2),
    }


def weigh(sums, weight_ref, square):
    result = None
    for inner in PLANE_SQUARES:
        term = weight_ref[ALL_SQUARES.index(inner + square)] * sums[inner]
        result = term if result is None else result + term
    return result


def forward_planes(plane, weight_ref):
    sums = plane_sums(plane)
    return [weigh(sums, weight_ref, square) for square in (0, 1, 4)]


def rows(x, layers, shift=0):
    return pl.ds(x * layers + shift, layers)


GAP = 8


def gapped(x, layers, shift=0):
    return pl.ds(GAP + x * (layers + GAP) + shift, layers)


def gap(x, layers):
    return pl.ds(x * (layers + GAP), GAP)


def pair_spot(x, own_planes):
    device = x // own_planes
    apart = device ^ lax.axis_index("space")
    return (apart ^ apart >> 1) & 1, device >> 1, x % own_planes


def edge_class(x, planes):
    return jnp.minimum(x, 2) + jnp.maximum(x - (planes - 3), 0)


def zero_edges(ref):
    planes = ref.shape[0]
    for place in (0, 1, planes - 2, planes - 1):
        ref[place] = jnp.zeros(ref.shape[1:], ref.dtype)


def prepare_kernel(
    radius_hbm,
    index_hbm,
    force_hbm,
    fixed_hbm,
    weight_ref,
    inverse_ref,
    free_ref,
    load_ref,
    spot_ref,
    radius_ref,
    index_ref,
    force_ref,
    fixed_ref,
    arrived,
):
    copies = [
        pltpu.make_async_copy(source, target, arrived.at[place])
        for place, (source, target) in enumerate(
            (
                (radius_hbm, radius_ref),
                (index_hbm, index_ref),
                (force_hbm, force_ref),
                (fixed_hbm, fixed_ref),
            )
        )
    ]
    for copy in copies:
        copy.start()
    for copy in copies:
        copy.wait()
    planes, layers, row_width = free_ref.shape
    load_place = lax.axis_index("space")
    shape = (layers, row_width)
    z = spot_iota(shape, 0)
    y = spot_iota(shape, 1)

    class_weights(radius_ref, weight_ref)
    ones = forward_planes(jnp.ones(shape, jnp.float32), weight_ref)
    for place, (lower, upper) in enumerate(((0, 2), (1, 2), (2, 2), (2, 1), (2, 0))):
        inverse_ref[place] = 1.0 / (
            ones[0] + min(lower, 1) * ones[1] + min(upper, 1) * ones[1]
            + (lower // 2) * ones[2] + (upper // 2) * ones[2]
        )

    def free_plane(x, carry):
        free_ref[x] = jnp.where(
            z == 0, 1.0 - fixed_ref[pl.ds(x, 1), :].astype(jnp.float32), 1.0
        )
        return carry

    lax.fori_loop(0, planes, free_plane, 0, unroll=16)

    own_index = index_ref[load_place]
    own_z = own_index // row_width % layers
    own_y = own_index % row_width
    hit = (z == own_z) & (y == own_y)
    for part in range(3):
        load_ref[part] = jnp.where(hit, force_ref[part, load_place], 0.0)
    spot_ref[0] = own_index // (layers * row_width)


def sweep_kernel(
    spot_ref,
    load_ref,
    weight_ref,
    inverse_ref,
    free_ref,
    density_ref,
    start_ref,
    disp_hbm,
    sens_ref,
    coef_ref,
    plane_ref,
    beside_ref,
    further_ref,
    near_ref,
    side_ref,
    far_ref,
    modulus_ref,
    across_ref,
    up_ref,
    right_ref,
    left_ref,
    rate_ref,
    first_ref,
    second_ref,
    disp_ref,
    stored,
):
    planes, layers, row_width = coef_ref.shape
    own_planes = density_ref.shape[2]
    load_cases = lax.axis_size("space")
    shape = (layers, row_width)
    z = spot_iota(shape, 0)
    y = spot_iota(shape, 1)
    zero = jnp.zeros(shape, jnp.float32)
    zero_gap = jnp.zeros((GAP, row_width), jnp.float32)

    for ref in (side_ref, far_ref):
        zero_edges(ref)
    for ref in (plane_ref, beside_ref, further_ref):
        ref[gap(planes, layers)] = zero_gap

    def spread_plane(x, carry):
        plane = density_ref[pair_spot(x, own_planes)]
        fields = (plane, shift_sum(plane, 1, 1), shift_sum(plane, 1, 2))
        for ref, field in zip((plane_ref, beside_ref, further_ref), fields):
            ref[gap(x, layers)] = zero_gap
            ref[gapped(x, layers)] = field
        return carry

    lax.fori_loop(0, planes, spread_plane, 0, unroll=16)

    def filter_plane(x, carry):
        def around(ref, distance):
            return ref[gapped(x, layers, distance)] + ref[gapped(x, layers, -distance)]

        beside = beside_ref[gapped(x, layers)]
        further = further_ref[gapped(x, layers)]
        sums = {
            0: plane_ref[gapped(x, layers)],
            1: beside + around(plane_ref, 1),
            2: around(beside_ref, 1),
            4: further + around(plane_ref, 2),
            5: around(further_ref, 1) + around(beside_ref, 2),
            8: around(further_ref, 2),
        }
        near_ref[x + 2] = weigh(sums, weight_ref, 0)
        side_ref[x + 2] = weigh(sums, weight_ref, 1)
        far_ref[x + 2] = weigh(sums, weight_ref, 4)
        return carry

    lax.fori_loop(0, planes, filter_plane, 0, unroll=16)

    def modulus_plane(x, carry):
        inverse = inverse_ref[edge_class(x, planes)]
        filtered = (
            near_ref[x + 2]
            + side_ref[x + 1]
            + side_ref[x + 3]
            + far_ref[x]
            + far_ref[x + 4]
        ) * inverse
        modulus = floor_modulus + (1.0 - floor_modulus) * (filtered * filtered * filtered)
        modulus_ref[rows(x, layers)] = modulus
        coef_ref[x] = 3.0 * (1.0 - floor_modulus) * (filtered * filtered) * inverse
        return carry

    lax.fori_loop(0, planes, modulus_plane, 0, unroll=16)

    modulus_ref[rows(planes, layers)] = zero
    across_ref[0] = zero
    across_ref[planes] = zero
    up_ref[rows(0, layers)] = zero
    for ref in (first_ref, second_ref):
        for part in range(3):
            ref[part, rows(0, layers)] = zero
            ref[part, rows(planes + 1, layers)] = zero

    def face_plane(x, carry):
        before = carry
        modulus = modulus_ref[rows(x, layers)]
        later = modulus_ref[rows(x + 1, layers)]
        ahead = jnp.where(x + 1 < planes, 0.5 * (modulus + later), 0.0)
        across_ref[x + 1] = ahead
        above = modulus_ref[rows(x, layers, 1)]
        up = jnp.where(z < layers - 1, 0.5 * (modulus + above), 0.0)
        right = jnp.where(
            y < row_width - 1, 0.5 * (modulus + pltpu.roll(modulus, row_width - 1, 1)), 0.0
        )
        left = pltpu.roll(right, 1, 1)
        up_ref[rows(x + 1, layers)] = up
        right_ref[x] = right
        left_ref[x] = left
        free = free_ref[x]
        sums = (before + ahead, up + pltpu.roll(up, 1, 0), left + right)
        every = sums[0] + sums[1] + sums[2]
        push = relax_factor * free
        diagonal = [every + part_sum for part_sum in sums]
        pair = diagonal[0] * diagonal[1]
        push = push / (pair * diagonal[2])
        side = push * diagonal[2]
        rate_ref[0, x] = side * diagonal[1]
        rate_ref[1, x] = side * diagonal[0]
        rate_ref[2, x] = push * pair
        for part in range(3):
            first_ref[part, rows(x + 1, layers)] = start_ref[part, x] * free
        return ahead

    lax.fori_loop(0, planes, face_plane, zero, unroll=16)

    own_x = spot_ref[0]

    def sweep(source, target, lead):
        def sweep_plane(x, carry):
            before, after = across_ref[x], across_ref[x + 1]
            up, down = up_ref[rows(x + 1, layers)], up_ref[rows(x + 1, layers, -1)]
            right, left = right_ref[x], left_ref[x]
            for part in range(3):
                here = source[part, rows(x + 1, layers)]
                pulls = [
                    before * source[part, rows(x, layers)]
                    + after * source[part, rows(x + 2, layers)],
                    up * source[part, rows(x + 1, layers, 1)]
                    + down * source[part, rows(x + 1, layers, -1)],
                    right * pltpu.roll(here, row_width - 1, 1) + left * pltpu.roll(here, 1, 1),
                ]
                pull = pulls[0] + pulls[1] + pulls[2] + pulls[part]
                target[part, rows(x + lead, layers)] = (
                    1.0 - relax_factor
                ) * here + rate_ref[part, x] * pull
            return carry

        lax.fori_loop(0, planes, sweep_plane, 0, unroll=16)
        for part in range(3):
            target[part, rows(own_x + lead, layers)] += rate_ref[part, own_x] * load_ref[part]

    stages = (first_ref, second_ref)
    for turn in range(SWEEPS - 1):
        sweep(stages[turn % 2], stages[(turn + 1) % 2], 1)
    sweep(stages[(SWEEPS - 1) % 2], disp_ref, 0)
    store = pltpu.make_async_copy(
        disp_ref.at[:, pl.ds(0, planes * layers)], disp_hbm, stored
    )
    store.start()

    def energy_plane(x, carry):
        later = jnp.minimum(x + 1, planes - 1)
        ahead, upward, right = zero, zero, zero
        for part in range(3):
            here = disp_ref[part, rows(x, layers)]
            step = disp_ref[part, rows(later, layers)] - here
            climb = disp_ref[part, rows(x, layers, 1)] - here
            slide = pltpu.roll(here, row_width - 1, 1) - here
            ahead = ahead + (2.0 if part == 0 else 1.0) * (step * step)
            upward = upward + (2.0 if part == 1 else 1.0) * (climb * climb)
            right = right + (2.0 if part == 2 else 1.0) * (slide * slide)
        upward = jnp.where(z < layers - 1, upward, 0.0)
        right = jnp.where(y < row_width - 1, right, 0.0)
        total = carry + ahead + upward + pltpu.roll(upward, 1, 0) + right + pltpu.roll(right, 1, 1)
        sens_ref[pair_spot(x, own_planes)] = (0.5 / load_cases) * total
        return ahead

    lax.fori_loop(0, planes, energy_plane, zero, unroll=16)
    store.wait()


def design_kernel(
    weight_ref,
    sens_ref,
    coef_ref,
    density_ref,
    new_ref,
    plane_ref,
    beside_ref,
    further_ref,
    level_ref,
    near_ref,
    far_ref,
    pull_ref,
    low_ref,
    high_ref,
):
    planes, layers, row_width = coef_ref.shape
    own_planes = density_ref.shape[2]
    place = lax.axis_index("space")
    shape = (layers, row_width)
    zero = jnp.zeros(shape, jnp.float32)
    zero_gap = jnp.zeros((GAP, row_width), jnp.float32)
    for ref in (plane_ref, beside_ref, further_ref):
        zero_edges(ref)
    for ref in (near_ref, far_ref):
        ref[gap(planes, layers)] = zero_gap

    def spread_plane(x, carry):
        plane = sens_ref[pair_spot(x, own_planes)] * coef_ref[x]
        plane_ref[x + 2] = plane
        beside_ref[x + 2] = shift_sum(plane, 1, 1)
        further_ref[x + 2] = shift_sum(plane, 1, 2)
        return carry

    lax.fori_loop(0, planes, spread_plane, 0, unroll=16)

    def filter_plane(x, carry):
        def around(ref, distance):
            return ref[x + 2 + distance] + ref[x + 2 - distance]

        sums = {
            0: plane_ref[x + 2],
            1: beside_ref[x + 2] + around(plane_ref, 1),
            2: around(beside_ref, 1),
            4: further_ref[x + 2] + around(plane_ref, 2),
            5: around(further_ref, 1) + around(beside_ref, 2),
            8: around(further_ref, 2),
        }
        level_ref[x] = weigh(sums, weight_ref, 0)
        for ref, square in ((near_ref, 1), (far_ref, 4)):
            ref[gap(x, layers)] = zero_gap
            ref[gapped(x, layers)] = weigh(sums, weight_ref, square)
        return carry

    lax.fori_loop(0, planes, filter_plane, 0, unroll=16)

    def root_plane(x, carry):
        root = jnp.sqrt(
            level_ref[x]
            + near_ref[gapped(x, layers, 1)]
            + near_ref[gapped(x, layers, -1)]
            + far_ref[gapped(x, layers, 2)]
            + far_ref[gapped(x, layers, -2)]
        )
        density = density_ref[pair_spot(x, own_planes)]
        pull_ref[x] = density * root
        low_ref[x] = jnp.maximum(density - move_limit, density_floor)
        high_ref[x] = jnp.minimum(density + move_limit, 1.0)
        return carry

    lax.fori_loop(0, planes, root_plane, 0, unroll=16)

    target = volume_share * planes * layers * row_width

    def trial(x, factor):
        return jnp.minimum(jnp.maximum(pull_ref[x] * factor, low_ref[x]), high_ref[x])

    def halve(step, state):
        lower, span = state
        half = span * 0.5
        middle = lower + half
        factor = jnp.exp(-0.5 * middle)
        total = lax.fori_loop(
            0, planes, lambda x, acc: acc + trial(x, factor), zero, unroll=16
        )
        volume = jnp.sum(jnp.sum(total, axis=0, keepdims=True), axis=1, keepdims=True)
        return jnp.where(volume > target, middle, lower), half

    start = (jnp.full((1, 1), log_lower, jnp.float32), jnp.full((1, 1), log_span, jnp.float32))
    lower, span = lax.fori_loop(0, SEARCH, halve, start)
    factor = jnp.exp(-0.5 * (lower + 0.5 * span))
    for own in range(own_planes):
        new_ref[own] = trial(place * own_planes + own, factor)


def in_vmem():
    return pl.BlockSpec(memory_space=pltpu.VMEM)


def in_smem():
    return pl.BlockSpec(memory_space=pltpu.SMEM)


KERNEL_VMEM = 24 * 2**20


def floats(*shape):
    return jax.ShapeDtypeStruct(shape, jnp.float32)


def prepare_call(radius, load_index, load_force, fixed):
    planes, row_width = fixed.shape
    layers = radius.shape[0]
    return pl.pallas_call(
        prepare_kernel,
        out_shape=[
            floats(len(ALL_SQUARES), layers, row_width),
            floats(2 * window_reach + 1, layers, row_width),
            floats(planes, layers, row_width),
            floats(3, layers, row_width),
            jax.ShapeDtypeStruct((1,), jnp.int32),
        ],
        in_specs=[pl.BlockSpec(memory_space=pltpu.HBM)] * 4,
        out_specs=[in_vmem()] * 4 + [in_smem()],
        scratch_shapes=[
            pltpu.SMEM(radius.shape, radius.dtype),
            pltpu.SMEM(load_index.shape, load_index.dtype),
            pltpu.SMEM(load_force.shape, load_force.dtype),
            pltpu.VMEM(fixed.shape, fixed.dtype),
            pltpu.SemaphoreType.DMA((4,)),
        ],
        compiler_params=pltpu.CompilerParams(vmem_limit_bytes=KERNEL_VMEM),
        cost_estimate=pl.CostEstimate(
            flops=40 * planes * layers * row_width,
            bytes_accessed=8 * planes * layers * row_width,
            transcendentals=0,
        ),
        name="prepare",
    )(
        *(
            pltpu.with_memory_space_constraint(array, pltpu.HBM)
            for array in (radius, load_index, load_force, fixed)
        )
    )


def sweep_call(spot, load, weights, inverses, free, density, displacement):
    cores, chips, own_planes, layers, row_width = density.shape
    planes = cores * chips * own_planes

    def scratch(*lead):
        return pltpu.VMEM(lead + (row_width,), jnp.float32)

    return pl.pallas_call(
        sweep_kernel,
        out_shape=[
            floats(3, planes * layers, row_width),
            floats(*density.shape),
            floats(planes, layers, row_width),
        ],
        in_specs=[in_smem()] + [in_vmem()] * 6,
        out_specs=[pl.BlockSpec(memory_space=pltpu.HBM), in_vmem(), in_vmem()],
        scratch_shapes=[
            scratch(planes * (layers + GAP) + GAP),
            scratch(planes * (layers + GAP) + GAP),
            scratch(planes * (layers + GAP) + GAP),
            scratch(planes + 4, layers),
            scratch(planes + 4, layers),
            scratch(planes + 4, layers),
            scratch((planes + 1) * layers),
            scratch(planes + 1, layers),
            scratch((planes + 1) * layers),
            scratch(planes, layers),
            scratch(planes, layers),
            scratch(3, planes, layers),
            scratch(3, (planes + 2) * layers),
            scratch(3, (planes + 2) * layers),
            scratch(3, (planes + 1) * layers),
            pltpu.SemaphoreType.DMA(()),
        ],
        compiler_params=pltpu.CompilerParams(vmem_limit_bytes=KERNEL_VMEM),
        name="sweeps",
    )(spot, load, weights, inverses, free, density, displacement)


def design_call(weights, sens, coef, density):
    cores, chips, own_planes, layers, row_width = density.shape
    planes = cores * chips * own_planes

    def scratch(*lead):
        return pltpu.VMEM(lead + (row_width,), jnp.float32)

    return pl.pallas_call(
        design_kernel,
        out_shape=floats(own_planes, layers, row_width),
        in_specs=[in_vmem()] * 4,
        out_specs=in_vmem(),
        scratch_shapes=[
            scratch(planes + 4, layers),
            scratch(planes + 4, layers),
            scratch(planes + 4, layers),
            scratch(planes, layers),
            scratch(planes * (layers + GAP) + GAP),
            scratch(planes * (layers + GAP) + GAP),
            scratch(planes, layers),
            scratch(planes, layers),
            scratch(planes, layers),
        ],
        compiler_params=pltpu.CompilerParams(vmem_limit_bytes=KERNEL_VMEM),
        name="design",
    )(weights, sens, coef, density)


def other_core(block):
    devices = lax.axis_size("space")
    return lax.ppermute(block, "space", [(i, i ^ 1) for i in range(devices)])


def chip_groups():
    chips = lax.axis_size("space") // 2
    return [[2 * chip + (chip ^ group) % 2 for chip in range(chips)] for group in range(2)]


def between_chips(pieces):
    return lax.all_to_all(pieces, "space", 0, 0, axis_index_groups=chip_groups())


def chip_gathered(block):
    chips = lax.axis_size("space") // 2
    return between_chips(jnp.broadcast_to(block[None], (chips,) + block.shape))


def with_other_core(blocks):
    return jnp.stack([blocks, other_core(blocks)])


def scattered_sum(pieces):
    return jnp.sum(between_chips(pieces[0] + other_core(pieces[1])), axis=0)


def one_slab(density, displacement, fixed, load_index, load_force, radius):
    same_group, small = lax.optimization_barrier(
        (chip_gathered(density), (radius, load_index, load_force.T, fixed))
    )
    whole = with_other_core(same_group)
    weights, inverses, free, load, spot = prepare_call(*small)
    new_displacement, sens, coef = sweep_call(
        spot, load, weights, inverses, free, whole, displacement[0]
    )
    sens = with_other_core(chip_gathered(scattered_sum(sens)))
    new_density = design_call(weights, sens, coef, whole)
    return new_density, new_displacement.reshape(displacement.shape)


def from_behind(block, axis, distance):
    devices = range(lax.axis_size(axis))
    route = [(i - distance, i) for i in devices if i - distance in devices]
    return lax.ppermute(block, axis, route)


def extended(x, sides, width):
    for axis, dim in sides:
        size, length = (lax.axis_size(axis), x.shape[dim])
        up = [(i, (i + 1) % size) for i in range(size - 1)]
        down = [(j, i) for i, j in up]
        last = lax.slice_in_dim(x, length - width, length, axis=dim)
        first = lax.slice_in_dim(x, 0, width, axis=dim)
        before = lax.ppermute(last, axis, up)
        after = lax.ppermute(first, axis, down)
        x = jnp.concatenate([before, x, after], axis=dim)
    return x


def from_partner(x, axis, bit):
    return lax.ppermute(x, axis, [(i, i ^ 1 << bit) for i in range(lax.axis_size(axis))])


def window_offsets():
    offsets_list = []
    for across in range(-window_reach, window_reach + 1):
        for upward in range(-window_reach, window_reach + 1):
            for sideways in range(-window_reach, window_reach + 1):
                length = math.sqrt(across * across + upward * upward + sideways * sideways)
                offsets_list.append((across, upward, sideways, length))
    return offsets_list


def layer_weights(radius):
    radial = radius.astype(jnp.float32)
    return jnp.stack(
        [jnp.maximum(radial - length, 0.0) for across, upward, sideways, length in window_offsets()]
    )


def pad_axis(grid_field, along_axis, before, after_cells):
    widths = [(0, 0)] * grid_field.ndim
    widths[along_axis] = (before, after_cells)
    return jnp.pad(grid_field, widths)


def pad_sides(grid_field):
    return jnp.pad(grid_field, ((0, 0), (window_reach, window_reach), (window_reach, window_reach)))


def filter_forward(padded, weights):
    out_rows = padded.shape[0] - 2 * window_reach
    layers = padded.shape[1] - 2 * window_reach
    row_width = padded.shape[2] - 2 * window_reach
    result = jnp.zeros((out_rows, layers, row_width), jnp.float32)
    for offset_index, (across, upward, sideways, length) in enumerate(window_offsets()):
        shifted = padded[
            window_reach + across : window_reach + across + out_rows,
            window_reach + upward : window_reach + upward + layers,
            window_reach + sideways : window_reach + sideways + row_width,
        ]
        result = result + weights[offset_index][None, :, None] * shifted
    return result


def filter_backward(padded, padded_weights):
    out_rows = padded.shape[0] - 2 * window_reach
    layers = padded.shape[1] - 2 * window_reach
    row_width = padded.shape[2] - 2 * window_reach
    result = jnp.zeros((out_rows, layers, row_width), jnp.float32)
    for offset_index, (across, upward, sideways, length) in enumerate(window_offsets()):
        shifted = padded[
            window_reach - across : window_reach - across + out_rows,
            window_reach - upward : window_reach - upward + layers,
            window_reach - sideways : window_reach - sideways + row_width,
        ]
        layer_part = padded_weights[
            offset_index, window_reach - upward : window_reach - upward + layers
        ]
        result = result + layer_part[None, :, None] * shifted
    return result


def stiff_factors(direction):
    return jnp.array(
        [2.0 if component == direction else 1.0 for component in range(3)], jnp.float32
    ).reshape(3, 1, 1, 1)


def relax_slab(padded, displace, face_x, face_z, face_y, force_field, free_cells, diagonal):
    flux_x = stiff_factors(0) * face_x * jnp.diff(padded, axis=1)
    stencil_image = flux_x[:, :-1] - flux_x[:, 1:]
    flux_z = stiff_factors(1) * face_z * jnp.diff(displace, axis=2)
    stencil_image = stencil_image + pad_axis(flux_z, 2, 1, 0) - pad_axis(flux_z, 2, 0, 1)
    flux_y = stiff_factors(2) * face_y * jnp.diff(displace, axis=3)
    stencil_image = stencil_image + pad_axis(flux_y, 3, 1, 0) - pad_axis(flux_y, 3, 0, 1)
    return free_cells * (displace + relax_factor * (force_field - stencil_image) / diagonal)


def slab_energy(grid_field, along_axis, direction, load_cases):
    change = jnp.diff(grid_field, axis=along_axis)
    return jnp.sum(stiff_factors(direction) * change * change, axis=0) / load_cases


def neighbour_planes(displace, load_cases, axis_devices):
    if axis_devices > load_cases:
        below = from_behind(displace[:, -1:], "space", load_cases)
        above = from_behind(displace[:, :1], "space", -load_cases)
    else:
        below = jnp.zeros_like(displace[:, :1])
        above = jnp.zeros_like(displace[:, :1])
    return jnp.concatenate([below, displace, above], axis=1)


def many_slabs(density, displacement, fixed, load_index, load_force, radius):
    slab_rows, layers, row_width = density.shape
    load_cases = load_index.shape[0]
    level_count = load_cases.bit_length() - 1
    axis_devices = lax.axis_size("space")
    axis_place = lax.axis_index("space")
    slab_planes = slab_rows * load_cases
    slab_place = axis_place // load_cases
    load_place = axis_place % load_cases
    total_rows = slab_rows * axis_devices
    weights = layer_weights(radius)
    padded_weights = pad_axis(weights, 1, window_reach, window_reach)
    global_rows = (
        jnp.arange(slab_rows + 2 * window_reach, dtype=jnp.int32)
        + axis_place * slab_rows
        - window_reach
    )
    deep_inside = ((global_rows >= 0) & (global_rows < total_rows)).astype(jnp.float32)
    inside_field = deep_inside[:, None, None] * pad_sides(
        jnp.ones((slab_rows + 2 * window_reach, layers, row_width), jnp.float32)
    )
    total_weight = filter_forward(inside_field, weights)
    slab_start = slab_place * slab_planes
    margin_rows = jnp.arange(slab_planes + 2, dtype=jnp.int32) + slab_start - 1
    margin_inside = ((margin_rows >= 0) & (margin_rows < total_rows)).astype(jnp.float32)
    face_valid = margin_inside[1:] * margin_inside[:-1]
    fixed_slab = lax.dynamic_slice_in_dim(fixed, slab_start, slab_planes, 0).astype(jnp.float32)
    bottom_layer = (jnp.arange(layers, dtype=jnp.int32) == 0).astype(jnp.float32)
    free_cells = 1.0 - bottom_layer[None, :, None] * fixed_slab[:, None, :]
    slab_cells = slab_planes * layers * row_width
    cell_index = jnp.arange(slab_cells, dtype=jnp.int32) + slab_place * slab_cells
    load_hot = jnp.arange(load_cases, dtype=jnp.int32) == load_place
    own_index = jnp.sum(jnp.where(load_hot, load_index, 0))
    own_force = jnp.sum(load_hot.astype(jnp.float32)[:, None] * load_force, axis=0)
    load_hits = (cell_index == own_index).astype(jnp.float32)
    force_field = (own_force[:, None] * load_hits[None, :]).reshape(
        3, slab_planes, layers, row_width
    )
    displace = displacement[0] * free_cells
    target = volume_share * total_rows * layers * row_width
    padded = neighbour_planes(displace, load_cases, axis_devices)
    halo_density = extended(density, (("space", 0),), window_reach)
    filtered = filter_forward(pad_sides(halo_density), weights) / total_weight
    whole_field = lax.all_gather(filtered, "space", axis=0, tiled=True)
    margin = lax.dynamic_slice_in_dim(
        pad_axis(whole_field, 0, 1, 1), slab_start, slab_planes + 2, 0
    )
    moduli = floor_modulus + (1.0 - floor_modulus) * margin**3
    face_x = 0.5 * (moduli[1:] + moduli[:-1]) * face_valid[:, None, None]
    inner_moduli = moduli[1:-1]
    face_z = 0.5 * (inner_moduli[:, 1:] + inner_moduli[:, :-1])
    face_y = 0.5 * (inner_moduli[:, :, 1:] + inner_moduli[:, :, :-1])
    sum_x = face_x[:-1] + face_x[1:]
    sum_z = pad_axis(face_z, 1, 1, 0) + pad_axis(face_z, 1, 0, 1)
    sum_y = pad_axis(face_y, 2, 1, 0) + pad_axis(face_y, 2, 0, 1)
    diagonal = stiff_factors(0) * sum_x + stiff_factors(1) * sum_z + stiff_factors(2) * sum_y
    for sweep_index in range(SWEEPS):
        displace = relax_slab(
            padded, displace, face_x, face_z, face_y, force_field, free_cells, diagonal
        )
        padded = neighbour_planes(displace, load_cases, axis_devices)
    energy_x = slab_energy(padded, 1, 0, load_cases) * face_valid[:, None, None]
    energy_z = slab_energy(displace, 2, 1, load_cases)
    energy_y = slab_energy(displace, 3, 2, load_cases)
    sens_term = 0.5 * (
        energy_x[:-1]
        + energy_x[1:]
        + pad_axis(energy_z, 1, 1, 0)
        + pad_axis(energy_z, 1, 0, 1)
        + pad_axis(energy_y, 2, 1, 0)
        + pad_axis(energy_y, 2, 0, 1)
    )
    sensitive = sens_term
    for level in reversed(range(level_count)):
        half_rows = sensitive.shape[0] // 2
        upper_side = load_place // 2**level % 2 == 1
        outgoing = jnp.where(upper_side, sensitive[:half_rows], sensitive[half_rows:])
        keeping = jnp.where(upper_side, sensitive[half_rows:], sensitive[:half_rows])
        sensitive = keeping + from_partner(outgoing, "space", level)
    weighted_share = 3.0 * (1.0 - floor_modulus) * filtered**2 * sensitive / total_weight
    halo_share = extended(weighted_share, (("space", 0),), window_reach)
    root_term = jnp.sqrt(filter_backward(pad_sides(halo_share), padded_weights))
    lowest = jnp.maximum(density - move_limit, density_floor)
    highest = jnp.minimum(density + move_limit, 1.0)
    design_now = density

    def trial_design(log_level):
        return jnp.clip(design_now * root_term * jnp.exp(-0.5 * log_level), lowest, highest)

    start_state = (jnp.asarray(log_lower, jnp.float32), jnp.asarray(log_span, jnp.float32))

    def halve(search_step, search_state):
        lower_end, span_width = search_state
        half_span = span_width * 0.5
        middle = lower_end + half_span
        volume_total = lax.psum(jnp.sum(trial_design(middle)), "space")
        return (jnp.where(volume_total > target, middle, lower_end), half_span)

    lower_end, span_width = lax.fori_loop(0, SEARCH, halve, start_state)
    density = trial_design(lower_end + 0.5 * span_width)
    new_displacement = displace[None]
    return (density, new_displacement)


def solution(mesh):
    in_specs = (
        P("space", "parts", None),
        P("space", None, None, "parts", None),
        P(None, "parts"),
        P("parts"),
        P("parts", None),
        P("parts"),
    )
    out_specs = (P("space", "parts", None), P("space", None, None, "parts", None))

    def local(density, displacement, fixed, load_index, load_force, radius):
        alone = lax.axis_size("space") == load_index.shape[0]
        run = one_slab if alone else many_slabs
        return run(density, displacement, fixed, load_index, load_force, radius)

    return jax.shard_map(local, mesh=mesh, in_specs=in_specs, out_specs=out_specs, check_vma=False)
```

```python
import math

import jax
import jax.numpy as jnp
from jax import lax
from jax.experimental import pallas as pl
from jax.experimental.pallas import tpu as pltpu
from jax.sharding import PartitionSpec as P

SWEEPS = 3
SEARCH = 12


floor_modulus = 0.05
relax_factor = 0.6
move_limit = 0.2
density_floor = 0.01
volume_share = 0.5
log_lower = -16.0
log_span = 32.0
window_reach = 2

PLANE_SQUARES = (0, 1, 2, 4, 5, 8)
ALL_SQUARES = (0, 1, 2, 3, 4, 5, 6, 8, 9, 12)


def spot_iota(shape, dim):
    return lax.broadcasted_iota(jnp.int32, shape, dim)


def layer_radius(radius_ref, layers, row_width):
    z = spot_iota((layers, row_width), 0)
    result = jnp.zeros((layers, row_width), jnp.int32)
    for layer in range(layers):
        result = jnp.where(z == layer, radius_ref[layer], result)
    return result.astype(jnp.float32)


def class_weights(radius_ref, weight_ref):
    layers, row_width = weight_ref.shape[1:]
    radial = layer_radius(radius_ref, layers, row_width)
    for place, square in enumerate(ALL_SQUARES):
        weight_ref[place] = jnp.maximum(radial - math.sqrt(square), 0.0)


def shift_sum(field, dim, distance):
    size = field.shape[dim]
    spot = spot_iota(field.shape, dim)
    ahead = jnp.where(spot < size - distance, pltpu.roll(field, size - distance, dim), 0.0)
    behind = jnp.where(spot >= distance, pltpu.roll(field, distance, dim), 0.0)
    return ahead + behind


def plane_sums(plane):
    beside = shift_sum(plane, 1, 1)
    further = shift_sum(plane, 1, 2)
    return {
        0: plane,
        1: beside + shift_sum(plane, 0, 1),
        2: shift_sum(beside, 0, 1),
        4: further + shift_sum(plane, 0, 2),
        5: shift_sum(further, 0, 1) + shift_sum(beside, 0, 2),
        8: shift_sum(further, 0, 2),
    }


def weigh(sums, weight_ref, square):
    result = None
    for inner in PLANE_SQUARES:
        term = weight_ref[ALL_SQUARES.index(inner + square)] * sums[inner]
        result = term if result is None else result + term
    return result


def forward_planes(plane, weight_ref):
    sums = plane_sums(plane)
    return [weigh(sums, weight_ref, square) for square in (0, 1, 4)]


def rows(x, layers, shift=0):
    return pl.ds(x * layers + shift, layers)


GAP = 8


def gapped(x, layers, shift=0):
    return pl.ds(GAP + x * (layers + GAP) + shift, layers)


def gap(x, layers):
    return pl.ds(x * (layers + GAP), GAP)


def pair_spot(x, own_planes):
    device = x // own_planes
    apart = device ^ lax.axis_index("space")
    return (apart ^ apart >> 1) & 1, device >> 1, x % own_planes


def edge_class(x, planes):
    return jnp.minimum(x, 2) + jnp.maximum(x - (planes - 3), 0)


def zero_edges(ref):
    planes = ref.shape[0]
    for place in (0, 1, planes - 2, planes - 1):
        ref[place] = jnp.zeros(ref.shape[1:], ref.dtype)


def prepare_kernel(
    radius_hbm,
    index_hbm,
    force_hbm,
    fixed_hbm,
    weight_ref,
    inverse_ref,
    free_ref,
    load_ref,
    spot_ref,
    radius_ref,
    index_ref,
    force_ref,
    fixed_ref,
    arrived,
):
    copies = [
        pltpu.make_async_copy(source, target, arrived.at[place])
        for place, (source, target) in enumerate(
            (
                (radius_hbm, radius_ref),
                (index_hbm, index_ref),
                (force_hbm, force_ref),
                (fixed_hbm, fixed_ref),
            )
        )
    ]
    for copy in copies:
        copy.start()
    for copy in copies:
        copy.wait()
    planes, layers, row_width = free_ref.shape
    load_place = lax.axis_index("space")
    shape = (layers, row_width)
    z = spot_iota(shape, 0)
    y = spot_iota(shape, 1)

    class_weights(radius_ref, weight_ref)
    ones = forward_planes(jnp.ones(shape, jnp.float32), weight_ref)
    for place, (lower, upper) in enumerate(((0, 2), (1, 2), (2, 2), (2, 1), (2, 0))):
        inverse_ref[place] = 1.0 / (
            ones[0] + min(lower, 1) * ones[1] + min(upper, 1) * ones[1]
            + (lower // 2) * ones[2] + (upper // 2) * ones[2]
        )

    def free_plane(x, carry):
        free_ref[x] = jnp.where(
            z == 0, 1.0 - fixed_ref[pl.ds(x, 1), :].astype(jnp.float32), 1.0
        )
        return carry

    lax.fori_loop(0, planes, free_plane, 0, unroll=16)

    own_index = index_ref[load_place]
    own_z = own_index // row_width % layers
    own_y = own_index % row_width
    hit = (z == own_z) & (y == own_y)
    for part in range(3):
        load_ref[part] = jnp.where(hit, force_ref[part, load_place], 0.0)
    spot_ref[0] = own_index // (layers * row_width)


def sweep_kernel(
    spot_ref,
    load_ref,
    weight_ref,
    inverse_ref,
    free_ref,
    density_ref,
    start_ref,
    disp_ref,
    coef_ref,
    plane_ref,
    beside_ref,
    further_ref,
    near_ref,
    side_ref,
    far_ref,
    modulus_ref,
    across_ref,
    up_ref,
    right_ref,
    left_ref,
    rate_ref,
    first_ref,
    second_ref,
):
    planes, layers, row_width = coef_ref.shape
    own_planes = density_ref.shape[2]
    shape = (layers, row_width)
    z = spot_iota(shape, 0)
    y = spot_iota(shape, 1)
    zero = jnp.zeros(shape, jnp.float32)
    zero_gap = jnp.zeros((GAP, row_width), jnp.float32)

    for ref in (side_ref, far_ref):
        zero_edges(ref)
    for ref in (plane_ref, beside_ref, further_ref):
        ref[gap(planes, layers)] = zero_gap

    def spread_plane(x, carry):
        plane = density_ref[pair_spot(x, own_planes)]
        fields = (plane, shift_sum(plane, 1, 1), shift_sum(plane, 1, 2))
        for ref, field in zip((plane_ref, beside_ref, further_ref), fields):
            ref[gap(x, layers)] = zero_gap
            ref[gapped(x, layers)] = field
        return carry

    lax.fori_loop(0, planes, spread_plane, 0, unroll=16)

    def filter_plane(x, carry):
        def around(ref, distance):
            return ref[gapped(x, layers, distance)] + ref[gapped(x, layers, -distance)]

        beside = beside_ref[gapped(x, layers)]
        further = further_ref[gapped(x, layers)]
        sums = {
            0: plane_ref[gapped(x, layers)],
            1: beside + around(plane_ref, 1),
            2: around(beside_ref, 1),
            4: further + around(plane_ref, 2),
            5: around(further_ref, 1) + around(beside_ref, 2),
            8: around(further_ref, 2),
        }
        near_ref[x + 2] = weigh(sums, weight_ref, 0)
        side_ref[x + 2] = weigh(sums, weight_ref, 1)
        far_ref[x + 2] = weigh(sums, weight_ref, 4)
        return carry

    lax.fori_loop(0, planes, filter_plane, 0, unroll=16)

    def modulus_plane(x, carry):
        inverse = inverse_ref[edge_class(x, planes)]
        filtered = (
            near_ref[x + 2]
            + side_ref[x + 1]
            + side_ref[x + 3]
            + far_ref[x]
            + far_ref[x + 4]
        ) * inverse
        modulus = floor_modulus + (1.0 - floor_modulus) * (filtered * filtered * filtered)
        modulus_ref[rows(x, layers)] = modulus
        coef_ref[x] = 3.0 * (1.0 - floor_modulus) * (filtered * filtered) * inverse
        return carry

    lax.fori_loop(0, planes, modulus_plane, 0, unroll=16)

    modulus_ref[rows(planes, layers)] = zero
    across_ref[0] = zero
    across_ref[planes] = zero
    up_ref[rows(0, layers)] = zero
    for ref in (first_ref, second_ref, disp_ref):
        for part in range(3):
            ref[part, rows(0, layers)] = zero
            ref[part, rows(planes + 1, layers)] = zero

    def face_plane(x, carry):
        before = carry
        modulus = modulus_ref[rows(x, layers)]
        later = modulus_ref[rows(x + 1, layers)]
        ahead = jnp.where(x + 1 < planes, 0.5 * (modulus + later), 0.0)
        across_ref[x + 1] = ahead
        above = modulus_ref[rows(x, layers, 1)]
        up = jnp.where(z < layers - 1, 0.5 * (modulus + above), 0.0)
        right = jnp.where(
            y < row_width - 1, 0.5 * (modulus + pltpu.roll(modulus, row_width - 1, 1)), 0.0
        )
        left = pltpu.roll(right, 1, 1)
        up_ref[rows(x + 1, layers)] = up
        right_ref[x] = right
        left_ref[x] = left
        free = free_ref[x]
        sums = (before + ahead, up + pltpu.roll(up, 1, 0), left + right)
        every = sums[0] + sums[1] + sums[2]
        push = relax_factor * free
        diagonal = [every + part_sum for part_sum in sums]
        pair = diagonal[0] * diagonal[1]
        push = push / (pair * diagonal[2])
        side = push * diagonal[2]
        rate_ref[0, x] = side * diagonal[1]
        rate_ref[1, x] = side * diagonal[0]
        rate_ref[2, x] = push * pair
        for part in range(3):
            first_ref[part, rows(x + 1, layers)] = start_ref[part, x] * free
        return ahead

    lax.fori_loop(0, planes, face_plane, zero, unroll=16)

    own_x = spot_ref[0]

    def sweep(source, target):
        def sweep_plane(x, carry):
            before, after = across_ref[x], across_ref[x + 1]
            up, down = up_ref[rows(x + 1, layers)], up_ref[rows(x + 1, layers, -1)]
            right, left = right_ref[x], left_ref[x]
            for part in range(3):
                here = source[part, rows(x + 1, layers)]
                pulls = [
                    before * source[part, rows(x, layers)]
                    + after * source[part, rows(x + 2, layers)],
                    up * source[part, rows(x + 1, layers, 1)]
                    + down * source[part, rows(x + 1, layers, -1)],
                    right * pltpu.roll(here, row_width - 1, 1) + left * pltpu.roll(here, 1, 1),
                ]
                pull = pulls[0] + pulls[1] + pulls[2] + pulls[part]
                target[part, rows(x + 1, layers)] = (
                    1.0 - relax_factor
                ) * here + rate_ref[part, x] * pull
            return carry

        lax.fori_loop(0, planes, sweep_plane, 0, unroll=16)
        for part in range(3):
            target[part, rows(own_x + 1, layers)] += rate_ref[part, own_x] * load_ref[part]

    stages = (first_ref, second_ref)
    for turn in range(SWEEPS - 1):
        sweep(stages[turn % 2], stages[(turn + 1) % 2])
    sweep(stages[(SWEEPS - 1) % 2], disp_ref)


def energy_planes(group, disp_ref, sens_ref):
    chips, own_planes, layers, row_width = sens_ref.shape
    planes = disp_ref.shape[1] // layers - 2
    load_cases = lax.axis_size("space")
    shape = (layers, row_width)
    z = spot_iota(shape, 0)
    y = spot_iota(shape, 1)
    zero = jnp.zeros(shape, jnp.float32)
    mine = lax.axis_index("space")
    core = mine ^ mine >> 1 ^ group

    def between(x):
        result = zero
        for part in range(3):
            step = disp_ref[part, rows(x + 1, layers)] - disp_ref[part, rows(x, layers)]
            result = result + (2.0 if part == 0 else 1.0) * (step * step)
        return jnp.where((x > 0) & (x < planes), result, 0.0)

    def inside(x):
        upward, right = zero, zero
        for part in range(3):
            here = disp_ref[part, rows(x + 1, layers)]
            climb = disp_ref[part, rows(x + 1, layers, 1)] - here
            slide = pltpu.roll(here, row_width - 1, 1) - here
            upward = upward + (2.0 if part == 1 else 1.0) * (climb * climb)
            right = right + (2.0 if part == 2 else 1.0) * (slide * slide)
        upward = jnp.where(z < layers - 1, upward, 0.0)
        right = jnp.where(y < row_width - 1, right, 0.0)
        return upward + pltpu.roll(upward, 1, 0) + right + pltpu.roll(right, 1, 1)

    for chip in range(chips):
        first = own_planes * (2 * chip + ((core ^ chip) & 1))
        before = between(first)
        for own in range(own_planes):
            after = between(first + own + 1)
            sens_ref[chip, own] = (0.5 / load_cases) * (before + after + inside(first + own))
            before = after


def sent_energy_kernel(disp_ref, sens_ref):
    energy_planes(1, disp_ref, sens_ref)


def kept_energy_kernel(disp_ref, disp_hbm, sens_ref, stored):
    layers = sens_ref.shape[2]
    inner = pl.ds(layers, disp_ref.shape[1] - 2 * layers)
    store = pltpu.make_async_copy(disp_ref.at[:, inner], disp_hbm, stored)
    store.start()
    energy_planes(0, disp_ref, sens_ref)
    store.wait()


def design_kernel(
    weight_ref,
    sens_ref,
    coef_ref,
    density_ref,
    new_ref,
    plane_ref,
    beside_ref,
    further_ref,
    level_ref,
    near_ref,
    far_ref,
    pull_ref,
    low_ref,
    high_ref,
):
    planes, layers, row_width = coef_ref.shape
    own_planes = density_ref.shape[2]
    place = lax.axis_index("space")
    shape = (layers, row_width)
    zero = jnp.zeros(shape, jnp.float32)
    zero_gap = jnp.zeros((GAP, row_width), jnp.float32)
    for ref in (plane_ref, beside_ref, further_ref):
        zero_edges(ref)
    for ref in (near_ref, far_ref):
        ref[gap(planes, layers)] = zero_gap

    def spread_plane(x, carry):
        plane = sens_ref[pair_spot(x, own_planes)] * coef_ref[x]
        plane_ref[x + 2] = plane
        beside_ref[x + 2] = shift_sum(plane, 1, 1)
        further_ref[x + 2] = shift_sum(plane, 1, 2)
        return carry

    lax.fori_loop(0, planes, spread_plane, 0, unroll=16)

    def filter_plane(x, carry):
        def around(ref, distance):
            return ref[x + 2 + distance] + ref[x + 2 - distance]

        sums = {
            0: plane_ref[x + 2],
            1: beside_ref[x + 2] + around(plane_ref, 1),
            2: around(beside_ref, 1),
            4: further_ref[x + 2] + around(plane_ref, 2),
            5: around(further_ref, 1) + around(beside_ref, 2),
            8: around(further_ref, 2),
        }
        level_ref[x] = weigh(sums, weight_ref, 0)
        for ref, square in ((near_ref, 1), (far_ref, 4)):
            ref[gap(x, layers)] = zero_gap
            ref[gapped(x, layers)] = weigh(sums, weight_ref, square)
        return carry

    lax.fori_loop(0, planes, filter_plane, 0, unroll=16)

    def root_plane(x, carry):
        root = jnp.sqrt(
            level_ref[x]
            + near_ref[gapped(x, layers, 1)]
            + near_ref[gapped(x, layers, -1)]
            + far_ref[gapped(x, layers, 2)]
            + far_ref[gapped(x, layers, -2)]
        )
        density = density_ref[pair_spot(x, own_planes)]
        pull_ref[x] = density * root
        low_ref[x] = jnp.maximum(density - move_limit, density_floor)
        high_ref[x] = jnp.minimum(density + move_limit, 1.0)
        return carry

    lax.fori_loop(0, planes, root_plane, 0, unroll=16)

    target = volume_share * planes * layers * row_width

    def trial(x, factor):
        return jnp.minimum(jnp.maximum(pull_ref[x] * factor, low_ref[x]), high_ref[x])

    def halve(step, state):
        lower, span = state
        half = span * 0.5
        middle = lower + half
        factor = jnp.exp(-0.5 * middle)
        total = lax.fori_loop(
            0, planes, lambda x, acc: acc + trial(x, factor), zero, unroll=16
        )
        volume = jnp.sum(jnp.sum(total, axis=0, keepdims=True), axis=1, keepdims=True)
        return jnp.where(volume > target, middle, lower), half

    start = (jnp.full((1, 1), log_lower, jnp.float32), jnp.full((1, 1), log_span, jnp.float32))
    lower, span = lax.fori_loop(0, SEARCH, halve, start)
    factor = jnp.exp(-0.5 * (lower + 0.5 * span))
    for own in range(own_planes):
        new_ref[own] = trial(place * own_planes + own, factor)


def in_vmem():
    return pl.BlockSpec(memory_space=pltpu.VMEM)


def in_smem():
    return pl.BlockSpec(memory_space=pltpu.SMEM)


KERNEL_VMEM = 24 * 2**20


def floats(*shape):
    return jax.ShapeDtypeStruct(shape, jnp.float32)


def prepare_call(radius, load_index, load_force, fixed):
    planes, row_width = fixed.shape
    layers = radius.shape[0]
    return pl.pallas_call(
        prepare_kernel,
        out_shape=[
            floats(len(ALL_SQUARES), layers, row_width),
            floats(2 * window_reach + 1, layers, row_width),
            floats(planes, layers, row_width),
            floats(3, layers, row_width),
            jax.ShapeDtypeStruct((1,), jnp.int32),
        ],
        in_specs=[pl.BlockSpec(memory_space=pltpu.HBM)] * 4,
        out_specs=[in_vmem()] * 4 + [in_smem()],
        scratch_shapes=[
            pltpu.SMEM(radius.shape, radius.dtype),
            pltpu.SMEM(load_index.shape, load_index.dtype),
            pltpu.SMEM(load_force.shape, load_force.dtype),
            pltpu.VMEM(fixed.shape, fixed.dtype),
            pltpu.SemaphoreType.DMA((4,)),
        ],
        compiler_params=pltpu.CompilerParams(vmem_limit_bytes=KERNEL_VMEM),
        cost_estimate=pl.CostEstimate(
            flops=40 * planes * layers * row_width,
            bytes_accessed=8 * planes * layers * row_width,
            transcendentals=0,
        ),
        name="prepare",
    )(
        *(
            pltpu.with_memory_space_constraint(array, pltpu.HBM)
            for array in (radius, load_index, load_force, fixed)
        )
    )


def sweep_call(spot, load, weights, inverses, free, density, displacement):
    cores, chips, own_planes, layers, row_width = density.shape
    planes = cores * chips * own_planes

    def scratch(*lead):
        return pltpu.VMEM(lead + (row_width,), jnp.float32)

    return pl.pallas_call(
        sweep_kernel,
        out_shape=[
            floats(3, (planes + 2) * layers, row_width),
            floats(planes, layers, row_width),
        ],
        in_specs=[in_smem()] + [in_vmem()] * 6,
        out_specs=[in_vmem()] * 2,
        scratch_shapes=[
            scratch(planes * (layers + GAP) + GAP),
            scratch(planes * (layers + GAP) + GAP),
            scratch(planes * (layers + GAP) + GAP),
            scratch(planes + 4, layers),
            scratch(planes + 4, layers),
            scratch(planes + 4, layers),
            scratch((planes + 1) * layers),
            scratch(planes + 1, layers),
            scratch((planes + 1) * layers),
            scratch(planes, layers),
            scratch(planes, layers),
            scratch(3, planes, layers),
            scratch(3, (planes + 2) * layers),
            scratch(3, (planes + 2) * layers),
        ],
        compiler_params=pltpu.CompilerParams(vmem_limit_bytes=KERNEL_VMEM),
        name="sweeps",
    )(spot, load, weights, inverses, free, density, displacement)


def sent_energy_call(disp, group_shape):
    return pl.pallas_call(
        sent_energy_kernel,
        out_shape=floats(*group_shape),
        in_specs=[in_vmem()],
        out_specs=in_vmem(),
        compiler_params=pltpu.CompilerParams(vmem_limit_bytes=KERNEL_VMEM),
        name="sent_energy",
    )(disp)


def kept_energy_call(disp, group_shape):
    parts, disp_rows, row_width = disp.shape
    layers = group_shape[2]
    return pl.pallas_call(
        kept_energy_kernel,
        out_shape=[floats(parts, disp_rows - 2 * layers, row_width), floats(*group_shape)],
        in_specs=[in_vmem()],
        out_specs=[pl.BlockSpec(memory_space=pltpu.HBM), in_vmem()],
        scratch_shapes=[pltpu.SemaphoreType.DMA(())],
        compiler_params=pltpu.CompilerParams(vmem_limit_bytes=KERNEL_VMEM),
        cost_estimate=pl.CostEstimate(
            flops=20 * disp.size, bytes_accessed=8 * disp.size, transcendentals=0
        ),
        name="kept_energy",
    )(disp)


def design_call(weights, sens, coef, density):
    cores, chips, own_planes, layers, row_width = density.shape
    planes = cores * chips * own_planes

    def scratch(*lead):
        return pltpu.VMEM(lead + (row_width,), jnp.float32)

    return pl.pallas_call(
        design_kernel,
        out_shape=floats(own_planes, layers, row_width),
        in_specs=[in_vmem()] * 4,
        out_specs=in_vmem(),
        scratch_shapes=[
            scratch(planes + 4, layers),
            scratch(planes + 4, layers),
            scratch(planes + 4, layers),
            scratch(planes, layers),
            scratch(planes * (layers + GAP) + GAP),
            scratch(planes * (layers + GAP) + GAP),
            scratch(planes, layers),
            scratch(planes, layers),
            scratch(planes, layers),
        ],
        compiler_params=pltpu.CompilerParams(vmem_limit_bytes=KERNEL_VMEM),
        name="design",
    )(weights, sens, coef, density)


def other_core(block):
    devices = lax.axis_size("space")
    return lax.ppermute(block, "space", [(i, i ^ 1) for i in range(devices)])


def chip_groups():
    chips = lax.axis_size("space") // 2
    return [[2 * chip + (chip ^ group) % 2 for chip in range(chips)] for group in range(2)]


def between_chips(pieces):
    return lax.all_to_all(pieces, "space", 0, 0, axis_index_groups=chip_groups())


def chip_gathered(block):
    chips = lax.axis_size("space") // 2
    return between_chips(jnp.broadcast_to(block[None], (chips,) + block.shape))


def with_other_core(blocks):
    return jnp.stack([blocks, other_core(blocks)])


def scattered_sum(sent, make_kept):
    received = other_core(sent)
    *others, kept = make_kept()
    return jnp.sum(between_chips(kept + received), axis=0), others


def one_slab(density, displacement, fixed, load_index, load_force, radius):
    same_group, small = lax.optimization_barrier(
        (chip_gathered(density), (radius, load_index, load_force.T, fixed))
    )
    whole = with_other_core(same_group)
    weights, inverses, free, load, spot = prepare_call(*small)
    disp, coef = sweep_call(spot, load, weights, inverses, free, whole, displacement[0])
    sent, disp = lax.optimization_barrier((sent_energy_call(disp, same_group.shape), disp))
    sens, (new_displacement,) = scattered_sum(
        sent, lambda: kept_energy_call(disp, same_group.shape)
    )
    sens = with_other_core(chip_gathered(sens))
    new_density = design_call(weights, sens, coef, whole)
    return new_density, new_displacement.reshape(displacement.shape)


def from_behind(block, axis, distance):
    devices = range(lax.axis_size(axis))
    route = [(i - distance, i) for i in devices if i - distance in devices]
    return lax.ppermute(block, axis, route)


def extended(x, sides, width):
    for axis, dim in sides:
        size, length = (lax.axis_size(axis), x.shape[dim])
        up = [(i, (i + 1) % size) for i in range(size - 1)]
        down = [(j, i) for i, j in up]
        last = lax.slice_in_dim(x, length - width, length, axis=dim)
        first = lax.slice_in_dim(x, 0, width, axis=dim)
        before = lax.ppermute(last, axis, up)
        after = lax.ppermute(first, axis, down)
        x = jnp.concatenate([before, x, after], axis=dim)
    return x


def from_partner(x, axis, bit):
    return lax.ppermute(x, axis, [(i, i ^ 1 << bit) for i in range(lax.axis_size(axis))])


def window_offsets():
    offsets_list = []
    for across in range(-window_reach, window_reach + 1):
        for upward in range(-window_reach, window_reach + 1):
            for sideways in range(-window_reach, window_reach + 1):
                length = math.sqrt(across * across + upward * upward + sideways * sideways)
                offsets_list.append((across, upward, sideways, length))
    return offsets_list


def layer_weights(radius):
    radial = radius.astype(jnp.float32)
    return jnp.stack(
        [jnp.maximum(radial - length, 0.0) for across, upward, sideways, length in window_offsets()]
    )


def pad_axis(grid_field, along_axis, before, after_cells):
    widths = [(0, 0)] * grid_field.ndim
    widths[along_axis] = (before, after_cells)
    return jnp.pad(grid_field, widths)


def pad_sides(grid_field):
    return jnp.pad(grid_field, ((0, 0), (window_reach, window_reach), (window_reach, window_reach)))


def filter_forward(padded, weights):
    out_rows = padded.shape[0] - 2 * window_reach
    layers = padded.shape[1] - 2 * window_reach
    row_width = padded.shape[2] - 2 * window_reach
    result = jnp.zeros((out_rows, layers, row_width), jnp.float32)
    for offset_index, (across, upward, sideways, length) in enumerate(window_offsets()):
        shifted = padded[
            window_reach + across : window_reach + across + out_rows,
            window_reach + upward : window_reach + upward + layers,
            window_reach + sideways : window_reach + sideways + row_width,
        ]
        result = result + weights[offset_index][None, :, None] * shifted
    return result


def filter_backward(padded, padded_weights):
    out_rows = padded.shape[0] - 2 * window_reach
    layers = padded.shape[1] - 2 * window_reach
    row_width = padded.shape[2] - 2 * window_reach
    result = jnp.zeros((out_rows, layers, row_width), jnp.float32)
    for offset_index, (across, upward, sideways, length) in enumerate(window_offsets()):
        shifted = padded[
            window_reach - across : window_reach - across + out_rows,
            window_reach - upward : window_reach - upward + layers,
            window_reach - sideways : window_reach - sideways + row_width,
        ]
        layer_part = padded_weights[
            offset_index, window_reach - upward : window_reach - upward + layers
        ]
        result = result + layer_part[None, :, None] * shifted
    return result


def stiff_factors(direction):
    return jnp.array(
        [2.0 if component == direction else 1.0 for component in range(3)], jnp.float32
    ).reshape(3, 1, 1, 1)


def relax_slab(padded, displace, face_x, face_z, face_y, force_field, free_cells, diagonal):
    flux_x = stiff_factors(0) * face_x * jnp.diff(padded, axis=1)
    stencil_image = flux_x[:, :-1] - flux_x[:, 1:]
    flux_z = stiff_factors(1) * face_z * jnp.diff(displace, axis=2)
    stencil_image = stencil_image + pad_axis(flux_z, 2, 1, 0) - pad_axis(flux_z, 2, 0, 1)
    flux_y = stiff_factors(2) * face_y * jnp.diff(displace, axis=3)
    stencil_image = stencil_image + pad_axis(flux_y, 3, 1, 0) - pad_axis(flux_y, 3, 0, 1)
    return free_cells * (displace + relax_factor * (force_field - stencil_image) / diagonal)


def slab_energy(grid_field, along_axis, direction, load_cases):
    change = jnp.diff(grid_field, axis=along_axis)
    return jnp.sum(stiff_factors(direction) * change * change, axis=0) / load_cases


def neighbour_planes(displace, load_cases, axis_devices):
    if axis_devices > load_cases:
        below = from_behind(displace[:, -1:], "space", load_cases)
        above = from_behind(displace[:, :1], "space", -load_cases)
    else:
        below = jnp.zeros_like(displace[:, :1])
        above = jnp.zeros_like(displace[:, :1])
    return jnp.concatenate([below, displace, above], axis=1)


def many_slabs(density, displacement, fixed, load_index, load_force, radius):
    slab_rows, layers, row_width = density.shape
    load_cases = load_index.shape[0]
    level_count = load_cases.bit_length() - 1
    axis_devices = lax.axis_size("space")
    axis_place = lax.axis_index("space")
    slab_planes = slab_rows * load_cases
    slab_place = axis_place // load_cases
    load_place = axis_place % load_cases
    total_rows = slab_rows * axis_devices
    weights = layer_weights(radius)
    padded_weights = pad_axis(weights, 1, window_reach, window_reach)
    global_rows = (
        jnp.arange(slab_rows + 2 * window_reach, dtype=jnp.int32)
        + axis_place * slab_rows
        - window_reach
    )
    deep_inside = ((global_rows >= 0) & (global_rows < total_rows)).astype(jnp.float32)
    inside_field = deep_inside[:, None, None] * pad_sides(
        jnp.ones((slab_rows + 2 * window_reach, layers, row_width), jnp.float32)
    )
    total_weight = filter_forward(inside_field, weights)
    slab_start = slab_place * slab_planes
    margin_rows = jnp.arange(slab_planes + 2, dtype=jnp.int32) + slab_start - 1
    margin_inside = ((margin_rows >= 0) & (margin_rows < total_rows)).astype(jnp.float32)
    face_valid = margin_inside[1:] * margin_inside[:-1]
    fixed_slab = lax.dynamic_slice_in_dim(fixed, slab_start, slab_planes, 0).astype(jnp.float32)
    bottom_layer = (jnp.arange(layers, dtype=jnp.int32) == 0).astype(jnp.float32)
    free_cells = 1.0 - bottom_layer[None, :, None] * fixed_slab[:, None, :]
    slab_cells = slab_planes * layers * row_width
    cell_index = jnp.arange(slab_cells, dtype=jnp.int32) + slab_place * slab_cells
    load_hot = jnp.arange(load_cases, dtype=jnp.int32) == load_place
    own_index = jnp.sum(jnp.where(load_hot, load_index, 0))
    own_force = jnp.sum(load_hot.astype(jnp.float32)[:, None] * load_force, axis=0)
    load_hits = (cell_index == own_index).astype(jnp.float32)
    force_field = (own_force[:, None] * load_hits[None, :]).reshape(
        3, slab_planes, layers, row_width
    )
    displace = displacement[0] * free_cells
    target = volume_share * total_rows * layers * row_width
    padded = neighbour_planes(displace, load_cases, axis_devices)
    halo_density = extended(density, (("space", 0),), window_reach)
    filtered = filter_forward(pad_sides(halo_density), weights) / total_weight
    whole_field = lax.all_gather(filtered, "space", axis=0, tiled=True)
    margin = lax.dynamic_slice_in_dim(
        pad_axis(whole_field, 0, 1, 1), slab_start, slab_planes + 2, 0
    )
    moduli = floor_modulus + (1.0 - floor_modulus) * margin**3
    face_x = 0.5 * (moduli[1:] + moduli[:-1]) * face_valid[:, None, None]
    inner_moduli = moduli[1:-1]
    face_z = 0.5 * (inner_moduli[:, 1:] + inner_moduli[:, :-1])
    face_y = 0.5 * (inner_moduli[:, :, 1:] + inner_moduli[:, :, :-1])
    sum_x = face_x[:-1] + face_x[1:]
    sum_z = pad_axis(face_z, 1, 1, 0) + pad_axis(face_z, 1, 0, 1)
    sum_y = pad_axis(face_y, 2, 1, 0) + pad_axis(face_y, 2, 0, 1)
    diagonal = stiff_factors(0) * sum_x + stiff_factors(1) * sum_z + stiff_factors(2) * sum_y
    for sweep_index in range(SWEEPS):
        displace = relax_slab(
            padded, displace, face_x, face_z, face_y, force_field, free_cells, diagonal
        )
        padded = neighbour_planes(displace, load_cases, axis_devices)
    energy_x = slab_energy(padded, 1, 0, load_cases) * face_valid[:, None, None]
    energy_z = slab_energy(displace, 2, 1, load_cases)
    energy_y = slab_energy(displace, 3, 2, load_cases)
    sens_term = 0.5 * (
        energy_x[:-1]
        + energy_x[1:]
        + pad_axis(energy_z, 1, 1, 0)
        + pad_axis(energy_z, 1, 0, 1)
        + pad_axis(energy_y, 2, 1, 0)
        + pad_axis(energy_y, 2, 0, 1)
    )
    sensitive = sens_term
    for level in reversed(range(level_count)):
        half_rows = sensitive.shape[0] // 2
        upper_side = load_place // 2**level % 2 == 1
        outgoing = jnp.where(upper_side, sensitive[:half_rows], sensitive[half_rows:])
        keeping = jnp.where(upper_side, sensitive[half_rows:], sensitive[:half_rows])
        sensitive = keeping + from_partner(outgoing, "space", level)
    weighted_share = 3.0 * (1.0 - floor_modulus) * filtered**2 * sensitive / total_weight
    halo_share = extended(weighted_share, (("space", 0),), window_reach)
    root_term = jnp.sqrt(filter_backward(pad_sides(halo_share), padded_weights))
    lowest = jnp.maximum(density - move_limit, density_floor)
    highest = jnp.minimum(density + move_limit, 1.0)
    design_now = density

    def trial_design(log_level):
        return jnp.clip(design_now * root_term * jnp.exp(-0.5 * log_level), lowest, highest)

    start_state = (jnp.asarray(log_lower, jnp.float32), jnp.asarray(log_span, jnp.float32))

    def halve(search_step, search_state):
        lower_end, span_width = search_state
        half_span = span_width * 0.5
        middle = lower_end + half_span
        volume_total = lax.psum(jnp.sum(trial_design(middle)), "space")
        return (jnp.where(volume_total > target, middle, lower_end), half_span)

    lower_end, span_width = lax.fori_loop(0, SEARCH, halve, start_state)
    density = trial_design(lower_end + 0.5 * span_width)
    new_displacement = displace[None]
    return (density, new_displacement)


def solution(mesh):
    in_specs = (
        P("space", "parts", None),
        P("space", None, None, "parts", None),
        P(None, "parts"),
        P("parts"),
        P("parts", None),
        P("parts"),
    )
    out_specs = (P("space", "parts", None), P("space", None, None, "parts", None))

    def local(density, displacement, fixed, load_index, load_force, radius):
        alone = lax.axis_size("space") == load_index.shape[0]
        run = one_slab if alone else many_slabs
        return run(density, displacement, fixed, load_index, load_force, radius)

    return jax.shard_map(local, mesh=mesh, in_specs=in_specs, out_specs=out_specs, check_vma=False)
```

```python
import math

import jax
import jax.numpy as jnp
from jax import lax
from jax.experimental import pallas as pl
from jax.experimental.pallas import tpu as pltpu
from jax.sharding import PartitionSpec as P

SWEEPS = 3
SEARCH = 12


floor_modulus = 0.05
relax_factor = 0.6
move_limit = 0.2
density_floor = 0.01
volume_share = 0.5
log_lower = -16.0
log_span = 32.0
window_reach = 2

PLANE_SQUARES = (0, 1, 2, 4, 5, 8)
ALL_SQUARES = (0, 1, 2, 3, 4, 5, 6, 8, 9, 12)


def spot_iota(shape, dim):
    return lax.broadcasted_iota(jnp.int32, shape, dim)


def each_plane(planes, body, carry):
    for x in range(planes):
        carry = body(x, carry)
    return carry


def layer_radius(radius_ref, layers, row_width):
    z = spot_iota((layers, row_width), 0)
    result = jnp.zeros((layers, row_width), jnp.int32)
    for layer in range(layers):
        result = jnp.where(z == layer, radius_ref[layer], result)
    return result.astype(jnp.float32)


def class_weights(radius_ref, weight_ref):
    layers, row_width = weight_ref.shape[1:]
    radial = layer_radius(radius_ref, layers, row_width)
    for place, square in enumerate(ALL_SQUARES):
        weight_ref[place] = jnp.maximum(radial - math.sqrt(square), 0.0)


def shift_sum(field, dim, distance):
    size = field.shape[dim]
    spot = spot_iota(field.shape, dim)
    ahead = jnp.where(spot < size - distance, pltpu.roll(field, size - distance, dim), 0.0)
    behind = jnp.where(spot >= distance, pltpu.roll(field, distance, dim), 0.0)
    return ahead + behind


def plane_sums(plane):
    beside = shift_sum(plane, 1, 1)
    further = shift_sum(plane, 1, 2)
    return {
        0: plane,
        1: beside + shift_sum(plane, 0, 1),
        2: shift_sum(beside, 0, 1),
        4: further + shift_sum(plane, 0, 2),
        5: shift_sum(further, 0, 1) + shift_sum(beside, 0, 2),
        8: shift_sum(further, 0, 2),
    }


def weigh(sums, weight_ref, square):
    result = None
    for inner in PLANE_SQUARES:
        term = weight_ref[ALL_SQUARES.index(inner + square)] * sums[inner]
        result = term if result is None else result + term
    return result


def forward_planes(plane, weight_ref):
    sums = plane_sums(plane)
    return [weigh(sums, weight_ref, square) for square in (0, 1, 4)]


def rows(x, layers, shift=0):
    return pl.ds(x * layers + shift, layers)


GAP = 8


def gapped(x, layers, shift=0):
    return pl.ds(GAP + x * (layers + GAP) + shift, layers)


def gap(x, layers):
    return pl.ds(x * (layers + GAP), GAP)


def pair_spot(x, own_planes):
    device = x // own_planes
    apart = device ^ lax.axis_index("space")
    return (apart ^ apart >> 1) & 1, device >> 1, x % own_planes


def edge_class(x, planes):
    return min(x, 2) + max(x - (planes - 3), 0)


def zero_edges(ref):
    planes = ref.shape[0]
    for place in (0, 1, planes - 2, planes - 1):
        ref[place] = jnp.zeros(ref.shape[1:], ref.dtype)


def prepare_kernel(
    radius_hbm,
    index_hbm,
    force_hbm,
    fixed_hbm,
    weight_ref,
    inverse_ref,
    free_ref,
    load_ref,
    spot_ref,
    radius_ref,
    index_ref,
    force_ref,
    fixed_ref,
    arrived,
):
    copies = [
        pltpu.make_async_copy(source, target, arrived.at[place])
        for place, (source, target) in enumerate(
            (
                (radius_hbm, radius_ref),
                (index_hbm, index_ref),
                (force_hbm, force_ref),
                (fixed_hbm, fixed_ref),
            )
        )
    ]
    for copy in copies:
        copy.start()
    for copy in copies:
        copy.wait()
    planes, layers, row_width = free_ref.shape
    load_place = lax.axis_index("space")
    shape = (layers, row_width)
    z = spot_iota(shape, 0)
    y = spot_iota(shape, 1)

    class_weights(radius_ref, weight_ref)
    ones = forward_planes(jnp.ones(shape, jnp.float32), weight_ref)
    for place, (lower, upper) in enumerate(((0, 2), (1, 2), (2, 2), (2, 1), (2, 0))):
        inverse_ref[place] = 1.0 / (
            ones[0] + min(lower, 1) * ones[1] + min(upper, 1) * ones[1]
            + (lower // 2) * ones[2] + (upper // 2) * ones[2]
        )

    def free_plane(x, carry):
        free_ref[x] = jnp.where(
            z == 0, 1.0 - fixed_ref[pl.ds(x, 1), :].astype(jnp.float32), 1.0
        )
        return carry

    each_plane(planes, free_plane, 0)

    own_index = index_ref[load_place]
    own_z = own_index // row_width % layers
    own_y = own_index % row_width
    hit = (z == own_z) & (y == own_y)
    for part in range(3):
        load_ref[part] = jnp.where(hit, force_ref[part, load_place], 0.0)
    spot_ref[0] = own_index // (layers * row_width)


def sweep_kernel(
    spot_ref,
    load_ref,
    weight_ref,
    inverse_ref,
    free_ref,
    density_ref,
    start_ref,
    disp_ref,
    coef_ref,
    plane_ref,
    beside_ref,
    further_ref,
    near_ref,
    side_ref,
    far_ref,
    modulus_ref,
    across_ref,
    up_ref,
    right_ref,
    left_ref,
    rate_ref,
    first_ref,
    second_ref,
):
    planes, layers, row_width = coef_ref.shape
    own_planes = density_ref.shape[2]
    shape = (layers, row_width)
    z = spot_iota(shape, 0)
    y = spot_iota(shape, 1)
    zero = jnp.zeros(shape, jnp.float32)
    zero_gap = jnp.zeros((GAP, row_width), jnp.float32)

    for ref in (side_ref, far_ref):
        zero_edges(ref)
    for ref in (plane_ref, beside_ref, further_ref):
        ref[gap(planes, layers)] = zero_gap

    def spread_plane(x, carry):
        plane = density_ref[pair_spot(x, own_planes)]
        fields = (plane, shift_sum(plane, 1, 1), shift_sum(plane, 1, 2))
        for ref, field in zip((plane_ref, beside_ref, further_ref), fields):
            ref[gap(x, layers)] = zero_gap
            ref[gapped(x, layers)] = field
        return carry

    each_plane(planes, spread_plane, 0)

    def filter_plane(x, carry):
        def around(ref, distance):
            return ref[gapped(x, layers, distance)] + ref[gapped(x, layers, -distance)]

        beside = beside_ref[gapped(x, layers)]
        further = further_ref[gapped(x, layers)]
        sums = {
            0: plane_ref[gapped(x, layers)],
            1: beside + around(plane_ref, 1),
            2: around(beside_ref, 1),
            4: further + around(plane_ref, 2),
            5: around(further_ref, 1) + around(beside_ref, 2),
            8: around(further_ref, 2),
        }
        near_ref[x + 2] = weigh(sums, weight_ref, 0)
        side_ref[x + 2] = weigh(sums, weight_ref, 1)
        far_ref[x + 2] = weigh(sums, weight_ref, 4)
        return carry

    each_plane(planes, filter_plane, 0)

    def modulus_plane(x, carry):
        inverse = inverse_ref[edge_class(x, planes)]
        filtered = (
            near_ref[x + 2]
            + side_ref[x + 1]
            + side_ref[x + 3]
            + far_ref[x]
            + far_ref[x + 4]
        ) * inverse
        modulus = floor_modulus + (1.0 - floor_modulus) * (filtered * filtered * filtered)
        modulus_ref[rows(x, layers)] = modulus
        coef_ref[x] = 3.0 * (1.0 - floor_modulus) * (filtered * filtered) * inverse
        return carry

    each_plane(planes, modulus_plane, 0)

    modulus_ref[rows(planes, layers)] = zero
    across_ref[0] = zero
    across_ref[planes] = zero
    up_ref[rows(0, layers)] = zero
    for ref in (first_ref, second_ref, disp_ref):
        for part in range(3):
            ref[part, rows(0, layers)] = zero
            ref[part, rows(planes + 1, layers)] = zero

    def face_plane(x, carry):
        before = carry
        modulus = modulus_ref[rows(x, layers)]
        later = modulus_ref[rows(x + 1, layers)]
        ahead = 0.5 * (modulus + later) if x + 1 < planes else zero
        across_ref[x + 1] = ahead
        above = modulus_ref[rows(x, layers, 1)]
        up = jnp.where(z < layers - 1, 0.5 * (modulus + above), 0.0)
        right = jnp.where(
            y < row_width - 1, 0.5 * (modulus + pltpu.roll(modulus, row_width - 1, 1)), 0.0
        )
        left = pltpu.roll(right, 1, 1)
        up_ref[rows(x + 1, layers)] = up
        right_ref[x] = right
        left_ref[x] = left
        free = free_ref[x]
        sums = (before + ahead, up + pltpu.roll(up, 1, 0), left + right)
        every = sums[0] + sums[1] + sums[2]
        push = relax_factor * free
        diagonal = [every + part_sum for part_sum in sums]
        pair = diagonal[0] * diagonal[1]
        push = push / (pair * diagonal[2])
        side = push * diagonal[2]
        rate_ref[0, x] = side * diagonal[1]
        rate_ref[1, x] = side * diagonal[0]
        rate_ref[2, x] = push * pair
        for part in range(3):
            first_ref[part, rows(x + 1, layers)] = start_ref[part, x] * free
        return ahead

    each_plane(planes, face_plane, zero)

    own_x = spot_ref[0]

    def sweep(source, target):
        def sweep_plane(x, carry):
            before, after = across_ref[x], across_ref[x + 1]
            up, down = up_ref[rows(x + 1, layers)], up_ref[rows(x + 1, layers, -1)]
            right, left = right_ref[x], left_ref[x]
            for part in range(3):
                here = source[part, rows(x + 1, layers)]
                pulls = [
                    before * source[part, rows(x, layers)]
                    + after * source[part, rows(x + 2, layers)],
                    up * source[part, rows(x + 1, layers, 1)]
                    + down * source[part, rows(x + 1, layers, -1)],
                    right * pltpu.roll(here, row_width - 1, 1) + left * pltpu.roll(here, 1, 1),
                ]
                pull = pulls[0] + pulls[1] + pulls[2] + pulls[part]
                target[part, rows(x + 1, layers)] = (
                    1.0 - relax_factor
                ) * here + rate_ref[part, x] * pull
            return carry

        each_plane(planes, sweep_plane, 0)
        for part in range(3):
            target[part, rows(own_x + 1, layers)] += rate_ref[part, own_x] * load_ref[part]

    stages = (first_ref, second_ref)
    for turn in range(SWEEPS - 1):
        sweep(stages[turn % 2], stages[(turn + 1) % 2])
    sweep(stages[(SWEEPS - 1) % 2], disp_ref)


def energy_planes(group, disp_ref, sens_ref):
    chips, own_planes, layers, row_width = sens_ref.shape
    planes = disp_ref.shape[1] // layers - 2
    load_cases = lax.axis_size("space")
    shape = (layers, row_width)
    z = spot_iota(shape, 0)
    y = spot_iota(shape, 1)
    zero = jnp.zeros(shape, jnp.float32)
    mine = lax.axis_index("space")
    core = mine ^ mine >> 1 ^ group

    def between(x):
        result = zero
        for part in range(3):
            step = disp_ref[part, rows(x + 1, layers)] - disp_ref[part, rows(x, layers)]
            result = result + (2.0 if part == 0 else 1.0) * (step * step)
        return jnp.where((x > 0) & (x < planes), result, 0.0)

    def inside(x):
        upward, right = zero, zero
        for part in range(3):
            here = disp_ref[part, rows(x + 1, layers)]
            climb = disp_ref[part, rows(x + 1, layers, 1)] - here
            slide = pltpu.roll(here, row_width - 1, 1) - here
            upward = upward + (2.0 if part == 1 else 1.0) * (climb * climb)
            right = right + (2.0 if part == 2 else 1.0) * (slide * slide)
        upward = jnp.where(z < layers - 1, upward, 0.0)
        right = jnp.where(y < row_width - 1, right, 0.0)
        return upward + pltpu.roll(upward, 1, 0) + right + pltpu.roll(right, 1, 1)

    for chip in range(chips):
        first = own_planes * (2 * chip + ((core ^ chip) & 1))
        before = between(first)
        for own in range(own_planes):
            after = between(first + own + 1)
            sens_ref[chip, own] = (0.5 / load_cases) * (before + after + inside(first + own))
            before = after


def sent_energy_kernel(disp_ref, sens_ref):
    energy_planes(1, disp_ref, sens_ref)


def kept_energy_kernel(disp_ref, disp_hbm, sens_ref, stored):
    layers = sens_ref.shape[2]
    inner = pl.ds(layers, disp_ref.shape[1] - 2 * layers)
    store = pltpu.make_async_copy(disp_ref.at[:, inner], disp_hbm, stored)
    store.start()
    energy_planes(0, disp_ref, sens_ref)
    store.wait()


def design_kernel(
    weight_ref,
    sens_ref,
    coef_ref,
    density_ref,
    new_ref,
    plane_ref,
    beside_ref,
    further_ref,
    level_ref,
    near_ref,
    far_ref,
    pull_ref,
    low_ref,
    high_ref,
):
    planes, layers, row_width = coef_ref.shape
    own_planes = density_ref.shape[2]
    place = lax.axis_index("space")
    shape = (layers, row_width)
    zero = jnp.zeros(shape, jnp.float32)
    zero_gap = jnp.zeros((GAP, row_width), jnp.float32)
    for ref in (plane_ref, beside_ref, further_ref):
        zero_edges(ref)
    for ref in (near_ref, far_ref):
        ref[gap(planes, layers)] = zero_gap

    def spread_plane(x, carry):
        plane = sens_ref[pair_spot(x, own_planes)] * coef_ref[x]
        plane_ref[x + 2] = plane
        beside_ref[x + 2] = shift_sum(plane, 1, 1)
        further_ref[x + 2] = shift_sum(plane, 1, 2)
        return carry

    each_plane(planes, spread_plane, 0)

    def filter_plane(x, carry):
        def around(ref, distance):
            return ref[x + 2 + distance] + ref[x + 2 - distance]

        sums = {
            0: plane_ref[x + 2],
            1: beside_ref[x + 2] + around(plane_ref, 1),
            2: around(beside_ref, 1),
            4: further_ref[x + 2] + around(plane_ref, 2),
            5: around(further_ref, 1) + around(beside_ref, 2),
            8: around(further_ref, 2),
        }
        level_ref[x] = weigh(sums, weight_ref, 0)
        for ref, square in ((near_ref, 1), (far_ref, 4)):
            ref[gap(x, layers)] = zero_gap
            ref[gapped(x, layers)] = weigh(sums, weight_ref, square)
        return carry

    each_plane(planes, filter_plane, 0)

    def root_plane(x, carry):
        root = jnp.sqrt(
            level_ref[x]
            + near_ref[gapped(x, layers, 1)]
            + near_ref[gapped(x, layers, -1)]
            + far_ref[gapped(x, layers, 2)]
            + far_ref[gapped(x, layers, -2)]
        )
        density = density_ref[pair_spot(x, own_planes)]
        pull_ref[x] = density * root
        low_ref[x] = jnp.maximum(density - move_limit, density_floor)
        high_ref[x] = jnp.minimum(density + move_limit, 1.0)
        return carry

    each_plane(planes, root_plane, 0)

    target = volume_share * planes * layers * row_width

    def trial(x, factor):
        return jnp.minimum(jnp.maximum(pull_ref[x] * factor, low_ref[x]), high_ref[x])

    def halve(step, state):
        lower, span = state
        half = span * 0.5
        middle = lower + half
        factor = jnp.exp(-0.5 * middle)
        total = each_plane(planes, lambda x, acc: acc + trial(x, factor), zero)
        volume = jnp.sum(jnp.sum(total, axis=0, keepdims=True), axis=1, keepdims=True)
        return jnp.where(volume > target, middle, lower), half

    start = (jnp.full((1, 1), log_lower, jnp.float32), jnp.full((1, 1), log_span, jnp.float32))
    lower, span = lax.fori_loop(0, SEARCH, halve, start)
    factor = jnp.exp(-0.5 * (lower + 0.5 * span))
    for own in range(own_planes):
        new_ref[own] = trial(place * own_planes + own, factor)


def in_vmem():
    return pl.BlockSpec(memory_space=pltpu.VMEM)


def in_smem():
    return pl.BlockSpec(memory_space=pltpu.SMEM)


KERNEL_VMEM = 24 * 2**20


def floats(*shape):
    return jax.ShapeDtypeStruct(shape, jnp.float32)


def prepare_call(radius, load_index, load_force, fixed):
    planes, row_width = fixed.shape
    layers = radius.shape[0]
    return pl.pallas_call(
        prepare_kernel,
        out_shape=[
            floats(len(ALL_SQUARES), layers, row_width),
            floats(2 * window_reach + 1, layers, row_width),
            floats(planes, layers, row_width),
            floats(3, layers, row_width),
            jax.ShapeDtypeStruct((1,), jnp.int32),
        ],
        in_specs=[pl.BlockSpec(memory_space=pltpu.HBM)] * 4,
        out_specs=[in_vmem()] * 4 + [in_smem()],
        scratch_shapes=[
            pltpu.SMEM(radius.shape, radius.dtype),
            pltpu.SMEM(load_index.shape, load_index.dtype),
            pltpu.SMEM(load_force.shape, load_force.dtype),
            pltpu.VMEM(fixed.shape, fixed.dtype),
            pltpu.SemaphoreType.DMA((4,)),
        ],
        compiler_params=pltpu.CompilerParams(vmem_limit_bytes=KERNEL_VMEM),
        cost_estimate=pl.CostEstimate(
            flops=40 * planes * layers * row_width,
            bytes_accessed=8 * planes * layers * row_width,
            transcendentals=0,
        ),
        name="prepare",
    )(
        *(
            pltpu.with_memory_space_constraint(array, pltpu.HBM)
            for array in (radius, load_index, load_force, fixed)
        )
    )


def sweep_call(spot, load, weights, inverses, free, density, displacement):
    cores, chips, own_planes, layers, row_width = density.shape
    planes = cores * chips * own_planes

    def scratch(*lead):
        return pltpu.VMEM(lead + (row_width,), jnp.float32)

    return pl.pallas_call(
        sweep_kernel,
        out_shape=[
            floats(3, (planes + 2) * layers, row_width),
            floats(planes, layers, row_width),
        ],
        in_specs=[in_smem()] + [in_vmem()] * 6,
        out_specs=[in_vmem()] * 2,
        scratch_shapes=[
            scratch(planes * (layers + GAP) + GAP),
            scratch(planes * (layers + GAP) + GAP),
            scratch(planes * (layers + GAP) + GAP),
            scratch(planes + 4, layers),
            scratch(planes + 4, layers),
            scratch(planes + 4, layers),
            scratch((planes + 1) * layers),
            scratch(planes + 1, layers),
            scratch((planes + 1) * layers),
            scratch(planes, layers),
            scratch(planes, layers),
            scratch(3, planes, layers),
            scratch(3, (planes + 2) * layers),
            scratch(3, (planes + 2) * layers),
        ],
        compiler_params=pltpu.CompilerParams(vmem_limit_bytes=KERNEL_VMEM),
        name="sweeps",
    )(spot, load, weights, inverses, free, density, displacement)


def sent_energy_call(disp, group_shape):
    return pl.pallas_call(
        sent_energy_kernel,
        out_shape=floats(*group_shape),
        in_specs=[in_vmem()],
        out_specs=in_vmem(),
        compiler_params=pltpu.CompilerParams(vmem_limit_bytes=KERNEL_VMEM),
        name="sent_energy",
    )(disp)


def kept_energy_call(disp, group_shape):
    parts, disp_rows, row_width = disp.shape
    layers = group_shape[2]
    return pl.pallas_call(
        kept_energy_kernel,
        out_shape=[floats(parts, disp_rows - 2 * layers, row_width), floats(*group_shape)],
        in_specs=[in_vmem()],
        out_specs=[pl.BlockSpec(memory_space=pltpu.HBM), in_vmem()],
        scratch_shapes=[pltpu.SemaphoreType.DMA(())],
        compiler_params=pltpu.CompilerParams(vmem_limit_bytes=KERNEL_VMEM),
        cost_estimate=pl.CostEstimate(
            flops=20 * disp.size, bytes_accessed=8 * disp.size, transcendentals=0
        ),
        name="kept_energy",
    )(disp)


def design_call(weights, sens, coef, density):
    cores, chips, own_planes, layers, row_width = density.shape
    planes = cores * chips * own_planes

    def scratch(*lead):
        return pltpu.VMEM(lead + (row_width,), jnp.float32)

    return pl.pallas_call(
        design_kernel,
        out_shape=floats(own_planes, layers, row_width),
        in_specs=[in_vmem()] * 4,
        out_specs=in_vmem(),
        scratch_shapes=[
            scratch(planes + 4, layers),
            scratch(planes + 4, layers),
            scratch(planes + 4, layers),
            scratch(planes, layers),
            scratch(planes * (layers + GAP) + GAP),
            scratch(planes * (layers + GAP) + GAP),
            scratch(planes, layers),
            scratch(planes, layers),
            scratch(planes, layers),
        ],
        compiler_params=pltpu.CompilerParams(vmem_limit_bytes=KERNEL_VMEM),
        name="design",
    )(weights, sens, coef, density)


def other_core(block):
    devices = lax.axis_size("space")
    return lax.ppermute(block, "space", [(i, i ^ 1) for i in range(devices)])


def chip_groups():
    chips = lax.axis_size("space") // 2
    return [[2 * chip + (chip ^ group) % 2 for chip in range(chips)] for group in range(2)]


def between_chips(pieces):
    return lax.all_to_all(pieces, "space", 0, 0, axis_index_groups=chip_groups())


def chip_gathered(block):
    chips = lax.axis_size("space") // 2
    return between_chips(jnp.broadcast_to(block[None], (chips,) + block.shape))


def with_other_core(blocks):
    return jnp.stack([blocks, other_core(blocks)])


def scattered_sum(sent, make_kept):
    received = other_core(sent)
    *others, kept = make_kept()
    return jnp.sum(between_chips(kept + received), axis=0), others


def one_slab(density, displacement, fixed, load_index, load_force, radius):
    same_group, small = lax.optimization_barrier(
        (chip_gathered(density), (radius, load_index, load_force.T, fixed))
    )
    whole = with_other_core(same_group)
    weights, inverses, free, load, spot = prepare_call(*small)
    disp, coef = sweep_call(spot, load, weights, inverses, free, whole, displacement[0])
    sent, disp = lax.optimization_barrier((sent_energy_call(disp, same_group.shape), disp))
    sens, (new_displacement,) = scattered_sum(
        sent, lambda: kept_energy_call(disp, same_group.shape)
    )
    sens = with_other_core(chip_gathered(sens))
    new_density = design_call(weights, sens, coef, whole)
    return new_density, new_displacement.reshape(displacement.shape)


def from_behind(block, axis, distance):
    devices = range(lax.axis_size(axis))
    route = [(i - distance, i) for i in devices if i - distance in devices]
    return lax.ppermute(block, axis, route)


def extended(x, sides, width):
    for axis, dim in sides:
        size, length = (lax.axis_size(axis), x.shape[dim])
        up = [(i, (i + 1) % size) for i in range(size - 1)]
        down = [(j, i) for i, j in up]
        last = lax.slice_in_dim(x, length - width, length, axis=dim)
        first = lax.slice_in_dim(x, 0, width, axis=dim)
        before = lax.ppermute(last, axis, up)
        after = lax.ppermute(first, axis, down)
        x = jnp.concatenate([before, x, after], axis=dim)
    return x


def from_partner(x, axis, bit):
    return lax.ppermute(x, axis, [(i, i ^ 1 << bit) for i in range(lax.axis_size(axis))])


def window_offsets():
    offsets_list = []
    for across in range(-window_reach, window_reach + 1):
        for upward in range(-window_reach, window_reach + 1):
            for sideways in range(-window_reach, window_reach + 1):
                length = math.sqrt(across * across + upward * upward + sideways * sideways)
                offsets_list.append((across, upward, sideways, length))
    return offsets_list


def layer_weights(radius):
    radial = radius.astype(jnp.float32)
    return jnp.stack(
        [jnp.maximum(radial - length, 0.0) for across, upward, sideways, length in window_offsets()]
    )


def pad_axis(grid_field, along_axis, before, after_cells):
    widths = [(0, 0)] * grid_field.ndim
    widths[along_axis] = (before, after_cells)
    return jnp.pad(grid_field, widths)


def pad_sides(grid_field):
    return jnp.pad(grid_field, ((0, 0), (window_reach, window_reach), (window_reach, window_reach)))


def filter_forward(padded, weights):
    out_rows = padded.shape[0] - 2 * window_reach
    layers = padded.shape[1] - 2 * window_reach
    row_width = padded.shape[2] - 2 * window_reach
    result = jnp.zeros((out_rows, layers, row_width), jnp.float32)
    for offset_index, (across, upward, sideways, length) in enumerate(window_offsets()):
        shifted = padded[
            window_reach + across : window_reach + across + out_rows,
            window_reach + upward : window_reach + upward + layers,
            window_reach + sideways : window_reach + sideways + row_width,
        ]
        result = result + weights[offset_index][None, :, None] * shifted
    return result


def filter_backward(padded, padded_weights):
    out_rows = padded.shape[0] - 2 * window_reach
    layers = padded.shape[1] - 2 * window_reach
    row_width = padded.shape[2] - 2 * window_reach
    result = jnp.zeros((out_rows, layers, row_width), jnp.float32)
    for offset_index, (across, upward, sideways, length) in enumerate(window_offsets()):
        shifted = padded[
            window_reach - across : window_reach - across + out_rows,
            window_reach - upward : window_reach - upward + layers,
            window_reach - sideways : window_reach - sideways + row_width,
        ]
        layer_part = padded_weights[
            offset_index, window_reach - upward : window_reach - upward + layers
        ]
        result = result + layer_part[None, :, None] * shifted
    return result


def stiff_factors(direction):
    return jnp.array(
        [2.0 if component == direction else 1.0 for component in range(3)], jnp.float32
    ).reshape(3, 1, 1, 1)


def relax_slab(padded, displace, face_x, face_z, face_y, force_field, free_cells, diagonal):
    flux_x = stiff_factors(0) * face_x * jnp.diff(padded, axis=1)
    stencil_image = flux_x[:, :-1] - flux_x[:, 1:]
    flux_z = stiff_factors(1) * face_z * jnp.diff(displace, axis=2)
    stencil_image = stencil_image + pad_axis(flux_z, 2, 1, 0) - pad_axis(flux_z, 2, 0, 1)
    flux_y = stiff_factors(2) * face_y * jnp.diff(displace, axis=3)
    stencil_image = stencil_image + pad_axis(flux_y, 3, 1, 0) - pad_axis(flux_y, 3, 0, 1)
    return free_cells * (displace + relax_factor * (force_field - stencil_image) / diagonal)


def slab_energy(grid_field, along_axis, direction, load_cases):
    change = jnp.diff(grid_field, axis=along_axis)
    return jnp.sum(stiff_factors(direction) * change * change, axis=0) / load_cases


def neighbour_planes(displace, load_cases, axis_devices):
    if axis_devices > load_cases:
        below = from_behind(displace[:, -1:], "space", load_cases)
        above = from_behind(displace[:, :1], "space", -load_cases)
    else:
        below = jnp.zeros_like(displace[:, :1])
        above = jnp.zeros_like(displace[:, :1])
    return jnp.concatenate([below, displace, above], axis=1)


def many_slabs(density, displacement, fixed, load_index, load_force, radius):
    slab_rows, layers, row_width = density.shape
    load_cases = load_index.shape[0]
    level_count = load_cases.bit_length() - 1
    axis_devices = lax.axis_size("space")
    axis_place = lax.axis_index("space")
    slab_planes = slab_rows * load_cases
    slab_place = axis_place // load_cases
    load_place = axis_place % load_cases
    total_rows = slab_rows * axis_devices
    weights = layer_weights(radius)
    padded_weights = pad_axis(weights, 1, window_reach, window_reach)
    global_rows = (
        jnp.arange(slab_rows + 2 * window_reach, dtype=jnp.int32)
        + axis_place * slab_rows
        - window_reach
    )
    deep_inside = ((global_rows >= 0) & (global_rows < total_rows)).astype(jnp.float32)
    inside_field = deep_inside[:, None, None] * pad_sides(
        jnp.ones((slab_rows + 2 * window_reach, layers, row_width), jnp.float32)
    )
    total_weight = filter_forward(inside_field, weights)
    slab_start = slab_place * slab_planes
    margin_rows = jnp.arange(slab_planes + 2, dtype=jnp.int32) + slab_start - 1
    margin_inside = ((margin_rows >= 0) & (margin_rows < total_rows)).astype(jnp.float32)
    face_valid = margin_inside[1:] * margin_inside[:-1]
    fixed_slab = lax.dynamic_slice_in_dim(fixed, slab_start, slab_planes, 0).astype(jnp.float32)
    bottom_layer = (jnp.arange(layers, dtype=jnp.int32) == 0).astype(jnp.float32)
    free_cells = 1.0 - bottom_layer[None, :, None] * fixed_slab[:, None, :]
    slab_cells = slab_planes * layers * row_width
    cell_index = jnp.arange(slab_cells, dtype=jnp.int32) + slab_place * slab_cells
    load_hot = jnp.arange(load_cases, dtype=jnp.int32) == load_place
    own_index = jnp.sum(jnp.where(load_hot, load_index, 0))
    own_force = jnp.sum(load_hot.astype(jnp.float32)[:, None] * load_force, axis=0)
    load_hits = (cell_index == own_index).astype(jnp.float32)
    force_field = (own_force[:, None] * load_hits[None, :]).reshape(
        3, slab_planes, layers, row_width
    )
    displace = displacement[0] * free_cells
    target = volume_share * total_rows * layers * row_width
    padded = neighbour_planes(displace, load_cases, axis_devices)
    halo_density = extended(density, (("space", 0),), window_reach)
    filtered = filter_forward(pad_sides(halo_density), weights) / total_weight
    whole_field = lax.all_gather(filtered, "space", axis=0, tiled=True)
    margin = lax.dynamic_slice_in_dim(
        pad_axis(whole_field, 0, 1, 1), slab_start, slab_planes + 2, 0
    )
    moduli = floor_modulus + (1.0 - floor_modulus) * margin**3
    face_x = 0.5 * (moduli[1:] + moduli[:-1]) * face_valid[:, None, None]
    inner_moduli = moduli[1:-1]
    face_z = 0.5 * (inner_moduli[:, 1:] + inner_moduli[:, :-1])
    face_y = 0.5 * (inner_moduli[:, :, 1:] + inner_moduli[:, :, :-1])
    sum_x = face_x[:-1] + face_x[1:]
    sum_z = pad_axis(face_z, 1, 1, 0) + pad_axis(face_z, 1, 0, 1)
    sum_y = pad_axis(face_y, 2, 1, 0) + pad_axis(face_y, 2, 0, 1)
    diagonal = stiff_factors(0) * sum_x + stiff_factors(1) * sum_z + stiff_factors(2) * sum_y
    for sweep_index in range(SWEEPS):
        displace = relax_slab(
            padded, displace, face_x, face_z, face_y, force_field, free_cells, diagonal
        )
        padded = neighbour_planes(displace, load_cases, axis_devices)
    energy_x = slab_energy(padded, 1, 0, load_cases) * face_valid[:, None, None]
    energy_z = slab_energy(displace, 2, 1, load_cases)
    energy_y = slab_energy(displace, 3, 2, load_cases)
    sens_term = 0.5 * (
        energy_x[:-1]
        + energy_x[1:]
        + pad_axis(energy_z, 1, 1, 0)
        + pad_axis(energy_z, 1, 0, 1)
        + pad_axis(energy_y, 2, 1, 0)
        + pad_axis(energy_y, 2, 0, 1)
    )
    sensitive = sens_term
    for level in reversed(range(level_count)):
        half_rows = sensitive.shape[0] // 2
        upper_side = load_place // 2**level % 2 == 1
        outgoing = jnp.where(upper_side, sensitive[:half_rows], sensitive[half_rows:])
        keeping = jnp.where(upper_side, sensitive[half_rows:], sensitive[:half_rows])
        sensitive = keeping + from_partner(outgoing, "space", level)
    weighted_share = 3.0 * (1.0 - floor_modulus) * filtered**2 * sensitive / total_weight
    halo_share = extended(weighted_share, (("space", 0),), window_reach)
    root_term = jnp.sqrt(filter_backward(pad_sides(halo_share), padded_weights))
    lowest = jnp.maximum(density - move_limit, density_floor)
    highest = jnp.minimum(density + move_limit, 1.0)
    design_now = density

    def trial_design(log_level):
        return jnp.clip(design_now * root_term * jnp.exp(-0.5 * log_level), lowest, highest)

    start_state = (jnp.asarray(log_lower, jnp.float32), jnp.asarray(log_span, jnp.float32))

    def halve(search_step, search_state):
        lower_end, span_width = search_state
        half_span = span_width * 0.5
        middle = lower_end + half_span
        volume_total = lax.psum(jnp.sum(trial_design(middle)), "space")
        return (jnp.where(volume_total > target, middle, lower_end), half_span)

    lower_end, span_width = lax.fori_loop(0, SEARCH, halve, start_state)
    density = trial_design(lower_end + 0.5 * span_width)
    new_displacement = displace[None]
    return (density, new_displacement)


def solution(mesh):
    in_specs = (
        P("space", "parts", None),
        P("space", None, None, "parts", None),
        P(None, "parts"),
        P("parts"),
        P("parts", None),
        P("parts"),
    )
    out_specs = (P("space", "parts", None), P("space", None, None, "parts", None))

    def local(density, displacement, fixed, load_index, load_force, radius):
        alone = lax.axis_size("space") == load_index.shape[0]
        run = one_slab if alone else many_slabs
        return run(density, displacement, fixed, load_index, load_force, radius)

    return jax.shard_map(local, mesh=mesh, in_specs=in_specs, out_specs=out_specs, check_vma=False)
```

```python
import math

import jax
import jax.numpy as jnp
from jax import lax
from jax.experimental import pallas as pl
from jax.experimental.pallas import tpu as pltpu
from jax.sharding import PartitionSpec as P

SWEEPS = 3
SEARCH = 12


floor_modulus = 0.05
relax_factor = 0.6
move_limit = 0.2
density_floor = 0.01
volume_share = 0.5
log_lower = -16.0
log_span = 32.0
window_reach = 2

PLANE_SQUARES = (0, 1, 2, 4, 5, 8)
ALL_SQUARES = (0, 1, 2, 3, 4, 5, 6, 8, 9, 12)


def spot_iota(shape, dim):
    return lax.broadcasted_iota(jnp.int32, shape, dim)


def each_plane(planes, body, carry):
    for x in range(planes):
        carry = body(x, carry)
    return carry


def each_half(planes, body, carry):
    count = planes // 2
    return lax.fori_loop(0, 2, lambda half, carry: body(half * count, count, carry), carry)


def layer_radius(radius_ref, layers, row_width):
    z = spot_iota((layers, row_width), 0)
    result = jnp.zeros((layers, row_width), jnp.int32)
    for layer in range(layers):
        result = jnp.where(z == layer, radius_ref[layer], result)
    return result.astype(jnp.float32)


def class_weights(radius_ref, weight_ref):
    layers, row_width = weight_ref.shape[1:]
    radial = layer_radius(radius_ref, layers, row_width)
    for place, square in enumerate(ALL_SQUARES):
        weight_ref[place] = jnp.maximum(radial - math.sqrt(square), 0.0)


def shift_sum(field, dim, distance):
    size = field.shape[dim]
    spot = spot_iota(field.shape, dim)
    ahead = jnp.where(spot < size - distance, pltpu.roll(field, size - distance, dim), 0.0)
    behind = jnp.where(spot >= distance, pltpu.roll(field, distance, dim), 0.0)
    return ahead + behind


def plane_sums(plane):
    beside = shift_sum(plane, 1, 1)
    further = shift_sum(plane, 1, 2)
    return {
        0: plane,
        1: beside + shift_sum(plane, 0, 1),
        2: shift_sum(beside, 0, 1),
        4: further + shift_sum(plane, 0, 2),
        5: shift_sum(further, 0, 1) + shift_sum(beside, 0, 2),
        8: shift_sum(further, 0, 2),
    }


def weigh(sums, weight_ref, square):
    result = None
    for inner in PLANE_SQUARES:
        term = weight_ref[ALL_SQUARES.index(inner + square)] * sums[inner]
        result = term if result is None else result + term
    return result


def forward_planes(plane, weight_ref):
    sums = plane_sums(plane)
    return [weigh(sums, weight_ref, square) for square in (0, 1, 4)]


def rows(x, layers, shift=0):
    return pl.ds(x * layers + shift, layers)


GAP = 8


def gapped(x, layers, shift=0):
    return pl.ds(GAP + x * (layers + GAP) + shift, layers)


def gap(x, layers):
    return pl.ds(x * (layers + GAP), GAP)


def pair_spot(x, own_planes):
    device = x // own_planes
    apart = device ^ lax.axis_index("space")
    return (apart ^ apart >> 1) & 1, device >> 1, x % own_planes


def half_views(ref, first, count):
    own_planes = ref.shape[2]
    mine = lax.axis_index("space")
    side = (mine ^ mine >> 1) & 1
    chips = pl.ds(first // (2 * own_planes), count // (2 * own_planes))
    views = (ref.at[side, chips], ref.at[1 - side, chips])

    def plane(p):
        device = p // own_planes
        return views[(device ^ device >> 1) & 1], (device >> 1, p % own_planes)

    return plane


def edge_class(x, planes):
    return jnp.minimum(x, 2) + jnp.maximum(x - (planes - 3), 0)


def zero_edges(ref):
    planes = ref.shape[0]
    for place in (0, 1, planes - 2, planes - 1):
        ref[place] = jnp.zeros(ref.shape[1:], ref.dtype)


def prepare_kernel(
    radius_hbm,
    index_hbm,
    force_hbm,
    fixed_hbm,
    weight_ref,
    inverse_ref,
    free_ref,
    load_ref,
    spot_ref,
    radius_ref,
    index_ref,
    force_ref,
    fixed_ref,
    arrived,
):
    copies = [
        pltpu.make_async_copy(source, target, arrived.at[place])
        for place, (source, target) in enumerate(
            (
                (radius_hbm, radius_ref),
                (index_hbm, index_ref),
                (force_hbm, force_ref),
                (fixed_hbm, fixed_ref),
            )
        )
    ]
    for copy in copies:
        copy.start()
    for copy in copies:
        copy.wait()
    planes, layers, row_width = free_ref.shape
    load_place = lax.axis_index("space")
    shape = (layers, row_width)
    z = spot_iota(shape, 0)
    y = spot_iota(shape, 1)

    class_weights(radius_ref, weight_ref)
    ones = forward_planes(jnp.ones(shape, jnp.float32), weight_ref)
    for place, (lower, upper) in enumerate(((0, 2), (1, 2), (2, 2), (2, 1), (2, 0))):
        inverse_ref[place] = 1.0 / (
            ones[0] + min(lower, 1) * ones[1] + min(upper, 1) * ones[1]
            + (lower // 2) * ones[2] + (upper // 2) * ones[2]
        )

    def free_plane(x, carry):
        free_ref[x] = jnp.where(
            z == 0, 1.0 - fixed_ref[pl.ds(x, 1), :].astype(jnp.float32), 1.0
        )
        return carry

    each_plane(planes, free_plane, 0)

    own_index = index_ref[load_place]
    own_z = own_index // row_width % layers
    own_y = own_index % row_width
    hit = (z == own_z) & (y == own_y)
    for part in range(3):
        load_ref[part] = jnp.where(hit, force_ref[part, load_place], 0.0)
    spot_ref[0] = own_index // (layers * row_width)


def sweep_kernel(
    spot_ref,
    load_ref,
    weight_ref,
    inverse_ref,
    free_ref,
    density_ref,
    start_ref,
    disp_ref,
    coef_ref,
    plane_ref,
    beside_ref,
    further_ref,
    near_ref,
    side_ref,
    far_ref,
    modulus_ref,
    across_ref,
    up_ref,
    right_ref,
    left_ref,
    rate_ref,
    first_ref,
):
    planes, layers, row_width = coef_ref.shape
    shape = (layers, row_width)
    z = spot_iota(shape, 0)
    y = spot_iota(shape, 1)
    zero = jnp.zeros(shape, jnp.float32)
    zero_gap = jnp.zeros((GAP, row_width), jnp.float32)

    for ref in (side_ref, far_ref):
        zero_edges(ref)
    def filter_half(first, count, carry):
        density = half_views(density_ref, first, count)
        spread = [
            ref.at[pl.ds(first * (layers + GAP), count * (layers + GAP) + GAP)]
            for ref in (plane_ref, beside_ref, further_ref)
        ]
        results = [ref.at[pl.ds(first + 2, count)] for ref in (near_ref, side_ref, far_ref)]
        for ref in spread:
            ref[gap(0, layers)] = zero_gap
        for p in range(count):
            view, spot = density(p)
            plane = view[spot]
            beside, further = shift_sum(plane, 1, 1), shift_sum(plane, 1, 2)
            for ref, field in zip(spread, (plane, beside, further)):
                ref[gapped(p, layers)] = field
                ref[gap(p + 1, layers)] = zero_gap

            def around(place, distance):
                ref = spread[place]
                return ref[gapped(p, layers, distance)] + ref[gapped(p, layers, -distance)]

            sums = {
                0: plane,
                1: beside + around(0, 1),
                2: around(1, 1),
                4: further + around(0, 2),
                5: around(2, 1) + around(1, 2),
                8: around(2, 2),
            }
            for ref, square in zip(results, (0, 1, 4)):
                ref[p] = weigh(sums, weight_ref, square)
        return carry

    each_half(planes, filter_half, 0)

    for ref in (first_ref, disp_ref):
        for part in range(3):
            ref[part, rows(0, layers)] = zero
            ref[part, rows(planes + 1, layers)] = zero

    def store_faces(slot, modulus, above, later, before, free, start, views):
        across, up_view, right_view, left_view, rate, source = views
        across[slot] = later
        up = jnp.where(z < layers - 1, 0.5 * (modulus + above), 0.0)
        right = jnp.where(
            y < row_width - 1, 0.5 * (modulus + pltpu.roll(modulus, row_width - 1, 1)), 0.0
        )
        left = pltpu.roll(right, 1, 1)
        up_view[rows(slot, layers)] = up
        right_view[slot] = right
        left_view[slot] = left
        sums = (before + later, up + pltpu.roll(up, 1, 0), left + right)
        every = sums[0] + sums[1] + sums[2]
        diagonal = [every + part_sum for part_sum in sums]
        pair = diagonal[0] * diagonal[1]
        push = relax_factor * free / (pair * diagonal[2])
        side = push * diagonal[2]
        for part, factor in enumerate((side * diagonal[1], side * diagonal[0], push * pair)):
            rate[part, slot] = factor
            source[part, rows(slot, layers)] = start[part] * free

    def modulus_half(first, count, carry):
        near = near_ref.at[pl.ds(first + 2, count)]
        side = side_ref.at[pl.ds(first + 1, count + 2)]
        far = far_ref.at[pl.ds(first, count + 4)]
        moduli = modulus_ref.at[pl.ds(first * layers, (count + 1) * layers)]
        coef = coef_ref.at[pl.ds(first, count)]
        free = free_ref.at[pl.ds(first, count)]
        views = (
            across_ref.at[pl.ds(first, count)],
            up_ref.at[pl.ds(first * layers, count * layers)],
            right_ref.at[pl.ds(first, count)],
            left_ref.at[pl.ds(first, count)],
            rate_ref.at[:, pl.ds(first, count)],
            first_ref.at[:, pl.ds(first * layers, count * layers)],
        )
        modulus, before = carry
        for p in range(count):
            inverse = inverse_ref[edge_class(first + p, planes)]
            filtered = near[p] + side[p] + side[p + 2] + far[p] + far[p + 4]
            filtered = filtered * inverse
            later = floor_modulus + (1.0 - floor_modulus) * (filtered * filtered * filtered)
            coef[p] = 3.0 * (1.0 - floor_modulus) * (filtered * filtered) * inverse
            moduli[rows(p + 1, layers)] = later
            ahead = 0.5 * (modulus + later)
            if p == 0:
                ahead = jnp.where(first > 0, ahead, 0.0)
            above = moduli[rows(p, layers, 1)] if p else pltpu.roll(modulus, layers - 1, 0)
            previous = jnp.maximum(first + p - 1, 0)
            store_faces(
                p,
                modulus,
                above,
                ahead,
                before,
                free_ref[previous],
                [start_ref[part, previous] for part in range(3)],
                views,
            )
            modulus, before = later, ahead
        return modulus, before

    modulus, before = each_half(planes, modulus_half, (jnp.ones(shape, jnp.float32), zero))
    store_faces(
        planes,
        modulus,
        pltpu.roll(modulus, layers - 1, 0),
        zero,
        before,
        free_ref[planes - 1],
        [start_ref[part, planes - 1] for part in range(3)],
        (across_ref, up_ref, right_ref, left_ref, rate_ref, first_ref),
    )

    own_x = spot_ref[0]

    def sweep(source, target):
        def sweep_half(first, count, carry):
            old = source.at[:, pl.ds(first * layers, (count + 2) * layers)]
            new = target.at[:, pl.ds((first + 1) * layers, count * layers)]
            across = across_ref.at[pl.ds(first, count + 1)]
            up = up_ref.at[pl.ds(first * layers, (count + 1) * layers)]
            right = right_ref.at[pl.ds(first + 1, count)]
            left = left_ref.at[pl.ds(first + 1, count)]
            rate = rate_ref.at[:, pl.ds(first + 1, count)]
            behind = [old[part, rows(0, layers)] for part in range(3)]
            here = [old[part, rows(1, layers)] for part in range(3)]
            for p in range(count):
                ahead = [old[part, rows(p + 2, layers)] for part in range(3)]
                for part in range(3):
                    pulls = [
                        across[p] * behind[part] + across[p + 1] * ahead[part],
                        up[rows(p + 1, layers)] * old[part, rows(p + 1, layers, 1)]
                        + up[rows(p + 1, layers, -1)] * old[part, rows(p + 1, layers, -1)],
                        right[p] * pltpu.roll(here[part], row_width - 1, 1)
                        + left[p] * pltpu.roll(here[part], 1, 1),
                    ]
                    pull = pulls[0] + pulls[1] + pulls[2] + pulls[part]
                    new[part, rows(p, layers)] = (
                        1.0 - relax_factor
                    ) * here[part] + rate[part, p] * pull
                behind, here = here, ahead
            return carry

        each_half(planes, sweep_half, 0)
        for part in range(3):
            target[part, rows(own_x + 1, layers)] += rate_ref[part, own_x + 1] * load_ref[part]

    def two_sweeps(turn, carry):
        sweep(first_ref, disp_ref)

        @pl.when(turn < SWEEPS // 2)
        def _():
            sweep(disp_ref, first_ref)

        return carry

    lax.fori_loop(0, SWEEPS // 2 + 1, two_sweeps, 0)


def energy_planes(group, disp_ref, sens_ref):
    chips, own_planes, layers, row_width = sens_ref.shape
    planes = disp_ref.shape[1] // layers - 2
    load_cases = lax.axis_size("space")
    shape = (layers, row_width)
    z = spot_iota(shape, 0)
    y = spot_iota(shape, 1)
    zero = jnp.zeros(shape, jnp.float32)
    mine = lax.axis_index("space")
    core = mine ^ mine >> 1 ^ group

    def between(x):
        result = zero
        for part in range(3):
            step = disp_ref[part, rows(x + 1, layers)] - disp_ref[part, rows(x, layers)]
            result = result + (2.0 if part == 0 else 1.0) * (step * step)
        return jnp.where((x > 0) & (x < planes), result, 0.0)

    def inside(x):
        upward, right = zero, zero
        for part in range(3):
            here = disp_ref[part, rows(x + 1, layers)]
            climb = disp_ref[part, rows(x + 1, layers, 1)] - here
            slide = pltpu.roll(here, row_width - 1, 1) - here
            upward = upward + (2.0 if part == 1 else 1.0) * (climb * climb)
            right = right + (2.0 if part == 2 else 1.0) * (slide * slide)
        upward = jnp.where(z < layers - 1, upward, 0.0)
        right = jnp.where(y < row_width - 1, right, 0.0)
        return upward + pltpu.roll(upward, 1, 0) + right + pltpu.roll(right, 1, 1)

    for chip in range(chips):
        first = own_planes * (2 * chip + ((core ^ chip) & 1))
        before = between(first)
        for own in range(own_planes):
            after = between(first + own + 1)
            sens_ref[chip, own] = (0.5 / load_cases) * (before + after + inside(first + own))
            before = after


def sent_energy_kernel(disp_ref, sens_ref):
    energy_planes(1, disp_ref, sens_ref)


def kept_energy_kernel(disp_ref, disp_hbm, sens_ref, stored):
    layers = sens_ref.shape[2]
    inner = pl.ds(layers, disp_ref.shape[1] - 2 * layers)
    store = pltpu.make_async_copy(disp_ref.at[:, inner], disp_hbm, stored)
    store.start()
    energy_planes(0, disp_ref, sens_ref)
    store.wait()


def design_kernel(
    weight_ref,
    sens_ref,
    coef_ref,
    density_ref,
    new_ref,
    plane_ref,
    beside_ref,
    further_ref,
    near_ref,
    far_ref,
    pull_ref,
    low_ref,
    high_ref,
):
    planes, layers, row_width = coef_ref.shape
    own_planes = density_ref.shape[2]
    place = lax.axis_index("space")
    shape = (layers, row_width)
    zero = jnp.zeros(shape, jnp.float32)
    zero_gap = jnp.zeros((GAP, row_width), jnp.float32)
    for ref in (plane_ref, beside_ref, further_ref):
        zero_edges(ref)

    def spread_half(first, count, carry):
        sens = half_views(sens_ref, first, count)
        coef = coef_ref.at[pl.ds(first, count)]
        plane_view, beside, further = (
            ref.at[pl.ds(first + 2, count)] for ref in (plane_ref, beside_ref, further_ref)
        )
        for p in range(count):
            view, spot = sens(p)
            plane = view[spot] * coef[p]
            plane_view[p] = plane
            beside[p] = shift_sum(plane, 1, 1)
            further[p] = shift_sum(plane, 1, 2)
        return carry

    each_half(planes, spread_half, 0)

    def root_half(first, count, carry):
        density_at = half_views(density_ref, first, count)
        plane_view, beside, further = (
            ref.at[pl.ds(first, count + 4)] for ref in (plane_ref, beside_ref, further_ref)
        )
        near, far = (
            ref.at[pl.ds(first * (layers + GAP), count * (layers + GAP) + GAP)]
            for ref in (near_ref, far_ref)
        )
        for ref in (near, far):
            ref[gap(0, layers)] = zero_gap
        pull, low, high = (
            ref.at[pl.ds(first, count)] for ref in (pull_ref, low_ref, high_ref)
        )
        for p in range(count):

            def around(ref, distance):
                return ref[p + 2 + distance] + ref[p + 2 - distance]

            sums = {
                0: plane_view[p + 2],
                1: beside[p + 2] + around(plane_view, 1),
                2: around(beside, 1),
                4: further[p + 2] + around(plane_view, 2),
                5: around(further, 1) + around(beside, 2),
                8: around(further, 2),
            }
            level = weigh(sums, weight_ref, 0)
            for ref, square in ((near, 1), (far, 4)):
                ref[gapped(p, layers)] = weigh(sums, weight_ref, square)
                ref[gap(p + 1, layers)] = zero_gap
            root = jnp.sqrt(
                level
                + near[gapped(p, layers, 1)]
                + near[gapped(p, layers, -1)]
                + far[gapped(p, layers, 2)]
                + far[gapped(p, layers, -2)]
            )
            view, spot = density_at(p)
            density = view[spot]
            pull[p] = density * root
            low[p] = jnp.maximum(density - move_limit, density_floor)
            high[p] = jnp.minimum(density + move_limit, 1.0)
        return carry

    each_half(planes, root_half, 0)

    target = volume_share * planes * layers * row_width

    def trial(x, factor):
        return jnp.minimum(jnp.maximum(pull_ref[x] * factor, low_ref[x]), high_ref[x])

    def factor_of(log_level):
        return jnp.broadcast_to(jnp.exp(-0.5 * log_level), shape)

    def exceeds(total):
        return jnp.sum(jnp.sum(total, axis=0, keepdims=True), axis=1, keepdims=True) > target

    def halve_twice(step, state):
        lower, span = state
        half, quarter = span * 0.5, span * 0.25
        middles = (lower + quarter, lower + half, lower + half + quarter)
        factors = [factor_of(middle) for middle in middles]
        totals = [zero, zero, zero]
        for x in range(planes):
            pull, low, high = pull_ref[x], low_ref[x], high_ref[x]
            totals = [
                total + jnp.minimum(jnp.maximum(pull * factor, low), high)
                for total, factor in zip(totals, factors)
            ]
        first, second, third = (exceeds(total) for total in totals)
        upper = jnp.where(third, middles[2], middles[1])
        below = jnp.where(first, middles[0], lower)
        return jnp.where(second, upper, below), quarter

    start = (jnp.full((1, 1), log_lower, jnp.float32), jnp.full((1, 1), log_span, jnp.float32))
    lower, span = lax.fori_loop(0, SEARCH // 2, halve_twice, start)
    factor = factor_of(lower + 0.5 * span)
    for own in range(own_planes):
        new_ref[own] = trial(place * own_planes + own, factor)


def in_vmem():
    return pl.BlockSpec(memory_space=pltpu.VMEM)


def in_smem():
    return pl.BlockSpec(memory_space=pltpu.SMEM)


KERNEL_VMEM = 24 * 2**20


def floats(*shape):
    return jax.ShapeDtypeStruct(shape, jnp.float32)


def prepare_call(radius, load_index, load_force, fixed):
    planes, row_width = fixed.shape
    layers = radius.shape[0]
    return pl.pallas_call(
        prepare_kernel,
        out_shape=[
            floats(len(ALL_SQUARES), layers, row_width),
            floats(2 * window_reach + 1, layers, row_width),
            floats(planes, layers, row_width),
            floats(3, layers, row_width),
            jax.ShapeDtypeStruct((1,), jnp.int32),
        ],
        in_specs=[pl.BlockSpec(memory_space=pltpu.HBM)] * 4,
        out_specs=[in_vmem()] * 4 + [in_smem()],
        scratch_shapes=[
            pltpu.SMEM(radius.shape, radius.dtype),
            pltpu.SMEM(load_index.shape, load_index.dtype),
            pltpu.SMEM(load_force.shape, load_force.dtype),
            pltpu.VMEM(fixed.shape, fixed.dtype),
            pltpu.SemaphoreType.DMA((4,)),
        ],
        compiler_params=pltpu.CompilerParams(vmem_limit_bytes=KERNEL_VMEM),
        cost_estimate=pl.CostEstimate(
            flops=40 * planes * layers * row_width,
            bytes_accessed=8 * planes * layers * row_width,
            transcendentals=0,
        ),
        name="prepare",
    )(
        *(
            pltpu.with_memory_space_constraint(array, pltpu.HBM)
            for array in (radius, load_index, load_force, fixed)
        )
    )


def sweep_call(spot, load, weights, inverses, free, density, displacement):
    cores, chips, own_planes, layers, row_width = density.shape
    planes = cores * chips * own_planes

    def scratch(*lead):
        return pltpu.VMEM(lead + (row_width,), jnp.float32)

    return pl.pallas_call(
        sweep_kernel,
        out_shape=[
            floats(3, (planes + 2) * layers, row_width),
            floats(planes, layers, row_width),
        ],
        in_specs=[in_smem()] + [in_vmem()] * 6,
        out_specs=[in_vmem()] * 2,
        scratch_shapes=[
            scratch(planes * (layers + GAP) + GAP),
            scratch(planes * (layers + GAP) + GAP),
            scratch(planes * (layers + GAP) + GAP),
            scratch(planes + 4, layers),
            scratch(planes + 4, layers),
            scratch(planes + 4, layers),
            scratch((planes + 1) * layers),
            scratch(planes + 1, layers),
            scratch((planes + 1) * layers),
            scratch(planes + 1, layers),
            scratch(planes + 1, layers),
            scratch(3, planes + 1, layers),
            scratch(3, (planes + 2) * layers),
        ],
        compiler_params=pltpu.CompilerParams(vmem_limit_bytes=KERNEL_VMEM),
        name="sweeps",
    )(spot, load, weights, inverses, free, density, displacement)


def sent_energy_call(disp, group_shape):
    return pl.pallas_call(
        sent_energy_kernel,
        out_shape=floats(*group_shape),
        in_specs=[in_vmem()],
        out_specs=in_vmem(),
        compiler_params=pltpu.CompilerParams(vmem_limit_bytes=KERNEL_VMEM),
        name="sent_energy",
    )(disp)


def kept_energy_call(disp, group_shape):
    parts, disp_rows, row_width = disp.shape
    layers = group_shape[2]
    return pl.pallas_call(
        kept_energy_kernel,
        out_shape=[floats(parts, disp_rows - 2 * layers, row_width), floats(*group_shape)],
        in_specs=[in_vmem()],
        out_specs=[pl.BlockSpec(memory_space=pltpu.HBM), in_vmem()],
        scratch_shapes=[pltpu.SemaphoreType.DMA(())],
        compiler_params=pltpu.CompilerParams(vmem_limit_bytes=KERNEL_VMEM),
        cost_estimate=pl.CostEstimate(
            flops=20 * disp.size, bytes_accessed=8 * disp.size, transcendentals=0
        ),
        name="kept_energy",
    )(disp)


def design_call(weights, sens, coef, density):
    cores, chips, own_planes, layers, row_width = density.shape
    planes = cores * chips * own_planes

    def scratch(*lead):
        return pltpu.VMEM(lead + (row_width,), jnp.float32)

    return pl.pallas_call(
        design_kernel,
        out_shape=floats(own_planes, layers, row_width),
        in_specs=[in_vmem()] * 4,
        out_specs=in_vmem(),
        scratch_shapes=[
            scratch(planes + 4, layers),
            scratch(planes + 4, layers),
            scratch(planes + 4, layers),
            scratch(planes * (layers + GAP) + GAP),
            scratch(planes * (layers + GAP) + GAP),
            scratch(planes, layers),
            scratch(planes, layers),
            scratch(planes, layers),
        ],
        compiler_params=pltpu.CompilerParams(vmem_limit_bytes=KERNEL_VMEM),
        name="design",
    )(weights, sens, coef, density)


def other_core(block):
    devices = lax.axis_size("space")
    return lax.ppermute(block, "space", [(i, i ^ 1) for i in range(devices)])


def chip_groups():
    chips = lax.axis_size("space") // 2
    return [[2 * chip + (chip ^ group) % 2 for chip in range(chips)] for group in range(2)]


def between_chips(pieces):
    return lax.all_to_all(pieces, "space", 0, 0, axis_index_groups=chip_groups())


def chip_gathered(block):
    chips = lax.axis_size("space") // 2
    return between_chips(jnp.broadcast_to(block[None], (chips,) + block.shape))


def with_other_core(blocks):
    return jnp.stack([blocks, other_core(blocks)])


def scattered_sum(sent, make_kept):
    received = other_core(sent)
    *others, kept = make_kept()
    return jnp.sum(between_chips(kept + received), axis=0), others


def one_slab(density, displacement, fixed, load_index, load_force, radius):
    same_group, small = lax.optimization_barrier(
        (chip_gathered(density), (radius, load_index, load_force.T, fixed))
    )
    whole = with_other_core(same_group)
    weights, inverses, free, load, spot = prepare_call(*small)
    disp, coef = sweep_call(spot, load, weights, inverses, free, whole, displacement[0])
    sent, disp = lax.optimization_barrier((sent_energy_call(disp, same_group.shape), disp))
    sens, (new_displacement,) = scattered_sum(
        sent, lambda: kept_energy_call(disp, same_group.shape)
    )
    sens = with_other_core(chip_gathered(sens))
    new_density = design_call(weights, sens, coef, whole)
    return new_density, new_displacement.reshape(displacement.shape)


def from_behind(block, axis, distance):
    devices = range(lax.axis_size(axis))
    route = [(i - distance, i) for i in devices if i - distance in devices]
    return lax.ppermute(block, axis, route)


def extended(x, sides, width):
    for axis, dim in sides:
        size, length = (lax.axis_size(axis), x.shape[dim])
        up = [(i, (i + 1) % size) for i in range(size - 1)]
        down = [(j, i) for i, j in up]
        last = lax.slice_in_dim(x, length - width, length, axis=dim)
        first = lax.slice_in_dim(x, 0, width, axis=dim)
        before = lax.ppermute(last, axis, up)
        after = lax.ppermute(first, axis, down)
        x = jnp.concatenate([before, x, after], axis=dim)
    return x


def from_partner(x, axis, bit):
    return lax.ppermute(x, axis, [(i, i ^ 1 << bit) for i in range(lax.axis_size(axis))])


def window_offsets():
    offsets_list = []
    for across in range(-window_reach, window_reach + 1):
        for upward in range(-window_reach, window_reach + 1):
            for sideways in range(-window_reach, window_reach + 1):
                length = math.sqrt(across * across + upward * upward + sideways * sideways)
                offsets_list.append((across, upward, sideways, length))
    return offsets_list


def layer_weights(radius):
    radial = radius.astype(jnp.float32)
    return jnp.stack(
        [jnp.maximum(radial - length, 0.0) for across, upward, sideways, length in window_offsets()]
    )


def pad_axis(grid_field, along_axis, before, after_cells):
    widths = [(0, 0)] * grid_field.ndim
    widths[along_axis] = (before, after_cells)
    return jnp.pad(grid_field, widths)


def pad_sides(grid_field):
    return jnp.pad(grid_field, ((0, 0), (window_reach, window_reach), (window_reach, window_reach)))


def filter_forward(padded, weights):
    out_rows = padded.shape[0] - 2 * window_reach
    layers = padded.shape[1] - 2 * window_reach
    row_width = padded.shape[2] - 2 * window_reach
    result = jnp.zeros((out_rows, layers, row_width), jnp.float32)
    for offset_index, (across, upward, sideways, length) in enumerate(window_offsets()):
        shifted = padded[
            window_reach + across : window_reach + across + out_rows,
            window_reach + upward : window_reach + upward + layers,
            window_reach + sideways : window_reach + sideways + row_width,
        ]
        result = result + weights[offset_index][None, :, None] * shifted
    return result


def filter_backward(padded, padded_weights):
    out_rows = padded.shape[0] - 2 * window_reach
    layers = padded.shape[1] - 2 * window_reach
    row_width = padded.shape[2] - 2 * window_reach
    result = jnp.zeros((out_rows, layers, row_width), jnp.float32)
    for offset_index, (across, upward, sideways, length) in enumerate(window_offsets()):
        shifted = padded[
            window_reach - across : window_reach - across + out_rows,
            window_reach - upward : window_reach - upward + layers,
            window_reach - sideways : window_reach - sideways + row_width,
        ]
        layer_part = padded_weights[
            offset_index, window_reach - upward : window_reach - upward + layers
        ]
        result = result + layer_part[None, :, None] * shifted
    return result


def stiff_factors(direction):
    return jnp.array(
        [2.0 if component == direction else 1.0 for component in range(3)], jnp.float32
    ).reshape(3, 1, 1, 1)


def relax_slab(padded, displace, face_x, face_z, face_y, force_field, free_cells, diagonal):
    flux_x = stiff_factors(0) * face_x * jnp.diff(padded, axis=1)
    stencil_image = flux_x[:, :-1] - flux_x[:, 1:]
    flux_z = stiff_factors(1) * face_z * jnp.diff(displace, axis=2)
    stencil_image = stencil_image + pad_axis(flux_z, 2, 1, 0) - pad_axis(flux_z, 2, 0, 1)
    flux_y = stiff_factors(2) * face_y * jnp.diff(displace, axis=3)
    stencil_image = stencil_image + pad_axis(flux_y, 3, 1, 0) - pad_axis(flux_y, 3, 0, 1)
    return free_cells * (displace + relax_factor * (force_field - stencil_image) / diagonal)


def slab_energy(grid_field, along_axis, direction, load_cases):
    change = jnp.diff(grid_field, axis=along_axis)
    return jnp.sum(stiff_factors(direction) * change * change, axis=0) / load_cases


def neighbour_planes(displace, load_cases, axis_devices):
    if axis_devices > load_cases:
        below = from_behind(displace[:, -1:], "space", load_cases)
        above = from_behind(displace[:, :1], "space", -load_cases)
    else:
        below = jnp.zeros_like(displace[:, :1])
        above = jnp.zeros_like(displace[:, :1])
    return jnp.concatenate([below, displace, above], axis=1)


def many_slabs(density, displacement, fixed, load_index, load_force, radius):
    slab_rows, layers, row_width = density.shape
    load_cases = load_index.shape[0]
    level_count = load_cases.bit_length() - 1
    axis_devices = lax.axis_size("space")
    axis_place = lax.axis_index("space")
    slab_planes = slab_rows * load_cases
    slab_place = axis_place // load_cases
    load_place = axis_place % load_cases
    total_rows = slab_rows * axis_devices
    weights = layer_weights(radius)
    padded_weights = pad_axis(weights, 1, window_reach, window_reach)
    global_rows = (
        jnp.arange(slab_rows + 2 * window_reach, dtype=jnp.int32)
        + axis_place * slab_rows
        - window_reach
    )
    deep_inside = ((global_rows >= 0) & (global_rows < total_rows)).astype(jnp.float32)
    inside_field = deep_inside[:, None, None] * pad_sides(
        jnp.ones((slab_rows + 2 * window_reach, layers, row_width), jnp.float32)
    )
    total_weight = filter_forward(inside_field, weights)
    slab_start = slab_place * slab_planes
    margin_rows = jnp.arange(slab_planes + 2, dtype=jnp.int32) + slab_start - 1
    margin_inside = ((margin_rows >= 0) & (margin_rows < total_rows)).astype(jnp.float32)
    face_valid = margin_inside[1:] * margin_inside[:-1]
    fixed_slab = lax.dynamic_slice_in_dim(fixed, slab_start, slab_planes, 0).astype(jnp.float32)
    bottom_layer = (jnp.arange(layers, dtype=jnp.int32) == 0).astype(jnp.float32)
    free_cells = 1.0 - bottom_layer[None, :, None] * fixed_slab[:, None, :]
    slab_cells = slab_planes * layers * row_width
    cell_index = jnp.arange(slab_cells, dtype=jnp.int32) + slab_place * slab_cells
    load_hot = jnp.arange(load_cases, dtype=jnp.int32) == load_place
    own_index = jnp.sum(jnp.where(load_hot, load_index, 0))
    own_force = jnp.sum(load_hot.astype(jnp.float32)[:, None] * load_force, axis=0)
    load_hits = (cell_index == own_index).astype(jnp.float32)
    force_field = (own_force[:, None] * load_hits[None, :]).reshape(
        3, slab_planes, layers, row_width
    )
    displace = displacement[0] * free_cells
    target = volume_share * total_rows * layers * row_width
    padded = neighbour_planes(displace, load_cases, axis_devices)
    halo_density = extended(density, (("space", 0),), window_reach)
    filtered = filter_forward(pad_sides(halo_density), weights) / total_weight
    whole_field = lax.all_gather(filtered, "space", axis=0, tiled=True)
    margin = lax.dynamic_slice_in_dim(
        pad_axis(whole_field, 0, 1, 1), slab_start, slab_planes + 2, 0
    )
    moduli = floor_modulus + (1.0 - floor_modulus) * margin**3
    face_x = 0.5 * (moduli[1:] + moduli[:-1]) * face_valid[:, None, None]
    inner_moduli = moduli[1:-1]
    face_z = 0.5 * (inner_moduli[:, 1:] + inner_moduli[:, :-1])
    face_y = 0.5 * (inner_moduli[:, :, 1:] + inner_moduli[:, :, :-1])
    sum_x = face_x[:-1] + face_x[1:]
    sum_z = pad_axis(face_z, 1, 1, 0) + pad_axis(face_z, 1, 0, 1)
    sum_y = pad_axis(face_y, 2, 1, 0) + pad_axis(face_y, 2, 0, 1)
    diagonal = stiff_factors(0) * sum_x + stiff_factors(1) * sum_z + stiff_factors(2) * sum_y
    for sweep_index in range(SWEEPS):
        displace = relax_slab(
            padded, displace, face_x, face_z, face_y, force_field, free_cells, diagonal
        )
        padded = neighbour_planes(displace, load_cases, axis_devices)
    energy_x = slab_energy(padded, 1, 0, load_cases) * face_valid[:, None, None]
    energy_z = slab_energy(displace, 2, 1, load_cases)
    energy_y = slab_energy(displace, 3, 2, load_cases)
    sens_term = 0.5 * (
        energy_x[:-1]
        + energy_x[1:]
        + pad_axis(energy_z, 1, 1, 0)
        + pad_axis(energy_z, 1, 0, 1)
        + pad_axis(energy_y, 2, 1, 0)
        + pad_axis(energy_y, 2, 0, 1)
    )
    sensitive = sens_term
    for level in reversed(range(level_count)):
        half_rows = sensitive.shape[0] // 2
        upper_side = load_place // 2**level % 2 == 1
        outgoing = jnp.where(upper_side, sensitive[:half_rows], sensitive[half_rows:])
        keeping = jnp.where(upper_side, sensitive[half_rows:], sensitive[:half_rows])
        sensitive = keeping + from_partner(outgoing, "space", level)
    weighted_share = 3.0 * (1.0 - floor_modulus) * filtered**2 * sensitive / total_weight
    halo_share = extended(weighted_share, (("space", 0),), window_reach)
    root_term = jnp.sqrt(filter_backward(pad_sides(halo_share), padded_weights))
    lowest = jnp.maximum(density - move_limit, density_floor)
    highest = jnp.minimum(density + move_limit, 1.0)
    design_now = density

    def trial_design(log_level):
        return jnp.clip(design_now * root_term * jnp.exp(-0.5 * log_level), lowest, highest)

    start_state = (jnp.asarray(log_lower, jnp.float32), jnp.asarray(log_span, jnp.float32))

    def halve(search_step, search_state):
        lower_end, span_width = search_state
        half_span = span_width * 0.5
        middle = lower_end + half_span
        volume_total = lax.psum(jnp.sum(trial_design(middle)), "space")
        return (jnp.where(volume_total > target, middle, lower_end), half_span)

    lower_end, span_width = lax.fori_loop(0, SEARCH, halve, start_state)
    density = trial_design(lower_end + 0.5 * span_width)
    new_displacement = displace[None]
    return (density, new_displacement)


def solution(mesh):
    in_specs = (
        P("space", "parts", None),
        P("space", None, None, "parts", None),
        P(None, "parts"),
        P("parts"),
        P("parts", None),
        P("parts"),
    )
    out_specs = (P("space", "parts", None), P("space", None, None, "parts", None))

    def local(density, displacement, fixed, load_index, load_force, radius):
        alone = lax.axis_size("space") == load_index.shape[0]
        run = one_slab if alone else many_slabs
        return run(density, displacement, fixed, load_index, load_force, radius)

    return jax.shard_map(local, mesh=mesh, in_specs=in_specs, out_specs=out_specs, check_vma=False)
```

```python
import math

import jax
import jax.numpy as jnp
from jax import lax
from jax.experimental import pallas as pl
from jax.experimental.pallas import tpu as pltpu
from jax.sharding import PartitionSpec as P

SWEEPS = 3
SEARCH = 12


floor_modulus = 0.05
relax_factor = 0.6
move_limit = 0.2
density_floor = 0.01
volume_share = 0.5
log_lower = -16.0
log_span = 32.0
window_reach = 2

PLANE_SQUARES = (0, 1, 2, 4, 5, 8)
ALL_SQUARES = (0, 1, 2, 3, 4, 5, 6, 8, 9, 12)


def spot_iota(shape, dim):
    return lax.broadcasted_iota(jnp.int32, shape, dim)


def each_plane(planes, body, carry):
    for x in range(planes):
        carry = body(x, carry)
    return carry


def each_half(planes, body, carry):
    count = planes // 2
    return lax.fori_loop(0, 2, lambda half, carry: body(half * count, count, carry), carry)


def layer_radius(radius_ref, layers, row_width):
    z = spot_iota((layers, row_width), 0)
    result = jnp.zeros((layers, row_width), jnp.int32)
    for layer in range(layers):
        result = jnp.where(z == layer, radius_ref[layer], result)
    return result.astype(jnp.float32)


def class_weights(radius_ref, weight_ref):
    layers, row_width = weight_ref.shape[1:]
    radial = layer_radius(radius_ref, layers, row_width)
    for place, square in enumerate(ALL_SQUARES):
        weight_ref[place] = jnp.maximum(radial - math.sqrt(square), 0.0)


def shift_sum(field, dim, distance):
    size = field.shape[dim]
    spot = spot_iota(field.shape, dim)
    ahead = jnp.where(spot < size - distance, pltpu.roll(field, size - distance, dim), 0.0)
    behind = jnp.where(spot >= distance, pltpu.roll(field, distance, dim), 0.0)
    return ahead + behind


def plane_sums(plane):
    beside = shift_sum(plane, 1, 1)
    further = shift_sum(plane, 1, 2)
    return {
        0: plane,
        1: beside + shift_sum(plane, 0, 1),
        2: shift_sum(beside, 0, 1),
        4: further + shift_sum(plane, 0, 2),
        5: shift_sum(further, 0, 1) + shift_sum(beside, 0, 2),
        8: shift_sum(further, 0, 2),
    }


def weigh(sums, weight_ref, square):
    result = None
    for inner in PLANE_SQUARES:
        term = weight_ref[ALL_SQUARES.index(inner + square)] * sums[inner]
        result = term if result is None else result + term
    return result


def forward_planes(plane, weight_ref):
    sums = plane_sums(plane)
    return [weigh(sums, weight_ref, square) for square in (0, 1, 4)]


def rows(x, layers, shift=0):
    return pl.ds(x * layers + shift, layers)


GAP = 8


def gapped(x, layers, shift=0):
    return pl.ds(GAP + x * (layers + GAP) + shift, layers)


def gap(x, layers):
    return pl.ds(x * (layers + GAP), GAP)


def pair_spot(x, own_planes):
    device = x // own_planes
    apart = device ^ lax.axis_index("space")
    return (apart ^ apart >> 1) & 1, device >> 1, x % own_planes


def half_views(ref, first, count):
    own_planes = ref.shape[2]
    mine = lax.axis_index("space")
    side = (mine ^ mine >> 1) & 1
    chips = pl.ds(first // (2 * own_planes), count // (2 * own_planes))
    views = (ref.at[side, chips], ref.at[1 - side, chips])

    def plane(p):
        device = p // own_planes
        return views[(device ^ device >> 1) & 1], (device >> 1, p % own_planes)

    return plane


def edge_class(x, planes):
    return jnp.minimum(x, 2) + jnp.maximum(x - (planes - 3), 0)


def zero_edges(ref):
    planes = ref.shape[0]
    for place in (0, 1, planes - 2, planes - 1):
        ref[place] = jnp.zeros(ref.shape[1:], ref.dtype)


def prepare_kernel(
    radius_hbm,
    index_hbm,
    force_hbm,
    fixed_hbm,
    weight_ref,
    inverse_ref,
    free_ref,
    load_ref,
    spot_ref,
    radius_ref,
    index_ref,
    force_ref,
    fixed_ref,
    arrived,
):
    copies = [
        pltpu.make_async_copy(source, target, arrived.at[place])
        for place, (source, target) in enumerate(
            (
                (radius_hbm, radius_ref),
                (index_hbm, index_ref),
                (force_hbm, force_ref),
                (fixed_hbm, fixed_ref),
            )
        )
    ]
    for copy in copies:
        copy.start()
    for copy in copies:
        copy.wait()
    planes, layers, row_width = free_ref.shape
    load_place = lax.axis_index("space")
    shape = (layers, row_width)
    z = spot_iota(shape, 0)
    y = spot_iota(shape, 1)

    class_weights(radius_ref, weight_ref)
    ones = forward_planes(jnp.ones(shape, jnp.float32), weight_ref)
    for place, (lower, upper) in enumerate(((0, 2), (1, 2), (2, 2), (2, 1), (2, 0))):
        inverse_ref[place] = 1.0 / (
            ones[0] + min(lower, 1) * ones[1] + min(upper, 1) * ones[1]
            + (lower // 2) * ones[2] + (upper // 2) * ones[2]
        )

    def free_plane(x, carry):
        free_ref[x] = jnp.where(
            z == 0, 1.0 - fixed_ref[pl.ds(x, 1), :].astype(jnp.float32), 1.0
        )
        return carry

    each_plane(planes, free_plane, 0)

    own_index = index_ref[load_place]
    own_z = own_index // row_width % layers
    own_y = own_index % row_width
    hit = (z == own_z) & (y == own_y)
    for part in range(3):
        load_ref[part] = jnp.where(hit, force_ref[part, load_place], 0.0)
    own_x = (own_index // (layers * row_width)).astype(jnp.float32)
    spot_ref[...] = jnp.full(spot_ref.shape, own_x)


def sweep_kernel(
    spot_ref,
    load_ref,
    weight_ref,
    inverse_ref,
    free_ref,
    density_ref,
    start_ref,
    disp_ref,
    coef_ref,
    plane_ref,
    beside_ref,
    further_ref,
    near_ref,
    side_ref,
    far_ref,
    modulus_ref,
    across_ref,
    up_ref,
    right_ref,
    left_ref,
    rate_ref,
    first_ref,
):
    planes, layers, row_width = coef_ref.shape
    shape = (layers, row_width)
    z = spot_iota(shape, 0)
    y = spot_iota(shape, 1)
    zero = jnp.zeros(shape, jnp.float32)
    zero_gap = jnp.zeros((GAP, row_width), jnp.float32)

    for ref in (side_ref, far_ref):
        zero_edges(ref)
    def filter_half(first, count, carry):
        density = half_views(density_ref, first, count)
        spread = [
            ref.at[pl.ds(first * (layers + GAP), count * (layers + GAP) + GAP)]
            for ref in (plane_ref, beside_ref, further_ref)
        ]
        results = [ref.at[pl.ds(first + 2, count)] for ref in (near_ref, side_ref, far_ref)]
        for ref in spread:
            ref[gap(0, layers)] = zero_gap
        for p in range(count):
            view, spot = density(p)
            plane = view[spot]
            beside, further = shift_sum(plane, 1, 1), shift_sum(plane, 1, 2)
            for ref, field in zip(spread, (plane, beside, further)):
                ref[gapped(p, layers)] = field
                ref[gap(p + 1, layers)] = zero_gap

            def around(place, distance):
                ref = spread[place]
                return ref[gapped(p, layers, distance)] + ref[gapped(p, layers, -distance)]

            sums = {
                0: plane,
                1: beside + around(0, 1),
                2: around(1, 1),
                4: further + around(0, 2),
                5: around(2, 1) + around(1, 2),
                8: around(2, 2),
            }
            for ref, square in zip(results, (0, 1, 4)):
                ref[p] = weigh(sums, weight_ref, square)
        return carry

    each_half(planes, filter_half, 0)

    for ref in (first_ref, disp_ref):
        for part in range(3):
            ref[part, rows(0, layers)] = zero
            ref[part, rows(planes + 1, layers)] = zero

    def store_faces(slot, modulus, above, later, before, free, start, views):
        across, up_view, right_view, left_view, rate, source = views
        across[slot] = later
        up = jnp.where(z < layers - 1, 0.5 * (modulus + above), 0.0)
        right = jnp.where(
            y < row_width - 1, 0.5 * (modulus + pltpu.roll(modulus, row_width - 1, 1)), 0.0
        )
        left = pltpu.roll(right, 1, 1)
        up_view[rows(slot, layers)] = up
        right_view[slot] = right
        left_view[slot] = left
        sums = (before + later, up + pltpu.roll(up, 1, 0), left + right)
        every = sums[0] + sums[1] + sums[2]
        diagonal = [every + part_sum for part_sum in sums]
        pair = diagonal[0] * diagonal[1]
        push = relax_factor * free / (pair * diagonal[2])
        side = push * diagonal[2]
        for part, factor in enumerate((side * diagonal[1], side * diagonal[0], push * pair)):
            rate[part, slot] = factor
            source[part, rows(slot, layers)] = start[part] * free

    def modulus_half(first, count, carry):
        near = near_ref.at[pl.ds(first + 2, count)]
        side = side_ref.at[pl.ds(first + 1, count + 2)]
        far = far_ref.at[pl.ds(first, count + 4)]
        moduli = modulus_ref.at[pl.ds(first * layers, (count + 1) * layers)]
        coef = coef_ref.at[pl.ds(first, count)]
        free = free_ref.at[pl.ds(first, count)]
        views = (
            across_ref.at[pl.ds(first, count)],
            up_ref.at[pl.ds(first * layers, count * layers)],
            right_ref.at[pl.ds(first, count)],
            left_ref.at[pl.ds(first, count)],
            rate_ref.at[:, pl.ds(first, count)],
            first_ref.at[:, pl.ds(first * layers, count * layers)],
        )
        modulus, before = carry
        for p in range(count):
            inverse = inverse_ref[edge_class(first + p, planes)]
            filtered = near[p] + side[p] + side[p + 2] + far[p] + far[p + 4]
            filtered = filtered * inverse
            later = floor_modulus + (1.0 - floor_modulus) * (filtered * filtered * filtered)
            coef[p] = 3.0 * (1.0 - floor_modulus) * (filtered * filtered) * inverse
            moduli[rows(p + 1, layers)] = later
            ahead = 0.5 * (modulus + later)
            if p == 0:
                ahead = jnp.where(first > 0, ahead, 0.0)
            above = moduli[rows(p, layers, 1)] if p else pltpu.roll(modulus, layers - 1, 0)
            previous = jnp.maximum(first + p - 1, 0)
            store_faces(
                p,
                modulus,
                above,
                ahead,
                before,
                free_ref[previous],
                [start_ref[part, previous] for part in range(3)],
                views,
            )
            modulus, before = later, ahead
        return modulus, before

    modulus, before = each_half(planes, modulus_half, (jnp.ones(shape, jnp.float32), zero))
    store_faces(
        planes,
        modulus,
        pltpu.roll(modulus, layers - 1, 0),
        zero,
        before,
        free_ref[planes - 1],
        [start_ref[part, planes - 1] for part in range(3)],
        (across_ref, up_ref, right_ref, left_ref, rate_ref, first_ref),
    )

    own_x = jnp.max(spot_ref[...]).astype(jnp.int32)

    def sweep(source, target):
        def sweep_half(first, count, carry):
            old = source.at[:, pl.ds(first * layers, (count + 2) * layers)]
            new = target.at[:, pl.ds((first + 1) * layers, count * layers)]
            across = across_ref.at[pl.ds(first, count + 1)]
            up = up_ref.at[pl.ds(first * layers, (count + 1) * layers)]
            right = right_ref.at[pl.ds(first + 1, count)]
            left = left_ref.at[pl.ds(first + 1, count)]
            rate = rate_ref.at[:, pl.ds(first + 1, count)]
            behind = [old[part, rows(0, layers)] for part in range(3)]
            here = [old[part, rows(1, layers)] for part in range(3)]
            for p in range(count):
                ahead = [old[part, rows(p + 2, layers)] for part in range(3)]
                for part in range(3):
                    pulls = [
                        across[p] * behind[part] + across[p + 1] * ahead[part],
                        up[rows(p + 1, layers)] * old[part, rows(p + 1, layers, 1)]
                        + up[rows(p + 1, layers, -1)] * old[part, rows(p + 1, layers, -1)],
                        right[p] * pltpu.roll(here[part], row_width - 1, 1)
                        + left[p] * pltpu.roll(here[part], 1, 1),
                    ]
                    pull = pulls[0] + pulls[1] + pulls[2] + pulls[part]
                    new[part, rows(p, layers)] = (
                        1.0 - relax_factor
                    ) * here[part] + rate[part, p] * pull
                behind, here = here, ahead
            return carry

        each_half(planes, sweep_half, 0)
        for part in range(3):
            target[part, rows(own_x + 1, layers)] += rate_ref[part, own_x + 1] * load_ref[part]

    def two_sweeps(turn, carry):
        sweep(first_ref, disp_ref)

        @pl.when(turn < SWEEPS // 2)
        def _():
            sweep(disp_ref, first_ref)

        return carry

    lax.fori_loop(0, SWEEPS // 2 + 1, two_sweeps, 0)


def energy_planes(group, disp_ref, sens_ref):
    chips, own_planes, layers, row_width = sens_ref.shape
    planes = disp_ref.shape[1] // layers - 2
    load_cases = lax.axis_size("space")
    shape = (layers, row_width)
    z = spot_iota(shape, 0)
    y = spot_iota(shape, 1)
    zero = jnp.zeros(shape, jnp.float32)
    mine = lax.axis_index("space")
    core = mine ^ mine >> 1 ^ group

    def between(x):
        result = zero
        for part in range(3):
            step = disp_ref[part, rows(x + 1, layers)] - disp_ref[part, rows(x, layers)]
            result = result + (2.0 if part == 0 else 1.0) * (step * step)
        return jnp.where((x > 0) & (x < planes), result, 0.0)

    def inside(x):
        upward, right = zero, zero
        for part in range(3):
            here = disp_ref[part, rows(x + 1, layers)]
            climb = disp_ref[part, rows(x + 1, layers, 1)] - here
            slide = pltpu.roll(here, row_width - 1, 1) - here
            upward = upward + (2.0 if part == 1 else 1.0) * (climb * climb)
            right = right + (2.0 if part == 2 else 1.0) * (slide * slide)
        upward = jnp.where(z < layers - 1, upward, 0.0)
        right = jnp.where(y < row_width - 1, right, 0.0)
        return upward + pltpu.roll(upward, 1, 0) + right + pltpu.roll(right, 1, 1)

    for chip in range(chips):
        first = own_planes * (2 * chip + ((core ^ chip) & 1))
        before = between(first)
        for own in range(own_planes):
            after = between(first + own + 1)
            sens_ref[chip, own] = (0.5 / load_cases) * (before + after + inside(first + own))
            before = after


def sent_energy_kernel(disp_ref, sens_ref):
    energy_planes(1, disp_ref, sens_ref)


def kept_energy_kernel(disp_ref, disp_hbm, sens_ref, stored):
    layers = sens_ref.shape[2]
    inner = pl.ds(layers, disp_ref.shape[1] - 2 * layers)
    store = pltpu.make_async_copy(disp_ref.at[:, inner], disp_hbm, stored)
    store.start()
    energy_planes(0, disp_ref, sens_ref)
    store.wait()


def design_kernel(
    weight_ref,
    sens_ref,
    coef_ref,
    density_ref,
    new_ref,
    plane_ref,
    beside_ref,
    further_ref,
    near_ref,
    far_ref,
    pull_ref,
    low_ref,
    high_ref,
):
    planes, layers, row_width = coef_ref.shape
    own_planes = density_ref.shape[2]
    place = lax.axis_index("space")
    shape = (layers, row_width)
    zero = jnp.zeros(shape, jnp.float32)
    zero_gap = jnp.zeros((GAP, row_width), jnp.float32)
    for ref in (plane_ref, beside_ref, further_ref):
        zero_edges(ref)

    def spread_half(first, count, carry):
        sens = half_views(sens_ref, first, count)
        coef = coef_ref.at[pl.ds(first, count)]
        plane_view, beside, further = (
            ref.at[pl.ds(first + 2, count)] for ref in (plane_ref, beside_ref, further_ref)
        )
        for p in range(count):
            view, spot = sens(p)
            plane = view[spot] * coef[p]
            plane_view[p] = plane
            beside[p] = shift_sum(plane, 1, 1)
            further[p] = shift_sum(plane, 1, 2)
        return carry

    each_half(planes, spread_half, 0)

    def root_half(first, count, carry):
        density_at = half_views(density_ref, first, count)
        plane_view, beside, further = (
            ref.at[pl.ds(first, count + 4)] for ref in (plane_ref, beside_ref, further_ref)
        )
        near, far = (
            ref.at[pl.ds(first * (layers + GAP), count * (layers + GAP) + GAP)]
            for ref in (near_ref, far_ref)
        )
        for ref in (near, far):
            ref[gap(0, layers)] = zero_gap
        pull, low, high = (
            ref.at[pl.ds(first, count)] for ref in (pull_ref, low_ref, high_ref)
        )
        for p in range(count):

            def around(ref, distance):
                return ref[p + 2 + distance] + ref[p + 2 - distance]

            sums = {
                0: plane_view[p + 2],
                1: beside[p + 2] + around(plane_view, 1),
                2: around(beside, 1),
                4: further[p + 2] + around(plane_view, 2),
                5: around(further, 1) + around(beside, 2),
                8: around(further, 2),
            }
            level = weigh(sums, weight_ref, 0)
            for ref, square in ((near, 1), (far, 4)):
                ref[gapped(p, layers)] = weigh(sums, weight_ref, square)
                ref[gap(p + 1, layers)] = zero_gap
            root = jnp.sqrt(
                level
                + near[gapped(p, layers, 1)]
                + near[gapped(p, layers, -1)]
                + far[gapped(p, layers, 2)]
                + far[gapped(p, layers, -2)]
            )
            view, spot = density_at(p)
            density = view[spot]
            pull[p] = density * root
            low[p] = jnp.maximum(density - move_limit, density_floor)
            high[p] = jnp.minimum(density + move_limit, 1.0)
        return carry

    each_half(planes, root_half, 0)

    target = volume_share * planes * layers * row_width

    def trial(x, factor):
        return jnp.minimum(jnp.maximum(pull_ref[x] * factor, low_ref[x]), high_ref[x])

    def factor_of(log_level):
        return jnp.broadcast_to(jnp.exp(-0.5 * log_level), shape)

    def exceeds(total):
        return jnp.sum(jnp.sum(total, axis=0, keepdims=True), axis=1, keepdims=True) > target

    def halve_twice(step, state):
        lower, span = state
        half, quarter = span * 0.5, span * 0.25
        middles = (lower + quarter, lower + half, lower + half + quarter)
        factors = [factor_of(middle) for middle in middles]
        totals = [zero, zero, zero]
        for x in range(planes):
            pull, low, high = pull_ref[x], low_ref[x], high_ref[x]
            totals = [
                total + jnp.minimum(jnp.maximum(pull * factor, low), high)
                for total, factor in zip(totals, factors)
            ]
        first, second, third = (exceeds(total) for total in totals)
        upper = jnp.where(third, middles[2], middles[1])
        below = jnp.where(first, middles[0], lower)
        return jnp.where(second, upper, below), quarter

    start = (jnp.full((1, 1), log_lower, jnp.float32), jnp.full((1, 1), log_span, jnp.float32))
    lower, span = lax.fori_loop(0, SEARCH // 2, halve_twice, start)
    factor = factor_of(lower + 0.5 * span)
    for own in range(own_planes):
        new_ref[own] = trial(place * own_planes + own, factor)


def in_vmem():
    return pl.BlockSpec(memory_space=pltpu.VMEM)


KERNEL_VMEM = 24 * 2**20


def floats(*shape):
    return jax.ShapeDtypeStruct(shape, jnp.float32)


def prepare_call(radius, load_index, load_force, fixed):
    planes, row_width = fixed.shape
    layers = radius.shape[0]
    return pl.pallas_call(
        prepare_kernel,
        out_shape=[
            floats(len(ALL_SQUARES), layers, row_width),
            floats(2 * window_reach + 1, layers, row_width),
            floats(planes, layers, row_width),
            floats(3, layers, row_width),
            floats(8, row_width),
        ],
        in_specs=[pl.BlockSpec(memory_space=pltpu.HBM)] * 4,
        out_specs=[in_vmem()] * 5,
        scratch_shapes=[
            pltpu.SMEM(radius.shape, radius.dtype),
            pltpu.SMEM(load_index.shape, load_index.dtype),
            pltpu.SMEM(load_force.shape, load_force.dtype),
            pltpu.VMEM(fixed.shape, fixed.dtype),
            pltpu.SemaphoreType.DMA((4,)),
        ],
        compiler_params=pltpu.CompilerParams(vmem_limit_bytes=KERNEL_VMEM),
        cost_estimate=pl.CostEstimate(
            flops=40 * planes * layers * row_width,
            bytes_accessed=8 * planes * layers * row_width,
            transcendentals=0,
        ),
        name="prepare",
    )(
        *(
            pltpu.with_memory_space_constraint(array, pltpu.HBM)
            for array in (radius, load_index, load_force, fixed)
        )
    )


def sweep_call(spot, load, weights, inverses, free, density, displacement):
    cores, chips, own_planes, layers, row_width = density.shape
    planes = cores * chips * own_planes

    def scratch(*lead):
        return pltpu.VMEM(lead + (row_width,), jnp.float32)

    return pl.pallas_call(
        sweep_kernel,
        out_shape=[
            floats(3, (planes + 2) * layers, row_width),
            floats(planes, layers, row_width),
        ],
        in_specs=[in_vmem()] * 7,
        out_specs=[in_vmem()] * 2,
        scratch_shapes=[
            scratch(planes * (layers + GAP) + GAP),
            scratch(planes * (layers + GAP) + GAP),
            scratch(planes * (layers + GAP) + GAP),
            scratch(planes + 4, layers),
            scratch(planes + 4, layers),
            scratch(planes + 4, layers),
            scratch((planes + 1) * layers),
            scratch(planes + 1, layers),
            scratch((planes + 1) * layers),
            scratch(planes + 1, layers),
            scratch(planes + 1, layers),
            scratch(3, planes + 1, layers),
            scratch(3, (planes + 2) * layers),
        ],
        compiler_params=pltpu.CompilerParams(vmem_limit_bytes=KERNEL_VMEM),
        name="sweeps",
    )(spot, load, weights, inverses, free, density, displacement)


def sent_energy_call(disp, group_shape):
    return pl.pallas_call(
        sent_energy_kernel,
        out_shape=floats(*group_shape),
        in_specs=[in_vmem()],
        out_specs=in_vmem(),
        compiler_params=pltpu.CompilerParams(vmem_limit_bytes=KERNEL_VMEM),
        name="sent_energy",
    )(disp)


def kept_energy_call(disp, group_shape):
    parts, disp_rows, row_width = disp.shape
    layers = group_shape[2]
    return pl.pallas_call(
        kept_energy_kernel,
        out_shape=[floats(parts, disp_rows - 2 * layers, row_width), floats(*group_shape)],
        in_specs=[in_vmem()],
        out_specs=[pl.BlockSpec(memory_space=pltpu.HBM), in_vmem()],
        scratch_shapes=[pltpu.SemaphoreType.DMA(())],
        compiler_params=pltpu.CompilerParams(vmem_limit_bytes=KERNEL_VMEM),
        cost_estimate=pl.CostEstimate(
            flops=20 * disp.size, bytes_accessed=8 * disp.size, transcendentals=0
        ),
        name="kept_energy",
    )(disp)


def design_call(weights, sens, coef, density):
    cores, chips, own_planes, layers, row_width = density.shape
    planes = cores * chips * own_planes

    def scratch(*lead):
        return pltpu.VMEM(lead + (row_width,), jnp.float32)

    return pl.pallas_call(
        design_kernel,
        out_shape=floats(own_planes, layers, row_width),
        in_specs=[in_vmem()] * 4,
        out_specs=in_vmem(),
        scratch_shapes=[
            scratch(planes + 4, layers),
            scratch(planes + 4, layers),
            scratch(planes + 4, layers),
            scratch(planes * (layers + GAP) + GAP),
            scratch(planes * (layers + GAP) + GAP),
            scratch(planes, layers),
            scratch(planes, layers),
            scratch(planes, layers),
        ],
        compiler_params=pltpu.CompilerParams(vmem_limit_bytes=KERNEL_VMEM),
        name="design",
    )(weights, sens, coef, density)


def other_core(block):
    devices = lax.axis_size("space")
    return lax.ppermute(block, "space", [(i, i ^ 1) for i in range(devices)])


def chip_groups():
    chips = lax.axis_size("space") // 2
    return [[2 * chip + (chip ^ group) % 2 for chip in range(chips)] for group in range(2)]


def between_chips(pieces):
    return lax.all_to_all(pieces, "space", 0, 0, axis_index_groups=chip_groups())


def chip_gathered(block):
    chips = lax.axis_size("space") // 2
    return between_chips(jnp.broadcast_to(block[None], (chips,) + block.shape))


def with_other_core(blocks):
    return jnp.stack([blocks, other_core(blocks)])


def scattered_sum(sent, make_kept):
    received = other_core(sent)
    *others, kept = make_kept()
    return jnp.sum(between_chips(kept + received), axis=0), others


def one_slab(density, displacement, fixed, load_index, load_force, radius):
    same_group, small = lax.optimization_barrier(
        (chip_gathered(density), (radius, load_index, load_force.T, fixed))
    )
    whole = with_other_core(same_group)
    weights, inverses, free, load, spot = prepare_call(*small)
    disp, coef = sweep_call(spot, load, weights, inverses, free, whole, displacement[0])
    sent, disp = lax.optimization_barrier((sent_energy_call(disp, same_group.shape), disp))
    sens, (new_displacement,) = scattered_sum(
        sent, lambda: kept_energy_call(disp, same_group.shape)
    )
    sens = with_other_core(chip_gathered(sens))
    new_density = design_call(weights, sens, coef, whole)
    return new_density, new_displacement.reshape(displacement.shape)


def from_behind(block, axis, distance):
    devices = range(lax.axis_size(axis))
    route = [(i - distance, i) for i in devices if i - distance in devices]
    return lax.ppermute(block, axis, route)


def extended(x, sides, width):
    for axis, dim in sides:
        size, length = (lax.axis_size(axis), x.shape[dim])
        up = [(i, (i + 1) % size) for i in range(size - 1)]
        down = [(j, i) for i, j in up]
        last = lax.slice_in_dim(x, length - width, length, axis=dim)
        first = lax.slice_in_dim(x, 0, width, axis=dim)
        before = lax.ppermute(last, axis, up)
        after = lax.ppermute(first, axis, down)
        x = jnp.concatenate([before, x, after], axis=dim)
    return x


def from_partner(x, axis, bit):
    return lax.ppermute(x, axis, [(i, i ^ 1 << bit) for i in range(lax.axis_size(axis))])


def window_offsets():
    offsets_list = []
    for across in range(-window_reach, window_reach + 1):
        for upward in range(-window_reach, window_reach + 1):
            for sideways in range(-window_reach, window_reach + 1):
                length = math.sqrt(across * across + upward * upward + sideways * sideways)
                offsets_list.append((across, upward, sideways, length))
    return offsets_list


def layer_weights(radius):
    radial = radius.astype(jnp.float32)
    return jnp.stack(
        [jnp.maximum(radial - length, 0.0) for across, upward, sideways, length in window_offsets()]
    )


def pad_axis(grid_field, along_axis, before, after_cells):
    widths = [(0, 0)] * grid_field.ndim
    widths[along_axis] = (before, after_cells)
    return jnp.pad(grid_field, widths)


def pad_sides(grid_field):
    return jnp.pad(grid_field, ((0, 0), (window_reach, window_reach), (window_reach, window_reach)))


def filter_forward(padded, weights):
    out_rows = padded.shape[0] - 2 * window_reach
    layers = padded.shape[1] - 2 * window_reach
    row_width = padded.shape[2] - 2 * window_reach
    result = jnp.zeros((out_rows, layers, row_width), jnp.float32)
    for offset_index, (across, upward, sideways, length) in enumerate(window_offsets()):
        shifted = padded[
            window_reach + across : window_reach + across + out_rows,
            window_reach + upward : window_reach + upward + layers,
            window_reach + sideways : window_reach + sideways + row_width,
        ]
        result = result + weights[offset_index][None, :, None] * shifted
    return result


def filter_backward(padded, padded_weights):
    out_rows = padded.shape[0] - 2 * window_reach
    layers = padded.shape[1] - 2 * window_reach
    row_width = padded.shape[2] - 2 * window_reach
    result = jnp.zeros((out_rows, layers, row_width), jnp.float32)
    for offset_index, (across, upward, sideways, length) in enumerate(window_offsets()):
        shifted = padded[
            window_reach - across : window_reach - across + out_rows,
            window_reach - upward : window_reach - upward + layers,
            window_reach - sideways : window_reach - sideways + row_width,
        ]
        layer_part = padded_weights[
            offset_index, window_reach - upward : window_reach - upward + layers
        ]
        result = result + layer_part[None, :, None] * shifted
    return result


def stiff_factors(direction):
    return jnp.array(
        [2.0 if component == direction else 1.0 for component in range(3)], jnp.float32
    ).reshape(3, 1, 1, 1)


def relax_slab(padded, displace, face_x, face_z, face_y, force_field, free_cells, diagonal):
    flux_x = stiff_factors(0) * face_x * jnp.diff(padded, axis=1)
    stencil_image = flux_x[:, :-1] - flux_x[:, 1:]
    flux_z = stiff_factors(1) * face_z * jnp.diff(displace, axis=2)
    stencil_image = stencil_image + pad_axis(flux_z, 2, 1, 0) - pad_axis(flux_z, 2, 0, 1)
    flux_y = stiff_factors(2) * face_y * jnp.diff(displace, axis=3)
    stencil_image = stencil_image + pad_axis(flux_y, 3, 1, 0) - pad_axis(flux_y, 3, 0, 1)
    return free_cells * (displace + relax_factor * (force_field - stencil_image) / diagonal)


def slab_energy(grid_field, along_axis, direction, load_cases):
    change = jnp.diff(grid_field, axis=along_axis)
    return jnp.sum(stiff_factors(direction) * change * change, axis=0) / load_cases


def neighbour_planes(displace, load_cases, axis_devices):
    if axis_devices > load_cases:
        below = from_behind(displace[:, -1:], "space", load_cases)
        above = from_behind(displace[:, :1], "space", -load_cases)
    else:
        below = jnp.zeros_like(displace[:, :1])
        above = jnp.zeros_like(displace[:, :1])
    return jnp.concatenate([below, displace, above], axis=1)


def many_slabs(density, displacement, fixed, load_index, load_force, radius):
    slab_rows, layers, row_width = density.shape
    load_cases = load_index.shape[0]
    level_count = load_cases.bit_length() - 1
    axis_devices = lax.axis_size("space")
    axis_place = lax.axis_index("space")
    slab_planes = slab_rows * load_cases
    slab_place = axis_place // load_cases
    load_place = axis_place % load_cases
    total_rows = slab_rows * axis_devices
    weights = layer_weights(radius)
    padded_weights = pad_axis(weights, 1, window_reach, window_reach)
    global_rows = (
        jnp.arange(slab_rows + 2 * window_reach, dtype=jnp.int32)
        + axis_place * slab_rows
        - window_reach
    )
    deep_inside = ((global_rows >= 0) & (global_rows < total_rows)).astype(jnp.float32)
    inside_field = deep_inside[:, None, None] * pad_sides(
        jnp.ones((slab_rows + 2 * window_reach, layers, row_width), jnp.float32)
    )
    total_weight = filter_forward(inside_field, weights)
    slab_start = slab_place * slab_planes
    margin_rows = jnp.arange(slab_planes + 2, dtype=jnp.int32) + slab_start - 1
    margin_inside = ((margin_rows >= 0) & (margin_rows < total_rows)).astype(jnp.float32)
    face_valid = margin_inside[1:] * margin_inside[:-1]
    fixed_slab = lax.dynamic_slice_in_dim(fixed, slab_start, slab_planes, 0).astype(jnp.float32)
    bottom_layer = (jnp.arange(layers, dtype=jnp.int32) == 0).astype(jnp.float32)
    free_cells = 1.0 - bottom_layer[None, :, None] * fixed_slab[:, None, :]
    slab_cells = slab_planes * layers * row_width
    cell_index = jnp.arange(slab_cells, dtype=jnp.int32) + slab_place * slab_cells
    load_hot = jnp.arange(load_cases, dtype=jnp.int32) == load_place
    own_index = jnp.sum(jnp.where(load_hot, load_index, 0))
    own_force = jnp.sum(load_hot.astype(jnp.float32)[:, None] * load_force, axis=0)
    load_hits = (cell_index == own_index).astype(jnp.float32)
    force_field = (own_force[:, None] * load_hits[None, :]).reshape(
        3, slab_planes, layers, row_width
    )
    displace = displacement[0] * free_cells
    target = volume_share * total_rows * layers * row_width
    padded = neighbour_planes(displace, load_cases, axis_devices)
    halo_density = extended(density, (("space", 0),), window_reach)
    filtered = filter_forward(pad_sides(halo_density), weights) / total_weight
    whole_field = lax.all_gather(filtered, "space", axis=0, tiled=True)
    margin = lax.dynamic_slice_in_dim(
        pad_axis(whole_field, 0, 1, 1), slab_start, slab_planes + 2, 0
    )
    moduli = floor_modulus + (1.0 - floor_modulus) * margin**3
    face_x = 0.5 * (moduli[1:] + moduli[:-1]) * face_valid[:, None, None]
    inner_moduli = moduli[1:-1]
    face_z = 0.5 * (inner_moduli[:, 1:] + inner_moduli[:, :-1])
    face_y = 0.5 * (inner_moduli[:, :, 1:] + inner_moduli[:, :, :-1])
    sum_x = face_x[:-1] + face_x[1:]
    sum_z = pad_axis(face_z, 1, 1, 0) + pad_axis(face_z, 1, 0, 1)
    sum_y = pad_axis(face_y, 2, 1, 0) + pad_axis(face_y, 2, 0, 1)
    diagonal = stiff_factors(0) * sum_x + stiff_factors(1) * sum_z + stiff_factors(2) * sum_y
    for sweep_index in range(SWEEPS):
        displace = relax_slab(
            padded, displace, face_x, face_z, face_y, force_field, free_cells, diagonal
        )
        padded = neighbour_planes(displace, load_cases, axis_devices)
    energy_x = slab_energy(padded, 1, 0, load_cases) * face_valid[:, None, None]
    energy_z = slab_energy(displace, 2, 1, load_cases)
    energy_y = slab_energy(displace, 3, 2, load_cases)
    sens_term = 0.5 * (
        energy_x[:-1]
        + energy_x[1:]
        + pad_axis(energy_z, 1, 1, 0)
        + pad_axis(energy_z, 1, 0, 1)
        + pad_axis(energy_y, 2, 1, 0)
        + pad_axis(energy_y, 2, 0, 1)
    )
    sensitive = sens_term
    for level in reversed(range(level_count)):
        half_rows = sensitive.shape[0] // 2
        upper_side = load_place // 2**level % 2 == 1
        outgoing = jnp.where(upper_side, sensitive[:half_rows], sensitive[half_rows:])
        keeping = jnp.where(upper_side, sensitive[half_rows:], sensitive[:half_rows])
        sensitive = keeping + from_partner(outgoing, "space", level)
    weighted_share = 3.0 * (1.0 - floor_modulus) * filtered**2 * sensitive / total_weight
    halo_share = extended(weighted_share, (("space", 0),), window_reach)
    root_term = jnp.sqrt(filter_backward(pad_sides(halo_share), padded_weights))
    lowest = jnp.maximum(density - move_limit, density_floor)
    highest = jnp.minimum(density + move_limit, 1.0)
    design_now = density

    def trial_design(log_level):
        return jnp.clip(design_now * root_term * jnp.exp(-0.5 * log_level), lowest, highest)

    start_state = (jnp.asarray(log_lower, jnp.float32), jnp.asarray(log_span, jnp.float32))

    def halve(search_step, search_state):
        lower_end, span_width = search_state
        half_span = span_width * 0.5
        middle = lower_end + half_span
        volume_total = lax.psum(jnp.sum(trial_design(middle)), "space")
        return (jnp.where(volume_total > target, middle, lower_end), half_span)

    lower_end, span_width = lax.fori_loop(0, SEARCH, halve, start_state)
    density = trial_design(lower_end + 0.5 * span_width)
    new_displacement = displace[None]
    return (density, new_displacement)


def solution(mesh):
    in_specs = (
        P("space", "parts", None),
        P("space", None, None, "parts", None),
        P(None, "parts"),
        P("parts"),
        P("parts", None),
        P("parts"),
    )
    out_specs = (P("space", "parts", None), P("space", None, None, "parts", None))

    def local(density, displacement, fixed, load_index, load_force, radius):
        alone = lax.axis_size("space") == load_index.shape[0]
        run = one_slab if alone else many_slabs
        return run(density, displacement, fixed, load_index, load_force, radius)

    return jax.shard_map(local, mesh=mesh, in_specs=in_specs, out_specs=out_specs, check_vma=False)
```

```python
import math

import jax
import jax.numpy as jnp
from jax import lax
from jax.experimental import pallas as pl
from jax.experimental.pallas import tpu as pltpu
from jax.sharding import PartitionSpec as P

SWEEPS = 3
SEARCH = 12


floor_modulus = 0.05
relax_factor = 0.6
move_limit = 0.2
density_floor = 0.01
volume_share = 0.5
log_lower = -16.0
log_span = 32.0
window_reach = 2

PLANE_SQUARES = (0, 1, 2, 4, 5, 8)
ALL_SQUARES = (0, 1, 2, 3, 4, 5, 6, 8, 9, 12)


def spot_iota(shape, dim):
    return lax.broadcasted_iota(jnp.int32, shape, dim)


def each_plane(planes, body, carry):
    for x in range(planes):
        carry = body(x, carry)
    return carry


def each_half(planes, body, carry):
    count = planes // 2
    return lax.fori_loop(0, 2, lambda half, carry: body(half * count, count, carry), carry)


def layer_radius(radius_ref, layers, row_width):
    z = spot_iota((layers, row_width), 0)
    result = jnp.zeros((layers, row_width), jnp.int32)
    for layer in range(layers):
        result = jnp.where(z == layer, radius_ref[layer], result)
    return result.astype(jnp.float32)


def class_weights(radius_ref, weight_ref):
    layers, row_width = weight_ref.shape[1:]
    radial = layer_radius(radius_ref, layers, row_width)
    for place, square in enumerate(ALL_SQUARES):
        weight_ref[place] = jnp.maximum(radial - math.sqrt(square), 0.0)


def shift_sum(field, dim, distance):
    size = field.shape[dim]
    spot = spot_iota(field.shape, dim)
    ahead = jnp.where(spot < size - distance, pltpu.roll(field, size - distance, dim), 0.0)
    behind = jnp.where(spot >= distance, pltpu.roll(field, distance, dim), 0.0)
    return ahead + behind


def plane_sums(plane):
    beside = shift_sum(plane, 1, 1)
    further = shift_sum(plane, 1, 2)
    return {
        0: plane,
        1: beside + shift_sum(plane, 0, 1),
        2: shift_sum(beside, 0, 1),
        4: further + shift_sum(plane, 0, 2),
        5: shift_sum(further, 0, 1) + shift_sum(beside, 0, 2),
        8: shift_sum(further, 0, 2),
    }


def weigh(sums, weight_ref, square):
    result = None
    for inner in PLANE_SQUARES:
        term = weight_ref[ALL_SQUARES.index(inner + square)] * sums[inner]
        result = term if result is None else result + term
    return result


def forward_planes(plane, weight_ref):
    sums = plane_sums(plane)
    return [weigh(sums, weight_ref, square) for square in (0, 1, 4)]


def rows(x, layers, shift=0):
    return pl.ds(x * layers + shift, layers)


GAP = 8


def gapped(x, layers, shift=0):
    return pl.ds(GAP + x * (layers + GAP) + shift, layers)


def gap(x, layers):
    return pl.ds(x * (layers + GAP), GAP)


def pair_spot(x, own_planes):
    device = x // own_planes
    apart = device ^ lax.axis_index("space")
    return (apart ^ apart >> 1) & 1, device >> 1, x % own_planes


def half_views(ref, first, count):
    own_planes = ref.shape[2]
    mine = lax.axis_index("space")
    side = (mine ^ mine >> 1) & 1
    chips = pl.ds(first // (2 * own_planes), count // (2 * own_planes))
    views = (ref.at[side, chips], ref.at[1 - side, chips])

    def plane(p):
        device = p // own_planes
        return views[(device ^ device >> 1) & 1], (device >> 1, p % own_planes)

    return plane


def edge_class(x, planes):
    return jnp.minimum(x, 2) + jnp.maximum(x - (planes - 3), 0)


def zero_edges(ref):
    planes = ref.shape[0]
    for place in (0, 1, planes - 2, planes - 1):
        ref[place] = jnp.zeros(ref.shape[1:], ref.dtype)


def group_spots(group, blocks):
    chips, own_planes = blocks.shape[:2]
    mine = lax.axis_index("space")
    core = mine ^ mine >> 1 ^ group
    return [
        (own_planes * (2 * chip + ((core ^ chip) & 1)) + own, (chip, own))
        for chip in range(chips)
        for own in range(own_planes)
    ]


def spread_group(blocks, spread):
    chips, own_planes, layers, row_width = blocks.shape
    zero_gap = jnp.zeros((GAP, row_width), jnp.float32)
    for ref in spread:
        ref[gap(0, layers)] = zero_gap
    for p in range(chips * own_planes):
        plane = blocks[p // own_planes, p % own_planes]
        for ref, field in zip(spread, (plane, shift_sum(plane, 1, 1), shift_sum(plane, 1, 2))):
            ref[gapped(p, layers)] = field
            ref[gap(p + 1, layers)] = zero_gap


def filter_plane(p, layers, spread, weight_ref):
    def around(place, distance):
        ref = spread[place]
        return ref[gapped(p, layers, distance)] + ref[gapped(p, layers, -distance)]

    sums = {
        0: spread[0][gapped(p, layers)],
        1: spread[1][gapped(p, layers)] + around(0, 1),
        2: around(1, 1),
        4: spread[2][gapped(p, layers)] + around(0, 2),
        5: around(2, 1) + around(1, 2),
        8: around(2, 2),
    }
    return [weigh(sums, weight_ref, square) for square in (0, 1, 4)]


def prepare_kernel(
    radius_hbm,
    index_hbm,
    force_hbm,
    fixed_hbm,
    density_ref,
    weight_ref,
    inverse_ref,
    free_ref,
    load_ref,
    spot_ref,
    filter_ref,
    radius_ref,
    index_ref,
    force_ref,
    fixed_ref,
    plane_ref,
    beside_ref,
    further_ref,
    arrived,
):
    copies = [
        pltpu.make_async_copy(source, target, arrived.at[place])
        for place, (source, target) in enumerate(
            (
                (radius_hbm, radius_ref),
                (index_hbm, index_ref),
                (force_hbm, force_ref),
                (fixed_hbm, fixed_ref),
            )
        )
    ]
    for copy in copies:
        copy.start()
    spread = (plane_ref, beside_ref, further_ref)
    spread_group(density_ref, spread)
    for copy in copies:
        copy.wait()
    planes, layers, row_width = free_ref.shape
    load_place = lax.axis_index("space")
    shape = (layers, row_width)
    z = spot_iota(shape, 0)
    y = spot_iota(shape, 1)

    class_weights(radius_ref, weight_ref)
    own_planes = density_ref.shape[1]
    for p in range(density_ref.shape[0] * own_planes):
        for place, field in enumerate(filter_plane(p, layers, spread, weight_ref)):
            filter_ref[place, p // own_planes, p % own_planes] = field

    ones = forward_planes(jnp.ones(shape, jnp.float32), weight_ref)
    for place, (lower, upper) in enumerate(((0, 2), (1, 2), (2, 2), (2, 1), (2, 0))):
        inverse_ref[place] = 1.0 / (
            ones[0] + min(lower, 1) * ones[1] + min(upper, 1) * ones[1]
            + (lower // 2) * ones[2] + (upper // 2) * ones[2]
        )

    def free_plane(x, carry):
        free_ref[x] = jnp.where(
            z == 0, 1.0 - fixed_ref[pl.ds(x, 1), :].astype(jnp.float32), 1.0
        )
        return carry

    each_plane(planes, free_plane, 0)

    own_index = index_ref[load_place]
    own_z = own_index // row_width % layers
    own_y = own_index % row_width
    hit = (z == own_z) & (y == own_y)
    for part in range(3):
        load_ref[part] = jnp.where(hit, force_ref[part, load_place], 0.0)
    own_x = (own_index // (layers * row_width)).astype(jnp.float32)
    spot_ref[...] = jnp.full(spot_ref.shape, own_x)


def sweep_kernel(
    spot_ref,
    load_ref,
    weight_ref,
    inverse_ref,
    free_ref,
    filter_ref,
    density_ref,
    start_ref,
    disp_ref,
    coef_ref,
    plane_ref,
    beside_ref,
    further_ref,
    near_ref,
    side_ref,
    far_ref,
    modulus_ref,
    across_ref,
    up_ref,
    right_ref,
    left_ref,
    rate_ref,
    first_ref,
):
    planes, layers, row_width = coef_ref.shape
    shape = (layers, row_width)
    z = spot_iota(shape, 0)
    y = spot_iota(shape, 1)
    zero = jnp.zeros(shape, jnp.float32)

    for ref in (side_ref, far_ref):
        zero_edges(ref)
    results = (near_ref, side_ref, far_ref)
    for x, spot in group_spots(0, density_ref):
        for place, ref in enumerate(results):
            ref[x + 2] = filter_ref[(place,) + spot]
    spread = (plane_ref, beside_ref, further_ref)
    spread_group(density_ref, spread)
    for p, (x, spot) in enumerate(group_spots(1, density_ref)):
        for ref, field in zip(results, filter_plane(p, layers, spread, weight_ref)):
            ref[x + 2] = field

    for ref in (first_ref, disp_ref):
        for part in range(3):
            ref[part, rows(0, layers)] = zero
            ref[part, rows(planes + 1, layers)] = zero

    def store_faces(slot, modulus, above, later, before, free, start, views):
        across, up_view, right_view, left_view, rate, source = views
        across[slot] = later
        up = jnp.where(z < layers - 1, 0.5 * (modulus + above), 0.0)
        right = jnp.where(
            y < row_width - 1, 0.5 * (modulus + pltpu.roll(modulus, row_width - 1, 1)), 0.0
        )
        left = pltpu.roll(right, 1, 1)
        up_view[rows(slot, layers)] = up
        right_view[slot] = right
        left_view[slot] = left
        sums = (before + later, up + pltpu.roll(up, 1, 0), left + right)
        every = sums[0] + sums[1] + sums[2]
        diagonal = [every + part_sum for part_sum in sums]
        pair = diagonal[0] * diagonal[1]
        push = relax_factor * free / (pair * diagonal[2])
        side = push * diagonal[2]
        for part, factor in enumerate((side * diagonal[1], side * diagonal[0], push * pair)):
            rate[part, slot] = factor
            source[part, rows(slot, layers)] = start[part] * free

    def modulus_half(first, count, carry):
        near = near_ref.at[pl.ds(first + 2, count)]
        side = side_ref.at[pl.ds(first + 1, count + 2)]
        far = far_ref.at[pl.ds(first, count + 4)]
        moduli = modulus_ref.at[pl.ds(first * layers, (count + 1) * layers)]
        coef = coef_ref.at[pl.ds(first, count)]
        free = free_ref.at[pl.ds(first, count)]
        views = (
            across_ref.at[pl.ds(first, count)],
            up_ref.at[pl.ds(first * layers, count * layers)],
            right_ref.at[pl.ds(first, count)],
            left_ref.at[pl.ds(first, count)],
            rate_ref.at[:, pl.ds(first, count)],
            first_ref.at[:, pl.ds(first * layers, count * layers)],
        )
        modulus, before = carry
        for p in range(count):
            inverse = inverse_ref[edge_class(first + p, planes)]
            filtered = near[p] + side[p] + side[p + 2] + far[p] + far[p + 4]
            filtered = filtered * inverse
            later = floor_modulus + (1.0 - floor_modulus) * (filtered * filtered * filtered)
            coef[p] = 3.0 * (1.0 - floor_modulus) * (filtered * filtered) * inverse
            moduli[rows(p + 1, layers)] = later
            ahead = 0.5 * (modulus + later)
            if p == 0:
                ahead = jnp.where(first > 0, ahead, 0.0)
            above = moduli[rows(p, layers, 1)] if p else pltpu.roll(modulus, layers - 1, 0)
            previous = jnp.maximum(first + p - 1, 0)
            store_faces(
                p,
                modulus,
                above,
                ahead,
                before,
                free_ref[previous],
                [start_ref[part, previous] for part in range(3)],
                views,
            )
            modulus, before = later, ahead
        return modulus, before

    modulus, before = each_half(planes, modulus_half, (jnp.ones(shape, jnp.float32), zero))
    store_faces(
        planes,
        modulus,
        pltpu.roll(modulus, layers - 1, 0),
        zero,
        before,
        free_ref[planes - 1],
        [start_ref[part, planes - 1] for part in range(3)],
        (across_ref, up_ref, right_ref, left_ref, rate_ref, first_ref),
    )

    own_x = jnp.max(spot_ref[...]).astype(jnp.int32)

    def sweep(source, target):
        def sweep_half(first, count, carry):
            old = source.at[:, pl.ds(first * layers, (count + 2) * layers)]
            new = target.at[:, pl.ds((first + 1) * layers, count * layers)]
            across = across_ref.at[pl.ds(first, count + 1)]
            up = up_ref.at[pl.ds(first * layers, (count + 1) * layers)]
            right = right_ref.at[pl.ds(first + 1, count)]
            left = left_ref.at[pl.ds(first + 1, count)]
            rate = rate_ref.at[:, pl.ds(first + 1, count)]
            behind = [old[part, rows(0, layers)] for part in range(3)]
            here = [old[part, rows(1, layers)] for part in range(3)]
            for p in range(count):
                ahead = [old[part, rows(p + 2, layers)] for part in range(3)]
                for part in range(3):
                    pulls = [
                        across[p] * behind[part] + across[p + 1] * ahead[part],
                        up[rows(p + 1, layers)] * old[part, rows(p + 1, layers, 1)]
                        + up[rows(p + 1, layers, -1)] * old[part, rows(p + 1, layers, -1)],
                        right[p] * pltpu.roll(here[part], row_width - 1, 1)
                        + left[p] * pltpu.roll(here[part], 1, 1),
                    ]
                    pull = pulls[0] + pulls[1] + pulls[2] + pulls[part]
                    new[part, rows(p, layers)] = (
                        1.0 - relax_factor
                    ) * here[part] + rate[part, p] * pull
                behind, here = here, ahead
            return carry

        each_half(planes, sweep_half, 0)
        for part in range(3):
            target[part, rows(own_x + 1, layers)] += rate_ref[part, own_x + 1] * load_ref[part]

    def two_sweeps(turn, carry):
        sweep(first_ref, disp_ref)

        @pl.when(turn < SWEEPS // 2)
        def _():
            sweep(disp_ref, first_ref)

        return carry

    lax.fori_loop(0, SWEEPS // 2 + 1, two_sweeps, 0)


def energy_planes(group, disp_ref, sens_ref):
    chips, own_planes, layers, row_width = sens_ref.shape
    planes = disp_ref.shape[1] // layers - 2
    load_cases = lax.axis_size("space")
    shape = (layers, row_width)
    z = spot_iota(shape, 0)
    y = spot_iota(shape, 1)
    zero = jnp.zeros(shape, jnp.float32)
    mine = lax.axis_index("space")
    core = mine ^ mine >> 1 ^ group

    def between(x):
        result = zero
        for part in range(3):
            step = disp_ref[part, rows(x + 1, layers)] - disp_ref[part, rows(x, layers)]
            result = result + (2.0 if part == 0 else 1.0) * (step * step)
        return jnp.where((x > 0) & (x < planes), result, 0.0)

    def inside(x):
        upward, right = zero, zero
        for part in range(3):
            here = disp_ref[part, rows(x + 1, layers)]
            climb = disp_ref[part, rows(x + 1, layers, 1)] - here
            slide = pltpu.roll(here, row_width - 1, 1) - here
            upward = upward + (2.0 if part == 1 else 1.0) * (climb * climb)
            right = right + (2.0 if part == 2 else 1.0) * (slide * slide)
        upward = jnp.where(z < layers - 1, upward, 0.0)
        right = jnp.where(y < row_width - 1, right, 0.0)
        return upward + pltpu.roll(upward, 1, 0) + right + pltpu.roll(right, 1, 1)

    for chip in range(chips):
        first = own_planes * (2 * chip + ((core ^ chip) & 1))
        before = between(first)
        for own in range(own_planes):
            after = between(first + own + 1)
            sens_ref[chip, own] = (0.5 / load_cases) * (before + after + inside(first + own))
            before = after


def sent_energy_kernel(disp_ref, sens_ref):
    energy_planes(1, disp_ref, sens_ref)


def kept_energy_kernel(disp_ref, disp_hbm, sens_ref, stored):
    layers = sens_ref.shape[2]
    inner = pl.ds(layers, disp_ref.shape[1] - 2 * layers)
    store = pltpu.make_async_copy(disp_ref.at[:, inner], disp_hbm, stored)
    store.start()
    energy_planes(0, disp_ref, sens_ref)
    store.wait()


def design_kernel(
    weight_ref,
    sens_ref,
    coef_ref,
    density_ref,
    new_ref,
    plane_ref,
    beside_ref,
    further_ref,
    near_ref,
    far_ref,
    pull_ref,
    low_ref,
    high_ref,
):
    planes, layers, row_width = coef_ref.shape
    own_planes = density_ref.shape[2]
    place = lax.axis_index("space")
    shape = (layers, row_width)
    zero = jnp.zeros(shape, jnp.float32)
    zero_gap = jnp.zeros((GAP, row_width), jnp.float32)
    for ref in (plane_ref, beside_ref, further_ref):
        zero_edges(ref)

    def spread_half(first, count, carry):
        sens = half_views(sens_ref, first, count)
        coef = coef_ref.at[pl.ds(first, count)]
        plane_view, beside, further = (
            ref.at[pl.ds(first + 2, count)] for ref in (plane_ref, beside_ref, further_ref)
        )
        for p in range(count):
            view, spot = sens(p)
            plane = view[spot] * coef[p]
            plane_view[p] = plane
            beside[p] = shift_sum(plane, 1, 1)
            further[p] = shift_sum(plane, 1, 2)
        return carry

    each_half(planes, spread_half, 0)

    def root_half(first, count, carry):
        density_at = half_views(density_ref, first, count)
        plane_view, beside, further = (
            ref.at[pl.ds(first, count + 4)] for ref in (plane_ref, beside_ref, further_ref)
        )
        near, far = (
            ref.at[pl.ds(first * (layers + GAP), count * (layers + GAP) + GAP)]
            for ref in (near_ref, far_ref)
        )
        for ref in (near, far):
            ref[gap(0, layers)] = zero_gap
        pull, low, high = (
            ref.at[pl.ds(first, count)] for ref in (pull_ref, low_ref, high_ref)
        )
        for p in range(count):

            def around(ref, distance):
                return ref[p + 2 + distance] + ref[p + 2 - distance]

            sums = {
                0: plane_view[p + 2],
                1: beside[p + 2] + around(plane_view, 1),
                2: around(beside, 1),
                4: further[p + 2] + around(plane_view, 2),
                5: around(further, 1) + around(beside, 2),
                8: around(further, 2),
            }
            level = weigh(sums, weight_ref, 0)
            for ref, square in ((near, 1), (far, 4)):
                ref[gapped(p, layers)] = weigh(sums, weight_ref, square)
                ref[gap(p + 1, layers)] = zero_gap
            root = jnp.sqrt(
                level
                + near[gapped(p, layers, 1)]
                + near[gapped(p, layers, -1)]
                + far[gapped(p, layers, 2)]
                + far[gapped(p, layers, -2)]
            )
            view, spot = density_at(p)
            density = view[spot]
            pull[p] = density * root
            low[p] = jnp.maximum(density - move_limit, density_floor)
            high[p] = jnp.minimum(density + move_limit, 1.0)
        return carry

    each_half(planes, root_half, 0)

    target = volume_share * planes * layers * row_width

    def trial(x, factor):
        return jnp.minimum(jnp.maximum(pull_ref[x] * factor, low_ref[x]), high_ref[x])

    def factor_of(log_level):
        return jnp.broadcast_to(jnp.exp(-0.5 * log_level), shape)

    def exceeds(total):
        return jnp.sum(jnp.sum(total, axis=0, keepdims=True), axis=1, keepdims=True) > target

    def halve_twice(step, state):
        lower, span = state
        half, quarter = span * 0.5, span * 0.25
        middles = (lower + quarter, lower + half, lower + half + quarter)
        factors = [factor_of(middle) for middle in middles]
        totals = [zero, zero, zero]
        for x in range(planes):
            pull, low, high = pull_ref[x], low_ref[x], high_ref[x]
            totals = [
                total + jnp.minimum(jnp.maximum(pull * factor, low), high)
                for total, factor in zip(totals, factors)
            ]
        first, second, third = (exceeds(total) for total in totals)
        upper = jnp.where(third, middles[2], middles[1])
        below = jnp.where(first, middles[0], lower)
        return jnp.where(second, upper, below), quarter

    start = (jnp.full((1, 1), log_lower, jnp.float32), jnp.full((1, 1), log_span, jnp.float32))
    lower, span = lax.fori_loop(0, SEARCH // 2, halve_twice, start)
    factor = factor_of(lower + 0.5 * span)
    for own in range(own_planes):
        new_ref[own] = trial(place * own_planes + own, factor)


def in_vmem():
    return pl.BlockSpec(memory_space=pltpu.VMEM)


KERNEL_VMEM = 24 * 2**20


def floats(*shape):
    return jax.ShapeDtypeStruct(shape, jnp.float32)


def prepare_call(density, radius, load_index, load_force, fixed):
    chips, own_planes, layers, row_width = density.shape
    planes = fixed.shape[0]
    spread = pltpu.VMEM((chips * own_planes * (layers + GAP) + GAP, row_width), jnp.float32)
    return pl.pallas_call(
        prepare_kernel,
        out_shape=[
            floats(len(ALL_SQUARES), layers, row_width),
            floats(2 * window_reach + 1, layers, row_width),
            floats(planes, layers, row_width),
            floats(3, layers, row_width),
            floats(8, row_width),
            floats(3, *density.shape),
        ],
        in_specs=[pl.BlockSpec(memory_space=pltpu.HBM)] * 4 + [in_vmem()],
        out_specs=[in_vmem()] * 6,
        scratch_shapes=[
            pltpu.SMEM(radius.shape, radius.dtype),
            pltpu.SMEM(load_index.shape, load_index.dtype),
            pltpu.SMEM(load_force.shape, load_force.dtype),
            pltpu.VMEM(fixed.shape, fixed.dtype),
            spread,
            spread,
            spread,
            pltpu.SemaphoreType.DMA((4,)),
        ],
        compiler_params=pltpu.CompilerParams(vmem_limit_bytes=KERNEL_VMEM),
        cost_estimate=pl.CostEstimate(
            flops=80 * planes * layers * row_width,
            bytes_accessed=8 * planes * layers * row_width,
            transcendentals=0,
        ),
        name="prepare",
    )(
        *(
            pltpu.with_memory_space_constraint(array, pltpu.HBM)
            for array in (radius, load_index, load_force, fixed)
        ),
        density,
    )


def sweep_call(spot, load, weights, inverses, free, filtered, density, displacement):
    chips, own_planes, layers, row_width = density.shape
    planes = 2 * chips * own_planes

    def scratch(*lead):
        return pltpu.VMEM(lead + (row_width,), jnp.float32)

    return pl.pallas_call(
        sweep_kernel,
        out_shape=[
            floats(3, (planes + 2) * layers, row_width),
            floats(planes, layers, row_width),
        ],
        in_specs=[in_vmem()] * 8,
        out_specs=[in_vmem()] * 2,
        scratch_shapes=[
            scratch(planes // 2 * (layers + GAP) + GAP),
            scratch(planes // 2 * (layers + GAP) + GAP),
            scratch(planes // 2 * (layers + GAP) + GAP),
            scratch(planes + 4, layers),
            scratch(planes + 4, layers),
            scratch(planes + 4, layers),
            scratch((planes + 1) * layers),
            scratch(planes + 1, layers),
            scratch((planes + 1) * layers),
            scratch(planes + 1, layers),
            scratch(planes + 1, layers),
            scratch(3, planes + 1, layers),
            scratch(3, (planes + 2) * layers),
        ],
        compiler_params=pltpu.CompilerParams(vmem_limit_bytes=KERNEL_VMEM),
        name="sweeps",
    )(spot, load, weights, inverses, free, filtered, density, displacement)


def sent_energy_call(disp, group_shape):
    return pl.pallas_call(
        sent_energy_kernel,
        out_shape=floats(*group_shape),
        in_specs=[in_vmem()],
        out_specs=in_vmem(),
        compiler_params=pltpu.CompilerParams(vmem_limit_bytes=KERNEL_VMEM),
        name="sent_energy",
    )(disp)


def kept_energy_call(disp, group_shape):
    parts, disp_rows, row_width = disp.shape
    layers = group_shape[2]
    return pl.pallas_call(
        kept_energy_kernel,
        out_shape=[floats(parts, disp_rows - 2 * layers, row_width), floats(*group_shape)],
        in_specs=[in_vmem()],
        out_specs=[pl.BlockSpec(memory_space=pltpu.HBM), in_vmem()],
        scratch_shapes=[pltpu.SemaphoreType.DMA(())],
        compiler_params=pltpu.CompilerParams(vmem_limit_bytes=KERNEL_VMEM),
        cost_estimate=pl.CostEstimate(
            flops=20 * disp.size, bytes_accessed=8 * disp.size, transcendentals=0
        ),
        name="kept_energy",
    )(disp)


def design_call(weights, sens, coef, density):
    cores, chips, own_planes, layers, row_width = density.shape
    planes = cores * chips * own_planes

    def scratch(*lead):
        return pltpu.VMEM(lead + (row_width,), jnp.float32)

    return pl.pallas_call(
        design_kernel,
        out_shape=floats(own_planes, layers, row_width),
        in_specs=[in_vmem()] * 4,
        out_specs=in_vmem(),
        scratch_shapes=[
            scratch(planes + 4, layers),
            scratch(planes + 4, layers),
            scratch(planes + 4, layers),
            scratch(planes * (layers + GAP) + GAP),
            scratch(planes * (layers + GAP) + GAP),
            scratch(planes, layers),
            scratch(planes, layers),
            scratch(planes, layers),
        ],
        compiler_params=pltpu.CompilerParams(vmem_limit_bytes=KERNEL_VMEM),
        name="design",
    )(weights, sens, coef, density)


def other_core(block):
    devices = lax.axis_size("space")
    return lax.ppermute(block, "space", [(i, i ^ 1) for i in range(devices)])


def chip_groups():
    chips = lax.axis_size("space") // 2
    return [[2 * chip + (chip ^ group) % 2 for chip in range(chips)] for group in range(2)]


def between_chips(pieces):
    return lax.all_to_all(pieces, "space", 0, 0, axis_index_groups=chip_groups())


def chip_gathered(block):
    chips = lax.axis_size("space") // 2
    return between_chips(jnp.broadcast_to(block[None], (chips,) + block.shape))


def with_other_core(blocks):
    return jnp.stack([blocks, other_core(blocks)])


def scattered_sum(sent, make_kept):
    received = other_core(sent)
    *others, kept = make_kept()
    return jnp.sum(between_chips(kept + received), axis=0), others


def one_slab(density, displacement, fixed, load_index, load_force, radius):
    same_group, small = lax.optimization_barrier(
        (chip_gathered(density), (radius, load_index, load_force.T, fixed))
    )
    other_group = other_core(same_group)
    weights, inverses, free, load, spot, filtered = prepare_call(same_group, *small)
    disp, coef = sweep_call(
        spot, load, weights, inverses, free, filtered, other_group, displacement[0]
    )
    whole = jnp.stack([same_group, other_group])
    sent, disp = lax.optimization_barrier((sent_energy_call(disp, same_group.shape), disp))
    sens, (new_displacement,) = scattered_sum(
        sent, lambda: kept_energy_call(disp, same_group.shape)
    )
    sens = with_other_core(chip_gathered(sens))
    new_density = design_call(weights, sens, coef, whole)
    return new_density, new_displacement.reshape(displacement.shape)


def from_behind(block, axis, distance):
    devices = range(lax.axis_size(axis))
    route = [(i - distance, i) for i in devices if i - distance in devices]
    return lax.ppermute(block, axis, route)


def extended(x, sides, width):
    for axis, dim in sides:
        size, length = (lax.axis_size(axis), x.shape[dim])
        up = [(i, (i + 1) % size) for i in range(size - 1)]
        down = [(j, i) for i, j in up]
        last = lax.slice_in_dim(x, length - width, length, axis=dim)
        first = lax.slice_in_dim(x, 0, width, axis=dim)
        before = lax.ppermute(last, axis, up)
        after = lax.ppermute(first, axis, down)
        x = jnp.concatenate([before, x, after], axis=dim)
    return x


def from_partner(x, axis, bit):
    return lax.ppermute(x, axis, [(i, i ^ 1 << bit) for i in range(lax.axis_size(axis))])


def window_offsets():
    offsets_list = []
    for across in range(-window_reach, window_reach + 1):
        for upward in range(-window_reach, window_reach + 1):
            for sideways in range(-window_reach, window_reach + 1):
                length = math.sqrt(across * across + upward * upward + sideways * sideways)
                offsets_list.append((across, upward, sideways, length))
    return offsets_list


def layer_weights(radius):
    radial = radius.astype(jnp.float32)
    return jnp.stack(
        [jnp.maximum(radial - length, 0.0) for across, upward, sideways, length in window_offsets()]
    )


def pad_axis(grid_field, along_axis, before, after_cells):
    widths = [(0, 0)] * grid_field.ndim
    widths[along_axis] = (before, after_cells)
    return jnp.pad(grid_field, widths)


def pad_sides(grid_field):
    return jnp.pad(grid_field, ((0, 0), (window_reach, window_reach), (window_reach, window_reach)))


def filter_forward(padded, weights):
    out_rows = padded.shape[0] - 2 * window_reach
    layers = padded.shape[1] - 2 * window_reach
    row_width = padded.shape[2] - 2 * window_reach
    result = jnp.zeros((out_rows, layers, row_width), jnp.float32)
    for offset_index, (across, upward, sideways, length) in enumerate(window_offsets()):
        shifted = padded[
            window_reach + across : window_reach + across + out_rows,
            window_reach + upward : window_reach + upward + layers,
            window_reach + sideways : window_reach + sideways + row_width,
        ]
        result = result + weights[offset_index][None, :, None] * shifted
    return result


def filter_backward(padded, padded_weights):
    out_rows = padded.shape[0] - 2 * window_reach
    layers = padded.shape[1] - 2 * window_reach
    row_width = padded.shape[2] - 2 * window_reach
    result = jnp.zeros((out_rows, layers, row_width), jnp.float32)
    for offset_index, (across, upward, sideways, length) in enumerate(window_offsets()):
        shifted = padded[
            window_reach - across : window_reach - across + out_rows,
            window_reach - upward : window_reach - upward + layers,
            window_reach - sideways : window_reach - sideways + row_width,
        ]
        layer_part = padded_weights[
            offset_index, window_reach - upward : window_reach - upward + layers
        ]
        result = result + layer_part[None, :, None] * shifted
    return result


def stiff_factors(direction):
    return jnp.array(
        [2.0 if component == direction else 1.0 for component in range(3)], jnp.float32
    ).reshape(3, 1, 1, 1)


def relax_slab(padded, displace, face_x, face_z, face_y, force_field, free_cells, diagonal):
    flux_x = stiff_factors(0) * face_x * jnp.diff(padded, axis=1)
    stencil_image = flux_x[:, :-1] - flux_x[:, 1:]
    flux_z = stiff_factors(1) * face_z * jnp.diff(displace, axis=2)
    stencil_image = stencil_image + pad_axis(flux_z, 2, 1, 0) - pad_axis(flux_z, 2, 0, 1)
    flux_y = stiff_factors(2) * face_y * jnp.diff(displace, axis=3)
    stencil_image = stencil_image + pad_axis(flux_y, 3, 1, 0) - pad_axis(flux_y, 3, 0, 1)
    return free_cells * (displace + relax_factor * (force_field - stencil_image) / diagonal)


def slab_energy(grid_field, along_axis, direction, load_cases):
    change = jnp.diff(grid_field, axis=along_axis)
    return jnp.sum(stiff_factors(direction) * change * change, axis=0) / load_cases


def neighbour_planes(displace, load_cases, axis_devices):
    if axis_devices > load_cases:
        below = from_behind(displace[:, -1:], "space", load_cases)
        above = from_behind(displace[:, :1], "space", -load_cases)
    else:
        below = jnp.zeros_like(displace[:, :1])
        above = jnp.zeros_like(displace[:, :1])
    return jnp.concatenate([below, displace, above], axis=1)


def many_slabs(density, displacement, fixed, load_index, load_force, radius):
    slab_rows, layers, row_width = density.shape
    load_cases = load_index.shape[0]
    level_count = load_cases.bit_length() - 1
    axis_devices = lax.axis_size("space")
    axis_place = lax.axis_index("space")
    slab_planes = slab_rows * load_cases
    slab_place = axis_place // load_cases
    load_place = axis_place % load_cases
    total_rows = slab_rows * axis_devices
    weights = layer_weights(radius)
    padded_weights = pad_axis(weights, 1, window_reach, window_reach)
    global_rows = (
        jnp.arange(slab_rows + 2 * window_reach, dtype=jnp.int32)
        + axis_place * slab_rows
        - window_reach
    )
    deep_inside = ((global_rows >= 0) & (global_rows < total_rows)).astype(jnp.float32)
    inside_field = deep_inside[:, None, None] * pad_sides(
        jnp.ones((slab_rows + 2 * window_reach, layers, row_width), jnp.float32)
    )
    total_weight = filter_forward(inside_field, weights)
    slab_start = slab_place * slab_planes
    margin_rows = jnp.arange(slab_planes + 2, dtype=jnp.int32) + slab_start - 1
    margin_inside = ((margin_rows >= 0) & (margin_rows < total_rows)).astype(jnp.float32)
    face_valid = margin_inside[1:] * margin_inside[:-1]
    fixed_slab = lax.dynamic_slice_in_dim(fixed, slab_start, slab_planes, 0).astype(jnp.float32)
    bottom_layer = (jnp.arange(layers, dtype=jnp.int32) == 0).astype(jnp.float32)
    free_cells = 1.0 - bottom_layer[None, :, None] * fixed_slab[:, None, :]
    slab_cells = slab_planes * layers * row_width
    cell_index = jnp.arange(slab_cells, dtype=jnp.int32) + slab_place * slab_cells
    load_hot = jnp.arange(load_cases, dtype=jnp.int32) == load_place
    own_index = jnp.sum(jnp.where(load_hot, load_index, 0))
    own_force = jnp.sum(load_hot.astype(jnp.float32)[:, None] * load_force, axis=0)
    load_hits = (cell_index == own_index).astype(jnp.float32)
    force_field = (own_force[:, None] * load_hits[None, :]).reshape(
        3, slab_planes, layers, row_width
    )
    displace = displacement[0] * free_cells
    target = volume_share * total_rows * layers * row_width
    padded = neighbour_planes(displace, load_cases, axis_devices)
    halo_density = extended(density, (("space", 0),), window_reach)
    filtered = filter_forward(pad_sides(halo_density), weights) / total_weight
    whole_field = lax.all_gather(filtered, "space", axis=0, tiled=True)
    margin = lax.dynamic_slice_in_dim(
        pad_axis(whole_field, 0, 1, 1), slab_start, slab_planes + 2, 0
    )
    moduli = floor_modulus + (1.0 - floor_modulus) * margin**3
    face_x = 0.5 * (moduli[1:] + moduli[:-1]) * face_valid[:, None, None]
    inner_moduli = moduli[1:-1]
    face_z = 0.5 * (inner_moduli[:, 1:] + inner_moduli[:, :-1])
    face_y = 0.5 * (inner_moduli[:, :, 1:] + inner_moduli[:, :, :-1])
    sum_x = face_x[:-1] + face_x[1:]
    sum_z = pad_axis(face_z, 1, 1, 0) + pad_axis(face_z, 1, 0, 1)
    sum_y = pad_axis(face_y, 2, 1, 0) + pad_axis(face_y, 2, 0, 1)
    diagonal = stiff_factors(0) * sum_x + stiff_factors(1) * sum_z + stiff_factors(2) * sum_y
    for sweep_index in range(SWEEPS):
        displace = relax_slab(
            padded, displace, face_x, face_z, face_y, force_field, free_cells, diagonal
        )
        padded = neighbour_planes(displace, load_cases, axis_devices)
    energy_x = slab_energy(padded, 1, 0, load_cases) * face_valid[:, None, None]
    energy_z = slab_energy(displace, 2, 1, load_cases)
    energy_y = slab_energy(displace, 3, 2, load_cases)
    sens_term = 0.5 * (
        energy_x[:-1]
        + energy_x[1:]
        + pad_axis(energy_z, 1, 1, 0)
        + pad_axis(energy_z, 1, 0, 1)
        + pad_axis(energy_y, 2, 1, 0)
        + pad_axis(energy_y, 2, 0, 1)
    )
    sensitive = sens_term
    for level in reversed(range(level_count)):
        half_rows = sensitive.shape[0] // 2
        upper_side = load_place // 2**level % 2 == 1
        outgoing = jnp.where(upper_side, sensitive[:half_rows], sensitive[half_rows:])
        keeping = jnp.where(upper_side, sensitive[half_rows:], sensitive[:half_rows])
        sensitive = keeping + from_partner(outgoing, "space", level)
    weighted_share = 3.0 * (1.0 - floor_modulus) * filtered**2 * sensitive / total_weight
    halo_share = extended(weighted_share, (("space", 0),), window_reach)
    root_term = jnp.sqrt(filter_backward(pad_sides(halo_share), padded_weights))
    lowest = jnp.maximum(density - move_limit, density_floor)
    highest = jnp.minimum(density + move_limit, 1.0)
    design_now = density

    def trial_design(log_level):
        return jnp.clip(design_now * root_term * jnp.exp(-0.5 * log_level), lowest, highest)

    start_state = (jnp.asarray(log_lower, jnp.float32), jnp.asarray(log_span, jnp.float32))

    def halve(search_step, search_state):
        lower_end, span_width = search_state
        half_span = span_width * 0.5
        middle = lower_end + half_span
        volume_total = lax.psum(jnp.sum(trial_design(middle)), "space")
        return (jnp.where(volume_total > target, middle, lower_end), half_span)

    lower_end, span_width = lax.fori_loop(0, SEARCH, halve, start_state)
    density = trial_design(lower_end + 0.5 * span_width)
    new_displacement = displace[None]
    return (density, new_displacement)


def solution(mesh):
    in_specs = (
        P("space", "parts", None),
        P("space", None, None, "parts", None),
        P(None, "parts"),
        P("parts"),
        P("parts", None),
        P("parts"),
    )
    out_specs = (P("space", "parts", None), P("space", None, None, "parts", None))

    def local(density, displacement, fixed, load_index, load_force, radius):
        alone = lax.axis_size("space") == load_index.shape[0]
        run = one_slab if alone else many_slabs
        return run(density, displacement, fixed, load_index, load_force, radius)

    return jax.shard_map(local, mesh=mesh, in_specs=in_specs, out_specs=out_specs, check_vma=False)
```

```python
import math

import jax
import jax.numpy as jnp
from jax import lax
from jax.experimental import pallas as pl
from jax.experimental.pallas import tpu as pltpu
from jax.sharding import PartitionSpec as P

SWEEPS = 3
SEARCH = 12


floor_modulus = 0.05
relax_factor = 0.6
move_limit = 0.2
density_floor = 0.01
volume_share = 0.5
log_lower = -16.0
log_span = 32.0
window_reach = 2

PLANE_SQUARES = (0, 1, 2, 4, 5, 8)
ALL_SQUARES = (0, 1, 2, 3, 4, 5, 6, 8, 9, 12)


def spot_iota(shape, dim):
    return lax.broadcasted_iota(jnp.int32, shape, dim)


def each_plane(planes, body, carry):
    for x in range(planes):
        carry = body(x, carry)
    return carry


def each_half(planes, body, carry):
    count = planes // 2
    return lax.fori_loop(0, 2, lambda half, carry: body(half * count, count, carry), carry)


def layer_radius(radius_ref, layers, row_width):
    z = spot_iota((layers, row_width), 0)
    result = jnp.zeros((layers, row_width), jnp.int32)
    for layer in range(layers):
        result = jnp.where(z == layer, radius_ref[layer], result)
    return result.astype(jnp.float32)


def class_weights(radius_ref, weight_ref):
    layers, row_width = weight_ref.shape[1:]
    radial = layer_radius(radius_ref, layers, row_width)
    for place, square in enumerate(ALL_SQUARES):
        weight_ref[place] = jnp.maximum(radial - math.sqrt(square), 0.0)


def shift_sum(field, dim, distance):
    size = field.shape[dim]
    spot = spot_iota(field.shape, dim)
    ahead = jnp.where(spot < size - distance, pltpu.roll(field, size - distance, dim), 0.0)
    behind = jnp.where(spot >= distance, pltpu.roll(field, distance, dim), 0.0)
    return ahead + behind


def plane_sums(plane):
    beside = shift_sum(plane, 1, 1)
    further = shift_sum(plane, 1, 2)
    return {
        0: plane,
        1: beside + shift_sum(plane, 0, 1),
        2: shift_sum(beside, 0, 1),
        4: further + shift_sum(plane, 0, 2),
        5: shift_sum(further, 0, 1) + shift_sum(beside, 0, 2),
        8: shift_sum(further, 0, 2),
    }


def weigh(sums, weight_ref, square):
    result = None
    for inner in PLANE_SQUARES:
        term = weight_ref[ALL_SQUARES.index(inner + square)] * sums[inner]
        result = term if result is None else result + term
    return result


def forward_planes(plane, weight_ref):
    sums = plane_sums(plane)
    return [weigh(sums, weight_ref, square) for square in (0, 1, 4)]


def rows(x, layers, shift=0):
    return pl.ds(x * layers + shift, layers)


GAP = 8


def gapped(x, layers, shift=0):
    return pl.ds(GAP + x * (layers + GAP) + shift, layers)


def gap(x, layers):
    return pl.ds(x * (layers + GAP), GAP)


def pair_spot(x, own_planes):
    device = x // own_planes
    apart = device ^ lax.axis_index("space")
    return (apart ^ apart >> 1) & 1, device >> 1, x % own_planes


def half_views(ref, first, count):
    own_planes = ref.shape[2]
    mine = lax.axis_index("space")
    side = (mine ^ mine >> 1) & 1
    chips = pl.ds(first // (2 * own_planes), count // (2 * own_planes))
    views = (ref.at[side, chips], ref.at[1 - side, chips])

    def plane(p):
        device = p // own_planes
        return views[(device ^ device >> 1) & 1], (device >> 1, p % own_planes)

    return plane


def edge_class(x, planes):
    return jnp.minimum(x, 2) + jnp.maximum(x - (planes - 3), 0)


def zero_edges(ref):
    planes = ref.shape[0]
    for place in (0, 1, planes - 2, planes - 1):
        ref[place] = jnp.zeros(ref.shape[1:], ref.dtype)


def group_spots(group, blocks):
    chips, own_planes = blocks.shape[:2]
    mine = lax.axis_index("space")
    core = mine ^ mine >> 1 ^ group
    return [
        (own_planes * (2 * chip + ((core ^ chip) & 1)) + own, (chip, own))
        for chip in range(chips)
        for own in range(own_planes)
    ]


def spread_group(blocks, spread):
    chips, own_planes, layers, row_width = blocks.shape
    zero_gap = jnp.zeros((GAP, row_width), jnp.float32)
    for ref in spread:
        ref[gap(0, layers)] = zero_gap
    for p in range(chips * own_planes):
        plane = blocks[p // own_planes, p % own_planes]
        for ref, field in zip(spread, (plane, shift_sum(plane, 1, 1), shift_sum(plane, 1, 2))):
            ref[gapped(p, layers)] = field
            ref[gap(p + 1, layers)] = zero_gap


def filter_plane(p, layers, spread, weight_ref):
    def around(place, distance):
        ref = spread[place]
        return ref[gapped(p, layers, distance)] + ref[gapped(p, layers, -distance)]

    sums = {
        0: spread[0][gapped(p, layers)],
        1: spread[1][gapped(p, layers)] + around(0, 1),
        2: around(1, 1),
        4: spread[2][gapped(p, layers)] + around(0, 2),
        5: around(2, 1) + around(1, 2),
        8: around(2, 2),
    }
    return [weigh(sums, weight_ref, square) for square in (0, 1, 4)]


def prepare_kernel(
    radius_hbm,
    index_hbm,
    force_hbm,
    fixed_hbm,
    density_ref,
    weight_ref,
    inverse_ref,
    free_ref,
    load_ref,
    spot_ref,
    filter_ref,
    radius_ref,
    index_ref,
    force_ref,
    fixed_ref,
    plane_ref,
    beside_ref,
    further_ref,
    arrived,
):
    copies = [
        pltpu.make_async_copy(source, target, arrived.at[place])
        for place, (source, target) in enumerate(
            (
                (radius_hbm, radius_ref),
                (index_hbm, index_ref),
                (force_hbm, force_ref),
                (fixed_hbm, fixed_ref),
            )
        )
    ]
    for copy in copies:
        copy.start()
    spread = (plane_ref, beside_ref, further_ref)
    spread_group(density_ref, spread)
    for copy in copies:
        copy.wait()
    planes, layers, row_width = free_ref.shape
    load_place = lax.axis_index("space")
    shape = (layers, row_width)
    z = spot_iota(shape, 0)
    y = spot_iota(shape, 1)

    class_weights(radius_ref, weight_ref)
    own_planes = density_ref.shape[1]
    for p in range(density_ref.shape[0] * own_planes):
        for place, field in enumerate(filter_plane(p, layers, spread, weight_ref)):
            filter_ref[place, p // own_planes, p % own_planes] = field

    ones = forward_planes(jnp.ones(shape, jnp.float32), weight_ref)
    for place, (lower, upper) in enumerate(((0, 2), (1, 2), (2, 2), (2, 1), (2, 0))):
        inverse_ref[place] = 1.0 / (
            ones[0] + min(lower, 1) * ones[1] + min(upper, 1) * ones[1]
            + (lower // 2) * ones[2] + (upper // 2) * ones[2]
        )

    def free_plane(x, carry):
        free_ref[x] = jnp.where(
            z == 0, 1.0 - fixed_ref[pl.ds(x, 1), :].astype(jnp.float32), 1.0
        )
        return carry

    each_plane(planes, free_plane, 0)

    own_index = index_ref[load_place]
    own_z = own_index // row_width % layers
    own_y = own_index % row_width
    hit = (z == own_z) & (y == own_y)
    for part in range(3):
        load_ref[part] = jnp.where(hit, force_ref[part, load_place], 0.0)
    own_x = (own_index // (layers * row_width)).astype(jnp.float32)
    spot_ref[...] = jnp.full(spot_ref.shape, own_x)


def sweep_kernel(
    spot_ref,
    load_ref,
    weight_ref,
    inverse_ref,
    free_ref,
    filter_ref,
    density_ref,
    start_hbm,
    disp_ref,
    coef_ref,
    plane_ref,
    beside_ref,
    further_ref,
    near_ref,
    side_ref,
    far_ref,
    modulus_ref,
    across_ref,
    up_ref,
    right_ref,
    left_ref,
    rate_ref,
    first_ref,
    arrived,
):
    planes, layers, row_width = coef_ref.shape
    fetch = pltpu.make_async_copy(
        start_hbm, first_ref.at[:, pl.ds(layers, planes * layers)], arrived
    )
    fetch.start()
    shape = (layers, row_width)
    z = spot_iota(shape, 0)
    y = spot_iota(shape, 1)
    zero = jnp.zeros(shape, jnp.float32)

    for ref in (side_ref, far_ref):
        zero_edges(ref)
    results = (near_ref, side_ref, far_ref)
    for x, spot in group_spots(0, density_ref):
        for place, ref in enumerate(results):
            ref[x + 2] = filter_ref[(place,) + spot]
    spread = (plane_ref, beside_ref, further_ref)
    spread_group(density_ref, spread)
    for p, (x, spot) in enumerate(group_spots(1, density_ref)):
        for ref, field in zip(results, filter_plane(p, layers, spread, weight_ref)):
            ref[x + 2] = field

    for ref in (first_ref, disp_ref):
        for part in range(3):
            ref[part, rows(0, layers)] = zero
            ref[part, rows(planes + 1, layers)] = zero

    def store_faces(slot, modulus, above, later, before, free, views):
        across, up_view, right_view, left_view, rate = views
        across[slot] = later
        up = jnp.where(z < layers - 1, 0.5 * (modulus + above), 0.0)
        right = jnp.where(
            y < row_width - 1, 0.5 * (modulus + pltpu.roll(modulus, row_width - 1, 1)), 0.0
        )
        left = pltpu.roll(right, 1, 1)
        up_view[rows(slot, layers)] = up
        right_view[slot] = right
        left_view[slot] = left
        sums = (before + later, up + pltpu.roll(up, 1, 0), left + right)
        every = sums[0] + sums[1] + sums[2]
        diagonal = [every + part_sum for part_sum in sums]
        pair = diagonal[0] * diagonal[1]
        push = relax_factor * free / (pair * diagonal[2])
        side = push * diagonal[2]
        for part, factor in enumerate((side * diagonal[1], side * diagonal[0], push * pair)):
            rate[part, slot] = factor

    def modulus_half(first, count, carry):
        near = near_ref.at[pl.ds(first + 2, count)]
        side = side_ref.at[pl.ds(first + 1, count + 2)]
        far = far_ref.at[pl.ds(first, count + 4)]
        moduli = modulus_ref.at[pl.ds(first * layers, (count + 1) * layers)]
        coef = coef_ref.at[pl.ds(first, count)]
        free = free_ref.at[pl.ds(first, count)]
        views = (
            across_ref.at[pl.ds(first, count)],
            up_ref.at[pl.ds(first * layers, count * layers)],
            right_ref.at[pl.ds(first, count)],
            left_ref.at[pl.ds(first, count)],
            rate_ref.at[:, pl.ds(first, count)],
        )
        modulus, before = carry
        for p in range(count):
            inverse = inverse_ref[edge_class(first + p, planes)]
            filtered = near[p] + side[p] + side[p + 2] + far[p] + far[p + 4]
            filtered = filtered * inverse
            later = floor_modulus + (1.0 - floor_modulus) * (filtered * filtered * filtered)
            coef[p] = 3.0 * (1.0 - floor_modulus) * (filtered * filtered) * inverse
            moduli[rows(p + 1, layers)] = later
            ahead = 0.5 * (modulus + later)
            if p == 0:
                ahead = jnp.where(first > 0, ahead, 0.0)
            above = moduli[rows(p, layers, 1)] if p else pltpu.roll(modulus, layers - 1, 0)
            previous = jnp.maximum(first + p - 1, 0)
            store_faces(
                p,
                modulus,
                above,
                ahead,
                before,
                free_ref[previous],
                views,
            )
            modulus, before = later, ahead
        return modulus, before

    modulus, before = each_half(planes, modulus_half, (jnp.ones(shape, jnp.float32), zero))
    store_faces(
        planes,
        modulus,
        pltpu.roll(modulus, layers - 1, 0),
        zero,
        before,
        free_ref[planes - 1],
        (across_ref, up_ref, right_ref, left_ref, rate_ref),
    )

    fetch.wait()
    bottom = min(layers, 8)
    for x in range(planes):
        free = free_ref[x, pl.ds(0, bottom)]
        for part in range(3):
            first_ref[part, pl.ds((x + 1) * layers, bottom)] *= free

    own_x = jnp.max(spot_ref[...]).astype(jnp.int32)

    def sweep(source, target):
        def sweep_half(first, count, carry):
            old = source.at[:, pl.ds(first * layers, (count + 2) * layers)]
            new = target.at[:, pl.ds((first + 1) * layers, count * layers)]
            across = across_ref.at[pl.ds(first, count + 1)]
            up = up_ref.at[pl.ds(first * layers, (count + 1) * layers)]
            right = right_ref.at[pl.ds(first + 1, count)]
            left = left_ref.at[pl.ds(first + 1, count)]
            rate = rate_ref.at[:, pl.ds(first + 1, count)]
            behind = [old[part, rows(0, layers)] for part in range(3)]
            here = [old[part, rows(1, layers)] for part in range(3)]
            for p in range(count):
                ahead = [old[part, rows(p + 2, layers)] for part in range(3)]
                for part in range(3):
                    pulls = [
                        across[p] * behind[part] + across[p + 1] * ahead[part],
                        up[rows(p + 1, layers)] * old[part, rows(p + 1, layers, 1)]
                        + up[rows(p + 1, layers, -1)] * old[part, rows(p + 1, layers, -1)],
                        right[p] * pltpu.roll(here[part], row_width - 1, 1)
                        + left[p] * pltpu.roll(here[part], 1, 1),
                    ]
                    pull = pulls[0] + pulls[1] + pulls[2] + pulls[part]
                    new[part, rows(p, layers)] = (
                        1.0 - relax_factor
                    ) * here[part] + rate[part, p] * pull
                behind, here = here, ahead
            return carry

        each_half(planes, sweep_half, 0)
        for part in range(3):
            target[part, rows(own_x + 1, layers)] += rate_ref[part, own_x + 1] * load_ref[part]

    def two_sweeps(turn, carry):
        sweep(first_ref, disp_ref)

        @pl.when(turn < SWEEPS // 2)
        def _():
            sweep(disp_ref, first_ref)

        return carry

    lax.fori_loop(0, SWEEPS // 2 + 1, two_sweeps, 0)


def energy_planes(group, disp_ref, sens_ref):
    chips, own_planes, layers, row_width = sens_ref.shape
    planes = disp_ref.shape[1] // layers - 2
    load_cases = lax.axis_size("space")
    shape = (layers, row_width)
    z = spot_iota(shape, 0)
    y = spot_iota(shape, 1)
    zero = jnp.zeros(shape, jnp.float32)
    mine = lax.axis_index("space")
    core = mine ^ mine >> 1 ^ group

    def between(x):
        result = zero
        for part in range(3):
            step = disp_ref[part, rows(x + 1, layers)] - disp_ref[part, rows(x, layers)]
            result = result + (2.0 if part == 0 else 1.0) * (step * step)
        return jnp.where((x > 0) & (x < planes), result, 0.0)

    def inside(x):
        upward, right = zero, zero
        for part in range(3):
            here = disp_ref[part, rows(x + 1, layers)]
            climb = disp_ref[part, rows(x + 1, layers, 1)] - here
            slide = pltpu.roll(here, row_width - 1, 1) - here
            upward = upward + (2.0 if part == 1 else 1.0) * (climb * climb)
            right = right + (2.0 if part == 2 else 1.0) * (slide * slide)
        upward = jnp.where(z < layers - 1, upward, 0.0)
        right = jnp.where(y < row_width - 1, right, 0.0)
        return upward + pltpu.roll(upward, 1, 0) + right + pltpu.roll(right, 1, 1)

    for chip in range(chips):
        first = own_planes * (2 * chip + ((core ^ chip) & 1))
        before = between(first)
        for own in range(own_planes):
            after = between(first + own + 1)
            sens_ref[chip, own] = (0.5 / load_cases) * (before + after + inside(first + own))
            before = after


def sent_energy_kernel(disp_ref, sens_ref):
    energy_planes(1, disp_ref, sens_ref)


def kept_energy_kernel(disp_ref, disp_hbm, sens_ref, stored):
    layers = sens_ref.shape[2]
    inner = pl.ds(layers, disp_ref.shape[1] - 2 * layers)
    store = pltpu.make_async_copy(disp_ref.at[:, inner], disp_hbm, stored)
    store.start()
    energy_planes(0, disp_ref, sens_ref)
    store.wait()


def design_kernel(
    weight_ref,
    sens_ref,
    coef_ref,
    density_ref,
    new_ref,
    plane_ref,
    beside_ref,
    further_ref,
    near_ref,
    far_ref,
    pull_ref,
    low_ref,
    high_ref,
):
    planes, layers, row_width = coef_ref.shape
    own_planes = density_ref.shape[2]
    place = lax.axis_index("space")
    shape = (layers, row_width)
    zero = jnp.zeros(shape, jnp.float32)
    zero_gap = jnp.zeros((GAP, row_width), jnp.float32)
    for ref in (plane_ref, beside_ref, further_ref):
        zero_edges(ref)

    def spread_half(first, count, carry):
        sens = half_views(sens_ref, first, count)
        coef = coef_ref.at[pl.ds(first, count)]
        plane_view, beside, further = (
            ref.at[pl.ds(first + 2, count)] for ref in (plane_ref, beside_ref, further_ref)
        )
        for p in range(count):
            view, spot = sens(p)
            plane = view[spot] * coef[p]
            plane_view[p] = plane
            beside[p] = shift_sum(plane, 1, 1)
            further[p] = shift_sum(plane, 1, 2)
        return carry

    each_half(planes, spread_half, 0)

    def root_half(first, count, carry):
        density_at = half_views(density_ref, first, count)
        plane_view, beside, further = (
            ref.at[pl.ds(first, count + 4)] for ref in (plane_ref, beside_ref, further_ref)
        )
        near, far = (
            ref.at[pl.ds(first * (layers + GAP), count * (layers + GAP) + GAP)]
            for ref in (near_ref, far_ref)
        )
        for ref in (near, far):
            ref[gap(0, layers)] = zero_gap
        pull, low, high = (
            ref.at[pl.ds(first, count)] for ref in (pull_ref, low_ref, high_ref)
        )
        for p in range(count):

            def around(ref, distance):
                return ref[p + 2 + distance] + ref[p + 2 - distance]

            sums = {
                0: plane_view[p + 2],
                1: beside[p + 2] + around(plane_view, 1),
                2: around(beside, 1),
                4: further[p + 2] + around(plane_view, 2),
                5: around(further, 1) + around(beside, 2),
                8: around(further, 2),
            }
            level = weigh(sums, weight_ref, 0)
            for ref, square in ((near, 1), (far, 4)):
                ref[gapped(p, layers)] = weigh(sums, weight_ref, square)
                ref[gap(p + 1, layers)] = zero_gap
            root = jnp.sqrt(
                level
                + near[gapped(p, layers, 1)]
                + near[gapped(p, layers, -1)]
                + far[gapped(p, layers, 2)]
                + far[gapped(p, layers, -2)]
            )
            view, spot = density_at(p)
            density = view[spot]
            pull[p] = density * root
            low[p] = jnp.maximum(density - move_limit, density_floor)
            high[p] = jnp.minimum(density + move_limit, 1.0)
        return carry

    each_half(planes, root_half, 0)

    target = volume_share * planes * layers * row_width

    def trial(x, factor):
        return jnp.minimum(jnp.maximum(pull_ref[x] * factor, low_ref[x]), high_ref[x])

    def factor_of(log_level):
        return jnp.broadcast_to(jnp.exp(-0.5 * log_level), shape)

    def exceeds(total):
        return jnp.sum(jnp.sum(total, axis=0, keepdims=True), axis=1, keepdims=True) > target

    def halve_twice(step, state):
        lower, span = state
        half, quarter = span * 0.5, span * 0.25
        middles = (lower + quarter, lower + half, lower + half + quarter)
        factors = [factor_of(middle) for middle in middles]
        totals = [zero, zero, zero]
        for x in range(planes):
            pull, low, high = pull_ref[x], low_ref[x], high_ref[x]
            totals = [
                total + jnp.minimum(jnp.maximum(pull * factor, low), high)
                for total, factor in zip(totals, factors)
            ]
        first, second, third = (exceeds(total) for total in totals)
        upper = jnp.where(third, middles[2], middles[1])
        below = jnp.where(first, middles[0], lower)
        return jnp.where(second, upper, below), quarter

    start = (jnp.full((1, 1), log_lower, jnp.float32), jnp.full((1, 1), log_span, jnp.float32))
    lower, span = lax.fori_loop(0, SEARCH // 2, halve_twice, start)
    factor = factor_of(lower + 0.5 * span)
    for own in range(own_planes):
        new_ref[own] = trial(place * own_planes + own, factor)


def in_vmem():
    return pl.BlockSpec(memory_space=pltpu.VMEM)


KERNEL_VMEM = 24 * 2**20


def floats(*shape):
    return jax.ShapeDtypeStruct(shape, jnp.float32)


def prepare_call(density, radius, load_index, load_force, fixed):
    chips, own_planes, layers, row_width = density.shape
    planes = fixed.shape[0]
    spread = pltpu.VMEM((chips * own_planes * (layers + GAP) + GAP, row_width), jnp.float32)
    return pl.pallas_call(
        prepare_kernel,
        out_shape=[
            floats(len(ALL_SQUARES), layers, row_width),
            floats(2 * window_reach + 1, layers, row_width),
            floats(planes, layers, row_width),
            floats(3, layers, row_width),
            floats(8, row_width),
            floats(3, *density.shape),
        ],
        in_specs=[pl.BlockSpec(memory_space=pltpu.HBM)] * 4 + [in_vmem()],
        out_specs=[in_vmem()] * 6,
        scratch_shapes=[
            pltpu.SMEM(radius.shape, radius.dtype),
            pltpu.SMEM(load_index.shape, load_index.dtype),
            pltpu.SMEM(load_force.shape, load_force.dtype),
            pltpu.VMEM(fixed.shape, fixed.dtype),
            spread,
            spread,
            spread,
            pltpu.SemaphoreType.DMA((4,)),
        ],
        compiler_params=pltpu.CompilerParams(vmem_limit_bytes=KERNEL_VMEM),
        cost_estimate=pl.CostEstimate(
            flops=80 * planes * layers * row_width,
            bytes_accessed=8 * planes * layers * row_width,
            transcendentals=0,
        ),
        name="prepare",
    )(
        *(
            pltpu.with_memory_space_constraint(array, pltpu.HBM)
            for array in (radius, load_index, load_force, fixed)
        ),
        density,
    )


def sweep_call(spot, load, weights, inverses, free, filtered, density, displacement):
    chips, own_planes, layers, row_width = density.shape
    planes = 2 * chips * own_planes

    def scratch(*lead):
        return pltpu.VMEM(lead + (row_width,), jnp.float32)

    return pl.pallas_call(
        sweep_kernel,
        out_shape=[
            floats(3, (planes + 2) * layers, row_width),
            floats(planes, layers, row_width),
        ],
        in_specs=[in_vmem()] * 7 + [pl.BlockSpec(memory_space=pltpu.HBM)],
        out_specs=[in_vmem()] * 2,
        scratch_shapes=[
            scratch(planes // 2 * (layers + GAP) + GAP),
            scratch(planes // 2 * (layers + GAP) + GAP),
            scratch(planes // 2 * (layers + GAP) + GAP),
            scratch(planes + 4, layers),
            scratch(planes + 4, layers),
            scratch(planes + 4, layers),
            scratch((planes + 1) * layers),
            scratch(planes + 1, layers),
            scratch((planes + 1) * layers),
            scratch(planes + 1, layers),
            scratch(planes + 1, layers),
            scratch(3, planes + 1, layers),
            scratch(3, (planes + 2) * layers),
            pltpu.SemaphoreType.DMA(()),
        ],
        compiler_params=pltpu.CompilerParams(vmem_limit_bytes=KERNEL_VMEM),
        name="sweeps",
    )(
        spot,
        load,
        weights,
        inverses,
        free,
        filtered,
        density,
        pltpu.with_memory_space_constraint(displacement, pltpu.HBM),
    )


def sent_energy_call(disp, group_shape):
    return pl.pallas_call(
        sent_energy_kernel,
        out_shape=floats(*group_shape),
        in_specs=[in_vmem()],
        out_specs=in_vmem(),
        compiler_params=pltpu.CompilerParams(vmem_limit_bytes=KERNEL_VMEM),
        name="sent_energy",
    )(disp)


def kept_energy_call(disp, group_shape):
    parts, disp_rows, row_width = disp.shape
    layers = group_shape[2]
    return pl.pallas_call(
        kept_energy_kernel,
        out_shape=[floats(parts, disp_rows - 2 * layers, row_width), floats(*group_shape)],
        in_specs=[in_vmem()],
        out_specs=[pl.BlockSpec(memory_space=pltpu.HBM), in_vmem()],
        scratch_shapes=[pltpu.SemaphoreType.DMA(())],
        compiler_params=pltpu.CompilerParams(vmem_limit_bytes=KERNEL_VMEM),
        cost_estimate=pl.CostEstimate(
            flops=20 * disp.size, bytes_accessed=8 * disp.size, transcendentals=0
        ),
        name="kept_energy",
    )(disp)


def design_call(weights, sens, coef, density):
    cores, chips, own_planes, layers, row_width = density.shape
    planes = cores * chips * own_planes

    def scratch(*lead):
        return pltpu.VMEM(lead + (row_width,), jnp.float32)

    return pl.pallas_call(
        design_kernel,
        out_shape=floats(own_planes, layers, row_width),
        in_specs=[in_vmem()] * 4,
        out_specs=in_vmem(),
        scratch_shapes=[
            scratch(planes + 4, layers),
            scratch(planes + 4, layers),
            scratch(planes + 4, layers),
            scratch(planes * (layers + GAP) + GAP),
            scratch(planes * (layers + GAP) + GAP),
            scratch(planes, layers),
            scratch(planes, layers),
            scratch(planes, layers),
        ],
        compiler_params=pltpu.CompilerParams(vmem_limit_bytes=KERNEL_VMEM),
        name="design",
    )(weights, sens, coef, density)


def other_core(block):
    devices = lax.axis_size("space")
    return lax.ppermute(block, "space", [(i, i ^ 1) for i in range(devices)])


def chip_groups():
    chips = lax.axis_size("space") // 2
    return [[2 * chip + (chip ^ group) % 2 for chip in range(chips)] for group in range(2)]


def between_chips(pieces):
    return lax.all_to_all(pieces, "space", 0, 0, axis_index_groups=chip_groups())


def chip_gathered(block):
    chips = lax.axis_size("space") // 2
    return between_chips(jnp.broadcast_to(block[None], (chips,) + block.shape))


def with_other_core(blocks):
    return jnp.stack([blocks, other_core(blocks)])


def scattered_sum(sent, make_kept):
    received = other_core(sent)
    *others, kept = make_kept()
    return jnp.sum(between_chips(kept + received), axis=0), others


def one_slab(density, displacement, fixed, load_index, load_force, radius):
    same_group, small = lax.optimization_barrier(
        (chip_gathered(density), (radius, load_index, load_force.T, fixed))
    )
    other_group = other_core(same_group)
    weights, inverses, free, load, spot, filtered = prepare_call(same_group, *small)
    start = displacement.reshape(3, -1, displacement.shape[-1])
    disp, coef = sweep_call(
        spot, load, weights, inverses, free, filtered, other_group, start
    )
    whole = jnp.stack([same_group, other_group])
    sent, disp = lax.optimization_barrier((sent_energy_call(disp, same_group.shape), disp))
    sens, (new_displacement,) = scattered_sum(
        sent, lambda: kept_energy_call(disp, same_group.shape)
    )
    sens = with_other_core(chip_gathered(sens))
    new_density = design_call(weights, sens, coef, whole)
    return new_density, new_displacement.reshape(displacement.shape)


def from_behind(block, axis, distance):
    devices = range(lax.axis_size(axis))
    route = [(i - distance, i) for i in devices if i - distance in devices]
    return lax.ppermute(block, axis, route)


def extended(x, sides, width):
    for axis, dim in sides:
        size, length = (lax.axis_size(axis), x.shape[dim])
        up = [(i, (i + 1) % size) for i in range(size - 1)]
        down = [(j, i) for i, j in up]
        last = lax.slice_in_dim(x, length - width, length, axis=dim)
        first = lax.slice_in_dim(x, 0, width, axis=dim)
        before = lax.ppermute(last, axis, up)
        after = lax.ppermute(first, axis, down)
        x = jnp.concatenate([before, x, after], axis=dim)
    return x


def from_partner(x, axis, bit):
    return lax.ppermute(x, axis, [(i, i ^ 1 << bit) for i in range(lax.axis_size(axis))])


def window_offsets():
    offsets_list = []
    for across in range(-window_reach, window_reach + 1):
        for upward in range(-window_reach, window_reach + 1):
            for sideways in range(-window_reach, window_reach + 1):
                length = math.sqrt(across * across + upward * upward + sideways * sideways)
                offsets_list.append((across, upward, sideways, length))
    return offsets_list


def layer_weights(radius):
    radial = radius.astype(jnp.float32)
    return jnp.stack(
        [jnp.maximum(radial - length, 0.0) for across, upward, sideways, length in window_offsets()]
    )


def pad_axis(grid_field, along_axis, before, after_cells):
    widths = [(0, 0)] * grid_field.ndim
    widths[along_axis] = (before, after_cells)
    return jnp.pad(grid_field, widths)


def pad_sides(grid_field):
    return jnp.pad(grid_field, ((0, 0), (window_reach, window_reach), (window_reach, window_reach)))


def filter_forward(padded, weights):
    out_rows = padded.shape[0] - 2 * window_reach
    layers = padded.shape[1] - 2 * window_reach
    row_width = padded.shape[2] - 2 * window_reach
    result = jnp.zeros((out_rows, layers, row_width), jnp.float32)
    for offset_index, (across, upward, sideways, length) in enumerate(window_offsets()):
        shifted = padded[
            window_reach + across : window_reach + across + out_rows,
            window_reach + upward : window_reach + upward + layers,
            window_reach + sideways : window_reach + sideways + row_width,
        ]
        result = result + weights[offset_index][None, :, None] * shifted
    return result


def filter_backward(padded, padded_weights):
    out_rows = padded.shape[0] - 2 * window_reach
    layers = padded.shape[1] - 2 * window_reach
    row_width = padded.shape[2] - 2 * window_reach
    result = jnp.zeros((out_rows, layers, row_width), jnp.float32)
    for offset_index, (across, upward, sideways, length) in enumerate(window_offsets()):
        shifted = padded[
            window_reach - across : window_reach - across + out_rows,
            window_reach - upward : window_reach - upward + layers,
            window_reach - sideways : window_reach - sideways + row_width,
        ]
        layer_part = padded_weights[
            offset_index, window_reach - upward : window_reach - upward + layers
        ]
        result = result + layer_part[None, :, None] * shifted
    return result


def stiff_factors(direction):
    return jnp.array(
        [2.0 if component == direction else 1.0 for component in range(3)], jnp.float32
    ).reshape(3, 1, 1, 1)


def relax_slab(padded, displace, face_x, face_z, face_y, force_field, free_cells, diagonal):
    flux_x = stiff_factors(0) * face_x * jnp.diff(padded, axis=1)
    stencil_image = flux_x[:, :-1] - flux_x[:, 1:]
    flux_z = stiff_factors(1) * face_z * jnp.diff(displace, axis=2)
    stencil_image = stencil_image + pad_axis(flux_z, 2, 1, 0) - pad_axis(flux_z, 2, 0, 1)
    flux_y = stiff_factors(2) * face_y * jnp.diff(displace, axis=3)
    stencil_image = stencil_image + pad_axis(flux_y, 3, 1, 0) - pad_axis(flux_y, 3, 0, 1)
    return free_cells * (displace + relax_factor * (force_field - stencil_image) / diagonal)


def slab_energy(grid_field, along_axis, direction, load_cases):
    change = jnp.diff(grid_field, axis=along_axis)
    return jnp.sum(stiff_factors(direction) * change * change, axis=0) / load_cases


def neighbour_planes(displace, load_cases, axis_devices):
    if axis_devices > load_cases:
        below = from_behind(displace[:, -1:], "space", load_cases)
        above = from_behind(displace[:, :1], "space", -load_cases)
    else:
        below = jnp.zeros_like(displace[:, :1])
        above = jnp.zeros_like(displace[:, :1])
    return jnp.concatenate([below, displace, above], axis=1)


def many_slabs(density, displacement, fixed, load_index, load_force, radius):
    slab_rows, layers, row_width = density.shape
    load_cases = load_index.shape[0]
    level_count = load_cases.bit_length() - 1
    axis_devices = lax.axis_size("space")
    axis_place = lax.axis_index("space")
    slab_planes = slab_rows * load_cases
    slab_place = axis_place // load_cases
    load_place = axis_place % load_cases
    total_rows = slab_rows * axis_devices
    weights = layer_weights(radius)
    padded_weights = pad_axis(weights, 1, window_reach, window_reach)
    global_rows = (
        jnp.arange(slab_rows + 2 * window_reach, dtype=jnp.int32)
        + axis_place * slab_rows
        - window_reach
    )
    deep_inside = ((global_rows >= 0) & (global_rows < total_rows)).astype(jnp.float32)
    inside_field = deep_inside[:, None, None] * pad_sides(
        jnp.ones((slab_rows + 2 * window_reach, layers, row_width), jnp.float32)
    )
    total_weight = filter_forward(inside_field, weights)
    slab_start = slab_place * slab_planes
    margin_rows = jnp.arange(slab_planes + 2, dtype=jnp.int32) + slab_start - 1
    margin_inside = ((margin_rows >= 0) & (margin_rows < total_rows)).astype(jnp.float32)
    face_valid = margin_inside[1:] * margin_inside[:-1]
    fixed_slab = lax.dynamic_slice_in_dim(fixed, slab_start, slab_planes, 0).astype(jnp.float32)
    bottom_layer = (jnp.arange(layers, dtype=jnp.int32) == 0).astype(jnp.float32)
    free_cells = 1.0 - bottom_layer[None, :, None] * fixed_slab[:, None, :]
    slab_cells = slab_planes * layers * row_width
    cell_index = jnp.arange(slab_cells, dtype=jnp.int32) + slab_place * slab_cells
    load_hot = jnp.arange(load_cases, dtype=jnp.int32) == load_place
    own_index = jnp.sum(jnp.where(load_hot, load_index, 0))
    own_force = jnp.sum(load_hot.astype(jnp.float32)[:, None] * load_force, axis=0)
    load_hits = (cell_index == own_index).astype(jnp.float32)
    force_field = (own_force[:, None] * load_hits[None, :]).reshape(
        3, slab_planes, layers, row_width
    )
    displace = displacement[0] * free_cells
    target = volume_share * total_rows * layers * row_width
    padded = neighbour_planes(displace, load_cases, axis_devices)
    halo_density = extended(density, (("space", 0),), window_reach)
    filtered = filter_forward(pad_sides(halo_density), weights) / total_weight
    whole_field = lax.all_gather(filtered, "space", axis=0, tiled=True)
    margin = lax.dynamic_slice_in_dim(
        pad_axis(whole_field, 0, 1, 1), slab_start, slab_planes + 2, 0
    )
    moduli = floor_modulus + (1.0 - floor_modulus) * margin**3
    face_x = 0.5 * (moduli[1:] + moduli[:-1]) * face_valid[:, None, None]
    inner_moduli = moduli[1:-1]
    face_z = 0.5 * (inner_moduli[:, 1:] + inner_moduli[:, :-1])
    face_y = 0.5 * (inner_moduli[:, :, 1:] + inner_moduli[:, :, :-1])
    sum_x = face_x[:-1] + face_x[1:]
    sum_z = pad_axis(face_z, 1, 1, 0) + pad_axis(face_z, 1, 0, 1)
    sum_y = pad_axis(face_y, 2, 1, 0) + pad_axis(face_y, 2, 0, 1)
    diagonal = stiff_factors(0) * sum_x + stiff_factors(1) * sum_z + stiff_factors(2) * sum_y
    for sweep_index in range(SWEEPS):
        displace = relax_slab(
            padded, displace, face_x, face_z, face_y, force_field, free_cells, diagonal
        )
        padded = neighbour_planes(displace, load_cases, axis_devices)
    energy_x = slab_energy(padded, 1, 0, load_cases) * face_valid[:, None, None]
    energy_z = slab_energy(displace, 2, 1, load_cases)
    energy_y = slab_energy(displace, 3, 2, load_cases)
    sens_term = 0.5 * (
        energy_x[:-1]
        + energy_x[1:]
        + pad_axis(energy_z, 1, 1, 0)
        + pad_axis(energy_z, 1, 0, 1)
        + pad_axis(energy_y, 2, 1, 0)
        + pad_axis(energy_y, 2, 0, 1)
    )
    sensitive = sens_term
    for level in reversed(range(level_count)):
        half_rows = sensitive.shape[0] // 2
        upper_side = load_place // 2**level % 2 == 1
        outgoing = jnp.where(upper_side, sensitive[:half_rows], sensitive[half_rows:])
        keeping = jnp.where(upper_side, sensitive[half_rows:], sensitive[:half_rows])
        sensitive = keeping + from_partner(outgoing, "space", level)
    weighted_share = 3.0 * (1.0 - floor_modulus) * filtered**2 * sensitive / total_weight
    halo_share = extended(weighted_share, (("space", 0),), window_reach)
    root_term = jnp.sqrt(filter_backward(pad_sides(halo_share), padded_weights))
    lowest = jnp.maximum(density - move_limit, density_floor)
    highest = jnp.minimum(density + move_limit, 1.0)
    design_now = density

    def trial_design(log_level):
        return jnp.clip(design_now * root_term * jnp.exp(-0.5 * log_level), lowest, highest)

    start_state = (jnp.asarray(log_lower, jnp.float32), jnp.asarray(log_span, jnp.float32))

    def halve(search_step, search_state):
        lower_end, span_width = search_state
        half_span = span_width * 0.5
        middle = lower_end + half_span
        volume_total = lax.psum(jnp.sum(trial_design(middle)), "space")
        return (jnp.where(volume_total > target, middle, lower_end), half_span)

    lower_end, span_width = lax.fori_loop(0, SEARCH, halve, start_state)
    density = trial_design(lower_end + 0.5 * span_width)
    new_displacement = displace[None]
    return (density, new_displacement)


def solution(mesh):
    in_specs = (
        P("space", "parts", None),
        P("space", None, None, "parts", None),
        P(None, "parts"),
        P("parts"),
        P("parts", None),
        P("parts"),
    )
    out_specs = (P("space", "parts", None), P("space", None, None, "parts", None))

    def local(density, displacement, fixed, load_index, load_force, radius):
        alone = lax.axis_size("space") == load_index.shape[0]
        run = one_slab if alone else many_slabs
        return run(density, displacement, fixed, load_index, load_force, radius)

    return jax.shard_map(local, mesh=mesh, in_specs=in_specs, out_specs=out_specs, check_vma=False)
```

```python
import math

import jax
import jax.numpy as jnp
from jax import lax
from jax.experimental import pallas as pl
from jax.experimental.pallas import tpu as pltpu
from jax.sharding import PartitionSpec as P

SWEEPS = 3
SEARCH = 12


floor_modulus = 0.05
relax_factor = 0.6
move_limit = 0.2
density_floor = 0.01
volume_share = 0.5
log_lower = -16.0
log_span = 32.0
window_reach = 2

PLANE_SQUARES = (0, 1, 2, 4, 5, 8)
ALL_SQUARES = (0, 1, 2, 3, 4, 5, 6, 8, 9, 12)


def spot_iota(shape, dim):
    return lax.broadcasted_iota(jnp.int32, shape, dim)


def each_plane(planes, body, carry):
    for x in range(planes):
        carry = body(x, carry)
    return carry


def each_half(planes, body, carry):
    count = planes // 2
    return lax.fori_loop(0, 2, lambda half, carry: body(half * count, count, carry), carry)


def layer_radius(radius_ref, layers, row_width):
    z = spot_iota((layers, row_width), 0)
    result = jnp.zeros((layers, row_width), jnp.int32)
    for layer in range(layers):
        result = jnp.where(z == layer, radius_ref[layer], result)
    return result.astype(jnp.float32)


def class_weights(radius_ref, weight_ref):
    layers, row_width = weight_ref.shape[1:]
    radial = layer_radius(radius_ref, layers, row_width)
    for place, square in enumerate(ALL_SQUARES):
        weight_ref[place] = jnp.maximum(radial - math.sqrt(square), 0.0)


def shift_sum(field, dim, distance):
    size = field.shape[dim]
    spot = spot_iota(field.shape, dim)
    ahead = jnp.where(spot < size - distance, pltpu.roll(field, size - distance, dim), 0.0)
    behind = jnp.where(spot >= distance, pltpu.roll(field, distance, dim), 0.0)
    return ahead + behind


def plane_sums(plane):
    beside = shift_sum(plane, 1, 1)
    further = shift_sum(plane, 1, 2)
    return {
        0: plane,
        1: beside + shift_sum(plane, 0, 1),
        2: shift_sum(beside, 0, 1),
        4: further + shift_sum(plane, 0, 2),
        5: shift_sum(further, 0, 1) + shift_sum(beside, 0, 2),
        8: shift_sum(further, 0, 2),
    }


def weigh(sums, weight_ref, square):
    result = None
    for inner in PLANE_SQUARES:
        term = weight_ref[ALL_SQUARES.index(inner + square)] * sums[inner]
        result = term if result is None else result + term
    return result


def forward_planes(plane, weight_ref):
    sums = plane_sums(plane)
    return [weigh(sums, weight_ref, square) for square in (0, 1, 4)]


def rows(x, layers, shift=0):
    return pl.ds(x * layers + shift, layers)


GAP = 8


def gapped(x, layers, shift=0):
    return pl.ds(GAP + x * (layers + GAP) + shift, layers)


def gap(x, layers):
    return pl.ds(x * (layers + GAP), GAP)


def pair_spot(x, own_planes):
    device = x // own_planes
    apart = device ^ lax.axis_index("space")
    return (apart ^ apart >> 1) & 1, device >> 1, x % own_planes


def half_views(ref, first, count):
    own_planes = ref.shape[2]
    mine = lax.axis_index("space")
    side = (mine ^ mine >> 1) & 1
    chips = pl.ds(first // (2 * own_planes), count // (2 * own_planes))
    views = (ref.at[side, chips], ref.at[1 - side, chips])

    def plane(p):
        device = p // own_planes
        return views[(device ^ device >> 1) & 1], (device >> 1, p % own_planes)

    return plane


def edge_class(x, planes):
    return jnp.minimum(x, 2) + jnp.maximum(x - (planes - 3), 0)


def zero_edges(ref):
    planes = ref.shape[0]
    for place in (0, 1, planes - 2, planes - 1):
        ref[place] = jnp.zeros(ref.shape[1:], ref.dtype)


def group_spots(group, blocks):
    chips, own_planes = blocks.shape[:2]
    mine = lax.axis_index("space")
    core = mine ^ mine >> 1 ^ group
    return [
        (own_planes * (2 * chip + ((core ^ chip) & 1)) + own, (chip, own))
        for chip in range(chips)
        for own in range(own_planes)
    ]


def spread_group(blocks, spread):
    chips, own_planes, layers, row_width = blocks.shape
    zero_gap = jnp.zeros((GAP, row_width), jnp.float32)
    for ref in spread:
        ref[gap(0, layers)] = zero_gap
    for p in range(chips * own_planes):
        plane = blocks[p // own_planes, p % own_planes]
        for ref, field in zip(spread, (plane, shift_sum(plane, 1, 1), shift_sum(plane, 1, 2))):
            ref[gapped(p, layers)] = field
            ref[gap(p + 1, layers)] = zero_gap


def filter_plane(p, layers, spread, weight_ref):
    def around(place, distance):
        ref = spread[place]
        return ref[gapped(p, layers, distance)] + ref[gapped(p, layers, -distance)]

    sums = {
        0: spread[0][gapped(p, layers)],
        1: spread[1][gapped(p, layers)] + around(0, 1),
        2: around(1, 1),
        4: spread[2][gapped(p, layers)] + around(0, 2),
        5: around(2, 1) + around(1, 2),
        8: around(2, 2),
    }
    return [weigh(sums, weight_ref, square) for square in (0, 1, 4)]


def prepare_kernel(
    radius_hbm,
    index_hbm,
    force_hbm,
    fixed_hbm,
    density_ref,
    weight_ref,
    inverse_ref,
    free_ref,
    load_ref,
    spot_ref,
    filter_ref,
    radius_ref,
    index_ref,
    force_ref,
    fixed_ref,
    plane_ref,
    beside_ref,
    further_ref,
    arrived,
):
    copies = [
        pltpu.make_async_copy(source, target, arrived.at[place])
        for place, (source, target) in enumerate(
            (
                (radius_hbm, radius_ref),
                (index_hbm, index_ref),
                (force_hbm, force_ref),
                (fixed_hbm, fixed_ref),
            )
        )
    ]
    for copy in copies:
        copy.start()
    spread = (plane_ref, beside_ref, further_ref)
    spread_group(density_ref, spread)
    for copy in copies:
        copy.wait()
    planes, layers, row_width = free_ref.shape
    load_place = lax.axis_index("space")
    shape = (layers, row_width)
    z = spot_iota(shape, 0)
    y = spot_iota(shape, 1)

    class_weights(radius_ref, weight_ref)
    own_planes = density_ref.shape[1]
    for p in range(density_ref.shape[0] * own_planes):
        for place, field in enumerate(filter_plane(p, layers, spread, weight_ref)):
            filter_ref[place, p // own_planes, p % own_planes] = field

    ones = forward_planes(jnp.ones(shape, jnp.float32), weight_ref)
    for place, (lower, upper) in enumerate(((0, 2), (1, 2), (2, 2), (2, 1), (2, 0))):
        inverse_ref[place] = 1.0 / (
            ones[0] + min(lower, 1) * ones[1] + min(upper, 1) * ones[1]
            + (lower // 2) * ones[2] + (upper // 2) * ones[2]
        )

    def free_plane(x, carry):
        free_ref[x] = jnp.where(
            z == 0, 1.0 - fixed_ref[pl.ds(x, 1), :].astype(jnp.float32), 1.0
        )
        return carry

    each_plane(planes, free_plane, 0)

    own_index = index_ref[load_place]
    own_z = own_index // row_width % layers
    own_y = own_index % row_width
    hit = (z == own_z) & (y == own_y)
    for part in range(3):
        load_ref[part] = jnp.where(hit, force_ref[part, load_place], 0.0)
    own_x = (own_index // (layers * row_width)).astype(jnp.float32)
    spot_ref[...] = jnp.full(spot_ref.shape, own_x)


def sweep_kernel(
    spot_ref,
    load_ref,
    weight_ref,
    inverse_ref,
    free_ref,
    filter_ref,
    density_ref,
    start_ref,
    disp_ref,
    coef_ref,
    plane_ref,
    beside_ref,
    further_ref,
    near_ref,
    side_ref,
    far_ref,
    modulus_ref,
    across_ref,
    up_ref,
    right_ref,
    left_ref,
    rate_ref,
    first_ref,
):
    planes, layers, row_width = coef_ref.shape
    shape = (layers, row_width)
    z = spot_iota(shape, 0)
    y = spot_iota(shape, 1)
    zero = jnp.zeros(shape, jnp.float32)

    for ref in (side_ref, far_ref):
        zero_edges(ref)
    results = (near_ref, side_ref, far_ref)
    other_ref = density_ref.at[1]
    for x, spot in group_spots(0, other_ref):
        for place, ref in enumerate(results):
            ref[x + 2] = filter_ref[(place,) + spot]
    spread = (plane_ref, beside_ref, further_ref)
    spread_group(other_ref, spread)
    for p, (x, spot) in enumerate(group_spots(1, other_ref)):
        for ref, field in zip(results, filter_plane(p, layers, spread, weight_ref)):
            ref[x + 2] = field

    for ref in (first_ref, disp_ref):
        for part in range(3):
            ref[part, rows(0, layers)] = zero
            ref[part, rows(planes + 1, layers)] = zero

    def store_faces(slot, modulus, above, later, before, free, start, views):
        across, up_view, right_view, left_view, rate, source = views
        across[slot] = later
        up = jnp.where(z < layers - 1, 0.5 * (modulus + above), 0.0)
        right = jnp.where(
            y < row_width - 1, 0.5 * (modulus + pltpu.roll(modulus, row_width - 1, 1)), 0.0
        )
        left = pltpu.roll(right, 1, 1)
        up_view[rows(slot, layers)] = up
        right_view[slot] = right
        left_view[slot] = left
        sums = (before + later, up + pltpu.roll(up, 1, 0), left + right)
        every = sums[0] + sums[1] + sums[2]
        diagonal = [every + part_sum for part_sum in sums]
        pair = diagonal[0] * diagonal[1]
        push = relax_factor * free / (pair * diagonal[2])
        side = push * diagonal[2]
        for part, factor in enumerate((side * diagonal[1], side * diagonal[0], push * pair)):
            rate[part, slot] = factor
            source[part, rows(slot, layers)] = start[part] * free

    def modulus_half(first, count, carry):
        near = near_ref.at[pl.ds(first + 2, count)]
        side = side_ref.at[pl.ds(first + 1, count + 2)]
        far = far_ref.at[pl.ds(first, count + 4)]
        moduli = modulus_ref.at[pl.ds(first * layers, (count + 1) * layers)]
        coef = coef_ref.at[pl.ds(first, count)]
        free = free_ref.at[pl.ds(first, count)]
        views = (
            across_ref.at[pl.ds(first, count)],
            up_ref.at[pl.ds(first * layers, count * layers)],
            right_ref.at[pl.ds(first, count)],
            left_ref.at[pl.ds(first, count)],
            rate_ref.at[:, pl.ds(first, count)],
            first_ref.at[:, pl.ds(first * layers, count * layers)],
        )
        modulus, before = carry
        for p in range(count):
            inverse = inverse_ref[edge_class(first + p, planes)]
            filtered = near[p] + side[p] + side[p + 2] + far[p] + far[p + 4]
            filtered = filtered * inverse
            later = floor_modulus + (1.0 - floor_modulus) * (filtered * filtered * filtered)
            coef[p] = 3.0 * (1.0 - floor_modulus) * (filtered * filtered) * inverse
            moduli[rows(p + 1, layers)] = later
            ahead = 0.5 * (modulus + later)
            if p == 0:
                ahead = jnp.where(first > 0, ahead, 0.0)
            above = moduli[rows(p, layers, 1)] if p else pltpu.roll(modulus, layers - 1, 0)
            previous = jnp.maximum(first + p - 1, 0)
            store_faces(
                p,
                modulus,
                above,
                ahead,
                before,
                free_ref[previous],
                [start_ref[part, previous] for part in range(3)],
                views,
            )
            modulus, before = later, ahead
        return modulus, before

    modulus, before = each_half(planes, modulus_half, (jnp.ones(shape, jnp.float32), zero))
    store_faces(
        planes,
        modulus,
        pltpu.roll(modulus, layers - 1, 0),
        zero,
        before,
        free_ref[planes - 1],
        [start_ref[part, planes - 1] for part in range(3)],
        (across_ref, up_ref, right_ref, left_ref, rate_ref, first_ref),
    )

    own_x = jnp.max(spot_ref[...]).astype(jnp.int32)

    def sweep(source, target):
        def sweep_half(first, count, carry):
            old = source.at[:, pl.ds(first * layers, (count + 2) * layers)]
            new = target.at[:, pl.ds((first + 1) * layers, count * layers)]
            across = across_ref.at[pl.ds(first, count + 1)]
            up = up_ref.at[pl.ds(first * layers, (count + 1) * layers)]
            right = right_ref.at[pl.ds(first + 1, count)]
            left = left_ref.at[pl.ds(first + 1, count)]
            rate = rate_ref.at[:, pl.ds(first + 1, count)]
            behind = [old[part, rows(0, layers)] for part in range(3)]
            here = [old[part, rows(1, layers)] for part in range(3)]
            for p in range(count):
                ahead = [old[part, rows(p + 2, layers)] for part in range(3)]
                for part in range(3):
                    pulls = [
                        across[p] * behind[part] + across[p + 1] * ahead[part],
                        up[rows(p + 1, layers)] * old[part, rows(p + 1, layers, 1)]
                        + up[rows(p + 1, layers, -1)] * old[part, rows(p + 1, layers, -1)],
                        right[p] * pltpu.roll(here[part], row_width - 1, 1)
                        + left[p] * pltpu.roll(here[part], 1, 1),
                    ]
                    pull = pulls[0] + pulls[1] + pulls[2] + pulls[part]
                    new[part, rows(p, layers)] = (
                        1.0 - relax_factor
                    ) * here[part] + rate[part, p] * pull
                behind, here = here, ahead
            return carry

        each_half(planes, sweep_half, 0)
        for part in range(3):
            target[part, rows(own_x + 1, layers)] += rate_ref[part, own_x + 1] * load_ref[part]

    def two_sweeps(turn, carry):
        sweep(first_ref, disp_ref)

        @pl.when(turn < SWEEPS // 2)
        def _():
            sweep(disp_ref, first_ref)

        return carry

    lax.fori_loop(0, SWEEPS // 2 + 1, two_sweeps, 0)


def energy_planes(group, disp_ref, sens_ref):
    chips, own_planes, layers, row_width = sens_ref.shape
    planes = disp_ref.shape[1] // layers - 2
    load_cases = lax.axis_size("space")
    shape = (layers, row_width)
    z = spot_iota(shape, 0)
    y = spot_iota(shape, 1)
    zero = jnp.zeros(shape, jnp.float32)
    mine = lax.axis_index("space")
    core = mine ^ mine >> 1 ^ group

    def between(x):
        result = zero
        for part in range(3):
            step = disp_ref[part, rows(x + 1, layers)] - disp_ref[part, rows(x, layers)]
            result = result + (2.0 if part == 0 else 1.0) * (step * step)
        return jnp.where((x > 0) & (x < planes), result, 0.0)

    def inside(x):
        upward, right = zero, zero
        for part in range(3):
            here = disp_ref[part, rows(x + 1, layers)]
            climb = disp_ref[part, rows(x + 1, layers, 1)] - here
            slide = pltpu.roll(here, row_width - 1, 1) - here
            upward = upward + (2.0 if part == 1 else 1.0) * (climb * climb)
            right = right + (2.0 if part == 2 else 1.0) * (slide * slide)
        upward = jnp.where(z < layers - 1, upward, 0.0)
        right = jnp.where(y < row_width - 1, right, 0.0)
        return upward + pltpu.roll(upward, 1, 0) + right + pltpu.roll(right, 1, 1)

    for chip in range(chips):
        first = own_planes * (2 * chip + ((core ^ chip) & 1))
        before = between(first)
        for own in range(own_planes):
            after = between(first + own + 1)
            sens_ref[chip, own] = (0.5 / load_cases) * (before + after + inside(first + own))
            before = after


def sent_energy_kernel(disp_ref, sens_ref):
    energy_planes(1, disp_ref, sens_ref)


def kept_energy_kernel(disp_ref, disp_hbm, sens_ref, stored):
    layers = sens_ref.shape[2]
    inner = pl.ds(layers, disp_ref.shape[1] - 2 * layers)
    store = pltpu.make_async_copy(disp_ref.at[:, inner], disp_hbm, stored)
    store.start()
    energy_planes(0, disp_ref, sens_ref)
    store.wait()


def design_kernel(
    weight_ref,
    sens_ref,
    coef_ref,
    density_ref,
    new_ref,
    plane_ref,
    beside_ref,
    further_ref,
    near_ref,
    far_ref,
    pull_ref,
    low_ref,
    high_ref,
):
    planes, layers, row_width = coef_ref.shape
    own_planes = density_ref.shape[2]
    place = lax.axis_index("space")
    shape = (layers, row_width)
    zero = jnp.zeros(shape, jnp.float32)
    zero_gap = jnp.zeros((GAP, row_width), jnp.float32)
    for ref in (plane_ref, beside_ref, further_ref):
        zero_edges(ref)

    def spread_half(first, count, carry):
        sens = half_views(sens_ref, first, count)
        coef = coef_ref.at[pl.ds(first, count)]
        plane_view, beside, further = (
            ref.at[pl.ds(first + 2, count)] for ref in (plane_ref, beside_ref, further_ref)
        )
        for p in range(count):
            view, spot = sens(p)
            plane = view[spot] * coef[p]
            plane_view[p] = plane
            beside[p] = shift_sum(plane, 1, 1)
            further[p] = shift_sum(plane, 1, 2)
        return carry

    each_half(planes, spread_half, 0)

    def root_half(first, count, carry):
        density_at = half_views(density_ref, first, count)
        plane_view, beside, further = (
            ref.at[pl.ds(first, count + 4)] for ref in (plane_ref, beside_ref, further_ref)
        )
        near, far = (
            ref.at[pl.ds(first * (layers + GAP), count * (layers + GAP) + GAP)]
            for ref in (near_ref, far_ref)
        )
        for ref in (near, far):
            ref[gap(0, layers)] = zero_gap
        pull, low, high = (
            ref.at[pl.ds(first, count)] for ref in (pull_ref, low_ref, high_ref)
        )
        for p in range(count):

            def around(ref, distance):
                return ref[p + 2 + distance] + ref[p + 2 - distance]

            sums = {
                0: plane_view[p + 2],
                1: beside[p + 2] + around(plane_view, 1),
                2: around(beside, 1),
                4: further[p + 2] + around(plane_view, 2),
                5: around(further, 1) + around(beside, 2),
                8: around(further, 2),
            }
            level = weigh(sums, weight_ref, 0)
            for ref, square in ((near, 1), (far, 4)):
                ref[gapped(p, layers)] = weigh(sums, weight_ref, square)
                ref[gap(p + 1, layers)] = zero_gap
            root = jnp.sqrt(
                level
                + near[gapped(p, layers, 1)]
                + near[gapped(p, layers, -1)]
                + far[gapped(p, layers, 2)]
                + far[gapped(p, layers, -2)]
            )
            view, spot = density_at(p)
            density = view[spot]
            pull[p] = density * root
            low[p] = jnp.maximum(density - move_limit, density_floor)
            high[p] = jnp.minimum(density + move_limit, 1.0)
        return carry

    each_half(planes, root_half, 0)

    target = volume_share * planes * layers * row_width

    def trial(x, factor):
        return jnp.minimum(jnp.maximum(pull_ref[x] * factor, low_ref[x]), high_ref[x])

    def factor_of(log_level):
        return jnp.broadcast_to(jnp.exp(-0.5 * log_level), shape)

    def exceeds(total):
        return jnp.sum(jnp.sum(total, axis=0, keepdims=True), axis=1, keepdims=True) > target

    def halve_twice(step, state):
        lower, span = state
        half, quarter = span * 0.5, span * 0.25
        middles = (lower + quarter, lower + half, lower + half + quarter)
        factors = [factor_of(middle) for middle in middles]
        totals = [zero, zero, zero]
        for x in range(planes):
            pull, low, high = pull_ref[x], low_ref[x], high_ref[x]
            totals = [
                total + jnp.minimum(jnp.maximum(pull * factor, low), high)
                for total, factor in zip(totals, factors)
            ]
        first, second, third = (exceeds(total) for total in totals)
        upper = jnp.where(third, middles[2], middles[1])
        below = jnp.where(first, middles[0], lower)
        return jnp.where(second, upper, below), quarter

    start = (jnp.full((1, 1), log_lower, jnp.float32), jnp.full((1, 1), log_span, jnp.float32))
    lower, span = lax.fori_loop(0, SEARCH // 2, halve_twice, start)
    factor = factor_of(lower + 0.5 * span)
    for own in range(own_planes):
        new_ref[own] = trial(place * own_planes + own, factor)


def in_vmem():
    return pl.BlockSpec(memory_space=pltpu.VMEM)


KERNEL_VMEM = 24 * 2**20


def floats(*shape):
    return jax.ShapeDtypeStruct(shape, jnp.float32)


def prepare_call(density, radius, load_index, load_force, fixed):
    chips, own_planes, layers, row_width = density.shape
    planes = fixed.shape[0]
    spread = pltpu.VMEM((chips * own_planes * (layers + GAP) + GAP, row_width), jnp.float32)
    return pl.pallas_call(
        prepare_kernel,
        out_shape=[
            floats(len(ALL_SQUARES), layers, row_width),
            floats(2 * window_reach + 1, layers, row_width),
            floats(planes, layers, row_width),
            floats(3, layers, row_width),
            floats(8, row_width),
            floats(3, *density.shape),
        ],
        in_specs=[pl.BlockSpec(memory_space=pltpu.HBM)] * 4 + [in_vmem()],
        out_specs=[in_vmem()] * 6,
        scratch_shapes=[
            pltpu.SMEM(radius.shape, radius.dtype),
            pltpu.SMEM(load_index.shape, load_index.dtype),
            pltpu.SMEM(load_force.shape, load_force.dtype),
            pltpu.VMEM(fixed.shape, fixed.dtype),
            spread,
            spread,
            spread,
            pltpu.SemaphoreType.DMA((4,)),
        ],
        compiler_params=pltpu.CompilerParams(vmem_limit_bytes=KERNEL_VMEM),
        cost_estimate=pl.CostEstimate(
            flops=80 * planes * layers * row_width,
            bytes_accessed=8 * planes * layers * row_width,
            transcendentals=0,
        ),
        name="prepare",
    )(
        *(
            pltpu.with_memory_space_constraint(array, pltpu.HBM)
            for array in (radius, load_index, load_force, fixed)
        ),
        density,
    )


def sweep_call(spot, load, weights, inverses, free, filtered, density, displacement):
    groups, chips, own_planes, layers, row_width = density.shape
    planes = groups * chips * own_planes

    def scratch(*lead):
        return pltpu.VMEM(lead + (row_width,), jnp.float32)

    return pl.pallas_call(
        sweep_kernel,
        out_shape=[
            floats(3, (planes + 2) * layers, row_width),
            floats(planes, layers, row_width),
        ],
        in_specs=[in_vmem()] * 8,
        out_specs=[in_vmem()] * 2,
        scratch_shapes=[
            scratch(planes // 2 * (layers + GAP) + GAP),
            scratch(planes // 2 * (layers + GAP) + GAP),
            scratch(planes // 2 * (layers + GAP) + GAP),
            scratch(planes + 4, layers),
            scratch(planes + 4, layers),
            scratch(planes + 4, layers),
            scratch((planes + 1) * layers),
            scratch(planes + 1, layers),
            scratch((planes + 1) * layers),
            scratch(planes + 1, layers),
            scratch(planes + 1, layers),
            scratch(3, planes + 1, layers),
            scratch(3, (planes + 2) * layers),
        ],
        compiler_params=pltpu.CompilerParams(vmem_limit_bytes=KERNEL_VMEM),
        name="sweeps",
    )(spot, load, weights, inverses, free, filtered, density, displacement)


def sent_energy_call(disp, group_shape):
    return pl.pallas_call(
        sent_energy_kernel,
        out_shape=floats(*group_shape),
        in_specs=[in_vmem()],
        out_specs=in_vmem(),
        compiler_params=pltpu.CompilerParams(vmem_limit_bytes=KERNEL_VMEM),
        name="sent_energy",
    )(disp)


def kept_energy_call(disp, group_shape):
    parts, disp_rows, row_width = disp.shape
    layers = group_shape[2]
    return pl.pallas_call(
        kept_energy_kernel,
        out_shape=[floats(parts, disp_rows - 2 * layers, row_width), floats(*group_shape)],
        in_specs=[in_vmem()],
        out_specs=[pl.BlockSpec(memory_space=pltpu.HBM), in_vmem()],
        scratch_shapes=[pltpu.SemaphoreType.DMA(())],
        compiler_params=pltpu.CompilerParams(vmem_limit_bytes=KERNEL_VMEM),
        cost_estimate=pl.CostEstimate(
            flops=20 * disp.size, bytes_accessed=8 * disp.size, transcendentals=0
        ),
        name="kept_energy",
    )(disp)


def design_call(weights, sens, coef, density):
    cores, chips, own_planes, layers, row_width = density.shape
    planes = cores * chips * own_planes

    def scratch(*lead):
        return pltpu.VMEM(lead + (row_width,), jnp.float32)

    return pl.pallas_call(
        design_kernel,
        out_shape=floats(own_planes, layers, row_width),
        in_specs=[in_vmem()] * 4,
        out_specs=in_vmem(),
        scratch_shapes=[
            scratch(planes + 4, layers),
            scratch(planes + 4, layers),
            scratch(planes + 4, layers),
            scratch(planes * (layers + GAP) + GAP),
            scratch(planes * (layers + GAP) + GAP),
            scratch(planes, layers),
            scratch(planes, layers),
            scratch(planes, layers),
        ],
        compiler_params=pltpu.CompilerParams(vmem_limit_bytes=KERNEL_VMEM),
        name="design",
    )(weights, sens, coef, density)


def other_core(block):
    devices = lax.axis_size("space")
    return lax.ppermute(block, "space", [(i, i ^ 1) for i in range(devices)])


def chip_groups():
    chips = lax.axis_size("space") // 2
    return [[2 * chip + (chip ^ group) % 2 for chip in range(chips)] for group in range(2)]


def between_chips(pieces):
    return lax.all_to_all(pieces, "space", 0, 0, axis_index_groups=chip_groups())


def chip_gathered(block):
    chips = lax.axis_size("space") // 2
    return between_chips(jnp.broadcast_to(block[None], (chips,) + block.shape))


def with_other_core(blocks):
    return jnp.stack([blocks, other_core(blocks)])


def scattered_sum(sent, make_kept):
    received = other_core(sent)
    *others, kept = make_kept()
    return jnp.sum(between_chips(kept + received), axis=0), others


def one_slab(density, displacement, fixed, load_index, load_force, radius):
    same_group, small = lax.optimization_barrier(
        (chip_gathered(density), (radius, load_index, load_force.T, fixed))
    )
    other_group = other_core(same_group)
    weights, inverses, free, load, spot, filtered = prepare_call(same_group, *small)
    whole = jnp.stack([same_group, other_group])
    disp, coef = sweep_call(
        spot, load, weights, inverses, free, filtered, whole, displacement[0]
    )
    sent, disp = lax.optimization_barrier((sent_energy_call(disp, same_group.shape), disp))
    sens, (new_displacement,) = scattered_sum(
        sent, lambda: kept_energy_call(disp, same_group.shape)
    )
    sens = with_other_core(chip_gathered(sens))
    new_density = design_call(weights, sens, coef, whole)
    return new_density, new_displacement.reshape(displacement.shape)


def from_behind(block, axis, distance):
    devices = range(lax.axis_size(axis))
    route = [(i - distance, i) for i in devices if i - distance in devices]
    return lax.ppermute(block, axis, route)


def extended(x, sides, width):
    for axis, dim in sides:
        size, length = (lax.axis_size(axis), x.shape[dim])
        up = [(i, (i + 1) % size) for i in range(size - 1)]
        down = [(j, i) for i, j in up]
        last = lax.slice_in_dim(x, length - width, length, axis=dim)
        first = lax.slice_in_dim(x, 0, width, axis=dim)
        before = lax.ppermute(last, axis, up)
        after = lax.ppermute(first, axis, down)
        x = jnp.concatenate([before, x, after], axis=dim)
    return x


def from_partner(x, axis, bit):
    return lax.ppermute(x, axis, [(i, i ^ 1 << bit) for i in range(lax.axis_size(axis))])


def window_offsets():
    offsets_list = []
    for across in range(-window_reach, window_reach + 1):
        for upward in range(-window_reach, window_reach + 1):
            for sideways in range(-window_reach, window_reach + 1):
                length = math.sqrt(across * across + upward * upward + sideways * sideways)
                offsets_list.append((across, upward, sideways, length))
    return offsets_list


def layer_weights(radius):
    radial = radius.astype(jnp.float32)
    return jnp.stack(
        [jnp.maximum(radial - length, 0.0) for across, upward, sideways, length in window_offsets()]
    )


def pad_axis(grid_field, along_axis, before, after_cells):
    widths = [(0, 0)] * grid_field.ndim
    widths[along_axis] = (before, after_cells)
    return jnp.pad(grid_field, widths)


def pad_sides(grid_field):
    return jnp.pad(grid_field, ((0, 0), (window_reach, window_reach), (window_reach, window_reach)))


def filter_forward(padded, weights):
    out_rows = padded.shape[0] - 2 * window_reach
    layers = padded.shape[1] - 2 * window_reach
    row_width = padded.shape[2] - 2 * window_reach
    result = jnp.zeros((out_rows, layers, row_width), jnp.float32)
    for offset_index, (across, upward, sideways, length) in enumerate(window_offsets()):
        shifted = padded[
            window_reach + across : window_reach + across + out_rows,
            window_reach + upward : window_reach + upward + layers,
            window_reach + sideways : window_reach + sideways + row_width,
        ]
        result = result + weights[offset_index][None, :, None] * shifted
    return result


def filter_backward(padded, padded_weights):
    out_rows = padded.shape[0] - 2 * window_reach
    layers = padded.shape[1] - 2 * window_reach
    row_width = padded.shape[2] - 2 * window_reach
    result = jnp.zeros((out_rows, layers, row_width), jnp.float32)
    for offset_index, (across, upward, sideways, length) in enumerate(window_offsets()):
        shifted = padded[
            window_reach - across : window_reach - across + out_rows,
            window_reach - upward : window_reach - upward + layers,
            window_reach - sideways : window_reach - sideways + row_width,
        ]
        layer_part = padded_weights[
            offset_index, window_reach - upward : window_reach - upward + layers
        ]
        result = result + layer_part[None, :, None] * shifted
    return result


def stiff_factors(direction):
    return jnp.array(
        [2.0 if component == direction else 1.0 for component in range(3)], jnp.float32
    ).reshape(3, 1, 1, 1)


def relax_slab(padded, displace, face_x, face_z, face_y, force_field, free_cells, diagonal):
    flux_x = stiff_factors(0) * face_x * jnp.diff(padded, axis=1)
    stencil_image = flux_x[:, :-1] - flux_x[:, 1:]
    flux_z = stiff_factors(1) * face_z * jnp.diff(displace, axis=2)
    stencil_image = stencil_image + pad_axis(flux_z, 2, 1, 0) - pad_axis(flux_z, 2, 0, 1)
    flux_y = stiff_factors(2) * face_y * jnp.diff(displace, axis=3)
    stencil_image = stencil_image + pad_axis(flux_y, 3, 1, 0) - pad_axis(flux_y, 3, 0, 1)
    return free_cells * (displace + relax_factor * (force_field - stencil_image) / diagonal)


def slab_energy(grid_field, along_axis, direction, load_cases):
    change = jnp.diff(grid_field, axis=along_axis)
    return jnp.sum(stiff_factors(direction) * change * change, axis=0) / load_cases


def neighbour_planes(displace, load_cases, axis_devices):
    if axis_devices > load_cases:
        below = from_behind(displace[:, -1:], "space", load_cases)
        above = from_behind(displace[:, :1], "space", -load_cases)
    else:
        below = jnp.zeros_like(displace[:, :1])
        above = jnp.zeros_like(displace[:, :1])
    return jnp.concatenate([below, displace, above], axis=1)


def many_slabs(density, displacement, fixed, load_index, load_force, radius):
    slab_rows, layers, row_width = density.shape
    load_cases = load_index.shape[0]
    level_count = load_cases.bit_length() - 1
    axis_devices = lax.axis_size("space")
    axis_place = lax.axis_index("space")
    slab_planes = slab_rows * load_cases
    slab_place = axis_place // load_cases
    load_place = axis_place % load_cases
    total_rows = slab_rows * axis_devices
    weights = layer_weights(radius)
    padded_weights = pad_axis(weights, 1, window_reach, window_reach)
    global_rows = (
        jnp.arange(slab_rows + 2 * window_reach, dtype=jnp.int32)
        + axis_place * slab_rows
        - window_reach
    )
    deep_inside = ((global_rows >= 0) & (global_rows < total_rows)).astype(jnp.float32)
    inside_field = deep_inside[:, None, None] * pad_sides(
        jnp.ones((slab_rows + 2 * window_reach, layers, row_width), jnp.float32)
    )
    total_weight = filter_forward(inside_field, weights)
    slab_start = slab_place * slab_planes
    margin_rows = jnp.arange(slab_planes + 2, dtype=jnp.int32) + slab_start - 1
    margin_inside = ((margin_rows >= 0) & (margin_rows < total_rows)).astype(jnp.float32)
    face_valid = margin_inside[1:] * margin_inside[:-1]
    fixed_slab = lax.dynamic_slice_in_dim(fixed, slab_start, slab_planes, 0).astype(jnp.float32)
    bottom_layer = (jnp.arange(layers, dtype=jnp.int32) == 0).astype(jnp.float32)
    free_cells = 1.0 - bottom_layer[None, :, None] * fixed_slab[:, None, :]
    slab_cells = slab_planes * layers * row_width
    cell_index = jnp.arange(slab_cells, dtype=jnp.int32) + slab_place * slab_cells
    load_hot = jnp.arange(load_cases, dtype=jnp.int32) == load_place
    own_index = jnp.sum(jnp.where(load_hot, load_index, 0))
    own_force = jnp.sum(load_hot.astype(jnp.float32)[:, None] * load_force, axis=0)
    load_hits = (cell_index == own_index).astype(jnp.float32)
    force_field = (own_force[:, None] * load_hits[None, :]).reshape(
        3, slab_planes, layers, row_width
    )
    displace = displacement[0] * free_cells
    target = volume_share * total_rows * layers * row_width
    padded = neighbour_planes(displace, load_cases, axis_devices)
    halo_density = extended(density, (("space", 0),), window_reach)
    filtered = filter_forward(pad_sides(halo_density), weights) / total_weight
    whole_field = lax.all_gather(filtered, "space", axis=0, tiled=True)
    margin = lax.dynamic_slice_in_dim(
        pad_axis(whole_field, 0, 1, 1), slab_start, slab_planes + 2, 0
    )
    moduli = floor_modulus + (1.0 - floor_modulus) * margin**3
    face_x = 0.5 * (moduli[1:] + moduli[:-1]) * face_valid[:, None, None]
    inner_moduli = moduli[1:-1]
    face_z = 0.5 * (inner_moduli[:, 1:] + inner_moduli[:, :-1])
    face_y = 0.5 * (inner_moduli[:, :, 1:] + inner_moduli[:, :, :-1])
    sum_x = face_x[:-1] + face_x[1:]
    sum_z = pad_axis(face_z, 1, 1, 0) + pad_axis(face_z, 1, 0, 1)
    sum_y = pad_axis(face_y, 2, 1, 0) + pad_axis(face_y, 2, 0, 1)
    diagonal = stiff_factors(0) * sum_x + stiff_factors(1) * sum_z + stiff_factors(2) * sum_y
    for sweep_index in range(SWEEPS):
        displace = relax_slab(
            padded, displace, face_x, face_z, face_y, force_field, free_cells, diagonal
        )
        padded = neighbour_planes(displace, load_cases, axis_devices)
    energy_x = slab_energy(padded, 1, 0, load_cases) * face_valid[:, None, None]
    energy_z = slab_energy(displace, 2, 1, load_cases)
    energy_y = slab_energy(displace, 3, 2, load_cases)
    sens_term = 0.5 * (
        energy_x[:-1]
        + energy_x[1:]
        + pad_axis(energy_z, 1, 1, 0)
        + pad_axis(energy_z, 1, 0, 1)
        + pad_axis(energy_y, 2, 1, 0)
        + pad_axis(energy_y, 2, 0, 1)
    )
    sensitive = sens_term
    for level in reversed(range(level_count)):
        half_rows = sensitive.shape[0] // 2
        upper_side = load_place // 2**level % 2 == 1
        outgoing = jnp.where(upper_side, sensitive[:half_rows], sensitive[half_rows:])
        keeping = jnp.where(upper_side, sensitive[half_rows:], sensitive[:half_rows])
        sensitive = keeping + from_partner(outgoing, "space", level)
    weighted_share = 3.0 * (1.0 - floor_modulus) * filtered**2 * sensitive / total_weight
    halo_share = extended(weighted_share, (("space", 0),), window_reach)
    root_term = jnp.sqrt(filter_backward(pad_sides(halo_share), padded_weights))
    lowest = jnp.maximum(density - move_limit, density_floor)
    highest = jnp.minimum(density + move_limit, 1.0)
    design_now = density

    def trial_design(log_level):
        return jnp.clip(design_now * root_term * jnp.exp(-0.5 * log_level), lowest, highest)

    start_state = (jnp.asarray(log_lower, jnp.float32), jnp.asarray(log_span, jnp.float32))

    def halve(search_step, search_state):
        lower_end, span_width = search_state
        half_span = span_width * 0.5
        middle = lower_end + half_span
        volume_total = lax.psum(jnp.sum(trial_design(middle)), "space")
        return (jnp.where(volume_total > target, middle, lower_end), half_span)

    lower_end, span_width = lax.fori_loop(0, SEARCH, halve, start_state)
    density = trial_design(lower_end + 0.5 * span_width)
    new_displacement = displace[None]
    return (density, new_displacement)


def solution(mesh):
    in_specs = (
        P("space", "parts", None),
        P("space", None, None, "parts", None),
        P(None, "parts"),
        P("parts"),
        P("parts", None),
        P("parts"),
    )
    out_specs = (P("space", "parts", None), P("space", None, None, "parts", None))

    def local(density, displacement, fixed, load_index, load_force, radius):
        alone = lax.axis_size("space") == load_index.shape[0]
        run = one_slab if alone else many_slabs
        return run(density, displacement, fixed, load_index, load_force, radius)

    return jax.shard_map(local, mesh=mesh, in_specs=in_specs, out_specs=out_specs, check_vma=False)
```

```python
import math

import jax
import jax.numpy as jnp
from jax import lax
from jax.experimental import pallas as pl
from jax.experimental.pallas import tpu as pltpu
from jax.sharding import PartitionSpec as P

SWEEPS = 3
SEARCH = 12


floor_modulus = 0.05
relax_factor = 0.6
move_limit = 0.2
density_floor = 0.01
volume_share = 0.5
log_lower = -16.0
log_span = 32.0
window_reach = 2

PLANE_SQUARES = (0, 1, 2, 4, 5, 8)
ALL_SQUARES = (0, 1, 2, 3, 4, 5, 6, 8, 9, 12)


def spot_iota(shape, dim):
    return lax.broadcasted_iota(jnp.int32, shape, dim)


def each_plane(planes, body, carry):
    for x in range(planes):
        carry = body(x, carry)
    return carry


def each_half(planes, body, carry):
    count = planes // 2
    return lax.fori_loop(0, 2, lambda half, carry: body(half * count, count, carry), carry)


def layer_radius(radius_ref, layers, row_width):
    z = spot_iota((layers, row_width), 0)
    result = jnp.zeros((layers, row_width), jnp.int32)
    for layer in range(layers):
        result = jnp.where(z == layer, radius_ref[layer], result)
    return result.astype(jnp.float32)


def class_weights(radius_ref, weight_ref):
    layers, row_width = weight_ref.shape[1:]
    radial = layer_radius(radius_ref, layers, row_width)
    for place, square in enumerate(ALL_SQUARES):
        weight_ref[place] = jnp.maximum(radial - math.sqrt(square), 0.0)


def shift_sum(field, dim, distance):
    size = field.shape[dim]
    spot = spot_iota(field.shape, dim)
    ahead = jnp.where(spot < size - distance, pltpu.roll(field, size - distance, dim), 0.0)
    behind = jnp.where(spot >= distance, pltpu.roll(field, distance, dim), 0.0)
    return ahead + behind


def plane_sums(plane):
    beside = shift_sum(plane, 1, 1)
    further = shift_sum(plane, 1, 2)
    return {
        0: plane,
        1: beside + shift_sum(plane, 0, 1),
        2: shift_sum(beside, 0, 1),
        4: further + shift_sum(plane, 0, 2),
        5: shift_sum(further, 0, 1) + shift_sum(beside, 0, 2),
        8: shift_sum(further, 0, 2),
    }


def weigh(sums, weight_ref, square):
    result = None
    for inner in PLANE_SQUARES:
        term = weight_ref[ALL_SQUARES.index(inner + square)] * sums[inner]
        result = term if result is None else result + term
    return result


def forward_planes(plane, weight_ref):
    sums = plane_sums(plane)
    return [weigh(sums, weight_ref, square) for square in (0, 1, 4)]


def rows(x, layers, shift=0):
    return pl.ds(x * layers + shift, layers)


GAP = 8


def gapped(x, layers, shift=0):
    return pl.ds(GAP + x * (layers + GAP) + shift, layers)


def gap(x, layers):
    return pl.ds(x * (layers + GAP), GAP)


def edge_class(x, planes):
    return jnp.minimum(x, 2) + jnp.maximum(x - (planes - 3), 0)


def zero_edges(ref):
    planes = ref.shape[0]
    for place in (0, 1, planes - 2, planes - 1):
        ref[place] = jnp.zeros(ref.shape[1:], ref.dtype)


def group_spots(group, blocks):
    chips, own_planes = blocks.shape[:2]
    mine = lax.axis_index("space")
    core = mine ^ mine >> 1 ^ group
    return [
        (own_planes * (2 * chip + ((core ^ chip) & 1)) + own, (chip, own))
        for chip in range(chips)
        for own in range(own_planes)
    ]


def spread_group(blocks, spread):
    chips, own_planes, layers, row_width = blocks.shape
    zero_gap = jnp.zeros((GAP, row_width), jnp.float32)
    for ref in spread:
        ref[gap(0, layers)] = zero_gap
    for p in range(chips * own_planes):
        plane = blocks[p // own_planes, p % own_planes]
        for ref, field in zip(spread, (plane, shift_sum(plane, 1, 1), shift_sum(plane, 1, 2))):
            ref[gapped(p, layers)] = field
            ref[gap(p + 1, layers)] = zero_gap


def filter_plane(p, layers, spread, weight_ref):
    def around(place, distance):
        ref = spread[place]
        return ref[gapped(p, layers, distance)] + ref[gapped(p, layers, -distance)]

    sums = {
        0: spread[0][gapped(p, layers)],
        1: spread[1][gapped(p, layers)] + around(0, 1),
        2: around(1, 1),
        4: spread[2][gapped(p, layers)] + around(0, 2),
        5: around(2, 1) + around(1, 2),
        8: around(2, 2),
    }
    return [weigh(sums, weight_ref, square) for square in (0, 1, 4)]


def prepare_kernel(
    radius_hbm,
    index_hbm,
    force_hbm,
    fixed_hbm,
    density_ref,
    weight_ref,
    inverse_ref,
    free_ref,
    load_ref,
    spot_ref,
    filter_ref,
    radius_ref,
    index_ref,
    force_ref,
    fixed_ref,
    plane_ref,
    beside_ref,
    further_ref,
    arrived,
):
    copies = [
        pltpu.make_async_copy(source, target, arrived.at[place])
        for place, (source, target) in enumerate(
            (
                (radius_hbm, radius_ref),
                (index_hbm, index_ref),
                (force_hbm, force_ref),
                (fixed_hbm, fixed_ref),
            )
        )
    ]
    for copy in copies:
        copy.start()
    spread = (plane_ref, beside_ref, further_ref)
    spread_group(density_ref, spread)
    for copy in copies:
        copy.wait()
    planes, layers, row_width = free_ref.shape
    load_place = lax.axis_index("space")
    shape = (layers, row_width)
    z = spot_iota(shape, 0)
    y = spot_iota(shape, 1)

    class_weights(radius_ref, weight_ref)
    own_planes = density_ref.shape[1]
    for p in range(density_ref.shape[0] * own_planes):
        for place, field in enumerate(filter_plane(p, layers, spread, weight_ref)):
            filter_ref[place, p // own_planes, p % own_planes] = field

    ones = forward_planes(jnp.ones(shape, jnp.float32), weight_ref)
    for place, (lower, upper) in enumerate(((0, 2), (1, 2), (2, 2), (2, 1), (2, 0))):
        inverse_ref[place] = 1.0 / (
            ones[0] + min(lower, 1) * ones[1] + min(upper, 1) * ones[1]
            + (lower // 2) * ones[2] + (upper // 2) * ones[2]
        )

    def free_plane(x, carry):
        free_ref[x] = jnp.where(
            z == 0, 1.0 - fixed_ref[pl.ds(x, 1), :].astype(jnp.float32), 1.0
        )
        return carry

    each_plane(planes, free_plane, 0)

    own_index = index_ref[load_place]
    own_z = own_index // row_width % layers
    own_y = own_index % row_width
    hit = (z == own_z) & (y == own_y)
    for part in range(3):
        load_ref[part] = jnp.where(hit, force_ref[part, load_place], 0.0)
    own_x = (own_index // (layers * row_width)).astype(jnp.float32)
    spot_ref[...] = jnp.full(spot_ref.shape, own_x)


def sweep_kernel(
    spot_ref,
    load_ref,
    weight_ref,
    inverse_ref,
    free_ref,
    filter_ref,
    density_ref,
    start_ref,
    disp_ref,
    coef_ref,
    plane_ref,
    beside_ref,
    further_ref,
    near_ref,
    side_ref,
    far_ref,
    modulus_ref,
    across_ref,
    up_ref,
    right_ref,
    left_ref,
    rate_ref,
    first_ref,
):
    planes, layers, row_width = coef_ref.shape
    shape = (layers, row_width)
    z = spot_iota(shape, 0)
    y = spot_iota(shape, 1)
    zero = jnp.zeros(shape, jnp.float32)

    for ref in (side_ref, far_ref):
        zero_edges(ref)
    results = (near_ref, side_ref, far_ref)
    other_ref = density_ref.at[1]
    for x, spot in group_spots(0, other_ref):
        for place, ref in enumerate(results):
            ref[x + 2] = filter_ref[(place,) + spot]
    spread = (plane_ref, beside_ref, further_ref)
    spread_group(other_ref, spread)
    for p, (x, spot) in enumerate(group_spots(1, other_ref)):
        for ref, field in zip(results, filter_plane(p, layers, spread, weight_ref)):
            ref[x + 2] = field

    for ref in (first_ref, disp_ref):
        for part in range(3):
            ref[part, rows(0, layers)] = zero
            ref[part, rows(planes + 1, layers)] = zero

    def store_faces(slot, modulus, above, later, before, free, start, views):
        across, up_view, right_view, left_view, rate, source = views
        across[slot] = later
        up = jnp.where(z < layers - 1, 0.5 * (modulus + above), 0.0)
        right = jnp.where(
            y < row_width - 1, 0.5 * (modulus + pltpu.roll(modulus, row_width - 1, 1)), 0.0
        )
        left = pltpu.roll(right, 1, 1)
        up_view[rows(slot, layers)] = up
        right_view[slot] = right
        left_view[slot] = left
        sums = (before + later, up + pltpu.roll(up, 1, 0), left + right)
        every = sums[0] + sums[1] + sums[2]
        diagonal = [every + part_sum for part_sum in sums]
        pair = diagonal[0] * diagonal[1]
        push = relax_factor * free / (pair * diagonal[2])
        side = push * diagonal[2]
        for part, factor in enumerate((side * diagonal[1], side * diagonal[0], push * pair)):
            rate[part, slot] = factor
            source[part, rows(slot, layers)] = start[part] * free

    def modulus_half(first, count, carry):
        near = near_ref.at[pl.ds(first + 2, count)]
        side = side_ref.at[pl.ds(first + 1, count + 2)]
        far = far_ref.at[pl.ds(first, count + 4)]
        moduli = modulus_ref.at[pl.ds(first * layers, (count + 1) * layers)]
        coef = coef_ref.at[pl.ds(first, count)]
        free = free_ref.at[pl.ds(first, count)]
        views = (
            across_ref.at[pl.ds(first, count)],
            up_ref.at[pl.ds(first * layers, count * layers)],
            right_ref.at[pl.ds(first, count)],
            left_ref.at[pl.ds(first, count)],
            rate_ref.at[:, pl.ds(first, count)],
            first_ref.at[:, pl.ds(first * layers, count * layers)],
        )
        modulus, before = carry
        for p in range(count):
            inverse = inverse_ref[edge_class(first + p, planes)]
            filtered = near[p] + side[p] + side[p + 2] + far[p] + far[p + 4]
            filtered = filtered * inverse
            later = floor_modulus + (1.0 - floor_modulus) * (filtered * filtered * filtered)
            coef[p] = 3.0 * (1.0 - floor_modulus) * (filtered * filtered) * inverse
            moduli[rows(p + 1, layers)] = later
            ahead = 0.5 * (modulus + later)
            if p == 0:
                ahead = jnp.where(first > 0, ahead, 0.0)
            above = moduli[rows(p, layers, 1)] if p else pltpu.roll(modulus, layers - 1, 0)
            previous = jnp.maximum(first + p - 1, 0)
            store_faces(
                p,
                modulus,
                above,
                ahead,
                before,
                free_ref[previous],
                [start_ref[part, previous] for part in range(3)],
                views,
            )
            modulus, before = later, ahead
        return modulus, before

    modulus, before = each_half(planes, modulus_half, (jnp.ones(shape, jnp.float32), zero))
    store_faces(
        planes,
        modulus,
        pltpu.roll(modulus, layers - 1, 0),
        zero,
        before,
        free_ref[planes - 1],
        [start_ref[part, planes - 1] for part in range(3)],
        (across_ref, up_ref, right_ref, left_ref, rate_ref, first_ref),
    )

    own_x = jnp.max(spot_ref[...]).astype(jnp.int32)

    def sweep(source, target):
        def sweep_half(first, count, carry):
            old = source.at[:, pl.ds(first * layers, (count + 2) * layers)]
            new = target.at[:, pl.ds((first + 1) * layers, count * layers)]
            across = across_ref.at[pl.ds(first, count + 1)]
            up = up_ref.at[pl.ds(first * layers, (count + 1) * layers)]
            right = right_ref.at[pl.ds(first + 1, count)]
            left = left_ref.at[pl.ds(first + 1, count)]
            rate = rate_ref.at[:, pl.ds(first + 1, count)]
            behind = [old[part, rows(0, layers)] for part in range(3)]
            here = [old[part, rows(1, layers)] for part in range(3)]
            for p in range(count):
                ahead = [old[part, rows(p + 2, layers)] for part in range(3)]
                for part in range(3):
                    pulls = [
                        across[p] * behind[part] + across[p + 1] * ahead[part],
                        up[rows(p + 1, layers)] * old[part, rows(p + 1, layers, 1)]
                        + up[rows(p + 1, layers, -1)] * old[part, rows(p + 1, layers, -1)],
                        right[p] * pltpu.roll(here[part], row_width - 1, 1)
                        + left[p] * pltpu.roll(here[part], 1, 1),
                    ]
                    pull = pulls[0] + pulls[1] + pulls[2] + pulls[part]
                    new[part, rows(p, layers)] = (
                        1.0 - relax_factor
                    ) * here[part] + rate[part, p] * pull
                behind, here = here, ahead
            return carry

        each_half(planes, sweep_half, 0)
        for part in range(3):
            target[part, rows(own_x + 1, layers)] += rate_ref[part, own_x + 1] * load_ref[part]

    def two_sweeps(turn, carry):
        sweep(first_ref, disp_ref)

        @pl.when(turn < SWEEPS // 2)
        def _():
            sweep(disp_ref, first_ref)

        return carry

    lax.fori_loop(0, SWEEPS // 2 + 1, two_sweeps, 0)


def filter_group(group, shares, weight_ref, near_ref, far_ref, result_ref):
    chips, own_planes, layers, row_width = result_ref.shape
    zero_gap = jnp.zeros((GAP, row_width), jnp.float32)
    mine = lax.axis_index("space")
    core = (mine ^ mine >> 1 ^ group) & 1
    count = shares[0].shape[0] - own_planes
    views = [
        [ref.at[pl.ds(own_planes * start, count)] for ref in shares] for start in (core, 1 - core)
    ]
    for ref in (near_ref, far_ref):
        ref[gap(0, layers)] = zero_gap
    for p in range(chips * own_planes):
        chip, own = p // own_planes, p % own_planes
        plane, beside, further = views[chip & 1]
        x = 2 * own_planes * chip + own + 2

        def around(ref, distance):
            return ref[x + distance] + ref[x - distance]

        sums = {
            0: plane[x],
            1: beside[x] + around(plane, 1),
            2: around(beside, 1),
            4: further[x] + around(plane, 2),
            5: around(further, 1) + around(beside, 2),
            8: around(further, 2),
        }
        level = weigh(sums, weight_ref, 0)
        for ref, square in ((near_ref, 1), (far_ref, 4)):
            ref[gapped(p, layers)] = weigh(sums, weight_ref, square)
            ref[gap(p + 1, layers)] = zero_gap
        result_ref[chip, own] = (
            level
            + near_ref[gapped(p, layers, 1)]
            + near_ref[gapped(p, layers, -1)]
            + far_ref[gapped(p, layers, 2)]
            + far_ref[gapped(p, layers, -2)]
        )


def share_kernel(
    disp_ref,
    coef_ref,
    weight_ref,
    sent_ref,
    plane_ref,
    beside_ref,
    further_ref,
    near_ref,
    far_ref,
):
    planes, layers, row_width = coef_ref.shape
    load_cases = lax.axis_size("space")
    shape = (layers, row_width)
    z = spot_iota(shape, 0)
    y = spot_iota(shape, 1)
    zero = jnp.zeros(shape, jnp.float32)
    shares = (plane_ref, beside_ref, further_ref)
    for ref in shares:
        zero_edges(ref)

    before = zero
    here = [disp_ref[part, rows(1, layers)] for part in range(3)]
    for x in range(planes):
        ahead, upward, right = zero, zero, zero
        later = here
        if x + 1 < planes:
            later = [disp_ref[part, rows(x + 2, layers)] for part in range(3)]
        for part in range(3):
            step = later[part] - here[part]
            climb = disp_ref[part, rows(x + 1, layers, 1)] - here[part]
            slide = pltpu.roll(here[part], row_width - 1, 1) - here[part]
            ahead = ahead + (2.0 if part == 0 else 1.0) * (step * step)
            upward = upward + (2.0 if part == 1 else 1.0) * (climb * climb)
            right = right + (2.0 if part == 2 else 1.0) * (slide * slide)
        upward = jnp.where(z < layers - 1, upward, 0.0)
        right = jnp.where(y < row_width - 1, right, 0.0)
        total = before + ahead + upward + pltpu.roll(upward, 1, 0) + right + pltpu.roll(right, 1, 1)
        share = (0.5 / load_cases) * total * coef_ref[x]
        plane_ref[x + 2] = share
        beside_ref[x + 2] = shift_sum(share, 1, 1)
        further_ref[x + 2] = shift_sum(share, 1, 2)
        before, here = ahead, later
    filter_group(1, shares, weight_ref, near_ref, far_ref, sent_ref)


def kept_kernel(
    disp_ref,
    weight_ref,
    plane_ref,
    beside_ref,
    further_ref,
    disp_hbm,
    kept_ref,
    near_ref,
    far_ref,
    stored,
):
    layers = kept_ref.shape[2]
    inner = pl.ds(layers, disp_ref.shape[1] - 2 * layers)
    store = pltpu.make_async_copy(disp_ref.at[:, inner], disp_hbm, stored)
    store.start()
    shares = (plane_ref, beside_ref, further_ref)
    filter_group(0, shares, weight_ref, near_ref, far_ref, kept_ref)
    store.wait()


def design_kernel(root_ref, density_ref, new_ref, pull_ref, low_ref, high_ref):
    groups, chips, own_planes, layers, row_width = density_ref.shape
    own_chip = lax.axis_index("space") >> 1
    shape = (layers, row_width)
    zero = jnp.zeros(shape, jnp.float32)
    planes = [
        (group, chip, own)
        for group in range(groups)
        for chip in range(chips)
        for own in range(own_planes)
    ]
    for spot in planes:
        density = density_ref[spot]
        pull_ref[spot] = density * root_ref[spot]
        low_ref[spot] = jnp.maximum(density - move_limit, density_floor)
        high_ref[spot] = jnp.minimum(density + move_limit, 1.0)

    target = volume_share * len(planes) * layers * row_width

    def factor_of(log_level):
        return jnp.broadcast_to(jnp.exp(-0.5 * log_level), shape)

    def exceeds(total):
        return jnp.sum(jnp.sum(total, axis=0, keepdims=True), axis=1, keepdims=True) > target

    def halve_twice(step, state):
        lower, span = state
        half, quarter = span * 0.5, span * 0.25
        middles = (lower + quarter, lower + half, lower + half + quarter)
        factors = [factor_of(middle) for middle in middles]
        totals = [zero, zero, zero]
        for spot in planes:
            pull, low, high = pull_ref[spot], low_ref[spot], high_ref[spot]
            totals = [
                total + jnp.minimum(jnp.maximum(pull * factor, low), high)
                for total, factor in zip(totals, factors)
            ]
        first, second, third = (exceeds(total) for total in totals)
        upper = jnp.where(third, middles[2], middles[1])
        below = jnp.where(first, middles[0], lower)
        return jnp.where(second, upper, below), quarter

    start = (jnp.full((1, 1), log_lower, jnp.float32), jnp.full((1, 1), log_span, jnp.float32))
    lower, span = lax.fori_loop(0, SEARCH // 2, halve_twice, start)
    factor = factor_of(lower + 0.5 * span)
    for own in range(own_planes):
        spot = (0, own_chip, own)
        new_ref[own] = jnp.minimum(
            jnp.maximum(pull_ref[spot] * factor, low_ref[spot]), high_ref[spot]
        )


def in_vmem():
    return pl.BlockSpec(memory_space=pltpu.VMEM)


KERNEL_VMEM = 24 * 2**20


def floats(*shape):
    return jax.ShapeDtypeStruct(shape, jnp.float32)


def prepare_call(density, radius, load_index, load_force, fixed):
    chips, own_planes, layers, row_width = density.shape
    planes = fixed.shape[0]
    spread = pltpu.VMEM((chips * own_planes * (layers + GAP) + GAP, row_width), jnp.float32)
    return pl.pallas_call(
        prepare_kernel,
        out_shape=[
            floats(len(ALL_SQUARES), layers, row_width),
            floats(2 * window_reach + 1, layers, row_width),
            floats(planes, layers, row_width),
            floats(3, layers, row_width),
            floats(8, row_width),
            floats(3, *density.shape),
        ],
        in_specs=[pl.BlockSpec(memory_space=pltpu.HBM)] * 4 + [in_vmem()],
        out_specs=[in_vmem()] * 6,
        scratch_shapes=[
            pltpu.SMEM(radius.shape, radius.dtype),
            pltpu.SMEM(load_index.shape, load_index.dtype),
            pltpu.SMEM(load_force.shape, load_force.dtype),
            pltpu.VMEM(fixed.shape, fixed.dtype),
            spread,
            spread,
            spread,
            pltpu.SemaphoreType.DMA((4,)),
        ],
        compiler_params=pltpu.CompilerParams(vmem_limit_bytes=KERNEL_VMEM),
        cost_estimate=pl.CostEstimate(
            flops=80 * planes * layers * row_width,
            bytes_accessed=8 * planes * layers * row_width,
            transcendentals=0,
        ),
        name="prepare",
    )(
        *(
            pltpu.with_memory_space_constraint(array, pltpu.HBM)
            for array in (radius, load_index, load_force, fixed)
        ),
        density,
    )


def sweep_call(spot, load, weights, inverses, free, filtered, density, displacement):
    groups, chips, own_planes, layers, row_width = density.shape
    planes = groups * chips * own_planes

    def scratch(*lead):
        return pltpu.VMEM(lead + (row_width,), jnp.float32)

    return pl.pallas_call(
        sweep_kernel,
        out_shape=[
            floats(3, (planes + 2) * layers, row_width),
            floats(planes, layers, row_width),
        ],
        in_specs=[in_vmem()] * 8,
        out_specs=[in_vmem()] * 2,
        scratch_shapes=[
            scratch(planes // 2 * (layers + GAP) + GAP),
            scratch(planes // 2 * (layers + GAP) + GAP),
            scratch(planes // 2 * (layers + GAP) + GAP),
            scratch(planes + 4, layers),
            scratch(planes + 4, layers),
            scratch(planes + 4, layers),
            scratch((planes + 1) * layers),
            scratch(planes + 1, layers),
            scratch((planes + 1) * layers),
            scratch(planes + 1, layers),
            scratch(planes + 1, layers),
            scratch(3, planes + 1, layers),
            scratch(3, (planes + 2) * layers),
        ],
        compiler_params=pltpu.CompilerParams(vmem_limit_bytes=KERNEL_VMEM),
        name="sweeps",
    )(spot, load, weights, inverses, free, filtered, density, displacement)


def share_call(disp, coef, weights, group_shape):
    planes, layers, row_width = coef.shape
    gaps = pltpu.VMEM((planes // 2 * (layers + GAP) + GAP, row_width), jnp.float32)
    return pl.pallas_call(
        share_kernel,
        out_shape=[floats(*group_shape)] + [floats(planes + 4, layers, row_width)] * 3,
        in_specs=[in_vmem()] * 3,
        out_specs=[in_vmem()] * 4,
        scratch_shapes=[gaps, gaps],
        compiler_params=pltpu.CompilerParams(vmem_limit_bytes=KERNEL_VMEM),
        name="share",
    )(disp, coef, weights)


def kept_call(disp, weights, shares, group_shape):
    parts, disp_rows, row_width = disp.shape
    chips, own_planes, layers = group_shape[:3]
    gaps = pltpu.VMEM((chips * own_planes * (layers + GAP) + GAP, row_width), jnp.float32)
    return pl.pallas_call(
        kept_kernel,
        out_shape=[floats(parts, disp_rows - 2 * layers, row_width), floats(*group_shape)],
        in_specs=[in_vmem()] * 5,
        out_specs=[pl.BlockSpec(memory_space=pltpu.HBM), in_vmem()],
        scratch_shapes=[gaps, gaps, pltpu.SemaphoreType.DMA(())],
        compiler_params=pltpu.CompilerParams(vmem_limit_bytes=KERNEL_VMEM),
        cost_estimate=pl.CostEstimate(
            flops=20 * disp.size, bytes_accessed=8 * disp.size, transcendentals=0
        ),
        name="kept",
    )(disp, weights, *shares)


def design_call(root, density):
    return pl.pallas_call(
        design_kernel,
        out_shape=floats(*density.shape[2:]),
        in_specs=[in_vmem()] * 2,
        out_specs=in_vmem(),
        scratch_shapes=[pltpu.VMEM(density.shape, jnp.float32)] * 3,
        compiler_params=pltpu.CompilerParams(vmem_limit_bytes=KERNEL_VMEM),
        name="design",
    )(root, density)


def other_core(block):
    devices = lax.axis_size("space")
    return lax.ppermute(block, "space", [(i, i ^ 1) for i in range(devices)])


def chip_groups():
    chips = lax.axis_size("space") // 2
    return [[2 * chip + (chip ^ group) % 2 for chip in range(chips)] for group in range(2)]


def between_chips(pieces):
    return lax.all_to_all(pieces, "space", 0, 0, axis_index_groups=chip_groups())


def chip_gathered(block):
    chips = lax.axis_size("space") // 2
    return between_chips(jnp.broadcast_to(block[None], (chips,) + block.shape))


def with_other_core(blocks):
    return jnp.stack([blocks, other_core(blocks)])


def scattered_sum(sent, make_kept):
    received = other_core(sent)
    *others, kept = make_kept()
    return jnp.sum(between_chips(kept + received), axis=0), others


def one_slab(density, displacement, fixed, load_index, load_force, radius):
    same_group, small = lax.optimization_barrier(
        (chip_gathered(density), (radius, load_index, load_force.T, fixed))
    )
    other_group = other_core(same_group)
    weights, inverses, free, load, spot, filtered = prepare_call(same_group, *small)
    whole = jnp.stack([same_group, other_group])
    disp, coef = sweep_call(
        spot, load, weights, inverses, free, filtered, whole, displacement[0]
    )
    sent, *shares = share_call(disp, coef, weights, same_group.shape)
    sent, disp, shares = lax.optimization_barrier((sent, disp, shares))
    squares, (new_displacement,) = scattered_sum(
        sent, lambda: kept_call(disp, weights, shares, same_group.shape)
    )
    root = with_other_core(chip_gathered(jnp.sqrt(squares)))
    new_density = design_call(root, whole)
    return new_density, new_displacement.reshape(displacement.shape)


def from_behind(block, axis, distance):
    devices = range(lax.axis_size(axis))
    route = [(i - distance, i) for i in devices if i - distance in devices]
    return lax.ppermute(block, axis, route)


def extended(x, sides, width):
    for axis, dim in sides:
        size, length = (lax.axis_size(axis), x.shape[dim])
        up = [(i, (i + 1) % size) for i in range(size - 1)]
        down = [(j, i) for i, j in up]
        last = lax.slice_in_dim(x, length - width, length, axis=dim)
        first = lax.slice_in_dim(x, 0, width, axis=dim)
        before = lax.ppermute(last, axis, up)
        after = lax.ppermute(first, axis, down)
        x = jnp.concatenate([before, x, after], axis=dim)
    return x


def from_partner(x, axis, bit):
    return lax.ppermute(x, axis, [(i, i ^ 1 << bit) for i in range(lax.axis_size(axis))])


def window_offsets():
    offsets_list = []
    for across in range(-window_reach, window_reach + 1):
        for upward in range(-window_reach, window_reach + 1):
            for sideways in range(-window_reach, window_reach + 1):
                length = math.sqrt(across * across + upward * upward + sideways * sideways)
                offsets_list.append((across, upward, sideways, length))
    return offsets_list


def layer_weights(radius):
    radial = radius.astype(jnp.float32)
    return jnp.stack(
        [jnp.maximum(radial - length, 0.0) for across, upward, sideways, length in window_offsets()]
    )


def pad_axis(grid_field, along_axis, before, after_cells):
    widths = [(0, 0)] * grid_field.ndim
    widths[along_axis] = (before, after_cells)
    return jnp.pad(grid_field, widths)


def pad_sides(grid_field):
    return jnp.pad(grid_field, ((0, 0), (window_reach, window_reach), (window_reach, window_reach)))


def filter_forward(padded, weights):
    out_rows = padded.shape[0] - 2 * window_reach
    layers = padded.shape[1] - 2 * window_reach
    row_width = padded.shape[2] - 2 * window_reach
    result = jnp.zeros((out_rows, layers, row_width), jnp.float32)
    for offset_index, (across, upward, sideways, length) in enumerate(window_offsets()):
        shifted = padded[
            window_reach + across : window_reach + across + out_rows,
            window_reach + upward : window_reach + upward + layers,
            window_reach + sideways : window_reach + sideways + row_width,
        ]
        result = result + weights[offset_index][None, :, None] * shifted
    return result


def filter_backward(padded, padded_weights):
    out_rows = padded.shape[0] - 2 * window_reach
    layers = padded.shape[1] - 2 * window_reach
    row_width = padded.shape[2] - 2 * window_reach
    result = jnp.zeros((out_rows, layers, row_width), jnp.float32)
    for offset_index, (across, upward, sideways, length) in enumerate(window_offsets()):
        shifted = padded[
            window_reach - across : window_reach - across + out_rows,
            window_reach - upward : window_reach - upward + layers,
            window_reach - sideways : window_reach - sideways + row_width,
        ]
        layer_part = padded_weights[
            offset_index, window_reach - upward : window_reach - upward + layers
        ]
        result = result + layer_part[None, :, None] * shifted
    return result


def stiff_factors(direction):
    return jnp.array(
        [2.0 if component == direction else 1.0 for component in range(3)], jnp.float32
    ).reshape(3, 1, 1, 1)


def relax_slab(padded, displace, face_x, face_z, face_y, force_field, free_cells, diagonal):
    flux_x = stiff_factors(0) * face_x * jnp.diff(padded, axis=1)
    stencil_image = flux_x[:, :-1] - flux_x[:, 1:]
    flux_z = stiff_factors(1) * face_z * jnp.diff(displace, axis=2)
    stencil_image = stencil_image + pad_axis(flux_z, 2, 1, 0) - pad_axis(flux_z, 2, 0, 1)
    flux_y = stiff_factors(2) * face_y * jnp.diff(displace, axis=3)
    stencil_image = stencil_image + pad_axis(flux_y, 3, 1, 0) - pad_axis(flux_y, 3, 0, 1)
    return free_cells * (displace + relax_factor * (force_field - stencil_image) / diagonal)


def slab_energy(grid_field, along_axis, direction, load_cases):
    change = jnp.diff(grid_field, axis=along_axis)
    return jnp.sum(stiff_factors(direction) * change * change, axis=0) / load_cases


def neighbour_planes(displace, load_cases, axis_devices):
    if axis_devices > load_cases:
        below = from_behind(displace[:, -1:], "space", load_cases)
        above = from_behind(displace[:, :1], "space", -load_cases)
    else:
        below = jnp.zeros_like(displace[:, :1])
        above = jnp.zeros_like(displace[:, :1])
    return jnp.concatenate([below, displace, above], axis=1)


def many_slabs(density, displacement, fixed, load_index, load_force, radius):
    slab_rows, layers, row_width = density.shape
    load_cases = load_index.shape[0]
    level_count = load_cases.bit_length() - 1
    axis_devices = lax.axis_size("space")
    axis_place = lax.axis_index("space")
    slab_planes = slab_rows * load_cases
    slab_place = axis_place // load_cases
    load_place = axis_place % load_cases
    total_rows = slab_rows * axis_devices
    weights = layer_weights(radius)
    padded_weights = pad_axis(weights, 1, window_reach, window_reach)
    global_rows = (
        jnp.arange(slab_rows + 2 * window_reach, dtype=jnp.int32)
        + axis_place * slab_rows
        - window_reach
    )
    deep_inside = ((global_rows >= 0) & (global_rows < total_rows)).astype(jnp.float32)
    inside_field = deep_inside[:, None, None] * pad_sides(
        jnp.ones((slab_rows + 2 * window_reach, layers, row_width), jnp.float32)
    )
    total_weight = filter_forward(inside_field, weights)
    slab_start = slab_place * slab_planes
    margin_rows = jnp.arange(slab_planes + 2, dtype=jnp.int32) + slab_start - 1
    margin_inside = ((margin_rows >= 0) & (margin_rows < total_rows)).astype(jnp.float32)
    face_valid = margin_inside[1:] * margin_inside[:-1]
    fixed_slab = lax.dynamic_slice_in_dim(fixed, slab_start, slab_planes, 0).astype(jnp.float32)
    bottom_layer = (jnp.arange(layers, dtype=jnp.int32) == 0).astype(jnp.float32)
    free_cells = 1.0 - bottom_layer[None, :, None] * fixed_slab[:, None, :]
    slab_cells = slab_planes * layers * row_width
    cell_index = jnp.arange(slab_cells, dtype=jnp.int32) + slab_place * slab_cells
    load_hot = jnp.arange(load_cases, dtype=jnp.int32) == load_place
    own_index = jnp.sum(jnp.where(load_hot, load_index, 0))
    own_force = jnp.sum(load_hot.astype(jnp.float32)[:, None] * load_force, axis=0)
    load_hits = (cell_index == own_index).astype(jnp.float32)
    force_field = (own_force[:, None] * load_hits[None, :]).reshape(
        3, slab_planes, layers, row_width
    )
    displace = displacement[0] * free_cells
    target = volume_share * total_rows * layers * row_width
    padded = neighbour_planes(displace, load_cases, axis_devices)
    halo_density = extended(density, (("space", 0),), window_reach)
    filtered = filter_forward(pad_sides(halo_density), weights) / total_weight
    whole_field = lax.all_gather(filtered, "space", axis=0, tiled=True)
    margin = lax.dynamic_slice_in_dim(
        pad_axis(whole_field, 0, 1, 1), slab_start, slab_planes + 2, 0
    )
    moduli = floor_modulus + (1.0 - floor_modulus) * margin**3
    face_x = 0.5 * (moduli[1:] + moduli[:-1]) * face_valid[:, None, None]
    inner_moduli = moduli[1:-1]
    face_z = 0.5 * (inner_moduli[:, 1:] + inner_moduli[:, :-1])
    face_y = 0.5 * (inner_moduli[:, :, 1:] + inner_moduli[:, :, :-1])
    sum_x = face_x[:-1] + face_x[1:]
    sum_z = pad_axis(face_z, 1, 1, 0) + pad_axis(face_z, 1, 0, 1)
    sum_y = pad_axis(face_y, 2, 1, 0) + pad_axis(face_y, 2, 0, 1)
    diagonal = stiff_factors(0) * sum_x + stiff_factors(1) * sum_z + stiff_factors(2) * sum_y
    for sweep_index in range(SWEEPS):
        displace = relax_slab(
            padded, displace, face_x, face_z, face_y, force_field, free_cells, diagonal
        )
        padded = neighbour_planes(displace, load_cases, axis_devices)
    energy_x = slab_energy(padded, 1, 0, load_cases) * face_valid[:, None, None]
    energy_z = slab_energy(displace, 2, 1, load_cases)
    energy_y = slab_energy(displace, 3, 2, load_cases)
    sens_term = 0.5 * (
        energy_x[:-1]
        + energy_x[1:]
        + pad_axis(energy_z, 1, 1, 0)
        + pad_axis(energy_z, 1, 0, 1)
        + pad_axis(energy_y, 2, 1, 0)
        + pad_axis(energy_y, 2, 0, 1)
    )
    sensitive = sens_term
    for level in reversed(range(level_count)):
        half_rows = sensitive.shape[0] // 2
        upper_side = load_place // 2**level % 2 == 1
        outgoing = jnp.where(upper_side, sensitive[:half_rows], sensitive[half_rows:])
        keeping = jnp.where(upper_side, sensitive[half_rows:], sensitive[:half_rows])
        sensitive = keeping + from_partner(outgoing, "space", level)
    weighted_share = 3.0 * (1.0 - floor_modulus) * filtered**2 * sensitive / total_weight
    halo_share = extended(weighted_share, (("space", 0),), window_reach)
    root_term = jnp.sqrt(filter_backward(pad_sides(halo_share), padded_weights))
    lowest = jnp.maximum(density - move_limit, density_floor)
    highest = jnp.minimum(density + move_limit, 1.0)
    design_now = density

    def trial_design(log_level):
        return jnp.clip(design_now * root_term * jnp.exp(-0.5 * log_level), lowest, highest)

    start_state = (jnp.asarray(log_lower, jnp.float32), jnp.asarray(log_span, jnp.float32))

    def halve(search_step, search_state):
        lower_end, span_width = search_state
        half_span = span_width * 0.5
        middle = lower_end + half_span
        volume_total = lax.psum(jnp.sum(trial_design(middle)), "space")
        return (jnp.where(volume_total > target, middle, lower_end), half_span)

    lower_end, span_width = lax.fori_loop(0, SEARCH, halve, start_state)
    density = trial_design(lower_end + 0.5 * span_width)
    new_displacement = displace[None]
    return (density, new_displacement)


def solution(mesh):
    in_specs = (
        P("space", "parts", None),
        P("space", None, None, "parts", None),
        P(None, "parts"),
        P("parts"),
        P("parts", None),
        P("parts"),
    )
    out_specs = (P("space", "parts", None), P("space", None, None, "parts", None))

    def local(density, displacement, fixed, load_index, load_force, radius):
        alone = lax.axis_size("space") == load_index.shape[0]
        run = one_slab if alone else many_slabs
        return run(density, displacement, fixed, load_index, load_force, radius)

    return jax.shard_map(local, mesh=mesh, in_specs=in_specs, out_specs=out_specs, check_vma=False)
```

```python
import math

import jax
import jax.numpy as jnp
from jax import lax
from jax.experimental import pallas as pl
from jax.experimental.pallas import tpu as pltpu
from jax.sharding import PartitionSpec as P

SWEEPS = 3
SEARCH = 12


floor_modulus = 0.05
relax_factor = 0.6
move_limit = 0.2
density_floor = 0.01
volume_share = 0.5
log_lower = -16.0
log_span = 32.0
window_reach = 2

PLANE_SQUARES = (0, 1, 2, 4, 5, 8)
ALL_SQUARES = (0, 1, 2, 3, 4, 5, 6, 8, 9, 12)


def spot_iota(shape, dim):
    return lax.broadcasted_iota(jnp.int32, shape, dim)


def each_plane(planes, body, carry):
    for x in range(planes):
        carry = body(x, carry)
    return carry


def each_chunk(planes, count, body, carry):
    return lax.fori_loop(0, planes // count, lambda i, carry: body(i * count, carry), carry)


def layer_radius(radius_ref, layers, row_width):
    z = spot_iota((layers, row_width), 0)
    result = jnp.zeros((layers, row_width), jnp.int32)
    for layer in range(layers):
        result = jnp.where(z == layer, radius_ref[layer], result)
    return result.astype(jnp.float32)


def class_weights(radius_ref, weight_ref):
    layers, row_width = weight_ref.shape[1:]
    radial = layer_radius(radius_ref, layers, row_width)
    for place, square in enumerate(ALL_SQUARES):
        weight_ref[place] = jnp.maximum(radial - math.sqrt(square), 0.0)


def shift_sum(field, dim, distance):
    size = field.shape[dim]
    spot = spot_iota(field.shape, dim)
    ahead = jnp.where(spot < size - distance, pltpu.roll(field, size - distance, dim), 0.0)
    behind = jnp.where(spot >= distance, pltpu.roll(field, distance, dim), 0.0)
    return ahead + behind


def plane_sums(plane):
    beside = shift_sum(plane, 1, 1)
    further = shift_sum(plane, 1, 2)
    return {
        0: plane,
        1: beside + shift_sum(plane, 0, 1),
        2: shift_sum(beside, 0, 1),
        4: further + shift_sum(plane, 0, 2),
        5: shift_sum(further, 0, 1) + shift_sum(beside, 0, 2),
        8: shift_sum(further, 0, 2),
    }


def weigh(sums, weight_ref, square):
    result = None
    for inner in PLANE_SQUARES:
        term = weight_ref[ALL_SQUARES.index(inner + square)] * sums[inner]
        result = term if result is None else result + term
    return result


def forward_planes(plane, weight_ref):
    sums = plane_sums(plane)
    return [weigh(sums, weight_ref, square) for square in (0, 1, 4)]


def rows(x, layers, shift=0):
    return pl.ds(x * layers + shift, layers)


GAP = 8


def gapped(x, layers, shift=0):
    return pl.ds(GAP + x * (layers + GAP) + shift, layers)


def gap(x, layers):
    return pl.ds(x * (layers + GAP), GAP)


def edge_class(x, planes):
    return jnp.minimum(x, 2) + jnp.maximum(x - (planes - 3), 0)


def zero_edges(ref):
    planes = ref.shape[0]
    for place in (0, 1, planes - 2, planes - 1):
        ref[place] = jnp.zeros(ref.shape[1:], ref.dtype)


def group_spots(group, blocks):
    chips, own_planes = blocks.shape[:2]
    mine = lax.axis_index("space")
    core = mine ^ mine >> 1 ^ group
    return [
        (own_planes * (2 * chip + ((core ^ chip) & 1)) + own, (chip, own))
        for chip in range(chips)
        for own in range(own_planes)
    ]


def spread_group(blocks, spread):
    chips, own_planes, layers, row_width = blocks.shape
    zero_gap = jnp.zeros((GAP, row_width), jnp.float32)
    for ref in spread:
        ref[gap(0, layers)] = zero_gap
    for p in range(chips * own_planes):
        plane = blocks[p // own_planes, p % own_planes]
        for ref, field in zip(spread, (plane, shift_sum(plane, 1, 1), shift_sum(plane, 1, 2))):
            ref[gapped(p, layers)] = field
            ref[gap(p + 1, layers)] = zero_gap


def filter_plane(p, layers, spread, weight_ref):
    def around(place, distance):
        ref = spread[place]
        return ref[gapped(p, layers, distance)] + ref[gapped(p, layers, -distance)]

    sums = {
        0: spread[0][gapped(p, layers)],
        1: spread[1][gapped(p, layers)] + around(0, 1),
        2: around(1, 1),
        4: spread[2][gapped(p, layers)] + around(0, 2),
        5: around(2, 1) + around(1, 2),
        8: around(2, 2),
    }
    return [weigh(sums, weight_ref, square) for square in (0, 1, 4)]


def prepare_kernel(
    radius_hbm,
    index_hbm,
    force_hbm,
    fixed_hbm,
    density_ref,
    weight_ref,
    inverse_ref,
    free_ref,
    load_ref,
    spot_ref,
    filter_ref,
    radius_ref,
    index_ref,
    force_ref,
    fixed_ref,
    plane_ref,
    beside_ref,
    further_ref,
    arrived,
):
    copies = [
        pltpu.make_async_copy(source, target, arrived.at[place])
        for place, (source, target) in enumerate(
            (
                (radius_hbm, radius_ref),
                (index_hbm, index_ref),
                (force_hbm, force_ref),
                (fixed_hbm, fixed_ref),
            )
        )
    ]
    for copy in copies:
        copy.start()
    spread = (plane_ref, beside_ref, further_ref)
    spread_group(density_ref, spread)
    for copy in copies:
        copy.wait()
    planes, layers, row_width = free_ref.shape
    load_place = lax.axis_index("space")
    shape = (layers, row_width)
    z = spot_iota(shape, 0)
    y = spot_iota(shape, 1)

    class_weights(radius_ref, weight_ref)
    own_planes = density_ref.shape[1]
    for p in range(density_ref.shape[0] * own_planes):
        for place, field in enumerate(filter_plane(p, layers, spread, weight_ref)):
            filter_ref[place, p // own_planes, p % own_planes] = field

    ones = forward_planes(jnp.ones(shape, jnp.float32), weight_ref)
    for place, (lower, upper) in enumerate(((0, 2), (1, 2), (2, 2), (2, 1), (2, 0))):
        inverse_ref[place] = 1.0 / (
            ones[0] + min(lower, 1) * ones[1] + min(upper, 1) * ones[1]
            + (lower // 2) * ones[2] + (upper // 2) * ones[2]
        )

    def free_plane(x, carry):
        free_ref[x] = jnp.where(
            z == 0, 1.0 - fixed_ref[pl.ds(x, 1), :].astype(jnp.float32), 1.0
        )
        return carry

    each_plane(planes, free_plane, 0)

    own_index = index_ref[load_place]
    own_z = own_index // row_width % layers
    own_y = own_index % row_width
    hit = (z == own_z) & (y == own_y)
    for part in range(3):
        load_ref[part] = jnp.where(hit, force_ref[part, load_place], 0.0)
    own_x = (own_index // (layers * row_width)).astype(jnp.float32)
    spot_ref[...] = jnp.full(spot_ref.shape, own_x)


def sweep_kernel(
    spot_ref,
    load_ref,
    weight_ref,
    inverse_ref,
    free_ref,
    filter_ref,
    density_ref,
    start_ref,
    disp_ref,
    coef_ref,
    plane_ref,
    beside_ref,
    further_ref,
    near_ref,
    side_ref,
    far_ref,
    modulus_ref,
    across_ref,
    up_ref,
    right_ref,
    left_ref,
    rate_ref,
    first_ref,
):
    planes, layers, row_width = coef_ref.shape
    shape = (layers, row_width)
    z = spot_iota(shape, 0)
    y = spot_iota(shape, 1)
    zero = jnp.zeros(shape, jnp.float32)

    for ref in (side_ref, far_ref):
        zero_edges(ref)
    results = (near_ref, side_ref, far_ref)
    other_ref = density_ref.at[1]
    for x, spot in group_spots(0, other_ref):
        for place, ref in enumerate(results):
            ref[x + 2] = filter_ref[(place,) + spot]
    spread = (plane_ref, beside_ref, further_ref)
    spread_group(other_ref, spread)
    for p, (x, spot) in enumerate(group_spots(1, other_ref)):
        for ref, field in zip(results, filter_plane(p, layers, spread, weight_ref)):
            ref[x + 2] = field

    for ref in (first_ref, disp_ref):
        for part in range(3):
            ref[part, rows(0, layers)] = zero
            ref[part, rows(planes + 1, layers)] = zero

    def store_faces(slot, modulus, above, later, before, free, start, views):
        across, up_view, right_view, left_view, rate, source = views
        across[slot] = later
        up = jnp.where(z < layers - 1, 0.5 * (modulus + above), 0.0)
        right = jnp.where(
            y < row_width - 1, 0.5 * (modulus + pltpu.roll(modulus, row_width - 1, 1)), 0.0
        )
        left = pltpu.roll(right, 1, 1)
        up_view[rows(slot, layers)] = up
        right_view[slot] = right
        left_view[slot] = left
        sums = (before + later, up + pltpu.roll(up, 1, 0), left + right)
        every = sums[0] + sums[1] + sums[2]
        diagonal = [every + part_sum for part_sum in sums]
        pair = diagonal[0] * diagonal[1]
        push = relax_factor * free / (pair * diagonal[2])
        side = push * diagonal[2]
        for part, factor in enumerate((side * diagonal[1], side * diagonal[0], push * pair)):
            rate[part, slot] = factor
            source[part, rows(slot, layers)] = start[part] * free

    half = planes // 2

    def modulus_half(first, carry):
        count = half
        near = near_ref.at[pl.ds(first + 2, count)]
        side = side_ref.at[pl.ds(first + 1, count + 2)]
        far = far_ref.at[pl.ds(first, count + 4)]
        moduli = modulus_ref.at[pl.ds(first * layers, (count + 1) * layers)]
        coef = coef_ref.at[pl.ds(first, count)]
        free = free_ref.at[pl.ds(first, count)]
        views = (
            across_ref.at[pl.ds(first, count)],
            up_ref.at[pl.ds(first * layers, count * layers)],
            right_ref.at[pl.ds(first, count)],
            left_ref.at[pl.ds(first, count)],
            rate_ref.at[:, pl.ds(first, count)],
            first_ref.at[:, pl.ds(first * layers, count * layers)],
        )
        modulus, before = carry
        for p in range(count):
            inverse = inverse_ref[edge_class(first + p, planes)]
            filtered = near[p] + side[p] + side[p + 2] + far[p] + far[p + 4]
            filtered = filtered * inverse
            later = floor_modulus + (1.0 - floor_modulus) * (filtered * filtered * filtered)
            coef[p] = 3.0 * (1.0 - floor_modulus) * (filtered * filtered) * inverse
            moduli[rows(p + 1, layers)] = later
            ahead = 0.5 * (modulus + later)
            if p == 0:
                ahead = jnp.where(first > 0, ahead, 0.0)
            above = moduli[rows(p, layers, 1)] if p else pltpu.roll(modulus, layers - 1, 0)
            previous = jnp.maximum(first + p - 1, 0)
            store_faces(
                p,
                modulus,
                above,
                ahead,
                before,
                free_ref[previous],
                [start_ref[part, previous] for part in range(3)],
                views,
            )
            modulus, before = later, ahead
        return modulus, before

    modulus, before = each_chunk(planes, half, modulus_half, (jnp.ones(shape, jnp.float32), zero))
    store_faces(
        planes,
        modulus,
        pltpu.roll(modulus, layers - 1, 0),
        zero,
        before,
        free_ref[planes - 1],
        [start_ref[part, planes - 1] for part in range(3)],
        (across_ref, up_ref, right_ref, left_ref, rate_ref, first_ref),
    )

    own_x = jnp.max(spot_ref[...]).astype(jnp.int32)

    def sweep(source, target):
        def sweep_half(first, carry):
            count = half
            old = source.at[:, pl.ds(first * layers, (count + 2) * layers)]
            new = target.at[:, pl.ds((first + 1) * layers, count * layers)]
            across = across_ref.at[pl.ds(first, count + 1)]
            up = up_ref.at[pl.ds(first * layers, (count + 1) * layers)]
            right = right_ref.at[pl.ds(first + 1, count)]
            left = left_ref.at[pl.ds(first + 1, count)]
            rate = rate_ref.at[:, pl.ds(first + 1, count)]
            behind = [old[part, rows(0, layers)] for part in range(3)]
            here = [old[part, rows(1, layers)] for part in range(3)]
            for p in range(count):
                ahead = [old[part, rows(p + 2, layers)] for part in range(3)]
                for part in range(3):
                    pulls = [
                        across[p] * behind[part] + across[p + 1] * ahead[part],
                        up[rows(p + 1, layers)] * old[part, rows(p + 1, layers, 1)]
                        + up[rows(p + 1, layers, -1)] * old[part, rows(p + 1, layers, -1)],
                        right[p] * pltpu.roll(here[part], row_width - 1, 1)
                        + left[p] * pltpu.roll(here[part], 1, 1),
                    ]
                    pull = pulls[0] + pulls[1] + pulls[2] + pulls[part]
                    new[part, rows(p, layers)] = (
                        1.0 - relax_factor
                    ) * here[part] + rate[part, p] * pull
                behind, here = here, ahead
            return carry

        each_chunk(planes, half, sweep_half, 0)
        for part in range(3):
            target[part, rows(own_x + 1, layers)] += rate_ref[part, own_x + 1] * load_ref[part]

    def two_sweeps(turn, carry):
        sweep(first_ref, disp_ref)

        @pl.when(turn < SWEEPS // 2)
        def _():
            sweep(disp_ref, first_ref)

        return carry

    lax.fori_loop(0, SWEEPS // 2 + 1, two_sweeps, 0)


def filter_group(group, shares, weight_ref, near_ref, far_ref, result_ref):
    chips, own_planes, layers, row_width = result_ref.shape
    zero_gap = jnp.zeros((GAP, row_width), jnp.float32)
    mine = lax.axis_index("space")
    core = (mine ^ mine >> 1 ^ group) & 1
    count = shares[0].shape[0] - own_planes
    views = [
        [ref.at[pl.ds(own_planes * start, count)] for ref in shares] for start in (core, 1 - core)
    ]
    for ref in (near_ref, far_ref):
        ref[gap(0, layers)] = zero_gap
    for p in range(chips * own_planes):
        chip, own = p // own_planes, p % own_planes
        plane, beside, further = views[chip & 1]
        x = 2 * own_planes * chip + own + 2

        def around(ref, distance):
            return ref[x + distance] + ref[x - distance]

        sums = {
            0: plane[x],
            1: beside[x] + around(plane, 1),
            2: around(beside, 1),
            4: further[x] + around(plane, 2),
            5: around(further, 1) + around(beside, 2),
            8: around(further, 2),
        }
        level = weigh(sums, weight_ref, 0)
        for ref, square in ((near_ref, 1), (far_ref, 4)):
            ref[gapped(p, layers)] = weigh(sums, weight_ref, square)
            ref[gap(p + 1, layers)] = zero_gap
        result_ref[chip, own] = (
            level
            + near_ref[gapped(p, layers, 1)]
            + near_ref[gapped(p, layers, -1)]
            + far_ref[gapped(p, layers, 2)]
            + far_ref[gapped(p, layers, -2)]
        )


def share_kernel(
    disp_ref,
    coef_ref,
    weight_ref,
    sent_ref,
    plane_ref,
    beside_ref,
    further_ref,
    near_ref,
    far_ref,
):
    planes, layers, row_width = coef_ref.shape
    load_cases = lax.axis_size("space")
    shape = (layers, row_width)
    z = spot_iota(shape, 0)
    y = spot_iota(shape, 1)
    zero = jnp.zeros(shape, jnp.float32)
    shares = (plane_ref, beside_ref, further_ref)
    for ref in shares:
        zero_edges(ref)

    count = planes // 4

    def share_chunk(first, before):
        disp = disp_ref.at[:, pl.ds((first + 1) * layers, (count + 1) * layers)]
        coef = coef_ref.at[pl.ds(first, count)]
        plane, beside, further = (ref.at[pl.ds(first + 2, count)] for ref in shares)
        here = [disp[part, rows(0, layers)] for part in range(3)]
        for p in range(count):
            later = [disp[part, rows(p + 1, layers)] for part in range(3)]
            ahead, upward, right = zero, zero, zero
            for part in range(3):
                step = later[part] - here[part]
                climb = disp[part, rows(p, layers, 1)] - here[part]
                slide = pltpu.roll(here[part], row_width - 1, 1) - here[part]
                ahead = ahead + (2.0 if part == 0 else 1.0) * (step * step)
                upward = upward + (2.0 if part == 1 else 1.0) * (climb * climb)
                right = right + (2.0 if part == 2 else 1.0) * (slide * slide)
            if p == count - 1:
                ahead = jnp.where(first + count < planes, ahead, 0.0)
            upward = jnp.where(z < layers - 1, upward, 0.0)
            right = jnp.where(y < row_width - 1, right, 0.0)
            total = before + ahead + upward + pltpu.roll(upward, 1, 0)
            total = total + right + pltpu.roll(right, 1, 1)
            share = (0.5 / load_cases) * total * coef[p]
            plane[p] = share
            beside[p] = shift_sum(share, 1, 1)
            further[p] = shift_sum(share, 1, 2)
            before, here = ahead, later
        return before

    each_chunk(planes, count, share_chunk, zero)
    filter_group(1, shares, weight_ref, near_ref, far_ref, sent_ref)


def kept_kernel(
    disp_ref,
    weight_ref,
    plane_ref,
    beside_ref,
    further_ref,
    disp_hbm,
    kept_ref,
    near_ref,
    far_ref,
    stored,
):
    layers = kept_ref.shape[2]
    inner = pl.ds(layers, disp_ref.shape[1] - 2 * layers)
    store = pltpu.make_async_copy(disp_ref.at[:, inner], disp_hbm, stored)
    store.start()
    shares = (plane_ref, beside_ref, further_ref)
    filter_group(0, shares, weight_ref, near_ref, far_ref, kept_ref)
    store.wait()


def design_kernel(root_ref, density_ref, new_ref, pull_ref, low_ref, high_ref):
    groups, chips, own_planes, layers, row_width = density_ref.shape
    own_chip = lax.axis_index("space") >> 1
    shape = (layers, row_width)
    zero = jnp.zeros(shape, jnp.float32)
    planes = [
        (group, chip, own)
        for group in range(groups)
        for chip in range(chips)
        for own in range(own_planes)
    ]
    for spot in planes:
        density = density_ref[spot]
        pull_ref[spot] = density * root_ref[spot]
        low_ref[spot] = jnp.maximum(density - move_limit, density_floor)
        high_ref[spot] = jnp.minimum(density + move_limit, 1.0)

    target = volume_share * len(planes) * layers * row_width

    def factor_of(log_level):
        return jnp.broadcast_to(jnp.exp(-0.5 * log_level), shape)

    def exceeds(total):
        return jnp.sum(jnp.sum(total, axis=0, keepdims=True), axis=1, keepdims=True) > target

    def halve_twice(step, state):
        lower, span = state
        half, quarter = span * 0.5, span * 0.25
        middles = (lower + quarter, lower + half, lower + half + quarter)
        factors = [factor_of(middle) for middle in middles]
        totals = [zero, zero, zero]
        for spot in planes:
            pull, low, high = pull_ref[spot], low_ref[spot], high_ref[spot]
            totals = [
                total + jnp.minimum(jnp.maximum(pull * factor, low), high)
                for total, factor in zip(totals, factors)
            ]
        first, second, third = (exceeds(total) for total in totals)
        upper = jnp.where(third, middles[2], middles[1])
        below = jnp.where(first, middles[0], lower)
        return jnp.where(second, upper, below), quarter

    start = (jnp.full((1, 1), log_lower, jnp.float32), jnp.full((1, 1), log_span, jnp.float32))
    lower, span = lax.fori_loop(0, SEARCH // 2, halve_twice, start)
    factor = factor_of(lower + 0.5 * span)
    for own in range(own_planes):
        spot = (0, own_chip, own)
        new_ref[own] = jnp.minimum(
            jnp.maximum(pull_ref[spot] * factor, low_ref[spot]), high_ref[spot]
        )


def in_vmem():
    return pl.BlockSpec(memory_space=pltpu.VMEM)


KERNEL_VMEM = 24 * 2**20


def floats(*shape):
    return jax.ShapeDtypeStruct(shape, jnp.float32)


def prepare_call(density, radius, load_index, load_force, fixed):
    chips, own_planes, layers, row_width = density.shape
    planes = fixed.shape[0]
    spread = pltpu.VMEM((chips * own_planes * (layers + GAP) + GAP, row_width), jnp.float32)
    return pl.pallas_call(
        prepare_kernel,
        out_shape=[
            floats(len(ALL_SQUARES), layers, row_width),
            floats(2 * window_reach + 1, layers, row_width),
            floats(planes, layers, row_width),
            floats(3, layers, row_width),
            floats(8, row_width),
            floats(3, *density.shape),
        ],
        in_specs=[pl.BlockSpec(memory_space=pltpu.HBM)] * 4 + [in_vmem()],
        out_specs=[in_vmem()] * 6,
        scratch_shapes=[
            pltpu.SMEM(radius.shape, radius.dtype),
            pltpu.SMEM(load_index.shape, load_index.dtype),
            pltpu.SMEM(load_force.shape, load_force.dtype),
            pltpu.VMEM(fixed.shape, fixed.dtype),
            spread,
            spread,
            spread,
            pltpu.SemaphoreType.DMA((4,)),
        ],
        compiler_params=pltpu.CompilerParams(vmem_limit_bytes=KERNEL_VMEM),
        cost_estimate=pl.CostEstimate(
            flops=80 * planes * layers * row_width,
            bytes_accessed=8 * planes * layers * row_width,
            transcendentals=0,
        ),
        name="prepare",
    )(
        *(
            pltpu.with_memory_space_constraint(array, pltpu.HBM)
            for array in (radius, load_index, load_force, fixed)
        ),
        density,
    )


def sweep_call(spot, load, weights, inverses, free, filtered, density, displacement):
    groups, chips, own_planes, layers, row_width = density.shape
    planes = groups * chips * own_planes

    def scratch(*lead):
        return pltpu.VMEM(lead + (row_width,), jnp.float32)

    return pl.pallas_call(
        sweep_kernel,
        out_shape=[
            floats(3, (planes + 2) * layers, row_width),
            floats(planes, layers, row_width),
        ],
        in_specs=[in_vmem()] * 8,
        out_specs=[in_vmem()] * 2,
        scratch_shapes=[
            scratch(planes // 2 * (layers + GAP) + GAP),
            scratch(planes // 2 * (layers + GAP) + GAP),
            scratch(planes // 2 * (layers + GAP) + GAP),
            scratch(planes + 4, layers),
            scratch(planes + 4, layers),
            scratch(planes + 4, layers),
            scratch((planes + 1) * layers),
            scratch(planes + 1, layers),
            scratch((planes + 1) * layers),
            scratch(planes + 1, layers),
            scratch(planes + 1, layers),
            scratch(3, planes + 1, layers),
            scratch(3, (planes + 2) * layers),
        ],
        compiler_params=pltpu.CompilerParams(vmem_limit_bytes=KERNEL_VMEM),
        name="sweeps",
    )(spot, load, weights, inverses, free, filtered, density, displacement)


def share_call(disp, coef, weights, group_shape):
    planes, layers, row_width = coef.shape
    gaps = pltpu.VMEM((planes // 2 * (layers + GAP) + GAP, row_width), jnp.float32)
    return pl.pallas_call(
        share_kernel,
        out_shape=[floats(*group_shape)] + [floats(planes + 4, layers, row_width)] * 3,
        in_specs=[in_vmem()] * 3,
        out_specs=[in_vmem()] * 4,
        scratch_shapes=[gaps, gaps],
        compiler_params=pltpu.CompilerParams(vmem_limit_bytes=KERNEL_VMEM),
        name="share",
    )(disp, coef, weights)


def kept_call(disp, weights, shares, group_shape):
    parts, disp_rows, row_width = disp.shape
    chips, own_planes, layers = group_shape[:3]
    gaps = pltpu.VMEM((chips * own_planes * (layers + GAP) + GAP, row_width), jnp.float32)
    return pl.pallas_call(
        kept_kernel,
        out_shape=[floats(parts, disp_rows - 2 * layers, row_width), floats(*group_shape)],
        in_specs=[in_vmem()] * 5,
        out_specs=[pl.BlockSpec(memory_space=pltpu.HBM), in_vmem()],
        scratch_shapes=[gaps, gaps, pltpu.SemaphoreType.DMA(())],
        compiler_params=pltpu.CompilerParams(vmem_limit_bytes=KERNEL_VMEM),
        cost_estimate=pl.CostEstimate(
            flops=20 * disp.size, bytes_accessed=8 * disp.size, transcendentals=0
        ),
        name="kept",
    )(disp, weights, *shares)


def design_call(root, density):
    return pl.pallas_call(
        design_kernel,
        out_shape=floats(*density.shape[2:]),
        in_specs=[in_vmem()] * 2,
        out_specs=in_vmem(),
        scratch_shapes=[pltpu.VMEM(density.shape, jnp.float32)] * 3,
        compiler_params=pltpu.CompilerParams(vmem_limit_bytes=KERNEL_VMEM),
        name="design",
    )(root, density)


def other_core(block):
    devices = lax.axis_size("space")
    return lax.ppermute(block, "space", [(i, i ^ 1) for i in range(devices)])


def chip_groups():
    chips = lax.axis_size("space") // 2
    return [[2 * chip + (chip ^ group) % 2 for chip in range(chips)] for group in range(2)]


def between_chips(pieces):
    return lax.all_to_all(pieces, "space", 0, 0, axis_index_groups=chip_groups())


def chip_gathered(block):
    chips = lax.axis_size("space") // 2
    return between_chips(jnp.broadcast_to(block[None], (chips,) + block.shape))


def with_other_core(blocks):
    return jnp.stack([blocks, other_core(blocks)])


def scattered_sum(sent, make_kept):
    received = other_core(sent)
    *others, kept = make_kept()
    return jnp.sum(between_chips(kept + received), axis=0), others


def one_slab(density, displacement, fixed, load_index, load_force, radius):
    same_group, small = lax.optimization_barrier(
        (chip_gathered(density), (radius, load_index, load_force.T, fixed))
    )
    other_group = other_core(same_group)
    weights, inverses, free, load, spot, filtered = prepare_call(same_group, *small)
    whole = jnp.stack([same_group, other_group])
    disp, coef = sweep_call(
        spot, load, weights, inverses, free, filtered, whole, displacement[0]
    )
    sent, *shares = share_call(disp, coef, weights, same_group.shape)
    sent, disp, shares = lax.optimization_barrier((sent, disp, shares))
    squares, (new_displacement,) = scattered_sum(
        sent, lambda: kept_call(disp, weights, shares, same_group.shape)
    )
    root = with_other_core(chip_gathered(jnp.sqrt(squares)))
    new_density = design_call(root, whole)
    return new_density, new_displacement.reshape(displacement.shape)


def from_behind(block, axis, distance):
    devices = range(lax.axis_size(axis))
    route = [(i - distance, i) for i in devices if i - distance in devices]
    return lax.ppermute(block, axis, route)


def extended(x, sides, width):
    for axis, dim in sides:
        size, length = (lax.axis_size(axis), x.shape[dim])
        up = [(i, (i + 1) % size) for i in range(size - 1)]
        down = [(j, i) for i, j in up]
        last = lax.slice_in_dim(x, length - width, length, axis=dim)
        first = lax.slice_in_dim(x, 0, width, axis=dim)
        before = lax.ppermute(last, axis, up)
        after = lax.ppermute(first, axis, down)
        x = jnp.concatenate([before, x, after], axis=dim)
    return x


def from_partner(x, axis, bit):
    return lax.ppermute(x, axis, [(i, i ^ 1 << bit) for i in range(lax.axis_size(axis))])


def window_offsets():
    offsets_list = []
    for across in range(-window_reach, window_reach + 1):
        for upward in range(-window_reach, window_reach + 1):
            for sideways in range(-window_reach, window_reach + 1):
                length = math.sqrt(across * across + upward * upward + sideways * sideways)
                offsets_list.append((across, upward, sideways, length))
    return offsets_list


def layer_weights(radius):
    radial = radius.astype(jnp.float32)
    return jnp.stack(
        [jnp.maximum(radial - length, 0.0) for across, upward, sideways, length in window_offsets()]
    )


def pad_axis(grid_field, along_axis, before, after_cells):
    widths = [(0, 0)] * grid_field.ndim
    widths[along_axis] = (before, after_cells)
    return jnp.pad(grid_field, widths)


def pad_sides(grid_field):
    return jnp.pad(grid_field, ((0, 0), (window_reach, window_reach), (window_reach, window_reach)))


def filter_forward(padded, weights):
    out_rows = padded.shape[0] - 2 * window_reach
    layers = padded.shape[1] - 2 * window_reach
    row_width = padded.shape[2] - 2 * window_reach
    result = jnp.zeros((out_rows, layers, row_width), jnp.float32)
    for offset_index, (across, upward, sideways, length) in enumerate(window_offsets()):
        shifted = padded[
            window_reach + across : window_reach + across + out_rows,
            window_reach + upward : window_reach + upward + layers,
            window_reach + sideways : window_reach + sideways + row_width,
        ]
        result = result + weights[offset_index][None, :, None] * shifted
    return result


def filter_backward(padded, padded_weights):
    out_rows = padded.shape[0] - 2 * window_reach
    layers = padded.shape[1] - 2 * window_reach
    row_width = padded.shape[2] - 2 * window_reach
    result = jnp.zeros((out_rows, layers, row_width), jnp.float32)
    for offset_index, (across, upward, sideways, length) in enumerate(window_offsets()):
        shifted = padded[
            window_reach - across : window_reach - across + out_rows,
            window_reach - upward : window_reach - upward + layers,
            window_reach - sideways : window_reach - sideways + row_width,
        ]
        layer_part = padded_weights[
            offset_index, window_reach - upward : window_reach - upward + layers
        ]
        result = result + layer_part[None, :, None] * shifted
    return result


def stiff_factors(direction):
    return jnp.array(
        [2.0 if component == direction else 1.0 for component in range(3)], jnp.float32
    ).reshape(3, 1, 1, 1)


def relax_slab(padded, displace, face_x, face_z, face_y, force_field, free_cells, diagonal):
    flux_x = stiff_factors(0) * face_x * jnp.diff(padded, axis=1)
    stencil_image = flux_x[:, :-1] - flux_x[:, 1:]
    flux_z = stiff_factors(1) * face_z * jnp.diff(displace, axis=2)
    stencil_image = stencil_image + pad_axis(flux_z, 2, 1, 0) - pad_axis(flux_z, 2, 0, 1)
    flux_y = stiff_factors(2) * face_y * jnp.diff(displace, axis=3)
    stencil_image = stencil_image + pad_axis(flux_y, 3, 1, 0) - pad_axis(flux_y, 3, 0, 1)
    return free_cells * (displace + relax_factor * (force_field - stencil_image) / diagonal)


def slab_energy(grid_field, along_axis, direction, load_cases):
    change = jnp.diff(grid_field, axis=along_axis)
    return jnp.sum(stiff_factors(direction) * change * change, axis=0) / load_cases


def neighbour_planes(displace, load_cases, axis_devices):
    if axis_devices > load_cases:
        below = from_behind(displace[:, -1:], "space", load_cases)
        above = from_behind(displace[:, :1], "space", -load_cases)
    else:
        below = jnp.zeros_like(displace[:, :1])
        above = jnp.zeros_like(displace[:, :1])
    return jnp.concatenate([below, displace, above], axis=1)


def many_slabs(density, displacement, fixed, load_index, load_force, radius):
    slab_rows, layers, row_width = density.shape
    load_cases = load_index.shape[0]
    level_count = load_cases.bit_length() - 1
    axis_devices = lax.axis_size("space")
    axis_place = lax.axis_index("space")
    slab_planes = slab_rows * load_cases
    slab_place = axis_place // load_cases
    load_place = axis_place % load_cases
    total_rows = slab_rows * axis_devices
    weights = layer_weights(radius)
    padded_weights = pad_axis(weights, 1, window_reach, window_reach)
    global_rows = (
        jnp.arange(slab_rows + 2 * window_reach, dtype=jnp.int32)
        + axis_place * slab_rows
        - window_reach
    )
    deep_inside = ((global_rows >= 0) & (global_rows < total_rows)).astype(jnp.float32)
    inside_field = deep_inside[:, None, None] * pad_sides(
        jnp.ones((slab_rows + 2 * window_reach, layers, row_width), jnp.float32)
    )
    total_weight = filter_forward(inside_field, weights)
    slab_start = slab_place * slab_planes
    margin_rows = jnp.arange(slab_planes + 2, dtype=jnp.int32) + slab_start - 1
    margin_inside = ((margin_rows >= 0) & (margin_rows < total_rows)).astype(jnp.float32)
    face_valid = margin_inside[1:] * margin_inside[:-1]
    fixed_slab = lax.dynamic_slice_in_dim(fixed, slab_start, slab_planes, 0).astype(jnp.float32)
    bottom_layer = (jnp.arange(layers, dtype=jnp.int32) == 0).astype(jnp.float32)
    free_cells = 1.0 - bottom_layer[None, :, None] * fixed_slab[:, None, :]
    slab_cells = slab_planes * layers * row_width
    cell_index = jnp.arange(slab_cells, dtype=jnp.int32) + slab_place * slab_cells
    load_hot = jnp.arange(load_cases, dtype=jnp.int32) == load_place
    own_index = jnp.sum(jnp.where(load_hot, load_index, 0))
    own_force = jnp.sum(load_hot.astype(jnp.float32)[:, None] * load_force, axis=0)
    load_hits = (cell_index == own_index).astype(jnp.float32)
    force_field = (own_force[:, None] * load_hits[None, :]).reshape(
        3, slab_planes, layers, row_width
    )
    displace = displacement[0] * free_cells
    target = volume_share * total_rows * layers * row_width
    padded = neighbour_planes(displace, load_cases, axis_devices)
    halo_density = extended(density, (("space", 0),), window_reach)
    filtered = filter_forward(pad_sides(halo_density), weights) / total_weight
    whole_field = lax.all_gather(filtered, "space", axis=0, tiled=True)
    margin = lax.dynamic_slice_in_dim(
        pad_axis(whole_field, 0, 1, 1), slab_start, slab_planes + 2, 0
    )
    moduli = floor_modulus + (1.0 - floor_modulus) * margin**3
    face_x = 0.5 * (moduli[1:] + moduli[:-1]) * face_valid[:, None, None]
    inner_moduli = moduli[1:-1]
    face_z = 0.5 * (inner_moduli[:, 1:] + inner_moduli[:, :-1])
    face_y = 0.5 * (inner_moduli[:, :, 1:] + inner_moduli[:, :, :-1])
    sum_x = face_x[:-1] + face_x[1:]
    sum_z = pad_axis(face_z, 1, 1, 0) + pad_axis(face_z, 1, 0, 1)
    sum_y = pad_axis(face_y, 2, 1, 0) + pad_axis(face_y, 2, 0, 1)
    diagonal = stiff_factors(0) * sum_x + stiff_factors(1) * sum_z + stiff_factors(2) * sum_y
    for sweep_index in range(SWEEPS):
        displace = relax_slab(
            padded, displace, face_x, face_z, face_y, force_field, free_cells, diagonal
        )
        padded = neighbour_planes(displace, load_cases, axis_devices)
    energy_x = slab_energy(padded, 1, 0, load_cases) * face_valid[:, None, None]
    energy_z = slab_energy(displace, 2, 1, load_cases)
    energy_y = slab_energy(displace, 3, 2, load_cases)
    sens_term = 0.5 * (
        energy_x[:-1]
        + energy_x[1:]
        + pad_axis(energy_z, 1, 1, 0)
        + pad_axis(energy_z, 1, 0, 1)
        + pad_axis(energy_y, 2, 1, 0)
        + pad_axis(energy_y, 2, 0, 1)
    )
    sensitive = sens_term
    for level in reversed(range(level_count)):
        half_rows = sensitive.shape[0] // 2
        upper_side = load_place // 2**level % 2 == 1
        outgoing = jnp.where(upper_side, sensitive[:half_rows], sensitive[half_rows:])
        keeping = jnp.where(upper_side, sensitive[half_rows:], sensitive[:half_rows])
        sensitive = keeping + from_partner(outgoing, "space", level)
    weighted_share = 3.0 * (1.0 - floor_modulus) * filtered**2 * sensitive / total_weight
    halo_share = extended(weighted_share, (("space", 0),), window_reach)
    root_term = jnp.sqrt(filter_backward(pad_sides(halo_share), padded_weights))
    lowest = jnp.maximum(density - move_limit, density_floor)
    highest = jnp.minimum(density + move_limit, 1.0)
    design_now = density

    def trial_design(log_level):
        return jnp.clip(design_now * root_term * jnp.exp(-0.5 * log_level), lowest, highest)

    start_state = (jnp.asarray(log_lower, jnp.float32), jnp.asarray(log_span, jnp.float32))

    def halve(search_step, search_state):
        lower_end, span_width = search_state
        half_span = span_width * 0.5
        middle = lower_end + half_span
        volume_total = lax.psum(jnp.sum(trial_design(middle)), "space")
        return (jnp.where(volume_total > target, middle, lower_end), half_span)

    lower_end, span_width = lax.fori_loop(0, SEARCH, halve, start_state)
    density = trial_design(lower_end + 0.5 * span_width)
    new_displacement = displace[None]
    return (density, new_displacement)


def solution(mesh):
    in_specs = (
        P("space", "parts", None),
        P("space", None, None, "parts", None),
        P(None, "parts"),
        P("parts"),
        P("parts", None),
        P("parts"),
    )
    out_specs = (P("space", "parts", None), P("space", None, None, "parts", None))

    def local(density, displacement, fixed, load_index, load_force, radius):
        alone = lax.axis_size("space") == load_index.shape[0]
        run = one_slab if alone else many_slabs
        return run(density, displacement, fixed, load_index, load_force, radius)

    return jax.shard_map(local, mesh=mesh, in_specs=in_specs, out_specs=out_specs, check_vma=False)
```

```python
import math

import jax
import jax.numpy as jnp
from jax import lax
from jax.experimental import pallas as pl
from jax.experimental.pallas import tpu as pltpu
from jax.sharding import PartitionSpec as P

SWEEPS = 3
SEARCH = 12


floor_modulus = 0.05
relax_factor = 0.6
move_limit = 0.2
density_floor = 0.01
volume_share = 0.5
log_lower = -16.0
log_span = 32.0
window_reach = 2

PLANE_SQUARES = (0, 1, 2, 4, 5, 8)
ALL_SQUARES = (0, 1, 2, 3, 4, 5, 6, 8, 9, 12)


def spot_iota(shape, dim):
    return lax.broadcasted_iota(jnp.int32, shape, dim)


def each_plane(planes, body, carry):
    for x in range(planes):
        carry = body(x, carry)
    return carry


def each_chunk(planes, count, body, carry):
    return lax.fori_loop(0, planes // count, lambda i, carry: body(i * count, carry), carry)


def layer_radius(radius_ref, layers, row_width):
    z = spot_iota((layers, row_width), 0)
    result = jnp.zeros((layers, row_width), jnp.int32)
    for layer in range(layers):
        result = jnp.where(z == layer, radius_ref[layer], result)
    return result.astype(jnp.float32)


def class_weights(radius_ref, weight_ref):
    layers, row_width = weight_ref.shape[1:]
    radial = layer_radius(radius_ref, layers, row_width)
    for place, square in enumerate(ALL_SQUARES):
        weight_ref[place] = jnp.maximum(radial - math.sqrt(square), 0.0)


def shift_sum(field, dim, distance):
    size = field.shape[dim]
    spot = spot_iota(field.shape, dim)
    ahead = jnp.where(spot < size - distance, pltpu.roll(field, size - distance, dim), 0.0)
    behind = jnp.where(spot >= distance, pltpu.roll(field, distance, dim), 0.0)
    return ahead + behind


def plane_sums(plane):
    beside = shift_sum(plane, 1, 1)
    further = shift_sum(plane, 1, 2)
    return {
        0: plane,
        1: beside + shift_sum(plane, 0, 1),
        2: shift_sum(beside, 0, 1),
        4: further + shift_sum(plane, 0, 2),
        5: shift_sum(further, 0, 1) + shift_sum(beside, 0, 2),
        8: shift_sum(further, 0, 2),
    }


def weigh(sums, weight_ref, square):
    result = None
    for inner in PLANE_SQUARES:
        term = weight_ref[ALL_SQUARES.index(inner + square)] * sums[inner]
        result = term if result is None else result + term
    return result


def forward_planes(plane, weight_ref):
    sums = plane_sums(plane)
    return [weigh(sums, weight_ref, square) for square in (0, 1, 4)]


def rows(x, layers, shift=0):
    return pl.ds(x * layers + shift, layers)


GAP = 8


def gapped(x, layers, shift=0):
    return pl.ds(GAP + x * (layers + GAP) + shift, layers)


def gap(x, layers):
    return pl.ds(x * (layers + GAP), GAP)


def edge_class(x, planes):
    return jnp.minimum(x, 2) + jnp.maximum(x - (planes - 3), 0)


def zero_edges(ref):
    planes = ref.shape[0]
    for place in (0, 1, planes - 2, planes - 1):
        ref[place] = jnp.zeros(ref.shape[1:], ref.dtype)


def group_spots(group, blocks):
    chips, own_planes = blocks.shape[:2]
    mine = lax.axis_index("space")
    core = mine ^ mine >> 1 ^ group
    return [
        (own_planes * (2 * chip + ((core ^ chip) & 1)) + own, (chip, own))
        for chip in range(chips)
        for own in range(own_planes)
    ]


def spread_group(blocks, spread):
    chips, own_planes, layers, row_width = blocks.shape
    zero_gap = jnp.zeros((GAP, row_width), jnp.float32)
    for ref in spread:
        ref[gap(0, layers)] = zero_gap
    for p in range(chips * own_planes):
        plane = blocks[p // own_planes, p % own_planes]
        for ref, field in zip(spread, (plane, shift_sum(plane, 1, 1), shift_sum(plane, 1, 2))):
            ref[gapped(p, layers)] = field
            ref[gap(p + 1, layers)] = zero_gap


def filter_plane(p, layers, spread, weight_ref):
    def around(place, distance):
        ref = spread[place]
        return ref[gapped(p, layers, distance)] + ref[gapped(p, layers, -distance)]

    sums = {
        0: spread[0][gapped(p, layers)],
        1: spread[1][gapped(p, layers)] + around(0, 1),
        2: around(1, 1),
        4: spread[2][gapped(p, layers)] + around(0, 2),
        5: around(2, 1) + around(1, 2),
        8: around(2, 2),
    }
    return [weigh(sums, weight_ref, square) for square in (0, 1, 4)]


def prepare_kernel(
    radius_hbm,
    index_hbm,
    force_hbm,
    fixed_hbm,
    density_ref,
    weight_ref,
    inverse_ref,
    free_ref,
    load_ref,
    spot_ref,
    filter_ref,
    radius_ref,
    index_ref,
    force_ref,
    fixed_ref,
    plane_ref,
    beside_ref,
    further_ref,
    arrived,
):
    copies = [
        pltpu.make_async_copy(source, target, arrived.at[place])
        for place, (source, target) in enumerate(
            (
                (radius_hbm, radius_ref),
                (index_hbm, index_ref),
                (force_hbm, force_ref),
                (fixed_hbm, fixed_ref),
            )
        )
    ]
    for copy in copies:
        copy.start()
    spread = (plane_ref, beside_ref, further_ref)
    spread_group(density_ref, spread)
    for copy in copies:
        copy.wait()
    planes, layers, row_width = free_ref.shape
    load_place = lax.axis_index("space")
    shape = (layers, row_width)
    z = spot_iota(shape, 0)
    y = spot_iota(shape, 1)

    class_weights(radius_ref, weight_ref)
    own_planes = density_ref.shape[1]
    for p in range(density_ref.shape[0] * own_planes):
        for place, field in enumerate(filter_plane(p, layers, spread, weight_ref)):
            filter_ref[place, p // own_planes, p % own_planes] = field

    ones = forward_planes(jnp.ones(shape, jnp.float32), weight_ref)
    for place, (lower, upper) in enumerate(((0, 2), (1, 2), (2, 2), (2, 1), (2, 0))):
        inverse_ref[place] = 1.0 / (
            ones[0] + min(lower, 1) * ones[1] + min(upper, 1) * ones[1]
            + (lower // 2) * ones[2] + (upper // 2) * ones[2]
        )

    def free_plane(x, carry):
        free_ref[x] = jnp.where(
            z == 0, 1.0 - fixed_ref[pl.ds(x, 1), :].astype(jnp.float32), 1.0
        )
        return carry

    each_plane(planes, free_plane, 0)

    own_index = index_ref[load_place]
    own_z = own_index // row_width % layers
    own_y = own_index % row_width
    hit = (z == own_z) & (y == own_y)
    for part in range(3):
        load_ref[part] = jnp.where(hit, force_ref[part, load_place], 0.0)
    own_x = (own_index // (layers * row_width)).astype(jnp.float32)
    spot_ref[...] = jnp.full(spot_ref.shape, own_x)


def sweep_kernel(
    spot_ref,
    load_ref,
    weight_ref,
    inverse_ref,
    free_ref,
    filter_ref,
    density_ref,
    start_ref,
    disp_ref,
    coef_ref,
    plane_ref,
    beside_ref,
    further_ref,
    near_ref,
    side_ref,
    far_ref,
    modulus_ref,
    across_ref,
    up_ref,
    right_ref,
    left_ref,
    rate_ref,
    first_ref,
):
    planes, layers, row_width = coef_ref.shape
    shape = (layers, row_width)
    z = spot_iota(shape, 0)
    y = spot_iota(shape, 1)
    zero = jnp.zeros(shape, jnp.float32)

    for ref in (side_ref, far_ref):
        zero_edges(ref)
    results = (near_ref, side_ref, far_ref)
    other_ref = density_ref.at[1]
    for x, spot in group_spots(0, other_ref):
        for place, ref in enumerate(results):
            ref[x + 2] = filter_ref[(place,) + spot]
    spread = (plane_ref, beside_ref, further_ref)
    spread_group(other_ref, spread)
    for p, (x, spot) in enumerate(group_spots(1, other_ref)):
        for ref, field in zip(results, filter_plane(p, layers, spread, weight_ref)):
            ref[x + 2] = field

    for ref in (first_ref, disp_ref):
        for part in range(3):
            ref[part, rows(0, layers)] = zero
            ref[part, rows(planes + 1, layers)] = zero

    def store_faces(slot, modulus, above, later, before, free, start, views):
        across, up_view, right_view, left_view, rate, source = views
        across[slot] = later
        up = jnp.where(z < layers - 1, 0.5 * (modulus + above), 0.0)
        right = jnp.where(
            y < row_width - 1, 0.5 * (modulus + pltpu.roll(modulus, row_width - 1, 1)), 0.0
        )
        left = pltpu.roll(right, 1, 1)
        up_view[rows(slot, layers)] = up
        right_view[slot] = right
        left_view[slot] = left
        sums = (before + later, up + pltpu.roll(up, 1, 0), left + right)
        every = sums[0] + sums[1] + sums[2]
        diagonal = [every + part_sum for part_sum in sums]
        pair = diagonal[0] * diagonal[1]
        push = relax_factor * free / (pair * diagonal[2])
        side = push * diagonal[2]
        for part, factor in enumerate((side * diagonal[1], side * diagonal[0], push * pair)):
            rate[part, slot] = factor
            source[part, rows(slot, layers)] = start[part] * free

    piece = planes // 4

    def modulus_piece(first, carry):
        count = piece
        near = near_ref.at[pl.ds(first + 2, count)]
        side = side_ref.at[pl.ds(first + 1, count + 2)]
        far = far_ref.at[pl.ds(first, count + 4)]
        moduli = modulus_ref.at[pl.ds(first * layers, (count + 1) * layers)]
        coef = coef_ref.at[pl.ds(first, count)]
        free = free_ref.at[pl.ds(first, count)]
        views = (
            across_ref.at[pl.ds(first, count)],
            up_ref.at[pl.ds(first * layers, count * layers)],
            right_ref.at[pl.ds(first, count)],
            left_ref.at[pl.ds(first, count)],
            rate_ref.at[:, pl.ds(first, count)],
            first_ref.at[:, pl.ds(first * layers, count * layers)],
        )
        modulus, before = carry
        for p in range(count):
            inverse = inverse_ref[edge_class(first + p, planes)]
            filtered = near[p] + side[p] + side[p + 2] + far[p] + far[p + 4]
            filtered = filtered * inverse
            later = floor_modulus + (1.0 - floor_modulus) * (filtered * filtered * filtered)
            coef[p] = 3.0 * (1.0 - floor_modulus) * (filtered * filtered) * inverse
            moduli[rows(p + 1, layers)] = later
            ahead = 0.5 * (modulus + later)
            if p == 0:
                ahead = jnp.where(first > 0, ahead, 0.0)
            above = moduli[rows(p, layers, 1)] if p else pltpu.roll(modulus, layers - 1, 0)
            previous = jnp.maximum(first + p - 1, 0)
            store_faces(
                p,
                modulus,
                above,
                ahead,
                before,
                free_ref[previous],
                [start_ref[part, previous] for part in range(3)],
                views,
            )
            modulus, before = later, ahead
        return modulus, before

    modulus, before = each_chunk(planes, piece, modulus_piece, (jnp.ones(shape, jnp.float32), zero))
    store_faces(
        planes,
        modulus,
        pltpu.roll(modulus, layers - 1, 0),
        zero,
        before,
        free_ref[planes - 1],
        [start_ref[part, planes - 1] for part in range(3)],
        (across_ref, up_ref, right_ref, left_ref, rate_ref, first_ref),
    )

    own_x = jnp.max(spot_ref[...]).astype(jnp.int32)

    def sweep(source, target):
        def sweep_piece(first, carry):
            count = piece
            old = source.at[:, pl.ds(first * layers, (count + 2) * layers)]
            new = target.at[:, pl.ds((first + 1) * layers, count * layers)]
            across = across_ref.at[pl.ds(first, count + 1)]
            up = up_ref.at[pl.ds(first * layers, (count + 1) * layers)]
            right = right_ref.at[pl.ds(first + 1, count)]
            left = left_ref.at[pl.ds(first + 1, count)]
            rate = rate_ref.at[:, pl.ds(first + 1, count)]
            behind = [old[part, rows(0, layers)] for part in range(3)]
            here = [old[part, rows(1, layers)] for part in range(3)]
            for p in range(count):
                ahead = [old[part, rows(p + 2, layers)] for part in range(3)]
                for part in range(3):
                    pulls = [
                        across[p] * behind[part] + across[p + 1] * ahead[part],
                        up[rows(p + 1, layers)] * old[part, rows(p + 1, layers, 1)]
                        + up[rows(p + 1, layers, -1)] * old[part, rows(p + 1, layers, -1)],
                        right[p] * pltpu.roll(here[part], row_width - 1, 1)
                        + left[p] * pltpu.roll(here[part], 1, 1),
                    ]
                    pull = pulls[0] + pulls[1] + pulls[2] + pulls[part]
                    new[part, rows(p, layers)] = (
                        1.0 - relax_factor
                    ) * here[part] + rate[part, p] * pull
                behind, here = here, ahead
            return carry

        each_chunk(planes, piece, sweep_piece, 0)
        for part in range(3):
            target[part, rows(own_x + 1, layers)] += rate_ref[part, own_x + 1] * load_ref[part]

    def two_sweeps(turn, carry):
        sweep(first_ref, disp_ref)

        @pl.when(turn < SWEEPS // 2)
        def _():
            sweep(disp_ref, first_ref)

        return carry

    lax.fori_loop(0, SWEEPS // 2 + 1, two_sweeps, 0)


def filter_group(group, shares, weight_ref, near_ref, far_ref, result_ref):
    chips, own_planes, layers, row_width = result_ref.shape
    zero_gap = jnp.zeros((GAP, row_width), jnp.float32)
    mine = lax.axis_index("space")
    core = (mine ^ mine >> 1 ^ group) & 1
    count = shares[0].shape[0] - own_planes
    views = [
        [ref.at[pl.ds(own_planes * start, count)] for ref in shares] for start in (core, 1 - core)
    ]
    for ref in (near_ref, far_ref):
        ref[gap(0, layers)] = zero_gap
    for p in range(chips * own_planes):
        chip, own = p // own_planes, p % own_planes
        plane, beside, further = views[chip & 1]
        x = 2 * own_planes * chip + own + 2

        def around(ref, distance):
            return ref[x + distance] + ref[x - distance]

        sums = {
            0: plane[x],
            1: beside[x] + around(plane, 1),
            2: around(beside, 1),
            4: further[x] + around(plane, 2),
            5: around(further, 1) + around(beside, 2),
            8: around(further, 2),
        }
        level = weigh(sums, weight_ref, 0)
        for ref, square in ((near_ref, 1), (far_ref, 4)):
            ref[gapped(p, layers)] = weigh(sums, weight_ref, square)
            ref[gap(p + 1, layers)] = zero_gap
        result_ref[chip, own] = (
            level
            + near_ref[gapped(p, layers, 1)]
            + near_ref[gapped(p, layers, -1)]
            + far_ref[gapped(p, layers, 2)]
            + far_ref[gapped(p, layers, -2)]
        )


def share_kernel(
    disp_ref,
    coef_ref,
    weight_ref,
    sent_ref,
    plane_ref,
    beside_ref,
    further_ref,
    near_ref,
    far_ref,
):
    planes, layers, row_width = coef_ref.shape
    load_cases = lax.axis_size("space")
    shape = (layers, row_width)
    z = spot_iota(shape, 0)
    y = spot_iota(shape, 1)
    zero = jnp.zeros(shape, jnp.float32)
    shares = (plane_ref, beside_ref, further_ref)
    for ref in shares:
        zero_edges(ref)

    count = planes // 8

    def share_chunk(first, before):
        disp = disp_ref.at[:, pl.ds((first + 1) * layers, (count + 1) * layers)]
        coef = coef_ref.at[pl.ds(first, count)]
        plane, beside, further = (ref.at[pl.ds(first + 2, count)] for ref in shares)
        here = [disp[part, rows(0, layers)] for part in range(3)]
        for p in range(count):
            later = [disp[part, rows(p + 1, layers)] for part in range(3)]
            ahead, upward, right = zero, zero, zero
            for part in range(3):
                step = later[part] - here[part]
                climb = disp[part, rows(p, layers, 1)] - here[part]
                slide = pltpu.roll(here[part], row_width - 1, 1) - here[part]
                ahead = ahead + (2.0 if part == 0 else 1.0) * (step * step)
                upward = upward + (2.0 if part == 1 else 1.0) * (climb * climb)
                right = right + (2.0 if part == 2 else 1.0) * (slide * slide)
            if p == count - 1:
                ahead = jnp.where(first + count < planes, ahead, 0.0)
            upward = jnp.where(z < layers - 1, upward, 0.0)
            right = jnp.where(y < row_width - 1, right, 0.0)
            total = before + ahead + upward + pltpu.roll(upward, 1, 0)
            total = total + right + pltpu.roll(right, 1, 1)
            share = (0.5 / load_cases) * total * coef[p]
            plane[p] = share
            beside[p] = shift_sum(share, 1, 1)
            further[p] = shift_sum(share, 1, 2)
            before, here = ahead, later
        return before

    each_chunk(planes, count, share_chunk, zero)
    filter_group(1, shares, weight_ref, near_ref, far_ref, sent_ref)


def kept_kernel(
    disp_ref,
    weight_ref,
    plane_ref,
    beside_ref,
    further_ref,
    disp_hbm,
    kept_ref,
    near_ref,
    far_ref,
    stored,
):
    layers = kept_ref.shape[2]
    inner = pl.ds(layers, disp_ref.shape[1] - 2 * layers)
    store = pltpu.make_async_copy(disp_ref.at[:, inner], disp_hbm, stored)
    store.start()
    shares = (plane_ref, beside_ref, further_ref)
    filter_group(0, shares, weight_ref, near_ref, far_ref, kept_ref)
    store.wait()


def design_kernel(root_ref, density_ref, new_ref, pull_ref, low_ref, high_ref):
    groups, chips, own_planes, layers, row_width = density_ref.shape
    own_chip = lax.axis_index("space") >> 1
    shape = (layers, row_width)
    zero = jnp.zeros(shape, jnp.float32)
    planes = [
        (group, chip, own)
        for group in range(groups)
        for chip in range(chips)
        for own in range(own_planes)
    ]
    for spot in planes:
        density = density_ref[spot]
        pull_ref[spot] = density * root_ref[spot]
        low_ref[spot] = jnp.maximum(density - move_limit, density_floor)
        high_ref[spot] = jnp.minimum(density + move_limit, 1.0)

    target = volume_share * len(planes) * layers * row_width

    def factor_of(log_level):
        return jnp.broadcast_to(jnp.exp(-0.5 * log_level), shape)

    def exceeds(total):
        return jnp.sum(jnp.sum(total, axis=0, keepdims=True), axis=1, keepdims=True) > target

    def halve_twice(step, state):
        lower, span = state
        half, quarter = span * 0.5, span * 0.25
        middles = (lower + quarter, lower + half, lower + half + quarter)
        factors = [factor_of(middle) for middle in middles]
        totals = [zero, zero, zero]
        for spot in planes:
            pull, low, high = pull_ref[spot], low_ref[spot], high_ref[spot]
            totals = [
                total + jnp.minimum(jnp.maximum(pull * factor, low), high)
                for total, factor in zip(totals, factors)
            ]
        first, second, third = (exceeds(total) for total in totals)
        upper = jnp.where(third, middles[2], middles[1])
        below = jnp.where(first, middles[0], lower)
        return jnp.where(second, upper, below), quarter

    start = (jnp.full((1, 1), log_lower, jnp.float32), jnp.full((1, 1), log_span, jnp.float32))
    lower, span = lax.fori_loop(0, SEARCH // 2, halve_twice, start)
    factor = factor_of(lower + 0.5 * span)
    for own in range(own_planes):
        spot = (0, own_chip, own)
        new_ref[own] = jnp.minimum(
            jnp.maximum(pull_ref[spot] * factor, low_ref[spot]), high_ref[spot]
        )


def in_vmem():
    return pl.BlockSpec(memory_space=pltpu.VMEM)


KERNEL_VMEM = 24 * 2**20


def floats(*shape):
    return jax.ShapeDtypeStruct(shape, jnp.float32)


def prepare_call(density, radius, load_index, load_force, fixed):
    chips, own_planes, layers, row_width = density.shape
    planes = fixed.shape[0]
    spread = pltpu.VMEM((chips * own_planes * (layers + GAP) + GAP, row_width), jnp.float32)
    return pl.pallas_call(
        prepare_kernel,
        out_shape=[
            floats(len(ALL_SQUARES), layers, row_width),
            floats(2 * window_reach + 1, layers, row_width),
            floats(planes, layers, row_width),
            floats(3, layers, row_width),
            floats(8, row_width),
            floats(3, *density.shape),
        ],
        in_specs=[pl.BlockSpec(memory_space=pltpu.HBM)] * 4 + [in_vmem()],
        out_specs=[in_vmem()] * 6,
        scratch_shapes=[
            pltpu.SMEM(radius.shape, radius.dtype),
            pltpu.SMEM(load_index.shape, load_index.dtype),
            pltpu.SMEM(load_force.shape, load_force.dtype),
            pltpu.VMEM(fixed.shape, fixed.dtype),
            spread,
            spread,
            spread,
            pltpu.SemaphoreType.DMA((4,)),
        ],
        compiler_params=pltpu.CompilerParams(vmem_limit_bytes=KERNEL_VMEM),
        cost_estimate=pl.CostEstimate(
            flops=80 * planes * layers * row_width,
            bytes_accessed=8 * planes * layers * row_width,
            transcendentals=0,
        ),
        name="prepare",
    )(
        *(
            pltpu.with_memory_space_constraint(array, pltpu.HBM)
            for array in (radius, load_index, load_force, fixed)
        ),
        density,
    )


def sweep_call(spot, load, weights, inverses, free, filtered, density, displacement):
    groups, chips, own_planes, layers, row_width = density.shape
    planes = groups * chips * own_planes

    def scratch(*lead):
        return pltpu.VMEM(lead + (row_width,), jnp.float32)

    return pl.pallas_call(
        sweep_kernel,
        out_shape=[
            floats(3, (planes + 2) * layers, row_width),
            floats(planes, layers, row_width),
        ],
        in_specs=[in_vmem()] * 8,
        out_specs=[in_vmem()] * 2,
        scratch_shapes=[
            scratch(planes // 2 * (layers + GAP) + GAP),
            scratch(planes // 2 * (layers + GAP) + GAP),
            scratch(planes // 2 * (layers + GAP) + GAP),
            scratch(planes + 4, layers),
            scratch(planes + 4, layers),
            scratch(planes + 4, layers),
            scratch((planes + 1) * layers),
            scratch(planes + 1, layers),
            scratch((planes + 1) * layers),
            scratch(planes + 1, layers),
            scratch(planes + 1, layers),
            scratch(3, planes + 1, layers),
            scratch(3, (planes + 2) * layers),
        ],
        compiler_params=pltpu.CompilerParams(vmem_limit_bytes=KERNEL_VMEM),
        name="sweeps",
    )(spot, load, weights, inverses, free, filtered, density, displacement)


def share_call(disp, coef, weights, group_shape):
    planes, layers, row_width = coef.shape
    gaps = pltpu.VMEM((planes // 2 * (layers + GAP) + GAP, row_width), jnp.float32)
    return pl.pallas_call(
        share_kernel,
        out_shape=[floats(*group_shape)] + [floats(planes + 4, layers, row_width)] * 3,
        in_specs=[in_vmem()] * 3,
        out_specs=[in_vmem()] * 4,
        scratch_shapes=[gaps, gaps],
        compiler_params=pltpu.CompilerParams(vmem_limit_bytes=KERNEL_VMEM),
        name="share",
    )(disp, coef, weights)


def kept_call(disp, weights, shares, group_shape):
    parts, disp_rows, row_width = disp.shape
    chips, own_planes, layers = group_shape[:3]
    gaps = pltpu.VMEM((chips * own_planes * (layers + GAP) + GAP, row_width), jnp.float32)
    return pl.pallas_call(
        kept_kernel,
        out_shape=[floats(parts, disp_rows - 2 * layers, row_width), floats(*group_shape)],
        in_specs=[in_vmem()] * 5,
        out_specs=[pl.BlockSpec(memory_space=pltpu.HBM), in_vmem()],
        scratch_shapes=[gaps, gaps, pltpu.SemaphoreType.DMA(())],
        compiler_params=pltpu.CompilerParams(vmem_limit_bytes=KERNEL_VMEM),
        cost_estimate=pl.CostEstimate(
            flops=20 * disp.size, bytes_accessed=8 * disp.size, transcendentals=0
        ),
        name="kept",
    )(disp, weights, *shares)


def design_call(root, density):
    return pl.pallas_call(
        design_kernel,
        out_shape=floats(*density.shape[2:]),
        in_specs=[in_vmem()] * 2,
        out_specs=in_vmem(),
        scratch_shapes=[pltpu.VMEM(density.shape, jnp.float32)] * 3,
        compiler_params=pltpu.CompilerParams(vmem_limit_bytes=KERNEL_VMEM),
        name="design",
    )(root, density)


def other_core(block):
    devices = lax.axis_size("space")
    return lax.ppermute(block, "space", [(i, i ^ 1) for i in range(devices)])


def chip_groups():
    chips = lax.axis_size("space") // 2
    return [[2 * chip + (chip ^ group) % 2 for chip in range(chips)] for group in range(2)]


def between_chips(pieces):
    return lax.all_to_all(pieces, "space", 0, 0, axis_index_groups=chip_groups())


def chip_gathered(block):
    chips = lax.axis_size("space") // 2
    return between_chips(jnp.broadcast_to(block[None], (chips,) + block.shape))


def with_other_core(blocks):
    return jnp.stack([blocks, other_core(blocks)])


def scattered_sum(sent, make_kept):
    received = other_core(sent)
    *others, kept = make_kept()
    return jnp.sum(between_chips(kept + received), axis=0), others


def one_slab(density, displacement, fixed, load_index, load_force, radius):
    same_group, small = lax.optimization_barrier(
        (chip_gathered(density), (radius, load_index, load_force.T, fixed))
    )
    other_group = other_core(same_group)
    weights, inverses, free, load, spot, filtered = prepare_call(same_group, *small)
    whole = jnp.stack([same_group, other_group])
    disp, coef = sweep_call(
        spot, load, weights, inverses, free, filtered, whole, displacement[0]
    )
    sent, *shares = share_call(disp, coef, weights, same_group.shape)
    sent, disp, shares = lax.optimization_barrier((sent, disp, shares))
    squares, (new_displacement,) = scattered_sum(
        sent, lambda: kept_call(disp, weights, shares, same_group.shape)
    )
    root = with_other_core(chip_gathered(jnp.sqrt(squares)))
    new_density = design_call(root, whole)
    return new_density, new_displacement.reshape(displacement.shape)


def from_behind(block, axis, distance):
    devices = range(lax.axis_size(axis))
    route = [(i - distance, i) for i in devices if i - distance in devices]
    return lax.ppermute(block, axis, route)


def extended(x, sides, width):
    for axis, dim in sides:
        size, length = (lax.axis_size(axis), x.shape[dim])
        up = [(i, (i + 1) % size) for i in range(size - 1)]
        down = [(j, i) for i, j in up]
        last = lax.slice_in_dim(x, length - width, length, axis=dim)
        first = lax.slice_in_dim(x, 0, width, axis=dim)
        before = lax.ppermute(last, axis, up)
        after = lax.ppermute(first, axis, down)
        x = jnp.concatenate([before, x, after], axis=dim)
    return x


def from_partner(x, axis, bit):
    return lax.ppermute(x, axis, [(i, i ^ 1 << bit) for i in range(lax.axis_size(axis))])


def window_offsets():
    offsets_list = []
    for across in range(-window_reach, window_reach + 1):
        for upward in range(-window_reach, window_reach + 1):
            for sideways in range(-window_reach, window_reach + 1):
                length = math.sqrt(across * across + upward * upward + sideways * sideways)
                offsets_list.append((across, upward, sideways, length))
    return offsets_list


def layer_weights(radius):
    radial = radius.astype(jnp.float32)
    return jnp.stack(
        [jnp.maximum(radial - length, 0.0) for across, upward, sideways, length in window_offsets()]
    )


def pad_axis(grid_field, along_axis, before, after_cells):
    widths = [(0, 0)] * grid_field.ndim
    widths[along_axis] = (before, after_cells)
    return jnp.pad(grid_field, widths)


def pad_sides(grid_field):
    return jnp.pad(grid_field, ((0, 0), (window_reach, window_reach), (window_reach, window_reach)))


def filter_forward(padded, weights):
    out_rows = padded.shape[0] - 2 * window_reach
    layers = padded.shape[1] - 2 * window_reach
    row_width = padded.shape[2] - 2 * window_reach
    result = jnp.zeros((out_rows, layers, row_width), jnp.float32)
    for offset_index, (across, upward, sideways, length) in enumerate(window_offsets()):
        shifted = padded[
            window_reach + across : window_reach + across + out_rows,
            window_reach + upward : window_reach + upward + layers,
            window_reach + sideways : window_reach + sideways + row_width,
        ]
        result = result + weights[offset_index][None, :, None] * shifted
    return result


def filter_backward(padded, padded_weights):
    out_rows = padded.shape[0] - 2 * window_reach
    layers = padded.shape[1] - 2 * window_reach
    row_width = padded.shape[2] - 2 * window_reach
    result = jnp.zeros((out_rows, layers, row_width), jnp.float32)
    for offset_index, (across, upward, sideways, length) in enumerate(window_offsets()):
        shifted = padded[
            window_reach - across : window_reach - across + out_rows,
            window_reach - upward : window_reach - upward + layers,
            window_reach - sideways : window_reach - sideways + row_width,
        ]
        layer_part = padded_weights[
            offset_index, window_reach - upward : window_reach - upward + layers
        ]
        result = result + layer_part[None, :, None] * shifted
    return result


def stiff_factors(direction):
    return jnp.array(
        [2.0 if component == direction else 1.0 for component in range(3)], jnp.float32
    ).reshape(3, 1, 1, 1)


def relax_slab(padded, displace, face_x, face_z, face_y, force_field, free_cells, diagonal):
    flux_x = stiff_factors(0) * face_x * jnp.diff(padded, axis=1)
    stencil_image = flux_x[:, :-1] - flux_x[:, 1:]
    flux_z = stiff_factors(1) * face_z * jnp.diff(displace, axis=2)
    stencil_image = stencil_image + pad_axis(flux_z, 2, 1, 0) - pad_axis(flux_z, 2, 0, 1)
    flux_y = stiff_factors(2) * face_y * jnp.diff(displace, axis=3)
    stencil_image = stencil_image + pad_axis(flux_y, 3, 1, 0) - pad_axis(flux_y, 3, 0, 1)
    return free_cells * (displace + relax_factor * (force_field - stencil_image) / diagonal)


def slab_energy(grid_field, along_axis, direction, load_cases):
    change = jnp.diff(grid_field, axis=along_axis)
    return jnp.sum(stiff_factors(direction) * change * change, axis=0) / load_cases


def neighbour_planes(displace, load_cases, axis_devices):
    if axis_devices > load_cases:
        below = from_behind(displace[:, -1:], "space", load_cases)
        above = from_behind(displace[:, :1], "space", -load_cases)
    else:
        below = jnp.zeros_like(displace[:, :1])
        above = jnp.zeros_like(displace[:, :1])
    return jnp.concatenate([below, displace, above], axis=1)


def many_slabs(density, displacement, fixed, load_index, load_force, radius):
    slab_rows, layers, row_width = density.shape
    load_cases = load_index.shape[0]
    level_count = load_cases.bit_length() - 1
    axis_devices = lax.axis_size("space")
    axis_place = lax.axis_index("space")
    slab_planes = slab_rows * load_cases
    slab_place = axis_place // load_cases
    load_place = axis_place % load_cases
    total_rows = slab_rows * axis_devices
    weights = layer_weights(radius)
    padded_weights = pad_axis(weights, 1, window_reach, window_reach)
    global_rows = (
        jnp.arange(slab_rows + 2 * window_reach, dtype=jnp.int32)
        + axis_place * slab_rows
        - window_reach
    )
    deep_inside = ((global_rows >= 0) & (global_rows < total_rows)).astype(jnp.float32)
    inside_field = deep_inside[:, None, None] * pad_sides(
        jnp.ones((slab_rows + 2 * window_reach, layers, row_width), jnp.float32)
    )
    total_weight = filter_forward(inside_field, weights)
    slab_start = slab_place * slab_planes
    margin_rows = jnp.arange(slab_planes + 2, dtype=jnp.int32) + slab_start - 1
    margin_inside = ((margin_rows >= 0) & (margin_rows < total_rows)).astype(jnp.float32)
    face_valid = margin_inside[1:] * margin_inside[:-1]
    fixed_slab = lax.dynamic_slice_in_dim(fixed, slab_start, slab_planes, 0).astype(jnp.float32)
    bottom_layer = (jnp.arange(layers, dtype=jnp.int32) == 0).astype(jnp.float32)
    free_cells = 1.0 - bottom_layer[None, :, None] * fixed_slab[:, None, :]
    slab_cells = slab_planes * layers * row_width
    cell_index = jnp.arange(slab_cells, dtype=jnp.int32) + slab_place * slab_cells
    load_hot = jnp.arange(load_cases, dtype=jnp.int32) == load_place
    own_index = jnp.sum(jnp.where(load_hot, load_index, 0))
    own_force = jnp.sum(load_hot.astype(jnp.float32)[:, None] * load_force, axis=0)
    load_hits = (cell_index == own_index).astype(jnp.float32)
    force_field = (own_force[:, None] * load_hits[None, :]).reshape(
        3, slab_planes, layers, row_width
    )
    displace = displacement[0] * free_cells
    target = volume_share * total_rows * layers * row_width
    padded = neighbour_planes(displace, load_cases, axis_devices)
    halo_density = extended(density, (("space", 0),), window_reach)
    filtered = filter_forward(pad_sides(halo_density), weights) / total_weight
    whole_field = lax.all_gather(filtered, "space", axis=0, tiled=True)
    margin = lax.dynamic_slice_in_dim(
        pad_axis(whole_field, 0, 1, 1), slab_start, slab_planes + 2, 0
    )
    moduli = floor_modulus + (1.0 - floor_modulus) * margin**3
    face_x = 0.5 * (moduli[1:] + moduli[:-1]) * face_valid[:, None, None]
    inner_moduli = moduli[1:-1]
    face_z = 0.5 * (inner_moduli[:, 1:] + inner_moduli[:, :-1])
    face_y = 0.5 * (inner_moduli[:, :, 1:] + inner_moduli[:, :, :-1])
    sum_x = face_x[:-1] + face_x[1:]
    sum_z = pad_axis(face_z, 1, 1, 0) + pad_axis(face_z, 1, 0, 1)
    sum_y = pad_axis(face_y, 2, 1, 0) + pad_axis(face_y, 2, 0, 1)
    diagonal = stiff_factors(0) * sum_x + stiff_factors(1) * sum_z + stiff_factors(2) * sum_y
    for sweep_index in range(SWEEPS):
        displace = relax_slab(
            padded, displace, face_x, face_z, face_y, force_field, free_cells, diagonal
        )
        padded = neighbour_planes(displace, load_cases, axis_devices)
    energy_x = slab_energy(padded, 1, 0, load_cases) * face_valid[:, None, None]
    energy_z = slab_energy(displace, 2, 1, load_cases)
    energy_y = slab_energy(displace, 3, 2, load_cases)
    sens_term = 0.5 * (
        energy_x[:-1]
        + energy_x[1:]
        + pad_axis(energy_z, 1, 1, 0)
        + pad_axis(energy_z, 1, 0, 1)
        + pad_axis(energy_y, 2, 1, 0)
        + pad_axis(energy_y, 2, 0, 1)
    )
    sensitive = sens_term
    for level in reversed(range(level_count)):
        half_rows = sensitive.shape[0] // 2
        upper_side = load_place // 2**level % 2 == 1
        outgoing = jnp.where(upper_side, sensitive[:half_rows], sensitive[half_rows:])
        keeping = jnp.where(upper_side, sensitive[half_rows:], sensitive[:half_rows])
        sensitive = keeping + from_partner(outgoing, "space", level)
    weighted_share = 3.0 * (1.0 - floor_modulus) * filtered**2 * sensitive / total_weight
    halo_share = extended(weighted_share, (("space", 0),), window_reach)
    root_term = jnp.sqrt(filter_backward(pad_sides(halo_share), padded_weights))
    lowest = jnp.maximum(density - move_limit, density_floor)
    highest = jnp.minimum(density + move_limit, 1.0)
    design_now = density

    def trial_design(log_level):
        return jnp.clip(design_now * root_term * jnp.exp(-0.5 * log_level), lowest, highest)

    start_state = (jnp.asarray(log_lower, jnp.float32), jnp.asarray(log_span, jnp.float32))

    def halve(search_step, search_state):
        lower_end, span_width = search_state
        half_span = span_width * 0.5
        middle = lower_end + half_span
        volume_total = lax.psum(jnp.sum(trial_design(middle)), "space")
        return (jnp.where(volume_total > target, middle, lower_end), half_span)

    lower_end, span_width = lax.fori_loop(0, SEARCH, halve, start_state)
    density = trial_design(lower_end + 0.5 * span_width)
    new_displacement = displace[None]
    return (density, new_displacement)


def solution(mesh):
    in_specs = (
        P("space", "parts", None),
        P("space", None, None, "parts", None),
        P(None, "parts"),
        P("parts"),
        P("parts", None),
        P("parts"),
    )
    out_specs = (P("space", "parts", None), P("space", None, None, "parts", None))

    def local(density, displacement, fixed, load_index, load_force, radius):
        alone = lax.axis_size("space") == load_index.shape[0]
        run = one_slab if alone else many_slabs
        return run(density, displacement, fixed, load_index, load_force, radius)

    return jax.shard_map(local, mesh=mesh, in_specs=in_specs, out_specs=out_specs, check_vma=False)
```

```python
import math

import jax
import jax.numpy as jnp
from jax import lax
from jax.experimental import pallas as pl
from jax.experimental.pallas import tpu as pltpu
from jax.sharding import PartitionSpec as P

SWEEPS = 3
SEARCH = 12


floor_modulus = 0.05
relax_factor = 0.6
move_limit = 0.2
density_floor = 0.01
volume_share = 0.5
log_lower = -16.0
log_span = 32.0
window_reach = 2

PLANE_SQUARES = (0, 1, 2, 4, 5, 8)
ALL_SQUARES = (0, 1, 2, 3, 4, 5, 6, 8, 9, 12)


def spot_iota(shape, dim):
    return lax.broadcasted_iota(jnp.int32, shape, dim)


def each_plane(planes, body, carry):
    for x in range(planes):
        carry = body(x, carry)
    return carry


def each_chunk(planes, count, body, carry):
    return lax.fori_loop(0, planes // count, lambda i, carry: body(i * count, carry), carry)


def layer_radius(radius_ref, layers, row_width):
    z = spot_iota((layers, row_width), 0)
    result = jnp.zeros((layers, row_width), jnp.int32)
    for layer in range(layers):
        result = jnp.where(z == layer, radius_ref[layer], result)
    return result.astype(jnp.float32)


def class_weights(radius_ref, weight_ref):
    layers, row_width = weight_ref.shape[1:]
    radial = layer_radius(radius_ref, layers, row_width)
    for place, square in enumerate(ALL_SQUARES):
        weight_ref[place] = jnp.maximum(radial - math.sqrt(square), 0.0)


def shift_sum(field, dim, distance):
    size = field.shape[dim]
    spot = spot_iota(field.shape, dim)
    ahead = jnp.where(spot < size - distance, pltpu.roll(field, size - distance, dim), 0.0)
    behind = jnp.where(spot >= distance, pltpu.roll(field, distance, dim), 0.0)
    return ahead + behind


def plane_sums(plane):
    beside = shift_sum(plane, 1, 1)
    further = shift_sum(plane, 1, 2)
    return {
        0: plane,
        1: beside + shift_sum(plane, 0, 1),
        2: shift_sum(beside, 0, 1),
        4: further + shift_sum(plane, 0, 2),
        5: shift_sum(further, 0, 1) + shift_sum(beside, 0, 2),
        8: shift_sum(further, 0, 2),
    }


def weigh(sums, weight_ref, square):
    result = None
    for inner in PLANE_SQUARES:
        term = weight_ref[ALL_SQUARES.index(inner + square)] * sums[inner]
        result = term if result is None else result + term
    return result


def forward_planes(plane, weight_ref):
    sums = plane_sums(plane)
    return [weigh(sums, weight_ref, square) for square in (0, 1, 4)]


def rows(x, layers, shift=0):
    return pl.ds(x * layers + shift, layers)


GAP = 8


def gapped(x, layers, shift=0):
    return pl.ds(GAP + x * (layers + GAP) + shift, layers)


def gap(x, layers):
    return pl.ds(x * (layers + GAP), GAP)


def edge_class(x, planes):
    return jnp.minimum(x, 2) + jnp.maximum(x - (planes - 3), 0)


def zero_edges(ref):
    planes = ref.shape[0]
    for place in (0, 1, planes - 2, planes - 1):
        ref[place] = jnp.zeros(ref.shape[1:], ref.dtype)


def group_spots(group, blocks):
    chips, own_planes = blocks.shape[:2]
    mine = lax.axis_index("space")
    core = mine ^ mine >> 1 ^ group
    return [
        (own_planes * (2 * chip + ((core ^ chip) & 1)) + own, (chip, own))
        for chip in range(chips)
        for own in range(own_planes)
    ]


def spread_group(blocks, spread):
    chips, own_planes, layers, row_width = blocks.shape
    zero_gap = jnp.zeros((GAP, row_width), jnp.float32)
    for ref in spread:
        ref[gap(0, layers)] = zero_gap
    for p in range(chips * own_planes):
        plane = blocks[p // own_planes, p % own_planes]
        for ref, field in zip(spread, (plane, shift_sum(plane, 1, 1), shift_sum(plane, 1, 2))):
            ref[gapped(p, layers)] = field
            ref[gap(p + 1, layers)] = zero_gap


def filter_plane(p, layers, spread, weight_ref):
    def around(place, distance):
        ref = spread[place]
        return ref[gapped(p, layers, distance)] + ref[gapped(p, layers, -distance)]

    sums = {
        0: spread[0][gapped(p, layers)],
        1: spread[1][gapped(p, layers)] + around(0, 1),
        2: around(1, 1),
        4: spread[2][gapped(p, layers)] + around(0, 2),
        5: around(2, 1) + around(1, 2),
        8: around(2, 2),
    }
    return [weigh(sums, weight_ref, square) for square in (0, 1, 4)]


def prepare_kernel(
    radius_hbm,
    index_hbm,
    force_hbm,
    fixed_hbm,
    density_ref,
    weight_ref,
    inverse_ref,
    free_ref,
    load_ref,
    spot_ref,
    filter_ref,
    radius_ref,
    index_ref,
    force_ref,
    fixed_ref,
    plane_ref,
    beside_ref,
    further_ref,
    arrived,
):
    copies = [
        pltpu.make_async_copy(source, target, arrived.at[place])
        for place, (source, target) in enumerate(
            (
                (radius_hbm, radius_ref),
                (index_hbm, index_ref),
                (force_hbm, force_ref),
                (fixed_hbm, fixed_ref),
            )
        )
    ]
    for copy in copies:
        copy.start()
    spread = (plane_ref, beside_ref, further_ref)
    spread_group(density_ref, spread)
    for copy in copies:
        copy.wait()
    planes, layers, row_width = free_ref.shape
    load_place = lax.axis_index("space")
    shape = (layers, row_width)
    z = spot_iota(shape, 0)
    y = spot_iota(shape, 1)

    class_weights(radius_ref, weight_ref)
    own_planes = density_ref.shape[1]
    for p in range(density_ref.shape[0] * own_planes):
        for place, field in enumerate(filter_plane(p, layers, spread, weight_ref)):
            filter_ref[place, p // own_planes, p % own_planes] = field

    ones = forward_planes(jnp.ones(shape, jnp.float32), weight_ref)
    for place, (lower, upper) in enumerate(((0, 2), (1, 2), (2, 2), (2, 1), (2, 0))):
        inverse_ref[place] = 1.0 / (
            ones[0] + min(lower, 1) * ones[1] + min(upper, 1) * ones[1]
            + (lower // 2) * ones[2] + (upper // 2) * ones[2]
        )

    def free_plane(x, carry):
        free_ref[x] = jnp.where(
            z == 0, 1.0 - fixed_ref[pl.ds(x, 1), :].astype(jnp.float32), 1.0
        )
        return carry

    each_plane(planes, free_plane, 0)

    own_index = index_ref[load_place]
    own_z = own_index // row_width % layers
    own_y = own_index % row_width
    hit = (z == own_z) & (y == own_y)
    for part in range(3):
        load_ref[part] = jnp.where(hit, force_ref[part, load_place], 0.0)
    own_x = (own_index // (layers * row_width)).astype(jnp.float32)
    spot_ref[...] = jnp.full(spot_ref.shape, own_x)


def sweep_kernel(
    spot_ref,
    load_ref,
    weight_ref,
    inverse_ref,
    free_ref,
    filter_ref,
    density_ref,
    start_ref,
    disp_ref,
    coef_ref,
    plane_ref,
    beside_ref,
    further_ref,
    near_ref,
    side_ref,
    far_ref,
    modulus_ref,
    across_ref,
    up_ref,
    right_ref,
    left_ref,
    rate_ref,
    first_ref,
):
    planes, layers, row_width = coef_ref.shape
    shape = (layers, row_width)
    z = spot_iota(shape, 0)
    y = spot_iota(shape, 1)
    zero = jnp.zeros(shape, jnp.float32)

    for ref in (side_ref, far_ref):
        zero_edges(ref)
    results = (near_ref, side_ref, far_ref)
    other_ref = density_ref.at[1]
    for x, spot in group_spots(0, other_ref):
        for place, ref in enumerate(results):
            ref[x + 2] = filter_ref[(place,) + spot]
    spread = (plane_ref, beside_ref, further_ref)
    spread_group(other_ref, spread)
    for p, (x, spot) in enumerate(group_spots(1, other_ref)):
        for ref, field in zip(results, filter_plane(p, layers, spread, weight_ref)):
            ref[x + 2] = field

    for ref in (first_ref, disp_ref):
        for part in range(3):
            ref[part, rows(0, layers)] = zero
            ref[part, rows(planes + 1, layers)] = zero

    def store_faces(slot, modulus, above, later, before, free, start, views):
        across, up_view, right_view, left_view, rate, source = views
        across[slot] = later
        up = jnp.where(z < layers - 1, 0.5 * (modulus + above), 0.0)
        right = jnp.where(
            y < row_width - 1, 0.5 * (modulus + pltpu.roll(modulus, row_width - 1, 1)), 0.0
        )
        left = pltpu.roll(right, 1, 1)
        up_view[rows(slot, layers)] = up
        right_view[slot] = right
        left_view[slot] = left
        sums = (before + later, up + pltpu.roll(up, 1, 0), left + right)
        every = sums[0] + sums[1] + sums[2]
        diagonal = [every + part_sum for part_sum in sums]
        pair = diagonal[0] * diagonal[1]
        push = relax_factor * free / (pair * diagonal[2])
        side = push * diagonal[2]
        for part, factor in enumerate((side * diagonal[1], side * diagonal[0], push * pair)):
            rate[part, slot] = factor
            source[part, rows(slot, layers)] = start[part] * free

    piece = planes // 2

    def modulus_piece(first, carry):
        count = piece
        near = near_ref.at[pl.ds(first + 2, count)]
        side = side_ref.at[pl.ds(first + 1, count + 2)]
        far = far_ref.at[pl.ds(first, count + 4)]
        moduli = modulus_ref.at[pl.ds(first * layers, (count + 1) * layers)]
        coef = coef_ref.at[pl.ds(first, count)]
        free = free_ref.at[pl.ds(first, count)]
        views = (
            across_ref.at[pl.ds(first, count)],
            up_ref.at[pl.ds(first * layers, count * layers)],
            right_ref.at[pl.ds(first, count)],
            left_ref.at[pl.ds(first, count)],
            rate_ref.at[:, pl.ds(first, count)],
            first_ref.at[:, pl.ds(first * layers, count * layers)],
        )
        modulus, before = carry
        for p in range(count):
            inverse = inverse_ref[edge_class(first + p, planes)]
            filtered = near[p] + side[p] + side[p + 2] + far[p] + far[p + 4]
            filtered = filtered * inverse
            later = floor_modulus + (1.0 - floor_modulus) * (filtered * filtered * filtered)
            coef[p] = 3.0 * (1.0 - floor_modulus) * (filtered * filtered) * inverse
            moduli[rows(p + 1, layers)] = later
            ahead = 0.5 * (modulus + later)
            if p == 0:
                ahead = jnp.where(first > 0, ahead, 0.0)
            above = moduli[rows(p, layers, 1)] if p else pltpu.roll(modulus, layers - 1, 0)
            previous = jnp.maximum(first + p - 1, 0)
            store_faces(
                p,
                modulus,
                above,
                ahead,
                before,
                free_ref[previous],
                [start_ref[part, previous] for part in range(3)],
                views,
            )
            modulus, before = later, ahead
        return modulus, before

    modulus, before = each_chunk(planes, piece, modulus_piece, (jnp.ones(shape, jnp.float32), zero))
    store_faces(
        planes,
        modulus,
        pltpu.roll(modulus, layers - 1, 0),
        zero,
        before,
        free_ref[planes - 1],
        [start_ref[part, planes - 1] for part in range(3)],
        (across_ref, up_ref, right_ref, left_ref, rate_ref, first_ref),
    )

    own_x = jnp.max(spot_ref[...]).astype(jnp.int32)

    def sweep(source, target):
        def sweep_piece(first, carry):
            count = piece
            old = source.at[:, pl.ds(first * layers, (count + 2) * layers)]
            new = target.at[:, pl.ds((first + 1) * layers, count * layers)]
            across = across_ref.at[pl.ds(first, count + 1)]
            up = up_ref.at[pl.ds(first * layers, (count + 1) * layers)]
            right = right_ref.at[pl.ds(first + 1, count)]
            left = left_ref.at[pl.ds(first + 1, count)]
            rate = rate_ref.at[:, pl.ds(first + 1, count)]
            behind = [old[part, rows(0, layers)] for part in range(3)]
            here = [old[part, rows(1, layers)] for part in range(3)]
            for p in range(count):
                ahead = [old[part, rows(p + 2, layers)] for part in range(3)]
                for part in range(3):
                    pulls = [
                        across[p] * behind[part] + across[p + 1] * ahead[part],
                        up[rows(p + 1, layers)] * old[part, rows(p + 1, layers, 1)]
                        + up[rows(p + 1, layers, -1)] * old[part, rows(p + 1, layers, -1)],
                        right[p] * pltpu.roll(here[part], row_width - 1, 1)
                        + left[p] * pltpu.roll(here[part], 1, 1),
                    ]
                    pull = pulls[0] + pulls[1] + pulls[2] + pulls[part]
                    new[part, rows(p, layers)] = (
                        1.0 - relax_factor
                    ) * here[part] + rate[part, p] * pull
                behind, here = here, ahead
            return carry

        each_chunk(planes, piece, sweep_piece, 0)
        for part in range(3):
            target[part, rows(own_x + 1, layers)] += rate_ref[part, own_x + 1] * load_ref[part]

    def two_sweeps(turn, carry):
        sweep(first_ref, disp_ref)

        @pl.when(turn < SWEEPS // 2)
        def _():
            sweep(disp_ref, first_ref)

        return carry

    lax.fori_loop(0, SWEEPS // 2 + 1, two_sweeps, 0)


def filter_group(group, shares, weight_ref, near_ref, far_ref, result_ref):
    chips, own_planes, layers, row_width = result_ref.shape
    zero_gap = jnp.zeros((GAP, row_width), jnp.float32)
    mine = lax.axis_index("space")
    core = (mine ^ mine >> 1 ^ group) & 1
    count = shares[0].shape[0] - own_planes
    views = [
        [ref.at[pl.ds(own_planes * start, count)] for ref in shares] for start in (core, 1 - core)
    ]
    for ref in (near_ref, far_ref):
        ref[gap(0, layers)] = zero_gap
    for p in range(chips * own_planes):
        chip, own = p // own_planes, p % own_planes
        plane, beside, further = views[chip & 1]
        x = 2 * own_planes * chip + own + 2

        def around(ref, distance):
            return ref[x + distance] + ref[x - distance]

        sums = {
            0: plane[x],
            1: beside[x] + around(plane, 1),
            2: around(beside, 1),
            4: further[x] + around(plane, 2),
            5: around(further, 1) + around(beside, 2),
            8: around(further, 2),
        }
        level = weigh(sums, weight_ref, 0)
        for ref, square in ((near_ref, 1), (far_ref, 4)):
            ref[gapped(p, layers)] = weigh(sums, weight_ref, square)
            ref[gap(p + 1, layers)] = zero_gap
        result_ref[chip, own] = (
            level
            + near_ref[gapped(p, layers, 1)]
            + near_ref[gapped(p, layers, -1)]
            + far_ref[gapped(p, layers, 2)]
            + far_ref[gapped(p, layers, -2)]
        )


def share_kernel(
    disp_ref,
    coef_ref,
    weight_ref,
    sent_ref,
    plane_ref,
    beside_ref,
    further_ref,
    near_ref,
    far_ref,
):
    planes, layers, row_width = coef_ref.shape
    load_cases = lax.axis_size("space")
    shape = (layers, row_width)
    z = spot_iota(shape, 0)
    y = spot_iota(shape, 1)
    zero = jnp.zeros(shape, jnp.float32)
    shares = (plane_ref, beside_ref, further_ref)
    for ref in shares:
        zero_edges(ref)

    count = planes // 2

    def share_chunk(first, before):
        disp = disp_ref.at[:, pl.ds((first + 1) * layers, (count + 1) * layers)]
        coef = coef_ref.at[pl.ds(first, count)]
        plane, beside, further = (ref.at[pl.ds(first + 2, count)] for ref in shares)
        here = [disp[part, rows(0, layers)] for part in range(3)]
        for p in range(count):
            later = [disp[part, rows(p + 1, layers)] for part in range(3)]
            ahead, upward, right = zero, zero, zero
            for part in range(3):
                step = later[part] - here[part]
                climb = disp[part, rows(p, layers, 1)] - here[part]
                slide = pltpu.roll(here[part], row_width - 1, 1) - here[part]
                ahead = ahead + (2.0 if part == 0 else 1.0) * (step * step)
                upward = upward + (2.0 if part == 1 else 1.0) * (climb * climb)
                right = right + (2.0 if part == 2 else 1.0) * (slide * slide)
            if p == count - 1:
                ahead = jnp.where(first + count < planes, ahead, 0.0)
            upward = jnp.where(z < layers - 1, upward, 0.0)
            right = jnp.where(y < row_width - 1, right, 0.0)
            total = before + ahead + upward + pltpu.roll(upward, 1, 0)
            total = total + right + pltpu.roll(right, 1, 1)
            share = (0.5 / load_cases) * total * coef[p]
            plane[p] = share
            beside[p] = shift_sum(share, 1, 1)
            further[p] = shift_sum(share, 1, 2)
            before, here = ahead, later
        return before

    each_chunk(planes, count, share_chunk, zero)
    filter_group(1, shares, weight_ref, near_ref, far_ref, sent_ref)


def kept_kernel(
    disp_ref,
    weight_ref,
    plane_ref,
    beside_ref,
    further_ref,
    disp_hbm,
    kept_ref,
    near_ref,
    far_ref,
    stored,
):
    layers = kept_ref.shape[2]
    inner = pl.ds(layers, disp_ref.shape[1] - 2 * layers)
    store = pltpu.make_async_copy(disp_ref.at[:, inner], disp_hbm, stored)
    store.start()
    shares = (plane_ref, beside_ref, further_ref)
    filter_group(0, shares, weight_ref, near_ref, far_ref, kept_ref)
    store.wait()


def design_kernel(root_ref, density_ref, new_ref, pull_ref, low_ref, high_ref):
    groups, chips, own_planes, layers, row_width = density_ref.shape
    own_chip = lax.axis_index("space") >> 1
    shape = (layers, row_width)
    zero = jnp.zeros(shape, jnp.float32)
    planes = [
        (group, chip, own)
        for group in range(groups)
        for chip in range(chips)
        for own in range(own_planes)
    ]
    for spot in planes:
        density = density_ref[spot]
        pull_ref[spot] = density * root_ref[spot]
        low_ref[spot] = jnp.maximum(density - move_limit, density_floor)
        high_ref[spot] = jnp.minimum(density + move_limit, 1.0)

    target = volume_share * len(planes) * layers * row_width

    def factor_of(log_level):
        return jnp.broadcast_to(jnp.exp(-0.5 * log_level), shape)

    def exceeds(total):
        return jnp.sum(jnp.sum(total, axis=0, keepdims=True), axis=1, keepdims=True) > target

    def halve_twice(step, state):
        lower, span = state
        half, quarter = span * 0.5, span * 0.25
        middles = (lower + quarter, lower + half, lower + half + quarter)
        factors = [factor_of(middle) for middle in middles]
        totals = [zero, zero, zero]
        for spot in planes:
            pull, low, high = pull_ref[spot], low_ref[spot], high_ref[spot]
            totals = [
                total + jnp.minimum(jnp.maximum(pull * factor, low), high)
                for total, factor in zip(totals, factors)
            ]
        first, second, third = (exceeds(total) for total in totals)
        upper = jnp.where(third, middles[2], middles[1])
        below = jnp.where(first, middles[0], lower)
        return jnp.where(second, upper, below), quarter

    start = (jnp.full((1, 1), log_lower, jnp.float32), jnp.full((1, 1), log_span, jnp.float32))
    lower, span = lax.fori_loop(0, SEARCH // 2, halve_twice, start)
    factor = factor_of(lower + 0.5 * span)
    for own in range(own_planes):
        spot = (0, own_chip, own)
        new_ref[own] = jnp.minimum(
            jnp.maximum(pull_ref[spot] * factor, low_ref[spot]), high_ref[spot]
        )


def in_vmem():
    return pl.BlockSpec(memory_space=pltpu.VMEM)


KERNEL_VMEM = 24 * 2**20


def floats(*shape):
    return jax.ShapeDtypeStruct(shape, jnp.float32)


def prepare_call(density, radius, load_index, load_force, fixed):
    chips, own_planes, layers, row_width = density.shape
    planes = fixed.shape[0]
    spread = pltpu.VMEM((chips * own_planes * (layers + GAP) + GAP, row_width), jnp.float32)
    return pl.pallas_call(
        prepare_kernel,
        out_shape=[
            floats(len(ALL_SQUARES), layers, row_width),
            floats(2 * window_reach + 1, layers, row_width),
            floats(planes, layers, row_width),
            floats(3, layers, row_width),
            floats(8, row_width),
            floats(3, *density.shape),
        ],
        in_specs=[pl.BlockSpec(memory_space=pltpu.HBM)] * 4 + [in_vmem()],
        out_specs=[in_vmem()] * 6,
        scratch_shapes=[
            pltpu.SMEM(radius.shape, radius.dtype),
            pltpu.SMEM(load_index.shape, load_index.dtype),
            pltpu.SMEM(load_force.shape, load_force.dtype),
            pltpu.VMEM(fixed.shape, fixed.dtype),
            spread,
            spread,
            spread,
            pltpu.SemaphoreType.DMA((4,)),
        ],
        compiler_params=pltpu.CompilerParams(vmem_limit_bytes=KERNEL_VMEM),
        cost_estimate=pl.CostEstimate(
            flops=80 * planes * layers * row_width,
            bytes_accessed=8 * planes * layers * row_width,
            transcendentals=0,
        ),
        name="prepare",
    )(
        *(
            pltpu.with_memory_space_constraint(array, pltpu.HBM)
            for array in (radius, load_index, load_force, fixed)
        ),
        density,
    )


def sweep_call(spot, load, weights, inverses, free, filtered, density, displacement):
    groups, chips, own_planes, layers, row_width = density.shape
    planes = groups * chips * own_planes

    def scratch(*lead):
        return pltpu.VMEM(lead + (row_width,), jnp.float32)

    return pl.pallas_call(
        sweep_kernel,
        out_shape=[
            floats(3, (planes + 2) * layers, row_width),
            floats(planes, layers, row_width),
        ],
        in_specs=[in_vmem()] * 8,
        out_specs=[in_vmem()] * 2,
        scratch_shapes=[
            scratch(planes // 2 * (layers + GAP) + GAP),
            scratch(planes // 2 * (layers + GAP) + GAP),
            scratch(planes // 2 * (layers + GAP) + GAP),
            scratch(planes + 4, layers),
            scratch(planes + 4, layers),
            scratch(planes + 4, layers),
            scratch((planes + 1) * layers),
            scratch(planes + 1, layers),
            scratch((planes + 1) * layers),
            scratch(planes + 1, layers),
            scratch(planes + 1, layers),
            scratch(3, planes + 1, layers),
            scratch(3, (planes + 2) * layers),
        ],
        compiler_params=pltpu.CompilerParams(vmem_limit_bytes=KERNEL_VMEM),
        name="sweeps",
    )(spot, load, weights, inverses, free, filtered, density, displacement)


def share_call(disp, coef, weights, group_shape):
    planes, layers, row_width = coef.shape
    gaps = pltpu.VMEM((planes // 2 * (layers + GAP) + GAP, row_width), jnp.float32)
    return pl.pallas_call(
        share_kernel,
        out_shape=[floats(*group_shape)] + [floats(planes + 4, layers, row_width)] * 3,
        in_specs=[in_vmem()] * 3,
        out_specs=[in_vmem()] * 4,
        scratch_shapes=[gaps, gaps],
        compiler_params=pltpu.CompilerParams(vmem_limit_bytes=KERNEL_VMEM),
        name="share",
    )(disp, coef, weights)


def kept_call(disp, weights, shares, group_shape):
    parts, disp_rows, row_width = disp.shape
    chips, own_planes, layers = group_shape[:3]
    gaps = pltpu.VMEM((chips * own_planes * (layers + GAP) + GAP, row_width), jnp.float32)
    return pl.pallas_call(
        kept_kernel,
        out_shape=[floats(parts, disp_rows - 2 * layers, row_width), floats(*group_shape)],
        in_specs=[in_vmem()] * 5,
        out_specs=[pl.BlockSpec(memory_space=pltpu.HBM), in_vmem()],
        scratch_shapes=[gaps, gaps, pltpu.SemaphoreType.DMA(())],
        compiler_params=pltpu.CompilerParams(vmem_limit_bytes=KERNEL_VMEM),
        cost_estimate=pl.CostEstimate(
            flops=20 * disp.size, bytes_accessed=8 * disp.size, transcendentals=0
        ),
        name="kept",
    )(disp, weights, *shares)


def design_call(root, density):
    return pl.pallas_call(
        design_kernel,
        out_shape=floats(*density.shape[2:]),
        in_specs=[in_vmem()] * 2,
        out_specs=in_vmem(),
        scratch_shapes=[pltpu.VMEM(density.shape, jnp.float32)] * 3,
        compiler_params=pltpu.CompilerParams(vmem_limit_bytes=KERNEL_VMEM),
        name="design",
    )(root, density)


def other_core(block):
    devices = lax.axis_size("space")
    return lax.ppermute(block, "space", [(i, i ^ 1) for i in range(devices)])


def chip_groups():
    chips = lax.axis_size("space") // 2
    return [[2 * chip + (chip ^ group) % 2 for chip in range(chips)] for group in range(2)]


def between_chips(pieces):
    return lax.all_to_all(pieces, "space", 0, 0, axis_index_groups=chip_groups())


def chip_gathered(block):
    chips = lax.axis_size("space") // 2
    return between_chips(jnp.broadcast_to(block[None], (chips,) + block.shape))


def with_other_core(blocks):
    return jnp.stack([blocks, other_core(blocks)])


def scattered_sum(sent, make_kept):
    received = other_core(sent)
    *others, kept = make_kept()
    return jnp.sum(between_chips(kept + received), axis=0), others


def one_slab(density, displacement, fixed, load_index, load_force, radius):
    same_group, small = lax.optimization_barrier(
        (chip_gathered(density), (radius, load_index, load_force.T, fixed))
    )
    other_group = other_core(same_group)
    weights, inverses, free, load, spot, filtered = prepare_call(same_group, *small)
    whole = jnp.stack([same_group, other_group])
    disp, coef = sweep_call(
        spot, load, weights, inverses, free, filtered, whole, displacement[0]
    )
    sent, *shares = share_call(disp, coef, weights, same_group.shape)
    sent, disp, shares = lax.optimization_barrier((sent, disp, shares))
    squares, (new_displacement,) = scattered_sum(
        sent, lambda: kept_call(disp, weights, shares, same_group.shape)
    )
    root = with_other_core(chip_gathered(jnp.sqrt(squares)))
    new_density = design_call(root, whole)
    return new_density, new_displacement.reshape(displacement.shape)


def from_behind(block, axis, distance):
    devices = range(lax.axis_size(axis))
    route = [(i - distance, i) for i in devices if i - distance in devices]
    return lax.ppermute(block, axis, route)


def extended(x, sides, width):
    for axis, dim in sides:
        size, length = (lax.axis_size(axis), x.shape[dim])
        up = [(i, (i + 1) % size) for i in range(size - 1)]
        down = [(j, i) for i, j in up]
        last = lax.slice_in_dim(x, length - width, length, axis=dim)
        first = lax.slice_in_dim(x, 0, width, axis=dim)
        before = lax.ppermute(last, axis, up)
        after = lax.ppermute(first, axis, down)
        x = jnp.concatenate([before, x, after], axis=dim)
    return x


def from_partner(x, axis, bit):
    return lax.ppermute(x, axis, [(i, i ^ 1 << bit) for i in range(lax.axis_size(axis))])


def window_offsets():
    offsets_list = []
    for across in range(-window_reach, window_reach + 1):
        for upward in range(-window_reach, window_reach + 1):
            for sideways in range(-window_reach, window_reach + 1):
                length = math.sqrt(across * across + upward * upward + sideways * sideways)
                offsets_list.append((across, upward, sideways, length))
    return offsets_list


def layer_weights(radius):
    radial = radius.astype(jnp.float32)
    return jnp.stack(
        [jnp.maximum(radial - length, 0.0) for across, upward, sideways, length in window_offsets()]
    )


def pad_axis(grid_field, along_axis, before, after_cells):
    widths = [(0, 0)] * grid_field.ndim
    widths[along_axis] = (before, after_cells)
    return jnp.pad(grid_field, widths)


def pad_sides(grid_field):
    return jnp.pad(grid_field, ((0, 0), (window_reach, window_reach), (window_reach, window_reach)))


def filter_forward(padded, weights):
    out_rows = padded.shape[0] - 2 * window_reach
    layers = padded.shape[1] - 2 * window_reach
    row_width = padded.shape[2] - 2 * window_reach
    result = jnp.zeros((out_rows, layers, row_width), jnp.float32)
    for offset_index, (across, upward, sideways, length) in enumerate(window_offsets()):
        shifted = padded[
            window_reach + across : window_reach + across + out_rows,
            window_reach + upward : window_reach + upward + layers,
            window_reach + sideways : window_reach + sideways + row_width,
        ]
        result = result + weights[offset_index][None, :, None] * shifted
    return result


def filter_backward(padded, padded_weights):
    out_rows = padded.shape[0] - 2 * window_reach
    layers = padded.shape[1] - 2 * window_reach
    row_width = padded.shape[2] - 2 * window_reach
    result = jnp.zeros((out_rows, layers, row_width), jnp.float32)
    for offset_index, (across, upward, sideways, length) in enumerate(window_offsets()):
        shifted = padded[
            window_reach - across : window_reach - across + out_rows,
            window_reach - upward : window_reach - upward + layers,
            window_reach - sideways : window_reach - sideways + row_width,
        ]
        layer_part = padded_weights[
            offset_index, window_reach - upward : window_reach - upward + layers
        ]
        result = result + layer_part[None, :, None] * shifted
    return result


def stiff_factors(direction):
    return jnp.array(
        [2.0 if component == direction else 1.0 for component in range(3)], jnp.float32
    ).reshape(3, 1, 1, 1)


def relax_slab(padded, displace, face_x, face_z, face_y, force_field, free_cells, diagonal):
    flux_x = stiff_factors(0) * face_x * jnp.diff(padded, axis=1)
    stencil_image = flux_x[:, :-1] - flux_x[:, 1:]
    flux_z = stiff_factors(1) * face_z * jnp.diff(displace, axis=2)
    stencil_image = stencil_image + pad_axis(flux_z, 2, 1, 0) - pad_axis(flux_z, 2, 0, 1)
    flux_y = stiff_factors(2) * face_y * jnp.diff(displace, axis=3)
    stencil_image = stencil_image + pad_axis(flux_y, 3, 1, 0) - pad_axis(flux_y, 3, 0, 1)
    return free_cells * (displace + relax_factor * (force_field - stencil_image) / diagonal)


def slab_energy(grid_field, along_axis, direction, load_cases):
    change = jnp.diff(grid_field, axis=along_axis)
    return jnp.sum(stiff_factors(direction) * change * change, axis=0) / load_cases


def neighbour_planes(displace, load_cases, axis_devices):
    if axis_devices > load_cases:
        below = from_behind(displace[:, -1:], "space", load_cases)
        above = from_behind(displace[:, :1], "space", -load_cases)
    else:
        below = jnp.zeros_like(displace[:, :1])
        above = jnp.zeros_like(displace[:, :1])
    return jnp.concatenate([below, displace, above], axis=1)


def many_slabs(density, displacement, fixed, load_index, load_force, radius):
    slab_rows, layers, row_width = density.shape
    load_cases = load_index.shape[0]
    level_count = load_cases.bit_length() - 1
    axis_devices = lax.axis_size("space")
    axis_place = lax.axis_index("space")
    slab_planes = slab_rows * load_cases
    slab_place = axis_place // load_cases
    load_place = axis_place % load_cases
    total_rows = slab_rows * axis_devices
    weights = layer_weights(radius)
    padded_weights = pad_axis(weights, 1, window_reach, window_reach)
    global_rows = (
        jnp.arange(slab_rows + 2 * window_reach, dtype=jnp.int32)
        + axis_place * slab_rows
        - window_reach
    )
    deep_inside = ((global_rows >= 0) & (global_rows < total_rows)).astype(jnp.float32)
    inside_field = deep_inside[:, None, None] * pad_sides(
        jnp.ones((slab_rows + 2 * window_reach, layers, row_width), jnp.float32)
    )
    total_weight = filter_forward(inside_field, weights)
    slab_start = slab_place * slab_planes
    margin_rows = jnp.arange(slab_planes + 2, dtype=jnp.int32) + slab_start - 1
    margin_inside = ((margin_rows >= 0) & (margin_rows < total_rows)).astype(jnp.float32)
    face_valid = margin_inside[1:] * margin_inside[:-1]
    fixed_slab = lax.dynamic_slice_in_dim(fixed, slab_start, slab_planes, 0).astype(jnp.float32)
    bottom_layer = (jnp.arange(layers, dtype=jnp.int32) == 0).astype(jnp.float32)
    free_cells = 1.0 - bottom_layer[None, :, None] * fixed_slab[:, None, :]
    slab_cells = slab_planes * layers * row_width
    cell_index = jnp.arange(slab_cells, dtype=jnp.int32) + slab_place * slab_cells
    load_hot = jnp.arange(load_cases, dtype=jnp.int32) == load_place
    own_index = jnp.sum(jnp.where(load_hot, load_index, 0))
    own_force = jnp.sum(load_hot.astype(jnp.float32)[:, None] * load_force, axis=0)
    load_hits = (cell_index == own_index).astype(jnp.float32)
    force_field = (own_force[:, None] * load_hits[None, :]).reshape(
        3, slab_planes, layers, row_width
    )
    displace = displacement[0] * free_cells
    target = volume_share * total_rows * layers * row_width
    padded = neighbour_planes(displace, load_cases, axis_devices)
    halo_density = extended(density, (("space", 0),), window_reach)
    filtered = filter_forward(pad_sides(halo_density), weights) / total_weight
    whole_field = lax.all_gather(filtered, "space", axis=0, tiled=True)
    margin = lax.dynamic_slice_in_dim(
        pad_axis(whole_field, 0, 1, 1), slab_start, slab_planes + 2, 0
    )
    moduli = floor_modulus + (1.0 - floor_modulus) * margin**3
    face_x = 0.5 * (moduli[1:] + moduli[:-1]) * face_valid[:, None, None]
    inner_moduli = moduli[1:-1]
    face_z = 0.5 * (inner_moduli[:, 1:] + inner_moduli[:, :-1])
    face_y = 0.5 * (inner_moduli[:, :, 1:] + inner_moduli[:, :, :-1])
    sum_x = face_x[:-1] + face_x[1:]
    sum_z = pad_axis(face_z, 1, 1, 0) + pad_axis(face_z, 1, 0, 1)
    sum_y = pad_axis(face_y, 2, 1, 0) + pad_axis(face_y, 2, 0, 1)
    diagonal = stiff_factors(0) * sum_x + stiff_factors(1) * sum_z + stiff_factors(2) * sum_y
    for sweep_index in range(SWEEPS):
        displace = relax_slab(
            padded, displace, face_x, face_z, face_y, force_field, free_cells, diagonal
        )
        padded = neighbour_planes(displace, load_cases, axis_devices)
    energy_x = slab_energy(padded, 1, 0, load_cases) * face_valid[:, None, None]
    energy_z = slab_energy(displace, 2, 1, load_cases)
    energy_y = slab_energy(displace, 3, 2, load_cases)
    sens_term = 0.5 * (
        energy_x[:-1]
        + energy_x[1:]
        + pad_axis(energy_z, 1, 1, 0)
        + pad_axis(energy_z, 1, 0, 1)
        + pad_axis(energy_y, 2, 1, 0)
        + pad_axis(energy_y, 2, 0, 1)
    )
    sensitive = sens_term
    for level in reversed(range(level_count)):
        half_rows = sensitive.shape[0] // 2
        upper_side = load_place // 2**level % 2 == 1
        outgoing = jnp.where(upper_side, sensitive[:half_rows], sensitive[half_rows:])
        keeping = jnp.where(upper_side, sensitive[half_rows:], sensitive[:half_rows])
        sensitive = keeping + from_partner(outgoing, "space", level)
    weighted_share = 3.0 * (1.0 - floor_modulus) * filtered**2 * sensitive / total_weight
    halo_share = extended(weighted_share, (("space", 0),), window_reach)
    root_term = jnp.sqrt(filter_backward(pad_sides(halo_share), padded_weights))
    lowest = jnp.maximum(density - move_limit, density_floor)
    highest = jnp.minimum(density + move_limit, 1.0)
    design_now = density

    def trial_design(log_level):
        return jnp.clip(design_now * root_term * jnp.exp(-0.5 * log_level), lowest, highest)

    start_state = (jnp.asarray(log_lower, jnp.float32), jnp.asarray(log_span, jnp.float32))

    def halve(search_step, search_state):
        lower_end, span_width = search_state
        half_span = span_width * 0.5
        middle = lower_end + half_span
        volume_total = lax.psum(jnp.sum(trial_design(middle)), "space")
        return (jnp.where(volume_total > target, middle, lower_end), half_span)

    lower_end, span_width = lax.fori_loop(0, SEARCH, halve, start_state)
    density = trial_design(lower_end + 0.5 * span_width)
    new_displacement = displace[None]
    return (density, new_displacement)


def solution(mesh):
    in_specs = (
        P("space", "parts", None),
        P("space", None, None, "parts", None),
        P(None, "parts"),
        P("parts"),
        P("parts", None),
        P("parts"),
    )
    out_specs = (P("space", "parts", None), P("space", None, None, "parts", None))

    def local(density, displacement, fixed, load_index, load_force, radius):
        alone = lax.axis_size("space") == load_index.shape[0]
        run = one_slab if alone else many_slabs
        return run(density, displacement, fixed, load_index, load_force, radius)

    return jax.shard_map(local, mesh=mesh, in_specs=in_specs, out_specs=out_specs, check_vma=False)
```

```python
import math

import jax
import jax.numpy as jnp
from jax import lax
from jax.experimental import pallas as pl
from jax.experimental.pallas import tpu as pltpu
from jax.sharding import PartitionSpec as P

SWEEPS = 3
SEARCH = 12


floor_modulus = 0.05
relax_factor = 0.6
move_limit = 0.2
density_floor = 0.01
volume_share = 0.5
log_lower = -16.0
log_span = 32.0
window_reach = 2

PLANE_SQUARES = (0, 1, 2, 4, 5, 8)
ALL_SQUARES = (0, 1, 2, 3, 4, 5, 6, 8, 9, 12)


def spot_iota(shape, dim):
    return lax.broadcasted_iota(jnp.int32, shape, dim)


def each_plane(planes, body, carry):
    for x in range(planes):
        carry = body(x, carry)
    return carry


def each_chunk(planes, count, body, carry):
    return lax.fori_loop(0, planes // count, lambda i, carry: body(i * count, carry), carry)


def layer_radius(radius_ref, layers, row_width):
    z = spot_iota((layers, row_width), 0)
    result = jnp.zeros((layers, row_width), jnp.int32)
    for layer in range(layers):
        result = jnp.where(z == layer, radius_ref[layer], result)
    return result.astype(jnp.float32)


def class_weights(radius_ref, weight_ref):
    layers, row_width = weight_ref.shape[1:]
    radial = layer_radius(radius_ref, layers, row_width)
    for place, square in enumerate(ALL_SQUARES):
        weight_ref[place] = jnp.maximum(radial - math.sqrt(square), 0.0)


def shift_sum(field, dim, distance):
    size = field.shape[dim]
    spot = spot_iota(field.shape, dim)
    ahead = jnp.where(spot < size - distance, pltpu.roll(field, size - distance, dim), 0.0)
    behind = jnp.where(spot >= distance, pltpu.roll(field, distance, dim), 0.0)
    return ahead + behind


def plane_sums(plane):
    beside = shift_sum(plane, 1, 1)
    further = shift_sum(plane, 1, 2)
    return {
        0: plane,
        1: beside + shift_sum(plane, 0, 1),
        2: shift_sum(beside, 0, 1),
        4: further + shift_sum(plane, 0, 2),
        5: shift_sum(further, 0, 1) + shift_sum(beside, 0, 2),
        8: shift_sum(further, 0, 2),
    }


def weigh(sums, weight_ref, square):
    result = None
    for inner in PLANE_SQUARES:
        term = weight_ref[ALL_SQUARES.index(inner + square)] * sums[inner]
        result = term if result is None else result + term
    return result


def forward_planes(plane, weight_ref):
    sums = plane_sums(plane)
    return [weigh(sums, weight_ref, square) for square in (0, 1, 4)]


def rows(x, layers, shift=0):
    return pl.ds(x * layers + shift, layers)


GAP = 8


def gapped(x, layers, shift=0):
    return pl.ds(GAP + x * (layers + GAP) + shift, layers)


def gap(x, layers):
    return pl.ds(x * (layers + GAP), GAP)


def edge_class(x, planes):
    return jnp.minimum(x, 2) + jnp.maximum(x - (planes - 3), 0)


def zero_edges(ref):
    planes = ref.shape[0]
    for place in (0, 1, planes - 2, planes - 1):
        ref[place] = jnp.zeros(ref.shape[1:], ref.dtype)


def group_spots(group, blocks):
    chips, own_planes = blocks.shape[:2]
    mine = lax.axis_index("space")
    core = mine ^ mine >> 1 ^ group
    return [
        (own_planes * (2 * chip + ((core ^ chip) & 1)) + own, (chip, own))
        for chip in range(chips)
        for own in range(own_planes)
    ]


def spread_group(blocks, spread):
    chips, own_planes, layers, row_width = blocks.shape
    zero_gap = jnp.zeros((GAP, row_width), jnp.float32)
    for ref in spread:
        ref[gap(0, layers)] = zero_gap
    for p in range(chips * own_planes):
        plane = blocks[p // own_planes, p % own_planes]
        for ref, field in zip(spread, (plane, shift_sum(plane, 1, 1), shift_sum(plane, 1, 2))):
            ref[gapped(p, layers)] = field
            ref[gap(p + 1, layers)] = zero_gap


def filter_plane(p, layers, spread, weight_ref):
    def around(place, distance):
        ref = spread[place]
        return ref[gapped(p, layers, distance)] + ref[gapped(p, layers, -distance)]

    sums = {
        0: spread[0][gapped(p, layers)],
        1: spread[1][gapped(p, layers)] + around(0, 1),
        2: around(1, 1),
        4: spread[2][gapped(p, layers)] + around(0, 2),
        5: around(2, 1) + around(1, 2),
        8: around(2, 2),
    }
    return [weigh(sums, weight_ref, square) for square in (0, 1, 4)]


def prepare_kernel(
    radius_hbm,
    index_hbm,
    force_hbm,
    fixed_hbm,
    density_ref,
    weight_ref,
    inverse_ref,
    free_ref,
    load_ref,
    spot_ref,
    filter_ref,
    radius_ref,
    index_ref,
    force_ref,
    fixed_ref,
    plane_ref,
    beside_ref,
    further_ref,
    arrived,
):
    copies = [
        pltpu.make_async_copy(source, target, arrived.at[place])
        for place, (source, target) in enumerate(
            (
                (radius_hbm, radius_ref),
                (index_hbm, index_ref),
                (force_hbm, force_ref),
                (fixed_hbm, fixed_ref),
            )
        )
    ]
    for copy in copies:
        copy.start()
    spread = (plane_ref, beside_ref, further_ref)
    spread_group(density_ref, spread)
    for copy in copies:
        copy.wait()
    planes, layers, row_width = free_ref.shape
    load_place = lax.axis_index("space")
    shape = (layers, row_width)
    z = spot_iota(shape, 0)
    y = spot_iota(shape, 1)

    class_weights(radius_ref, weight_ref)
    own_planes = density_ref.shape[1]
    for p in range(density_ref.shape[0] * own_planes):
        for place, field in enumerate(filter_plane(p, layers, spread, weight_ref)):
            filter_ref[place, p // own_planes, p % own_planes] = field

    ones = forward_planes(jnp.ones(shape, jnp.float32), weight_ref)
    for place, (lower, upper) in enumerate(((0, 2), (1, 2), (2, 2), (2, 1), (2, 0))):
        inverse_ref[place] = 1.0 / (
            ones[0] + min(lower, 1) * ones[1] + min(upper, 1) * ones[1]
            + (lower // 2) * ones[2] + (upper // 2) * ones[2]
        )

    def free_plane(x, carry):
        free_ref[x] = jnp.where(
            z == 0, 1.0 - fixed_ref[pl.ds(x, 1), :].astype(jnp.float32), 1.0
        )
        return carry

    each_plane(planes, free_plane, 0)

    own_index = index_ref[load_place]
    own_z = own_index // row_width % layers
    own_y = own_index % row_width
    hit = (z == own_z) & (y == own_y)
    for part in range(3):
        load_ref[part] = jnp.where(hit, force_ref[part, load_place], 0.0)
    own_x = (own_index // (layers * row_width)).astype(jnp.float32)
    spot_ref[...] = jnp.full(spot_ref.shape, own_x)


def sweep_kernel(
    spot_ref,
    load_ref,
    weight_ref,
    inverse_ref,
    free_ref,
    filter_ref,
    density_ref,
    start_ref,
    disp_ref,
    coef_ref,
    plane_ref,
    beside_ref,
    further_ref,
    near_ref,
    side_ref,
    far_ref,
    modulus_ref,
    across_ref,
    up_ref,
    right_ref,
    left_ref,
    rate_ref,
    first_ref,
):
    planes, layers, row_width = coef_ref.shape
    shape = (layers, row_width)
    z = spot_iota(shape, 0)
    y = spot_iota(shape, 1)
    zero = jnp.zeros(shape, jnp.float32)

    for ref in (side_ref, far_ref):
        zero_edges(ref)
    results = (near_ref, side_ref, far_ref)
    other_ref = density_ref.at[1]
    for x, spot in group_spots(0, other_ref):
        for place, ref in enumerate(results):
            ref[x + 2] = filter_ref[(place,) + spot]
    spread = (plane_ref, beside_ref, further_ref)
    spread_group(other_ref, spread)
    for p, (x, spot) in enumerate(group_spots(1, other_ref)):
        for ref, field in zip(results, filter_plane(p, layers, spread, weight_ref)):
            ref[x + 2] = field

    for ref in (first_ref, disp_ref):
        for part in range(3):
            ref[part, rows(0, layers)] = zero
            ref[part, rows(planes + 1, layers)] = zero

    def store_faces(slot, modulus, above, later, before, free, start, views):
        across, up_view, right_view, left_view, rate, source = views
        across[slot] = later
        up = jnp.where(z < layers - 1, 0.5 * (modulus + above), 0.0)
        right = jnp.where(
            y < row_width - 1, 0.5 * (modulus + pltpu.roll(modulus, row_width - 1, 1)), 0.0
        )
        left = pltpu.roll(right, 1, 1)
        up_view[rows(slot, layers)] = up
        right_view[slot] = right
        left_view[slot] = left
        sums = (before + later, up + pltpu.roll(up, 1, 0), left + right)
        every = sums[0] + sums[1] + sums[2]
        diagonal = [every + part_sum for part_sum in sums]
        pair = diagonal[0] * diagonal[1]
        push = relax_factor * free / (pair * diagonal[2])
        side = push * diagonal[2]
        for part, factor in enumerate((side * diagonal[1], side * diagonal[0], push * pair)):
            rate[part, slot] = factor
            source[part, rows(slot, layers)] = start[part] * free

    piece = planes // 2

    def modulus_piece(first, carry):
        count = piece
        near = near_ref.at[pl.ds(first + 2, count)]
        side = side_ref.at[pl.ds(first + 1, count + 2)]
        far = far_ref.at[pl.ds(first, count + 4)]
        moduli = modulus_ref.at[pl.ds(first * layers, (count + 1) * layers)]
        coef = coef_ref.at[pl.ds(first, count)]
        free = free_ref.at[pl.ds(first, count)]
        views = (
            across_ref.at[pl.ds(first, count)],
            up_ref.at[pl.ds(first * layers, count * layers)],
            right_ref.at[pl.ds(first, count)],
            left_ref.at[pl.ds(first, count)],
            rate_ref.at[:, pl.ds(first, count)],
            first_ref.at[:, pl.ds(first * layers, count * layers)],
        )
        modulus, before = carry
        for p in range(count):
            inverse = inverse_ref[edge_class(first + p, planes)]
            filtered = near[p] + side[p] + side[p + 2] + far[p] + far[p + 4]
            filtered = filtered * inverse
            later = floor_modulus + (1.0 - floor_modulus) * (filtered * filtered * filtered)
            coef[p] = 3.0 * (1.0 - floor_modulus) * (filtered * filtered) * inverse
            moduli[rows(p + 1, layers)] = later
            ahead = 0.5 * (modulus + later)
            if p == 0:
                ahead = jnp.where(first > 0, ahead, 0.0)
            above = moduli[rows(p, layers, 1)] if p else pltpu.roll(modulus, layers - 1, 0)
            previous = jnp.maximum(first + p - 1, 0)
            store_faces(
                p,
                modulus,
                above,
                ahead,
                before,
                free_ref[previous],
                [start_ref[part, previous] for part in range(3)],
                views,
            )
            modulus, before = later, ahead
        return modulus, before

    modulus, before = each_chunk(planes, piece, modulus_piece, (jnp.ones(shape, jnp.float32), zero))
    store_faces(
        planes,
        modulus,
        pltpu.roll(modulus, layers - 1, 0),
        zero,
        before,
        free_ref[planes - 1],
        [start_ref[part, planes - 1] for part in range(3)],
        (across_ref, up_ref, right_ref, left_ref, rate_ref, first_ref),
    )

    own_x = jnp.max(spot_ref[...]).astype(jnp.int32)

    def sweep(source, target):
        def sweep_piece(first, carry):
            count = planes
            old = source.at[:, pl.ds(first * layers, (count + 2) * layers)]
            new = target.at[:, pl.ds((first + 1) * layers, count * layers)]
            across = across_ref.at[pl.ds(first, count + 1)]
            up = up_ref.at[pl.ds(first * layers, (count + 1) * layers)]
            right = right_ref.at[pl.ds(first + 1, count)]
            left = left_ref.at[pl.ds(first + 1, count)]
            rate = rate_ref.at[:, pl.ds(first + 1, count)]
            behind = [old[part, rows(0, layers)] for part in range(3)]
            here = [old[part, rows(1, layers)] for part in range(3)]
            for p in range(count):
                ahead = [old[part, rows(p + 2, layers)] for part in range(3)]
                for part in range(3):
                    pulls = [
                        across[p] * behind[part] + across[p + 1] * ahead[part],
                        up[rows(p + 1, layers)] * old[part, rows(p + 1, layers, 1)]
                        + up[rows(p + 1, layers, -1)] * old[part, rows(p + 1, layers, -1)],
                        right[p] * pltpu.roll(here[part], row_width - 1, 1)
                        + left[p] * pltpu.roll(here[part], 1, 1),
                    ]
                    pull = pulls[0] + pulls[1] + pulls[2] + pulls[part]
                    new[part, rows(p, layers)] = (
                        1.0 - relax_factor
                    ) * here[part] + rate[part, p] * pull
                behind, here = here, ahead
            return carry

        sweep_piece(0, 0)
        for part in range(3):
            target[part, rows(own_x + 1, layers)] += rate_ref[part, own_x + 1] * load_ref[part]

    def two_sweeps(turn, carry):
        sweep(first_ref, disp_ref)

        @pl.when(turn < SWEEPS // 2)
        def _():
            sweep(disp_ref, first_ref)

        return carry

    lax.fori_loop(0, SWEEPS // 2 + 1, two_sweeps, 0)


def filter_group(group, shares, weight_ref, near_ref, far_ref, result_ref):
    chips, own_planes, layers, row_width = result_ref.shape
    zero_gap = jnp.zeros((GAP, row_width), jnp.float32)
    mine = lax.axis_index("space")
    core = (mine ^ mine >> 1 ^ group) & 1
    count = shares[0].shape[0] - own_planes
    views = [
        [ref.at[pl.ds(own_planes * start, count)] for ref in shares] for start in (core, 1 - core)
    ]
    for ref in (near_ref, far_ref):
        ref[gap(0, layers)] = zero_gap
    for p in range(chips * own_planes):
        chip, own = p // own_planes, p % own_planes
        plane, beside, further = views[chip & 1]
        x = 2 * own_planes * chip + own + 2

        def around(ref, distance):
            return ref[x + distance] + ref[x - distance]

        sums = {
            0: plane[x],
            1: beside[x] + around(plane, 1),
            2: around(beside, 1),
            4: further[x] + around(plane, 2),
            5: around(further, 1) + around(beside, 2),
            8: around(further, 2),
        }
        level = weigh(sums, weight_ref, 0)
        for ref, square in ((near_ref, 1), (far_ref, 4)):
            ref[gapped(p, layers)] = weigh(sums, weight_ref, square)
            ref[gap(p + 1, layers)] = zero_gap
        result_ref[chip, own] = (
            level
            + near_ref[gapped(p, layers, 1)]
            + near_ref[gapped(p, layers, -1)]
            + far_ref[gapped(p, layers, 2)]
            + far_ref[gapped(p, layers, -2)]
        )


def share_kernel(
    disp_ref,
    coef_ref,
    weight_ref,
    sent_ref,
    plane_ref,
    beside_ref,
    further_ref,
    near_ref,
    far_ref,
):
    planes, layers, row_width = coef_ref.shape
    load_cases = lax.axis_size("space")
    shape = (layers, row_width)
    z = spot_iota(shape, 0)
    y = spot_iota(shape, 1)
    zero = jnp.zeros(shape, jnp.float32)
    shares = (plane_ref, beside_ref, further_ref)
    for ref in shares:
        zero_edges(ref)

    count = planes // 2

    def share_chunk(first, before):
        disp = disp_ref.at[:, pl.ds((first + 1) * layers, (count + 1) * layers)]
        coef = coef_ref.at[pl.ds(first, count)]
        plane, beside, further = (ref.at[pl.ds(first + 2, count)] for ref in shares)
        here = [disp[part, rows(0, layers)] for part in range(3)]
        for p in range(count):
            later = [disp[part, rows(p + 1, layers)] for part in range(3)]
            ahead, upward, right = zero, zero, zero
            for part in range(3):
                step = later[part] - here[part]
                climb = disp[part, rows(p, layers, 1)] - here[part]
                slide = pltpu.roll(here[part], row_width - 1, 1) - here[part]
                ahead = ahead + (2.0 if part == 0 else 1.0) * (step * step)
                upward = upward + (2.0 if part == 1 else 1.0) * (climb * climb)
                right = right + (2.0 if part == 2 else 1.0) * (slide * slide)
            if p == count - 1:
                ahead = jnp.where(first + count < planes, ahead, 0.0)
            upward = jnp.where(z < layers - 1, upward, 0.0)
            right = jnp.where(y < row_width - 1, right, 0.0)
            total = before + ahead + upward + pltpu.roll(upward, 1, 0)
            total = total + right + pltpu.roll(right, 1, 1)
            share = (0.5 / load_cases) * total * coef[p]
            plane[p] = share
            beside[p] = shift_sum(share, 1, 1)
            further[p] = shift_sum(share, 1, 2)
            before, here = ahead, later
        return before

    each_chunk(planes, count, share_chunk, zero)
    filter_group(1, shares, weight_ref, near_ref, far_ref, sent_ref)


def kept_kernel(
    disp_ref,
    weight_ref,
    plane_ref,
    beside_ref,
    further_ref,
    disp_hbm,
    kept_ref,
    near_ref,
    far_ref,
    stored,
):
    layers = kept_ref.shape[2]
    inner = pl.ds(layers, disp_ref.shape[1] - 2 * layers)
    store = pltpu.make_async_copy(disp_ref.at[:, inner], disp_hbm, stored)
    store.start()
    shares = (plane_ref, beside_ref, further_ref)
    filter_group(0, shares, weight_ref, near_ref, far_ref, kept_ref)
    store.wait()


def design_kernel(root_ref, density_ref, new_ref, pull_ref, low_ref, high_ref):
    groups, chips, own_planes, layers, row_width = density_ref.shape
    own_chip = lax.axis_index("space") >> 1
    shape = (layers, row_width)
    zero = jnp.zeros(shape, jnp.float32)
    planes = [
        (group, chip, own)
        for group in range(groups)
        for chip in range(chips)
        for own in range(own_planes)
    ]
    for spot in planes:
        density = density_ref[spot]
        pull_ref[spot] = density * root_ref[spot]
        low_ref[spot] = jnp.maximum(density - move_limit, density_floor)
        high_ref[spot] = jnp.minimum(density + move_limit, 1.0)

    target = volume_share * len(planes) * layers * row_width

    def factor_of(log_level):
        return jnp.broadcast_to(jnp.exp(-0.5 * log_level), shape)

    def exceeds(total):
        return jnp.sum(jnp.sum(total, axis=0, keepdims=True), axis=1, keepdims=True) > target

    def halve_twice(step, state):
        lower, span = state
        half, quarter = span * 0.5, span * 0.25
        middles = (lower + quarter, lower + half, lower + half + quarter)
        factors = [factor_of(middle) for middle in middles]
        totals = [zero, zero, zero]
        for spot in planes:
            pull, low, high = pull_ref[spot], low_ref[spot], high_ref[spot]
            totals = [
                total + jnp.minimum(jnp.maximum(pull * factor, low), high)
                for total, factor in zip(totals, factors)
            ]
        first, second, third = (exceeds(total) for total in totals)
        upper = jnp.where(third, middles[2], middles[1])
        below = jnp.where(first, middles[0], lower)
        return jnp.where(second, upper, below), quarter

    start = (jnp.full((1, 1), log_lower, jnp.float32), jnp.full((1, 1), log_span, jnp.float32))
    lower, span = lax.fori_loop(0, SEARCH // 2, halve_twice, start)
    factor = factor_of(lower + 0.5 * span)
    for own in range(own_planes):
        spot = (0, own_chip, own)
        new_ref[own] = jnp.minimum(
            jnp.maximum(pull_ref[spot] * factor, low_ref[spot]), high_ref[spot]
        )


def in_vmem():
    return pl.BlockSpec(memory_space=pltpu.VMEM)


KERNEL_VMEM = 24 * 2**20


def floats(*shape):
    return jax.ShapeDtypeStruct(shape, jnp.float32)


def spread_call(block, count):
    def kernel(block_hbm, copies_ref, arrived):
        copies = [
            pltpu.make_async_copy(block_hbm, copies_ref.at[place], arrived.at[place])
            for place in range(count)
        ]
        for copy in copies:
            copy.start()
        for copy in copies:
            copy.wait()

    return pl.pallas_call(
        kernel,
        out_shape=floats(count, *block.shape),
        in_specs=[pl.BlockSpec(memory_space=pltpu.HBM)],
        out_specs=in_vmem(),
        scratch_shapes=[pltpu.SemaphoreType.DMA((count,))],
        name="copies",
    )(pltpu.with_memory_space_constraint(block, pltpu.HBM))


def prepare_call(density, radius, load_index, load_force, fixed):
    chips, own_planes, layers, row_width = density.shape
    planes = fixed.shape[0]
    spread = pltpu.VMEM((chips * own_planes * (layers + GAP) + GAP, row_width), jnp.float32)
    return pl.pallas_call(
        prepare_kernel,
        out_shape=[
            floats(len(ALL_SQUARES), layers, row_width),
            floats(2 * window_reach + 1, layers, row_width),
            floats(planes, layers, row_width),
            floats(3, layers, row_width),
            floats(8, row_width),
            floats(3, *density.shape),
        ],
        in_specs=[pl.BlockSpec(memory_space=pltpu.HBM)] * 4 + [in_vmem()],
        out_specs=[in_vmem()] * 6,
        scratch_shapes=[
            pltpu.SMEM(radius.shape, radius.dtype),
            pltpu.SMEM(load_index.shape, load_index.dtype),
            pltpu.SMEM(load_force.shape, load_force.dtype),
            pltpu.VMEM(fixed.shape, fixed.dtype),
            spread,
            spread,
            spread,
            pltpu.SemaphoreType.DMA((4,)),
        ],
        compiler_params=pltpu.CompilerParams(vmem_limit_bytes=KERNEL_VMEM),
        cost_estimate=pl.CostEstimate(
            flops=80 * planes * layers * row_width,
            bytes_accessed=8 * planes * layers * row_width,
            transcendentals=0,
        ),
        name="prepare",
    )(
        *(
            pltpu.with_memory_space_constraint(array, pltpu.HBM)
            for array in (radius, load_index, load_force, fixed)
        ),
        density,
    )


def sweep_call(spot, load, weights, inverses, free, filtered, density, displacement):
    groups, chips, own_planes, layers, row_width = density.shape
    planes = groups * chips * own_planes

    def scratch(*lead):
        return pltpu.VMEM(lead + (row_width,), jnp.float32)

    return pl.pallas_call(
        sweep_kernel,
        out_shape=[
            floats(3, (planes + 2) * layers, row_width),
            floats(planes, layers, row_width),
        ],
        in_specs=[in_vmem()] * 8,
        out_specs=[in_vmem()] * 2,
        scratch_shapes=[
            scratch(planes // 2 * (layers + GAP) + GAP),
            scratch(planes // 2 * (layers + GAP) + GAP),
            scratch(planes // 2 * (layers + GAP) + GAP),
            scratch(planes + 4, layers),
            scratch(planes + 4, layers),
            scratch(planes + 4, layers),
            scratch((planes + 1) * layers),
            scratch(planes + 1, layers),
            scratch((planes + 1) * layers),
            scratch(planes + 1, layers),
            scratch(planes + 1, layers),
            scratch(3, planes + 1, layers),
            scratch(3, (planes + 2) * layers),
        ],
        compiler_params=pltpu.CompilerParams(vmem_limit_bytes=KERNEL_VMEM),
        name="sweeps",
    )(spot, load, weights, inverses, free, filtered, density, displacement)


def share_call(disp, coef, weights, group_shape):
    planes, layers, row_width = coef.shape
    gaps = pltpu.VMEM((planes // 2 * (layers + GAP) + GAP, row_width), jnp.float32)
    return pl.pallas_call(
        share_kernel,
        out_shape=[floats(*group_shape)] + [floats(planes + 4, layers, row_width)] * 3,
        in_specs=[in_vmem()] * 3,
        out_specs=[in_vmem()] * 4,
        scratch_shapes=[gaps, gaps],
        compiler_params=pltpu.CompilerParams(vmem_limit_bytes=KERNEL_VMEM),
        name="share",
    )(disp, coef, weights)


def kept_call(disp, weights, shares, group_shape):
    parts, disp_rows, row_width = disp.shape
    chips, own_planes, layers = group_shape[:3]
    gaps = pltpu.VMEM((chips * own_planes * (layers + GAP) + GAP, row_width), jnp.float32)
    return pl.pallas_call(
        kept_kernel,
        out_shape=[floats(parts, disp_rows - 2 * layers, row_width), floats(*group_shape)],
        in_specs=[in_vmem()] * 5,
        out_specs=[pl.BlockSpec(memory_space=pltpu.HBM), in_vmem()],
        scratch_shapes=[gaps, gaps, pltpu.SemaphoreType.DMA(())],
        compiler_params=pltpu.CompilerParams(vmem_limit_bytes=KERNEL_VMEM),
        cost_estimate=pl.CostEstimate(
            flops=20 * disp.size, bytes_accessed=8 * disp.size, transcendentals=0
        ),
        name="kept",
    )(disp, weights, *shares)


def design_call(root, density):
    return pl.pallas_call(
        design_kernel,
        out_shape=floats(*density.shape[2:]),
        in_specs=[in_vmem()] * 2,
        out_specs=in_vmem(),
        scratch_shapes=[pltpu.VMEM(density.shape, jnp.float32)] * 3,
        compiler_params=pltpu.CompilerParams(vmem_limit_bytes=KERNEL_VMEM),
        name="design",
    )(root, density)


def other_core(block):
    devices = lax.axis_size("space")
    return lax.ppermute(block, "space", [(i, i ^ 1) for i in range(devices)])


def chip_groups():
    chips = lax.axis_size("space") // 2
    return [[2 * chip + (chip ^ group) % 2 for chip in range(chips)] for group in range(2)]


def between_chips(pieces):
    return lax.all_to_all(pieces, "space", 0, 0, axis_index_groups=chip_groups())


def chip_gathered(block):
    chips = lax.axis_size("space") // 2
    return between_chips(jnp.broadcast_to(block[None], (chips,) + block.shape))


def with_other_core(blocks):
    return jnp.stack([blocks, other_core(blocks)])


def scattered_sum(sent, make_kept):
    received = other_core(sent)
    *others, kept = make_kept()
    return jnp.sum(between_chips(kept + received), axis=0), others


def one_slab(density, displacement, fixed, load_index, load_force, radius):
    chips = lax.axis_size("space") // 2
    same_group, small = lax.optimization_barrier(
        (between_chips(spread_call(density, chips)), (radius, load_index, load_force.T, fixed))
    )
    other_group = other_core(same_group)
    weights, inverses, free, load, spot, filtered = prepare_call(same_group, *small)
    whole = jnp.stack([same_group, other_group])
    disp, coef = sweep_call(
        spot, load, weights, inverses, free, filtered, whole, displacement[0]
    )
    sent, *shares = share_call(disp, coef, weights, same_group.shape)
    sent, disp, shares = lax.optimization_barrier((sent, disp, shares))
    squares, (new_displacement,) = scattered_sum(
        sent, lambda: kept_call(disp, weights, shares, same_group.shape)
    )
    root = with_other_core(chip_gathered(jnp.sqrt(squares)))
    new_density = design_call(root, whole)
    return new_density, new_displacement.reshape(displacement.shape)


def from_behind(block, axis, distance):
    devices = range(lax.axis_size(axis))
    route = [(i - distance, i) for i in devices if i - distance in devices]
    return lax.ppermute(block, axis, route)


def extended(x, sides, width):
    for axis, dim in sides:
        size, length = (lax.axis_size(axis), x.shape[dim])
        up = [(i, (i + 1) % size) for i in range(size - 1)]
        down = [(j, i) for i, j in up]
        last = lax.slice_in_dim(x, length - width, length, axis=dim)
        first = lax.slice_in_dim(x, 0, width, axis=dim)
        before = lax.ppermute(last, axis, up)
        after = lax.ppermute(first, axis, down)
        x = jnp.concatenate([before, x, after], axis=dim)
    return x


def from_partner(x, axis, bit):
    return lax.ppermute(x, axis, [(i, i ^ 1 << bit) for i in range(lax.axis_size(axis))])


def window_offsets():
    offsets_list = []
    for across in range(-window_reach, window_reach + 1):
        for upward in range(-window_reach, window_reach + 1):
            for sideways in range(-window_reach, window_reach + 1):
                length = math.sqrt(across * across + upward * upward + sideways * sideways)
                offsets_list.append((across, upward, sideways, length))
    return offsets_list


def layer_weights(radius):
    radial = radius.astype(jnp.float32)
    return jnp.stack(
        [jnp.maximum(radial - length, 0.0) for across, upward, sideways, length in window_offsets()]
    )


def pad_axis(grid_field, along_axis, before, after_cells):
    widths = [(0, 0)] * grid_field.ndim
    widths[along_axis] = (before, after_cells)
    return jnp.pad(grid_field, widths)


def pad_sides(grid_field):
    return jnp.pad(grid_field, ((0, 0), (window_reach, window_reach), (window_reach, window_reach)))


def filter_forward(padded, weights):
    out_rows = padded.shape[0] - 2 * window_reach
    layers = padded.shape[1] - 2 * window_reach
    row_width = padded.shape[2] - 2 * window_reach
    result = jnp.zeros((out_rows, layers, row_width), jnp.float32)
    for offset_index, (across, upward, sideways, length) in enumerate(window_offsets()):
        shifted = padded[
            window_reach + across : window_reach + across + out_rows,
            window_reach + upward : window_reach + upward + layers,
            window_reach + sideways : window_reach + sideways + row_width,
        ]
        result = result + weights[offset_index][None, :, None] * shifted
    return result


def filter_backward(padded, padded_weights):
    out_rows = padded.shape[0] - 2 * window_reach
    layers = padded.shape[1] - 2 * window_reach
    row_width = padded.shape[2] - 2 * window_reach
    result = jnp.zeros((out_rows, layers, row_width), jnp.float32)
    for offset_index, (across, upward, sideways, length) in enumerate(window_offsets()):
        shifted = padded[
            window_reach - across : window_reach - across + out_rows,
            window_reach - upward : window_reach - upward + layers,
            window_reach - sideways : window_reach - sideways + row_width,
        ]
        layer_part = padded_weights[
            offset_index, window_reach - upward : window_reach - upward + layers
        ]
        result = result + layer_part[None, :, None] * shifted
    return result


def stiff_factors(direction):
    return jnp.array(
        [2.0 if component == direction else 1.0 for component in range(3)], jnp.float32
    ).reshape(3, 1, 1, 1)


def relax_slab(padded, displace, face_x, face_z, face_y, force_field, free_cells, diagonal):
    flux_x = stiff_factors(0) * face_x * jnp.diff(padded, axis=1)
    stencil_image = flux_x[:, :-1] - flux_x[:, 1:]
    flux_z = stiff_factors(1) * face_z * jnp.diff(displace, axis=2)
    stencil_image = stencil_image + pad_axis(flux_z, 2, 1, 0) - pad_axis(flux_z, 2, 0, 1)
    flux_y = stiff_factors(2) * face_y * jnp.diff(displace, axis=3)
    stencil_image = stencil_image + pad_axis(flux_y, 3, 1, 0) - pad_axis(flux_y, 3, 0, 1)
    return free_cells * (displace + relax_factor * (force_field - stencil_image) / diagonal)


def slab_energy(grid_field, along_axis, direction, load_cases):
    change = jnp.diff(grid_field, axis=along_axis)
    return jnp.sum(stiff_factors(direction) * change * change, axis=0) / load_cases


def neighbour_planes(displace, load_cases, axis_devices):
    if axis_devices > load_cases:
        below = from_behind(displace[:, -1:], "space", load_cases)
        above = from_behind(displace[:, :1], "space", -load_cases)
    else:
        below = jnp.zeros_like(displace[:, :1])
        above = jnp.zeros_like(displace[:, :1])
    return jnp.concatenate([below, displace, above], axis=1)


def many_slabs(density, displacement, fixed, load_index, load_force, radius):
    slab_rows, layers, row_width = density.shape
    load_cases = load_index.shape[0]
    level_count = load_cases.bit_length() - 1
    axis_devices = lax.axis_size("space")
    axis_place = lax.axis_index("space")
    slab_planes = slab_rows * load_cases
    slab_place = axis_place // load_cases
    load_place = axis_place % load_cases
    total_rows = slab_rows * axis_devices
    weights = layer_weights(radius)
    padded_weights = pad_axis(weights, 1, window_reach, window_reach)
    global_rows = (
        jnp.arange(slab_rows + 2 * window_reach, dtype=jnp.int32)
        + axis_place * slab_rows
        - window_reach
    )
    deep_inside = ((global_rows >= 0) & (global_rows < total_rows)).astype(jnp.float32)
    inside_field = deep_inside[:, None, None] * pad_sides(
        jnp.ones((slab_rows + 2 * window_reach, layers, row_width), jnp.float32)
    )
    total_weight = filter_forward(inside_field, weights)
    slab_start = slab_place * slab_planes
    margin_rows = jnp.arange(slab_planes + 2, dtype=jnp.int32) + slab_start - 1
    margin_inside = ((margin_rows >= 0) & (margin_rows < total_rows)).astype(jnp.float32)
    face_valid = margin_inside[1:] * margin_inside[:-1]
    fixed_slab = lax.dynamic_slice_in_dim(fixed, slab_start, slab_planes, 0).astype(jnp.float32)
    bottom_layer = (jnp.arange(layers, dtype=jnp.int32) == 0).astype(jnp.float32)
    free_cells = 1.0 - bottom_layer[None, :, None] * fixed_slab[:, None, :]
    slab_cells = slab_planes * layers * row_width
    cell_index = jnp.arange(slab_cells, dtype=jnp.int32) + slab_place * slab_cells
    load_hot = jnp.arange(load_cases, dtype=jnp.int32) == load_place
    own_index = jnp.sum(jnp.where(load_hot, load_index, 0))
    own_force = jnp.sum(load_hot.astype(jnp.float32)[:, None] * load_force, axis=0)
    load_hits = (cell_index == own_index).astype(jnp.float32)
    force_field = (own_force[:, None] * load_hits[None, :]).reshape(
        3, slab_planes, layers, row_width
    )
    displace = displacement[0] * free_cells
    target = volume_share * total_rows * layers * row_width
    padded = neighbour_planes(displace, load_cases, axis_devices)
    halo_density = extended(density, (("space", 0),), window_reach)
    filtered = filter_forward(pad_sides(halo_density), weights) / total_weight
    whole_field = lax.all_gather(filtered, "space", axis=0, tiled=True)
    margin = lax.dynamic_slice_in_dim(
        pad_axis(whole_field, 0, 1, 1), slab_start, slab_planes + 2, 0
    )
    moduli = floor_modulus + (1.0 - floor_modulus) * margin**3
    face_x = 0.5 * (moduli[1:] + moduli[:-1]) * face_valid[:, None, None]
    inner_moduli = moduli[1:-1]
    face_z = 0.5 * (inner_moduli[:, 1:] + inner_moduli[:, :-1])
    face_y = 0.5 * (inner_moduli[:, :, 1:] + inner_moduli[:, :, :-1])
    sum_x = face_x[:-1] + face_x[1:]
    sum_z = pad_axis(face_z, 1, 1, 0) + pad_axis(face_z, 1, 0, 1)
    sum_y = pad_axis(face_y, 2, 1, 0) + pad_axis(face_y, 2, 0, 1)
    diagonal = stiff_factors(0) * sum_x + stiff_factors(1) * sum_z + stiff_factors(2) * sum_y
    for sweep_index in range(SWEEPS):
        displace = relax_slab(
            padded, displace, face_x, face_z, face_y, force_field, free_cells, diagonal
        )
        padded = neighbour_planes(displace, load_cases, axis_devices)
    energy_x = slab_energy(padded, 1, 0, load_cases) * face_valid[:, None, None]
    energy_z = slab_energy(displace, 2, 1, load_cases)
    energy_y = slab_energy(displace, 3, 2, load_cases)
    sens_term = 0.5 * (
        energy_x[:-1]
        + energy_x[1:]
        + pad_axis(energy_z, 1, 1, 0)
        + pad_axis(energy_z, 1, 0, 1)
        + pad_axis(energy_y, 2, 1, 0)
        + pad_axis(energy_y, 2, 0, 1)
    )
    sensitive = sens_term
    for level in reversed(range(level_count)):
        half_rows = sensitive.shape[0] // 2
        upper_side = load_place // 2**level % 2 == 1
        outgoing = jnp.where(upper_side, sensitive[:half_rows], sensitive[half_rows:])
        keeping = jnp.where(upper_side, sensitive[half_rows:], sensitive[:half_rows])
        sensitive = keeping + from_partner(outgoing, "space", level)
    weighted_share = 3.0 * (1.0 - floor_modulus) * filtered**2 * sensitive / total_weight
    halo_share = extended(weighted_share, (("space", 0),), window_reach)
    root_term = jnp.sqrt(filter_backward(pad_sides(halo_share), padded_weights))
    lowest = jnp.maximum(density - move_limit, density_floor)
    highest = jnp.minimum(density + move_limit, 1.0)
    design_now = density

    def trial_design(log_level):
        return jnp.clip(design_now * root_term * jnp.exp(-0.5 * log_level), lowest, highest)

    start_state = (jnp.asarray(log_lower, jnp.float32), jnp.asarray(log_span, jnp.float32))

    def halve(search_step, search_state):
        lower_end, span_width = search_state
        half_span = span_width * 0.5
        middle = lower_end + half_span
        volume_total = lax.psum(jnp.sum(trial_design(middle)), "space")
        return (jnp.where(volume_total > target, middle, lower_end), half_span)

    lower_end, span_width = lax.fori_loop(0, SEARCH, halve, start_state)
    density = trial_design(lower_end + 0.5 * span_width)
    new_displacement = displace[None]
    return (density, new_displacement)


def solution(mesh):
    in_specs = (
        P("space", "parts", None),
        P("space", None, None, "parts", None),
        P(None, "parts"),
        P("parts"),
        P("parts", None),
        P("parts"),
    )
    out_specs = (P("space", "parts", None), P("space", None, None, "parts", None))

    def local(density, displacement, fixed, load_index, load_force, radius):
        alone = lax.axis_size("space") == load_index.shape[0]
        run = one_slab if alone else many_slabs
        return run(density, displacement, fixed, load_index, load_force, radius)

    return jax.shard_map(local, mesh=mesh, in_specs=in_specs, out_specs=out_specs, check_vma=False)
```

```python
import math

import jax
import jax.numpy as jnp
from jax import lax
from jax.experimental import pallas as pl
from jax.experimental.pallas import tpu as pltpu
from jax.sharding import PartitionSpec as P

SWEEPS = 3
SEARCH = 12


floor_modulus = 0.05
relax_factor = 0.6
move_limit = 0.2
density_floor = 0.01
volume_share = 0.5
log_lower = -16.0
log_span = 32.0
window_reach = 2

PLANE_SQUARES = (0, 1, 2, 4, 5, 8)
ALL_SQUARES = (0, 1, 2, 3, 4, 5, 6, 8, 9, 12)


def spot_iota(shape, dim):
    return lax.broadcasted_iota(jnp.int32, shape, dim)


def each_plane(planes, body, carry):
    for x in range(planes):
        carry = body(x, carry)
    return carry


def each_chunk(planes, count, body, carry):
    return lax.fori_loop(0, planes // count, lambda i, carry: body(i * count, carry), carry)


def layer_radius(radius_ref, layers, row_width):
    z = spot_iota((layers, row_width), 0)
    result = jnp.zeros((layers, row_width), jnp.int32)
    for layer in range(layers):
        result = jnp.where(z == layer, radius_ref[layer], result)
    return result.astype(jnp.float32)


def class_weights(radius_ref, weight_ref):
    layers, row_width = weight_ref.shape[1:]
    radial = layer_radius(radius_ref, layers, row_width)
    for place, square in enumerate(ALL_SQUARES):
        weight_ref[place] = jnp.maximum(radial - math.sqrt(square), 0.0)


def shift_sum(field, dim, distance):
    size = field.shape[dim]
    spot = spot_iota(field.shape, dim)
    ahead = jnp.where(spot < size - distance, pltpu.roll(field, size - distance, dim), 0.0)
    behind = jnp.where(spot >= distance, pltpu.roll(field, distance, dim), 0.0)
    return ahead + behind


def plane_sums(plane):
    beside = shift_sum(plane, 1, 1)
    further = shift_sum(plane, 1, 2)
    return {
        0: plane,
        1: beside + shift_sum(plane, 0, 1),
        2: shift_sum(beside, 0, 1),
        4: further + shift_sum(plane, 0, 2),
        5: shift_sum(further, 0, 1) + shift_sum(beside, 0, 2),
        8: shift_sum(further, 0, 2),
    }


def weigh(sums, weight_ref, square):
    result = None
    for inner in PLANE_SQUARES:
        term = weight_ref[ALL_SQUARES.index(inner + square)] * sums[inner]
        result = term if result is None else result + term
    return result


def forward_planes(plane, weight_ref):
    sums = plane_sums(plane)
    return [weigh(sums, weight_ref, square) for square in (0, 1, 4)]


def rows(x, layers, shift=0):
    return pl.ds(x * layers + shift, layers)


GAP = 8


def gapped(x, layers, shift=0):
    return pl.ds(GAP + x * (layers + GAP) + shift, layers)


def gap(x, layers):
    return pl.ds(x * (layers + GAP), GAP)


def edge_class(x, planes):
    return jnp.minimum(x, 2) + jnp.maximum(x - (planes - 3), 0)


def zero_edges(ref):
    planes = ref.shape[0]
    for place in (0, 1, planes - 2, planes - 1):
        ref[place] = jnp.zeros(ref.shape[1:], ref.dtype)


def group_spots(group, blocks):
    chips, own_planes = blocks.shape[:2]
    mine = lax.axis_index("space")
    core = mine ^ mine >> 1 ^ group
    return [
        (own_planes * (2 * chip + ((core ^ chip) & 1)) + own, (chip, own))
        for chip in range(chips)
        for own in range(own_planes)
    ]


def spread_group(blocks, spread):
    chips, own_planes, layers, row_width = blocks.shape
    zero_gap = jnp.zeros((GAP, row_width), jnp.float32)
    for ref in spread:
        ref[gap(0, layers)] = zero_gap
    for p in range(chips * own_planes):
        plane = blocks[p // own_planes, p % own_planes]
        for ref, field in zip(spread, (plane, shift_sum(plane, 1, 1), shift_sum(plane, 1, 2))):
            ref[gapped(p, layers)] = field
            ref[gap(p + 1, layers)] = zero_gap


def filter_plane(p, layers, spread, weight_ref):
    def around(place, distance):
        ref = spread[place]
        return ref[gapped(p, layers, distance)] + ref[gapped(p, layers, -distance)]

    sums = {
        0: spread[0][gapped(p, layers)],
        1: spread[1][gapped(p, layers)] + around(0, 1),
        2: around(1, 1),
        4: spread[2][gapped(p, layers)] + around(0, 2),
        5: around(2, 1) + around(1, 2),
        8: around(2, 2),
    }
    return [weigh(sums, weight_ref, square) for square in (0, 1, 4)]


def prepare_kernel(
    radius_hbm,
    index_hbm,
    force_hbm,
    fixed_hbm,
    density_ref,
    weight_ref,
    inverse_ref,
    free_ref,
    load_ref,
    spot_ref,
    filter_ref,
    radius_ref,
    index_ref,
    force_ref,
    fixed_ref,
    plane_ref,
    beside_ref,
    further_ref,
    arrived,
):
    copies = [
        pltpu.make_async_copy(source, target, arrived.at[place])
        for place, (source, target) in enumerate(
            (
                (radius_hbm, radius_ref),
                (index_hbm, index_ref),
                (force_hbm, force_ref),
                (fixed_hbm, fixed_ref),
            )
        )
    ]
    for copy in copies:
        copy.start()
    spread = (plane_ref, beside_ref, further_ref)
    spread_group(density_ref, spread)
    for copy in copies:
        copy.wait()
    planes, layers, row_width = free_ref.shape
    load_place = lax.axis_index("space")
    shape = (layers, row_width)
    z = spot_iota(shape, 0)
    y = spot_iota(shape, 1)

    class_weights(radius_ref, weight_ref)
    own_planes = density_ref.shape[1]
    for p in range(density_ref.shape[0] * own_planes):
        for place, field in enumerate(filter_plane(p, layers, spread, weight_ref)):
            filter_ref[place, p // own_planes, p % own_planes] = field

    ones = forward_planes(jnp.ones(shape, jnp.float32), weight_ref)
    for place, (lower, upper) in enumerate(((0, 2), (1, 2), (2, 2), (2, 1), (2, 0))):
        inverse_ref[place] = 1.0 / (
            ones[0] + min(lower, 1) * ones[1] + min(upper, 1) * ones[1]
            + (lower // 2) * ones[2] + (upper // 2) * ones[2]
        )

    def free_plane(x, carry):
        free_ref[x] = jnp.where(
            z == 0, 1.0 - fixed_ref[pl.ds(x, 1), :].astype(jnp.float32), 1.0
        )
        return carry

    each_plane(planes, free_plane, 0)

    own_index = index_ref[load_place]
    own_z = own_index // row_width % layers
    own_y = own_index % row_width
    hit = (z == own_z) & (y == own_y)
    for part in range(3):
        load_ref[part] = jnp.where(hit, force_ref[part, load_place], 0.0)
    own_x = (own_index // (layers * row_width)).astype(jnp.float32)
    spot_ref[...] = jnp.full(spot_ref.shape, own_x)


def sweep_kernel(
    spot_ref,
    load_ref,
    weight_ref,
    inverse_ref,
    free_ref,
    filter_ref,
    density_ref,
    start_ref,
    disp_ref,
    coef_ref,
    plane_ref,
    beside_ref,
    further_ref,
    near_ref,
    side_ref,
    far_ref,
    modulus_ref,
    across_ref,
    up_ref,
    right_ref,
    left_ref,
    rate_ref,
    first_ref,
):
    planes, layers, row_width = coef_ref.shape
    shape = (layers, row_width)
    z = spot_iota(shape, 0)
    y = spot_iota(shape, 1)
    zero = jnp.zeros(shape, jnp.float32)

    for ref in (side_ref, far_ref):
        zero_edges(ref)
    results = (near_ref, side_ref, far_ref)
    other_ref = density_ref.at[1]
    for x, spot in group_spots(0, other_ref):
        for place, ref in enumerate(results):
            ref[x + 2] = filter_ref[(place,) + spot]
    spread = (plane_ref, beside_ref, further_ref)
    spread_group(other_ref, spread)
    for p, (x, spot) in enumerate(group_spots(1, other_ref)):
        for ref, field in zip(results, filter_plane(p, layers, spread, weight_ref)):
            ref[x + 2] = field

    for ref in (first_ref, disp_ref):
        for part in range(3):
            ref[part, rows(0, layers)] = zero
            ref[part, rows(planes + 1, layers)] = zero

    def store_faces(slot, modulus, above, later, before, free, start, views):
        across, up_view, right_view, left_view, rate, source = views
        across[slot] = later
        up = jnp.where(z < layers - 1, 0.5 * (modulus + above), 0.0)
        right = jnp.where(
            y < row_width - 1, 0.5 * (modulus + pltpu.roll(modulus, row_width - 1, 1)), 0.0
        )
        left = pltpu.roll(right, 1, 1)
        up_view[rows(slot, layers)] = up
        right_view[slot] = right
        left_view[slot] = left
        sums = (before + later, up + pltpu.roll(up, 1, 0), left + right)
        every = sums[0] + sums[1] + sums[2]
        diagonal = [every + part_sum for part_sum in sums]
        pair = diagonal[0] * diagonal[1]
        push = relax_factor * free / (pair * diagonal[2])
        side = push * diagonal[2]
        for part, factor in enumerate((side * diagonal[1], side * diagonal[0], push * pair)):
            rate[part, slot] = factor
            source[part, rows(slot, layers)] = start[part] * free

    def modulus_piece(first, carry):
        count = planes
        near = near_ref.at[pl.ds(first + 2, count)]
        side = side_ref.at[pl.ds(first + 1, count + 2)]
        far = far_ref.at[pl.ds(first, count + 4)]
        moduli = modulus_ref.at[pl.ds(first * layers, (count + 1) * layers)]
        coef = coef_ref.at[pl.ds(first, count)]
        free = free_ref.at[pl.ds(first, count)]
        views = (
            across_ref.at[pl.ds(first, count)],
            up_ref.at[pl.ds(first * layers, count * layers)],
            right_ref.at[pl.ds(first, count)],
            left_ref.at[pl.ds(first, count)],
            rate_ref.at[:, pl.ds(first, count)],
            first_ref.at[:, pl.ds(first * layers, count * layers)],
        )
        modulus, before = carry
        for p in range(count):
            inverse = inverse_ref[edge_class(first + p, planes)]
            filtered = near[p] + side[p] + side[p + 2] + far[p] + far[p + 4]
            filtered = filtered * inverse
            later = floor_modulus + (1.0 - floor_modulus) * (filtered * filtered * filtered)
            coef[p] = 3.0 * (1.0 - floor_modulus) * (filtered * filtered) * inverse
            moduli[rows(p + 1, layers)] = later
            ahead = 0.5 * (modulus + later)
            if p == 0:
                ahead = jnp.where(first > 0, ahead, 0.0)
            above = moduli[rows(p, layers, 1)] if p else pltpu.roll(modulus, layers - 1, 0)
            previous = jnp.maximum(first + p - 1, 0)
            store_faces(
                p,
                modulus,
                above,
                ahead,
                before,
                free_ref[previous],
                [start_ref[part, previous] for part in range(3)],
                views,
            )
            modulus, before = later, ahead
        return modulus, before

    modulus, before = each_chunk(planes, planes, modulus_piece, (jnp.ones(shape, jnp.float32), zero))
    store_faces(
        planes,
        modulus,
        pltpu.roll(modulus, layers - 1, 0),
        zero,
        before,
        free_ref[planes - 1],
        [start_ref[part, planes - 1] for part in range(3)],
        (across_ref, up_ref, right_ref, left_ref, rate_ref, first_ref),
    )

    own_x = jnp.max(spot_ref[...]).astype(jnp.int32)

    def sweep(source, target):
        def sweep_piece(first, carry):
            count = planes
            old = source.at[:, pl.ds(first * layers, (count + 2) * layers)]
            new = target.at[:, pl.ds((first + 1) * layers, count * layers)]
            across = across_ref.at[pl.ds(first, count + 1)]
            up = up_ref.at[pl.ds(first * layers, (count + 1) * layers)]
            right = right_ref.at[pl.ds(first + 1, count)]
            left = left_ref.at[pl.ds(first + 1, count)]
            rate = rate_ref.at[:, pl.ds(first + 1, count)]
            behind = [old[part, rows(0, layers)] for part in range(3)]
            here = [old[part, rows(1, layers)] for part in range(3)]
            for p in range(count):
                ahead = [old[part, rows(p + 2, layers)] for part in range(3)]
                for part in range(3):
                    pulls = [
                        across[p] * behind[part] + across[p + 1] * ahead[part],
                        up[rows(p + 1, layers)] * old[part, rows(p + 1, layers, 1)]
                        + up[rows(p + 1, layers, -1)] * old[part, rows(p + 1, layers, -1)],
                        right[p] * pltpu.roll(here[part], row_width - 1, 1)
                        + left[p] * pltpu.roll(here[part], 1, 1),
                    ]
                    pull = pulls[0] + pulls[1] + pulls[2] + pulls[part]
                    new[part, rows(p, layers)] = (
                        1.0 - relax_factor
                    ) * here[part] + rate[part, p] * pull
                behind, here = here, ahead
            return carry

        sweep_piece(0, 0)
        for part in range(3):
            target[part, rows(own_x + 1, layers)] += rate_ref[part, own_x + 1] * load_ref[part]

    def two_sweeps(turn, carry):
        sweep(first_ref, disp_ref)

        @pl.when(turn < SWEEPS // 2)
        def _():
            sweep(disp_ref, first_ref)

        return carry

    lax.fori_loop(0, SWEEPS // 2 + 1, two_sweeps, 0)


def filter_group(group, shares, weight_ref, near_ref, far_ref, result_ref):
    chips, own_planes, layers, row_width = result_ref.shape
    zero_gap = jnp.zeros((GAP, row_width), jnp.float32)
    mine = lax.axis_index("space")
    core = (mine ^ mine >> 1 ^ group) & 1
    count = shares[0].shape[0] - own_planes
    views = [
        [ref.at[pl.ds(own_planes * start, count)] for ref in shares] for start in (core, 1 - core)
    ]
    for ref in (near_ref, far_ref):
        ref[gap(0, layers)] = zero_gap
    for p in range(chips * own_planes):
        chip, own = p // own_planes, p % own_planes
        plane, beside, further = views[chip & 1]
        x = 2 * own_planes * chip + own + 2

        def around(ref, distance):
            return ref[x + distance] + ref[x - distance]

        sums = {
            0: plane[x],
            1: beside[x] + around(plane, 1),
            2: around(beside, 1),
            4: further[x] + around(plane, 2),
            5: around(further, 1) + around(beside, 2),
            8: around(further, 2),
        }
        level = weigh(sums, weight_ref, 0)
        for ref, square in ((near_ref, 1), (far_ref, 4)):
            ref[gapped(p, layers)] = weigh(sums, weight_ref, square)
            ref[gap(p + 1, layers)] = zero_gap
        result_ref[chip, own] = (
            level
            + near_ref[gapped(p, layers, 1)]
            + near_ref[gapped(p, layers, -1)]
            + far_ref[gapped(p, layers, 2)]
            + far_ref[gapped(p, layers, -2)]
        )


def share_kernel(
    disp_ref,
    coef_ref,
    weight_ref,
    sent_ref,
    plane_ref,
    beside_ref,
    further_ref,
    near_ref,
    far_ref,
):
    planes, layers, row_width = coef_ref.shape
    load_cases = lax.axis_size("space")
    shape = (layers, row_width)
    z = spot_iota(shape, 0)
    y = spot_iota(shape, 1)
    zero = jnp.zeros(shape, jnp.float32)
    shares = (plane_ref, beside_ref, further_ref)
    for ref in shares:
        zero_edges(ref)

    count = planes // 2

    def share_chunk(first, before):
        disp = disp_ref.at[:, pl.ds((first + 1) * layers, (count + 1) * layers)]
        coef = coef_ref.at[pl.ds(first, count)]
        plane, beside, further = (ref.at[pl.ds(first + 2, count)] for ref in shares)
        here = [disp[part, rows(0, layers)] for part in range(3)]
        for p in range(count):
            later = [disp[part, rows(p + 1, layers)] for part in range(3)]
            ahead, upward, right = zero, zero, zero
            for part in range(3):
                step = later[part] - here[part]
                climb = disp[part, rows(p, layers, 1)] - here[part]
                slide = pltpu.roll(here[part], row_width - 1, 1) - here[part]
                ahead = ahead + (2.0 if part == 0 else 1.0) * (step * step)
                upward = upward + (2.0 if part == 1 else 1.0) * (climb * climb)
                right = right + (2.0 if part == 2 else 1.0) * (slide * slide)
            if p == count - 1:
                ahead = jnp.where(first + count < planes, ahead, 0.0)
            upward = jnp.where(z < layers - 1, upward, 0.0)
            right = jnp.where(y < row_width - 1, right, 0.0)
            total = before + ahead + upward + pltpu.roll(upward, 1, 0)
            total = total + right + pltpu.roll(right, 1, 1)
            share = (0.5 / load_cases) * total * coef[p]
            plane[p] = share
            beside[p] = shift_sum(share, 1, 1)
            further[p] = shift_sum(share, 1, 2)
            before, here = ahead, later
        return before

    each_chunk(planes, count, share_chunk, zero)
    filter_group(1, shares, weight_ref, near_ref, far_ref, sent_ref)


def kept_kernel(
    disp_ref,
    weight_ref,
    plane_ref,
    beside_ref,
    further_ref,
    disp_hbm,
    kept_ref,
    near_ref,
    far_ref,
    stored,
):
    layers = kept_ref.shape[2]
    inner = pl.ds(layers, disp_ref.shape[1] - 2 * layers)
    store = pltpu.make_async_copy(disp_ref.at[:, inner], disp_hbm, stored)
    store.start()
    shares = (plane_ref, beside_ref, further_ref)
    filter_group(0, shares, weight_ref, near_ref, far_ref, kept_ref)
    store.wait()


def design_kernel(root_ref, density_ref, new_ref, pull_ref, low_ref, high_ref):
    groups, chips, own_planes, layers, row_width = density_ref.shape
    own_chip = lax.axis_index("space") >> 1
    shape = (layers, row_width)
    zero = jnp.zeros(shape, jnp.float32)
    planes = [
        (group, chip, own)
        for group in range(groups)
        for chip in range(chips)
        for own in range(own_planes)
    ]
    for spot in planes:
        density = density_ref[spot]
        pull_ref[spot] = density * root_ref[spot]
        low_ref[spot] = jnp.maximum(density - move_limit, density_floor)
        high_ref[spot] = jnp.minimum(density + move_limit, 1.0)

    target = volume_share * len(planes) * layers * row_width

    def factor_of(log_level):
        return jnp.broadcast_to(jnp.exp(-0.5 * log_level), shape)

    def exceeds(total):
        return jnp.sum(jnp.sum(total, axis=0, keepdims=True), axis=1, keepdims=True) > target

    def halve_twice(step, state):
        lower, span = state
        half, quarter = span * 0.5, span * 0.25
        middles = (lower + quarter, lower + half, lower + half + quarter)
        factors = [factor_of(middle) for middle in middles]
        totals = [zero, zero, zero]
        for spot in planes:
            pull, low, high = pull_ref[spot], low_ref[spot], high_ref[spot]
            totals = [
                total + jnp.minimum(jnp.maximum(pull * factor, low), high)
                for total, factor in zip(totals, factors)
            ]
        first, second, third = (exceeds(total) for total in totals)
        upper = jnp.where(third, middles[2], middles[1])
        below = jnp.where(first, middles[0], lower)
        return jnp.where(second, upper, below), quarter

    start = (jnp.full((1, 1), log_lower, jnp.float32), jnp.full((1, 1), log_span, jnp.float32))
    lower, span = lax.fori_loop(0, SEARCH // 2, halve_twice, start)
    factor = factor_of(lower + 0.5 * span)
    for own in range(own_planes):
        spot = (0, own_chip, own)
        new_ref[own] = jnp.minimum(
            jnp.maximum(pull_ref[spot] * factor, low_ref[spot]), high_ref[spot]
        )


def in_vmem():
    return pl.BlockSpec(memory_space=pltpu.VMEM)


KERNEL_VMEM = 24 * 2**20


def floats(*shape):
    return jax.ShapeDtypeStruct(shape, jnp.float32)


def prepare_call(density, radius, load_index, load_force, fixed):
    chips, own_planes, layers, row_width = density.shape
    planes = fixed.shape[0]
    spread = pltpu.VMEM((chips * own_planes * (layers + GAP) + GAP, row_width), jnp.float32)
    return pl.pallas_call(
        prepare_kernel,
        out_shape=[
            floats(len(ALL_SQUARES), layers, row_width),
            floats(2 * window_reach + 1, layers, row_width),
            floats(planes, layers, row_width),
            floats(3, layers, row_width),
            floats(8, row_width),
            floats(3, *density.shape),
        ],
        in_specs=[pl.BlockSpec(memory_space=pltpu.HBM)] * 4 + [in_vmem()],
        out_specs=[in_vmem()] * 6,
        scratch_shapes=[
            pltpu.SMEM(radius.shape, radius.dtype),
            pltpu.SMEM(load_index.shape, load_index.dtype),
            pltpu.SMEM(load_force.shape, load_force.dtype),
            pltpu.VMEM(fixed.shape, fixed.dtype),
            spread,
            spread,
            spread,
            pltpu.SemaphoreType.DMA((4,)),
        ],
        compiler_params=pltpu.CompilerParams(vmem_limit_bytes=KERNEL_VMEM),
        cost_estimate=pl.CostEstimate(
            flops=80 * planes * layers * row_width,
            bytes_accessed=8 * planes * layers * row_width,
            transcendentals=0,
        ),
        name="prepare",
    )(
        *(
            pltpu.with_memory_space_constraint(array, pltpu.HBM)
            for array in (radius, load_index, load_force, fixed)
        ),
        density,
    )


def sweep_call(spot, load, weights, inverses, free, filtered, density, displacement):
    groups, chips, own_planes, layers, row_width = density.shape
    planes = groups * chips * own_planes

    def scratch(*lead):
        return pltpu.VMEM(lead + (row_width,), jnp.float32)

    return pl.pallas_call(
        sweep_kernel,
        out_shape=[
            floats(3, (planes + 2) * layers, row_width),
            floats(planes, layers, row_width),
        ],
        in_specs=[in_vmem()] * 8,
        out_specs=[in_vmem()] * 2,
        scratch_shapes=[
            scratch(planes // 2 * (layers + GAP) + GAP),
            scratch(planes // 2 * (layers + GAP) + GAP),
            scratch(planes // 2 * (layers + GAP) + GAP),
            scratch(planes + 4, layers),
            scratch(planes + 4, layers),
            scratch(planes + 4, layers),
            scratch((planes + 1) * layers),
            scratch(planes + 1, layers),
            scratch((planes + 1) * layers),
            scratch(planes + 1, layers),
            scratch(planes + 1, layers),
            scratch(3, planes + 1, layers),
            scratch(3, (planes + 2) * layers),
        ],
        compiler_params=pltpu.CompilerParams(vmem_limit_bytes=KERNEL_VMEM),
        name="sweeps",
    )(spot, load, weights, inverses, free, filtered, density, displacement)


def share_call(disp, coef, weights, group_shape):
    planes, layers, row_width = coef.shape
    gaps = pltpu.VMEM((planes // 2 * (layers + GAP) + GAP, row_width), jnp.float32)
    return pl.pallas_call(
        share_kernel,
        out_shape=[floats(*group_shape)] + [floats(planes + 4, layers, row_width)] * 3,
        in_specs=[in_vmem()] * 3,
        out_specs=[in_vmem()] * 4,
        scratch_shapes=[gaps, gaps],
        compiler_params=pltpu.CompilerParams(vmem_limit_bytes=KERNEL_VMEM),
        name="share",
    )(disp, coef, weights)


def kept_call(disp, weights, shares, group_shape):
    parts, disp_rows, row_width = disp.shape
    chips, own_planes, layers = group_shape[:3]
    gaps = pltpu.VMEM((chips * own_planes * (layers + GAP) + GAP, row_width), jnp.float32)
    return pl.pallas_call(
        kept_kernel,
        out_shape=[floats(parts, disp_rows - 2 * layers, row_width), floats(*group_shape)],
        in_specs=[in_vmem()] * 5,
        out_specs=[pl.BlockSpec(memory_space=pltpu.HBM), in_vmem()],
        scratch_shapes=[gaps, gaps, pltpu.SemaphoreType.DMA(())],
        compiler_params=pltpu.CompilerParams(vmem_limit_bytes=KERNEL_VMEM),
        cost_estimate=pl.CostEstimate(
            flops=20 * disp.size, bytes_accessed=8 * disp.size, transcendentals=0
        ),
        name="kept",
    )(disp, weights, *shares)


def design_call(root, density):
    return pl.pallas_call(
        design_kernel,
        out_shape=floats(*density.shape[2:]),
        in_specs=[in_vmem()] * 2,
        out_specs=in_vmem(),
        scratch_shapes=[pltpu.VMEM(density.shape, jnp.float32)] * 3,
        compiler_params=pltpu.CompilerParams(vmem_limit_bytes=KERNEL_VMEM),
        name="design",
    )(root, density)


def other_core(block):
    devices = lax.axis_size("space")
    return lax.ppermute(block, "space", [(i, i ^ 1) for i in range(devices)])


def chip_groups():
    chips = lax.axis_size("space") // 2
    return [[2 * chip + (chip ^ group) % 2 for chip in range(chips)] for group in range(2)]


def between_chips(pieces):
    return lax.all_to_all(pieces, "space", 0, 0, axis_index_groups=chip_groups())


def chip_gathered(block):
    chips = lax.axis_size("space") // 2
    return between_chips(jnp.broadcast_to(block[None], (chips,) + block.shape))


def with_other_core(blocks):
    return jnp.stack([blocks, other_core(blocks)])


def scattered_sum(sent, make_kept):
    received = other_core(sent)
    *others, kept = make_kept()
    return jnp.sum(between_chips(kept + received), axis=0), others


def one_slab(density, displacement, fixed, load_index, load_force, radius):
    same_group, small = lax.optimization_barrier(
        (chip_gathered(density), (radius, load_index, load_force.T, fixed))
    )
    other_group = other_core(same_group)
    weights, inverses, free, load, spot, filtered = prepare_call(same_group, *small)
    whole = jnp.stack([same_group, other_group])
    disp, coef = sweep_call(
        spot, load, weights, inverses, free, filtered, whole, displacement[0]
    )
    sent, *shares = share_call(disp, coef, weights, same_group.shape)
    sent, disp, shares = lax.optimization_barrier((sent, disp, shares))
    squares, (new_displacement,) = scattered_sum(
        sent, lambda: kept_call(disp, weights, shares, same_group.shape)
    )
    root = with_other_core(chip_gathered(jnp.sqrt(squares)))
    new_density = design_call(root, whole)
    return new_density, new_displacement.reshape(displacement.shape)


def from_behind(block, axis, distance):
    devices = range(lax.axis_size(axis))
    route = [(i - distance, i) for i in devices if i - distance in devices]
    return lax.ppermute(block, axis, route)


def extended(x, sides, width):
    for axis, dim in sides:
        size, length = (lax.axis_size(axis), x.shape[dim])
        up = [(i, (i + 1) % size) for i in range(size - 1)]
        down = [(j, i) for i, j in up]
        last = lax.slice_in_dim(x, length - width, length, axis=dim)
        first = lax.slice_in_dim(x, 0, width, axis=dim)
        before = lax.ppermute(last, axis, up)
        after = lax.ppermute(first, axis, down)
        x = jnp.concatenate([before, x, after], axis=dim)
    return x


def from_partner(x, axis, bit):
    return lax.ppermute(x, axis, [(i, i ^ 1 << bit) for i in range(lax.axis_size(axis))])


def window_offsets():
    offsets_list = []
    for across in range(-window_reach, window_reach + 1):
        for upward in range(-window_reach, window_reach + 1):
            for sideways in range(-window_reach, window_reach + 1):
                length = math.sqrt(across * across + upward * upward + sideways * sideways)
                offsets_list.append((across, upward, sideways, length))
    return offsets_list


def layer_weights(radius):
    radial = radius.astype(jnp.float32)
    return jnp.stack(
        [jnp.maximum(radial - length, 0.0) for across, upward, sideways, length in window_offsets()]
    )


def pad_axis(grid_field, along_axis, before, after_cells):
    widths = [(0, 0)] * grid_field.ndim
    widths[along_axis] = (before, after_cells)
    return jnp.pad(grid_field, widths)


def pad_sides(grid_field):
    return jnp.pad(grid_field, ((0, 0), (window_reach, window_reach), (window_reach, window_reach)))


def filter_forward(padded, weights):
    out_rows = padded.shape[0] - 2 * window_reach
    layers = padded.shape[1] - 2 * window_reach
    row_width = padded.shape[2] - 2 * window_reach
    result = jnp.zeros((out_rows, layers, row_width), jnp.float32)
    for offset_index, (across, upward, sideways, length) in enumerate(window_offsets()):
        shifted = padded[
            window_reach + across : window_reach + across + out_rows,
            window_reach + upward : window_reach + upward + layers,
            window_reach + sideways : window_reach + sideways + row_width,
        ]
        result = result + weights[offset_index][None, :, None] * shifted
    return result


def filter_backward(padded, padded_weights):
    out_rows = padded.shape[0] - 2 * window_reach
    layers = padded.shape[1] - 2 * window_reach
    row_width = padded.shape[2] - 2 * window_reach
    result = jnp.zeros((out_rows, layers, row_width), jnp.float32)
    for offset_index, (across, upward, sideways, length) in enumerate(window_offsets()):
        shifted = padded[
            window_reach - across : window_reach - across + out_rows,
            window_reach - upward : window_reach - upward + layers,
            window_reach - sideways : window_reach - sideways + row_width,
        ]
        layer_part = padded_weights[
            offset_index, window_reach - upward : window_reach - upward + layers
        ]
        result = result + layer_part[None, :, None] * shifted
    return result


def stiff_factors(direction):
    return jnp.array(
        [2.0 if component == direction else 1.0 for component in range(3)], jnp.float32
    ).reshape(3, 1, 1, 1)


def relax_slab(padded, displace, face_x, face_z, face_y, force_field, free_cells, diagonal):
    flux_x = stiff_factors(0) * face_x * jnp.diff(padded, axis=1)
    stencil_image = flux_x[:, :-1] - flux_x[:, 1:]
    flux_z = stiff_factors(1) * face_z * jnp.diff(displace, axis=2)
    stencil_image = stencil_image + pad_axis(flux_z, 2, 1, 0) - pad_axis(flux_z, 2, 0, 1)
    flux_y = stiff_factors(2) * face_y * jnp.diff(displace, axis=3)
    stencil_image = stencil_image + pad_axis(flux_y, 3, 1, 0) - pad_axis(flux_y, 3, 0, 1)
    return free_cells * (displace + relax_factor * (force_field - stencil_image) / diagonal)


def slab_energy(grid_field, along_axis, direction, load_cases):
    change = jnp.diff(grid_field, axis=along_axis)
    return jnp.sum(stiff_factors(direction) * change * change, axis=0) / load_cases


def neighbour_planes(displace, load_cases, axis_devices):
    if axis_devices > load_cases:
        below = from_behind(displace[:, -1:], "space", load_cases)
        above = from_behind(displace[:, :1], "space", -load_cases)
    else:
        below = jnp.zeros_like(displace[:, :1])
        above = jnp.zeros_like(displace[:, :1])
    return jnp.concatenate([below, displace, above], axis=1)


def many_slabs(density, displacement, fixed, load_index, load_force, radius):
    slab_rows, layers, row_width = density.shape
    load_cases = load_index.shape[0]
    level_count = load_cases.bit_length() - 1
    axis_devices = lax.axis_size("space")
    axis_place = lax.axis_index("space")
    slab_planes = slab_rows * load_cases
    slab_place = axis_place // load_cases
    load_place = axis_place % load_cases
    total_rows = slab_rows * axis_devices
    weights = layer_weights(radius)
    padded_weights = pad_axis(weights, 1, window_reach, window_reach)
    global_rows = (
        jnp.arange(slab_rows + 2 * window_reach, dtype=jnp.int32)
        + axis_place * slab_rows
        - window_reach
    )
    deep_inside = ((global_rows >= 0) & (global_rows < total_rows)).astype(jnp.float32)
    inside_field = deep_inside[:, None, None] * pad_sides(
        jnp.ones((slab_rows + 2 * window_reach, layers, row_width), jnp.float32)
    )
    total_weight = filter_forward(inside_field, weights)
    slab_start = slab_place * slab_planes
    margin_rows = jnp.arange(slab_planes + 2, dtype=jnp.int32) + slab_start - 1
    margin_inside = ((margin_rows >= 0) & (margin_rows < total_rows)).astype(jnp.float32)
    face_valid = margin_inside[1:] * margin_inside[:-1]
    fixed_slab = lax.dynamic_slice_in_dim(fixed, slab_start, slab_planes, 0).astype(jnp.float32)
    bottom_layer = (jnp.arange(layers, dtype=jnp.int32) == 0).astype(jnp.float32)
    free_cells = 1.0 - bottom_layer[None, :, None] * fixed_slab[:, None, :]
    slab_cells = slab_planes * layers * row_width
    cell_index = jnp.arange(slab_cells, dtype=jnp.int32) + slab_place * slab_cells
    load_hot = jnp.arange(load_cases, dtype=jnp.int32) == load_place
    own_index = jnp.sum(jnp.where(load_hot, load_index, 0))
    own_force = jnp.sum(load_hot.astype(jnp.float32)[:, None] * load_force, axis=0)
    load_hits = (cell_index == own_index).astype(jnp.float32)
    force_field = (own_force[:, None] * load_hits[None, :]).reshape(
        3, slab_planes, layers, row_width
    )
    displace = displacement[0] * free_cells
    target = volume_share * total_rows * layers * row_width
    padded = neighbour_planes(displace, load_cases, axis_devices)
    halo_density = extended(density, (("space", 0),), window_reach)
    filtered = filter_forward(pad_sides(halo_density), weights) / total_weight
    whole_field = lax.all_gather(filtered, "space", axis=0, tiled=True)
    margin = lax.dynamic_slice_in_dim(
        pad_axis(whole_field, 0, 1, 1), slab_start, slab_planes + 2, 0
    )
    moduli = floor_modulus + (1.0 - floor_modulus) * margin**3
    face_x = 0.5 * (moduli[1:] + moduli[:-1]) * face_valid[:, None, None]
    inner_moduli = moduli[1:-1]
    face_z = 0.5 * (inner_moduli[:, 1:] + inner_moduli[:, :-1])
    face_y = 0.5 * (inner_moduli[:, :, 1:] + inner_moduli[:, :, :-1])
    sum_x = face_x[:-1] + face_x[1:]
    sum_z = pad_axis(face_z, 1, 1, 0) + pad_axis(face_z, 1, 0, 1)
    sum_y = pad_axis(face_y, 2, 1, 0) + pad_axis(face_y, 2, 0, 1)
    diagonal = stiff_factors(0) * sum_x + stiff_factors(1) * sum_z + stiff_factors(2) * sum_y
    for sweep_index in range(SWEEPS):
        displace = relax_slab(
            padded, displace, face_x, face_z, face_y, force_field, free_cells, diagonal
        )
        padded = neighbour_planes(displace, load_cases, axis_devices)
    energy_x = slab_energy(padded, 1, 0, load_cases) * face_valid[:, None, None]
    energy_z = slab_energy(displace, 2, 1, load_cases)
    energy_y = slab_energy(displace, 3, 2, load_cases)
    sens_term = 0.5 * (
        energy_x[:-1]
        + energy_x[1:]
        + pad_axis(energy_z, 1, 1, 0)
        + pad_axis(energy_z, 1, 0, 1)
        + pad_axis(energy_y, 2, 1, 0)
        + pad_axis(energy_y, 2, 0, 1)
    )
    sensitive = sens_term
    for level in reversed(range(level_count)):
        half_rows = sensitive.shape[0] // 2
        upper_side = load_place // 2**level % 2 == 1
        outgoing = jnp.where(upper_side, sensitive[:half_rows], sensitive[half_rows:])
        keeping = jnp.where(upper_side, sensitive[half_rows:], sensitive[:half_rows])
        sensitive = keeping + from_partner(outgoing, "space", level)
    weighted_share = 3.0 * (1.0 - floor_modulus) * filtered**2 * sensitive / total_weight
    halo_share = extended(weighted_share, (("space", 0),), window_reach)
    root_term = jnp.sqrt(filter_backward(pad_sides(halo_share), padded_weights))
    lowest = jnp.maximum(density - move_limit, density_floor)
    highest = jnp.minimum(density + move_limit, 1.0)
    design_now = density

    def trial_design(log_level):
        return jnp.clip(design_now * root_term * jnp.exp(-0.5 * log_level), lowest, highest)

    start_state = (jnp.asarray(log_lower, jnp.float32), jnp.asarray(log_span, jnp.float32))

    def halve(search_step, search_state):
        lower_end, span_width = search_state
        half_span = span_width * 0.5
        middle = lower_end + half_span
        volume_total = lax.psum(jnp.sum(trial_design(middle)), "space")
        return (jnp.where(volume_total > target, middle, lower_end), half_span)

    lower_end, span_width = lax.fori_loop(0, SEARCH, halve, start_state)
    density = trial_design(lower_end + 0.5 * span_width)
    new_displacement = displace[None]
    return (density, new_displacement)


def solution(mesh):
    in_specs = (
        P("space", "parts", None),
        P("space", None, None, "parts", None),
        P(None, "parts"),
        P("parts"),
        P("parts", None),
        P("parts"),
    )
    out_specs = (P("space", "parts", None), P("space", None, None, "parts", None))

    def local(density, displacement, fixed, load_index, load_force, radius):
        alone = lax.axis_size("space") == load_index.shape[0]
        run = one_slab if alone else many_slabs
        return run(density, displacement, fixed, load_index, load_force, radius)

    return jax.shard_map(local, mesh=mesh, in_specs=in_specs, out_specs=out_specs, check_vma=False)
```

```python
import math

import jax
import jax.numpy as jnp
from jax import lax
from jax.experimental import pallas as pl
from jax.experimental.pallas import tpu as pltpu
from jax.sharding import PartitionSpec as P

SWEEPS = 3
SEARCH = 12


floor_modulus = 0.05
relax_factor = 0.6
move_limit = 0.2
density_floor = 0.01
volume_share = 0.5
log_lower = -16.0
log_span = 32.0
window_reach = 2

PLANE_SQUARES = (0, 1, 2, 4, 5, 8)
ALL_SQUARES = (0, 1, 2, 3, 4, 5, 6, 8, 9, 12)


def spot_iota(shape, dim):
    return lax.broadcasted_iota(jnp.int32, shape, dim)


def each_plane(planes, body, carry):
    for x in range(planes):
        carry = body(x, carry)
    return carry


def each_chunk(planes, count, body, carry):
    return lax.fori_loop(0, planes // count, lambda i, carry: body(i * count, carry), carry)


def layer_radius(radius_ref, layers, row_width):
    z = spot_iota((layers, row_width), 0)
    result = jnp.zeros((layers, row_width), jnp.int32)
    for layer in range(layers):
        result = jnp.where(z == layer, radius_ref[layer], result)
    return result.astype(jnp.float32)


def class_weights(radius_ref, weight_ref):
    layers, row_width = weight_ref.shape[1:]
    radial = layer_radius(radius_ref, layers, row_width)
    for place, square in enumerate(ALL_SQUARES):
        weight_ref[place] = jnp.maximum(radial - math.sqrt(square), 0.0)


def shift_sum(field, dim, distance):
    size = field.shape[dim]
    spot = spot_iota(field.shape, dim)
    ahead = jnp.where(spot < size - distance, pltpu.roll(field, size - distance, dim), 0.0)
    behind = jnp.where(spot >= distance, pltpu.roll(field, distance, dim), 0.0)
    return ahead + behind


def plane_sums(plane):
    beside = shift_sum(plane, 1, 1)
    further = shift_sum(plane, 1, 2)
    return {
        0: plane,
        1: beside + shift_sum(plane, 0, 1),
        2: shift_sum(beside, 0, 1),
        4: further + shift_sum(plane, 0, 2),
        5: shift_sum(further, 0, 1) + shift_sum(beside, 0, 2),
        8: shift_sum(further, 0, 2),
    }


def weigh(sums, weight_ref, square):
    result = None
    for inner in PLANE_SQUARES:
        term = weight_ref[ALL_SQUARES.index(inner + square)] * sums[inner]
        result = term if result is None else result + term
    return result


def forward_planes(plane, weight_ref):
    sums = plane_sums(plane)
    return [weigh(sums, weight_ref, square) for square in (0, 1, 4)]


def rows(x, layers, shift=0):
    return pl.ds(x * layers + shift, layers)


GAP = 8


def gapped(x, layers, shift=0):
    return pl.ds(GAP + x * (layers + GAP) + shift, layers)


def gap(x, layers):
    return pl.ds(x * (layers + GAP), GAP)


def edge_class(x, planes):
    return jnp.minimum(x, 2) + jnp.maximum(x - (planes - 3), 0)


def zero_edges(ref):
    planes = ref.shape[0]
    for place in (0, 1, planes - 2, planes - 1):
        ref[place] = jnp.zeros(ref.shape[1:], ref.dtype)


def group_spots(group, blocks):
    chips, own_planes = blocks.shape[:2]
    mine = lax.axis_index("space")
    core = mine ^ mine >> 1 ^ group
    return [
        (own_planes * (2 * chip + ((core ^ chip) & 1)) + own, (chip, own))
        for chip in range(chips)
        for own in range(own_planes)
    ]


def spread_group(blocks, spread):
    chips, own_planes, layers, row_width = blocks.shape
    zero_gap = jnp.zeros((GAP, row_width), jnp.float32)
    for ref in spread:
        ref[gap(0, layers)] = zero_gap
    for p in range(chips * own_planes):
        plane = blocks[p // own_planes, p % own_planes]
        for ref, field in zip(spread, (plane, shift_sum(plane, 1, 1), shift_sum(plane, 1, 2))):
            ref[gapped(p, layers)] = field
            ref[gap(p + 1, layers)] = zero_gap


def filter_plane(p, layers, spread, weight_ref):
    def around(place, distance):
        ref = spread[place]
        return ref[gapped(p, layers, distance)] + ref[gapped(p, layers, -distance)]

    sums = {
        0: spread[0][gapped(p, layers)],
        1: spread[1][gapped(p, layers)] + around(0, 1),
        2: around(1, 1),
        4: spread[2][gapped(p, layers)] + around(0, 2),
        5: around(2, 1) + around(1, 2),
        8: around(2, 2),
    }
    return [weigh(sums, weight_ref, square) for square in (0, 1, 4)]


def prepare_kernel(
    radius_hbm,
    index_hbm,
    force_hbm,
    fixed_hbm,
    density_ref,
    weight_ref,
    inverse_ref,
    free_ref,
    load_ref,
    spot_ref,
    filter_ref,
    radius_ref,
    index_ref,
    force_ref,
    fixed_ref,
    plane_ref,
    beside_ref,
    further_ref,
    arrived,
):
    copies = [
        pltpu.make_async_copy(source, target, arrived.at[place])
        for place, (source, target) in enumerate(
            (
                (radius_hbm, radius_ref),
                (index_hbm, index_ref),
                (force_hbm, force_ref),
                (fixed_hbm, fixed_ref),
            )
        )
    ]
    for copy in copies:
        copy.start()
    spread = (plane_ref, beside_ref, further_ref)
    spread_group(density_ref, spread)
    for copy in copies:
        copy.wait()
    planes, layers, row_width = free_ref.shape
    load_place = lax.axis_index("space")
    shape = (layers, row_width)
    z = spot_iota(shape, 0)
    y = spot_iota(shape, 1)

    class_weights(radius_ref, weight_ref)
    own_planes = density_ref.shape[1]
    for p in range(density_ref.shape[0] * own_planes):
        for place, field in enumerate(filter_plane(p, layers, spread, weight_ref)):
            filter_ref[place, p // own_planes, p % own_planes] = field

    ones = forward_planes(jnp.ones(shape, jnp.float32), weight_ref)
    for place, (lower, upper) in enumerate(((0, 2), (1, 2), (2, 2), (2, 1), (2, 0))):
        inverse_ref[place] = 1.0 / (
            ones[0] + min(lower, 1) * ones[1] + min(upper, 1) * ones[1]
            + (lower // 2) * ones[2] + (upper // 2) * ones[2]
        )

    def free_plane(x, carry):
        free_ref[x] = jnp.where(
            z == 0, 1.0 - fixed_ref[pl.ds(x, 1), :].astype(jnp.float32), 1.0
        )
        return carry

    each_plane(planes, free_plane, 0)

    own_index = index_ref[load_place]
    own_z = own_index // row_width % layers
    own_y = own_index % row_width
    hit = (z == own_z) & (y == own_y)
    for part in range(3):
        load_ref[part] = jnp.where(hit, force_ref[part, load_place], 0.0)
    own_x = (own_index // (layers * row_width)).astype(jnp.float32)
    spot_ref[...] = jnp.full(spot_ref.shape, own_x)


def sweep_kernel(
    spot_ref,
    load_ref,
    weight_ref,
    inverse_ref,
    free_ref,
    filter_ref,
    density_ref,
    start_ref,
    disp_ref,
    coef_ref,
    plane_ref,
    beside_ref,
    further_ref,
    near_ref,
    side_ref,
    far_ref,
    modulus_ref,
    across_ref,
    up_ref,
    right_ref,
    left_ref,
    rate_ref,
    first_ref,
):
    planes, layers, row_width = coef_ref.shape
    shape = (layers, row_width)
    z = spot_iota(shape, 0)
    y = spot_iota(shape, 1)
    zero = jnp.zeros(shape, jnp.float32)

    for ref in (side_ref, far_ref):
        zero_edges(ref)
    results = (near_ref, side_ref, far_ref)
    other_ref = density_ref.at[1]
    for x, spot in group_spots(0, other_ref):
        for place, ref in enumerate(results):
            ref[x + 2] = filter_ref[(place,) + spot]
    spread = (plane_ref, beside_ref, further_ref)
    spread_group(other_ref, spread)
    for p, (x, spot) in enumerate(group_spots(1, other_ref)):
        for ref, field in zip(results, filter_plane(p, layers, spread, weight_ref)):
            ref[x + 2] = field

    for ref in (first_ref, disp_ref):
        for part in range(3):
            ref[part, rows(0, layers)] = zero
            ref[part, rows(planes + 1, layers)] = zero

    def store_faces(slot, modulus, above, below, later, before, free, start, views):
        across, up_view, right_view, left_view, rate, source = views
        across[slot] = later
        up = jnp.where(z < layers - 1, 0.5 * (modulus + above), 0.0)
        right = jnp.where(
            y < row_width - 1, 0.5 * (modulus + pltpu.roll(modulus, row_width - 1, 1)), 0.0
        )
        left = jnp.where(y > 0, 0.5 * (modulus + pltpu.roll(modulus, 1, 1)), 0.0)
        down = jnp.where(z > 0, 0.5 * (modulus + below), 0.0)
        up_view[rows(slot, layers)] = up
        right_view[slot] = right
        left_view[slot] = left
        sums = (before + later, up + down, left + right)
        every = sums[0] + sums[1] + sums[2]
        diagonal = [every + part_sum for part_sum in sums]
        pair = diagonal[0] * diagonal[1]
        push = relax_factor * free / (pair * diagonal[2])
        side = push * diagonal[2]
        for part, factor in enumerate((side * diagonal[1], side * diagonal[0], push * pair)):
            rate[part, slot] = factor
            source[part, rows(slot, layers)] = start[part] * free

    piece = planes // 2

    def modulus_piece(first, carry):
        count = piece
        near = near_ref.at[pl.ds(first + 2, count)]
        side = side_ref.at[pl.ds(first + 1, count + 2)]
        far = far_ref.at[pl.ds(first, count + 4)]
        moduli = modulus_ref.at[pl.ds(first * layers, (count + 1) * layers)]
        coef = coef_ref.at[pl.ds(first, count)]
        free = free_ref.at[pl.ds(first, count)]
        views = (
            across_ref.at[pl.ds(first, count)],
            up_ref.at[pl.ds(first * layers, count * layers)],
            right_ref.at[pl.ds(first, count)],
            left_ref.at[pl.ds(first, count)],
            rate_ref.at[:, pl.ds(first, count)],
            first_ref.at[:, pl.ds(first * layers, count * layers)],
        )
        modulus, before = carry
        for p in range(count):
            inverse = inverse_ref[edge_class(first + p, planes)]
            filtered = near[p] + side[p] + side[p + 2] + far[p] + far[p + 4]
            filtered = filtered * inverse
            later = floor_modulus + (1.0 - floor_modulus) * (filtered * filtered * filtered)
            coef[p] = 3.0 * (1.0 - floor_modulus) * (filtered * filtered) * inverse
            moduli[rows(p + 1, layers)] = later
            ahead = 0.5 * (modulus + later)
            if p == 0:
                ahead = jnp.where(first > 0, ahead, 0.0)
            above = moduli[rows(p, layers, 1)] if p else pltpu.roll(modulus, layers - 1, 0)
            below = moduli[rows(p, layers, -1)] if p else pltpu.roll(modulus, 1, 0)
            previous = jnp.maximum(first + p - 1, 0)
            store_faces(
                p,
                modulus,
                above,
                below,
                ahead,
                before,
                free_ref[previous],
                [start_ref[part, previous] for part in range(3)],
                views,
            )
            modulus, before = later, ahead
        return modulus, before

    modulus, before = each_chunk(
        planes, piece, modulus_piece, (jnp.ones(shape, jnp.float32), zero)
    )
    store_faces(
        planes,
        modulus,
        pltpu.roll(modulus, layers - 1, 0),
        pltpu.roll(modulus, 1, 0),
        zero,
        before,
        free_ref[planes - 1],
        [start_ref[part, planes - 1] for part in range(3)],
        (across_ref, up_ref, right_ref, left_ref, rate_ref, first_ref),
    )

    own_x = jnp.max(spot_ref[...]).astype(jnp.int32)

    def sweep(source, target):
        def sweep_piece(first, carry):
            count = planes
            old = source.at[:, pl.ds(first * layers, (count + 2) * layers)]
            new = target.at[:, pl.ds((first + 1) * layers, count * layers)]
            across = across_ref.at[pl.ds(first, count + 1)]
            up = up_ref.at[pl.ds(first * layers, (count + 1) * layers)]
            right = right_ref.at[pl.ds(first + 1, count)]
            left = left_ref.at[pl.ds(first + 1, count)]
            rate = rate_ref.at[:, pl.ds(first + 1, count)]
            behind = [old[part, rows(0, layers)] for part in range(3)]
            here = [old[part, rows(1, layers)] for part in range(3)]
            for p in range(count):
                ahead = [old[part, rows(p + 2, layers)] for part in range(3)]
                for part in range(3):
                    pulls = [
                        across[p] * behind[part] + across[p + 1] * ahead[part],
                        up[rows(p + 1, layers)] * old[part, rows(p + 1, layers, 1)]
                        + up[rows(p + 1, layers, -1)] * old[part, rows(p + 1, layers, -1)],
                        right[p] * pltpu.roll(here[part], row_width - 1, 1)
                        + left[p] * pltpu.roll(here[part], 1, 1),
                    ]
                    pull = pulls[0] + pulls[1] + pulls[2] + pulls[part]
                    new[part, rows(p, layers)] = (
                        1.0 - relax_factor
                    ) * here[part] + rate[part, p] * pull
                behind, here = here, ahead
            return carry

        sweep_piece(0, 0)
        for part in range(3):
            target[part, rows(own_x + 1, layers)] += rate_ref[part, own_x + 1] * load_ref[part]

    def two_sweeps(turn, carry):
        sweep(first_ref, disp_ref)

        @pl.when(turn < SWEEPS // 2)
        def _():
            sweep(disp_ref, first_ref)

        return carry

    lax.fori_loop(0, SWEEPS // 2 + 1, two_sweeps, 0)


def filter_group(group, shares, weight_ref, near_ref, far_ref, result_ref):
    chips, own_planes, layers, row_width = result_ref.shape
    zero_gap = jnp.zeros((GAP, row_width), jnp.float32)
    mine = lax.axis_index("space")
    core = (mine ^ mine >> 1 ^ group) & 1
    count = shares[0].shape[0] - own_planes
    views = [
        [ref.at[pl.ds(own_planes * start, count)] for ref in shares] for start in (core, 1 - core)
    ]
    for ref in (near_ref, far_ref):
        ref[gap(0, layers)] = zero_gap
    for p in range(chips * own_planes):
        chip, own = p // own_planes, p % own_planes
        plane, beside, further = views[chip & 1]
        x = 2 * own_planes * chip + own + 2

        def around(ref, distance):
            return ref[x + distance] + ref[x - distance]

        sums = {
            0: plane[x],
            1: beside[x] + around(plane, 1),
            2: around(beside, 1),
            4: further[x] + around(plane, 2),
            5: around(further, 1) + around(beside, 2),
            8: around(further, 2),
        }
        level = weigh(sums, weight_ref, 0)
        for ref, square in ((near_ref, 1), (far_ref, 4)):
            ref[gapped(p, layers)] = weigh(sums, weight_ref, square)
            ref[gap(p + 1, layers)] = zero_gap
        result_ref[chip, own] = (
            level
            + near_ref[gapped(p, layers, 1)]
            + near_ref[gapped(p, layers, -1)]
            + far_ref[gapped(p, layers, 2)]
            + far_ref[gapped(p, layers, -2)]
        )


def share_kernel(
    disp_ref,
    coef_ref,
    weight_ref,
    sent_ref,
    plane_ref,
    beside_ref,
    further_ref,
    near_ref,
    far_ref,
):
    planes, layers, row_width = coef_ref.shape
    load_cases = lax.axis_size("space")
    shape = (layers, row_width)
    z = spot_iota(shape, 0)
    y = spot_iota(shape, 1)
    zero = jnp.zeros(shape, jnp.float32)
    shares = (plane_ref, beside_ref, further_ref)
    for ref in shares:
        zero_edges(ref)

    count = planes // 2

    def share_chunk(first, before):
        disp = disp_ref.at[:, pl.ds((first + 1) * layers, (count + 1) * layers)]
        coef = coef_ref.at[pl.ds(first, count)]
        plane, beside, further = (ref.at[pl.ds(first + 2, count)] for ref in shares)
        here = [disp[part, rows(0, layers)] for part in range(3)]
        for p in range(count):
            later = [disp[part, rows(p + 1, layers)] for part in range(3)]
            ahead, upward, right = zero, zero, zero
            for part in range(3):
                step = later[part] - here[part]
                climb = disp[part, rows(p, layers, 1)] - here[part]
                slide = pltpu.roll(here[part], row_width - 1, 1) - here[part]
                ahead = ahead + (2.0 if part == 0 else 1.0) * (step * step)
                upward = upward + (2.0 if part == 1 else 1.0) * (climb * climb)
                right = right + (2.0 if part == 2 else 1.0) * (slide * slide)
            if p == count - 1:
                ahead = jnp.where(first + count < planes, ahead, 0.0)
            upward = jnp.where(z < layers - 1, upward, 0.0)
            right = jnp.where(y < row_width - 1, right, 0.0)
            total = before + ahead + upward + pltpu.roll(upward, 1, 0)
            total = total + right + pltpu.roll(right, 1, 1)
            share = (0.5 / load_cases) * total * coef[p]
            plane[p] = share
            beside[p] = shift_sum(share, 1, 1)
            further[p] = shift_sum(share, 1, 2)
            before, here = ahead, later
        return before

    each_chunk(planes, count, share_chunk, zero)
    filter_group(1, shares, weight_ref, near_ref, far_ref, sent_ref)


def kept_kernel(
    disp_ref,
    weight_ref,
    plane_ref,
    beside_ref,
    further_ref,
    disp_hbm,
    kept_ref,
    near_ref,
    far_ref,
    stored,
):
    layers = kept_ref.shape[2]
    inner = pl.ds(layers, disp_ref.shape[1] - 2 * layers)
    store = pltpu.make_async_copy(disp_ref.at[:, inner], disp_hbm, stored)
    store.start()
    shares = (plane_ref, beside_ref, further_ref)
    filter_group(0, shares, weight_ref, near_ref, far_ref, kept_ref)
    store.wait()


def design_kernel(root_ref, density_ref, new_ref, pull_ref, low_ref, high_ref):
    groups, chips, own_planes, layers, row_width = density_ref.shape
    own_chip = lax.axis_index("space") >> 1
    shape = (layers, row_width)
    zero = jnp.zeros(shape, jnp.float32)
    planes = [
        (group, chip, own)
        for group in range(groups)
        for chip in range(chips)
        for own in range(own_planes)
    ]
    for spot in planes:
        density = density_ref[spot]
        pull_ref[spot] = density * root_ref[spot]
        low_ref[spot] = jnp.maximum(density - move_limit, density_floor)
        high_ref[spot] = jnp.minimum(density + move_limit, 1.0)

    target = volume_share * len(planes) * layers * row_width

    def factor_of(log_level):
        return jnp.broadcast_to(jnp.exp(-0.5 * log_level), shape)

    def exceeds(total):
        return jnp.sum(jnp.sum(total, axis=0, keepdims=True), axis=1, keepdims=True) > target

    def halve_twice(step, state):
        lower, span = state
        half, quarter = span * 0.5, span * 0.25
        middles = (lower + quarter, lower + half, lower + half + quarter)
        factors = [factor_of(middle) for middle in middles]
        totals = [zero, zero, zero]
        for spot in planes:
            pull, low, high = pull_ref[spot], low_ref[spot], high_ref[spot]
            totals = [
                total + jnp.minimum(jnp.maximum(pull * factor, low), high)
                for total, factor in zip(totals, factors)
            ]
        first, second, third = (exceeds(total) for total in totals)
        upper = jnp.where(third, middles[2], middles[1])
        below = jnp.where(first, middles[0], lower)
        return jnp.where(second, upper, below), quarter

    start = (jnp.full((1, 1), log_lower, jnp.float32), jnp.full((1, 1), log_span, jnp.float32))
    lower, span = lax.fori_loop(0, SEARCH // 2, halve_twice, start)
    factor = factor_of(lower + 0.5 * span)
    for own in range(own_planes):
        spot = (0, own_chip, own)
        new_ref[own] = jnp.minimum(
            jnp.maximum(pull_ref[spot] * factor, low_ref[spot]), high_ref[spot]
        )


def in_vmem():
    return pl.BlockSpec(memory_space=pltpu.VMEM)


KERNEL_VMEM = 24 * 2**20


def floats(*shape):
    return jax.ShapeDtypeStruct(shape, jnp.float32)


def prepare_call(density, radius, load_index, load_force, fixed):
    chips, own_planes, layers, row_width = density.shape
    planes = fixed.shape[0]
    spread = pltpu.VMEM((chips * own_planes * (layers + GAP) + GAP, row_width), jnp.float32)
    return pl.pallas_call(
        prepare_kernel,
        out_shape=[
            floats(len(ALL_SQUARES), layers, row_width),
            floats(2 * window_reach + 1, layers, row_width),
            floats(planes, layers, row_width),
            floats(3, layers, row_width),
            floats(8, row_width),
            floats(3, *density.shape),
        ],
        in_specs=[pl.BlockSpec(memory_space=pltpu.HBM)] * 4 + [in_vmem()],
        out_specs=[in_vmem()] * 6,
        scratch_shapes=[
            pltpu.SMEM(radius.shape, radius.dtype),
            pltpu.SMEM(load_index.shape, load_index.dtype),
            pltpu.SMEM(load_force.shape, load_force.dtype),
            pltpu.VMEM(fixed.shape, fixed.dtype),
            spread,
            spread,
            spread,
            pltpu.SemaphoreType.DMA((4,)),
        ],
        compiler_params=pltpu.CompilerParams(vmem_limit_bytes=KERNEL_VMEM),
        cost_estimate=pl.CostEstimate(
            flops=80 * planes * layers * row_width,
            bytes_accessed=8 * planes * layers * row_width,
            transcendentals=0,
        ),
        name="prepare",
    )(
        *(
            pltpu.with_memory_space_constraint(array, pltpu.HBM)
            for array in (radius, load_index, load_force, fixed)
        ),
        density,
    )


def sweep_call(spot, load, weights, inverses, free, filtered, density, displacement):
    groups, chips, own_planes, layers, row_width = density.shape
    planes = groups * chips * own_planes

    def scratch(*lead):
        return pltpu.VMEM(lead + (row_width,), jnp.float32)

    return pl.pallas_call(
        sweep_kernel,
        out_shape=[
            floats(3, (planes + 2) * layers, row_width),
            floats(planes, layers, row_width),
        ],
        in_specs=[in_vmem()] * 8,
        out_specs=[in_vmem()] * 2,
        scratch_shapes=[
            scratch(planes // 2 * (layers + GAP) + GAP),
            scratch(planes // 2 * (layers + GAP) + GAP),
            scratch(planes // 2 * (layers + GAP) + GAP),
            scratch(planes + 4, layers),
            scratch(planes + 4, layers),
            scratch(planes + 4, layers),
            scratch((planes + 1) * layers),
            scratch(planes + 1, layers),
            scratch((planes + 1) * layers),
            scratch(planes + 1, layers),
            scratch(planes + 1, layers),
            scratch(3, planes + 1, layers),
            scratch(3, (planes + 2) * layers),
        ],
        compiler_params=pltpu.CompilerParams(vmem_limit_bytes=KERNEL_VMEM),
        name="sweeps",
    )(spot, load, weights, inverses, free, filtered, density, displacement)


def share_call(disp, coef, weights, group_shape):
    planes, layers, row_width = coef.shape
    gaps = pltpu.VMEM((planes // 2 * (layers + GAP) + GAP, row_width), jnp.float32)
    return pl.pallas_call(
        share_kernel,
        out_shape=[floats(*group_shape)] + [floats(planes + 4, layers, row_width)] * 3,
        in_specs=[in_vmem()] * 3,
        out_specs=[in_vmem()] * 4,
        scratch_shapes=[gaps, gaps],
        compiler_params=pltpu.CompilerParams(vmem_limit_bytes=KERNEL_VMEM),
        name="share",
    )(disp, coef, weights)


def kept_call(disp, weights, shares, group_shape):
    parts, disp_rows, row_width = disp.shape
    chips, own_planes, layers = group_shape[:3]
    gaps = pltpu.VMEM((chips * own_planes * (layers + GAP) + GAP, row_width), jnp.float32)
    return pl.pallas_call(
        kept_kernel,
        out_shape=[floats(parts, disp_rows - 2 * layers, row_width), floats(*group_shape)],
        in_specs=[in_vmem()] * 5,
        out_specs=[pl.BlockSpec(memory_space=pltpu.HBM), in_vmem()],
        scratch_shapes=[gaps, gaps, pltpu.SemaphoreType.DMA(())],
        compiler_params=pltpu.CompilerParams(vmem_limit_bytes=KERNEL_VMEM),
        cost_estimate=pl.CostEstimate(
            flops=20 * disp.size, bytes_accessed=8 * disp.size, transcendentals=0
        ),
        name="kept",
    )(disp, weights, *shares)


def design_call(root, density):
    return pl.pallas_call(
        design_kernel,
        out_shape=floats(*density.shape[2:]),
        in_specs=[in_vmem()] * 2,
        out_specs=in_vmem(),
        scratch_shapes=[pltpu.VMEM(density.shape, jnp.float32)] * 3,
        compiler_params=pltpu.CompilerParams(vmem_limit_bytes=KERNEL_VMEM),
        name="design",
    )(root, density)


def other_core(block):
    devices = lax.axis_size("space")
    return lax.ppermute(block, "space", [(i, i ^ 1) for i in range(devices)])


def chip_groups():
    chips = lax.axis_size("space") // 2
    return [[2 * chip + (chip ^ group) % 2 for chip in range(chips)] for group in range(2)]


def between_chips(pieces):
    return lax.all_to_all(pieces, "space", 0, 0, axis_index_groups=chip_groups())


def chip_gathered(block):
    chips = lax.axis_size("space") // 2
    return between_chips(jnp.broadcast_to(block[None], (chips,) + block.shape))


def with_other_core(blocks):
    return jnp.stack([blocks, other_core(blocks)])


def scattered_sum(sent, make_kept):
    received = other_core(sent)
    *others, kept = make_kept()
    return jnp.sum(between_chips(kept + received), axis=0), others


def one_slab(density, displacement, fixed, load_index, load_force, radius):
    same_group, small = lax.optimization_barrier(
        (chip_gathered(density), (radius, load_index, load_force.T, fixed))
    )
    other_group = other_core(same_group)
    weights, inverses, free, load, spot, filtered = prepare_call(same_group, *small)
    whole = jnp.stack([same_group, other_group])
    disp, coef = sweep_call(
        spot, load, weights, inverses, free, filtered, whole, displacement[0]
    )
    sent, *shares = share_call(disp, coef, weights, same_group.shape)
    sent, disp, shares = lax.optimization_barrier((sent, disp, shares))
    squares, (new_displacement,) = scattered_sum(
        sent, lambda: kept_call(disp, weights, shares, same_group.shape)
    )
    root = with_other_core(chip_gathered(jnp.sqrt(squares)))
    new_density = design_call(root, whole)
    return new_density, new_displacement.reshape(displacement.shape)


def from_behind(block, axis, distance):
    devices = range(lax.axis_size(axis))
    route = [(i - distance, i) for i in devices if i - distance in devices]
    return lax.ppermute(block, axis, route)


def extended(x, sides, width):
    for axis, dim in sides:
        size, length = (lax.axis_size(axis), x.shape[dim])
        up = [(i, (i + 1) % size) for i in range(size - 1)]
        down = [(j, i) for i, j in up]
        last = lax.slice_in_dim(x, length - width, length, axis=dim)
        first = lax.slice_in_dim(x, 0, width, axis=dim)
        before = lax.ppermute(last, axis, up)
        after = lax.ppermute(first, axis, down)
        x = jnp.concatenate([before, x, after], axis=dim)
    return x


def from_partner(x, axis, bit):
    return lax.ppermute(x, axis, [(i, i ^ 1 << bit) for i in range(lax.axis_size(axis))])


def window_offsets():
    offsets_list = []
    for across in range(-window_reach, window_reach + 1):
        for upward in range(-window_reach, window_reach + 1):
            for sideways in range(-window_reach, window_reach + 1):
                length = math.sqrt(across * across + upward * upward + sideways * sideways)
                offsets_list.append((across, upward, sideways, length))
    return offsets_list


def layer_weights(radius):
    radial = radius.astype(jnp.float32)
    return jnp.stack(
        [jnp.maximum(radial - length, 0.0) for across, upward, sideways, length in window_offsets()]
    )


def pad_axis(grid_field, along_axis, before, after_cells):
    widths = [(0, 0)] * grid_field.ndim
    widths[along_axis] = (before, after_cells)
    return jnp.pad(grid_field, widths)


def pad_sides(grid_field):
    return jnp.pad(grid_field, ((0, 0), (window_reach, window_reach), (window_reach, window_reach)))


def filter_forward(padded, weights):
    out_rows = padded.shape[0] - 2 * window_reach
    layers = padded.shape[1] - 2 * window_reach
    row_width = padded.shape[2] - 2 * window_reach
    result = jnp.zeros((out_rows, layers, row_width), jnp.float32)
    for offset_index, (across, upward, sideways, length) in enumerate(window_offsets()):
        shifted = padded[
            window_reach + across : window_reach + across + out_rows,
            window_reach + upward : window_reach + upward + layers,
            window_reach + sideways : window_reach + sideways + row_width,
        ]
        result = result + weights[offset_index][None, :, None] * shifted
    return result


def filter_backward(padded, padded_weights):
    out_rows = padded.shape[0] - 2 * window_reach
    layers = padded.shape[1] - 2 * window_reach
    row_width = padded.shape[2] - 2 * window_reach
    result = jnp.zeros((out_rows, layers, row_width), jnp.float32)
    for offset_index, (across, upward, sideways, length) in enumerate(window_offsets()):
        shifted = padded[
            window_reach - across : window_reach - across + out_rows,
            window_reach - upward : window_reach - upward + layers,
            window_reach - sideways : window_reach - sideways + row_width,
        ]
        layer_part = padded_weights[
            offset_index, window_reach - upward : window_reach - upward + layers
        ]
        result = result + layer_part[None, :, None] * shifted
    return result


def stiff_factors(direction):
    return jnp.array(
        [2.0 if component == direction else 1.0 for component in range(3)], jnp.float32
    ).reshape(3, 1, 1, 1)


def relax_slab(padded, displace, face_x, face_z, face_y, force_field, free_cells, diagonal):
    flux_x = stiff_factors(0) * face_x * jnp.diff(padded, axis=1)
    stencil_image = flux_x[:, :-1] - flux_x[:, 1:]
    flux_z = stiff_factors(1) * face_z * jnp.diff(displace, axis=2)
    stencil_image = stencil_image + pad_axis(flux_z, 2, 1, 0) - pad_axis(flux_z, 2, 0, 1)
    flux_y = stiff_factors(2) * face_y * jnp.diff(displace, axis=3)
    stencil_image = stencil_image + pad_axis(flux_y, 3, 1, 0) - pad_axis(flux_y, 3, 0, 1)
    return free_cells * (displace + relax_factor * (force_field - stencil_image) / diagonal)


def slab_energy(grid_field, along_axis, direction, load_cases):
    change = jnp.diff(grid_field, axis=along_axis)
    return jnp.sum(stiff_factors(direction) * change * change, axis=0) / load_cases


def neighbour_planes(displace, load_cases, axis_devices):
    if axis_devices > load_cases:
        below = from_behind(displace[:, -1:], "space", load_cases)
        above = from_behind(displace[:, :1], "space", -load_cases)
    else:
        below = jnp.zeros_like(displace[:, :1])
        above = jnp.zeros_like(displace[:, :1])
    return jnp.concatenate([below, displace, above], axis=1)


def many_slabs(density, displacement, fixed, load_index, load_force, radius):
    slab_rows, layers, row_width = density.shape
    load_cases = load_index.shape[0]
    level_count = load_cases.bit_length() - 1
    axis_devices = lax.axis_size("space")
    axis_place = lax.axis_index("space")
    slab_planes = slab_rows * load_cases
    slab_place = axis_place // load_cases
    load_place = axis_place % load_cases
    total_rows = slab_rows * axis_devices
    weights = layer_weights(radius)
    padded_weights = pad_axis(weights, 1, window_reach, window_reach)
    global_rows = (
        jnp.arange(slab_rows + 2 * window_reach, dtype=jnp.int32)
        + axis_place * slab_rows
        - window_reach
    )
    deep_inside = ((global_rows >= 0) & (global_rows < total_rows)).astype(jnp.float32)
    inside_field = deep_inside[:, None, None] * pad_sides(
        jnp.ones((slab_rows + 2 * window_reach, layers, row_width), jnp.float32)
    )
    total_weight = filter_forward(inside_field, weights)
    slab_start = slab_place * slab_planes
    margin_rows = jnp.arange(slab_planes + 2, dtype=jnp.int32) + slab_start - 1
    margin_inside = ((margin_rows >= 0) & (margin_rows < total_rows)).astype(jnp.float32)
    face_valid = margin_inside[1:] * margin_inside[:-1]
    fixed_slab = lax.dynamic_slice_in_dim(fixed, slab_start, slab_planes, 0).astype(jnp.float32)
    bottom_layer = (jnp.arange(layers, dtype=jnp.int32) == 0).astype(jnp.float32)
    free_cells = 1.0 - bottom_layer[None, :, None] * fixed_slab[:, None, :]
    slab_cells = slab_planes * layers * row_width
    cell_index = jnp.arange(slab_cells, dtype=jnp.int32) + slab_place * slab_cells
    load_hot = jnp.arange(load_cases, dtype=jnp.int32) == load_place
    own_index = jnp.sum(jnp.where(load_hot, load_index, 0))
    own_force = jnp.sum(load_hot.astype(jnp.float32)[:, None] * load_force, axis=0)
    load_hits = (cell_index == own_index).astype(jnp.float32)
    force_field = (own_force[:, None] * load_hits[None, :]).reshape(
        3, slab_planes, layers, row_width
    )
    displace = displacement[0] * free_cells
    target = volume_share * total_rows * layers * row_width
    padded = neighbour_planes(displace, load_cases, axis_devices)
    halo_density = extended(density, (("space", 0),), window_reach)
    filtered = filter_forward(pad_sides(halo_density), weights) / total_weight
    whole_field = lax.all_gather(filtered, "space", axis=0, tiled=True)
    margin = lax.dynamic_slice_in_dim(
        pad_axis(whole_field, 0, 1, 1), slab_start, slab_planes + 2, 0
    )
    moduli = floor_modulus + (1.0 - floor_modulus) * margin**3
    face_x = 0.5 * (moduli[1:] + moduli[:-1]) * face_valid[:, None, None]
    inner_moduli = moduli[1:-1]
    face_z = 0.5 * (inner_moduli[:, 1:] + inner_moduli[:, :-1])
    face_y = 0.5 * (inner_moduli[:, :, 1:] + inner_moduli[:, :, :-1])
    sum_x = face_x[:-1] + face_x[1:]
    sum_z = pad_axis(face_z, 1, 1, 0) + pad_axis(face_z, 1, 0, 1)
    sum_y = pad_axis(face_y, 2, 1, 0) + pad_axis(face_y, 2, 0, 1)
    diagonal = stiff_factors(0) * sum_x + stiff_factors(1) * sum_z + stiff_factors(2) * sum_y
    for sweep_index in range(SWEEPS):
        displace = relax_slab(
            padded, displace, face_x, face_z, face_y, force_field, free_cells, diagonal
        )
        padded = neighbour_planes(displace, load_cases, axis_devices)
    energy_x = slab_energy(padded, 1, 0, load_cases) * face_valid[:, None, None]
    energy_z = slab_energy(displace, 2, 1, load_cases)
    energy_y = slab_energy(displace, 3, 2, load_cases)
    sens_term = 0.5 * (
        energy_x[:-1]
        + energy_x[1:]
        + pad_axis(energy_z, 1, 1, 0)
        + pad_axis(energy_z, 1, 0, 1)
        + pad_axis(energy_y, 2, 1, 0)
        + pad_axis(energy_y, 2, 0, 1)
    )
    sensitive = sens_term
    for level in reversed(range(level_count)):
        half_rows = sensitive.shape[0] // 2
        upper_side = load_place // 2**level % 2 == 1
        outgoing = jnp.where(upper_side, sensitive[:half_rows], sensitive[half_rows:])
        keeping = jnp.where(upper_side, sensitive[half_rows:], sensitive[:half_rows])
        sensitive = keeping + from_partner(outgoing, "space", level)
    weighted_share = 3.0 * (1.0 - floor_modulus) * filtered**2 * sensitive / total_weight
    halo_share = extended(weighted_share, (("space", 0),), window_reach)
    root_term = jnp.sqrt(filter_backward(pad_sides(halo_share), padded_weights))
    lowest = jnp.maximum(density - move_limit, density_floor)
    highest = jnp.minimum(density + move_limit, 1.0)
    design_now = density

    def trial_design(log_level):
        return jnp.clip(design_now * root_term * jnp.exp(-0.5 * log_level), lowest, highest)

    start_state = (jnp.asarray(log_lower, jnp.float32), jnp.asarray(log_span, jnp.float32))

    def halve(search_step, search_state):
        lower_end, span_width = search_state
        half_span = span_width * 0.5
        middle = lower_end + half_span
        volume_total = lax.psum(jnp.sum(trial_design(middle)), "space")
        return (jnp.where(volume_total > target, middle, lower_end), half_span)

    lower_end, span_width = lax.fori_loop(0, SEARCH, halve, start_state)
    density = trial_design(lower_end + 0.5 * span_width)
    new_displacement = displace[None]
    return (density, new_displacement)


def solution(mesh):
    in_specs = (
        P("space", "parts", None),
        P("space", None, None, "parts", None),
        P(None, "parts"),
        P("parts"),
        P("parts", None),
        P("parts"),
    )
    out_specs = (P("space", "parts", None), P("space", None, None, "parts", None))

    def local(density, displacement, fixed, load_index, load_force, radius):
        alone = lax.axis_size("space") == load_index.shape[0]
        run = one_slab if alone else many_slabs
        return run(density, displacement, fixed, load_index, load_force, radius)

    return jax.shard_map(local, mesh=mesh, in_specs=in_specs, out_specs=out_specs, check_vma=False)
```

```python
import math

import jax
import jax.numpy as jnp
from jax import lax
from jax.experimental import pallas as pl
from jax.experimental.pallas import tpu as pltpu
from jax.sharding import PartitionSpec as P

SWEEPS = 3
SEARCH = 12


floor_modulus = 0.05
relax_factor = 0.6
move_limit = 0.2
density_floor = 0.01
volume_share = 0.5
log_lower = -16.0
log_span = 32.0
window_reach = 2

PLANE_SQUARES = (0, 1, 2, 4, 5, 8)
ALL_SQUARES = (0, 1, 2, 3, 4, 5, 6, 8, 9, 12)


def spot_iota(shape, dim):
    return lax.broadcasted_iota(jnp.int32, shape, dim)


def each_plane(planes, body, carry):
    for x in range(planes):
        carry = body(x, carry)
    return carry


def each_chunk(planes, count, body, carry):
    return lax.fori_loop(0, planes // count, lambda i, carry: body(i * count, carry), carry)


def layer_radius(radius_ref, layers, row_width):
    z = spot_iota((layers, row_width), 0)
    result = jnp.zeros((layers, row_width), jnp.int32)
    for layer in range(layers):
        result = jnp.where(z == layer, radius_ref[layer], result)
    return result.astype(jnp.float32)


def class_weights(radius_ref, weight_ref):
    layers, row_width = weight_ref.shape[1:]
    radial = layer_radius(radius_ref, layers, row_width)
    for place, square in enumerate(ALL_SQUARES):
        weight_ref[place] = jnp.maximum(radial - math.sqrt(square), 0.0)


def shift_sum(field, dim, distance):
    size = field.shape[dim]
    spot = spot_iota(field.shape, dim)
    ahead = jnp.where(spot < size - distance, pltpu.roll(field, size - distance, dim), 0.0)
    behind = jnp.where(spot >= distance, pltpu.roll(field, distance, dim), 0.0)
    return ahead + behind


def plane_sums(plane):
    beside = shift_sum(plane, 1, 1)
    further = shift_sum(plane, 1, 2)
    return {
        0: plane,
        1: beside + shift_sum(plane, 0, 1),
        2: shift_sum(beside, 0, 1),
        4: further + shift_sum(plane, 0, 2),
        5: shift_sum(further, 0, 1) + shift_sum(beside, 0, 2),
        8: shift_sum(further, 0, 2),
    }


def weigh(sums, weight_ref, square):
    result = None
    for inner in PLANE_SQUARES:
        term = weight_ref[ALL_SQUARES.index(inner + square)] * sums[inner]
        result = term if result is None else result + term
    return result


def forward_planes(plane, weight_ref):
    sums = plane_sums(plane)
    return [weigh(sums, weight_ref, square) for square in (0, 1, 4)]


def rows(x, layers, shift=0):
    return pl.ds(x * layers + shift, layers)


GAP = 8


def gapped(x, layers, shift=0):
    return pl.ds(GAP + x * (layers + GAP) + shift, layers)


def gap(x, layers):
    return pl.ds(x * (layers + GAP), GAP)


def edge_class(x, planes):
    return jnp.minimum(x, 2) + jnp.maximum(x - (planes - 3), 0)


def zero_edges(ref):
    planes = ref.shape[0]
    for place in (0, 1, planes - 2, planes - 1):
        ref[place] = jnp.zeros(ref.shape[1:], ref.dtype)


def far_half(chip):
    return chip * 4 // lax.axis_size("space")


def own_core(group):
    mine = lax.axis_index("space")
    return (mine ^ far_half(mine >> 1) ^ group) & 1


def group_spots(group, blocks):
    chips, own_planes = blocks.shape[:2]
    core = own_core(group)
    return [
        (own_planes * (2 * chip + (core ^ far_half(chip))) + own, (chip, own))
        for chip in range(chips)
        for own in range(own_planes)
    ]


def spread_group(blocks, spread):
    chips, own_planes, layers, row_width = blocks.shape
    zero_gap = jnp.zeros((GAP, row_width), jnp.float32)
    for ref in spread:
        ref[gap(0, layers)] = zero_gap
    for p in range(chips * own_planes):
        plane = blocks[p // own_planes, p % own_planes]
        for ref, field in zip(spread, (plane, shift_sum(plane, 1, 1), shift_sum(plane, 1, 2))):
            ref[gapped(p, layers)] = field
            ref[gap(p + 1, layers)] = zero_gap


def filter_plane(p, layers, spread, weight_ref):
    def around(place, distance):
        ref = spread[place]
        return ref[gapped(p, layers, distance)] + ref[gapped(p, layers, -distance)]

    sums = {
        0: spread[0][gapped(p, layers)],
        1: spread[1][gapped(p, layers)] + around(0, 1),
        2: around(1, 1),
        4: spread[2][gapped(p, layers)] + around(0, 2),
        5: around(2, 1) + around(1, 2),
        8: around(2, 2),
    }
    return [weigh(sums, weight_ref, square) for square in (0, 1, 4)]


def prepare_kernel(
    radius_hbm,
    index_hbm,
    force_hbm,
    fixed_hbm,
    density_ref,
    weight_ref,
    inverse_ref,
    free_ref,
    load_ref,
    spot_ref,
    filter_ref,
    radius_ref,
    index_ref,
    force_ref,
    fixed_ref,
    plane_ref,
    beside_ref,
    further_ref,
    arrived,
):
    copies = [
        pltpu.make_async_copy(source, target, arrived.at[place])
        for place, (source, target) in enumerate(
            (
                (radius_hbm, radius_ref),
                (index_hbm, index_ref),
                (force_hbm, force_ref),
                (fixed_hbm, fixed_ref),
            )
        )
    ]
    for copy in copies:
        copy.start()
    spread = (plane_ref, beside_ref, further_ref)
    spread_group(density_ref, spread)
    for copy in copies:
        copy.wait()
    planes, layers, row_width = free_ref.shape
    load_place = lax.axis_index("space")
    shape = (layers, row_width)
    z = spot_iota(shape, 0)
    y = spot_iota(shape, 1)

    class_weights(radius_ref, weight_ref)
    own_planes = density_ref.shape[1]
    for p in range(density_ref.shape[0] * own_planes):
        for place, field in enumerate(filter_plane(p, layers, spread, weight_ref)):
            filter_ref[place, p // own_planes, p % own_planes] = field

    ones = forward_planes(jnp.ones(shape, jnp.float32), weight_ref)
    for place, (lower, upper) in enumerate(((0, 2), (1, 2), (2, 2), (2, 1), (2, 0))):
        inverse_ref[place] = 1.0 / (
            ones[0] + min(lower, 1) * ones[1] + min(upper, 1) * ones[1]
            + (lower // 2) * ones[2] + (upper // 2) * ones[2]
        )

    def free_plane(x, carry):
        free_ref[x] = jnp.where(
            z == 0, 1.0 - fixed_ref[pl.ds(x, 1), :].astype(jnp.float32), 1.0
        )
        return carry

    each_plane(planes, free_plane, 0)

    own_index = index_ref[load_place]
    own_z = own_index // row_width % layers
    own_y = own_index % row_width
    hit = (z == own_z) & (y == own_y)
    for part in range(3):
        load_ref[part] = jnp.where(hit, force_ref[part, load_place], 0.0)
    own_x = (own_index // (layers * row_width)).astype(jnp.float32)
    spot_ref[...] = jnp.full(spot_ref.shape, own_x)


def sweep_kernel(
    spot_ref,
    load_ref,
    weight_ref,
    inverse_ref,
    free_ref,
    filter_ref,
    density_ref,
    start_ref,
    disp_ref,
    coef_ref,
    plane_ref,
    beside_ref,
    further_ref,
    near_ref,
    side_ref,
    far_ref,
    modulus_ref,
    across_ref,
    up_ref,
    right_ref,
    left_ref,
    rate_ref,
    first_ref,
):
    planes, layers, row_width = coef_ref.shape
    shape = (layers, row_width)
    z = spot_iota(shape, 0)
    y = spot_iota(shape, 1)
    zero = jnp.zeros(shape, jnp.float32)

    for ref in (side_ref, far_ref):
        zero_edges(ref)
    results = (near_ref, side_ref, far_ref)
    other_ref = density_ref.at[1]
    for x, spot in group_spots(0, other_ref):
        for place, ref in enumerate(results):
            ref[x + 2] = filter_ref[(place,) + spot]
    spread = (plane_ref, beside_ref, further_ref)
    spread_group(other_ref, spread)
    for p, (x, spot) in enumerate(group_spots(1, other_ref)):
        for ref, field in zip(results, filter_plane(p, layers, spread, weight_ref)):
            ref[x + 2] = field

    for ref in (first_ref, disp_ref):
        for part in range(3):
            ref[part, rows(0, layers)] = zero
            ref[part, rows(planes + 1, layers)] = zero

    def store_faces(slot, modulus, above, below, later, before, free, start, views):
        across, up_view, right_view, left_view, rate, source = views
        across[slot] = later
        up = jnp.where(z < layers - 1, 0.5 * (modulus + above), 0.0)
        right = jnp.where(
            y < row_width - 1, 0.5 * (modulus + pltpu.roll(modulus, row_width - 1, 1)), 0.0
        )
        left = jnp.where(y > 0, 0.5 * (modulus + pltpu.roll(modulus, 1, 1)), 0.0)
        down = jnp.where(z > 0, 0.5 * (modulus + below), 0.0)
        up_view[rows(slot, layers)] = up
        right_view[slot] = right
        left_view[slot] = left
        sums = (before + later, up + down, left + right)
        every = sums[0] + sums[1] + sums[2]
        diagonal = [every + part_sum for part_sum in sums]
        pair = diagonal[0] * diagonal[1]
        push = relax_factor * free / (pair * diagonal[2])
        side = push * diagonal[2]
        for part, factor in enumerate((side * diagonal[1], side * diagonal[0], push * pair)):
            rate[part, slot] = factor
            source[part, rows(slot, layers)] = start[part] * free

    piece = planes // 2

    def modulus_piece(first, carry):
        count = piece
        near = near_ref.at[pl.ds(first + 2, count)]
        side = side_ref.at[pl.ds(first + 1, count + 2)]
        far = far_ref.at[pl.ds(first, count + 4)]
        moduli = modulus_ref.at[pl.ds(first * layers, (count + 1) * layers)]
        coef = coef_ref.at[pl.ds(first, count)]
        free = free_ref.at[pl.ds(first, count)]
        views = (
            across_ref.at[pl.ds(first, count)],
            up_ref.at[pl.ds(first * layers, count * layers)],
            right_ref.at[pl.ds(first, count)],
            left_ref.at[pl.ds(first, count)],
            rate_ref.at[:, pl.ds(first, count)],
            first_ref.at[:, pl.ds(first * layers, count * layers)],
        )
        modulus, before = carry
        for p in range(count):
            inverse = inverse_ref[edge_class(first + p, planes)]
            filtered = near[p] + side[p] + side[p + 2] + far[p] + far[p + 4]
            filtered = filtered * inverse
            later = floor_modulus + (1.0 - floor_modulus) * (filtered * filtered * filtered)
            coef[p] = 3.0 * (1.0 - floor_modulus) * (filtered * filtered) * inverse
            moduli[rows(p + 1, layers)] = later
            ahead = 0.5 * (modulus + later)
            if p == 0:
                ahead = jnp.where(first > 0, ahead, 0.0)
            above = moduli[rows(p, layers, 1)] if p else pltpu.roll(modulus, layers - 1, 0)
            below = moduli[rows(p, layers, -1)] if p else pltpu.roll(modulus, 1, 0)
            previous = jnp.maximum(first + p - 1, 0)
            store_faces(
                p,
                modulus,
                above,
                below,
                ahead,
                before,
                free_ref[previous],
                [start_ref[part, previous] for part in range(3)],
                views,
            )
            modulus, before = later, ahead
        return modulus, before

    modulus, before = each_chunk(
        planes, piece, modulus_piece, (jnp.ones(shape, jnp.float32), zero)
    )
    store_faces(
        planes,
        modulus,
        pltpu.roll(modulus, layers - 1, 0),
        pltpu.roll(modulus, 1, 0),
        zero,
        before,
        free_ref[planes - 1],
        [start_ref[part, planes - 1] for part in range(3)],
        (across_ref, up_ref, right_ref, left_ref, rate_ref, first_ref),
    )

    own_x = jnp.max(spot_ref[...]).astype(jnp.int32)

    def sweep(source, target):
        def sweep_piece(first, carry):
            count = planes
            old = source.at[:, pl.ds(first * layers, (count + 2) * layers)]
            new = target.at[:, pl.ds((first + 1) * layers, count * layers)]
            across = across_ref.at[pl.ds(first, count + 1)]
            up = up_ref.at[pl.ds(first * layers, (count + 1) * layers)]
            right = right_ref.at[pl.ds(first + 1, count)]
            left = left_ref.at[pl.ds(first + 1, count)]
            rate = rate_ref.at[:, pl.ds(first + 1, count)]
            behind = [old[part, rows(0, layers)] for part in range(3)]
            here = [old[part, rows(1, layers)] for part in range(3)]
            for p in range(count):
                ahead = [old[part, rows(p + 2, layers)] for part in range(3)]
                for part in range(3):
                    pulls = [
                        across[p] * behind[part] + across[p + 1] * ahead[part],
                        up[rows(p + 1, layers)] * old[part, rows(p + 1, layers, 1)]
                        + up[rows(p + 1, layers, -1)] * old[part, rows(p + 1, layers, -1)],
                        right[p] * pltpu.roll(here[part], row_width - 1, 1)
                        + left[p] * pltpu.roll(here[part], 1, 1),
                    ]
                    pull = pulls[0] + pulls[1] + pulls[2] + pulls[part]
                    new[part, rows(p, layers)] = (
                        1.0 - relax_factor
                    ) * here[part] + rate[part, p] * pull
                behind, here = here, ahead
            return carry

        sweep_piece(0, 0)
        for part in range(3):
            target[part, rows(own_x + 1, layers)] += rate_ref[part, own_x + 1] * load_ref[part]

    def two_sweeps(turn, carry):
        sweep(first_ref, disp_ref)

        @pl.when(turn < SWEEPS // 2)
        def _():
            sweep(disp_ref, first_ref)

        return carry

    lax.fori_loop(0, SWEEPS // 2 + 1, two_sweeps, 0)


def filter_group(group, shares, weight_ref, near_ref, far_ref, result_ref):
    chips, own_planes, layers, row_width = result_ref.shape
    zero_gap = jnp.zeros((GAP, row_width), jnp.float32)
    core = own_core(group)
    count = shares[0].shape[0] - own_planes
    views = [
        [ref.at[pl.ds(own_planes * start, count)] for ref in shares] for start in (core, 1 - core)
    ]
    for ref in (near_ref, far_ref):
        ref[gap(0, layers)] = zero_gap
    for p in range(chips * own_planes):
        chip, own = p // own_planes, p % own_planes
        plane, beside, further = views[far_half(chip)]
        x = 2 * own_planes * chip + own + 2

        def around(ref, distance):
            return ref[x + distance] + ref[x - distance]

        sums = {
            0: plane[x],
            1: beside[x] + around(plane, 1),
            2: around(beside, 1),
            4: further[x] + around(plane, 2),
            5: around(further, 1) + around(beside, 2),
            8: around(further, 2),
        }
        level = weigh(sums, weight_ref, 0)
        for ref, square in ((near_ref, 1), (far_ref, 4)):
            ref[gapped(p, layers)] = weigh(sums, weight_ref, square)
            ref[gap(p + 1, layers)] = zero_gap
        result_ref[chip, own] = (
            level
            + near_ref[gapped(p, layers, 1)]
            + near_ref[gapped(p, layers, -1)]
            + far_ref[gapped(p, layers, 2)]
            + far_ref[gapped(p, layers, -2)]
        )


def share_kernel(
    disp_ref,
    coef_ref,
    weight_ref,
    sent_ref,
    plane_ref,
    beside_ref,
    further_ref,
    near_ref,
    far_ref,
):
    planes, layers, row_width = coef_ref.shape
    load_cases = lax.axis_size("space")
    shape = (layers, row_width)
    z = spot_iota(shape, 0)
    y = spot_iota(shape, 1)
    zero = jnp.zeros(shape, jnp.float32)
    shares = (plane_ref, beside_ref, further_ref)
    for ref in shares:
        zero_edges(ref)

    count = planes // 2

    def share_chunk(first, before):
        disp = disp_ref.at[:, pl.ds((first + 1) * layers, (count + 1) * layers)]
        coef = coef_ref.at[pl.ds(first, count)]
        plane, beside, further = (ref.at[pl.ds(first + 2, count)] for ref in shares)
        here = [disp[part, rows(0, layers)] for part in range(3)]
        for p in range(count):
            later = [disp[part, rows(p + 1, layers)] for part in range(3)]
            ahead, upward, right = zero, zero, zero
            for part in range(3):
                step = later[part] - here[part]
                climb = disp[part, rows(p, layers, 1)] - here[part]
                slide = pltpu.roll(here[part], row_width - 1, 1) - here[part]
                ahead = ahead + (2.0 if part == 0 else 1.0) * (step * step)
                upward = upward + (2.0 if part == 1 else 1.0) * (climb * climb)
                right = right + (2.0 if part == 2 else 1.0) * (slide * slide)
            if p == count - 1:
                ahead = jnp.where(first + count < planes, ahead, 0.0)
            upward = jnp.where(z < layers - 1, upward, 0.0)
            right = jnp.where(y < row_width - 1, right, 0.0)
            total = before + ahead + upward + pltpu.roll(upward, 1, 0)
            total = total + right + pltpu.roll(right, 1, 1)
            share = (0.5 / load_cases) * total * coef[p]
            plane[p] = share
            beside[p] = shift_sum(share, 1, 1)
            further[p] = shift_sum(share, 1, 2)
            before, here = ahead, later
        return before

    each_chunk(planes, count, share_chunk, zero)
    filter_group(1, shares, weight_ref, near_ref, far_ref, sent_ref)


def kept_kernel(
    disp_ref,
    weight_ref,
    plane_ref,
    beside_ref,
    further_ref,
    disp_hbm,
    kept_ref,
    near_ref,
    far_ref,
    stored,
):
    layers = kept_ref.shape[2]
    inner = pl.ds(layers, disp_ref.shape[1] - 2 * layers)
    store = pltpu.make_async_copy(disp_ref.at[:, inner], disp_hbm, stored)
    store.start()
    shares = (plane_ref, beside_ref, further_ref)
    filter_group(0, shares, weight_ref, near_ref, far_ref, kept_ref)
    store.wait()


def design_kernel(root_ref, density_ref, new_ref, pull_ref, low_ref, high_ref):
    groups, chips, own_planes, layers, row_width = density_ref.shape
    own_chip = lax.axis_index("space") >> 1
    shape = (layers, row_width)
    zero = jnp.zeros(shape, jnp.float32)
    planes = [
        (group, chip, own)
        for group in range(groups)
        for chip in range(chips)
        for own in range(own_planes)
    ]
    for spot in planes:
        density = density_ref[spot]
        pull_ref[spot] = density * root_ref[spot]
        low_ref[spot] = jnp.maximum(density - move_limit, density_floor)
        high_ref[spot] = jnp.minimum(density + move_limit, 1.0)

    target = volume_share * len(planes) * layers * row_width

    def factor_of(log_level):
        return jnp.broadcast_to(jnp.exp(-0.5 * log_level), shape)

    def exceeds(total):
        return jnp.sum(jnp.sum(total, axis=0, keepdims=True), axis=1, keepdims=True) > target

    def halve_twice(step, state):
        lower, span = state
        half, quarter = span * 0.5, span * 0.25
        middles = (lower + quarter, lower + half, lower + half + quarter)
        factors = [factor_of(middle) for middle in middles]
        totals = [zero, zero, zero]
        for spot in planes:
            pull, low, high = pull_ref[spot], low_ref[spot], high_ref[spot]
            totals = [
                total + jnp.minimum(jnp.maximum(pull * factor, low), high)
                for total, factor in zip(totals, factors)
            ]
        first, second, third = (exceeds(total) for total in totals)
        upper = jnp.where(third, middles[2], middles[1])
        below = jnp.where(first, middles[0], lower)
        return jnp.where(second, upper, below), quarter

    start = (jnp.full((1, 1), log_lower, jnp.float32), jnp.full((1, 1), log_span, jnp.float32))
    lower, span = lax.fori_loop(0, SEARCH // 2, halve_twice, start)
    factor = factor_of(lower + 0.5 * span)
    for own in range(own_planes):
        spot = (0, own_chip, own)
        new_ref[own] = jnp.minimum(
            jnp.maximum(pull_ref[spot] * factor, low_ref[spot]), high_ref[spot]
        )


def in_vmem():
    return pl.BlockSpec(memory_space=pltpu.VMEM)


KERNEL_VMEM = 24 * 2**20


def floats(*shape):
    return jax.ShapeDtypeStruct(shape, jnp.float32)


def prepare_call(density, radius, load_index, load_force, fixed):
    chips, own_planes, layers, row_width = density.shape
    planes = fixed.shape[0]
    spread = pltpu.VMEM((chips * own_planes * (layers + GAP) + GAP, row_width), jnp.float32)
    return pl.pallas_call(
        prepare_kernel,
        out_shape=[
            floats(len(ALL_SQUARES), layers, row_width),
            floats(2 * window_reach + 1, layers, row_width),
            floats(planes, layers, row_width),
            floats(3, layers, row_width),
            floats(8, row_width),
            floats(3, *density.shape),
        ],
        in_specs=[pl.BlockSpec(memory_space=pltpu.HBM)] * 4 + [in_vmem()],
        out_specs=[in_vmem()] * 6,
        scratch_shapes=[
            pltpu.SMEM(radius.shape, radius.dtype),
            pltpu.SMEM(load_index.shape, load_index.dtype),
            pltpu.SMEM(load_force.shape, load_force.dtype),
            pltpu.VMEM(fixed.shape, fixed.dtype),
            spread,
            spread,
            spread,
            pltpu.SemaphoreType.DMA((4,)),
        ],
        compiler_params=pltpu.CompilerParams(vmem_limit_bytes=KERNEL_VMEM),
        cost_estimate=pl.CostEstimate(
            flops=80 * planes * layers * row_width,
            bytes_accessed=8 * planes * layers * row_width,
            transcendentals=0,
        ),
        name="prepare",
    )(
        *(
            pltpu.with_memory_space_constraint(array, pltpu.HBM)
            for array in (radius, load_index, load_force, fixed)
        ),
        density,
    )


def sweep_call(spot, load, weights, inverses, free, filtered, density, displacement):
    groups, chips, own_planes, layers, row_width = density.shape
    planes = groups * chips * own_planes

    def scratch(*lead):
        return pltpu.VMEM(lead + (row_width,), jnp.float32)

    return pl.pallas_call(
        sweep_kernel,
        out_shape=[
            floats(3, (planes + 2) * layers, row_width),
            floats(planes, layers, row_width),
        ],
        in_specs=[in_vmem()] * 8,
        out_specs=[in_vmem()] * 2,
        scratch_shapes=[
            scratch(planes // 2 * (layers + GAP) + GAP),
            scratch(planes // 2 * (layers + GAP) + GAP),
            scratch(planes // 2 * (layers + GAP) + GAP),
            scratch(planes + 4, layers),
            scratch(planes + 4, layers),
            scratch(planes + 4, layers),
            scratch((planes + 1) * layers),
            scratch(planes + 1, layers),
            scratch((planes + 1) * layers),
            scratch(planes + 1, layers),
            scratch(planes + 1, layers),
            scratch(3, planes + 1, layers),
            scratch(3, (planes + 2) * layers),
        ],
        compiler_params=pltpu.CompilerParams(vmem_limit_bytes=KERNEL_VMEM),
        name="sweeps",
    )(spot, load, weights, inverses, free, filtered, density, displacement)


def share_call(disp, coef, weights, group_shape):
    planes, layers, row_width = coef.shape
    gaps = pltpu.VMEM((planes // 2 * (layers + GAP) + GAP, row_width), jnp.float32)
    return pl.pallas_call(
        share_kernel,
        out_shape=[floats(*group_shape)] + [floats(planes + 4, layers, row_width)] * 3,
        in_specs=[in_vmem()] * 3,
        out_specs=[in_vmem()] * 4,
        scratch_shapes=[gaps, gaps],
        compiler_params=pltpu.CompilerParams(vmem_limit_bytes=KERNEL_VMEM),
        name="share",
    )(disp, coef, weights)


def kept_call(disp, weights, shares, group_shape):
    parts, disp_rows, row_width = disp.shape
    chips, own_planes, layers = group_shape[:3]
    gaps = pltpu.VMEM((chips * own_planes * (layers + GAP) + GAP, row_width), jnp.float32)
    return pl.pallas_call(
        kept_kernel,
        out_shape=[floats(parts, disp_rows - 2 * layers, row_width), floats(*group_shape)],
        in_specs=[in_vmem()] * 5,
        out_specs=[pl.BlockSpec(memory_space=pltpu.HBM), in_vmem()],
        scratch_shapes=[gaps, gaps, pltpu.SemaphoreType.DMA(())],
        compiler_params=pltpu.CompilerParams(vmem_limit_bytes=KERNEL_VMEM),
        cost_estimate=pl.CostEstimate(
            flops=20 * disp.size, bytes_accessed=8 * disp.size, transcendentals=0
        ),
        name="kept",
    )(disp, weights, *shares)


def design_call(root, density):
    return pl.pallas_call(
        design_kernel,
        out_shape=floats(*density.shape[2:]),
        in_specs=[in_vmem()] * 2,
        out_specs=in_vmem(),
        scratch_shapes=[pltpu.VMEM(density.shape, jnp.float32)] * 3,
        compiler_params=pltpu.CompilerParams(vmem_limit_bytes=KERNEL_VMEM),
        name="design",
    )(root, density)


def other_core(block):
    devices = lax.axis_size("space")
    return lax.ppermute(block, "space", [(i, i ^ 1) for i in range(devices)])


def chip_groups():
    chips = lax.axis_size("space") // 2
    return [[2 * chip + (far_half(chip) ^ group) for chip in range(chips)] for group in range(2)]


def between_chips(pieces):
    return lax.all_to_all(pieces, "space", 0, 0, axis_index_groups=chip_groups())


def chip_gathered(block):
    chips = lax.axis_size("space") // 2
    return between_chips(jnp.broadcast_to(block[None], (chips,) + block.shape))


def with_other_core(blocks):
    return jnp.stack([blocks, other_core(blocks)])


def scattered_sum(sent, make_kept):
    received = other_core(sent)
    *others, kept = make_kept()
    return jnp.sum(between_chips(kept + received), axis=0), others


def one_slab(density, displacement, fixed, load_index, load_force, radius):
    same_group, small = lax.optimization_barrier(
        (chip_gathered(density), (radius, load_index, load_force.T, fixed))
    )
    other_group = other_core(same_group)
    weights, inverses, free, load, spot, filtered = prepare_call(same_group, *small)
    whole = jnp.stack([same_group, other_group])
    disp, coef = sweep_call(
        spot, load, weights, inverses, free, filtered, whole, displacement[0]
    )
    sent, *shares = share_call(disp, coef, weights, same_group.shape)
    sent, disp, shares = lax.optimization_barrier((sent, disp, shares))
    squares, (new_displacement,) = scattered_sum(
        sent, lambda: kept_call(disp, weights, shares, same_group.shape)
    )
    root = with_other_core(chip_gathered(jnp.sqrt(squares)))
    new_density = design_call(root, whole)
    return new_density, new_displacement.reshape(displacement.shape)


def from_behind(block, axis, distance):
    devices = range(lax.axis_size(axis))
    route = [(i - distance, i) for i in devices if i - distance in devices]
    return lax.ppermute(block, axis, route)


def extended(x, sides, width):
    for axis, dim in sides:
        size, length = (lax.axis_size(axis), x.shape[dim])
        up = [(i, (i + 1) % size) for i in range(size - 1)]
        down = [(j, i) for i, j in up]
        last = lax.slice_in_dim(x, length - width, length, axis=dim)
        first = lax.slice_in_dim(x, 0, width, axis=dim)
        before = lax.ppermute(last, axis, up)
        after = lax.ppermute(first, axis, down)
        x = jnp.concatenate([before, x, after], axis=dim)
    return x


def from_partner(x, axis, bit):
    return lax.ppermute(x, axis, [(i, i ^ 1 << bit) for i in range(lax.axis_size(axis))])


def window_offsets():
    offsets_list = []
    for across in range(-window_reach, window_reach + 1):
        for upward in range(-window_reach, window_reach + 1):
            for sideways in range(-window_reach, window_reach + 1):
                length = math.sqrt(across * across + upward * upward + sideways * sideways)
                offsets_list.append((across, upward, sideways, length))
    return offsets_list


def layer_weights(radius):
    radial = radius.astype(jnp.float32)
    return jnp.stack(
        [jnp.maximum(radial - length, 0.0) for across, upward, sideways, length in window_offsets()]
    )


def pad_axis(grid_field, along_axis, before, after_cells):
    widths = [(0, 0)] * grid_field.ndim
    widths[along_axis] = (before, after_cells)
    return jnp.pad(grid_field, widths)


def pad_sides(grid_field):
    return jnp.pad(grid_field, ((0, 0), (window_reach, window_reach), (window_reach, window_reach)))


def filter_forward(padded, weights):
    out_rows = padded.shape[0] - 2 * window_reach
    layers = padded.shape[1] - 2 * window_reach
    row_width = padded.shape[2] - 2 * window_reach
    result = jnp.zeros((out_rows, layers, row_width), jnp.float32)
    for offset_index, (across, upward, sideways, length) in enumerate(window_offsets()):
        shifted = padded[
            window_reach + across : window_reach + across + out_rows,
            window_reach + upward : window_reach + upward + layers,
            window_reach + sideways : window_reach + sideways + row_width,
        ]
        result = result + weights[offset_index][None, :, None] * shifted
    return result


def filter_backward(padded, padded_weights):
    out_rows = padded.shape[0] - 2 * window_reach
    layers = padded.shape[1] - 2 * window_reach
    row_width = padded.shape[2] - 2 * window_reach
    result = jnp.zeros((out_rows, layers, row_width), jnp.float32)
    for offset_index, (across, upward, sideways, length) in enumerate(window_offsets()):
        shifted = padded[
            window_reach - across : window_reach - across + out_rows,
            window_reach - upward : window_reach - upward + layers,
            window_reach - sideways : window_reach - sideways + row_width,
        ]
        layer_part = padded_weights[
            offset_index, window_reach - upward : window_reach - upward + layers
        ]
        result = result + layer_part[None, :, None] * shifted
    return result


def stiff_factors(direction):
    return jnp.array(
        [2.0 if component == direction else 1.0 for component in range(3)], jnp.float32
    ).reshape(3, 1, 1, 1)


def relax_slab(padded, displace, face_x, face_z, face_y, force_field, free_cells, diagonal):
    flux_x = stiff_factors(0) * face_x * jnp.diff(padded, axis=1)
    stencil_image = flux_x[:, :-1] - flux_x[:, 1:]
    flux_z = stiff_factors(1) * face_z * jnp.diff(displace, axis=2)
    stencil_image = stencil_image + pad_axis(flux_z, 2, 1, 0) - pad_axis(flux_z, 2, 0, 1)
    flux_y = stiff_factors(2) * face_y * jnp.diff(displace, axis=3)
    stencil_image = stencil_image + pad_axis(flux_y, 3, 1, 0) - pad_axis(flux_y, 3, 0, 1)
    return free_cells * (displace + relax_factor * (force_field - stencil_image) / diagonal)


def slab_energy(grid_field, along_axis, direction, load_cases):
    change = jnp.diff(grid_field, axis=along_axis)
    return jnp.sum(stiff_factors(direction) * change * change, axis=0) / load_cases


def neighbour_planes(displace, load_cases, axis_devices):
    if axis_devices > load_cases:
        below = from_behind(displace[:, -1:], "space", load_cases)
        above = from_behind(displace[:, :1], "space", -load_cases)
    else:
        below = jnp.zeros_like(displace[:, :1])
        above = jnp.zeros_like(displace[:, :1])
    return jnp.concatenate([below, displace, above], axis=1)


def many_slabs(density, displacement, fixed, load_index, load_force, radius):
    slab_rows, layers, row_width = density.shape
    load_cases = load_index.shape[0]
    level_count = load_cases.bit_length() - 1
    axis_devices = lax.axis_size("space")
    axis_place = lax.axis_index("space")
    slab_planes = slab_rows * load_cases
    slab_place = axis_place // load_cases
    load_place = axis_place % load_cases
    total_rows = slab_rows * axis_devices
    weights = layer_weights(radius)
    padded_weights = pad_axis(weights, 1, window_reach, window_reach)
    global_rows = (
        jnp.arange(slab_rows + 2 * window_reach, dtype=jnp.int32)
        + axis_place * slab_rows
        - window_reach
    )
    deep_inside = ((global_rows >= 0) & (global_rows < total_rows)).astype(jnp.float32)
    inside_field = deep_inside[:, None, None] * pad_sides(
        jnp.ones((slab_rows + 2 * window_reach, layers, row_width), jnp.float32)
    )
    total_weight = filter_forward(inside_field, weights)
    slab_start = slab_place * slab_planes
    margin_rows = jnp.arange(slab_planes + 2, dtype=jnp.int32) + slab_start - 1
    margin_inside = ((margin_rows >= 0) & (margin_rows < total_rows)).astype(jnp.float32)
    face_valid = margin_inside[1:] * margin_inside[:-1]
    fixed_slab = lax.dynamic_slice_in_dim(fixed, slab_start, slab_planes, 0).astype(jnp.float32)
    bottom_layer = (jnp.arange(layers, dtype=jnp.int32) == 0).astype(jnp.float32)
    free_cells = 1.0 - bottom_layer[None, :, None] * fixed_slab[:, None, :]
    slab_cells = slab_planes * layers * row_width
    cell_index = jnp.arange(slab_cells, dtype=jnp.int32) + slab_place * slab_cells
    load_hot = jnp.arange(load_cases, dtype=jnp.int32) == load_place
    own_index = jnp.sum(jnp.where(load_hot, load_index, 0))
    own_force = jnp.sum(load_hot.astype(jnp.float32)[:, None] * load_force, axis=0)
    load_hits = (cell_index == own_index).astype(jnp.float32)
    force_field = (own_force[:, None] * load_hits[None, :]).reshape(
        3, slab_planes, layers, row_width
    )
    displace = displacement[0] * free_cells
    target = volume_share * total_rows * layers * row_width
    padded = neighbour_planes(displace, load_cases, axis_devices)
    halo_density = extended(density, (("space", 0),), window_reach)
    filtered = filter_forward(pad_sides(halo_density), weights) / total_weight
    whole_field = lax.all_gather(filtered, "space", axis=0, tiled=True)
    margin = lax.dynamic_slice_in_dim(
        pad_axis(whole_field, 0, 1, 1), slab_start, slab_planes + 2, 0
    )
    moduli = floor_modulus + (1.0 - floor_modulus) * margin**3
    face_x = 0.5 * (moduli[1:] + moduli[:-1]) * face_valid[:, None, None]
    inner_moduli = moduli[1:-1]
    face_z = 0.5 * (inner_moduli[:, 1:] + inner_moduli[:, :-1])
    face_y = 0.5 * (inner_moduli[:, :, 1:] + inner_moduli[:, :, :-1])
    sum_x = face_x[:-1] + face_x[1:]
    sum_z = pad_axis(face_z, 1, 1, 0) + pad_axis(face_z, 1, 0, 1)
    sum_y = pad_axis(face_y, 2, 1, 0) + pad_axis(face_y, 2, 0, 1)
    diagonal = stiff_factors(0) * sum_x + stiff_factors(1) * sum_z + stiff_factors(2) * sum_y
    for sweep_index in range(SWEEPS):
        displace = relax_slab(
            padded, displace, face_x, face_z, face_y, force_field, free_cells, diagonal
        )
        padded = neighbour_planes(displace, load_cases, axis_devices)
    energy_x = slab_energy(padded, 1, 0, load_cases) * face_valid[:, None, None]
    energy_z = slab_energy(displace, 2, 1, load_cases)
    energy_y = slab_energy(displace, 3, 2, load_cases)
    sens_term = 0.5 * (
        energy_x[:-1]
        + energy_x[1:]
        + pad_axis(energy_z, 1, 1, 0)
        + pad_axis(energy_z, 1, 0, 1)
        + pad_axis(energy_y, 2, 1, 0)
        + pad_axis(energy_y, 2, 0, 1)
    )
    sensitive = sens_term
    for level in reversed(range(level_count)):
        half_rows = sensitive.shape[0] // 2
        upper_side = load_place // 2**level % 2 == 1
        outgoing = jnp.where(upper_side, sensitive[:half_rows], sensitive[half_rows:])
        keeping = jnp.where(upper_side, sensitive[half_rows:], sensitive[:half_rows])
        sensitive = keeping + from_partner(outgoing, "space", level)
    weighted_share = 3.0 * (1.0 - floor_modulus) * filtered**2 * sensitive / total_weight
    halo_share = extended(weighted_share, (("space", 0),), window_reach)
    root_term = jnp.sqrt(filter_backward(pad_sides(halo_share), padded_weights))
    lowest = jnp.maximum(density - move_limit, density_floor)
    highest = jnp.minimum(density + move_limit, 1.0)
    design_now = density

    def trial_design(log_level):
        return jnp.clip(design_now * root_term * jnp.exp(-0.5 * log_level), lowest, highest)

    start_state = (jnp.asarray(log_lower, jnp.float32), jnp.asarray(log_span, jnp.float32))

    def halve(search_step, search_state):
        lower_end, span_width = search_state
        half_span = span_width * 0.5
        middle = lower_end + half_span
        volume_total = lax.psum(jnp.sum(trial_design(middle)), "space")
        return (jnp.where(volume_total > target, middle, lower_end), half_span)

    lower_end, span_width = lax.fori_loop(0, SEARCH, halve, start_state)
    density = trial_design(lower_end + 0.5 * span_width)
    new_displacement = displace[None]
    return (density, new_displacement)


def solution(mesh):
    in_specs = (
        P("space", "parts", None),
        P("space", None, None, "parts", None),
        P(None, "parts"),
        P("parts"),
        P("parts", None),
        P("parts"),
    )
    out_specs = (P("space", "parts", None), P("space", None, None, "parts", None))

    def local(density, displacement, fixed, load_index, load_force, radius):
        alone = lax.axis_size("space") == load_index.shape[0]
        run = one_slab if alone else many_slabs
        return run(density, displacement, fixed, load_index, load_force, radius)

    return jax.shard_map(local, mesh=mesh, in_specs=in_specs, out_specs=out_specs, check_vma=False)
```

```python
import math

import jax
import jax.numpy as jnp
from jax import lax
from jax.experimental import pallas as pl
from jax.experimental.pallas import tpu as pltpu
from jax.sharding import PartitionSpec as P

SWEEPS = 3
SEARCH = 12


floor_modulus = 0.05
relax_factor = 0.6
move_limit = 0.2
density_floor = 0.01
volume_share = 0.5
log_lower = -16.0
log_span = 32.0
window_reach = 2

PLANE_SQUARES = (0, 1, 2, 4, 5, 8)
ALL_SQUARES = (0, 1, 2, 3, 4, 5, 6, 8, 9, 12)


def spot_iota(shape, dim):
    return lax.broadcasted_iota(jnp.int32, shape, dim)


def each_plane(planes, body, carry):
    for x in range(planes):
        carry = body(x, carry)
    return carry


def each_chunk(planes, count, body, carry):
    return lax.fori_loop(0, planes // count, lambda i, carry: body(i * count, carry), carry)


def layer_radius(radius_ref, layers, row_width):
    z = spot_iota((layers, row_width), 0)
    result = jnp.zeros((layers, row_width), jnp.int32)
    for layer in range(layers):
        result = jnp.where(z == layer, radius_ref[layer], result)
    return result.astype(jnp.float32)


def class_weights(radius_ref, weight_ref):
    layers, row_width = weight_ref.shape[1:]
    radial = layer_radius(radius_ref, layers, row_width)
    for place, square in enumerate(ALL_SQUARES):
        weight_ref[place] = jnp.maximum(radial - math.sqrt(square), 0.0)


def shift_sum(field, dim, distance):
    size = field.shape[dim]
    spot = spot_iota(field.shape, dim)
    ahead = jnp.where(spot < size - distance, pltpu.roll(field, size - distance, dim), 0.0)
    behind = jnp.where(spot >= distance, pltpu.roll(field, distance, dim), 0.0)
    return ahead + behind


def plane_sums(plane):
    beside = shift_sum(plane, 1, 1)
    further = shift_sum(plane, 1, 2)
    return {
        0: plane,
        1: beside + shift_sum(plane, 0, 1),
        2: shift_sum(beside, 0, 1),
        4: further + shift_sum(plane, 0, 2),
        5: shift_sum(further, 0, 1) + shift_sum(beside, 0, 2),
        8: shift_sum(further, 0, 2),
    }


def weigh(sums, weight_ref, square):
    result = None
    for inner in PLANE_SQUARES:
        term = weight_ref[ALL_SQUARES.index(inner + square)] * sums[inner]
        result = term if result is None else result + term
    return result


def forward_planes(plane, weight_ref):
    sums = plane_sums(plane)
    return [weigh(sums, weight_ref, square) for square in (0, 1, 4)]


def rows(x, layers, shift=0):
    return pl.ds(x * layers + shift, layers)


GAP = 8


def gapped(x, layers, shift=0):
    return pl.ds(GAP + x * (layers + GAP) + shift, layers)


def gap(x, layers):
    return pl.ds(x * (layers + GAP), GAP)


def edge_class(x, planes):
    return jnp.minimum(x, 2) + jnp.maximum(x - (planes - 3), 0)


def zero_edges(ref):
    planes = ref.shape[0]
    for place in (0, 1, planes - 2, planes - 1):
        ref[place] = jnp.zeros(ref.shape[1:], ref.dtype)


def group_spots(group, blocks):
    chips, own_planes = blocks.shape[:2]
    mine = lax.axis_index("space")
    core = mine ^ mine >> 1 ^ group
    return [
        (own_planes * (2 * chip + ((core ^ chip) & 1)) + own, (chip, own))
        for chip in range(chips)
        for own in range(own_planes)
    ]


def spread_group(blocks, spread):
    chips, own_planes, layers, row_width = blocks.shape
    zero_gap = jnp.zeros((GAP, row_width), jnp.float32)
    for ref in spread:
        ref[gap(0, layers)] = zero_gap
    for p in range(chips * own_planes):
        plane = blocks[p // own_planes, p % own_planes]
        for ref, field in zip(spread, (plane, shift_sum(plane, 1, 1), shift_sum(plane, 1, 2))):
            ref[gapped(p, layers)] = field
            ref[gap(p + 1, layers)] = zero_gap


def filter_plane(p, layers, spread, weight_ref):
    def around(place, distance):
        ref = spread[place]
        return ref[gapped(p, layers, distance)] + ref[gapped(p, layers, -distance)]

    sums = {
        0: spread[0][gapped(p, layers)],
        1: spread[1][gapped(p, layers)] + around(0, 1),
        2: around(1, 1),
        4: spread[2][gapped(p, layers)] + around(0, 2),
        5: around(2, 1) + around(1, 2),
        8: around(2, 2),
    }
    return [weigh(sums, weight_ref, square) for square in (0, 1, 4)]


def prepare_kernel(
    radius_hbm,
    index_hbm,
    force_hbm,
    fixed_hbm,
    density_ref,
    weight_ref,
    inverse_ref,
    free_ref,
    load_ref,
    spot_ref,
    filter_ref,
    radius_ref,
    index_ref,
    force_ref,
    fixed_ref,
    plane_ref,
    beside_ref,
    further_ref,
    arrived,
):
    copies = [
        pltpu.make_async_copy(source, target, arrived.at[place])
        for place, (source, target) in enumerate(
            (
                (radius_hbm, radius_ref),
                (index_hbm, index_ref),
                (force_hbm, force_ref),
                (fixed_hbm, fixed_ref),
            )
        )
    ]
    for copy in copies:
        copy.start()
    spread = (plane_ref, beside_ref, further_ref)
    spread_group(density_ref, spread)
    for copy in copies:
        copy.wait()
    planes, layers, row_width = free_ref.shape
    load_place = lax.axis_index("space")
    shape = (layers, row_width)
    z = spot_iota(shape, 0)
    y = spot_iota(shape, 1)

    class_weights(radius_ref, weight_ref)
    own_planes = density_ref.shape[1]
    for p in range(density_ref.shape[0] * own_planes):
        for place, field in enumerate(filter_plane(p, layers, spread, weight_ref)):
            filter_ref[place, p // own_planes, p % own_planes] = field

    ones = forward_planes(jnp.ones(shape, jnp.float32), weight_ref)
    for place, (lower, upper) in enumerate(((0, 2), (1, 2), (2, 2), (2, 1), (2, 0))):
        inverse_ref[place] = 1.0 / (
            ones[0] + min(lower, 1) * ones[1] + min(upper, 1) * ones[1]
            + (lower // 2) * ones[2] + (upper // 2) * ones[2]
        )

    def free_plane(x, carry):
        free_ref[x] = jnp.where(
            z == 0, 1.0 - fixed_ref[pl.ds(x, 1), :].astype(jnp.float32), 1.0
        )
        return carry

    each_plane(planes, free_plane, 0)

    own_index = index_ref[load_place]
    own_z = own_index // row_width % layers
    own_y = own_index % row_width
    hit = (z == own_z) & (y == own_y)
    for part in range(3):
        load_ref[part] = jnp.where(hit, force_ref[part, load_place], 0.0)
    own_x = (own_index // (layers * row_width)).astype(jnp.float32)
    spot_ref[...] = jnp.full(spot_ref.shape, own_x)


def sweep_kernel(
    spot_ref,
    load_ref,
    weight_ref,
    inverse_ref,
    free_ref,
    filter_ref,
    density_ref,
    start_ref,
    disp_ref,
    coef_ref,
    plane_ref,
    beside_ref,
    further_ref,
    near_ref,
    side_ref,
    far_ref,
    modulus_ref,
    across_ref,
    up_ref,
    right_ref,
    left_ref,
    rate_ref,
    first_ref,
):
    planes, layers, row_width = coef_ref.shape
    shape = (layers, row_width)
    z = spot_iota(shape, 0)
    y = spot_iota(shape, 1)
    zero = jnp.zeros(shape, jnp.float32)

    for ref in (side_ref, far_ref):
        zero_edges(ref)
    results = (near_ref, side_ref, far_ref)
    other_ref = density_ref.at[1]
    for x, spot in group_spots(0, other_ref):
        for place, ref in enumerate(results):
            ref[x + 2] = filter_ref[(place,) + spot]
    spread = (plane_ref, beside_ref, further_ref)
    spread_group(other_ref, spread)
    for p, (x, spot) in enumerate(group_spots(1, other_ref)):
        for ref, field in zip(results, filter_plane(p, layers, spread, weight_ref)):
            ref[x + 2] = field

    for ref in (first_ref, disp_ref):
        for part in range(3):
            ref[part, rows(0, layers)] = zero
            ref[part, rows(planes + 1, layers)] = zero

    def store_faces(slot, modulus, above, below, later, before, free, start, views):
        across, up_view, right_view, left_view, rate, source = views
        across[slot] = later
        up = jnp.where(z < layers - 1, 0.5 * (modulus + above), 0.0)
        right = jnp.where(
            y < row_width - 1, 0.5 * (modulus + pltpu.roll(modulus, row_width - 1, 1)), 0.0
        )
        left = jnp.where(y > 0, 0.5 * (modulus + pltpu.roll(modulus, 1, 1)), 0.0)
        down = jnp.where(z > 0, 0.5 * (modulus + below), 0.0)
        up_view[rows(slot, layers)] = up
        right_view[slot] = right
        left_view[slot] = left
        sums = (before + later, up + down, left + right)
        every = sums[0] + sums[1] + sums[2]
        diagonal = [every + part_sum for part_sum in sums]
        pair = diagonal[0] * diagonal[1]
        push = relax_factor * free / (pair * diagonal[2])
        side = push * diagonal[2]
        for part, factor in enumerate((side * diagonal[1], side * diagonal[0], push * pair)):
            rate[part, slot] = factor
            source[part, rows(slot, layers)] = start[part] * free

    piece = planes // 2

    def modulus_piece(first, carry):
        count = piece
        near = near_ref.at[pl.ds(first + 2, count)]
        side = side_ref.at[pl.ds(first + 1, count + 2)]
        far = far_ref.at[pl.ds(first, count + 4)]
        moduli = modulus_ref.at[pl.ds(first * layers, (count + 1) * layers)]
        coef = coef_ref.at[pl.ds(first, count)]
        free = free_ref.at[pl.ds(first, count)]
        views = (
            across_ref.at[pl.ds(first, count)],
            up_ref.at[pl.ds(first * layers, count * layers)],
            right_ref.at[pl.ds(first, count)],
            left_ref.at[pl.ds(first, count)],
            rate_ref.at[:, pl.ds(first, count)],
            first_ref.at[:, pl.ds(first * layers, count * layers)],
        )
        modulus, before = carry
        for p in range(count):
            inverse = inverse_ref[edge_class(first + p, planes)]
            filtered = near[p] + side[p] + side[p + 2] + far[p] + far[p + 4]
            filtered = filtered * inverse
            later = floor_modulus + (1.0 - floor_modulus) * (filtered * filtered * filtered)
            coef[p] = 3.0 * (1.0 - floor_modulus) * (filtered * filtered) * inverse
            moduli[rows(p + 1, layers)] = later
            ahead = 0.5 * (modulus + later)
            if p == 0:
                ahead = jnp.where(first > 0, ahead, 0.0)
            above = moduli[rows(p, layers, 1)] if p else pltpu.roll(modulus, layers - 1, 0)
            below = moduli[rows(p, layers, -1)] if p else pltpu.roll(modulus, 1, 0)
            previous = jnp.maximum(first + p - 1, 0)
            store_faces(
                p,
                modulus,
                above,
                below,
                ahead,
                before,
                free_ref[previous],
                [start_ref[part, previous] for part in range(3)],
                views,
            )
            modulus, before = later, ahead
        return modulus, before

    modulus, before = each_chunk(
        planes, piece, modulus_piece, (jnp.ones(shape, jnp.float32), zero)
    )
    store_faces(
        planes,
        modulus,
        pltpu.roll(modulus, layers - 1, 0),
        pltpu.roll(modulus, 1, 0),
        zero,
        before,
        free_ref[planes - 1],
        [start_ref[part, planes - 1] for part in range(3)],
        (across_ref, up_ref, right_ref, left_ref, rate_ref, first_ref),
    )

    own_x = jnp.max(spot_ref[...]).astype(jnp.int32)

    def sweep(source, target):
        def sweep_piece(first, carry):
            count = planes
            old = source.at[:, pl.ds(first * layers, (count + 2) * layers)]
            new = target.at[:, pl.ds((first + 1) * layers, count * layers)]
            across = across_ref.at[pl.ds(first, count + 1)]
            up = up_ref.at[pl.ds(first * layers, (count + 1) * layers)]
            right = right_ref.at[pl.ds(first + 1, count)]
            left = left_ref.at[pl.ds(first + 1, count)]
            rate = rate_ref.at[:, pl.ds(first + 1, count)]
            behind = [old[part, rows(0, layers)] for part in range(3)]
            here = [old[part, rows(1, layers)] for part in range(3)]
            for p in range(count):
                ahead = [old[part, rows(p + 2, layers)] for part in range(3)]
                for part in range(3):
                    pulls = [
                        across[p] * behind[part] + across[p + 1] * ahead[part],
                        up[rows(p + 1, layers)] * old[part, rows(p + 1, layers, 1)]
                        + up[rows(p + 1, layers, -1)] * old[part, rows(p + 1, layers, -1)],
                        right[p] * pltpu.roll(here[part], row_width - 1, 1)
                        + left[p] * pltpu.roll(here[part], 1, 1),
                    ]
                    pull = pulls[0] + pulls[1] + pulls[2] + pulls[part]
                    new[part, rows(p, layers)] = (
                        1.0 - relax_factor
                    ) * here[part] + rate[part, p] * pull
                behind, here = here, ahead
            return carry

        sweep_piece(0, 0)
        for part in range(3):
            target[part, rows(own_x + 1, layers)] += rate_ref[part, own_x + 1] * load_ref[part]

    def two_sweeps(turn, carry):
        sweep(first_ref, disp_ref)

        @pl.when(turn < SWEEPS // 2)
        def _():
            sweep(disp_ref, first_ref)

        return carry

    lax.fori_loop(0, SWEEPS // 2 + 1, two_sweeps, 0)


def filter_group(group, shares, weight_ref, near_ref, far_ref, result_ref):
    chips, own_planes, layers, row_width = result_ref.shape
    zero_gap = jnp.zeros((GAP, row_width), jnp.float32)
    mine = lax.axis_index("space")
    core = (mine ^ mine >> 1 ^ group) & 1
    count = shares[0].shape[0] - own_planes
    views = [
        [ref.at[pl.ds(own_planes * start, count)] for ref in shares] for start in (core, 1 - core)
    ]
    for ref in (near_ref, far_ref):
        ref[gap(0, layers)] = zero_gap
    for p in range(chips * own_planes):
        chip, own = p // own_planes, p % own_planes
        plane, beside, further = views[chip & 1]
        x = 2 * own_planes * chip + own + 2

        def around(ref, distance):
            return ref[x + distance] + ref[x - distance]

        sums = {
            0: plane[x],
            1: beside[x] + around(plane, 1),
            2: around(beside, 1),
            4: further[x] + around(plane, 2),
            5: around(further, 1) + around(beside, 2),
            8: around(further, 2),
        }
        level = weigh(sums, weight_ref, 0)
        for ref, square in ((near_ref, 1), (far_ref, 4)):
            ref[gapped(p, layers)] = weigh(sums, weight_ref, square)
            ref[gap(p + 1, layers)] = zero_gap
        result_ref[chip, own] = (
            level
            + near_ref[gapped(p, layers, 1)]
            + near_ref[gapped(p, layers, -1)]
            + far_ref[gapped(p, layers, 2)]
            + far_ref[gapped(p, layers, -2)]
        )


def share_kernel(
    disp_ref,
    coef_ref,
    weight_ref,
    sent_ref,
    plane_ref,
    beside_ref,
    further_ref,
    near_ref,
    far_ref,
):
    planes, layers, row_width = coef_ref.shape
    load_cases = lax.axis_size("space")
    shape = (layers, row_width)
    z = spot_iota(shape, 0)
    y = spot_iota(shape, 1)
    zero = jnp.zeros(shape, jnp.float32)
    shares = (plane_ref, beside_ref, further_ref)
    for ref in shares:
        zero_edges(ref)

    before = zero
    here = [disp_ref[part, rows(1, layers)] for part in range(3)]
    for x in range(planes):
        later = [disp_ref[part, rows(x + 2, layers)] for part in range(3)]
        ahead, upward, right = zero, zero, zero
        for part in range(3):
            step = later[part] - here[part]
            climb = disp_ref[part, rows(x + 1, layers, 1)] - here[part]
            slide = pltpu.roll(here[part], row_width - 1, 1) - here[part]
            ahead = ahead + (2.0 if part == 0 else 1.0) * (step * step)
            upward = upward + (2.0 if part == 1 else 1.0) * (climb * climb)
            right = right + (2.0 if part == 2 else 1.0) * (slide * slide)
        if x + 1 == planes:
            ahead = zero
        upward = jnp.where(z < layers - 1, upward, 0.0)
        right = jnp.where(y < row_width - 1, right, 0.0)
        total = before + ahead + upward + pltpu.roll(upward, 1, 0)
        total = total + right + pltpu.roll(right, 1, 1)
        plane_ref[x + 2] = (0.5 / load_cases) * total * coef_ref[x]
        before, here = ahead, later

    count = planes // 2

    def spread_piece(first, carry):
        plane, beside, further = (ref.at[pl.ds(first + 2, count)] for ref in shares)
        for p in range(count):
            share = plane[p]
            beside[p] = shift_sum(share, 1, 1)
            further[p] = shift_sum(share, 1, 2)
        return carry

    each_chunk(planes, count, spread_piece, 0)
    filter_group(1, shares, weight_ref, near_ref, far_ref, sent_ref)


def kept_kernel(
    disp_ref,
    weight_ref,
    plane_ref,
    beside_ref,
    further_ref,
    disp_hbm,
    kept_ref,
    near_ref,
    far_ref,
    stored,
):
    layers = kept_ref.shape[2]
    inner = pl.ds(layers, disp_ref.shape[1] - 2 * layers)
    store = pltpu.make_async_copy(disp_ref.at[:, inner], disp_hbm, stored)
    store.start()
    shares = (plane_ref, beside_ref, further_ref)
    filter_group(0, shares, weight_ref, near_ref, far_ref, kept_ref)
    store.wait()


def design_kernel(root_ref, density_ref, new_ref, pull_ref, low_ref, high_ref):
    groups, chips, own_planes, layers, row_width = density_ref.shape
    own_chip = lax.axis_index("space") >> 1
    shape = (layers, row_width)
    zero = jnp.zeros(shape, jnp.float32)
    planes = [
        (group, chip, own)
        for group in range(groups)
        for chip in range(chips)
        for own in range(own_planes)
    ]
    for spot in planes:
        density = density_ref[spot]
        pull_ref[spot] = density * root_ref[spot]
        low_ref[spot] = jnp.maximum(density - move_limit, density_floor)
        high_ref[spot] = jnp.minimum(density + move_limit, 1.0)

    target = volume_share * len(planes) * layers * row_width

    def factor_of(log_level):
        return jnp.broadcast_to(jnp.exp(-0.5 * log_level), shape)

    def exceeds(total):
        return jnp.sum(jnp.sum(total, axis=0, keepdims=True), axis=1, keepdims=True) > target

    def halve_twice(step, state):
        lower, span = state
        half, quarter = span * 0.5, span * 0.25
        middles = (lower + quarter, lower + half, lower + half + quarter)
        factors = [factor_of(middle) for middle in middles]
        totals = [zero, zero, zero]
        for spot in planes:
            pull, low, high = pull_ref[spot], low_ref[spot], high_ref[spot]
            totals = [
                total + jnp.minimum(jnp.maximum(pull * factor, low), high)
                for total, factor in zip(totals, factors)
            ]
        first, second, third = (exceeds(total) for total in totals)
        upper = jnp.where(third, middles[2], middles[1])
        below = jnp.where(first, middles[0], lower)
        return jnp.where(second, upper, below), quarter

    start = (jnp.full((1, 1), log_lower, jnp.float32), jnp.full((1, 1), log_span, jnp.float32))
    lower, span = lax.fori_loop(0, SEARCH // 2, halve_twice, start)
    factor = factor_of(lower + 0.5 * span)
    for own in range(own_planes):
        spot = (0, own_chip, own)
        new_ref[own] = jnp.minimum(
            jnp.maximum(pull_ref[spot] * factor, low_ref[spot]), high_ref[spot]
        )


def in_vmem():
    return pl.BlockSpec(memory_space=pltpu.VMEM)


KERNEL_VMEM = 24 * 2**20


def floats(*shape):
    return jax.ShapeDtypeStruct(shape, jnp.float32)


def prepare_call(density, radius, load_index, load_force, fixed):
    chips, own_planes, layers, row_width = density.shape
    planes = fixed.shape[0]
    spread = pltpu.VMEM((chips * own_planes * (layers + GAP) + GAP, row_width), jnp.float32)
    return pl.pallas_call(
        prepare_kernel,
        out_shape=[
            floats(len(ALL_SQUARES), layers, row_width),
            floats(2 * window_reach + 1, layers, row_width),
            floats(planes, layers, row_width),
            floats(3, layers, row_width),
            floats(8, row_width),
            floats(3, *density.shape),
        ],
        in_specs=[pl.BlockSpec(memory_space=pltpu.HBM)] * 4 + [in_vmem()],
        out_specs=[in_vmem()] * 6,
        scratch_shapes=[
            pltpu.SMEM(radius.shape, radius.dtype),
            pltpu.SMEM(load_index.shape, load_index.dtype),
            pltpu.SMEM(load_force.shape, load_force.dtype),
            pltpu.VMEM(fixed.shape, fixed.dtype),
            spread,
            spread,
            spread,
            pltpu.SemaphoreType.DMA((4,)),
        ],
        compiler_params=pltpu.CompilerParams(vmem_limit_bytes=KERNEL_VMEM),
        cost_estimate=pl.CostEstimate(
            flops=80 * planes * layers * row_width,
            bytes_accessed=8 * planes * layers * row_width,
            transcendentals=0,
        ),
        name="prepare",
    )(
        *(
            pltpu.with_memory_space_constraint(array, pltpu.HBM)
            for array in (radius, load_index, load_force, fixed)
        ),
        density,
    )


def sweep_call(spot, load, weights, inverses, free, filtered, density, displacement):
    groups, chips, own_planes, layers, row_width = density.shape
    planes = groups * chips * own_planes

    def scratch(*lead):
        return pltpu.VMEM(lead + (row_width,), jnp.float32)

    return pl.pallas_call(
        sweep_kernel,
        out_shape=[
            floats(3, (planes + 2) * layers, row_width),
            floats(planes, layers, row_width),
        ],
        in_specs=[in_vmem()] * 8,
        out_specs=[in_vmem()] * 2,
        scratch_shapes=[
            scratch(planes // 2 * (layers + GAP) + GAP),
            scratch(planes // 2 * (layers + GAP) + GAP),
            scratch(planes // 2 * (layers + GAP) + GAP),
            scratch(planes + 4, layers),
            scratch(planes + 4, layers),
            scratch(planes + 4, layers),
            scratch((planes + 1) * layers),
            scratch(planes + 1, layers),
            scratch((planes + 1) * layers),
            scratch(planes + 1, layers),
            scratch(planes + 1, layers),
            scratch(3, planes + 1, layers),
            scratch(3, (planes + 2) * layers),
        ],
        compiler_params=pltpu.CompilerParams(vmem_limit_bytes=KERNEL_VMEM),
        name="sweeps",
    )(spot, load, weights, inverses, free, filtered, density, displacement)


def share_call(disp, coef, weights, group_shape):
    planes, layers, row_width = coef.shape
    gaps = pltpu.VMEM((planes // 2 * (layers + GAP) + GAP, row_width), jnp.float32)
    return pl.pallas_call(
        share_kernel,
        out_shape=[floats(*group_shape)] + [floats(planes + 4, layers, row_width)] * 3,
        in_specs=[in_vmem()] * 3,
        out_specs=[in_vmem()] * 4,
        scratch_shapes=[gaps, gaps],
        compiler_params=pltpu.CompilerParams(vmem_limit_bytes=KERNEL_VMEM),
        name="share",
    )(disp, coef, weights)


def kept_call(disp, weights, shares, group_shape):
    parts, disp_rows, row_width = disp.shape
    chips, own_planes, layers = group_shape[:3]
    gaps = pltpu.VMEM((chips * own_planes * (layers + GAP) + GAP, row_width), jnp.float32)
    return pl.pallas_call(
        kept_kernel,
        out_shape=[floats(parts, disp_rows - 2 * layers, row_width), floats(*group_shape)],
        in_specs=[in_vmem()] * 5,
        out_specs=[pl.BlockSpec(memory_space=pltpu.HBM), in_vmem()],
        scratch_shapes=[gaps, gaps, pltpu.SemaphoreType.DMA(())],
        compiler_params=pltpu.CompilerParams(vmem_limit_bytes=KERNEL_VMEM),
        cost_estimate=pl.CostEstimate(
            flops=20 * disp.size, bytes_accessed=8 * disp.size, transcendentals=0
        ),
        name="kept",
    )(disp, weights, *shares)


def design_call(root, density):
    return pl.pallas_call(
        design_kernel,
        out_shape=floats(*density.shape[2:]),
        in_specs=[in_vmem()] * 2,
        out_specs=in_vmem(),
        scratch_shapes=[pltpu.VMEM(density.shape, jnp.float32)] * 3,
        compiler_params=pltpu.CompilerParams(vmem_limit_bytes=KERNEL_VMEM),
        name="design",
    )(root, density)


def other_core(block):
    devices = lax.axis_size("space")
    return lax.ppermute(block, "space", [(i, i ^ 1) for i in range(devices)])


def chip_groups():
    chips = lax.axis_size("space") // 2
    return [[2 * chip + (chip ^ group) % 2 for chip in range(chips)] for group in range(2)]


def between_chips(pieces):
    return lax.all_to_all(pieces, "space", 0, 0, axis_index_groups=chip_groups())


def chip_gathered(block):
    chips = lax.axis_size("space") // 2
    return between_chips(jnp.broadcast_to(block[None], (chips,) + block.shape))


def with_other_core(blocks):
    return jnp.stack([blocks, other_core(blocks)])


def scattered_sum(sent, make_kept):
    received = other_core(sent)
    *others, kept = make_kept()
    return jnp.sum(between_chips(kept + received), axis=0), others


def one_slab(density, displacement, fixed, load_index, load_force, radius):
    same_group, small = lax.optimization_barrier(
        (chip_gathered(density), (radius, load_index, load_force.T, fixed))
    )
    other_group = other_core(same_group)
    weights, inverses, free, load, spot, filtered = prepare_call(same_group, *small)
    whole = jnp.stack([same_group, other_group])
    disp, coef = sweep_call(
        spot, load, weights, inverses, free, filtered, whole, displacement[0]
    )
    sent, *shares = share_call(disp, coef, weights, same_group.shape)
    sent, disp, shares = lax.optimization_barrier((sent, disp, shares))
    squares, (new_displacement,) = scattered_sum(
        sent, lambda: kept_call(disp, weights, shares, same_group.shape)
    )
    root = with_other_core(chip_gathered(jnp.sqrt(squares)))
    new_density = design_call(root, whole)
    return new_density, new_displacement.reshape(displacement.shape)


def from_behind(block, axis, distance):
    devices = range(lax.axis_size(axis))
    route = [(i - distance, i) for i in devices if i - distance in devices]
    return lax.ppermute(block, axis, route)


def extended(x, sides, width):
    for axis, dim in sides:
        size, length = (lax.axis_size(axis), x.shape[dim])
        up = [(i, (i + 1) % size) for i in range(size - 1)]
        down = [(j, i) for i, j in up]
        last = lax.slice_in_dim(x, length - width, length, axis=dim)
        first = lax.slice_in_dim(x, 0, width, axis=dim)
        before = lax.ppermute(last, axis, up)
        after = lax.ppermute(first, axis, down)
        x = jnp.concatenate([before, x, after], axis=dim)
    return x


def from_partner(x, axis, bit):
    return lax.ppermute(x, axis, [(i, i ^ 1 << bit) for i in range(lax.axis_size(axis))])


def window_offsets():
    offsets_list = []
    for across in range(-window_reach, window_reach + 1):
        for upward in range(-window_reach, window_reach + 1):
            for sideways in range(-window_reach, window_reach + 1):
                length = math.sqrt(across * across + upward * upward + sideways * sideways)
                offsets_list.append((across, upward, sideways, length))
    return offsets_list


def layer_weights(radius):
    radial = radius.astype(jnp.float32)
    return jnp.stack(
        [jnp.maximum(radial - length, 0.0) for across, upward, sideways, length in window_offsets()]
    )


def pad_axis(grid_field, along_axis, before, after_cells):
    widths = [(0, 0)] * grid_field.ndim
    widths[along_axis] = (before, after_cells)
    return jnp.pad(grid_field, widths)


def pad_sides(grid_field):
    return jnp.pad(grid_field, ((0, 0), (window_reach, window_reach), (window_reach, window_reach)))


def filter_forward(padded, weights):
    out_rows = padded.shape[0] - 2 * window_reach
    layers = padded.shape[1] - 2 * window_reach
    row_width = padded.shape[2] - 2 * window_reach
    result = jnp.zeros((out_rows, layers, row_width), jnp.float32)
    for offset_index, (across, upward, sideways, length) in enumerate(window_offsets()):
        shifted = padded[
            window_reach + across : window_reach + across + out_rows,
            window_reach + upward : window_reach + upward + layers,
            window_reach + sideways : window_reach + sideways + row_width,
        ]
        result = result + weights[offset_index][None, :, None] * shifted
    return result


def filter_backward(padded, padded_weights):
    out_rows = padded.shape[0] - 2 * window_reach
    layers = padded.shape[1] - 2 * window_reach
    row_width = padded.shape[2] - 2 * window_reach
    result = jnp.zeros((out_rows, layers, row_width), jnp.float32)
    for offset_index, (across, upward, sideways, length) in enumerate(window_offsets()):
        shifted = padded[
            window_reach - across : window_reach - across + out_rows,
            window_reach - upward : window_reach - upward + layers,
            window_reach - sideways : window_reach - sideways + row_width,
        ]
        layer_part = padded_weights[
            offset_index, window_reach - upward : window_reach - upward + layers
        ]
        result = result + layer_part[None, :, None] * shifted
    return result


def stiff_factors(direction):
    return jnp.array(
        [2.0 if component == direction else 1.0 for component in range(3)], jnp.float32
    ).reshape(3, 1, 1, 1)


def relax_slab(padded, displace, face_x, face_z, face_y, force_field, free_cells, diagonal):
    flux_x = stiff_factors(0) * face_x * jnp.diff(padded, axis=1)
    stencil_image = flux_x[:, :-1] - flux_x[:, 1:]
    flux_z = stiff_factors(1) * face_z * jnp.diff(displace, axis=2)
    stencil_image = stencil_image + pad_axis(flux_z, 2, 1, 0) - pad_axis(flux_z, 2, 0, 1)
    flux_y = stiff_factors(2) * face_y * jnp.diff(displace, axis=3)
    stencil_image = stencil_image + pad_axis(flux_y, 3, 1, 0) - pad_axis(flux_y, 3, 0, 1)
    return free_cells * (displace + relax_factor * (force_field - stencil_image) / diagonal)


def slab_energy(grid_field, along_axis, direction, load_cases):
    change = jnp.diff(grid_field, axis=along_axis)
    return jnp.sum(stiff_factors(direction) * change * change, axis=0) / load_cases


def neighbour_planes(displace, load_cases, axis_devices):
    if axis_devices > load_cases:
        below = from_behind(displace[:, -1:], "space", load_cases)
        above = from_behind(displace[:, :1], "space", -load_cases)
    else:
        below = jnp.zeros_like(displace[:, :1])
        above = jnp.zeros_like(displace[:, :1])
    return jnp.concatenate([below, displace, above], axis=1)


def many_slabs(density, displacement, fixed, load_index, load_force, radius):
    slab_rows, layers, row_width = density.shape
    load_cases = load_index.shape[0]
    level_count = load_cases.bit_length() - 1
    axis_devices = lax.axis_size("space")
    axis_place = lax.axis_index("space")
    slab_planes = slab_rows * load_cases
    slab_place = axis_place // load_cases
    load_place = axis_place % load_cases
    total_rows = slab_rows * axis_devices
    weights = layer_weights(radius)
    padded_weights = pad_axis(weights, 1, window_reach, window_reach)
    global_rows = (
        jnp.arange(slab_rows + 2 * window_reach, dtype=jnp.int32)
        + axis_place * slab_rows
        - window_reach
    )
    deep_inside = ((global_rows >= 0) & (global_rows < total_rows)).astype(jnp.float32)
    inside_field = deep_inside[:, None, None] * pad_sides(
        jnp.ones((slab_rows + 2 * window_reach, layers, row_width), jnp.float32)
    )
    total_weight = filter_forward(inside_field, weights)
    slab_start = slab_place * slab_planes
    margin_rows = jnp.arange(slab_planes + 2, dtype=jnp.int32) + slab_start - 1
    margin_inside = ((margin_rows >= 0) & (margin_rows < total_rows)).astype(jnp.float32)
    face_valid = margin_inside[1:] * margin_inside[:-1]
    fixed_slab = lax.dynamic_slice_in_dim(fixed, slab_start, slab_planes, 0).astype(jnp.float32)
    bottom_layer = (jnp.arange(layers, dtype=jnp.int32) == 0).astype(jnp.float32)
    free_cells = 1.0 - bottom_layer[None, :, None] * fixed_slab[:, None, :]
    slab_cells = slab_planes * layers * row_width
    cell_index = jnp.arange(slab_cells, dtype=jnp.int32) + slab_place * slab_cells
    load_hot = jnp.arange(load_cases, dtype=jnp.int32) == load_place
    own_index = jnp.sum(jnp.where(load_hot, load_index, 0))
    own_force = jnp.sum(load_hot.astype(jnp.float32)[:, None] * load_force, axis=0)
    load_hits = (cell_index == own_index).astype(jnp.float32)
    force_field = (own_force[:, None] * load_hits[None, :]).reshape(
        3, slab_planes, layers, row_width
    )
    displace = displacement[0] * free_cells
    target = volume_share * total_rows * layers * row_width
    padded = neighbour_planes(displace, load_cases, axis_devices)
    halo_density = extended(density, (("space", 0),), window_reach)
    filtered = filter_forward(pad_sides(halo_density), weights) / total_weight
    whole_field = lax.all_gather(filtered, "space", axis=0, tiled=True)
    margin = lax.dynamic_slice_in_dim(
        pad_axis(whole_field, 0, 1, 1), slab_start, slab_planes + 2, 0
    )
    moduli = floor_modulus + (1.0 - floor_modulus) * margin**3
    face_x = 0.5 * (moduli[1:] + moduli[:-1]) * face_valid[:, None, None]
    inner_moduli = moduli[1:-1]
    face_z = 0.5 * (inner_moduli[:, 1:] + inner_moduli[:, :-1])
    face_y = 0.5 * (inner_moduli[:, :, 1:] + inner_moduli[:, :, :-1])
    sum_x = face_x[:-1] + face_x[1:]
    sum_z = pad_axis(face_z, 1, 1, 0) + pad_axis(face_z, 1, 0, 1)
    sum_y = pad_axis(face_y, 2, 1, 0) + pad_axis(face_y, 2, 0, 1)
    diagonal = stiff_factors(0) * sum_x + stiff_factors(1) * sum_z + stiff_factors(2) * sum_y
    for sweep_index in range(SWEEPS):
        displace = relax_slab(
            padded, displace, face_x, face_z, face_y, force_field, free_cells, diagonal
        )
        padded = neighbour_planes(displace, load_cases, axis_devices)
    energy_x = slab_energy(padded, 1, 0, load_cases) * face_valid[:, None, None]
    energy_z = slab_energy(displace, 2, 1, load_cases)
    energy_y = slab_energy(displace, 3, 2, load_cases)
    sens_term = 0.5 * (
        energy_x[:-1]
        + energy_x[1:]
        + pad_axis(energy_z, 1, 1, 0)
        + pad_axis(energy_z, 1, 0, 1)
        + pad_axis(energy_y, 2, 1, 0)
        + pad_axis(energy_y, 2, 0, 1)
    )
    sensitive = sens_term
    for level in reversed(range(level_count)):
        half_rows = sensitive.shape[0] // 2
        upper_side = load_place // 2**level % 2 == 1
        outgoing = jnp.where(upper_side, sensitive[:half_rows], sensitive[half_rows:])
        keeping = jnp.where(upper_side, sensitive[half_rows:], sensitive[:half_rows])
        sensitive = keeping + from_partner(outgoing, "space", level)
    weighted_share = 3.0 * (1.0 - floor_modulus) * filtered**2 * sensitive / total_weight
    halo_share = extended(weighted_share, (("space", 0),), window_reach)
    root_term = jnp.sqrt(filter_backward(pad_sides(halo_share), padded_weights))
    lowest = jnp.maximum(density - move_limit, density_floor)
    highest = jnp.minimum(density + move_limit, 1.0)
    design_now = density

    def trial_design(log_level):
        return jnp.clip(design_now * root_term * jnp.exp(-0.5 * log_level), lowest, highest)

    start_state = (jnp.asarray(log_lower, jnp.float32), jnp.asarray(log_span, jnp.float32))

    def halve(search_step, search_state):
        lower_end, span_width = search_state
        half_span = span_width * 0.5
        middle = lower_end + half_span
        volume_total = lax.psum(jnp.sum(trial_design(middle)), "space")
        return (jnp.where(volume_total > target, middle, lower_end), half_span)

    lower_end, span_width = lax.fori_loop(0, SEARCH, halve, start_state)
    density = trial_design(lower_end + 0.5 * span_width)
    new_displacement = displace[None]
    return (density, new_displacement)


def solution(mesh):
    in_specs = (
        P("space", "parts", None),
        P("space", None, None, "parts", None),
        P(None, "parts"),
        P("parts"),
        P("parts", None),
        P("parts"),
    )
    out_specs = (P("space", "parts", None), P("space", None, None, "parts", None))

    def local(density, displacement, fixed, load_index, load_force, radius):
        alone = lax.axis_size("space") == load_index.shape[0]
        run = one_slab if alone else many_slabs
        return run(density, displacement, fixed, load_index, load_force, radius)

    return jax.shard_map(local, mesh=mesh, in_specs=in_specs, out_specs=out_specs, check_vma=False)
```

```python
import math

import jax
import jax.numpy as jnp
from jax import lax
from jax.experimental import pallas as pl
from jax.experimental.pallas import tpu as pltpu
from jax.sharding import PartitionSpec as P

SWEEPS = 3
SEARCH = 12


floor_modulus = 0.05
relax_factor = 0.6
move_limit = 0.2
density_floor = 0.01
volume_share = 0.5
log_lower = -16.0
log_span = 32.0
window_reach = 2

PLANE_SQUARES = (0, 1, 2, 4, 5, 8)
ALL_SQUARES = (0, 1, 2, 3, 4, 5, 6, 8, 9, 12)


def spot_iota(shape, dim):
    return lax.broadcasted_iota(jnp.int32, shape, dim)


def each_plane(planes, body, carry):
    for x in range(planes):
        carry = body(x, carry)
    return carry


def each_chunk(planes, count, body, carry):
    return lax.fori_loop(0, planes // count, lambda i, carry: body(i * count, carry), carry)


def layer_radius(radius_ref, layers, row_width):
    z = spot_iota((layers, row_width), 0)
    result = jnp.zeros((layers, row_width), jnp.int32)
    for layer in range(layers):
        result = jnp.where(z == layer, radius_ref[layer], result)
    return result.astype(jnp.float32)


def class_weights(radius_ref, weight_ref):
    layers, row_width = weight_ref.shape[1:]
    radial = layer_radius(radius_ref, layers, row_width)
    for place, square in enumerate(ALL_SQUARES):
        weight_ref[place] = jnp.maximum(radial - math.sqrt(square), 0.0)


def shift_sum(field, dim, distance):
    size = field.shape[dim]
    spot = spot_iota(field.shape, dim)
    ahead = jnp.where(spot < size - distance, pltpu.roll(field, size - distance, dim), 0.0)
    behind = jnp.where(spot >= distance, pltpu.roll(field, distance, dim), 0.0)
    return ahead + behind


def plane_sums(plane):
    beside = shift_sum(plane, 1, 1)
    further = shift_sum(plane, 1, 2)
    return {
        0: plane,
        1: beside + shift_sum(plane, 0, 1),
        2: shift_sum(beside, 0, 1),
        4: further + shift_sum(plane, 0, 2),
        5: shift_sum(further, 0, 1) + shift_sum(beside, 0, 2),
        8: shift_sum(further, 0, 2),
    }


def weigh(sums, weight_ref, square):
    result = None
    for inner in PLANE_SQUARES:
        term = weight_ref[ALL_SQUARES.index(inner + square)] * sums[inner]
        result = term if result is None else result + term
    return result


def forward_planes(plane, weight_ref):
    sums = plane_sums(plane)
    return [weigh(sums, weight_ref, square) for square in (0, 1, 4)]


def rows(x, layers, shift=0):
    return pl.ds(x * layers + shift, layers)


GAP = 8


def gapped(x, layers, shift=0):
    return pl.ds(GAP + x * (layers + GAP) + shift, layers)


def gap(x, layers):
    return pl.ds(x * (layers + GAP), GAP)


def edge_class(x, planes):
    return jnp.minimum(x, 2) + jnp.maximum(x - (planes - 3), 0)


def zero_edges(ref):
    planes = ref.shape[0]
    for place in (0, 1, planes - 2, planes - 1):
        ref[place] = jnp.zeros(ref.shape[1:], ref.dtype)


def group_spots(group, blocks):
    chips, own_planes = blocks.shape[:2]
    mine = lax.axis_index("space")
    core = mine ^ mine >> 1 ^ group
    return [
        (own_planes * (2 * chip + ((core ^ chip) & 1)) + own, (chip, own))
        for chip in range(chips)
        for own in range(own_planes)
    ]


def spread_group(blocks, spread):
    chips, own_planes, layers, row_width = blocks.shape
    zero_gap = jnp.zeros((GAP, row_width), jnp.float32)
    for ref in spread:
        ref[gap(0, layers)] = zero_gap
    for p in range(chips * own_planes):
        plane = blocks[p // own_planes, p % own_planes]
        for ref, field in zip(spread, (plane, shift_sum(plane, 1, 1), shift_sum(plane, 1, 2))):
            ref[gapped(p, layers)] = field
            ref[gap(p + 1, layers)] = zero_gap


def filter_plane(p, layers, spread, weight_ref):
    def around(place, distance):
        ref = spread[place]
        return ref[gapped(p, layers, distance)] + ref[gapped(p, layers, -distance)]

    sums = {
        0: spread[0][gapped(p, layers)],
        1: spread[1][gapped(p, layers)] + around(0, 1),
        2: around(1, 1),
        4: spread[2][gapped(p, layers)] + around(0, 2),
        5: around(2, 1) + around(1, 2),
        8: around(2, 2),
    }
    return [weigh(sums, weight_ref, square) for square in (0, 1, 4)]


def prepare_kernel(
    radius_hbm,
    index_hbm,
    force_hbm,
    fixed_hbm,
    density_ref,
    weight_ref,
    inverse_ref,
    free_ref,
    load_ref,
    spot_ref,
    filter_ref,
    radius_ref,
    index_ref,
    force_ref,
    fixed_ref,
    plane_ref,
    beside_ref,
    further_ref,
    arrived,
):
    copies = [
        pltpu.make_async_copy(source, target, arrived.at[place])
        for place, (source, target) in enumerate(
            (
                (radius_hbm, radius_ref),
                (index_hbm, index_ref),
                (force_hbm, force_ref),
                (fixed_hbm, fixed_ref),
            )
        )
    ]
    for copy in copies:
        copy.start()
    spread = (plane_ref, beside_ref, further_ref)
    spread_group(density_ref, spread)
    for copy in copies:
        copy.wait()
    planes, layers, row_width = free_ref.shape
    load_place = lax.axis_index("space")
    shape = (layers, row_width)
    z = spot_iota(shape, 0)
    y = spot_iota(shape, 1)

    class_weights(radius_ref, weight_ref)
    own_planes = density_ref.shape[1]
    for p in range(density_ref.shape[0] * own_planes):
        for place, field in enumerate(filter_plane(p, layers, spread, weight_ref)):
            filter_ref[place, p // own_planes, p % own_planes] = field

    ones = forward_planes(jnp.ones(shape, jnp.float32), weight_ref)
    for place, (lower, upper) in enumerate(((0, 2), (1, 2), (2, 2), (2, 1), (2, 0))):
        inverse_ref[place] = 1.0 / (
            ones[0] + min(lower, 1) * ones[1] + min(upper, 1) * ones[1]
            + (lower // 2) * ones[2] + (upper // 2) * ones[2]
        )

    def free_plane(x, carry):
        free_ref[x] = jnp.where(
            z == 0, 1.0 - fixed_ref[pl.ds(x, 1), :].astype(jnp.float32), 1.0
        )
        return carry

    each_plane(planes, free_plane, 0)

    own_index = index_ref[load_place]
    own_z = own_index // row_width % layers
    own_y = own_index % row_width
    hit = (z == own_z) & (y == own_y)
    for part in range(3):
        load_ref[part] = jnp.where(hit, force_ref[part, load_place], 0.0)
    own_x = (own_index // (layers * row_width)).astype(jnp.float32)
    spot_ref[...] = jnp.full(spot_ref.shape, own_x)


def sweep_kernel(
    spot_ref,
    load_ref,
    weight_ref,
    inverse_ref,
    free_ref,
    filter_ref,
    density_ref,
    start_ref,
    disp_ref,
    coef_ref,
    plane_ref,
    beside_ref,
    further_ref,
    near_ref,
    side_ref,
    far_ref,
    modulus_ref,
    across_ref,
    up_ref,
    right_ref,
    left_ref,
    rate_ref,
    first_ref,
):
    planes, layers, row_width = coef_ref.shape
    shape = (layers, row_width)
    z = spot_iota(shape, 0)
    y = spot_iota(shape, 1)
    zero = jnp.zeros(shape, jnp.float32)

    for ref in (side_ref, far_ref):
        zero_edges(ref)
    results = (near_ref, side_ref, far_ref)
    other_ref = density_ref.at[1]
    for x, spot in group_spots(0, other_ref):
        for place, ref in enumerate(results):
            ref[x + 2] = filter_ref[(place,) + spot]
    spread = (plane_ref, beside_ref, further_ref)
    spread_group(other_ref, spread)
    for p, (x, spot) in enumerate(group_spots(1, other_ref)):
        for ref, field in zip(results, filter_plane(p, layers, spread, weight_ref)):
            ref[x + 2] = field

    for ref in (first_ref, disp_ref):
        for part in range(3):
            ref[part, rows(0, layers)] = zero
            ref[part, rows(planes + 1, layers)] = zero

    def store_faces(slot, modulus, above, below, later, before, free, start, views):
        across, up_view, right_view, left_view, rate, source = views
        across[slot] = later
        up = jnp.where(z < layers - 1, 0.5 * (modulus + above), 0.0)
        right = jnp.where(
            y < row_width - 1, 0.5 * (modulus + pltpu.roll(modulus, row_width - 1, 1)), 0.0
        )
        left = jnp.where(y > 0, 0.5 * (modulus + pltpu.roll(modulus, 1, 1)), 0.0)
        down = jnp.where(z > 0, 0.5 * (modulus + below), 0.0)
        up_view[rows(slot, layers)] = up
        right_view[slot] = right
        left_view[slot] = left
        sums = (before + later, up + down, left + right)
        every = sums[0] + sums[1] + sums[2]
        diagonal = [every + part_sum for part_sum in sums]
        pair = diagonal[0] * diagonal[1]
        push = relax_factor * free / (pair * diagonal[2])
        side = push * diagonal[2]
        for part, factor in enumerate((side * diagonal[1], side * diagonal[0], push * pair)):
            rate[part, slot] = factor
            source[part, rows(slot, layers)] = start[part] * free

    piece = planes // 2

    def modulus_piece(first, carry):
        count = piece
        near = near_ref.at[pl.ds(first + 2, count)]
        side = side_ref.at[pl.ds(first + 1, count + 2)]
        far = far_ref.at[pl.ds(first, count + 4)]
        moduli = modulus_ref.at[pl.ds(first * layers, (count + 1) * layers)]
        coef = coef_ref.at[pl.ds(first, count)]
        free = free_ref.at[pl.ds(first, count)]
        views = (
            across_ref.at[pl.ds(first, count)],
            up_ref.at[pl.ds(first * layers, count * layers)],
            right_ref.at[pl.ds(first, count)],
            left_ref.at[pl.ds(first, count)],
            rate_ref.at[:, pl.ds(first, count)],
            first_ref.at[:, pl.ds(first * layers, count * layers)],
        )
        modulus, before = carry
        for p in range(count):
            inverse = inverse_ref[edge_class(first + p, planes)]
            filtered = near[p] + side[p] + side[p + 2] + far[p] + far[p + 4]
            filtered = filtered * inverse
            later = floor_modulus + (1.0 - floor_modulus) * (filtered * filtered * filtered)
            coef[p] = 3.0 * (1.0 - floor_modulus) * (filtered * filtered) * inverse
            moduli[rows(p + 1, layers)] = later
            ahead = 0.5 * (modulus + later)
            if p == 0:
                ahead = jnp.where(first > 0, ahead, 0.0)
            above = moduli[rows(p, layers, 1)] if p else pltpu.roll(modulus, layers - 1, 0)
            below = moduli[rows(p, layers, -1)] if p else pltpu.roll(modulus, 1, 0)
            previous = jnp.maximum(first + p - 1, 0)
            store_faces(
                p,
                modulus,
                above,
                below,
                ahead,
                before,
                free_ref[previous],
                [start_ref[part, previous] for part in range(3)],
                views,
            )
            modulus, before = later, ahead
        return modulus, before

    modulus, before = each_chunk(
        planes, piece, modulus_piece, (jnp.ones(shape, jnp.float32), zero)
    )
    store_faces(
        planes,
        modulus,
        pltpu.roll(modulus, layers - 1, 0),
        pltpu.roll(modulus, 1, 0),
        zero,
        before,
        free_ref[planes - 1],
        [start_ref[part, planes - 1] for part in range(3)],
        (across_ref, up_ref, right_ref, left_ref, rate_ref, first_ref),
    )

    own_x = jnp.max(spot_ref[...]).astype(jnp.int32)

    def sweep(source, target):
        def sweep_piece(first, carry):
            count = planes
            old = source.at[:, pl.ds(first * layers, (count + 2) * layers)]
            new = target.at[:, pl.ds((first + 1) * layers, count * layers)]
            across = across_ref.at[pl.ds(first, count + 1)]
            up = up_ref.at[pl.ds(first * layers, (count + 1) * layers)]
            right = right_ref.at[pl.ds(first + 1, count)]
            left = left_ref.at[pl.ds(first + 1, count)]
            rate = rate_ref.at[:, pl.ds(first + 1, count)]
            behind = [old[part, rows(0, layers)] for part in range(3)]
            here = [old[part, rows(1, layers)] for part in range(3)]
            for p in range(count):
                ahead = [old[part, rows(p + 2, layers)] for part in range(3)]
                for part in range(3):
                    pulls = [
                        across[p] * behind[part] + across[p + 1] * ahead[part],
                        up[rows(p + 1, layers)] * old[part, rows(p + 1, layers, 1)]
                        + up[rows(p + 1, layers, -1)] * old[part, rows(p + 1, layers, -1)],
                        right[p] * pltpu.roll(here[part], row_width - 1, 1)
                        + left[p] * pltpu.roll(here[part], 1, 1),
                    ]
                    pull = pulls[0] + pulls[1] + pulls[2] + pulls[part]
                    new[part, rows(p, layers)] = (
                        1.0 - relax_factor
                    ) * here[part] + rate[part, p] * pull
                behind, here = here, ahead
            return carry

        sweep_piece(0, 0)
        for part in range(3):
            target[part, rows(own_x + 1, layers)] += rate_ref[part, own_x + 1] * load_ref[part]

    def two_sweeps(turn, carry):
        sweep(first_ref, disp_ref)

        @pl.when(turn < SWEEPS // 2)
        def _():
            sweep(disp_ref, first_ref)

        return carry

    lax.fori_loop(0, SWEEPS // 2 + 1, two_sweeps, 0)


def filter_group(group, shares, weight_ref, near_ref, far_ref, result_ref):
    chips, own_planes, layers, row_width = result_ref.shape
    zero_gap = jnp.zeros((GAP, row_width), jnp.float32)
    mine = lax.axis_index("space")
    core = (mine ^ mine >> 1 ^ group) & 1
    count = shares[0].shape[0] - own_planes
    views = [
        [ref.at[pl.ds(own_planes * start, count)] for ref in shares] for start in (core, 1 - core)
    ]
    for ref in (near_ref, far_ref):
        ref[gap(0, layers)] = zero_gap
    for p in range(chips * own_planes):
        chip, own = p // own_planes, p % own_planes
        plane, beside, further = views[chip & 1]
        x = 2 * own_planes * chip + own + 2

        def around(ref, distance):
            return ref[x + distance] + ref[x - distance]

        sums = {
            0: plane[x],
            1: beside[x] + around(plane, 1),
            2: around(beside, 1),
            4: further[x] + around(plane, 2),
            5: around(further, 1) + around(beside, 2),
            8: around(further, 2),
        }
        level = weigh(sums, weight_ref, 0)
        for ref, square in ((near_ref, 1), (far_ref, 4)):
            ref[gapped(p, layers)] = weigh(sums, weight_ref, square)
            ref[gap(p + 1, layers)] = zero_gap
        result_ref[chip, own] = (
            level
            + near_ref[gapped(p, layers, 1)]
            + near_ref[gapped(p, layers, -1)]
            + far_ref[gapped(p, layers, 2)]
            + far_ref[gapped(p, layers, -2)]
        )


def share_kernel(
    disp_ref,
    coef_ref,
    weight_ref,
    sent_ref,
    plane_ref,
    beside_ref,
    further_ref,
    near_ref,
    far_ref,
):
    planes, layers, row_width = coef_ref.shape
    load_cases = lax.axis_size("space")
    shape = (layers, row_width)
    z = spot_iota(shape, 0)
    y = spot_iota(shape, 1)
    zero = jnp.zeros(shape, jnp.float32)
    shares = (plane_ref, beside_ref, further_ref)
    for ref in shares:
        zero_edges(ref)

    count = planes // 2

    def share_chunk(first, before):
        disp = disp_ref.at[:, pl.ds((first + 1) * layers, (count + 1) * layers)]
        coef = coef_ref.at[pl.ds(first, count)]
        plane, beside, further = (ref.at[pl.ds(first + 2, count)] for ref in shares)
        here = [disp[part, rows(0, layers)] for part in range(3)]
        for p in range(count):
            later = [disp[part, rows(p + 1, layers)] for part in range(3)]
            ahead, upward, right = zero, zero, zero
            for part in range(3):
                step = later[part] - here[part]
                climb = disp[part, rows(p, layers, 1)] - here[part]
                slide = pltpu.roll(here[part], row_width - 1, 1) - here[part]
                ahead = ahead + (2.0 if part == 0 else 1.0) * (step * step)
                upward = upward + (2.0 if part == 1 else 1.0) * (climb * climb)
                right = right + (2.0 if part == 2 else 1.0) * (slide * slide)
            if p == count - 1:
                ahead = jnp.where(first + count < planes, ahead, 0.0)
            upward = jnp.where(z < layers - 1, upward, 0.0)
            right = jnp.where(y < row_width - 1, right, 0.0)
            total = before + ahead + upward + pltpu.roll(upward, 1, 0)
            total = total + right + pltpu.roll(right, 1, 1)
            share = (0.5 / load_cases) * total * coef[p]
            plane[p] = share
            beside[p] = shift_sum(share, 1, 1)
            further[p] = shift_sum(share, 1, 2)
            before, here = ahead, later
        return before

    each_chunk(planes, count, share_chunk, zero)
    filter_group(1, shares, weight_ref, near_ref, far_ref, sent_ref)


def kept_kernel(
    disp_ref,
    weight_ref,
    plane_ref,
    beside_ref,
    further_ref,
    disp_hbm,
    kept_ref,
    near_ref,
    far_ref,
    stored,
):
    layers = kept_ref.shape[2]
    inner = pl.ds(layers, disp_ref.shape[1] - 2 * layers)
    store = pltpu.make_async_copy(disp_ref.at[:, inner], disp_hbm, stored)
    store.start()
    shares = (plane_ref, beside_ref, further_ref)
    filter_group(0, shares, weight_ref, near_ref, far_ref, kept_ref)
    store.wait()


def design_kernel(root_ref, density_ref, new_ref, pull_ref, low_ref, high_ref):
    groups, chips, own_planes, layers, row_width = density_ref.shape
    tile_rows = pull_ref.shape[1]
    steps = layers // tile_rows
    shape = (tile_rows, row_width)
    zero = jnp.zeros(shape, jnp.float32)
    tiles = [
        (group, chip, own, pl.ds(step * tile_rows, tile_rows))
        for group in range(groups)
        for chip in range(chips)
        for own in range(own_planes)
        for step in range(steps)
    ]
    for place, spot in enumerate(tiles):
        density = density_ref[spot]
        pull_ref[place] = density * root_ref[spot]
        low_ref[place] = jnp.maximum(density - move_limit, density_floor)
        high_ref[place] = jnp.minimum(density + move_limit, 1.0)

    target = volume_share * len(tiles) * tile_rows * row_width

    def exceeds(total):
        volume = jnp.sum(jnp.sum(total, axis=0, keepdims=True), axis=1, keepdims=True)
        return jnp.broadcast_to(volume, shape) > target

    def middles_of(lower, span):
        half, quarter = span * 0.5, span * 0.25
        return lower + quarter, lower + half, lower + half + quarter

    def factors_of(lower, span):
        return [jnp.exp(-0.5 * middle) for middle in middles_of(lower, span)]

    def halve_twice(step, state):
        lower, span, *factors = state
        places = (lower,) + middles_of(lower, span)
        quarter = span * 0.25
        ahead = [factors_of(place, quarter) for place in places]
        totals = [[zero, zero] for _ in factors]
        for place in range(len(tiles)):
            pull, low, high = pull_ref[place], low_ref[place], high_ref[place]
            for total, factor in zip(totals, factors):
                trial = jnp.minimum(jnp.maximum(pull * factor, low), high)
                total[place % 2] = total[place % 2] + trial
        first, second, third = (exceeds(even + odd) for even, odd in totals)

        def pick(options):
            upper = jnp.where(third, options[3], options[2])
            return jnp.where(second, upper, jnp.where(first, options[1], options[0]))

        return (pick(places), quarter, *(pick(options) for options in zip(*ahead)))

    lower, span = jnp.full(shape, log_lower), jnp.full(shape, log_span)
    state = (lower, span, *factors_of(lower, span))
    lower, span, *_ = lax.fori_loop(0, SEARCH // 2, halve_twice, state)
    factor = jnp.exp(-0.5 * (lower + 0.5 * span))
    own_chip = lax.axis_index("space") >> 1
    for own in range(own_planes):
        for step in range(steps):
            place = (own_chip * own_planes + own) * steps + step
            new_ref[own, pl.ds(step * tile_rows, tile_rows)] = jnp.minimum(
                jnp.maximum(pull_ref[place] * factor, low_ref[place]), high_ref[place]
            )


def in_vmem():
    return pl.BlockSpec(memory_space=pltpu.VMEM)


KERNEL_VMEM = 24 * 2**20


def floats(*shape):
    return jax.ShapeDtypeStruct(shape, jnp.float32)


def prepare_call(density, radius, load_index, load_force, fixed):
    chips, own_planes, layers, row_width = density.shape
    planes = fixed.shape[0]
    spread = pltpu.VMEM((chips * own_planes * (layers + GAP) + GAP, row_width), jnp.float32)
    return pl.pallas_call(
        prepare_kernel,
        out_shape=[
            floats(len(ALL_SQUARES), layers, row_width),
            floats(2 * window_reach + 1, layers, row_width),
            floats(planes, layers, row_width),
            floats(3, layers, row_width),
            floats(8, row_width),
            floats(3, *density.shape),
        ],
        in_specs=[pl.BlockSpec(memory_space=pltpu.HBM)] * 4 + [in_vmem()],
        out_specs=[in_vmem()] * 6,
        scratch_shapes=[
            pltpu.SMEM(radius.shape, radius.dtype),
            pltpu.SMEM(load_index.shape, load_index.dtype),
            pltpu.SMEM(load_force.shape, load_force.dtype),
            pltpu.VMEM(fixed.shape, fixed.dtype),
            spread,
            spread,
            spread,
            pltpu.SemaphoreType.DMA((4,)),
        ],
        compiler_params=pltpu.CompilerParams(vmem_limit_bytes=KERNEL_VMEM),
        cost_estimate=pl.CostEstimate(
            flops=80 * planes * layers * row_width,
            bytes_accessed=8 * planes * layers * row_width,
            transcendentals=0,
        ),
        name="prepare",
    )(
        *(
            pltpu.with_memory_space_constraint(array, pltpu.HBM)
            for array in (radius, load_index, load_force, fixed)
        ),
        density,
    )


def sweep_call(spot, load, weights, inverses, free, filtered, density, displacement):
    groups, chips, own_planes, layers, row_width = density.shape
    planes = groups * chips * own_planes

    def scratch(*lead):
        return pltpu.VMEM(lead + (row_width,), jnp.float32)

    return pl.pallas_call(
        sweep_kernel,
        out_shape=[
            floats(3, (planes + 2) * layers, row_width),
            floats(planes, layers, row_width),
        ],
        in_specs=[in_vmem()] * 8,
        out_specs=[in_vmem()] * 2,
        scratch_shapes=[
            scratch(planes // 2 * (layers + GAP) + GAP),
            scratch(planes // 2 * (layers + GAP) + GAP),
            scratch(planes // 2 * (layers + GAP) + GAP),
            scratch(planes + 4, layers),
            scratch(planes + 4, layers),
            scratch(planes + 4, layers),
            scratch((planes + 1) * layers),
            scratch(planes + 1, layers),
            scratch((planes + 1) * layers),
            scratch(planes + 1, layers),
            scratch(planes + 1, layers),
            scratch(3, planes + 1, layers),
            scratch(3, (planes + 2) * layers),
        ],
        compiler_params=pltpu.CompilerParams(vmem_limit_bytes=KERNEL_VMEM),
        name="sweeps",
    )(spot, load, weights, inverses, free, filtered, density, displacement)


def share_call(disp, coef, weights, group_shape):
    planes, layers, row_width = coef.shape
    gaps = pltpu.VMEM((planes // 2 * (layers + GAP) + GAP, row_width), jnp.float32)
    return pl.pallas_call(
        share_kernel,
        out_shape=[floats(*group_shape)] + [floats(planes + 4, layers, row_width)] * 3,
        in_specs=[in_vmem()] * 3,
        out_specs=[in_vmem()] * 4,
        scratch_shapes=[gaps, gaps],
        compiler_params=pltpu.CompilerParams(vmem_limit_bytes=KERNEL_VMEM),
        name="share",
    )(disp, coef, weights)


def kept_call(disp, weights, shares, group_shape):
    parts, disp_rows, row_width = disp.shape
    chips, own_planes, layers = group_shape[:3]
    gaps = pltpu.VMEM((chips * own_planes * (layers + GAP) + GAP, row_width), jnp.float32)
    return pl.pallas_call(
        kept_kernel,
        out_shape=[floats(parts, disp_rows - 2 * layers, row_width), floats(*group_shape)],
        in_specs=[in_vmem()] * 5,
        out_specs=[pl.BlockSpec(memory_space=pltpu.HBM), in_vmem()],
        scratch_shapes=[gaps, gaps, pltpu.SemaphoreType.DMA(())],
        compiler_params=pltpu.CompilerParams(vmem_limit_bytes=KERNEL_VMEM),
        cost_estimate=pl.CostEstimate(
            flops=20 * disp.size, bytes_accessed=8 * disp.size, transcendentals=0
        ),
        name="kept",
    )(disp, weights, *shares)


def design_call(root, density):
    tile_rows = min(8, density.shape[-2])
    row_width = density.shape[-1]
    tiles = pltpu.VMEM((density.size // (tile_rows * row_width), tile_rows, row_width), jnp.float32)
    return pl.pallas_call(
        design_kernel,
        out_shape=floats(*density.shape[2:]),
        in_specs=[in_vmem()] * 2,
        out_specs=in_vmem(),
        scratch_shapes=[tiles] * 3,
        compiler_params=pltpu.CompilerParams(vmem_limit_bytes=KERNEL_VMEM),
        name="design",
    )(root, density)


def other_core(block):
    devices = lax.axis_size("space")
    return lax.ppermute(block, "space", [(i, i ^ 1) for i in range(devices)])


def chip_groups():
    chips = lax.axis_size("space") // 2
    return [[2 * chip + (chip ^ group) % 2 for chip in range(chips)] for group in range(2)]


def between_chips(pieces):
    return lax.all_to_all(pieces, "space", 0, 0, axis_index_groups=chip_groups())


def chip_gathered(block):
    chips = lax.axis_size("space") // 2
    return between_chips(jnp.broadcast_to(block[None], (chips,) + block.shape))


def with_other_core(blocks):
    return jnp.stack([blocks, other_core(blocks)])


def scattered_sum(sent, make_kept):
    received = other_core(sent)
    *others, kept = make_kept()
    return jnp.sum(between_chips(kept + received), axis=0), others


def one_slab(density, displacement, fixed, load_index, load_force, radius):
    same_group, small = lax.optimization_barrier(
        (chip_gathered(density), (radius, load_index, load_force.T, fixed))
    )
    other_group = other_core(same_group)
    weights, inverses, free, load, spot, filtered = prepare_call(same_group, *small)
    whole = jnp.stack([same_group, other_group])
    disp, coef = sweep_call(
        spot, load, weights, inverses, free, filtered, whole, displacement[0]
    )
    sent, *shares = share_call(disp, coef, weights, same_group.shape)
    sent, disp, shares = lax.optimization_barrier((sent, disp, shares))
    squares, (new_displacement,) = scattered_sum(
        sent, lambda: kept_call(disp, weights, shares, same_group.shape)
    )
    root = with_other_core(chip_gathered(jnp.sqrt(squares)))
    new_density = design_call(root, whole)
    return new_density, new_displacement.reshape(displacement.shape)


def from_behind(block, axis, distance):
    devices = range(lax.axis_size(axis))
    route = [(i - distance, i) for i in devices if i - distance in devices]
    return lax.ppermute(block, axis, route)


def extended(x, sides, width):
    for axis, dim in sides:
        size, length = (lax.axis_size(axis), x.shape[dim])
        up = [(i, (i + 1) % size) for i in range(size - 1)]
        down = [(j, i) for i, j in up]
        last = lax.slice_in_dim(x, length - width, length, axis=dim)
        first = lax.slice_in_dim(x, 0, width, axis=dim)
        before = lax.ppermute(last, axis, up)
        after = lax.ppermute(first, axis, down)
        x = jnp.concatenate([before, x, after], axis=dim)
    return x


def from_partner(x, axis, bit):
    return lax.ppermute(x, axis, [(i, i ^ 1 << bit) for i in range(lax.axis_size(axis))])


def window_offsets():
    offsets_list = []
    for across in range(-window_reach, window_reach + 1):
        for upward in range(-window_reach, window_reach + 1):
            for sideways in range(-window_reach, window_reach + 1):
                length = math.sqrt(across * across + upward * upward + sideways * sideways)
                offsets_list.append((across, upward, sideways, length))
    return offsets_list


def layer_weights(radius):
    radial = radius.astype(jnp.float32)
    return jnp.stack(
        [jnp.maximum(radial - length, 0.0) for across, upward, sideways, length in window_offsets()]
    )


def pad_axis(grid_field, along_axis, before, after_cells):
    widths = [(0, 0)] * grid_field.ndim
    widths[along_axis] = (before, after_cells)
    return jnp.pad(grid_field, widths)


def pad_sides(grid_field):
    return jnp.pad(grid_field, ((0, 0), (window_reach, window_reach), (window_reach, window_reach)))


def filter_forward(padded, weights):
    out_rows = padded.shape[0] - 2 * window_reach
    layers = padded.shape[1] - 2 * window_reach
    row_width = padded.shape[2] - 2 * window_reach
    result = jnp.zeros((out_rows, layers, row_width), jnp.float32)
    for offset_index, (across, upward, sideways, length) in enumerate(window_offsets()):
        shifted = padded[
            window_reach + across : window_reach + across + out_rows,
            window_reach + upward : window_reach + upward + layers,
            window_reach + sideways : window_reach + sideways + row_width,
        ]
        result = result + weights[offset_index][None, :, None] * shifted
    return result


def filter_backward(padded, padded_weights):
    out_rows = padded.shape[0] - 2 * window_reach
    layers = padded.shape[1] - 2 * window_reach
    row_width = padded.shape[2] - 2 * window_reach
    result = jnp.zeros((out_rows, layers, row_width), jnp.float32)
    for offset_index, (across, upward, sideways, length) in enumerate(window_offsets()):
        shifted = padded[
            window_reach - across : window_reach - across + out_rows,
            window_reach - upward : window_reach - upward + layers,
            window_reach - sideways : window_reach - sideways + row_width,
        ]
        layer_part = padded_weights[
            offset_index, window_reach - upward : window_reach - upward + layers
        ]
        result = result + layer_part[None, :, None] * shifted
    return result


def stiff_factors(direction):
    return jnp.array(
        [2.0 if component == direction else 1.0 for component in range(3)], jnp.float32
    ).reshape(3, 1, 1, 1)


def relax_slab(padded, displace, face_x, face_z, face_y, force_field, free_cells, diagonal):
    flux_x = stiff_factors(0) * face_x * jnp.diff(padded, axis=1)
    stencil_image = flux_x[:, :-1] - flux_x[:, 1:]
    flux_z = stiff_factors(1) * face_z * jnp.diff(displace, axis=2)
    stencil_image = stencil_image + pad_axis(flux_z, 2, 1, 0) - pad_axis(flux_z, 2, 0, 1)
    flux_y = stiff_factors(2) * face_y * jnp.diff(displace, axis=3)
    stencil_image = stencil_image + pad_axis(flux_y, 3, 1, 0) - pad_axis(flux_y, 3, 0, 1)
    return free_cells * (displace + relax_factor * (force_field - stencil_image) / diagonal)


def slab_energy(grid_field, along_axis, direction, load_cases):
    change = jnp.diff(grid_field, axis=along_axis)
    return jnp.sum(stiff_factors(direction) * change * change, axis=0) / load_cases


def neighbour_planes(displace, load_cases, axis_devices):
    if axis_devices > load_cases:
        below = from_behind(displace[:, -1:], "space", load_cases)
        above = from_behind(displace[:, :1], "space", -load_cases)
    else:
        below = jnp.zeros_like(displace[:, :1])
        above = jnp.zeros_like(displace[:, :1])
    return jnp.concatenate([below, displace, above], axis=1)


def many_slabs(density, displacement, fixed, load_index, load_force, radius):
    slab_rows, layers, row_width = density.shape
    load_cases = load_index.shape[0]
    level_count = load_cases.bit_length() - 1
    axis_devices = lax.axis_size("space")
    axis_place = lax.axis_index("space")
    slab_planes = slab_rows * load_cases
    slab_place = axis_place // load_cases
    load_place = axis_place % load_cases
    total_rows = slab_rows * axis_devices
    weights = layer_weights(radius)
    padded_weights = pad_axis(weights, 1, window_reach, window_reach)
    global_rows = (
        jnp.arange(slab_rows + 2 * window_reach, dtype=jnp.int32)
        + axis_place * slab_rows
        - window_reach
    )
    deep_inside = ((global_rows >= 0) & (global_rows < total_rows)).astype(jnp.float32)
    inside_field = deep_inside[:, None, None] * pad_sides(
        jnp.ones((slab_rows + 2 * window_reach, layers, row_width), jnp.float32)
    )
    total_weight = filter_forward(inside_field, weights)
    slab_start = slab_place * slab_planes
    margin_rows = jnp.arange(slab_planes + 2, dtype=jnp.int32) + slab_start - 1
    margin_inside = ((margin_rows >= 0) & (margin_rows < total_rows)).astype(jnp.float32)
    face_valid = margin_inside[1:] * margin_inside[:-1]
    fixed_slab = lax.dynamic_slice_in_dim(fixed, slab_start, slab_planes, 0).astype(jnp.float32)
    bottom_layer = (jnp.arange(layers, dtype=jnp.int32) == 0).astype(jnp.float32)
    free_cells = 1.0 - bottom_layer[None, :, None] * fixed_slab[:, None, :]
    slab_cells = slab_planes * layers * row_width
    cell_index = jnp.arange(slab_cells, dtype=jnp.int32) + slab_place * slab_cells
    load_hot = jnp.arange(load_cases, dtype=jnp.int32) == load_place
    own_index = jnp.sum(jnp.where(load_hot, load_index, 0))
    own_force = jnp.sum(load_hot.astype(jnp.float32)[:, None] * load_force, axis=0)
    load_hits = (cell_index == own_index).astype(jnp.float32)
    force_field = (own_force[:, None] * load_hits[None, :]).reshape(
        3, slab_planes, layers, row_width
    )
    displace = displacement[0] * free_cells
    target = volume_share * total_rows * layers * row_width
    padded = neighbour_planes(displace, load_cases, axis_devices)
    halo_density = extended(density, (("space", 0),), window_reach)
    filtered = filter_forward(pad_sides(halo_density), weights) / total_weight
    whole_field = lax.all_gather(filtered, "space", axis=0, tiled=True)
    margin = lax.dynamic_slice_in_dim(
        pad_axis(whole_field, 0, 1, 1), slab_start, slab_planes + 2, 0
    )
    moduli = floor_modulus + (1.0 - floor_modulus) * margin**3
    face_x = 0.5 * (moduli[1:] + moduli[:-1]) * face_valid[:, None, None]
    inner_moduli = moduli[1:-1]
    face_z = 0.5 * (inner_moduli[:, 1:] + inner_moduli[:, :-1])
    face_y = 0.5 * (inner_moduli[:, :, 1:] + inner_moduli[:, :, :-1])
    sum_x = face_x[:-1] + face_x[1:]
    sum_z = pad_axis(face_z, 1, 1, 0) + pad_axis(face_z, 1, 0, 1)
    sum_y = pad_axis(face_y, 2, 1, 0) + pad_axis(face_y, 2, 0, 1)
    diagonal = stiff_factors(0) * sum_x + stiff_factors(1) * sum_z + stiff_factors(2) * sum_y
    for sweep_index in range(SWEEPS):
        displace = relax_slab(
            padded, displace, face_x, face_z, face_y, force_field, free_cells, diagonal
        )
        padded = neighbour_planes(displace, load_cases, axis_devices)
    energy_x = slab_energy(padded, 1, 0, load_cases) * face_valid[:, None, None]
    energy_z = slab_energy(displace, 2, 1, load_cases)
    energy_y = slab_energy(displace, 3, 2, load_cases)
    sens_term = 0.5 * (
        energy_x[:-1]
        + energy_x[1:]
        + pad_axis(energy_z, 1, 1, 0)
        + pad_axis(energy_z, 1, 0, 1)
        + pad_axis(energy_y, 2, 1, 0)
        + pad_axis(energy_y, 2, 0, 1)
    )
    sensitive = sens_term
    for level in reversed(range(level_count)):
        half_rows = sensitive.shape[0] // 2
        upper_side = load_place // 2**level % 2 == 1
        outgoing = jnp.where(upper_side, sensitive[:half_rows], sensitive[half_rows:])
        keeping = jnp.where(upper_side, sensitive[half_rows:], sensitive[:half_rows])
        sensitive = keeping + from_partner(outgoing, "space", level)
    weighted_share = 3.0 * (1.0 - floor_modulus) * filtered**2 * sensitive / total_weight
    halo_share = extended(weighted_share, (("space", 0),), window_reach)
    root_term = jnp.sqrt(filter_backward(pad_sides(halo_share), padded_weights))
    lowest = jnp.maximum(density - move_limit, density_floor)
    highest = jnp.minimum(density + move_limit, 1.0)
    design_now = density

    def trial_design(log_level):
        return jnp.clip(design_now * root_term * jnp.exp(-0.5 * log_level), lowest, highest)

    start_state = (jnp.asarray(log_lower, jnp.float32), jnp.asarray(log_span, jnp.float32))

    def halve(search_step, search_state):
        lower_end, span_width = search_state
        half_span = span_width * 0.5
        middle = lower_end + half_span
        volume_total = lax.psum(jnp.sum(trial_design(middle)), "space")
        return (jnp.where(volume_total > target, middle, lower_end), half_span)

    lower_end, span_width = lax.fori_loop(0, SEARCH, halve, start_state)
    density = trial_design(lower_end + 0.5 * span_width)
    new_displacement = displace[None]
    return (density, new_displacement)


def solution(mesh):
    in_specs = (
        P("space", "parts", None),
        P("space", None, None, "parts", None),
        P(None, "parts"),
        P("parts"),
        P("parts", None),
        P("parts"),
    )
    out_specs = (P("space", "parts", None), P("space", None, None, "parts", None))

    def local(density, displacement, fixed, load_index, load_force, radius):
        alone = lax.axis_size("space") == load_index.shape[0]
        run = one_slab if alone else many_slabs
        return run(density, displacement, fixed, load_index, load_force, radius)

    return jax.shard_map(local, mesh=mesh, in_specs=in_specs, out_specs=out_specs, check_vma=False)
```

```python
import math

import jax
import jax.numpy as jnp
from jax import lax
from jax.experimental import pallas as pl
from jax.experimental.pallas import tpu as pltpu
from jax.sharding import PartitionSpec as P

SWEEPS = 3
SEARCH = 12


floor_modulus = 0.05
relax_factor = 0.6
move_limit = 0.2
density_floor = 0.01
volume_share = 0.5
log_lower = -16.0
log_span = 32.0
window_reach = 2

PLANE_SQUARES = (0, 1, 2, 4, 5, 8)
ALL_SQUARES = (0, 1, 2, 3, 4, 5, 6, 8, 9, 12)


def spot_iota(shape, dim):
    return lax.broadcasted_iota(jnp.int32, shape, dim)


def each_plane(planes, body, carry):
    for x in range(planes):
        carry = body(x, carry)
    return carry


def each_chunk(planes, count, body, carry):
    return lax.fori_loop(0, planes // count, lambda i, carry: body(i * count, carry), carry)


def layer_radius(radius_ref, layers, row_width):
    z = spot_iota((layers, row_width), 0)
    result = jnp.zeros((layers, row_width), jnp.int32)
    for layer in range(layers):
        result = jnp.where(z == layer, radius_ref[layer], result)
    return result.astype(jnp.float32)


def class_weights(radius_ref, weight_ref):
    layers, row_width = weight_ref.shape[1:]
    radial = layer_radius(radius_ref, layers, row_width)
    for place, square in enumerate(ALL_SQUARES):
        weight_ref[place] = jnp.maximum(radial - math.sqrt(square), 0.0)


def shift_sum(field, dim, distance):
    size = field.shape[dim]
    spot = spot_iota(field.shape, dim)
    ahead = jnp.where(spot < size - distance, pltpu.roll(field, size - distance, dim), 0.0)
    behind = jnp.where(spot >= distance, pltpu.roll(field, distance, dim), 0.0)
    return ahead + behind


def plane_sums(plane):
    beside = shift_sum(plane, 1, 1)
    further = shift_sum(plane, 1, 2)
    return {
        0: plane,
        1: beside + shift_sum(plane, 0, 1),
        2: shift_sum(beside, 0, 1),
        4: further + shift_sum(plane, 0, 2),
        5: shift_sum(further, 0, 1) + shift_sum(beside, 0, 2),
        8: shift_sum(further, 0, 2),
    }


def weigh(sums, weight_ref, square):
    result = None
    for inner in PLANE_SQUARES:
        term = weight_ref[ALL_SQUARES.index(inner + square)] * sums[inner]
        result = term if result is None else result + term
    return result


def forward_planes(plane, weight_ref):
    sums = plane_sums(plane)
    return [weigh(sums, weight_ref, square) for square in (0, 1, 4)]


def rows(x, layers, shift=0):
    return pl.ds(x * layers + shift, layers)


GAP = 8


def gapped(x, layers, shift=0):
    return pl.ds(GAP + x * (layers + GAP) + shift, layers)


def gap(x, layers):
    return pl.ds(x * (layers + GAP), GAP)


def edge_class(x, planes):
    return jnp.minimum(x, 2) + jnp.maximum(x - (planes - 3), 0)


def zero_edges(ref):
    planes = ref.shape[0]
    for place in (0, 1, planes - 2, planes - 1):
        ref[place] = jnp.zeros(ref.shape[1:], ref.dtype)


def group_spots(group, blocks):
    chips, own_planes = blocks.shape[:2]
    mine = lax.axis_index("space")
    core = mine ^ mine >> 1 ^ group
    return [
        (own_planes * (2 * chip + ((core ^ chip) & 1)) + own, (chip, own))
        for chip in range(chips)
        for own in range(own_planes)
    ]


def spread_group(blocks, spread):
    chips, own_planes, layers, row_width = blocks.shape
    zero_gap = jnp.zeros((GAP, row_width), jnp.float32)
    for ref in spread:
        ref[gap(0, layers)] = zero_gap
    for p in range(chips * own_planes):
        plane = blocks[p // own_planes, p % own_planes]
        for ref, field in zip(spread, (plane, shift_sum(plane, 1, 1), shift_sum(plane, 1, 2))):
            ref[gapped(p, layers)] = field
            ref[gap(p + 1, layers)] = zero_gap


def filter_plane(p, layers, spread, weight_ref):
    def around(place, distance):
        ref = spread[place]
        return ref[gapped(p, layers, distance)] + ref[gapped(p, layers, -distance)]

    sums = {
        0: spread[0][gapped(p, layers)],
        1: spread[1][gapped(p, layers)] + around(0, 1),
        2: around(1, 1),
        4: spread[2][gapped(p, layers)] + around(0, 2),
        5: around(2, 1) + around(1, 2),
        8: around(2, 2),
    }
    return [weigh(sums, weight_ref, square) for square in (0, 1, 4)]


def prepare_kernel(
    radius_hbm,
    index_hbm,
    force_hbm,
    fixed_hbm,
    density_ref,
    weight_ref,
    inverse_ref,
    free_ref,
    load_ref,
    spot_ref,
    filter_ref,
    radius_ref,
    index_ref,
    force_ref,
    fixed_ref,
    plane_ref,
    beside_ref,
    further_ref,
    arrived,
):
    copies = [
        pltpu.make_async_copy(source, target, arrived.at[place])
        for place, (source, target) in enumerate(
            (
                (radius_hbm, radius_ref),
                (index_hbm, index_ref),
                (force_hbm, force_ref),
                (fixed_hbm, fixed_ref),
            )
        )
    ]
    for copy in copies:
        copy.start()
    spread = (plane_ref, beside_ref, further_ref)
    spread_group(density_ref, spread)
    for copy in copies:
        copy.wait()
    planes, layers, row_width = free_ref.shape
    load_place = lax.axis_index("space")
    shape = (layers, row_width)
    z = spot_iota(shape, 0)
    y = spot_iota(shape, 1)

    class_weights(radius_ref, weight_ref)
    own_planes = density_ref.shape[1]
    for p in range(density_ref.shape[0] * own_planes):
        for place, field in enumerate(filter_plane(p, layers, spread, weight_ref)):
            filter_ref[place, p // own_planes, p % own_planes] = field

    ones = forward_planes(jnp.ones(shape, jnp.float32), weight_ref)
    for place, (lower, upper) in enumerate(((0, 2), (1, 2), (2, 2), (2, 1), (2, 0))):
        inverse_ref[place] = 1.0 / (
            ones[0] + min(lower, 1) * ones[1] + min(upper, 1) * ones[1]
            + (lower // 2) * ones[2] + (upper // 2) * ones[2]
        )

    def free_plane(x, carry):
        free_ref[x] = jnp.where(
            z == 0, 1.0 - fixed_ref[pl.ds(x, 1), :].astype(jnp.float32), 1.0
        )
        return carry

    each_plane(planes, free_plane, 0)

    own_index = index_ref[load_place]
    own_z = own_index // row_width % layers
    own_y = own_index % row_width
    hit = (z == own_z) & (y == own_y)
    for part in range(3):
        load_ref[part] = jnp.where(hit, force_ref[part, load_place], 0.0)
    own_x = (own_index // (layers * row_width)).astype(jnp.float32)
    spot_ref[...] = jnp.full(spot_ref.shape, own_x)


def sweep_kernel(
    spot_ref,
    load_ref,
    weight_ref,
    inverse_ref,
    free_ref,
    filter_ref,
    density_ref,
    start_ref,
    disp_ref,
    coef_ref,
    plane_ref,
    beside_ref,
    further_ref,
    near_ref,
    side_ref,
    far_ref,
    modulus_ref,
    across_ref,
    up_ref,
    right_ref,
    left_ref,
    rate_ref,
    first_ref,
):
    planes, layers, row_width = coef_ref.shape
    shape = (layers, row_width)
    z = spot_iota(shape, 0)
    y = spot_iota(shape, 1)
    zero = jnp.zeros(shape, jnp.float32)

    for ref in (side_ref, far_ref):
        zero_edges(ref)
    results = (near_ref, side_ref, far_ref)
    other_ref = density_ref.at[1]
    for x, spot in group_spots(0, other_ref):
        for place, ref in enumerate(results):
            ref[x + 2] = filter_ref[(place,) + spot]
    spread = (plane_ref, beside_ref, further_ref)
    spread_group(other_ref, spread)
    for p, (x, spot) in enumerate(group_spots(1, other_ref)):
        for ref, field in zip(results, filter_plane(p, layers, spread, weight_ref)):
            ref[x + 2] = field

    for ref in (first_ref, disp_ref):
        for part in range(3):
            ref[part, rows(0, layers)] = zero
            ref[part, rows(planes + 1, layers)] = zero

    def store_faces(slot, modulus, above, below, later, before, free, start, views):
        across, up_view, right_view, left_view, rate, source = views
        across[slot] = later
        up = jnp.where(z < layers - 1, 0.5 * (modulus + above), 0.0)
        right = jnp.where(
            y < row_width - 1, 0.5 * (modulus + pltpu.roll(modulus, row_width - 1, 1)), 0.0
        )
        left = jnp.where(y > 0, 0.5 * (modulus + pltpu.roll(modulus, 1, 1)), 0.0)
        down = jnp.where(z > 0, 0.5 * (modulus + below), 0.0)
        up_view[rows(slot, layers)] = up
        right_view[slot] = right
        left_view[slot] = left
        sums = (before + later, up + down, left + right)
        every = sums[0] + sums[1] + sums[2]
        diagonal = [every + part_sum for part_sum in sums]
        pair = diagonal[0] * diagonal[1]
        push = relax_factor * free / (pair * diagonal[2])
        side = push * diagonal[2]
        for part, factor in enumerate((side * diagonal[1], side * diagonal[0], push * pair)):
            rate[part, slot] = factor
            source[part, rows(slot, layers)] = start[part] * free

    piece = planes // 2

    def modulus_piece(first, carry):
        count = piece
        near = near_ref.at[pl.ds(first + 2, count)]
        side = side_ref.at[pl.ds(first + 1, count + 2)]
        far = far_ref.at[pl.ds(first, count + 4)]
        moduli = modulus_ref.at[pl.ds(first * layers, (count + 1) * layers)]
        coef = coef_ref.at[pl.ds(first, count)]
        free = free_ref.at[pl.ds(first, count)]
        views = (
            across_ref.at[pl.ds(first, count)],
            up_ref.at[pl.ds(first * layers, count * layers)],
            right_ref.at[pl.ds(first, count)],
            left_ref.at[pl.ds(first, count)],
            rate_ref.at[:, pl.ds(first, count)],
            first_ref.at[:, pl.ds(first * layers, count * layers)],
        )
        modulus, before = carry
        for p in range(count):
            inverse = inverse_ref[edge_class(first + p, planes)]
            filtered = near[p] + side[p] + side[p + 2] + far[p] + far[p + 4]
            filtered = filtered * inverse
            later = floor_modulus + (1.0 - floor_modulus) * (filtered * filtered * filtered)
            coef[p] = 3.0 * (1.0 - floor_modulus) * (filtered * filtered) * inverse
            moduli[rows(p + 1, layers)] = later
            ahead = 0.5 * (modulus + later)
            if p == 0:
                ahead = jnp.where(first > 0, ahead, 0.0)
            above = moduli[rows(p, layers, 1)] if p else pltpu.roll(modulus, layers - 1, 0)
            below = moduli[rows(p, layers, -1)] if p else pltpu.roll(modulus, 1, 0)
            previous = jnp.maximum(first + p - 1, 0)
            store_faces(
                p,
                modulus,
                above,
                below,
                ahead,
                before,
                free_ref[previous],
                [start_ref[part, previous] for part in range(3)],
                views,
            )
            modulus, before = later, ahead
        return modulus, before

    modulus, before = each_chunk(
        planes, piece, modulus_piece, (jnp.ones(shape, jnp.float32), zero)
    )
    store_faces(
        planes,
        modulus,
        pltpu.roll(modulus, layers - 1, 0),
        pltpu.roll(modulus, 1, 0),
        zero,
        before,
        free_ref[planes - 1],
        [start_ref[part, planes - 1] for part in range(3)],
        (across_ref, up_ref, right_ref, left_ref, rate_ref, first_ref),
    )

    own_x = jnp.max(spot_ref[...]).astype(jnp.int32)

    def sweep(source, target):
        def sweep_piece(first, carry):
            count = planes
            old = source.at[:, pl.ds(first * layers, (count + 2) * layers)]
            new = target.at[:, pl.ds((first + 1) * layers, count * layers)]
            across = across_ref.at[pl.ds(first, count + 1)]
            up = up_ref.at[pl.ds(first * layers, (count + 1) * layers)]
            right = right_ref.at[pl.ds(first + 1, count)]
            left = left_ref.at[pl.ds(first + 1, count)]
            rate = rate_ref.at[:, pl.ds(first + 1, count)]
            behind = [old[part, rows(0, layers)] for part in range(3)]
            here = [old[part, rows(1, layers)] for part in range(3)]
            for p in range(count):
                ahead = [old[part, rows(p + 2, layers)] for part in range(3)]
                for part in range(3):
                    pulls = [
                        across[p] * behind[part] + across[p + 1] * ahead[part],
                        up[rows(p + 1, layers)] * old[part, rows(p + 1, layers, 1)]
                        + up[rows(p + 1, layers, -1)] * old[part, rows(p + 1, layers, -1)],
                        right[p] * pltpu.roll(here[part], row_width - 1, 1)
                        + left[p] * pltpu.roll(here[part], 1, 1),
                    ]
                    pull = pulls[0] + pulls[1] + pulls[2] + pulls[part]
                    new[part, rows(p, layers)] = (
                        1.0 - relax_factor
                    ) * here[part] + rate[part, p] * pull
                behind, here = here, ahead
            return carry

        sweep_piece(0, 0)
        for part in range(3):
            target[part, rows(own_x + 1, layers)] += rate_ref[part, own_x + 1] * load_ref[part]

    def two_sweeps(turn, carry):
        sweep(first_ref, disp_ref)

        @pl.when(turn < SWEEPS // 2)
        def _():
            sweep(disp_ref, first_ref)

        return carry

    lax.fori_loop(0, SWEEPS // 2 + 1, two_sweeps, 0)


def filter_group(group, shares, weight_ref, near_ref, far_ref, result_ref):
    chips, own_planes, layers, row_width = result_ref.shape
    zero_gap = jnp.zeros((GAP, row_width), jnp.float32)
    mine = lax.axis_index("space")
    core = (mine ^ mine >> 1 ^ group) & 1
    count = shares[0].shape[0] - own_planes
    views = [
        [ref.at[pl.ds(own_planes * start, count)] for ref in shares] for start in (core, 1 - core)
    ]
    for ref in (near_ref, far_ref):
        ref[gap(0, layers)] = zero_gap
    for p in range(chips * own_planes):
        chip, own = p // own_planes, p % own_planes
        plane, beside, further = views[chip & 1]
        x = 2 * own_planes * chip + own + 2

        def around(ref, distance):
            return ref[x + distance] + ref[x - distance]

        sums = {
            0: plane[x],
            1: beside[x] + around(plane, 1),
            2: around(beside, 1),
            4: further[x] + around(plane, 2),
            5: around(further, 1) + around(beside, 2),
            8: around(further, 2),
        }
        level = weigh(sums, weight_ref, 0)
        for ref, square in ((near_ref, 1), (far_ref, 4)):
            ref[gapped(p, layers)] = weigh(sums, weight_ref, square)
            ref[gap(p + 1, layers)] = zero_gap
        result_ref[chip, own] = (
            level
            + near_ref[gapped(p, layers, 1)]
            + near_ref[gapped(p, layers, -1)]
            + far_ref[gapped(p, layers, 2)]
            + far_ref[gapped(p, layers, -2)]
        )


def share_kernel(
    disp_ref,
    coef_ref,
    weight_ref,
    sent_ref,
    plane_ref,
    beside_ref,
    further_ref,
    near_ref,
    far_ref,
):
    planes, layers, row_width = coef_ref.shape
    load_cases = lax.axis_size("space")
    shape = (layers, row_width)
    z = spot_iota(shape, 0)
    y = spot_iota(shape, 1)
    zero = jnp.zeros(shape, jnp.float32)
    shares = (plane_ref, beside_ref, further_ref)
    for ref in shares:
        zero_edges(ref)

    count = planes // 2

    def share_chunk(first, before):
        disp = disp_ref.at[:, pl.ds((first + 1) * layers, (count + 1) * layers)]
        coef = coef_ref.at[pl.ds(first, count)]
        plane = plane_ref.at[pl.ds(first + 2, count)]
        here = [disp[part, rows(0, layers)] for part in range(3)]
        for p in range(count):
            later = [disp[part, rows(p + 1, layers)] for part in range(3)]
            ahead, upward, right = zero, zero, zero
            for part in range(3):
                step = later[part] - here[part]
                climb = disp[part, rows(p, layers, 1)] - here[part]
                slide = pltpu.roll(here[part], row_width - 1, 1) - here[part]
                ahead = ahead + (2.0 if part == 0 else 1.0) * (step * step)
                upward = upward + (2.0 if part == 1 else 1.0) * (climb * climb)
                right = right + (2.0 if part == 2 else 1.0) * (slide * slide)
            if p == count - 1:
                ahead = jnp.where(first + count < planes, ahead, 0.0)
            upward = jnp.where(z < layers - 1, upward, 0.0)
            right = jnp.where(y < row_width - 1, right, 0.0)
            total = before + ahead + upward + pltpu.roll(upward, 1, 0)
            total = total + right + pltpu.roll(right, 1, 1)
            plane[p] = (0.5 / load_cases) * total * coef[p]
            before, here = ahead, later
        return before

    each_chunk(planes, count, share_chunk, zero)

    def spread_chunk(first, carry):
        plane, beside, further = (ref.at[pl.ds(first + 2, count)] for ref in shares)
        for p in range(count):
            share = plane[p]
            beside[p] = shift_sum(share, 1, 1)
            further[p] = shift_sum(share, 1, 2)
        return carry

    each_chunk(planes, count, spread_chunk, 0)
    filter_group(1, shares, weight_ref, near_ref, far_ref, sent_ref)


def kept_kernel(
    disp_ref,
    weight_ref,
    plane_ref,
    beside_ref,
    further_ref,
    disp_hbm,
    kept_ref,
    near_ref,
    far_ref,
    stored,
):
    layers = kept_ref.shape[2]
    inner = pl.ds(layers, disp_ref.shape[1] - 2 * layers)
    store = pltpu.make_async_copy(disp_ref.at[:, inner], disp_hbm, stored)
    store.start()
    shares = (plane_ref, beside_ref, further_ref)
    filter_group(0, shares, weight_ref, near_ref, far_ref, kept_ref)
    store.wait()


def design_kernel(root_ref, density_ref, new_ref, pull_ref, low_ref, high_ref):
    groups, chips, own_planes, layers, row_width = density_ref.shape
    tile_rows = pull_ref.shape[1]
    steps = layers // tile_rows
    shape = (tile_rows, row_width)
    zero = jnp.zeros(shape, jnp.float32)
    tiles = [
        (group, chip, own, pl.ds(step * tile_rows, tile_rows))
        for group in range(groups)
        for chip in range(chips)
        for own in range(own_planes)
        for step in range(steps)
    ]
    for place, spot in enumerate(tiles):
        density = density_ref[spot]
        pull_ref[place] = density * root_ref[spot]
        low_ref[place] = jnp.maximum(density - move_limit, density_floor)
        high_ref[place] = jnp.minimum(density + move_limit, 1.0)

    target = volume_share * len(tiles) * tile_rows * row_width

    def exceeds(total):
        volume = jnp.sum(jnp.sum(total, axis=0, keepdims=True), axis=1, keepdims=True)
        return jnp.broadcast_to(volume, shape) > target

    def middles_of(lower, span):
        half, quarter = span * 0.5, span * 0.25
        return lower + quarter, lower + half, lower + half + quarter

    def factors_of(lower, span):
        return [jnp.exp(-0.5 * middle) for middle in middles_of(lower, span)]

    def halve_twice(step, state):
        lower, span, *factors = state
        places = (lower,) + middles_of(lower, span)
        quarter = span * 0.25
        ahead = [factors_of(place, quarter) for place in places]
        totals = [[zero, zero] for _ in factors]
        for place in range(len(tiles)):
            pull, low, high = pull_ref[place], low_ref[place], high_ref[place]
            for total, factor in zip(totals, factors):
                trial = jnp.minimum(jnp.maximum(pull * factor, low), high)
                total[place % 2] = total[place % 2] + trial
        first, second, third = (exceeds(even + odd) for even, odd in totals)

        def pick(options):
            upper = jnp.where(third, options[3], options[2])
            return jnp.where(second, upper, jnp.where(first, options[1], options[0]))

        return (pick(places), quarter, *(pick(options) for options in zip(*ahead)))

    lower, span = jnp.full(shape, log_lower), jnp.full(shape, log_span)
    state = (lower, span, *factors_of(lower, span))
    lower, span, *_ = lax.fori_loop(0, SEARCH // 2, halve_twice, state)
    factor = jnp.exp(-0.5 * (lower + 0.5 * span))
    own_chip = lax.axis_index("space") >> 1
    for own in range(own_planes):
        for step in range(steps):
            place = (own_chip * own_planes + own) * steps + step
            new_ref[own, pl.ds(step * tile_rows, tile_rows)] = jnp.minimum(
                jnp.maximum(pull_ref[place] * factor, low_ref[place]), high_ref[place]
            )


def in_vmem():
    return pl.BlockSpec(memory_space=pltpu.VMEM)


KERNEL_VMEM = 24 * 2**20


def floats(*shape):
    return jax.ShapeDtypeStruct(shape, jnp.float32)


def prepare_call(density, radius, load_index, load_force, fixed):
    chips, own_planes, layers, row_width = density.shape
    planes = fixed.shape[0]
    spread = pltpu.VMEM((chips * own_planes * (layers + GAP) + GAP, row_width), jnp.float32)
    return pl.pallas_call(
        prepare_kernel,
        out_shape=[
            floats(len(ALL_SQUARES), layers, row_width),
            floats(2 * window_reach + 1, layers, row_width),
            floats(planes, layers, row_width),
            floats(3, layers, row_width),
            floats(8, row_width),
            floats(3, *density.shape),
        ],
        in_specs=[pl.BlockSpec(memory_space=pltpu.HBM)] * 4 + [in_vmem()],
        out_specs=[in_vmem()] * 6,
        scratch_shapes=[
            pltpu.SMEM(radius.shape, radius.dtype),
            pltpu.SMEM(load_index.shape, load_index.dtype),
            pltpu.SMEM(load_force.shape, load_force.dtype),
            pltpu.VMEM(fixed.shape, fixed.dtype),
            spread,
            spread,
            spread,
            pltpu.SemaphoreType.DMA((4,)),
        ],
        compiler_params=pltpu.CompilerParams(vmem_limit_bytes=KERNEL_VMEM),
        cost_estimate=pl.CostEstimate(
            flops=80 * planes * layers * row_width,
            bytes_accessed=8 * planes * layers * row_width,
            transcendentals=0,
        ),
        name="prepare",
    )(
        *(
            pltpu.with_memory_space_constraint(array, pltpu.HBM)
            for array in (radius, load_index, load_force, fixed)
        ),
        density,
    )


def sweep_call(spot, load, weights, inverses, free, filtered, density, displacement):
    groups, chips, own_planes, layers, row_width = density.shape
    planes = groups * chips * own_planes

    def scratch(*lead):
        return pltpu.VMEM(lead + (row_width,), jnp.float32)

    return pl.pallas_call(
        sweep_kernel,
        out_shape=[
            floats(3, (planes + 2) * layers, row_width),
            floats(planes, layers, row_width),
        ],
        in_specs=[in_vmem()] * 8,
        out_specs=[in_vmem()] * 2,
        scratch_shapes=[
            scratch(planes // 2 * (layers + GAP) + GAP),
            scratch(planes // 2 * (layers + GAP) + GAP),
            scratch(planes // 2 * (layers + GAP) + GAP),
            scratch(planes + 4, layers),
            scratch(planes + 4, layers),
            scratch(planes + 4, layers),
            scratch((planes + 1) * layers),
            scratch(planes + 1, layers),
            scratch((planes + 1) * layers),
            scratch(planes + 1, layers),
            scratch(planes + 1, layers),
            scratch(3, planes + 1, layers),
            scratch(3, (planes + 2) * layers),
        ],
        compiler_params=pltpu.CompilerParams(vmem_limit_bytes=KERNEL_VMEM),
        name="sweeps",
    )(spot, load, weights, inverses, free, filtered, density, displacement)


def share_call(disp, coef, weights, group_shape):
    planes, layers, row_width = coef.shape
    gaps = pltpu.VMEM((planes // 2 * (layers + GAP) + GAP, row_width), jnp.float32)
    return pl.pallas_call(
        share_kernel,
        out_shape=[floats(*group_shape)] + [floats(planes + 4, layers, row_width)] * 3,
        in_specs=[in_vmem()] * 3,
        out_specs=[in_vmem()] * 4,
        scratch_shapes=[gaps, gaps],
        compiler_params=pltpu.CompilerParams(vmem_limit_bytes=KERNEL_VMEM),
        name="share",
    )(disp, coef, weights)


def kept_call(disp, weights, shares, group_shape):
    parts, disp_rows, row_width = disp.shape
    chips, own_planes, layers = group_shape[:3]
    gaps = pltpu.VMEM((chips * own_planes * (layers + GAP) + GAP, row_width), jnp.float32)
    return pl.pallas_call(
        kept_kernel,
        out_shape=[floats(parts, disp_rows - 2 * layers, row_width), floats(*group_shape)],
        in_specs=[in_vmem()] * 5,
        out_specs=[pl.BlockSpec(memory_space=pltpu.HBM), in_vmem()],
        scratch_shapes=[gaps, gaps, pltpu.SemaphoreType.DMA(())],
        compiler_params=pltpu.CompilerParams(vmem_limit_bytes=KERNEL_VMEM),
        cost_estimate=pl.CostEstimate(
            flops=20 * disp.size, bytes_accessed=8 * disp.size, transcendentals=0
        ),
        name="kept",
    )(disp, weights, *shares)


def design_call(root, density):
    tile_rows = min(8, density.shape[-2])
    row_width = density.shape[-1]
    tiles = pltpu.VMEM((density.size // (tile_rows * row_width), tile_rows, row_width), jnp.float32)
    return pl.pallas_call(
        design_kernel,
        out_shape=floats(*density.shape[2:]),
        in_specs=[in_vmem()] * 2,
        out_specs=in_vmem(),
        scratch_shapes=[tiles] * 3,
        compiler_params=pltpu.CompilerParams(vmem_limit_bytes=KERNEL_VMEM),
        name="design",
    )(root, density)


def other_core(block):
    devices = lax.axis_size("space")
    return lax.ppermute(block, "space", [(i, i ^ 1) for i in range(devices)])


def chip_groups():
    chips = lax.axis_size("space") // 2
    return [[2 * chip + (chip ^ group) % 2 for chip in range(chips)] for group in range(2)]


def between_chips(pieces):
    return lax.all_to_all(pieces, "space", 0, 0, axis_index_groups=chip_groups())


def chip_gathered(block):
    chips = lax.axis_size("space") // 2
    return between_chips(jnp.broadcast_to(block[None], (chips,) + block.shape))


def with_other_core(blocks):
    return jnp.stack([blocks, other_core(blocks)])


def scattered_sum(sent, make_kept):
    received = other_core(sent)
    *others, kept = make_kept()
    return jnp.sum(between_chips(kept + received), axis=0), others


def one_slab(density, displacement, fixed, load_index, load_force, radius):
    same_group, small = lax.optimization_barrier(
        (chip_gathered(density), (radius, load_index, load_force.T, fixed))
    )
    other_group = other_core(same_group)
    weights, inverses, free, load, spot, filtered = prepare_call(same_group, *small)
    whole = jnp.stack([same_group, other_group])
    disp, coef = sweep_call(
        spot, load, weights, inverses, free, filtered, whole, displacement[0]
    )
    sent, *shares = share_call(disp, coef, weights, same_group.shape)
    sent, disp, shares = lax.optimization_barrier((sent, disp, shares))
    squares, (new_displacement,) = scattered_sum(
        sent, lambda: kept_call(disp, weights, shares, same_group.shape)
    )
    root = with_other_core(chip_gathered(jnp.sqrt(squares)))
    new_density = design_call(root, whole)
    return new_density, new_displacement.reshape(displacement.shape)


def from_behind(block, axis, distance):
    devices = range(lax.axis_size(axis))
    route = [(i - distance, i) for i in devices if i - distance in devices]
    return lax.ppermute(block, axis, route)


def extended(x, sides, width):
    for axis, dim in sides:
        size, length = (lax.axis_size(axis), x.shape[dim])
        up = [(i, (i + 1) % size) for i in range(size - 1)]
        down = [(j, i) for i, j in up]
        last = lax.slice_in_dim(x, length - width, length, axis=dim)
        first = lax.slice_in_dim(x, 0, width, axis=dim)
        before = lax.ppermute(last, axis, up)
        after = lax.ppermute(first, axis, down)
        x = jnp.concatenate([before, x, after], axis=dim)
    return x


def from_partner(x, axis, bit):
    return lax.ppermute(x, axis, [(i, i ^ 1 << bit) for i in range(lax.axis_size(axis))])


def window_offsets():
    offsets_list = []
    for across in range(-window_reach, window_reach + 1):
        for upward in range(-window_reach, window_reach + 1):
            for sideways in range(-window_reach, window_reach + 1):
                length = math.sqrt(across * across + upward * upward + sideways * sideways)
                offsets_list.append((across, upward, sideways, length))
    return offsets_list


def layer_weights(radius):
    radial = radius.astype(jnp.float32)
    return jnp.stack(
        [jnp.maximum(radial - length, 0.0) for across, upward, sideways, length in window_offsets()]
    )


def pad_axis(grid_field, along_axis, before, after_cells):
    widths = [(0, 0)] * grid_field.ndim
    widths[along_axis] = (before, after_cells)
    return jnp.pad(grid_field, widths)


def pad_sides(grid_field):
    return jnp.pad(grid_field, ((0, 0), (window_reach, window_reach), (window_reach, window_reach)))


def filter_forward(padded, weights):
    out_rows = padded.shape[0] - 2 * window_reach
    layers = padded.shape[1] - 2 * window_reach
    row_width = padded.shape[2] - 2 * window_reach
    result = jnp.zeros((out_rows, layers, row_width), jnp.float32)
    for offset_index, (across, upward, sideways, length) in enumerate(window_offsets()):
        shifted = padded[
            window_reach + across : window_reach + across + out_rows,
            window_reach + upward : window_reach + upward + layers,
            window_reach + sideways : window_reach + sideways + row_width,
        ]
        result = result + weights[offset_index][None, :, None] * shifted
    return result


def filter_backward(padded, padded_weights):
    out_rows = padded.shape[0] - 2 * window_reach
    layers = padded.shape[1] - 2 * window_reach
    row_width = padded.shape[2] - 2 * window_reach
    result = jnp.zeros((out_rows, layers, row_width), jnp.float32)
    for offset_index, (across, upward, sideways, length) in enumerate(window_offsets()):
        shifted = padded[
            window_reach - across : window_reach - across + out_rows,
            window_reach - upward : window_reach - upward + layers,
            window_reach - sideways : window_reach - sideways + row_width,
        ]
        layer_part = padded_weights[
            offset_index, window_reach - upward : window_reach - upward + layers
        ]
        result = result + layer_part[None, :, None] * shifted
    return result


def stiff_factors(direction):
    return jnp.array(
        [2.0 if component == direction else 1.0 for component in range(3)], jnp.float32
    ).reshape(3, 1, 1, 1)


def relax_slab(padded, displace, face_x, face_z, face_y, force_field, free_cells, diagonal):
    flux_x = stiff_factors(0) * face_x * jnp.diff(padded, axis=1)
    stencil_image = flux_x[:, :-1] - flux_x[:, 1:]
    flux_z = stiff_factors(1) * face_z * jnp.diff(displace, axis=2)
    stencil_image = stencil_image + pad_axis(flux_z, 2, 1, 0) - pad_axis(flux_z, 2, 0, 1)
    flux_y = stiff_factors(2) * face_y * jnp.diff(displace, axis=3)
    stencil_image = stencil_image + pad_axis(flux_y, 3, 1, 0) - pad_axis(flux_y, 3, 0, 1)
    return free_cells * (displace + relax_factor * (force_field - stencil_image) / diagonal)


def slab_energy(grid_field, along_axis, direction, load_cases):
    change = jnp.diff(grid_field, axis=along_axis)
    return jnp.sum(stiff_factors(direction) * change * change, axis=0) / load_cases


def neighbour_planes(displace, load_cases, axis_devices):
    if axis_devices > load_cases:
        below = from_behind(displace[:, -1:], "space", load_cases)
        above = from_behind(displace[:, :1], "space", -load_cases)
    else:
        below = jnp.zeros_like(displace[:, :1])
        above = jnp.zeros_like(displace[:, :1])
    return jnp.concatenate([below, displace, above], axis=1)


def many_slabs(density, displacement, fixed, load_index, load_force, radius):
    slab_rows, layers, row_width = density.shape
    load_cases = load_index.shape[0]
    level_count = load_cases.bit_length() - 1
    axis_devices = lax.axis_size("space")
    axis_place = lax.axis_index("space")
    slab_planes = slab_rows * load_cases
    slab_place = axis_place // load_cases
    load_place = axis_place % load_cases
    total_rows = slab_rows * axis_devices
    weights = layer_weights(radius)
    padded_weights = pad_axis(weights, 1, window_reach, window_reach)
    global_rows = (
        jnp.arange(slab_rows + 2 * window_reach, dtype=jnp.int32)
        + axis_place * slab_rows
        - window_reach
    )
    deep_inside = ((global_rows >= 0) & (global_rows < total_rows)).astype(jnp.float32)
    inside_field = deep_inside[:, None, None] * pad_sides(
        jnp.ones((slab_rows + 2 * window_reach, layers, row_width), jnp.float32)
    )
    total_weight = filter_forward(inside_field, weights)
    slab_start = slab_place * slab_planes
    margin_rows = jnp.arange(slab_planes + 2, dtype=jnp.int32) + slab_start - 1
    margin_inside = ((margin_rows >= 0) & (margin_rows < total_rows)).astype(jnp.float32)
    face_valid = margin_inside[1:] * margin_inside[:-1]
    fixed_slab = lax.dynamic_slice_in_dim(fixed, slab_start, slab_planes, 0).astype(jnp.float32)
    bottom_layer = (jnp.arange(layers, dtype=jnp.int32) == 0).astype(jnp.float32)
    free_cells = 1.0 - bottom_layer[None, :, None] * fixed_slab[:, None, :]
    slab_cells = slab_planes * layers * row_width
    cell_index = jnp.arange(slab_cells, dtype=jnp.int32) + slab_place * slab_cells
    load_hot = jnp.arange(load_cases, dtype=jnp.int32) == load_place
    own_index = jnp.sum(jnp.where(load_hot, load_index, 0))
    own_force = jnp.sum(load_hot.astype(jnp.float32)[:, None] * load_force, axis=0)
    load_hits = (cell_index == own_index).astype(jnp.float32)
    force_field = (own_force[:, None] * load_hits[None, :]).reshape(
        3, slab_planes, layers, row_width
    )
    displace = displacement[0] * free_cells
    target = volume_share * total_rows * layers * row_width
    padded = neighbour_planes(displace, load_cases, axis_devices)
    halo_density = extended(density, (("space", 0),), window_reach)
    filtered = filter_forward(pad_sides(halo_density), weights) / total_weight
    whole_field = lax.all_gather(filtered, "space", axis=0, tiled=True)
    margin = lax.dynamic_slice_in_dim(
        pad_axis(whole_field, 0, 1, 1), slab_start, slab_planes + 2, 0
    )
    moduli = floor_modulus + (1.0 - floor_modulus) * margin**3
    face_x = 0.5 * (moduli[1:] + moduli[:-1]) * face_valid[:, None, None]
    inner_moduli = moduli[1:-1]
    face_z = 0.5 * (inner_moduli[:, 1:] + inner_moduli[:, :-1])
    face_y = 0.5 * (inner_moduli[:, :, 1:] + inner_moduli[:, :, :-1])
    sum_x = face_x[:-1] + face_x[1:]
    sum_z = pad_axis(face_z, 1, 1, 0) + pad_axis(face_z, 1, 0, 1)
    sum_y = pad_axis(face_y, 2, 1, 0) + pad_axis(face_y, 2, 0, 1)
    diagonal = stiff_factors(0) * sum_x + stiff_factors(1) * sum_z + stiff_factors(2) * sum_y
    for sweep_index in range(SWEEPS):
        displace = relax_slab(
            padded, displace, face_x, face_z, face_y, force_field, free_cells, diagonal
        )
        padded = neighbour_planes(displace, load_cases, axis_devices)
    energy_x = slab_energy(padded, 1, 0, load_cases) * face_valid[:, None, None]
    energy_z = slab_energy(displace, 2, 1, load_cases)
    energy_y = slab_energy(displace, 3, 2, load_cases)
    sens_term = 0.5 * (
        energy_x[:-1]
        + energy_x[1:]
        + pad_axis(energy_z, 1, 1, 0)
        + pad_axis(energy_z, 1, 0, 1)
        + pad_axis(energy_y, 2, 1, 0)
        + pad_axis(energy_y, 2, 0, 1)
    )
    sensitive = sens_term
    for level in reversed(range(level_count)):
        half_rows = sensitive.shape[0] // 2
        upper_side = load_place // 2**level % 2 == 1
        outgoing = jnp.where(upper_side, sensitive[:half_rows], sensitive[half_rows:])
        keeping = jnp.where(upper_side, sensitive[half_rows:], sensitive[:half_rows])
        sensitive = keeping + from_partner(outgoing, "space", level)
    weighted_share = 3.0 * (1.0 - floor_modulus) * filtered**2 * sensitive / total_weight
    halo_share = extended(weighted_share, (("space", 0),), window_reach)
    root_term = jnp.sqrt(filter_backward(pad_sides(halo_share), padded_weights))
    lowest = jnp.maximum(density - move_limit, density_floor)
    highest = jnp.minimum(density + move_limit, 1.0)
    design_now = density

    def trial_design(log_level):
        return jnp.clip(design_now * root_term * jnp.exp(-0.5 * log_level), lowest, highest)

    start_state = (jnp.asarray(log_lower, jnp.float32), jnp.asarray(log_span, jnp.float32))

    def halve(search_step, search_state):
        lower_end, span_width = search_state
        half_span = span_width * 0.5
        middle = lower_end + half_span
        volume_total = lax.psum(jnp.sum(trial_design(middle)), "space")
        return (jnp.where(volume_total > target, middle, lower_end), half_span)

    lower_end, span_width = lax.fori_loop(0, SEARCH, halve, start_state)
    density = trial_design(lower_end + 0.5 * span_width)
    new_displacement = displace[None]
    return (density, new_displacement)


def solution(mesh):
    in_specs = (
        P("space", "parts", None),
        P("space", None, None, "parts", None),
        P(None, "parts"),
        P("parts"),
        P("parts", None),
        P("parts"),
    )
    out_specs = (P("space", "parts", None), P("space", None, None, "parts", None))

    def local(density, displacement, fixed, load_index, load_force, radius):
        alone = lax.axis_size("space") == load_index.shape[0]
        run = one_slab if alone else many_slabs
        return run(density, displacement, fixed, load_index, load_force, radius)

    return jax.shard_map(local, mesh=mesh, in_specs=in_specs, out_specs=out_specs, check_vma=False)
```

```python
import math

import jax
import jax.numpy as jnp
from jax import lax
from jax.experimental import pallas as pl
from jax.experimental.pallas import tpu as pltpu
from jax.sharding import PartitionSpec as P

SWEEPS = 3
SEARCH = 12


floor_modulus = 0.05
relax_factor = 0.6
move_limit = 0.2
density_floor = 0.01
volume_share = 0.5
log_lower = -16.0
log_span = 32.0
window_reach = 2

PLANE_SQUARES = (0, 1, 2, 4, 5, 8)
ALL_SQUARES = (0, 1, 2, 3, 4, 5, 6, 8, 9, 12)


def spot_iota(shape, dim):
    return lax.broadcasted_iota(jnp.int32, shape, dim)


def each_plane(planes, body, carry):
    for x in range(planes):
        carry = body(x, carry)
    return carry


def each_chunk(planes, count, body, carry):
    return lax.fori_loop(0, planes // count, lambda i, carry: body(i * count, carry), carry)


def layer_radius(radius_ref, layers, row_width):
    z = spot_iota((layers, row_width), 0)
    result = jnp.zeros((layers, row_width), jnp.int32)
    for layer in range(layers):
        result = jnp.where(z == layer, radius_ref[layer], result)
    return result.astype(jnp.float32)


def class_weights(radius_ref, weight_ref):
    layers, row_width = weight_ref.shape[1:]
    radial = layer_radius(radius_ref, layers, row_width)
    for place, square in enumerate(ALL_SQUARES):
        weight_ref[place] = jnp.maximum(radial - math.sqrt(square), 0.0)


def shift_sum(field, dim, distance):
    size = field.shape[dim]
    spot = spot_iota(field.shape, dim)
    ahead = jnp.where(spot < size - distance, pltpu.roll(field, size - distance, dim), 0.0)
    behind = jnp.where(spot >= distance, pltpu.roll(field, distance, dim), 0.0)
    return ahead + behind


def plane_sums(plane):
    beside = shift_sum(plane, 1, 1)
    further = shift_sum(plane, 1, 2)
    return {
        0: plane,
        1: beside + shift_sum(plane, 0, 1),
        2: shift_sum(beside, 0, 1),
        4: further + shift_sum(plane, 0, 2),
        5: shift_sum(further, 0, 1) + shift_sum(beside, 0, 2),
        8: shift_sum(further, 0, 2),
    }


def weigh(sums, weight_ref, square):
    result = None
    for inner in PLANE_SQUARES:
        term = weight_ref[ALL_SQUARES.index(inner + square)] * sums[inner]
        result = term if result is None else result + term
    return result


def forward_planes(plane, weight_ref):
    sums = plane_sums(plane)
    return [weigh(sums, weight_ref, square) for square in (0, 1, 4)]


def rows(x, layers, shift=0):
    return pl.ds(x * layers + shift, layers)


GAP = 8


def gapped(x, layers, shift=0):
    return pl.ds(GAP + x * (layers + GAP) + shift, layers)


def gap(x, layers):
    return pl.ds(x * (layers + GAP), GAP)


def edge_class(x, planes):
    return jnp.minimum(x, 2) + jnp.maximum(x - (planes - 3), 0)


def zero_edges(ref):
    planes = ref.shape[0]
    for place in (0, 1, planes - 2, planes - 1):
        ref[place] = jnp.zeros(ref.shape[1:], ref.dtype)


def group_spots(group, blocks):
    chips, own_planes = blocks.shape[:2]
    mine = lax.axis_index("space")
    core = mine ^ mine >> 1 ^ group
    return [
        (own_planes * (2 * chip + ((core ^ chip) & 1)) + own, (chip, own))
        for chip in range(chips)
        for own in range(own_planes)
    ]


def spread_group(blocks, spread):
    chips, own_planes, layers, row_width = blocks.shape
    zero_gap = jnp.zeros((GAP, row_width), jnp.float32)
    for ref in spread:
        ref[gap(0, layers)] = zero_gap
    for p in range(chips * own_planes):
        plane = blocks[p // own_planes, p % own_planes]
        for ref, field in zip(spread, (plane, shift_sum(plane, 1, 1), shift_sum(plane, 1, 2))):
            ref[gapped(p, layers)] = field
            ref[gap(p + 1, layers)] = zero_gap


def filter_plane(p, layers, spread, weight_ref):
    def around(place, distance):
        ref = spread[place]
        return ref[gapped(p, layers, distance)] + ref[gapped(p, layers, -distance)]

    sums = {
        0: spread[0][gapped(p, layers)],
        1: spread[1][gapped(p, layers)] + around(0, 1),
        2: around(1, 1),
        4: spread[2][gapped(p, layers)] + around(0, 2),
        5: around(2, 1) + around(1, 2),
        8: around(2, 2),
    }
    return [weigh(sums, weight_ref, square) for square in (0, 1, 4)]


def prepare_kernel(
    radius_hbm,
    index_hbm,
    force_hbm,
    fixed_hbm,
    density_ref,
    weight_ref,
    inverse_ref,
    free_ref,
    load_ref,
    spot_ref,
    filter_ref,
    radius_ref,
    index_ref,
    force_ref,
    fixed_ref,
    plane_ref,
    beside_ref,
    further_ref,
    arrived,
):
    copies = [
        pltpu.make_async_copy(source, target, arrived.at[place])
        for place, (source, target) in enumerate(
            (
                (radius_hbm, radius_ref),
                (index_hbm, index_ref),
                (force_hbm, force_ref),
                (fixed_hbm, fixed_ref),
            )
        )
    ]
    for copy in copies:
        copy.start()
    spread = (plane_ref, beside_ref, further_ref)
    spread_group(density_ref, spread)
    for copy in copies:
        copy.wait()
    planes, layers, row_width = free_ref.shape
    load_place = lax.axis_index("space")
    shape = (layers, row_width)
    z = spot_iota(shape, 0)
    y = spot_iota(shape, 1)

    class_weights(radius_ref, weight_ref)
    own_planes = density_ref.shape[1]
    for p in range(density_ref.shape[0] * own_planes):
        for place, field in enumerate(filter_plane(p, layers, spread, weight_ref)):
            filter_ref[place, p // own_planes, p % own_planes] = field

    ones = forward_planes(jnp.ones(shape, jnp.float32), weight_ref)
    for place, (lower, upper) in enumerate(((0, 2), (1, 2), (2, 2), (2, 1), (2, 0))):
        inverse_ref[place] = 1.0 / (
            ones[0] + min(lower, 1) * ones[1] + min(upper, 1) * ones[1]
            + (lower // 2) * ones[2] + (upper // 2) * ones[2]
        )

    def free_plane(x, carry):
        free_ref[x] = jnp.where(
            z == 0, 1.0 - fixed_ref[pl.ds(x, 1), :].astype(jnp.float32), 1.0
        )
        return carry

    each_plane(planes, free_plane, 0)

    own_index = index_ref[load_place]
    own_z = own_index // row_width % layers
    own_y = own_index % row_width
    hit = (z == own_z) & (y == own_y)
    for part in range(3):
        load_ref[part] = jnp.where(hit, force_ref[part, load_place], 0.0)
    own_x = (own_index // (layers * row_width)).astype(jnp.float32)
    spot_ref[...] = jnp.full(spot_ref.shape, own_x)


def sweep_kernel(
    spot_ref,
    load_ref,
    weight_ref,
    inverse_ref,
    free_ref,
    filter_ref,
    density_ref,
    start_ref,
    disp_ref,
    coef_ref,
    plane_ref,
    beside_ref,
    further_ref,
    near_ref,
    side_ref,
    far_ref,
    modulus_ref,
    across_ref,
    up_ref,
    right_ref,
    left_ref,
    rate_ref,
    first_ref,
):
    planes, layers, row_width = coef_ref.shape
    shape = (layers, row_width)
    z = spot_iota(shape, 0)
    y = spot_iota(shape, 1)
    zero = jnp.zeros(shape, jnp.float32)

    for ref in (side_ref, far_ref):
        zero_edges(ref)
    results = (near_ref, side_ref, far_ref)
    other_ref = density_ref.at[1]
    for x, spot in group_spots(0, other_ref):
        for place, ref in enumerate(results):
            ref[x + 2] = filter_ref[(place,) + spot]
    spread = (plane_ref, beside_ref, further_ref)
    spread_group(other_ref, spread)
    for p, (x, spot) in enumerate(group_spots(1, other_ref)):
        for ref, field in zip(results, filter_plane(p, layers, spread, weight_ref)):
            ref[x + 2] = field

    for ref in (first_ref, disp_ref):
        for part in range(3):
            ref[part, rows(0, layers)] = zero
            ref[part, rows(planes + 1, layers)] = zero

    def store_faces(slot, modulus, above, below, later, before, free, start, views):
        across, up_view, right_view, left_view, rate, source = views
        across[slot] = later
        up = jnp.where(z < layers - 1, 0.5 * (modulus + above), 0.0)
        right = jnp.where(
            y < row_width - 1, 0.5 * (modulus + pltpu.roll(modulus, row_width - 1, 1)), 0.0
        )
        left = jnp.where(y > 0, 0.5 * (modulus + pltpu.roll(modulus, 1, 1)), 0.0)
        down = jnp.where(z > 0, 0.5 * (modulus + below), 0.0)
        up_view[rows(slot, layers)] = up
        right_view[slot] = right
        left_view[slot] = left
        sums = (before + later, up + down, left + right)
        every = sums[0] + sums[1] + sums[2]
        diagonal = [every + part_sum for part_sum in sums]
        pair = diagonal[0] * diagonal[1]
        push = relax_factor * free / (pair * diagonal[2])
        side = push * diagonal[2]
        for part, factor in enumerate((side * diagonal[1], side * diagonal[0], push * pair)):
            rate[part, slot] = factor
            source[part, rows(slot, layers)] = start[part] * free

    piece = planes // 2

    def modulus_piece(first, carry):
        count = piece
        near = near_ref.at[pl.ds(first + 2, count)]
        side = side_ref.at[pl.ds(first + 1, count + 2)]
        far = far_ref.at[pl.ds(first, count + 4)]
        moduli = modulus_ref.at[pl.ds(first * layers, (count + 1) * layers)]
        coef = coef_ref.at[pl.ds(first, count)]
        free = free_ref.at[pl.ds(first, count)]
        views = (
            across_ref.at[pl.ds(first, count)],
            up_ref.at[pl.ds(first * layers, count * layers)],
            right_ref.at[pl.ds(first, count)],
            left_ref.at[pl.ds(first, count)],
            rate_ref.at[:, pl.ds(first, count)],
            first_ref.at[:, pl.ds(first * layers, count * layers)],
        )
        modulus, before = carry
        for p in range(count):
            inverse = inverse_ref[edge_class(first + p, planes)]
            filtered = near[p] + side[p] + side[p + 2] + far[p] + far[p + 4]
            filtered = filtered * inverse
            later = floor_modulus + (1.0 - floor_modulus) * (filtered * filtered * filtered)
            coef[p] = 3.0 * (1.0 - floor_modulus) * (filtered * filtered) * inverse
            moduli[rows(p + 1, layers)] = later
            ahead = 0.5 * (modulus + later)
            if p == 0:
                ahead = jnp.where(first > 0, ahead, 0.0)
            above = moduli[rows(p, layers, 1)] if p else pltpu.roll(modulus, layers - 1, 0)
            below = moduli[rows(p, layers, -1)] if p else pltpu.roll(modulus, 1, 0)
            previous = jnp.maximum(first + p - 1, 0)
            store_faces(
                p,
                modulus,
                above,
                below,
                ahead,
                before,
                free_ref[previous],
                [start_ref[part, previous] for part in range(3)],
                views,
            )
            modulus, before = later, ahead
        return modulus, before

    modulus, before = each_chunk(
        planes, piece, modulus_piece, (jnp.ones(shape, jnp.float32), zero)
    )
    store_faces(
        planes,
        modulus,
        pltpu.roll(modulus, layers - 1, 0),
        pltpu.roll(modulus, 1, 0),
        zero,
        before,
        free_ref[planes - 1],
        [start_ref[part, planes - 1] for part in range(3)],
        (across_ref, up_ref, right_ref, left_ref, rate_ref, first_ref),
    )

    own_x = jnp.max(spot_ref[...]).astype(jnp.int32)

    def sweep(source, target):
        def sweep_piece(first, carry):
            count = planes
            old = source.at[:, pl.ds(first * layers, (count + 2) * layers)]
            new = target.at[:, pl.ds((first + 1) * layers, count * layers)]
            across = across_ref.at[pl.ds(first, count + 1)]
            up = up_ref.at[pl.ds(first * layers, (count + 1) * layers)]
            right = right_ref.at[pl.ds(first + 1, count)]
            left = left_ref.at[pl.ds(first + 1, count)]
            rate = rate_ref.at[:, pl.ds(first + 1, count)]
            behind = [old[part, rows(0, layers)] for part in range(3)]
            here = [old[part, rows(1, layers)] for part in range(3)]
            for p in range(count):
                ahead = [old[part, rows(p + 2, layers)] for part in range(3)]
                for part in range(3):
                    pulls = [
                        across[p] * behind[part] + across[p + 1] * ahead[part],
                        up[rows(p + 1, layers)] * old[part, rows(p + 1, layers, 1)]
                        + up[rows(p + 1, layers, -1)] * old[part, rows(p + 1, layers, -1)],
                        right[p] * pltpu.roll(here[part], row_width - 1, 1)
                        + left[p] * pltpu.roll(here[part], 1, 1),
                    ]
                    pull = pulls[0] + pulls[1] + pulls[2] + pulls[part]
                    new[part, rows(p, layers)] = (
                        1.0 - relax_factor
                    ) * here[part] + rate[part, p] * pull
                behind, here = here, ahead
            return carry

        sweep_piece(0, 0)
        for part in range(3):
            target[part, rows(own_x + 1, layers)] += rate_ref[part, own_x + 1] * load_ref[part]

    def two_sweeps(turn, carry):
        sweep(first_ref, disp_ref)

        @pl.when(turn < SWEEPS // 2)
        def _():
            sweep(disp_ref, first_ref)

        return carry

    lax.fori_loop(0, SWEEPS // 2 + 1, two_sweeps, 0)


def filter_group(group, shares, weight_ref, near_ref, far_ref, result_ref):
    chips, own_planes, layers, row_width = result_ref.shape
    zero_gap = jnp.zeros((GAP, row_width), jnp.float32)
    mine = lax.axis_index("space")
    core = (mine ^ mine >> 1 ^ group) & 1
    count = shares[0].shape[0] - own_planes
    views = [
        [ref.at[pl.ds(own_planes * start, count)] for ref in shares] for start in (core, 1 - core)
    ]
    for ref in (near_ref, far_ref):
        ref[gap(0, layers)] = zero_gap
    for p in range(chips * own_planes):
        chip, own = p // own_planes, p % own_planes
        plane, beside, further = views[chip & 1]
        x = 2 * own_planes * chip + own + 2

        def around(ref, distance):
            return ref[x + distance] + ref[x - distance]

        sums = {
            0: plane[x],
            1: beside[x] + around(plane, 1),
            2: around(beside, 1),
            4: further[x] + around(plane, 2),
            5: around(further, 1) + around(beside, 2),
            8: around(further, 2),
        }
        level = weigh(sums, weight_ref, 0)
        for ref, square in ((near_ref, 1), (far_ref, 4)):
            ref[gapped(p, layers)] = weigh(sums, weight_ref, square)
            ref[gap(p + 1, layers)] = zero_gap
        result_ref[chip, own] = (
            level
            + near_ref[gapped(p, layers, 1)]
            + near_ref[gapped(p, layers, -1)]
            + far_ref[gapped(p, layers, 2)]
            + far_ref[gapped(p, layers, -2)]
        )


def share_kernel(
    disp_ref,
    coef_ref,
    weight_ref,
    sent_ref,
    plane_ref,
    beside_ref,
    further_ref,
    near_ref,
    far_ref,
):
    planes, layers, row_width = coef_ref.shape
    load_cases = lax.axis_size("space")
    shape = (layers, row_width)
    z = spot_iota(shape, 0)
    y = spot_iota(shape, 1)
    zero = jnp.zeros(shape, jnp.float32)
    shares = (plane_ref, beside_ref, further_ref)
    for ref in shares:
        zero_edges(ref)

    count = planes // 2

    def share_chunk(first, before):
        disp = disp_ref.at[:, pl.ds((first + 1) * layers, (count + 1) * layers)]
        coef = coef_ref.at[pl.ds(first, count)]
        plane = plane_ref.at[pl.ds(first + 2, count)]
        here = [disp[part, rows(0, layers)] for part in range(3)]
        for p in range(count):
            later = [disp[part, rows(p + 1, layers)] for part in range(3)]
            ahead, upward, right = zero, zero, zero
            for part in range(3):
                step = later[part] - here[part]
                climb = disp[part, rows(p, layers, 1)] - here[part]
                slide = pltpu.roll(here[part], row_width - 1, 1) - here[part]
                ahead = ahead + (2.0 if part == 0 else 1.0) * (step * step)
                upward = upward + (2.0 if part == 1 else 1.0) * (climb * climb)
                right = right + (2.0 if part == 2 else 1.0) * (slide * slide)
            if p == count - 1:
                ahead = jnp.where(first + count < planes, ahead, 0.0)
            upward = jnp.where(z < layers - 1, upward, 0.0)
            right = jnp.where(y < row_width - 1, right, 0.0)
            total = before + ahead + upward + pltpu.roll(upward, 1, 0)
            total = total + right + pltpu.roll(right, 1, 1)
            plane[p] = (0.5 / load_cases) * total * coef[p]
            before, here = ahead, later
        return before

    each_chunk(planes, count, share_chunk, zero)

    for x in range(planes):
        share = plane_ref[x + 2]
        beside_ref[x + 2] = shift_sum(share, 1, 1)
        further_ref[x + 2] = shift_sum(share, 1, 2)
    filter_group(1, shares, weight_ref, near_ref, far_ref, sent_ref)


def kept_kernel(
    disp_ref,
    weight_ref,
    plane_ref,
    beside_ref,
    further_ref,
    disp_hbm,
    kept_ref,
    near_ref,
    far_ref,
    stored,
):
    layers = kept_ref.shape[2]
    inner = pl.ds(layers, disp_ref.shape[1] - 2 * layers)
    store = pltpu.make_async_copy(disp_ref.at[:, inner], disp_hbm, stored)
    store.start()
    shares = (plane_ref, beside_ref, further_ref)
    filter_group(0, shares, weight_ref, near_ref, far_ref, kept_ref)
    store.wait()


def design_kernel(root_ref, density_ref, new_ref, pull_ref, low_ref, high_ref):
    groups, chips, own_planes, layers, row_width = density_ref.shape
    tile_rows = pull_ref.shape[1]
    steps = layers // tile_rows
    shape = (tile_rows, row_width)
    zero = jnp.zeros(shape, jnp.float32)
    tiles = [
        (group, chip, own, pl.ds(step * tile_rows, tile_rows))
        for group in range(groups)
        for chip in range(chips)
        for own in range(own_planes)
        for step in range(steps)
    ]
    for place, spot in enumerate(tiles):
        density = density_ref[spot]
        pull_ref[place] = density * root_ref[spot]
        low_ref[place] = jnp.maximum(density - move_limit, density_floor)
        high_ref[place] = jnp.minimum(density + move_limit, 1.0)

    target = volume_share * len(tiles) * tile_rows * row_width

    def exceeds(total):
        volume = jnp.sum(jnp.sum(total, axis=0, keepdims=True), axis=1, keepdims=True)
        return jnp.broadcast_to(volume, shape) > target

    def middles_of(lower, span):
        half, quarter = span * 0.5, span * 0.25
        return lower + quarter, lower + half, lower + half + quarter

    def factors_of(lower, span):
        return [jnp.exp(-0.5 * middle) for middle in middles_of(lower, span)]

    def halve_twice(step, state):
        lower, span, *factors = state
        places = (lower,) + middles_of(lower, span)
        quarter = span * 0.25
        ahead = [factors_of(place, quarter) for place in places]
        totals = [[zero, zero] for _ in factors]
        for place in range(len(tiles)):
            pull, low, high = pull_ref[place], low_ref[place], high_ref[place]
            for total, factor in zip(totals, factors):
                trial = jnp.minimum(jnp.maximum(pull * factor, low), high)
                total[place % 2] = total[place % 2] + trial
        first, second, third = (exceeds(even + odd) for even, odd in totals)

        def pick(options):
            upper = jnp.where(third, options[3], options[2])
            return jnp.where(second, upper, jnp.where(first, options[1], options[0]))

        return (pick(places), quarter, *(pick(options) for options in zip(*ahead)))

    lower, span = jnp.full(shape, log_lower), jnp.full(shape, log_span)
    state = (lower, span, *factors_of(lower, span))
    lower, span, *_ = lax.fori_loop(0, SEARCH // 2, halve_twice, state)
    factor = jnp.exp(-0.5 * (lower + 0.5 * span))
    own_chip = lax.axis_index("space") >> 1
    for own in range(own_planes):
        for step in range(steps):
            place = (own_chip * own_planes + own) * steps + step
            new_ref[own, pl.ds(step * tile_rows, tile_rows)] = jnp.minimum(
                jnp.maximum(pull_ref[place] * factor, low_ref[place]), high_ref[place]
            )


def in_vmem():
    return pl.BlockSpec(memory_space=pltpu.VMEM)


KERNEL_VMEM = 24 * 2**20


def floats(*shape):
    return jax.ShapeDtypeStruct(shape, jnp.float32)


def prepare_call(density, radius, load_index, load_force, fixed):
    chips, own_planes, layers, row_width = density.shape
    planes = fixed.shape[0]
    spread = pltpu.VMEM((chips * own_planes * (layers + GAP) + GAP, row_width), jnp.float32)
    return pl.pallas_call(
        prepare_kernel,
        out_shape=[
            floats(len(ALL_SQUARES), layers, row_width),
            floats(2 * window_reach + 1, layers, row_width),
            floats(planes, layers, row_width),
            floats(3, layers, row_width),
            floats(8, row_width),
            floats(3, *density.shape),
        ],
        in_specs=[pl.BlockSpec(memory_space=pltpu.HBM)] * 4 + [in_vmem()],
        out_specs=[in_vmem()] * 6,
        scratch_shapes=[
            pltpu.SMEM(radius.shape, radius.dtype),
            pltpu.SMEM(load_index.shape, load_index.dtype),
            pltpu.SMEM(load_force.shape, load_force.dtype),
            pltpu.VMEM(fixed.shape, fixed.dtype),
            spread,
            spread,
            spread,
            pltpu.SemaphoreType.DMA((4,)),
        ],
        compiler_params=pltpu.CompilerParams(vmem_limit_bytes=KERNEL_VMEM),
        cost_estimate=pl.CostEstimate(
            flops=80 * planes * layers * row_width,
            bytes_accessed=8 * planes * layers * row_width,
            transcendentals=0,
        ),
        name="prepare",
    )(
        *(
            pltpu.with_memory_space_constraint(array, pltpu.HBM)
            for array in (radius, load_index, load_force, fixed)
        ),
        density,
    )


def sweep_call(spot, load, weights, inverses, free, filtered, density, displacement):
    groups, chips, own_planes, layers, row_width = density.shape
    planes = groups * chips * own_planes

    def scratch(*lead):
        return pltpu.VMEM(lead + (row_width,), jnp.float32)

    return pl.pallas_call(
        sweep_kernel,
        out_shape=[
            floats(3, (planes + 2) * layers, row_width),
            floats(planes, layers, row_width),
        ],
        in_specs=[in_vmem()] * 8,
        out_specs=[in_vmem()] * 2,
        scratch_shapes=[
            scratch(planes // 2 * (layers + GAP) + GAP),
            scratch(planes // 2 * (layers + GAP) + GAP),
            scratch(planes // 2 * (layers + GAP) + GAP),
            scratch(planes + 4, layers),
            scratch(planes + 4, layers),
            scratch(planes + 4, layers),
            scratch((planes + 1) * layers),
            scratch(planes + 1, layers),
            scratch((planes + 1) * layers),
            scratch(planes + 1, layers),
            scratch(planes + 1, layers),
            scratch(3, planes + 1, layers),
            scratch(3, (planes + 2) * layers),
        ],
        compiler_params=pltpu.CompilerParams(vmem_limit_bytes=KERNEL_VMEM),
        name="sweeps",
    )(spot, load, weights, inverses, free, filtered, density, displacement)


def share_call(disp, coef, weights, group_shape):
    planes, layers, row_width = coef.shape
    gaps = pltpu.VMEM((planes // 2 * (layers + GAP) + GAP, row_width), jnp.float32)
    return pl.pallas_call(
        share_kernel,
        out_shape=[floats(*group_shape)] + [floats(planes + 4, layers, row_width)] * 3,
        in_specs=[in_vmem()] * 3,
        out_specs=[in_vmem()] * 4,
        scratch_shapes=[gaps, gaps],
        compiler_params=pltpu.CompilerParams(vmem_limit_bytes=KERNEL_VMEM),
        name="share",
    )(disp, coef, weights)


def kept_call(disp, weights, shares, group_shape):
    parts, disp_rows, row_width = disp.shape
    chips, own_planes, layers = group_shape[:3]
    gaps = pltpu.VMEM((chips * own_planes * (layers + GAP) + GAP, row_width), jnp.float32)
    return pl.pallas_call(
        kept_kernel,
        out_shape=[floats(parts, disp_rows - 2 * layers, row_width), floats(*group_shape)],
        in_specs=[in_vmem()] * 5,
        out_specs=[pl.BlockSpec(memory_space=pltpu.HBM), in_vmem()],
        scratch_shapes=[gaps, gaps, pltpu.SemaphoreType.DMA(())],
        compiler_params=pltpu.CompilerParams(vmem_limit_bytes=KERNEL_VMEM),
        cost_estimate=pl.CostEstimate(
            flops=20 * disp.size, bytes_accessed=8 * disp.size, transcendentals=0
        ),
        name="kept",
    )(disp, weights, *shares)


def design_call(root, density):
    tile_rows = min(8, density.shape[-2])
    row_width = density.shape[-1]
    tiles = pltpu.VMEM((density.size // (tile_rows * row_width), tile_rows, row_width), jnp.float32)
    return pl.pallas_call(
        design_kernel,
        out_shape=floats(*density.shape[2:]),
        in_specs=[in_vmem()] * 2,
        out_specs=in_vmem(),
        scratch_shapes=[tiles] * 3,
        compiler_params=pltpu.CompilerParams(vmem_limit_bytes=KERNEL_VMEM),
        name="design",
    )(root, density)


def other_core(block):
    devices = lax.axis_size("space")
    return lax.ppermute(block, "space", [(i, i ^ 1) for i in range(devices)])


def chip_groups():
    chips = lax.axis_size("space") // 2
    return [[2 * chip + (chip ^ group) % 2 for chip in range(chips)] for group in range(2)]


def between_chips(pieces):
    return lax.all_to_all(pieces, "space", 0, 0, axis_index_groups=chip_groups())


def chip_gathered(block):
    chips = lax.axis_size("space") // 2
    return between_chips(jnp.broadcast_to(block[None], (chips,) + block.shape))


def with_other_core(blocks):
    return jnp.stack([blocks, other_core(blocks)])


def scattered_sum(sent, make_kept):
    received = other_core(sent)
    *others, kept = make_kept()
    return jnp.sum(between_chips(kept + received), axis=0), others


def one_slab(density, displacement, fixed, load_index, load_force, radius):
    same_group, small = lax.optimization_barrier(
        (chip_gathered(density), (radius, load_index, load_force.T, fixed))
    )
    other_group = other_core(same_group)
    weights, inverses, free, load, spot, filtered = prepare_call(same_group, *small)
    whole = jnp.stack([same_group, other_group])
    disp, coef = sweep_call(
        spot, load, weights, inverses, free, filtered, whole, displacement[0]
    )
    sent, *shares = share_call(disp, coef, weights, same_group.shape)
    sent, disp, shares = lax.optimization_barrier((sent, disp, shares))
    squares, (new_displacement,) = scattered_sum(
        sent, lambda: kept_call(disp, weights, shares, same_group.shape)
    )
    root = with_other_core(chip_gathered(jnp.sqrt(squares)))
    new_density = design_call(root, whole)
    return new_density, new_displacement.reshape(displacement.shape)


def from_behind(block, axis, distance):
    devices = range(lax.axis_size(axis))
    route = [(i - distance, i) for i in devices if i - distance in devices]
    return lax.ppermute(block, axis, route)


def extended(x, sides, width):
    for axis, dim in sides:
        size, length = (lax.axis_size(axis), x.shape[dim])
        up = [(i, (i + 1) % size) for i in range(size - 1)]
        down = [(j, i) for i, j in up]
        last = lax.slice_in_dim(x, length - width, length, axis=dim)
        first = lax.slice_in_dim(x, 0, width, axis=dim)
        before = lax.ppermute(last, axis, up)
        after = lax.ppermute(first, axis, down)
        x = jnp.concatenate([before, x, after], axis=dim)
    return x


def from_partner(x, axis, bit):
    return lax.ppermute(x, axis, [(i, i ^ 1 << bit) for i in range(lax.axis_size(axis))])


def window_offsets():
    offsets_list = []
    for across in range(-window_reach, window_reach + 1):
        for upward in range(-window_reach, window_reach + 1):
            for sideways in range(-window_reach, window_reach + 1):
                length = math.sqrt(across * across + upward * upward + sideways * sideways)
                offsets_list.append((across, upward, sideways, length))
    return offsets_list


def layer_weights(radius):
    radial = radius.astype(jnp.float32)
    return jnp.stack(
        [jnp.maximum(radial - length, 0.0) for across, upward, sideways, length in window_offsets()]
    )


def pad_axis(grid_field, along_axis, before, after_cells):
    widths = [(0, 0)] * grid_field.ndim
    widths[along_axis] = (before, after_cells)
    return jnp.pad(grid_field, widths)


def pad_sides(grid_field):
    return jnp.pad(grid_field, ((0, 0), (window_reach, window_reach), (window_reach, window_reach)))


def filter_forward(padded, weights):
    out_rows = padded.shape[0] - 2 * window_reach
    layers = padded.shape[1] - 2 * window_reach
    row_width = padded.shape[2] - 2 * window_reach
    result = jnp.zeros((out_rows, layers, row_width), jnp.float32)
    for offset_index, (across, upward, sideways, length) in enumerate(window_offsets()):
        shifted = padded[
            window_reach + across : window_reach + across + out_rows,
            window_reach + upward : window_reach + upward + layers,
            window_reach + sideways : window_reach + sideways + row_width,
        ]
        result = result + weights[offset_index][None, :, None] * shifted
    return result


def filter_backward(padded, padded_weights):
    out_rows = padded.shape[0] - 2 * window_reach
    layers = padded.shape[1] - 2 * window_reach
    row_width = padded.shape[2] - 2 * window_reach
    result = jnp.zeros((out_rows, layers, row_width), jnp.float32)
    for offset_index, (across, upward, sideways, length) in enumerate(window_offsets()):
        shifted = padded[
            window_reach - across : window_reach - across + out_rows,
            window_reach - upward : window_reach - upward + layers,
            window_reach - sideways : window_reach - sideways + row_width,
        ]
        layer_part = padded_weights[
            offset_index, window_reach - upward : window_reach - upward + layers
        ]
        result = result + layer_part[None, :, None] * shifted
    return result


def stiff_factors(direction):
    return jnp.array(
        [2.0 if component == direction else 1.0 for component in range(3)], jnp.float32
    ).reshape(3, 1, 1, 1)


def relax_slab(padded, displace, face_x, face_z, face_y, force_field, free_cells, diagonal):
    flux_x = stiff_factors(0) * face_x * jnp.diff(padded, axis=1)
    stencil_image = flux_x[:, :-1] - flux_x[:, 1:]
    flux_z = stiff_factors(1) * face_z * jnp.diff(displace, axis=2)
    stencil_image = stencil_image + pad_axis(flux_z, 2, 1, 0) - pad_axis(flux_z, 2, 0, 1)
    flux_y = stiff_factors(2) * face_y * jnp.diff(displace, axis=3)
    stencil_image = stencil_image + pad_axis(flux_y, 3, 1, 0) - pad_axis(flux_y, 3, 0, 1)
    return free_cells * (displace + relax_factor * (force_field - stencil_image) / diagonal)


def slab_energy(grid_field, along_axis, direction, load_cases):
    change = jnp.diff(grid_field, axis=along_axis)
    return jnp.sum(stiff_factors(direction) * change * change, axis=0) / load_cases


def neighbour_planes(displace, load_cases, axis_devices):
    if axis_devices > load_cases:
        below = from_behind(displace[:, -1:], "space", load_cases)
        above = from_behind(displace[:, :1], "space", -load_cases)
    else:
        below = jnp.zeros_like(displace[:, :1])
        above = jnp.zeros_like(displace[:, :1])
    return jnp.concatenate([below, displace, above], axis=1)


def many_slabs(density, displacement, fixed, load_index, load_force, radius):
    slab_rows, layers, row_width = density.shape
    load_cases = load_index.shape[0]
    level_count = load_cases.bit_length() - 1
    axis_devices = lax.axis_size("space")
    axis_place = lax.axis_index("space")
    slab_planes = slab_rows * load_cases
    slab_place = axis_place // load_cases
    load_place = axis_place % load_cases
    total_rows = slab_rows * axis_devices
    weights = layer_weights(radius)
    padded_weights = pad_axis(weights, 1, window_reach, window_reach)
    global_rows = (
        jnp.arange(slab_rows + 2 * window_reach, dtype=jnp.int32)
        + axis_place * slab_rows
        - window_reach
    )
    deep_inside = ((global_rows >= 0) & (global_rows < total_rows)).astype(jnp.float32)
    inside_field = deep_inside[:, None, None] * pad_sides(
        jnp.ones((slab_rows + 2 * window_reach, layers, row_width), jnp.float32)
    )
    total_weight = filter_forward(inside_field, weights)
    slab_start = slab_place * slab_planes
    margin_rows = jnp.arange(slab_planes + 2, dtype=jnp.int32) + slab_start - 1
    margin_inside = ((margin_rows >= 0) & (margin_rows < total_rows)).astype(jnp.float32)
    face_valid = margin_inside[1:] * margin_inside[:-1]
    fixed_slab = lax.dynamic_slice_in_dim(fixed, slab_start, slab_planes, 0).astype(jnp.float32)
    bottom_layer = (jnp.arange(layers, dtype=jnp.int32) == 0).astype(jnp.float32)
    free_cells = 1.0 - bottom_layer[None, :, None] * fixed_slab[:, None, :]
    slab_cells = slab_planes * layers * row_width
    cell_index = jnp.arange(slab_cells, dtype=jnp.int32) + slab_place * slab_cells
    load_hot = jnp.arange(load_cases, dtype=jnp.int32) == load_place
    own_index = jnp.sum(jnp.where(load_hot, load_index, 0))
    own_force = jnp.sum(load_hot.astype(jnp.float32)[:, None] * load_force, axis=0)
    load_hits = (cell_index == own_index).astype(jnp.float32)
    force_field = (own_force[:, None] * load_hits[None, :]).reshape(
        3, slab_planes, layers, row_width
    )
    displace = displacement[0] * free_cells
    target = volume_share * total_rows * layers * row_width
    padded = neighbour_planes(displace, load_cases, axis_devices)
    halo_density = extended(density, (("space", 0),), window_reach)
    filtered = filter_forward(pad_sides(halo_density), weights) / total_weight
    whole_field = lax.all_gather(filtered, "space", axis=0, tiled=True)
    margin = lax.dynamic_slice_in_dim(
        pad_axis(whole_field, 0, 1, 1), slab_start, slab_planes + 2, 0
    )
    moduli = floor_modulus + (1.0 - floor_modulus) * margin**3
    face_x = 0.5 * (moduli[1:] + moduli[:-1]) * face_valid[:, None, None]
    inner_moduli = moduli[1:-1]
    face_z = 0.5 * (inner_moduli[:, 1:] + inner_moduli[:, :-1])
    face_y = 0.5 * (inner_moduli[:, :, 1:] + inner_moduli[:, :, :-1])
    sum_x = face_x[:-1] + face_x[1:]
    sum_z = pad_axis(face_z, 1, 1, 0) + pad_axis(face_z, 1, 0, 1)
    sum_y = pad_axis(face_y, 2, 1, 0) + pad_axis(face_y, 2, 0, 1)
    diagonal = stiff_factors(0) * sum_x + stiff_factors(1) * sum_z + stiff_factors(2) * sum_y
    for sweep_index in range(SWEEPS):
        displace = relax_slab(
            padded, displace, face_x, face_z, face_y, force_field, free_cells, diagonal
        )
        padded = neighbour_planes(displace, load_cases, axis_devices)
    energy_x = slab_energy(padded, 1, 0, load_cases) * face_valid[:, None, None]
    energy_z = slab_energy(displace, 2, 1, load_cases)
    energy_y = slab_energy(displace, 3, 2, load_cases)
    sens_term = 0.5 * (
        energy_x[:-1]
        + energy_x[1:]
        + pad_axis(energy_z, 1, 1, 0)
        + pad_axis(energy_z, 1, 0, 1)
        + pad_axis(energy_y, 2, 1, 0)
        + pad_axis(energy_y, 2, 0, 1)
    )
    sensitive = sens_term
    for level in reversed(range(level_count)):
        half_rows = sensitive.shape[0] // 2
        upper_side = load_place // 2**level % 2 == 1
        outgoing = jnp.where(upper_side, sensitive[:half_rows], sensitive[half_rows:])
        keeping = jnp.where(upper_side, sensitive[half_rows:], sensitive[:half_rows])
        sensitive = keeping + from_partner(outgoing, "space", level)
    weighted_share = 3.0 * (1.0 - floor_modulus) * filtered**2 * sensitive / total_weight
    halo_share = extended(weighted_share, (("space", 0),), window_reach)
    root_term = jnp.sqrt(filter_backward(pad_sides(halo_share), padded_weights))
    lowest = jnp.maximum(density - move_limit, density_floor)
    highest = jnp.minimum(density + move_limit, 1.0)
    design_now = density

    def trial_design(log_level):
        return jnp.clip(design_now * root_term * jnp.exp(-0.5 * log_level), lowest, highest)

    start_state = (jnp.asarray(log_lower, jnp.float32), jnp.asarray(log_span, jnp.float32))

    def halve(search_step, search_state):
        lower_end, span_width = search_state
        half_span = span_width * 0.5
        middle = lower_end + half_span
        volume_total = lax.psum(jnp.sum(trial_design(middle)), "space")
        return (jnp.where(volume_total > target, middle, lower_end), half_span)

    lower_end, span_width = lax.fori_loop(0, SEARCH, halve, start_state)
    density = trial_design(lower_end + 0.5 * span_width)
    new_displacement = displace[None]
    return (density, new_displacement)


def solution(mesh):
    in_specs = (
        P("space", "parts", None),
        P("space", None, None, "parts", None),
        P(None, "parts"),
        P("parts"),
        P("parts", None),
        P("parts"),
    )
    out_specs = (P("space", "parts", None), P("space", None, None, "parts", None))

    def local(density, displacement, fixed, load_index, load_force, radius):
        alone = lax.axis_size("space") == load_index.shape[0]
        run = one_slab if alone else many_slabs
        return run(density, displacement, fixed, load_index, load_force, radius)

    return jax.shard_map(local, mesh=mesh, in_specs=in_specs, out_specs=out_specs, check_vma=False)
```

```python
import math

import jax
import jax.numpy as jnp
from jax import lax
from jax.experimental import pallas as pl
from jax.experimental.pallas import tpu as pltpu
from jax.sharding import PartitionSpec as P

SWEEPS = 3
SEARCH = 12


floor_modulus = 0.05
relax_factor = 0.6
move_limit = 0.2
density_floor = 0.01
volume_share = 0.5
log_lower = -16.0
log_span = 32.0
window_reach = 2

PLANE_SQUARES = (0, 1, 2, 4, 5, 8)
ALL_SQUARES = (0, 1, 2, 3, 4, 5, 6, 8, 9, 12)


def spot_iota(shape, dim):
    return lax.broadcasted_iota(jnp.int32, shape, dim)


def each_plane(planes, body, carry):
    for x in range(planes):
        carry = body(x, carry)
    return carry


def each_chunk(planes, count, body, carry):
    return lax.fori_loop(0, planes // count, lambda i, carry: body(i * count, carry), carry)


def layer_radius(radius_ref, layers, row_width):
    z = spot_iota((layers, row_width), 0)
    result = jnp.zeros((layers, row_width), jnp.int32)
    for layer in range(layers):
        result = jnp.where(z == layer, radius_ref[layer], result)
    return result.astype(jnp.float32)


def class_weights(radius_ref, weight_ref):
    layers, row_width = weight_ref.shape[1:]
    radial = layer_radius(radius_ref, layers, row_width)
    for place, square in enumerate(ALL_SQUARES):
        weight_ref[place] = jnp.maximum(radial - math.sqrt(square), 0.0)


def shift_sum(field, dim, distance):
    size = field.shape[dim]
    spot = spot_iota(field.shape, dim)
    ahead = jnp.where(spot < size - distance, pltpu.roll(field, size - distance, dim), 0.0)
    behind = jnp.where(spot >= distance, pltpu.roll(field, distance, dim), 0.0)
    return ahead + behind


def plane_sums(plane):
    beside = shift_sum(plane, 1, 1)
    further = shift_sum(plane, 1, 2)
    return {
        0: plane,
        1: beside + shift_sum(plane, 0, 1),
        2: shift_sum(beside, 0, 1),
        4: further + shift_sum(plane, 0, 2),
        5: shift_sum(further, 0, 1) + shift_sum(beside, 0, 2),
        8: shift_sum(further, 0, 2),
    }


def weigh(sums, weight_ref, square):
    result = None
    for inner in PLANE_SQUARES:
        term = weight_ref[ALL_SQUARES.index(inner + square)] * sums[inner]
        result = term if result is None else result + term
    return result


def forward_planes(plane, weight_ref):
    sums = plane_sums(plane)
    return [weigh(sums, weight_ref, square) for square in (0, 1, 4)]


def rows(x, layers, shift=0):
    return pl.ds(x * layers + shift, layers)


GAP = 8


def gapped(x, layers, shift=0):
    return pl.ds(GAP + x * (layers + GAP) + shift, layers)


def gap(x, layers):
    return pl.ds(x * (layers + GAP), GAP)


def edge_class(x, planes):
    return min(x, 2) + max(x - (planes - 3), 0)


def zero_edges(ref):
    planes = ref.shape[0]
    for place in (0, 1, planes - 2, planes - 1):
        ref[place] = jnp.zeros(ref.shape[1:], ref.dtype)


def group_spots(group, blocks):
    chips, own_planes = blocks.shape[:2]
    mine = lax.axis_index("space")
    core = mine ^ mine >> 1 ^ group
    return [
        (own_planes * (2 * chip + ((core ^ chip) & 1)) + own, (chip, own))
        for chip in range(chips)
        for own in range(own_planes)
    ]


def spread_group(blocks, spread):
    chips, own_planes, layers, row_width = blocks.shape
    zero_gap = jnp.zeros((GAP, row_width), jnp.float32)
    for ref in spread:
        ref[gap(0, layers)] = zero_gap
    for p in range(chips * own_planes):
        plane = blocks[p // own_planes, p % own_planes]
        for ref, field in zip(spread, (plane, shift_sum(plane, 1, 1), shift_sum(plane, 1, 2))):
            ref[gapped(p, layers)] = field
            ref[gap(p + 1, layers)] = zero_gap


def filter_plane(p, layers, spread, weight_ref):
    def around(place, distance):
        ref = spread[place]
        return ref[gapped(p, layers, distance)] + ref[gapped(p, layers, -distance)]

    sums = {
        0: spread[0][gapped(p, layers)],
        1: spread[1][gapped(p, layers)] + around(0, 1),
        2: around(1, 1),
        4: spread[2][gapped(p, layers)] + around(0, 2),
        5: around(2, 1) + around(1, 2),
        8: around(2, 2),
    }
    return [weigh(sums, weight_ref, square) for square in (0, 1, 4)]


def prepare_kernel(
    radius_hbm,
    index_hbm,
    force_hbm,
    fixed_hbm,
    density_ref,
    weight_ref,
    inverse_ref,
    free_ref,
    load_ref,
    spot_ref,
    filter_ref,
    radius_ref,
    index_ref,
    force_ref,
    fixed_ref,
    plane_ref,
    beside_ref,
    further_ref,
    arrived,
):
    copies = [
        pltpu.make_async_copy(source, target, arrived.at[place])
        for place, (source, target) in enumerate(
            (
                (radius_hbm, radius_ref),
                (index_hbm, index_ref),
                (force_hbm, force_ref),
                (fixed_hbm, fixed_ref),
            )
        )
    ]
    for copy in copies:
        copy.start()
    spread = (plane_ref, beside_ref, further_ref)
    spread_group(density_ref, spread)
    for copy in copies:
        copy.wait()
    planes, layers, row_width = free_ref.shape
    load_place = lax.axis_index("space")
    shape = (layers, row_width)
    z = spot_iota(shape, 0)
    y = spot_iota(shape, 1)

    class_weights(radius_ref, weight_ref)
    own_planes = density_ref.shape[1]
    for p in range(density_ref.shape[0] * own_planes):
        for place, field in enumerate(filter_plane(p, layers, spread, weight_ref)):
            filter_ref[place, p // own_planes, p % own_planes] = field

    ones = forward_planes(jnp.ones(shape, jnp.float32), weight_ref)
    for place, (lower, upper) in enumerate(((0, 2), (1, 2), (2, 2), (2, 1), (2, 0))):
        inverse_ref[place] = 1.0 / (
            ones[0] + min(lower, 1) * ones[1] + min(upper, 1) * ones[1]
            + (lower // 2) * ones[2] + (upper // 2) * ones[2]
        )

    def free_plane(x, carry):
        free_ref[x] = jnp.where(
            z == 0, 1.0 - fixed_ref[pl.ds(x, 1), :].astype(jnp.float32), 1.0
        )
        return carry

    each_plane(planes, free_plane, 0)

    own_index = index_ref[load_place]
    own_z = own_index // row_width % layers
    own_y = own_index % row_width
    hit = (z == own_z) & (y == own_y)
    for part in range(3):
        load_ref[part] = jnp.where(hit, force_ref[part, load_place], 0.0)
    own_x = (own_index // (layers * row_width)).astype(jnp.float32)
    spot_ref[...] = jnp.full(spot_ref.shape, own_x)


def sweep_kernel(
    spot_ref,
    load_ref,
    weight_ref,
    inverse_ref,
    free_ref,
    filter_ref,
    density_ref,
    start_ref,
    disp_ref,
    coef_ref,
    plane_ref,
    beside_ref,
    further_ref,
    near_ref,
    side_ref,
    far_ref,
    modulus_ref,
    across_ref,
    up_ref,
    right_ref,
    left_ref,
    rate_ref,
    first_ref,
):
    planes, layers, row_width = coef_ref.shape
    shape = (layers, row_width)
    z = spot_iota(shape, 0)
    y = spot_iota(shape, 1)
    zero = jnp.zeros(shape, jnp.float32)

    for ref in (side_ref, far_ref):
        zero_edges(ref)
    results = (near_ref, side_ref, far_ref)
    other_ref = density_ref.at[1]
    for x, spot in group_spots(0, other_ref):
        for place, ref in enumerate(results):
            ref[x + 2] = filter_ref[(place,) + spot]
    spread = (plane_ref, beside_ref, further_ref)
    spread_group(other_ref, spread)
    for p, (x, spot) in enumerate(group_spots(1, other_ref)):
        for ref, field in zip(results, filter_plane(p, layers, spread, weight_ref)):
            ref[x + 2] = field

    for ref in (first_ref, disp_ref):
        for part in range(3):
            ref[part, rows(0, layers)] = zero
            ref[part, rows(planes + 1, layers)] = zero

    def store_faces(slot, modulus, above, below, later, before, free, start, views):
        across, up_view, right_view, left_view, rate, source = views
        across[slot] = later
        up = jnp.where(z < layers - 1, 0.5 * (modulus + above), 0.0)
        right = jnp.where(
            y < row_width - 1, 0.5 * (modulus + pltpu.roll(modulus, row_width - 1, 1)), 0.0
        )
        left = jnp.where(y > 0, 0.5 * (modulus + pltpu.roll(modulus, 1, 1)), 0.0)
        down = jnp.where(z > 0, 0.5 * (modulus + below), 0.0)
        up_view[rows(slot, layers)] = up
        right_view[slot] = right
        left_view[slot] = left
        sums = (before + later, up + down, left + right)
        every = sums[0] + sums[1] + sums[2]
        diagonal = [every + part_sum for part_sum in sums]
        pair = diagonal[0] * diagonal[1]
        push = relax_factor * free / (pair * diagonal[2])
        side = push * diagonal[2]
        for part, factor in enumerate((side * diagonal[1], side * diagonal[0], push * pair)):
            rate[part, slot] = factor
            source[part, rows(slot, layers)] = start[part] * free

    for x in range(planes):
        inverse = inverse_ref[edge_class(x, planes)]
        filtered = near_ref[x + 2] + side_ref[x + 1] + side_ref[x + 3] + far_ref[x] + far_ref[x + 4]
        filtered = filtered * inverse
        modulus_ref[rows(x + 1, layers)] = floor_modulus + (1.0 - floor_modulus) * (
            filtered * filtered * filtered
        )
        coef_ref[x] = 3.0 * (1.0 - floor_modulus) * (filtered * filtered) * inverse

    modulus_ref[rows(planes + 1, layers)] = zero
    across_ref[0] = zero
    up_ref[rows(0, layers)] = zero
    count = planes // 2

    def face_piece(first, before):
        moduli = modulus_ref.at[pl.ds(first * layers, (count + 2) * layers)]
        free = free_ref.at[pl.ds(first, count)]
        start = start_ref.at[:, pl.ds(first, count)]
        views = (
            across_ref.at[pl.ds(first + 1, count)],
            up_ref.at[pl.ds((first + 1) * layers, count * layers)],
            right_ref.at[pl.ds(first + 1, count)],
            left_ref.at[pl.ds(first + 1, count)],
            rate_ref.at[:, pl.ds(first + 1, count)],
            first_ref.at[:, pl.ds((first + 1) * layers, count * layers)],
        )
        for p in range(count):
            modulus = moduli[rows(p + 1, layers)]
            ahead = 0.5 * (modulus + moduli[rows(p + 2, layers)])
            if p == count - 1:
                ahead = jnp.where(first + count < planes, ahead, 0.0)
            store_faces(
                p,
                modulus,
                moduli[rows(p + 1, layers, 1)],
                moduli[rows(p + 1, layers, -1)],
                ahead,
                before,
                free[p],
                [start[part, p] for part in range(3)],
                views,
            )
            before = ahead
        return before

    each_chunk(planes, count, face_piece, zero)

    own_x = jnp.max(spot_ref[...]).astype(jnp.int32)

    def sweep(source, target):
        def sweep_piece(first, carry):
            count = planes
            old = source.at[:, pl.ds(first * layers, (count + 2) * layers)]
            new = target.at[:, pl.ds((first + 1) * layers, count * layers)]
            across = across_ref.at[pl.ds(first, count + 1)]
            up = up_ref.at[pl.ds(first * layers, (count + 1) * layers)]
            right = right_ref.at[pl.ds(first + 1, count)]
            left = left_ref.at[pl.ds(first + 1, count)]
            rate = rate_ref.at[:, pl.ds(first + 1, count)]
            behind = [old[part, rows(0, layers)] for part in range(3)]
            here = [old[part, rows(1, layers)] for part in range(3)]
            for p in range(count):
                ahead = [old[part, rows(p + 2, layers)] for part in range(3)]
                for part in range(3):
                    pulls = [
                        across[p] * behind[part] + across[p + 1] * ahead[part],
                        up[rows(p + 1, layers)] * old[part, rows(p + 1, layers, 1)]
                        + up[rows(p + 1, layers, -1)] * old[part, rows(p + 1, layers, -1)],
                        right[p] * pltpu.roll(here[part], row_width - 1, 1)
                        + left[p] * pltpu.roll(here[part], 1, 1),
                    ]
                    pull = pulls[0] + pulls[1] + pulls[2] + pulls[part]
                    new[part, rows(p, layers)] = (
                        1.0 - relax_factor
                    ) * here[part] + rate[part, p] * pull
                behind, here = here, ahead
            return carry

        sweep_piece(0, 0)
        for part in range(3):
            target[part, rows(own_x + 1, layers)] += rate_ref[part, own_x + 1] * load_ref[part]

    def two_sweeps(turn, carry):
        sweep(first_ref, disp_ref)

        @pl.when(turn < SWEEPS // 2)
        def _():
            sweep(disp_ref, first_ref)

        return carry

    lax.fori_loop(0, SWEEPS // 2 + 1, two_sweeps, 0)


def filter_group(group, shares, weight_ref, near_ref, far_ref, result_ref):
    chips, own_planes, layers, row_width = result_ref.shape
    zero_gap = jnp.zeros((GAP, row_width), jnp.float32)
    mine = lax.axis_index("space")
    core = (mine ^ mine >> 1 ^ group) & 1
    count = shares[0].shape[0] - own_planes
    views = [
        [ref.at[pl.ds(own_planes * start, count)] for ref in shares] for start in (core, 1 - core)
    ]
    for ref in (near_ref, far_ref):
        ref[gap(0, layers)] = zero_gap
    for p in range(chips * own_planes):
        chip, own = p // own_planes, p % own_planes
        plane, beside, further = views[chip & 1]
        x = 2 * own_planes * chip + own + 2

        def around(ref, distance):
            return ref[x + distance] + ref[x - distance]

        sums = {
            0: plane[x],
            1: beside[x] + around(plane, 1),
            2: around(beside, 1),
            4: further[x] + around(plane, 2),
            5: around(further, 1) + around(beside, 2),
            8: around(further, 2),
        }
        level = weigh(sums, weight_ref, 0)
        for ref, square in ((near_ref, 1), (far_ref, 4)):
            ref[gapped(p, layers)] = weigh(sums, weight_ref, square)
            ref[gap(p + 1, layers)] = zero_gap
        result_ref[chip, own] = (
            level
            + near_ref[gapped(p, layers, 1)]
            + near_ref[gapped(p, layers, -1)]
            + far_ref[gapped(p, layers, 2)]
            + far_ref[gapped(p, layers, -2)]
        )


def share_kernel(
    disp_ref,
    coef_ref,
    weight_ref,
    sent_ref,
    plane_ref,
    beside_ref,
    further_ref,
    near_ref,
    far_ref,
):
    planes, layers, row_width = coef_ref.shape
    load_cases = lax.axis_size("space")
    shape = (layers, row_width)
    z = spot_iota(shape, 0)
    y = spot_iota(shape, 1)
    zero = jnp.zeros(shape, jnp.float32)
    shares = (plane_ref, beside_ref, further_ref)
    for ref in shares:
        zero_edges(ref)

    count = planes // 2

    def share_chunk(first, before):
        disp = disp_ref.at[:, pl.ds((first + 1) * layers, (count + 1) * layers)]
        coef = coef_ref.at[pl.ds(first, count)]
        plane = plane_ref.at[pl.ds(first + 2, count)]
        here = [disp[part, rows(0, layers)] for part in range(3)]
        for p in range(count):
            later = [disp[part, rows(p + 1, layers)] for part in range(3)]
            ahead, upward, right = zero, zero, zero
            for part in range(3):
                step = later[part] - here[part]
                climb = disp[part, rows(p, layers, 1)] - here[part]
                slide = pltpu.roll(here[part], row_width - 1, 1) - here[part]
                ahead = ahead + (2.0 if part == 0 else 1.0) * (step * step)
                upward = upward + (2.0 if part == 1 else 1.0) * (climb * climb)
                right = right + (2.0 if part == 2 else 1.0) * (slide * slide)
            if p == count - 1:
                ahead = jnp.where(first + count < planes, ahead, 0.0)
            upward = jnp.where(z < layers - 1, upward, 0.0)
            right = jnp.where(y < row_width - 1, right, 0.0)
            total = before + ahead + upward + pltpu.roll(upward, 1, 0)
            total = total + right + pltpu.roll(right, 1, 1)
            plane[p] = (0.5 / load_cases) * total * coef[p]
            before, here = ahead, later
        return before

    each_chunk(planes, count, share_chunk, zero)

    for x in range(planes):
        share = plane_ref[x + 2]
        beside_ref[x + 2] = shift_sum(share, 1, 1)
        further_ref[x + 2] = shift_sum(share, 1, 2)
    filter_group(1, shares, weight_ref, near_ref, far_ref, sent_ref)


def kept_kernel(
    disp_ref,
    weight_ref,
    plane_ref,
    beside_ref,
    further_ref,
    disp_hbm,
    kept_ref,
    near_ref,
    far_ref,
    stored,
):
    layers = kept_ref.shape[2]
    inner = pl.ds(layers, disp_ref.shape[1] - 2 * layers)
    store = pltpu.make_async_copy(disp_ref.at[:, inner], disp_hbm, stored)
    store.start()
    shares = (plane_ref, beside_ref, further_ref)
    filter_group(0, shares, weight_ref, near_ref, far_ref, kept_ref)
    store.wait()


def design_kernel(root_ref, density_ref, new_ref, pull_ref, low_ref, high_ref):
    groups, chips, own_planes, layers, row_width = density_ref.shape
    tile_rows = pull_ref.shape[1]
    steps = layers // tile_rows
    shape = (tile_rows, row_width)
    zero = jnp.zeros(shape, jnp.float32)
    tiles = [
        (group, chip, own, pl.ds(step * tile_rows, tile_rows))
        for group in range(groups)
        for chip in range(chips)
        for own in range(own_planes)
        for step in range(steps)
    ]
    for place, spot in enumerate(tiles):
        density = density_ref[spot]
        pull_ref[place] = density * root_ref[spot]
        low_ref[place] = jnp.maximum(density - move_limit, density_floor)
        high_ref[place] = jnp.minimum(density + move_limit, 1.0)

    target = volume_share * len(tiles) * tile_rows * row_width

    def exceeds(total):
        volume = jnp.sum(jnp.sum(total, axis=0, keepdims=True), axis=1, keepdims=True)
        return jnp.broadcast_to(volume, shape) > target

    def middles_of(lower, span):
        half, quarter = span * 0.5, span * 0.25
        return lower + quarter, lower + half, lower + half + quarter

    def factors_of(lower, span):
        return [jnp.exp(-0.5 * middle) for middle in middles_of(lower, span)]

    def halve_twice(step, state):
        lower, span, *factors = state
        places = (lower,) + middles_of(lower, span)
        quarter = span * 0.25
        ahead = [factors_of(place, quarter) for place in places]
        totals = [[zero, zero] for _ in factors]
        for place in range(len(tiles)):
            pull, low, high = pull_ref[place], low_ref[place], high_ref[place]
            for total, factor in zip(totals, factors):
                trial = jnp.minimum(jnp.maximum(pull * factor, low), high)
                total[place % 2] = total[place % 2] + trial
        first, second, third = (exceeds(even + odd) for even, odd in totals)

        def pick(options):
            upper = jnp.where(third, options[3], options[2])
            return jnp.where(second, upper, jnp.where(first, options[1], options[0]))

        return (pick(places), quarter, *(pick(options) for options in zip(*ahead)))

    lower, span = jnp.full(shape, log_lower), jnp.full(shape, log_span)
    state = (lower, span, *factors_of(lower, span))
    lower, span, *_ = lax.fori_loop(0, SEARCH // 2, halve_twice, state)
    factor = jnp.exp(-0.5 * (lower + 0.5 * span))
    own_chip = lax.axis_index("space") >> 1
    for own in range(own_planes):
        for step in range(steps):
            place = (own_chip * own_planes + own) * steps + step
            new_ref[own, pl.ds(step * tile_rows, tile_rows)] = jnp.minimum(
                jnp.maximum(pull_ref[place] * factor, low_ref[place]), high_ref[place]
            )


def in_vmem():
    return pl.BlockSpec(memory_space=pltpu.VMEM)


KERNEL_VMEM = 24 * 2**20


def floats(*shape):
    return jax.ShapeDtypeStruct(shape, jnp.float32)


def prepare_call(density, radius, load_index, load_force, fixed):
    chips, own_planes, layers, row_width = density.shape
    planes = fixed.shape[0]
    spread = pltpu.VMEM((chips * own_planes * (layers + GAP) + GAP, row_width), jnp.float32)
    return pl.pallas_call(
        prepare_kernel,
        out_shape=[
            floats(len(ALL_SQUARES), layers, row_width),
            floats(2 * window_reach + 1, layers, row_width),
            floats(planes, layers, row_width),
            floats(3, layers, row_width),
            floats(8, row_width),
            floats(3, *density.shape),
        ],
        in_specs=[pl.BlockSpec(memory_space=pltpu.HBM)] * 4 + [in_vmem()],
        out_specs=[in_vmem()] * 6,
        scratch_shapes=[
            pltpu.SMEM(radius.shape, radius.dtype),
            pltpu.SMEM(load_index.shape, load_index.dtype),
            pltpu.SMEM(load_force.shape, load_force.dtype),
            pltpu.VMEM(fixed.shape, fixed.dtype),
            spread,
            spread,
            spread,
            pltpu.SemaphoreType.DMA((4,)),
        ],
        compiler_params=pltpu.CompilerParams(vmem_limit_bytes=KERNEL_VMEM),
        cost_estimate=pl.CostEstimate(
            flops=80 * planes * layers * row_width,
            bytes_accessed=8 * planes * layers * row_width,
            transcendentals=0,
        ),
        name="prepare",
    )(
        *(
            pltpu.with_memory_space_constraint(array, pltpu.HBM)
            for array in (radius, load_index, load_force, fixed)
        ),
        density,
    )


def sweep_call(spot, load, weights, inverses, free, filtered, density, displacement):
    groups, chips, own_planes, layers, row_width = density.shape
    planes = groups * chips * own_planes

    def scratch(*lead):
        return pltpu.VMEM(lead + (row_width,), jnp.float32)

    return pl.pallas_call(
        sweep_kernel,
        out_shape=[
            floats(3, (planes + 2) * layers, row_width),
            floats(planes, layers, row_width),
        ],
        in_specs=[in_vmem()] * 8,
        out_specs=[in_vmem()] * 2,
        scratch_shapes=[
            scratch(planes // 2 * (layers + GAP) + GAP),
            scratch(planes // 2 * (layers + GAP) + GAP),
            scratch(planes // 2 * (layers + GAP) + GAP),
            scratch(planes + 4, layers),
            scratch(planes + 4, layers),
            scratch(planes + 4, layers),
            scratch((planes + 2) * layers),
            scratch(planes + 1, layers),
            scratch((planes + 1) * layers),
            scratch(planes + 1, layers),
            scratch(planes + 1, layers),
            scratch(3, planes + 1, layers),
            scratch(3, (planes + 2) * layers),
        ],
        compiler_params=pltpu.CompilerParams(vmem_limit_bytes=KERNEL_VMEM),
        name="sweeps",
    )(spot, load, weights, inverses, free, filtered, density, displacement)


def share_call(disp, coef, weights, group_shape):
    planes, layers, row_width = coef.shape
    gaps = pltpu.VMEM((planes // 2 * (layers + GAP) + GAP, row_width), jnp.float32)
    return pl.pallas_call(
        share_kernel,
        out_shape=[floats(*group_shape)] + [floats(planes + 4, layers, row_width)] * 3,
        in_specs=[in_vmem()] * 3,
        out_specs=[in_vmem()] * 4,
        scratch_shapes=[gaps, gaps],
        compiler_params=pltpu.CompilerParams(vmem_limit_bytes=KERNEL_VMEM),
        name="share",
    )(disp, coef, weights)


def kept_call(disp, weights, shares, group_shape):
    parts, disp_rows, row_width = disp.shape
    chips, own_planes, layers = group_shape[:3]
    gaps = pltpu.VMEM((chips * own_planes * (layers + GAP) + GAP, row_width), jnp.float32)
    return pl.pallas_call(
        kept_kernel,
        out_shape=[floats(parts, disp_rows - 2 * layers, row_width), floats(*group_shape)],
        in_specs=[in_vmem()] * 5,
        out_specs=[pl.BlockSpec(memory_space=pltpu.HBM), in_vmem()],
        scratch_shapes=[gaps, gaps, pltpu.SemaphoreType.DMA(())],
        compiler_params=pltpu.CompilerParams(vmem_limit_bytes=KERNEL_VMEM),
        cost_estimate=pl.CostEstimate(
            flops=20 * disp.size, bytes_accessed=8 * disp.size, transcendentals=0
        ),
        name="kept",
    )(disp, weights, *shares)


def design_call(root, density):
    tile_rows = min(8, density.shape[-2])
    row_width = density.shape[-1]
    tiles = pltpu.VMEM((density.size // (tile_rows * row_width), tile_rows, row_width), jnp.float32)
    return pl.pallas_call(
        design_kernel,
        out_shape=floats(*density.shape[2:]),
        in_specs=[in_vmem()] * 2,
        out_specs=in_vmem(),
        scratch_shapes=[tiles] * 3,
        compiler_params=pltpu.CompilerParams(vmem_limit_bytes=KERNEL_VMEM),
        name="design",
    )(root, density)


def other_core(block):
    devices = lax.axis_size("space")
    return lax.ppermute(block, "space", [(i, i ^ 1) for i in range(devices)])


def chip_groups():
    chips = lax.axis_size("space") // 2
    return [[2 * chip + (chip ^ group) % 2 for chip in range(chips)] for group in range(2)]


def between_chips(pieces):
    return lax.all_to_all(pieces, "space", 0, 0, axis_index_groups=chip_groups())


def chip_gathered(block):
    chips = lax.axis_size("space") // 2
    return between_chips(jnp.broadcast_to(block[None], (chips,) + block.shape))


def with_other_core(blocks):
    return jnp.stack([blocks, other_core(blocks)])


def scattered_sum(sent, make_kept):
    received = other_core(sent)
    *others, kept = make_kept()
    return jnp.sum(between_chips(kept + received), axis=0), others


def one_slab(density, displacement, fixed, load_index, load_force, radius):
    same_group, small = lax.optimization_barrier(
        (chip_gathered(density), (radius, load_index, load_force.T, fixed))
    )
    other_group = other_core(same_group)
    weights, inverses, free, load, spot, filtered = prepare_call(same_group, *small)
    whole = jnp.stack([same_group, other_group])
    disp, coef = sweep_call(
        spot, load, weights, inverses, free, filtered, whole, displacement[0]
    )
    sent, *shares = share_call(disp, coef, weights, same_group.shape)
    sent, disp, shares = lax.optimization_barrier((sent, disp, shares))
    squares, (new_displacement,) = scattered_sum(
        sent, lambda: kept_call(disp, weights, shares, same_group.shape)
    )
    root = with_other_core(chip_gathered(jnp.sqrt(squares)))
    new_density = design_call(root, whole)
    return new_density, new_displacement.reshape(displacement.shape)


def from_behind(block, axis, distance):
    devices = range(lax.axis_size(axis))
    route = [(i - distance, i) for i in devices if i - distance in devices]
    return lax.ppermute(block, axis, route)


def extended(x, sides, width):
    for axis, dim in sides:
        size, length = (lax.axis_size(axis), x.shape[dim])
        up = [(i, (i + 1) % size) for i in range(size - 1)]
        down = [(j, i) for i, j in up]
        last = lax.slice_in_dim(x, length - width, length, axis=dim)
        first = lax.slice_in_dim(x, 0, width, axis=dim)
        before = lax.ppermute(last, axis, up)
        after = lax.ppermute(first, axis, down)
        x = jnp.concatenate([before, x, after], axis=dim)
    return x


def from_partner(x, axis, bit):
    return lax.ppermute(x, axis, [(i, i ^ 1 << bit) for i in range(lax.axis_size(axis))])


def window_offsets():
    offsets_list = []
    for across in range(-window_reach, window_reach + 1):
        for upward in range(-window_reach, window_reach + 1):
            for sideways in range(-window_reach, window_reach + 1):
                length = math.sqrt(across * across + upward * upward + sideways * sideways)
                offsets_list.append((across, upward, sideways, length))
    return offsets_list


def layer_weights(radius):
    radial = radius.astype(jnp.float32)
    return jnp.stack(
        [jnp.maximum(radial - length, 0.0) for across, upward, sideways, length in window_offsets()]
    )


def pad_axis(grid_field, along_axis, before, after_cells):
    widths = [(0, 0)] * grid_field.ndim
    widths[along_axis] = (before, after_cells)
    return jnp.pad(grid_field, widths)


def pad_sides(grid_field):
    return jnp.pad(grid_field, ((0, 0), (window_reach, window_reach), (window_reach, window_reach)))


def filter_forward(padded, weights):
    out_rows = padded.shape[0] - 2 * window_reach
    layers = padded.shape[1] - 2 * window_reach
    row_width = padded.shape[2] - 2 * window_reach
    result = jnp.zeros((out_rows, layers, row_width), jnp.float32)
    for offset_index, (across, upward, sideways, length) in enumerate(window_offsets()):
        shifted = padded[
            window_reach + across : window_reach + across + out_rows,
            window_reach + upward : window_reach + upward + layers,
            window_reach + sideways : window_reach + sideways + row_width,
        ]
        result = result + weights[offset_index][None, :, None] * shifted
    return result


def filter_backward(padded, padded_weights):
    out_rows = padded.shape[0] - 2 * window_reach
    layers = padded.shape[1] - 2 * window_reach
    row_width = padded.shape[2] - 2 * window_reach
    result = jnp.zeros((out_rows, layers, row_width), jnp.float32)
    for offset_index, (across, upward, sideways, length) in enumerate(window_offsets()):
        shifted = padded[
            window_reach - across : window_reach - across + out_rows,
            window_reach - upward : window_reach - upward + layers,
            window_reach - sideways : window_reach - sideways + row_width,
        ]
        layer_part = padded_weights[
            offset_index, window_reach - upward : window_reach - upward + layers
        ]
        result = result + layer_part[None, :, None] * shifted
    return result


def stiff_factors(direction):
    return jnp.array(
        [2.0 if component == direction else 1.0 for component in range(3)], jnp.float32
    ).reshape(3, 1, 1, 1)


def relax_slab(padded, displace, face_x, face_z, face_y, force_field, free_cells, diagonal):
    flux_x = stiff_factors(0) * face_x * jnp.diff(padded, axis=1)
    stencil_image = flux_x[:, :-1] - flux_x[:, 1:]
    flux_z = stiff_factors(1) * face_z * jnp.diff(displace, axis=2)
    stencil_image = stencil_image + pad_axis(flux_z, 2, 1, 0) - pad_axis(flux_z, 2, 0, 1)
    flux_y = stiff_factors(2) * face_y * jnp.diff(displace, axis=3)
    stencil_image = stencil_image + pad_axis(flux_y, 3, 1, 0) - pad_axis(flux_y, 3, 0, 1)
    return free_cells * (displace + relax_factor * (force_field - stencil_image) / diagonal)


def slab_energy(grid_field, along_axis, direction, load_cases):
    change = jnp.diff(grid_field, axis=along_axis)
    return jnp.sum(stiff_factors(direction) * change * change, axis=0) / load_cases


def neighbour_planes(displace, load_cases, axis_devices):
    if axis_devices > load_cases:
        below = from_behind(displace[:, -1:], "space", load_cases)
        above = from_behind(displace[:, :1], "space", -load_cases)
    else:
        below = jnp.zeros_like(displace[:, :1])
        above = jnp.zeros_like(displace[:, :1])
    return jnp.concatenate([below, displace, above], axis=1)


def many_slabs(density, displacement, fixed, load_index, load_force, radius):
    slab_rows, layers, row_width = density.shape
    load_cases = load_index.shape[0]
    level_count = load_cases.bit_length() - 1
    axis_devices = lax.axis_size("space")
    axis_place = lax.axis_index("space")
    slab_planes = slab_rows * load_cases
    slab_place = axis_place // load_cases
    load_place = axis_place % load_cases
    total_rows = slab_rows * axis_devices
    weights = layer_weights(radius)
    padded_weights = pad_axis(weights, 1, window_reach, window_reach)
    global_rows = (
        jnp.arange(slab_rows + 2 * window_reach, dtype=jnp.int32)
        + axis_place * slab_rows
        - window_reach
    )
    deep_inside = ((global_rows >= 0) & (global_rows < total_rows)).astype(jnp.float32)
    inside_field = deep_inside[:, None, None] * pad_sides(
        jnp.ones((slab_rows + 2 * window_reach, layers, row_width), jnp.float32)
    )
    total_weight = filter_forward(inside_field, weights)
    slab_start = slab_place * slab_planes
    margin_rows = jnp.arange(slab_planes + 2, dtype=jnp.int32) + slab_start - 1
    margin_inside = ((margin_rows >= 0) & (margin_rows < total_rows)).astype(jnp.float32)
    face_valid = margin_inside[1:] * margin_inside[:-1]
    fixed_slab = lax.dynamic_slice_in_dim(fixed, slab_start, slab_planes, 0).astype(jnp.float32)
    bottom_layer = (jnp.arange(layers, dtype=jnp.int32) == 0).astype(jnp.float32)
    free_cells = 1.0 - bottom_layer[None, :, None] * fixed_slab[:, None, :]
    slab_cells = slab_planes * layers * row_width
    cell_index = jnp.arange(slab_cells, dtype=jnp.int32) + slab_place * slab_cells
    load_hot = jnp.arange(load_cases, dtype=jnp.int32) == load_place
    own_index = jnp.sum(jnp.where(load_hot, load_index, 0))
    own_force = jnp.sum(load_hot.astype(jnp.float32)[:, None] * load_force, axis=0)
    load_hits = (cell_index == own_index).astype(jnp.float32)
    force_field = (own_force[:, None] * load_hits[None, :]).reshape(
        3, slab_planes, layers, row_width
    )
    displace = displacement[0] * free_cells
    target = volume_share * total_rows * layers * row_width
    padded = neighbour_planes(displace, load_cases, axis_devices)
    halo_density = extended(density, (("space", 0),), window_reach)
    filtered = filter_forward(pad_sides(halo_density), weights) / total_weight
    whole_field = lax.all_gather(filtered, "space", axis=0, tiled=True)
    margin = lax.dynamic_slice_in_dim(
        pad_axis(whole_field, 0, 1, 1), slab_start, slab_planes + 2, 0
    )
    moduli = floor_modulus + (1.0 - floor_modulus) * margin**3
    face_x = 0.5 * (moduli[1:] + moduli[:-1]) * face_valid[:, None, None]
    inner_moduli = moduli[1:-1]
    face_z = 0.5 * (inner_moduli[:, 1:] + inner_moduli[:, :-1])
    face_y = 0.5 * (inner_moduli[:, :, 1:] + inner_moduli[:, :, :-1])
    sum_x = face_x[:-1] + face_x[1:]
    sum_z = pad_axis(face_z, 1, 1, 0) + pad_axis(face_z, 1, 0, 1)
    sum_y = pad_axis(face_y, 2, 1, 0) + pad_axis(face_y, 2, 0, 1)
    diagonal = stiff_factors(0) * sum_x + stiff_factors(1) * sum_z + stiff_factors(2) * sum_y
    for sweep_index in range(SWEEPS):
        displace = relax_slab(
            padded, displace, face_x, face_z, face_y, force_field, free_cells, diagonal
        )
        padded = neighbour_planes(displace, load_cases, axis_devices)
    energy_x = slab_energy(padded, 1, 0, load_cases) * face_valid[:, None, None]
    energy_z = slab_energy(displace, 2, 1, load_cases)
    energy_y = slab_energy(displace, 3, 2, load_cases)
    sens_term = 0.5 * (
        energy_x[:-1]
        + energy_x[1:]
        + pad_axis(energy_z, 1, 1, 0)
        + pad_axis(energy_z, 1, 0, 1)
        + pad_axis(energy_y, 2, 1, 0)
        + pad_axis(energy_y, 2, 0, 1)
    )
    sensitive = sens_term
    for level in reversed(range(level_count)):
        half_rows = sensitive.shape[0] // 2
        upper_side = load_place // 2**level % 2 == 1
        outgoing = jnp.where(upper_side, sensitive[:half_rows], sensitive[half_rows:])
        keeping = jnp.where(upper_side, sensitive[half_rows:], sensitive[:half_rows])
        sensitive = keeping + from_partner(outgoing, "space", level)
    weighted_share = 3.0 * (1.0 - floor_modulus) * filtered**2 * sensitive / total_weight
    halo_share = extended(weighted_share, (("space", 0),), window_reach)
    root_term = jnp.sqrt(filter_backward(pad_sides(halo_share), padded_weights))
    lowest = jnp.maximum(density - move_limit, density_floor)
    highest = jnp.minimum(density + move_limit, 1.0)
    design_now = density

    def trial_design(log_level):
        return jnp.clip(design_now * root_term * jnp.exp(-0.5 * log_level), lowest, highest)

    start_state = (jnp.asarray(log_lower, jnp.float32), jnp.asarray(log_span, jnp.float32))

    def halve(search_step, search_state):
        lower_end, span_width = search_state
        half_span = span_width * 0.5
        middle = lower_end + half_span
        volume_total = lax.psum(jnp.sum(trial_design(middle)), "space")
        return (jnp.where(volume_total > target, middle, lower_end), half_span)

    lower_end, span_width = lax.fori_loop(0, SEARCH, halve, start_state)
    density = trial_design(lower_end + 0.5 * span_width)
    new_displacement = displace[None]
    return (density, new_displacement)


def solution(mesh):
    in_specs = (
        P("space", "parts", None),
        P("space", None, None, "parts", None),
        P(None, "parts"),
        P("parts"),
        P("parts", None),
        P("parts"),
    )
    out_specs = (P("space", "parts", None), P("space", None, None, "parts", None))

    def local(density, displacement, fixed, load_index, load_force, radius):
        alone = lax.axis_size("space") == load_index.shape[0]
        run = one_slab if alone else many_slabs
        return run(density, displacement, fixed, load_index, load_force, radius)

    return jax.shard_map(local, mesh=mesh, in_specs=in_specs, out_specs=out_specs, check_vma=False)
```

```python
import math

import jax
import jax.numpy as jnp
from jax import lax
from jax.experimental import pallas as pl
from jax.experimental.pallas import tpu as pltpu
from jax.sharding import PartitionSpec as P

SWEEPS = 3
SEARCH = 12


floor_modulus = 0.05
relax_factor = 0.6
move_limit = 0.2
density_floor = 0.01
volume_share = 0.5
log_lower = -16.0
log_span = 32.0
window_reach = 2

PLANE_SQUARES = (0, 1, 2, 4, 5, 8)
ALL_SQUARES = (0, 1, 2, 3, 4, 5, 6, 8, 9, 12)


def spot_iota(shape, dim):
    return lax.broadcasted_iota(jnp.int32, shape, dim)


def each_plane(planes, body, carry):
    for x in range(planes):
        carry = body(x, carry)
    return carry


def each_chunk(planes, count, body, carry):
    return lax.fori_loop(0, planes // count, lambda i, carry: body(i * count, carry), carry)


def layer_radius(radius_ref, layers, row_width):
    z = spot_iota((layers, row_width), 0)
    result = jnp.zeros((layers, row_width), jnp.int32)
    for layer in range(layers):
        result = jnp.where(z == layer, radius_ref[layer], result)
    return result.astype(jnp.float32)


def class_weights(radius_ref, weight_ref):
    layers, row_width = weight_ref.shape[1:]
    radial = layer_radius(radius_ref, layers, row_width)
    for place, square in enumerate(ALL_SQUARES):
        weight_ref[place] = jnp.maximum(radial - math.sqrt(square), 0.0)


def shift_sum(field, dim, distance):
    size = field.shape[dim]
    spot = spot_iota(field.shape, dim)
    ahead = jnp.where(spot < size - distance, pltpu.roll(field, size - distance, dim), 0.0)
    behind = jnp.where(spot >= distance, pltpu.roll(field, distance, dim), 0.0)
    return ahead + behind


def plane_sums(plane):
    beside = shift_sum(plane, 1, 1)
    further = shift_sum(plane, 1, 2)
    return {
        0: plane,
        1: beside + shift_sum(plane, 0, 1),
        2: shift_sum(beside, 0, 1),
        4: further + shift_sum(plane, 0, 2),
        5: shift_sum(further, 0, 1) + shift_sum(beside, 0, 2),
        8: shift_sum(further, 0, 2),
    }


def weigh(sums, weight_ref, square):
    result = None
    for inner in PLANE_SQUARES:
        term = weight_ref[ALL_SQUARES.index(inner + square)] * sums[inner]
        result = term if result is None else result + term
    return result


def forward_planes(plane, weight_ref):
    sums = plane_sums(plane)
    return [weigh(sums, weight_ref, square) for square in (0, 1, 4)]


def rows(x, layers, shift=0):
    return pl.ds(x * layers + shift, layers)


GAP = 8


def gapped(x, layers, shift=0):
    return pl.ds(GAP + x * (layers + GAP) + shift, layers)


def gap(x, layers):
    return pl.ds(x * (layers + GAP), GAP)


def edge_class(x, planes):
    return min(x, 2) + max(x - (planes - 3), 0)


def zero_edges(ref):
    planes = ref.shape[0]
    for place in (0, 1, planes - 2, planes - 1):
        ref[place] = jnp.zeros(ref.shape[1:], ref.dtype)


def group_spots(group, blocks):
    chips, own_planes = blocks.shape[:2]
    mine = lax.axis_index("space")
    core = mine ^ mine >> 1 ^ group
    return [
        (own_planes * (2 * chip + ((core ^ chip) & 1)) + own, (chip, own))
        for chip in range(chips)
        for own in range(own_planes)
    ]


def spread_group(blocks, spread):
    chips, own_planes, layers, row_width = blocks.shape
    zero_gap = jnp.zeros((GAP, row_width), jnp.float32)
    for ref in spread:
        ref[gap(0, layers)] = zero_gap
    for p in range(chips * own_planes):
        plane = blocks[p // own_planes, p % own_planes]
        for ref, field in zip(spread, (plane, shift_sum(plane, 1, 1), shift_sum(plane, 1, 2))):
            ref[gapped(p, layers)] = field
            ref[gap(p + 1, layers)] = zero_gap


def filter_plane(p, layers, spread, weight_ref):
    def around(place, distance):
        ref = spread[place]
        return ref[gapped(p, layers, distance)] + ref[gapped(p, layers, -distance)]

    sums = {
        0: spread[0][gapped(p, layers)],
        1: spread[1][gapped(p, layers)] + around(0, 1),
        2: around(1, 1),
        4: spread[2][gapped(p, layers)] + around(0, 2),
        5: around(2, 1) + around(1, 2),
        8: around(2, 2),
    }
    return [weigh(sums, weight_ref, square) for square in (0, 1, 4)]


def prepare_kernel(
    radius_hbm,
    index_hbm,
    force_hbm,
    fixed_hbm,
    density_ref,
    weight_ref,
    inverse_ref,
    free_ref,
    load_ref,
    spot_ref,
    filter_ref,
    radius_ref,
    index_ref,
    force_ref,
    fixed_ref,
    plane_ref,
    beside_ref,
    further_ref,
    arrived,
):
    copies = [
        pltpu.make_async_copy(source, target, arrived.at[place])
        for place, (source, target) in enumerate(
            (
                (radius_hbm, radius_ref),
                (index_hbm, index_ref),
                (force_hbm, force_ref),
                (fixed_hbm, fixed_ref),
            )
        )
    ]
    for copy in copies:
        copy.start()
    spread = (plane_ref, beside_ref, further_ref)
    spread_group(density_ref, spread)
    for copy in copies:
        copy.wait()
    planes, layers, row_width = free_ref.shape
    load_place = lax.axis_index("space")
    shape = (layers, row_width)
    z = spot_iota(shape, 0)
    y = spot_iota(shape, 1)

    class_weights(radius_ref, weight_ref)
    own_planes = density_ref.shape[1]
    for p in range(density_ref.shape[0] * own_planes):
        for place, field in enumerate(filter_plane(p, layers, spread, weight_ref)):
            filter_ref[place, p // own_planes, p % own_planes] = field

    ones = forward_planes(jnp.ones(shape, jnp.float32), weight_ref)
    for place, (lower, upper) in enumerate(((0, 2), (1, 2), (2, 2), (2, 1), (2, 0))):
        inverse_ref[place] = 1.0 / (
            ones[0] + min(lower, 1) * ones[1] + min(upper, 1) * ones[1]
            + (lower // 2) * ones[2] + (upper // 2) * ones[2]
        )

    def free_plane(x, carry):
        free_ref[x] = jnp.where(
            z == 0, 1.0 - fixed_ref[pl.ds(x, 1), :].astype(jnp.float32), 1.0
        )
        return carry

    each_plane(planes, free_plane, 0)

    own_index = index_ref[load_place]
    own_z = own_index // row_width % layers
    own_y = own_index % row_width
    hit = (z == own_z) & (y == own_y)
    for part in range(3):
        load_ref[part] = jnp.where(hit, force_ref[part, load_place], 0.0)
    own_x = (own_index // (layers * row_width)).astype(jnp.float32)
    spot_ref[...] = jnp.full(spot_ref.shape, own_x)


def sweep_kernel(
    spot_ref,
    load_ref,
    weight_ref,
    inverse_ref,
    free_ref,
    filter_ref,
    density_ref,
    start_ref,
    disp_ref,
    coef_ref,
    plane_ref,
    beside_ref,
    further_ref,
    near_ref,
    side_ref,
    far_ref,
    modulus_ref,
    across_ref,
    up_ref,
    right_ref,
    left_ref,
    rate_ref,
    first_ref,
):
    planes, layers, row_width = coef_ref.shape
    shape = (layers, row_width)
    z = spot_iota(shape, 0)
    y = spot_iota(shape, 1)
    zero = jnp.zeros(shape, jnp.float32)

    for ref in (side_ref, far_ref):
        zero_edges(ref)
    results = (near_ref, side_ref, far_ref)
    other_ref = density_ref.at[1]
    for x, spot in group_spots(0, other_ref):
        for place, ref in enumerate(results):
            ref[x + 2] = filter_ref[(place,) + spot]
    spread = (plane_ref, beside_ref, further_ref)
    spread_group(other_ref, spread)
    for p, (x, spot) in enumerate(group_spots(1, other_ref)):
        for ref, field in zip(results, filter_plane(p, layers, spread, weight_ref)):
            ref[x + 2] = field

    for ref in (first_ref, disp_ref):
        for part in range(3):
            ref[part, rows(0, layers)] = zero
            ref[part, rows(planes + 1, layers)] = zero

    def store_faces(slot, modulus, above, below, later, before, free, start, views):
        across, up_view, right_view, left_view, rate, source = views
        across[slot] = later
        up = jnp.where(z < layers - 1, 0.5 * (modulus + above), 0.0)
        right = jnp.where(
            y < row_width - 1, 0.5 * (modulus + pltpu.roll(modulus, row_width - 1, 1)), 0.0
        )
        left = jnp.where(y > 0, 0.5 * (modulus + pltpu.roll(modulus, 1, 1)), 0.0)
        down = jnp.where(z > 0, 0.5 * (modulus + below), 0.0)
        up_view[rows(slot, layers)] = up
        right_view[slot] = right
        left_view[slot] = left
        sums = (before + later, up + down, left + right)
        every = sums[0] + sums[1] + sums[2]
        diagonal = [every + part_sum for part_sum in sums]
        pair = diagonal[0] * diagonal[1]
        push = relax_factor * free / (pair * diagonal[2])
        side = push * diagonal[2]
        for part, factor in enumerate((side * diagonal[1], side * diagonal[0], push * pair)):
            rate[part, slot] = factor
            source[part, rows(slot, layers)] = start[part] * free

    for x in range(planes):
        inverse = inverse_ref[edge_class(x, planes)]
        filtered = near_ref[x + 2] + side_ref[x + 1] + side_ref[x + 3] + far_ref[x] + far_ref[x + 4]
        filtered = filtered * inverse
        modulus_ref[rows(x + 1, layers)] = floor_modulus + (1.0 - floor_modulus) * (
            filtered * filtered * filtered
        )
        coef_ref[x] = 3.0 * (1.0 - floor_modulus) * (filtered * filtered) * inverse

    modulus_ref[rows(planes + 1, layers)] = zero
    across_ref[0] = zero
    up_ref[rows(0, layers)] = zero
    count = planes // 2

    def face_piece(first, before):
        moduli = modulus_ref.at[pl.ds(first * layers, (count + 2) * layers)]
        free = free_ref.at[pl.ds(first, count)]
        start = start_ref.at[:, pl.ds(first, count)]
        views = (
            across_ref.at[pl.ds(first + 1, count)],
            up_ref.at[pl.ds((first + 1) * layers, count * layers)],
            right_ref.at[pl.ds(first + 1, count)],
            left_ref.at[pl.ds(first + 1, count)],
            rate_ref.at[:, pl.ds(first + 1, count)],
            first_ref.at[:, pl.ds((first + 1) * layers, count * layers)],
        )
        for p in range(count):
            modulus = moduli[rows(p + 1, layers)]
            ahead = 0.5 * (modulus + moduli[rows(p + 2, layers)])
            if p == count - 1:
                ahead = jnp.where(first + count < planes, ahead, 0.0)
            store_faces(
                p,
                modulus,
                moduli[rows(p + 1, layers, 1)],
                moduli[rows(p + 1, layers, -1)],
                ahead,
                before,
                free[p],
                [start[part, p] for part in range(3)],
                views,
            )
            before = ahead
        return before

    each_chunk(planes, count, face_piece, zero)

    own_x = jnp.max(spot_ref[...]).astype(jnp.int32)

    def sweep(source, target):
        def sweep_piece(first, carry):
            count = planes
            old = source.at[:, pl.ds(first * layers, (count + 2) * layers)]
            new = target.at[:, pl.ds((first + 1) * layers, count * layers)]
            across = across_ref.at[pl.ds(first, count + 1)]
            up = up_ref.at[pl.ds(first * layers, (count + 1) * layers)]
            right = right_ref.at[pl.ds(first + 1, count)]
            left = left_ref.at[pl.ds(first + 1, count)]
            rate = rate_ref.at[:, pl.ds(first + 1, count)]
            behind = [old[part, rows(0, layers)] for part in range(3)]
            here = [old[part, rows(1, layers)] for part in range(3)]
            for p in range(count):
                ahead = [old[part, rows(p + 2, layers)] for part in range(3)]
                for part in range(3):
                    pulls = [
                        across[p] * behind[part] + across[p + 1] * ahead[part],
                        up[rows(p + 1, layers)] * old[part, rows(p + 1, layers, 1)]
                        + up[rows(p + 1, layers, -1)] * old[part, rows(p + 1, layers, -1)],
                        right[p] * pltpu.roll(here[part], row_width - 1, 1)
                        + left[p] * pltpu.roll(here[part], 1, 1),
                    ]
                    pull = pulls[0] + pulls[1] + pulls[2] + pulls[part]
                    new[part, rows(p, layers)] = (
                        1.0 - relax_factor
                    ) * here[part] + rate[part, p] * pull
                behind, here = here, ahead
            return carry

        sweep_piece(0, 0)
        for part in range(3):
            target[part, rows(own_x + 1, layers)] += rate_ref[part, own_x + 1] * load_ref[part]

    def two_sweeps(turn, carry):
        sweep(first_ref, disp_ref)

        @pl.when(turn < SWEEPS // 2)
        def _():
            sweep(disp_ref, first_ref)

        return carry

    lax.fori_loop(0, SWEEPS // 2 + 1, two_sweeps, 0)


def filter_group(group, shares, weight_ref, near_ref, far_ref, result_ref):
    chips, own_planes, layers, row_width = result_ref.shape
    zero_gap = jnp.zeros((GAP, row_width), jnp.float32)
    mine = lax.axis_index("space")
    core = (mine ^ mine >> 1 ^ group) & 1
    count = shares[0].shape[0] - own_planes
    views = [
        [ref.at[pl.ds(own_planes * start, count)] for ref in shares] for start in (core, 1 - core)
    ]
    for ref in (near_ref, far_ref):
        ref[gap(0, layers)] = zero_gap
    for p in range(chips * own_planes):
        chip, own = p // own_planes, p % own_planes
        plane, beside, further = views[chip & 1]
        x = 2 * own_planes * chip + own + 2

        def around(ref, distance):
            return ref[x + distance] + ref[x - distance]

        sums = {
            0: plane[x],
            1: beside[x] + around(plane, 1),
            2: around(beside, 1),
            4: further[x] + around(plane, 2),
            5: around(further, 1) + around(beside, 2),
            8: around(further, 2),
        }
        level = weigh(sums, weight_ref, 0)
        for ref, square in ((near_ref, 1), (far_ref, 4)):
            ref[gapped(p, layers)] = weigh(sums, weight_ref, square)
            ref[gap(p + 1, layers)] = zero_gap
        result_ref[chip, own] = (
            level
            + near_ref[gapped(p, layers, 1)]
            + near_ref[gapped(p, layers, -1)]
            + far_ref[gapped(p, layers, 2)]
            + far_ref[gapped(p, layers, -2)]
        )


def share_kernel(
    disp_ref,
    coef_ref,
    weight_ref,
    sent_ref,
    plane_ref,
    beside_ref,
    further_ref,
    near_ref,
    far_ref,
):
    planes, layers, row_width = coef_ref.shape
    load_cases = lax.axis_size("space")
    shape = (layers, row_width)
    z = spot_iota(shape, 0)
    y = spot_iota(shape, 1)
    zero = jnp.zeros(shape, jnp.float32)
    shares = (plane_ref, beside_ref, further_ref)
    for ref in shares:
        zero_edges(ref)

    count = planes // 2

    def share_chunk(first, before):
        disp = disp_ref.at[:, pl.ds((first + 1) * layers, (count + 1) * layers)]
        coef = coef_ref.at[pl.ds(first, count)]
        plane = plane_ref.at[pl.ds(first + 2, count)]
        here = [disp[part, rows(0, layers)] for part in range(3)]
        for p in range(count):
            later = [disp[part, rows(p + 1, layers)] for part in range(3)]
            ahead, upward, right = zero, zero, zero
            for part in range(3):
                step = later[part] - here[part]
                climb = disp[part, rows(p, layers, 1)] - here[part]
                slide = pltpu.roll(here[part], row_width - 1, 1) - here[part]
                ahead = ahead + (2.0 if part == 0 else 1.0) * (step * step)
                upward = upward + (2.0 if part == 1 else 1.0) * (climb * climb)
                right = right + (2.0 if part == 2 else 1.0) * (slide * slide)
            if p == count - 1:
                ahead = jnp.where(first + count < planes, ahead, 0.0)
            upward = jnp.where(z < layers - 1, upward, 0.0)
            right = jnp.where(y < row_width - 1, right, 0.0)
            total = before + ahead + upward + pltpu.roll(upward, 1, 0)
            total = total + right + pltpu.roll(right, 1, 1)
            plane[p] = (0.5 / load_cases) * total * coef[p]
            before, here = ahead, later
        return before

    each_chunk(planes, count, share_chunk, zero)

    for x in range(planes):
        share = plane_ref[x + 2]
        beside_ref[x + 2] = shift_sum(share, 1, 1)
        further_ref[x + 2] = shift_sum(share, 1, 2)
    filter_group(1, shares, weight_ref, near_ref, far_ref, sent_ref)


def kept_kernel(
    disp_ref,
    weight_ref,
    plane_ref,
    beside_ref,
    further_ref,
    density_ref,
    disp_hbm,
    kept_ref,
    low_ref,
    high_ref,
    near_ref,
    far_ref,
    stored,
):
    layers = kept_ref.shape[2]
    inner = pl.ds(layers, disp_ref.shape[1] - 2 * layers)
    store = pltpu.make_async_copy(disp_ref.at[:, inner], disp_hbm, stored)
    store.start()
    shares = (plane_ref, beside_ref, further_ref)
    filter_group(0, shares, weight_ref, near_ref, far_ref, kept_ref)
    groups, chips, own_planes = density_ref.shape[:3]
    for group in range(groups):
        for chip in range(chips):
            for own in range(own_planes):
                density = density_ref[group, chip, own]
                low_ref[group, chip, own] = jnp.maximum(density - move_limit, density_floor)
                high_ref[group, chip, own] = jnp.minimum(density + move_limit, 1.0)
    store.wait()


def design_kernel(root_ref, density_ref, low_ref, high_ref, new_ref, pull_ref):
    groups, chips, own_planes, layers, row_width = density_ref.shape
    tile_rows = pull_ref.shape[1]
    steps = layers // tile_rows
    shape = (tile_rows, row_width)
    zero = jnp.zeros(shape, jnp.float32)
    tiles = [
        (group, chip, own, pl.ds(step * tile_rows, tile_rows))
        for group in range(groups)
        for chip in range(chips)
        for own in range(own_planes)
        for step in range(steps)
    ]
    for place, spot in enumerate(tiles):
        pull_ref[place] = density_ref[spot] * root_ref[spot]

    target = volume_share * len(tiles) * tile_rows * row_width

    def exceeds(total):
        volume = jnp.sum(jnp.sum(total, axis=0, keepdims=True), axis=1, keepdims=True)
        return jnp.broadcast_to(volume, shape) > target

    def middles_of(lower, span):
        half, quarter = span * 0.5, span * 0.25
        return lower + quarter, lower + half, lower + half + quarter

    def factors_of(lower, span):
        return [jnp.exp(-0.5 * middle) for middle in middles_of(lower, span)]

    def halve_twice(step, state):
        lower, span, *factors = state
        places = (lower,) + middles_of(lower, span)
        quarter = span * 0.25
        ahead = [factors_of(place, quarter) for place in places]
        totals = [[zero, zero] for _ in factors]
        for place, spot in enumerate(tiles):
            pull, low, high = pull_ref[place], low_ref[spot], high_ref[spot]
            for total, factor in zip(totals, factors):
                trial = jnp.minimum(jnp.maximum(pull * factor, low), high)
                total[place % 2] = total[place % 2] + trial
        first, second, third = (exceeds(even + odd) for even, odd in totals)

        def pick(options):
            upper = jnp.where(third, options[3], options[2])
            return jnp.where(second, upper, jnp.where(first, options[1], options[0]))

        return (pick(places), quarter, *(pick(options) for options in zip(*ahead)))

    lower, span = jnp.full(shape, log_lower), jnp.full(shape, log_span)
    state = (lower, span, *factors_of(lower, span))
    lower, span, *_ = lax.fori_loop(0, SEARCH // 2, halve_twice, state)
    factor = jnp.exp(-0.5 * (lower + 0.5 * span))
    own_chip = lax.axis_index("space") >> 1
    for own in range(own_planes):
        for step in range(steps):
            place = (own_chip * own_planes + own) * steps + step
            part = pl.ds(step * tile_rows, tile_rows)
            spot = (0, own_chip, own, part)
            new_ref[own, part] = jnp.minimum(
                jnp.maximum(pull_ref[place] * factor, low_ref[spot]), high_ref[spot]
            )


def in_vmem():
    return pl.BlockSpec(memory_space=pltpu.VMEM)


KERNEL_VMEM = 24 * 2**20


def floats(*shape):
    return jax.ShapeDtypeStruct(shape, jnp.float32)


def prepare_call(density, radius, load_index, load_force, fixed):
    chips, own_planes, layers, row_width = density.shape
    planes = fixed.shape[0]
    spread = pltpu.VMEM((chips * own_planes * (layers + GAP) + GAP, row_width), jnp.float32)
    return pl.pallas_call(
        prepare_kernel,
        out_shape=[
            floats(len(ALL_SQUARES), layers, row_width),
            floats(2 * window_reach + 1, layers, row_width),
            floats(planes, layers, row_width),
            floats(3, layers, row_width),
            floats(8, row_width),
            floats(3, *density.shape),
        ],
        in_specs=[pl.BlockSpec(memory_space=pltpu.HBM)] * 4 + [in_vmem()],
        out_specs=[in_vmem()] * 6,
        scratch_shapes=[
            pltpu.SMEM(radius.shape, radius.dtype),
            pltpu.SMEM(load_index.shape, load_index.dtype),
            pltpu.SMEM(load_force.shape, load_force.dtype),
            pltpu.VMEM(fixed.shape, fixed.dtype),
            spread,
            spread,
            spread,
            pltpu.SemaphoreType.DMA((4,)),
        ],
        compiler_params=pltpu.CompilerParams(vmem_limit_bytes=KERNEL_VMEM),
        cost_estimate=pl.CostEstimate(
            flops=80 * planes * layers * row_width,
            bytes_accessed=8 * planes * layers * row_width,
            transcendentals=0,
        ),
        name="prepare",
    )(
        *(
            pltpu.with_memory_space_constraint(array, pltpu.HBM)
            for array in (radius, load_index, load_force, fixed)
        ),
        density,
    )


def sweep_call(spot, load, weights, inverses, free, filtered, density, displacement):
    groups, chips, own_planes, layers, row_width = density.shape
    planes = groups * chips * own_planes

    def scratch(*lead):
        return pltpu.VMEM(lead + (row_width,), jnp.float32)

    return pl.pallas_call(
        sweep_kernel,
        out_shape=[
            floats(3, (planes + 2) * layers, row_width),
            floats(planes, layers, row_width),
        ],
        in_specs=[in_vmem()] * 8,
        out_specs=[in_vmem()] * 2,
        scratch_shapes=[
            scratch(planes // 2 * (layers + GAP) + GAP),
            scratch(planes // 2 * (layers + GAP) + GAP),
            scratch(planes // 2 * (layers + GAP) + GAP),
            scratch(planes + 4, layers),
            scratch(planes + 4, layers),
            scratch(planes + 4, layers),
            scratch((planes + 2) * layers),
            scratch(planes + 1, layers),
            scratch((planes + 1) * layers),
            scratch(planes + 1, layers),
            scratch(planes + 1, layers),
            scratch(3, planes + 1, layers),
            scratch(3, (planes + 2) * layers),
        ],
        compiler_params=pltpu.CompilerParams(vmem_limit_bytes=KERNEL_VMEM),
        name="sweeps",
    )(spot, load, weights, inverses, free, filtered, density, displacement)


def share_call(disp, coef, weights, group_shape):
    planes, layers, row_width = coef.shape
    gaps = pltpu.VMEM((planes // 2 * (layers + GAP) + GAP, row_width), jnp.float32)
    return pl.pallas_call(
        share_kernel,
        out_shape=[floats(*group_shape)] + [floats(planes + 4, layers, row_width)] * 3,
        in_specs=[in_vmem()] * 3,
        out_specs=[in_vmem()] * 4,
        scratch_shapes=[gaps, gaps],
        compiler_params=pltpu.CompilerParams(vmem_limit_bytes=KERNEL_VMEM),
        name="share",
    )(disp, coef, weights)


def kept_call(disp, weights, shares, density, group_shape):
    parts, disp_rows, row_width = disp.shape
    chips, own_planes, layers = group_shape[:3]
    gaps = pltpu.VMEM((chips * own_planes * (layers + GAP) + GAP, row_width), jnp.float32)
    return pl.pallas_call(
        kept_kernel,
        out_shape=[
            floats(parts, disp_rows - 2 * layers, row_width),
            floats(*group_shape),
            floats(*density.shape),
            floats(*density.shape),
        ],
        in_specs=[in_vmem()] * 6,
        out_specs=[pl.BlockSpec(memory_space=pltpu.HBM)] + [in_vmem()] * 3,
        scratch_shapes=[gaps, gaps, pltpu.SemaphoreType.DMA(())],
        compiler_params=pltpu.CompilerParams(vmem_limit_bytes=KERNEL_VMEM),
        cost_estimate=pl.CostEstimate(
            flops=20 * disp.size, bytes_accessed=8 * disp.size, transcendentals=0
        ),
        name="kept",
    )(disp, weights, *shares, density)


def design_call(root, density, low, high):
    tile_rows = min(8, density.shape[-2])
    row_width = density.shape[-1]
    tiles = pltpu.VMEM((density.size // (tile_rows * row_width), tile_rows, row_width), jnp.float32)
    return pl.pallas_call(
        design_kernel,
        out_shape=floats(*density.shape[2:]),
        in_specs=[in_vmem()] * 4,
        out_specs=in_vmem(),
        scratch_shapes=[tiles],
        compiler_params=pltpu.CompilerParams(vmem_limit_bytes=KERNEL_VMEM),
        name="design",
    )(root, density, low, high)


def other_core(block):
    devices = lax.axis_size("space")
    return lax.ppermute(block, "space", [(i, i ^ 1) for i in range(devices)])


def chip_groups():
    chips = lax.axis_size("space") // 2
    return [[2 * chip + (chip ^ group) % 2 for chip in range(chips)] for group in range(2)]


def between_chips(pieces):
    return lax.all_to_all(pieces, "space", 0, 0, axis_index_groups=chip_groups())


def chip_gathered(block):
    chips = lax.axis_size("space") // 2
    return between_chips(jnp.broadcast_to(block[None], (chips,) + block.shape))


def with_other_core(blocks):
    return jnp.stack([blocks, other_core(blocks)])


def scattered_sum(sent, make_kept):
    received = other_core(sent)
    kept, *others = make_kept()
    return jnp.sum(between_chips(kept + received), axis=0), others


def one_slab(density, displacement, fixed, load_index, load_force, radius):
    same_group, small = lax.optimization_barrier(
        (chip_gathered(density), (radius, load_index, load_force.T, fixed))
    )
    other_group = other_core(same_group)
    weights, inverses, free, load, spot, filtered = prepare_call(same_group, *small)
    whole = jnp.stack([same_group, other_group])
    disp, coef = sweep_call(
        spot, load, weights, inverses, free, filtered, whole, displacement[0]
    )
    sent, *shares = share_call(disp, coef, weights, same_group.shape)
    sent, disp, shares = lax.optimization_barrier((sent, disp, shares))
    def make_kept():
        stored, kept, *limits = kept_call(disp, weights, shares, whole, same_group.shape)
        return kept, stored, *limits

    squares, (new_displacement, low, high) = scattered_sum(sent, make_kept)
    root = with_other_core(chip_gathered(jnp.sqrt(squares)))
    new_density = design_call(root, whole, low, high)
    return new_density, new_displacement.reshape(displacement.shape)


def from_behind(block, axis, distance):
    devices = range(lax.axis_size(axis))
    route = [(i - distance, i) for i in devices if i - distance in devices]
    return lax.ppermute(block, axis, route)


def extended(x, sides, width):
    for axis, dim in sides:
        size, length = (lax.axis_size(axis), x.shape[dim])
        up = [(i, (i + 1) % size) for i in range(size - 1)]
        down = [(j, i) for i, j in up]
        last = lax.slice_in_dim(x, length - width, length, axis=dim)
        first = lax.slice_in_dim(x, 0, width, axis=dim)
        before = lax.ppermute(last, axis, up)
        after = lax.ppermute(first, axis, down)
        x = jnp.concatenate([before, x, after], axis=dim)
    return x


def from_partner(x, axis, bit):
    return lax.ppermute(x, axis, [(i, i ^ 1 << bit) for i in range(lax.axis_size(axis))])


def window_offsets():
    offsets_list = []
    for across in range(-window_reach, window_reach + 1):
        for upward in range(-window_reach, window_reach + 1):
            for sideways in range(-window_reach, window_reach + 1):
                length = math.sqrt(across * across + upward * upward + sideways * sideways)
                offsets_list.append((across, upward, sideways, length))
    return offsets_list


def layer_weights(radius):
    radial = radius.astype(jnp.float32)
    return jnp.stack(
        [jnp.maximum(radial - length, 0.0) for across, upward, sideways, length in window_offsets()]
    )


def pad_axis(grid_field, along_axis, before, after_cells):
    widths = [(0, 0)] * grid_field.ndim
    widths[along_axis] = (before, after_cells)
    return jnp.pad(grid_field, widths)


def pad_sides(grid_field):
    return jnp.pad(grid_field, ((0, 0), (window_reach, window_reach), (window_reach, window_reach)))


def filter_forward(padded, weights):
    out_rows = padded.shape[0] - 2 * window_reach
    layers = padded.shape[1] - 2 * window_reach
    row_width = padded.shape[2] - 2 * window_reach
    result = jnp.zeros((out_rows, layers, row_width), jnp.float32)
    for offset_index, (across, upward, sideways, length) in enumerate(window_offsets()):
        shifted = padded[
            window_reach + across : window_reach + across + out_rows,
            window_reach + upward : window_reach + upward + layers,
            window_reach + sideways : window_reach + sideways + row_width,
        ]
        result = result + weights[offset_index][None, :, None] * shifted
    return result


def filter_backward(padded, padded_weights):
    out_rows = padded.shape[0] - 2 * window_reach
    layers = padded.shape[1] - 2 * window_reach
    row_width = padded.shape[2] - 2 * window_reach
    result = jnp.zeros((out_rows, layers, row_width), jnp.float32)
    for offset_index, (across, upward, sideways, length) in enumerate(window_offsets()):
        shifted = padded[
            window_reach - across : window_reach - across + out_rows,
            window_reach - upward : window_reach - upward + layers,
            window_reach - sideways : window_reach - sideways + row_width,
        ]
        layer_part = padded_weights[
            offset_index, window_reach - upward : window_reach - upward + layers
        ]
        result = result + layer_part[None, :, None] * shifted
    return result


def stiff_factors(direction):
    return jnp.array(
        [2.0 if component == direction else 1.0 for component in range(3)], jnp.float32
    ).reshape(3, 1, 1, 1)


def relax_slab(padded, displace, face_x, face_z, face_y, force_field, free_cells, diagonal):
    flux_x = stiff_factors(0) * face_x * jnp.diff(padded, axis=1)
    stencil_image = flux_x[:, :-1] - flux_x[:, 1:]
    flux_z = stiff_factors(1) * face_z * jnp.diff(displace, axis=2)
    stencil_image = stencil_image + pad_axis(flux_z, 2, 1, 0) - pad_axis(flux_z, 2, 0, 1)
    flux_y = stiff_factors(2) * face_y * jnp.diff(displace, axis=3)
    stencil_image = stencil_image + pad_axis(flux_y, 3, 1, 0) - pad_axis(flux_y, 3, 0, 1)
    return free_cells * (displace + relax_factor * (force_field - stencil_image) / diagonal)


def slab_energy(grid_field, along_axis, direction, load_cases):
    change = jnp.diff(grid_field, axis=along_axis)
    return jnp.sum(stiff_factors(direction) * change * change, axis=0) / load_cases


def neighbour_planes(displace, load_cases, axis_devices):
    if axis_devices > load_cases:
        below = from_behind(displace[:, -1:], "space", load_cases)
        above = from_behind(displace[:, :1], "space", -load_cases)
    else:
        below = jnp.zeros_like(displace[:, :1])
        above = jnp.zeros_like(displace[:, :1])
    return jnp.concatenate([below, displace, above], axis=1)


def many_slabs(density, displacement, fixed, load_index, load_force, radius):
    slab_rows, layers, row_width = density.shape
    load_cases = load_index.shape[0]
    level_count = load_cases.bit_length() - 1
    axis_devices = lax.axis_size("space")
    axis_place = lax.axis_index("space")
    slab_planes = slab_rows * load_cases
    slab_place = axis_place // load_cases
    load_place = axis_place % load_cases
    total_rows = slab_rows * axis_devices
    weights = layer_weights(radius)
    padded_weights = pad_axis(weights, 1, window_reach, window_reach)
    global_rows = (
        jnp.arange(slab_rows + 2 * window_reach, dtype=jnp.int32)
        + axis_place * slab_rows
        - window_reach
    )
    deep_inside = ((global_rows >= 0) & (global_rows < total_rows)).astype(jnp.float32)
    inside_field = deep_inside[:, None, None] * pad_sides(
        jnp.ones((slab_rows + 2 * window_reach, layers, row_width), jnp.float32)
    )
    total_weight = filter_forward(inside_field, weights)
    slab_start = slab_place * slab_planes
    margin_rows = jnp.arange(slab_planes + 2, dtype=jnp.int32) + slab_start - 1
    margin_inside = ((margin_rows >= 0) & (margin_rows < total_rows)).astype(jnp.float32)
    face_valid = margin_inside[1:] * margin_inside[:-1]
    fixed_slab = lax.dynamic_slice_in_dim(fixed, slab_start, slab_planes, 0).astype(jnp.float32)
    bottom_layer = (jnp.arange(layers, dtype=jnp.int32) == 0).astype(jnp.float32)
    free_cells = 1.0 - bottom_layer[None, :, None] * fixed_slab[:, None, :]
    slab_cells = slab_planes * layers * row_width
    cell_index = jnp.arange(slab_cells, dtype=jnp.int32) + slab_place * slab_cells
    load_hot = jnp.arange(load_cases, dtype=jnp.int32) == load_place
    own_index = jnp.sum(jnp.where(load_hot, load_index, 0))
    own_force = jnp.sum(load_hot.astype(jnp.float32)[:, None] * load_force, axis=0)
    load_hits = (cell_index == own_index).astype(jnp.float32)
    force_field = (own_force[:, None] * load_hits[None, :]).reshape(
        3, slab_planes, layers, row_width
    )
    displace = displacement[0] * free_cells
    target = volume_share * total_rows * layers * row_width
    padded = neighbour_planes(displace, load_cases, axis_devices)
    halo_density = extended(density, (("space", 0),), window_reach)
    filtered = filter_forward(pad_sides(halo_density), weights) / total_weight
    whole_field = lax.all_gather(filtered, "space", axis=0, tiled=True)
    margin = lax.dynamic_slice_in_dim(
        pad_axis(whole_field, 0, 1, 1), slab_start, slab_planes + 2, 0
    )
    moduli = floor_modulus + (1.0 - floor_modulus) * margin**3
    face_x = 0.5 * (moduli[1:] + moduli[:-1]) * face_valid[:, None, None]
    inner_moduli = moduli[1:-1]
    face_z = 0.5 * (inner_moduli[:, 1:] + inner_moduli[:, :-1])
    face_y = 0.5 * (inner_moduli[:, :, 1:] + inner_moduli[:, :, :-1])
    sum_x = face_x[:-1] + face_x[1:]
    sum_z = pad_axis(face_z, 1, 1, 0) + pad_axis(face_z, 1, 0, 1)
    sum_y = pad_axis(face_y, 2, 1, 0) + pad_axis(face_y, 2, 0, 1)
    diagonal = stiff_factors(0) * sum_x + stiff_factors(1) * sum_z + stiff_factors(2) * sum_y
    for sweep_index in range(SWEEPS):
        displace = relax_slab(
            padded, displace, face_x, face_z, face_y, force_field, free_cells, diagonal
        )
        padded = neighbour_planes(displace, load_cases, axis_devices)
    energy_x = slab_energy(padded, 1, 0, load_cases) * face_valid[:, None, None]
    energy_z = slab_energy(displace, 2, 1, load_cases)
    energy_y = slab_energy(displace, 3, 2, load_cases)
    sens_term = 0.5 * (
        energy_x[:-1]
        + energy_x[1:]
        + pad_axis(energy_z, 1, 1, 0)
        + pad_axis(energy_z, 1, 0, 1)
        + pad_axis(energy_y, 2, 1, 0)
        + pad_axis(energy_y, 2, 0, 1)
    )
    sensitive = sens_term
    for level in reversed(range(level_count)):
        half_rows = sensitive.shape[0] // 2
        upper_side = load_place // 2**level % 2 == 1
        outgoing = jnp.where(upper_side, sensitive[:half_rows], sensitive[half_rows:])
        keeping = jnp.where(upper_side, sensitive[half_rows:], sensitive[:half_rows])
        sensitive = keeping + from_partner(outgoing, "space", level)
    weighted_share = 3.0 * (1.0 - floor_modulus) * filtered**2 * sensitive / total_weight
    halo_share = extended(weighted_share, (("space", 0),), window_reach)
    root_term = jnp.sqrt(filter_backward(pad_sides(halo_share), padded_weights))
    lowest = jnp.maximum(density - move_limit, density_floor)
    highest = jnp.minimum(density + move_limit, 1.0)
    design_now = density

    def trial_design(log_level):
        return jnp.clip(design_now * root_term * jnp.exp(-0.5 * log_level), lowest, highest)

    start_state = (jnp.asarray(log_lower, jnp.float32), jnp.asarray(log_span, jnp.float32))

    def halve(search_step, search_state):
        lower_end, span_width = search_state
        half_span = span_width * 0.5
        middle = lower_end + half_span
        volume_total = lax.psum(jnp.sum(trial_design(middle)), "space")
        return (jnp.where(volume_total > target, middle, lower_end), half_span)

    lower_end, span_width = lax.fori_loop(0, SEARCH, halve, start_state)
    density = trial_design(lower_end + 0.5 * span_width)
    new_displacement = displace[None]
    return (density, new_displacement)


def solution(mesh):
    in_specs = (
        P("space", "parts", None),
        P("space", None, None, "parts", None),
        P(None, "parts"),
        P("parts"),
        P("parts", None),
        P("parts"),
    )
    out_specs = (P("space", "parts", None), P("space", None, None, "parts", None))

    def local(density, displacement, fixed, load_index, load_force, radius):
        alone = lax.axis_size("space") == load_index.shape[0]
        run = one_slab if alone else many_slabs
        return run(density, displacement, fixed, load_index, load_force, radius)

    return jax.shard_map(local, mesh=mesh, in_specs=in_specs, out_specs=out_specs, check_vma=False)
```
